32 devices in a mesh: batch: 8 (over z, core), expert: 4 (over y, x).
Axes of the slice: x: 2, y: 2, z: 4, core: 2. Of those that a mesh axis runs over, the one named last changes fastest.
Arguments:
- tokens: bfloat16 [8, 1024, 1536], P('batch', 'expert'), may hold values from -6 to 6
- cotangent: bfloat16 [8, 1024, 1536], P('batch', 'expert'), may hold values from -6 to 6
- attn_gain: bfloat16 [1536], P(('batch', 'expert')), may hold values from 0.5 to 1.5
- query_weight: bfloat16 [1536, 1536], P(('batch', 'expert')), may hold values from -0.15625 to 0.15625
- key_weight: bfloat16 [1536, 512], P(('batch', 'expert')), may hold values from -0.15625 to 0.15625
- value_weight: bfloat16 [1536, 512], P(('batch', 'expert')), may hold values from -0.15625 to 0.15625
- out_weight: bfloat16 [1536, 1536], P(('batch', 'expert')), may hold values from -1 to 1
- ffn_gain: bfloat16 [1536], P(('batch', 'expert')), may hold values from 0.5 to 1.5
- router_weight: bfloat16 [1536, 20], P(('batch', 'expert')), may hold values from -0.078125 to 0.078125
- gate_weight: bfloat16 [20, 1536, 512], P('expert', 'batch'), may hold values from -0.15625 to 0.15625
- up_weight: bfloat16 [20, 1536, 512], P('expert', 'batch'), may hold values from -0.15625 to 0.15625
- down_weight: bfloat16 [20, 512, 1536], P('expert', 'batch'), may hold values from -1 to 1
- routes: int32 [8, 1024, 8], P('batch', 'expert'), may hold values from 0 to 19, all different within a row
- ranking: int32 [8, 1024], P('batch', 'expert'), may hold values from 0 to 1023, each once within a row
Outputs:
- layer_out: bfloat16 [8, 1024, 1536], P('batch', 'expert')
- input_grad: float32 [8, 1024, 1536], P('batch', 'expert')
- attn_gain_grad: float32 [1536], P(('batch', 'expert'))
- query_grad: float32 [1536, 1536], P(('batch', 'expert'))
- key_grad: float32 [1536, 512], P(('batch', 'expert'))
- value_grad: float32 [1536, 512], P(('batch', 'expert'))
- out_proj_grad: float32 [1536, 1536], P(('batch', 'expert'))
- ffn_gain_grad: float32 [1536], P(('batch', 'expert'))
- router_grad: float32 [1536, 20], P(('batch', 'expert'))
- gate_proj_grad: float32 [20, 1536, 512], P('expert', 'batch')
- up_proj_grad: float32 [20, 1536, 512], P('expert', 'batch')
- down_proj_grad: float32 [20, 512, 1536], P('expert', 'batch')
The draws below stay inside these ranges and needn't reach their ends.
Inputs may be any that keep to these rules, and one draw needn't show every extreme that they name: `routes`: each token names 8 different experts, and every expert is named by some token. `ranking`: within each group a permutation of the rows.
All inputs are finite; a program needn't handle non-finite values.
Results may differ from the reference program's by a relative error of at most 0.02.
Values may be sent and summed in bfloat16 or wider, within the bound.
No kernel may reach another device: no remote copies, remote signals or barrier semaphores. Data moves between devices by JAX's collectives and lax.ppermute only.
A program may use at most 256 MiB of HBM per device.

```python
import jax
import jax.numpy as jnp
from jax import lax

D = 1536
HEADS = 24
KV_HEADS = 8
HEAD_DIM = 64
FF = 512
TOP = 8
PROMPT = 512
CLEN = 256
GROUP = 1024
GROUPS = 8
EXPERTS = 20
CAP = 512


def block_scale(stream_key, shape, cuts, least, high):
    factor_of = 1.0
    for dim, blocks in cuts:
        draws = jax.random.uniform(jax.random.fold_in(jax.random.fold_in(stream_key, 6), dim), (blocks,), jnp.float32, least / len(cuts), high / len(cuts))
        factor_of = factor_of * jnp.repeat(jnp.exp(draws), shape[dim] // blocks).reshape((-1,) + (1,) * (len(shape) - 1 - dim))
    return factor_of


def different_ones(stream_key, rows, amount, top, lift):
    order = jax.random.permutation(jax.random.fold_in(stream_key, 1), amount)
    boost = order
    for power in range(3):
        boost = boost * boost // amount
    boost = boost * lift // amount
    chance = jax.random.randint(jax.random.fold_in(stream_key, 2), (rows, amount), 0, 4096) + boost
    fixed_rows = jax.random.permutation(jax.random.fold_in(stream_key, 3), rows)[jnp.arange(amount) % rows]
    chance = jnp.where(jnp.arange(rows)[:, None] == fixed_rows[None, :], 1 << 14, chance)
    priority = chance * amount + jnp.arange(amount)
    return lax.top_k(priority.astype(jnp.int32), top)[1].astype(jnp.int32)


def gaussian(key, shape, deviation, most, pieces=(), kind=jnp.bfloat16):
    level = block_scale(key, shape, pieces, -0.22, 0.18) if pieces else 1.0
    values = jax.random.normal(key, shape, jnp.float32) * deviation * level
    return jnp.minimum(jnp.maximum(values, -most), most).astype(kind)


def setup_inputs(seed: int = 0) -> dict:
    streams_of = jax.random.split(jax.random.key(seed), 15)
    return {
        "tokens": gaussian(streams_of[0], (GROUPS, GROUP, D), 1.0, 6.0, ((0, 8), (1, 4))),
        "cotangent": gaussian(streams_of[1], (GROUPS, GROUP, D), 1.0, 6.0, ((0, 8), (1, 4))),
        "attn_gain": jnp.clip(1.0 + 0.1 * jax.random.normal(streams_of[2], (D,), jnp.float32), 0.5, 1.5).astype(jnp.bfloat16),
        "query_weight": gaussian(streams_of[3], (D, HEADS * HEAD_DIM), D ** -0.5, 0.15625, ((0, 32),)),
        "key_weight": gaussian(streams_of[4], (D, KV_HEADS * HEAD_DIM), D ** -0.5, 0.15625, ((0, 32),)),
        "value_weight": gaussian(streams_of[5], (D, KV_HEADS * HEAD_DIM), D ** -0.5, 0.15625, ((0, 32),)),
        "out_weight": gaussian(streams_of[6], (HEADS * HEAD_DIM, D), 32 ** -0.5, 1.0, ((0, 32),)),
        "ffn_gain": jnp.clip(1.0 + 0.1 * jax.random.normal(streams_of[7], (D,), jnp.float32), 0.5, 1.5).astype(jnp.bfloat16),
        "router_weight": gaussian(streams_of[8], (D, EXPERTS), (4 * D) ** -0.5, 0.078125, ((0, 32),)),
        "gate_weight": gaussian(streams_of[9], (EXPERTS, D, FF), D ** -0.5, 0.15625, ((0, 4), (1, 8))),
        "up_weight": gaussian(streams_of[10], (EXPERTS, D, FF), D ** -0.5, 0.15625, ((0, 4), (1, 8))),
        "down_weight": gaussian(streams_of[11], (EXPERTS, FF, D), (FF // 16) ** -0.5, 1.0, ((0, 4), (1, 8))),
        "routes": different_ones(streams_of[12], GROUPS * GROUP, EXPERTS, TOP, 3276).reshape((GROUPS, GROUP, TOP)),
        "ranking": jax.vmap(lambda own: jax.random.permutation(own, GROUP))(jax.random.split(streams_of[13], GROUPS)).reshape((GROUPS, GROUP)).astype(jnp.int32),
    }


EPS = 1e-06
THETA = 10000.0
HIGHEST = lax.Precision.HIGHEST

@jax.custom_vjp
def low(v):
    return lax.optimization_barrier(v.astype(jnp.bfloat16)).astype(jnp.float32)

@jax.custom_vjp
def low_back(v):
    return v

def low_keep(v):
    return (low(v), None)

def low_pass(kept, grad):
    return (grad,)

def back_keep(v):
    return (v, None)

def back_low(kept, grad):
    return (low(grad),)
low.defvjp(low_keep, low_pass)
low_back.defvjp(back_keep, back_low)

def matmul(left, right):
    return jnp.dot(left, right, precision=HIGHEST, preferred_element_type=jnp.float32)

def positions():
    row_ids = jnp.arange(GROUP, dtype=jnp.int32)
    return jnp.where(row_ids < PROMPT, row_ids, PROMPT + (row_ids - PROMPT) % CLEN)

def rotary_tables(rotary_place):
    half_dim = HEAD_DIM // 2
    frequency = THETA ** (-jnp.arange(half_dim, dtype=jnp.float32) / half_dim)
    angles = rotary_place.astype(jnp.float32)[:, None] * frequency[None, :]
    return (jnp.cos(angles)[:, None, :], jnp.sin(angles)[:, None, :])

def rotate(values, cosine, sine_part):
    half_dim = values.shape[-1] // 2
    front_half = values[..., :half_dim]
    back_half = values[..., half_dim:]
    return jnp.concatenate([front_half * cosine - back_half * sine_part, back_half * cosine + front_half * sine_part], axis=-1)

def visible(query_ids, key_ids):
    causal = key_ids[None, :] <= query_ids[:, None]
    same_run = (key_ids[None, :] - PROMPT) // CLEN == (query_ids[:, None] - PROMPT) // CLEN
    return causal & ((key_ids[None, :] < PROMPT) | same_run)

def rms_scale(values):
    return lax.rsqrt(lax.optimization_barrier(jnp.mean(values * values, axis=-1, keepdims=True)) + EPS)

def slot_table(route_rows, rank_rows):
    member = lax.optimization_barrier(jnp.sum((route_rows[:, :, None] == jnp.arange(EXPERTS, dtype=jnp.int32)[None, None, :]).astype(jnp.int32), axis=1))
    ranked = jnp.argsort(rank_rows).astype(jnp.int32)
    sorted_member = member[ranked]
    before = jnp.cumsum(sorted_member, axis=0) - sorted_member
    counts = jnp.zeros_like(before).at[ranked].set(before)
    slot_index = jnp.take_along_axis(counts, route_rows, axis=1)
    kept_pair = slot_index < CAP
    flat_slot = jnp.where(kept_pair, route_rows * CAP + slot_index, EXPERTS * CAP).reshape(-1)
    token_ids = jnp.broadcast_to(jnp.arange(GROUP, dtype=jnp.int32)[:, None], (GROUP, TOP)).reshape(-1)
    pair_ids = jnp.arange(GROUP * TOP, dtype=jnp.int32)
    slot_token = jnp.full((EXPERTS * CAP + 1,), GROUP, jnp.int32).at[flat_slot].set(token_ids)[:EXPERTS * CAP]
    pair_index = jnp.full((EXPERTS * CAP + 1,), GROUP * TOP, jnp.int32).at[flat_slot].set(pair_ids)[:EXPERTS * CAP]
    return (slot_token, pair_index)

def group_forward(params, rows_in, route_rows, rank_rows):
    attn_gain, query_weight, key_weight, value_weight, out_weight, ffn_gain, router_weight, gate_weight, up_weight, down_weight = params
    cosine, sine_part = rotary_tables(positions())
    normed = low(rows_in * rms_scale(rows_in) * attn_gain)
    queries = low_back(matmul(normed, query_weight)).reshape(GROUP, HEADS, HEAD_DIM)
    queries = low(rotate(queries, cosine, sine_part))
    key_rows = low_back(matmul(normed, key_weight)).reshape(GROUP, KV_HEADS, HEAD_DIM)
    key_rows = low(rotate(key_rows, cosine, sine_part))
    value_rows = low(low_back(matmul(normed, value_weight))).reshape(GROUP, KV_HEADS, HEAD_DIM)
    repeat = HEADS // KV_HEADS
    query_heads = queries.reshape(GROUP, KV_HEADS, repeat, HEAD_DIM)
    scores = jnp.einsum('qgrd,kgd->grqk', query_heads, key_rows, precision=HIGHEST) * HEAD_DIM ** (-0.5)
    scores = low_back(scores)
    row_ids = jnp.arange(GROUP, dtype=jnp.int32)
    scores = jnp.where(visible(row_ids, row_ids)[None, None], scores, -jnp.inf)
    weights_low = low(jax.nn.softmax(scores, axis=-1))
    attended = jnp.einsum('grqk,kgd->qgrd', weights_low, value_rows, precision=HIGHEST)
    attended = low(low_back(attended)).reshape(GROUP, HEADS * HEAD_DIM)
    residual = rows_in + low_back(matmul(attended, out_weight))
    normed_two = low(residual * rms_scale(residual) * ffn_gain)
    logits = low_back(matmul(normed_two, router_weight))
    chosen = jnp.take_along_axis(logits, route_rows, axis=1)
    gate_probs = low(jax.nn.softmax(chosen, axis=-1))
    slot_token, pair_index = slot_table(route_rows, rank_rows)
    padded = jnp.concatenate([normed_two, jnp.zeros((1, D), jnp.float32)], axis=0)
    slot_inputs = padded[slot_token].reshape(EXPERTS, CAP, D)
    gate_pre = low_back(jnp.einsum('ecd,edf->ecf', slot_inputs, gate_weight, precision=HIGHEST))
    up_pre = low_back(jnp.einsum('ecd,edf->ecf', slot_inputs, up_weight, precision=HIGHEST))
    hidden = low(jax.nn.silu(gate_pre) * up_pre)
    expert_out = low_back(jnp.einsum('ecf,efd->ecd', hidden, down_weight, precision=HIGHEST)).reshape(EXPERTS * CAP, D)
    gate_pad = jnp.concatenate([gate_probs.reshape(-1), jnp.zeros((1,), jnp.float32)])
    slot_gates = gate_pad[pair_index]
    combined = jnp.zeros((GROUP + 1, D), jnp.float32).at[slot_token].add(slot_gates[:, None] * expert_out)[:GROUP]
    return residual + combined

def reference(tokens, cotangent, attn_gain, query_weight, key_weight, value_weight, out_weight, ffn_gain, router_weight, gate_weight, up_weight, down_weight, routes, ranking):
    params = tuple((argument.astype(jnp.float32) for argument in (attn_gain, query_weight, key_weight, value_weight, out_weight, ffn_gain, router_weight, gate_weight, up_weight, down_weight)))

    def forward_all(params, inputs):

        def per_group(carried, group_data):
            return (carried, jax.checkpoint(group_forward)(params, group_data[0], group_data[1], group_data[2]))
        return lax.scan(per_group, jnp.int32(0), (inputs, routes, ranking))[1]
    result, pullback = jax.vjp(forward_all, params, tokens.astype(jnp.float32))
    gradients, input_grad = pullback(cotangent.astype(jnp.float32))
    return (result.astype(jnp.bfloat16), input_grad, gradients[0], gradients[1], gradients[2], gradients[3], gradients[4], gradients[5], gradients[6], gradients[7], gradients[8], gradients[9])
```

```python
from functools import partial

import jax
import jax.numpy as jnp
from jax import lax
from jax.sharding import PartitionSpec as P

HEADS = 24
KV_HEADS = 8
HEAD_DIM = 64
PROMPT = 512
CLEN = 256


EPS = 1e-06
THETA = 10000.0


def product(left, right):
    return jnp.dot(left, right, preferred_element_type=jnp.float32)


def rms_scale(values):
    return lax.rsqrt(jnp.mean(values * values, axis=-1, keepdims=True) + EPS)


def place_of(row_ids):
    return jnp.where(row_ids < PROMPT, row_ids, PROMPT + (row_ids - PROMPT) % CLEN)


def rotary_tables(rotary_place):
    half_dim = HEAD_DIM // 2
    frequency = THETA ** (-jnp.arange(half_dim, dtype=jnp.float32) / half_dim)
    angles = rotary_place.astype(jnp.float32)[:, None] * frequency[None, :]
    return (jnp.cos(angles)[:, None, :], jnp.sin(angles)[:, None, :])


def rotate(values, cosine, sine_part):
    half_dim = values.shape[-1] // 2
    front_half = values[..., :half_dim]
    back_half = values[..., half_dim:]
    return jnp.concatenate(
        [front_half * cosine - back_half * sine_part, back_half * cosine + front_half * sine_part],
        axis=-1,
    )


def unrotate(gradients, cosine, sine_part):
    half_dim = gradients.shape[-1] // 2
    front_half = gradients[..., :half_dim]
    back_half = gradients[..., half_dim:]
    return jnp.concatenate(
        [front_half * cosine + back_half * sine_part, back_half * cosine - front_half * sine_part],
        axis=-1,
    )


def visible(query_ids, key_ids):
    causal = key_ids[None, :] <= query_ids[:, None]
    same_run = (key_ids[None, :] - PROMPT) // CLEN == (query_ids[:, None] - PROMPT) // CLEN
    return causal & ((key_ids[None, :] < PROMPT) | same_run)


def head_scores(visible_mask, query_block, key_block):
    scores = jnp.einsum("rqd,kd->rqk", query_block, key_block, preferred_element_type=jnp.float32)
    scores = scores * query_block.shape[-1] ** (-0.5)
    return jnp.where(visible_mask[None], scores, -jnp.inf)


def head_forward(visible_mask, operands):
    query_block, key_block, value_block = operands
    scores = head_scores(visible_mask, query_block, key_block)
    row_peak = jnp.max(scores, axis=-1, keepdims=True)
    lifted = jnp.exp(scores - row_peak)
    row_total = jnp.sum(lifted, axis=-1, keepdims=True)
    weights_low = (lifted / row_total).astype(jnp.bfloat16)
    attended = jnp.einsum(
        "rqk,kd->rqd", weights_low, value_block, preferred_element_type=jnp.float32
    )
    return (attended, row_peak + jnp.log(row_total))


def head_backward(visible_mask, operands):
    query_block, key_block, value_block, grad_block, log_total = operands
    scale_factor = query_block.shape[-1] ** (-0.5)
    scores = head_scores(visible_mask, query_block, key_block)
    weights_full = jnp.exp(scores - log_total)
    grad_values = jnp.einsum(
        "rqk,rqd->kd",
        weights_full.astype(jnp.bfloat16),
        grad_block,
        preferred_element_type=jnp.float32,
    )
    grad_weights = jnp.einsum(
        "rqd,kd->rqk", grad_block, value_block, preferred_element_type=jnp.float32
    )
    grad_scores = weights_full * (
        grad_weights - jnp.sum(weights_full * grad_weights, axis=-1, keepdims=True)
    )
    grad_scores = grad_scores.astype(jnp.bfloat16)
    grad_queries = (
        jnp.einsum("rqk,kd->rqd", grad_scores, key_block, preferred_element_type=jnp.float32)
        * scale_factor
    )
    grad_keys = (
        jnp.einsum("rqk,rqd->kd", grad_scores, query_block, preferred_element_type=jnp.float32)
        * scale_factor
    )
    return (grad_queries, grad_keys, grad_values)


def pair_moves(size, flip):
    return [(i, i ^ flip) for i in range(size)]


def gather_blocks(rows):
    size = lax.axis_size("expert")
    if size != 4:
        stacked = lax.all_gather(rows, "expert", axis=0)
        own = lax.axis_index("expert")
        return [
            lax.dynamic_index_in_dim(stacked, own ^ r, axis=0, keepdims=False) for r in range(size)
        ]
    across, along = pair_moves(size, 1), pair_moves(size, 2)
    half = rows.shape[0] // 2
    first = lax.ppermute(rows, "expert", across)
    second = lax.ppermute(rows, "expert", along)
    top = lax.ppermute(second[:half], "expert", across)
    bottom = lax.ppermute(first[half:], "expert", along)
    return [rows, first, second, jnp.concatenate([top, bottom], axis=0)]


def scatter_blocks(parts):
    size = lax.axis_size("expert")
    low = jnp.bfloat16
    if size != 4:
        own = lax.axis_index("expert")
        order = jnp.arange(size, dtype=jnp.int32) ^ own
        stacked = jnp.take(jnp.stack(parts), order, axis=0).astype(low)
        return lax.psum_scatter(stacked, "expert", scatter_dimension=0).astype(jnp.float32)
    across, along = pair_moves(size, 1), pair_moves(size, 2)
    half = parts[0].shape[0] // 2
    far = parts[3].astype(low)
    top = lax.ppermute(far[:half], "expert", across).astype(jnp.float32)
    bottom = lax.ppermute(far[half:], "expert", along).astype(jnp.float32)
    for_second = jnp.concatenate([parts[2][:half] + top, parts[2][half:]], axis=0)
    for_first = jnp.concatenate([parts[1][:half], parts[1][half:] + bottom], axis=0)
    from_first = lax.ppermute(for_first.astype(low), "expert", across)
    from_second = lax.ppermute(for_second.astype(low), "expert", along)
    return parts[0] + from_first.astype(jnp.float32) + from_second.astype(jnp.float32)


def in_order(blocks):
    own = lax.axis_index("expert")
    return jnp.concatenate(
        [lax.select_n(own ^ k, *blocks) if len(blocks) > 1 else blocks[0] for k in range(len(blocks))],
        axis=0,
    )


def from_order(values, count):
    own = lax.axis_index("expert")
    rows = values.shape[0] // count
    return [
        lax.dynamic_slice_in_dim(values, (own ^ r) * rows, rows, axis=0) for r in range(count)
    ]


def local(
    tokens,
    cotangent,
    attn_gain,
    query_weight,
    key_weight,
    value_weight,
    out_weight,
    ffn_gain,
    router_weight,
    gate_weight,
    up_weight,
    down_weight,
    routes,
    ranking,
):
    low = jnp.bfloat16
    both = ("batch", "expert")
    query_width = HEADS * HEAD_DIM
    kv_width = KV_HEADS * HEAD_DIM
    qkv_width = query_width + 2 * kv_width
    width = tokens.shape[2]
    experts_total = router_weight.shape[1]
    extra = -(-(experts_total + 2) // 128) * 128
    local_experts, model_part, hidden_width = gate_weight.shape
    hidden_all = local_experts * hidden_width
    member_count = lax.axis_size("expert")
    member_id = lax.axis_index("expert")
    local_rows = tokens.shape[1]
    group_rows = local_rows * member_count
    dense = lax.all_gather(
        jnp.concatenate(
            [
                query_weight,
                key_weight,
                value_weight,
                out_weight,
                router_weight,
                attn_gain[:, None],
                ffn_gain[:, None],
                jnp.zeros((query_weight.shape[0], extra - experts_total - 2), low),
            ],
            axis=1,
        ),
        both,
        axis=0,
        tiled=True,
    )
    qkv_full = dense[:, :qkv_width]
    out_full = dense[:, qkv_width : qkv_width + width]
    small = dense[:, qkv_width + width :]
    router_full = small[:, :experts_total]
    gain_first = small[:, experts_total].astype(jnp.float32)
    gain_second = small[:, experts_total + 1].astype(jnp.float32)

    dense, down_local = lax.optimization_barrier((dense, down_weight))
    down_full = lax.all_gather(down_local, "batch", axis=1, tiled=True)
    pair_local = jnp.concatenate(
        [
            gate_weight.transpose(1, 0, 2).reshape(model_part, hidden_all),
            up_weight.transpose(1, 0, 2).reshape(model_part, hidden_all),
        ],
        axis=1,
    )
    down_full, pair_local = lax.optimization_barrier((down_full, pair_local))
    pair_full = lax.all_gather(pair_local, "batch", axis=0, tiled=True)
    down_full = down_full.reshape(hidden_all, width)

    inputs = tokens[0].astype(jnp.float32)
    row_ids = member_id * local_rows + jnp.arange(local_rows, dtype=jnp.int32)
    group_ids = jnp.arange(group_rows, dtype=jnp.int32)
    cosine, sine_part = rotary_tables(place_of(row_ids))
    repeat = HEADS // KV_HEADS
    grad_out = cotangent[0]
    grad_blocks = gather_blocks(grad_out)

    scale_one = rms_scale(inputs)
    normed = (inputs * scale_one * gain_first).astype(low)
    qkv = product(normed, qkv_full)
    query_pre = qkv[:, :query_width].reshape(local_rows, HEADS, HEAD_DIM)
    queries = rotate(query_pre, cosine, sine_part).astype(low)
    key_pre = qkv[:, query_width : query_width + kv_width].reshape(local_rows, KV_HEADS, HEAD_DIM)
    key_rows = rotate(key_pre, cosine, sine_part).astype(low).reshape(local_rows, kv_width)
    value_rows = qkv[:, query_width + kv_width :].astype(low)

    route_rows = routes[0]
    rank_rows = ranking[0]
    picked = route_rows[:, :, None] == jnp.arange(experts_total, dtype=jnp.int32)[None, None, :]
    member = jnp.any(picked, axis=1)
    shared = jnp.concatenate(
        [
            key_rows,
            value_rows,
            member.astype(low),
            (rank_rows // 32).astype(low)[:, None],
            (rank_rows % 32).astype(low)[:, None],
            jnp.zeros((local_rows, extra - experts_total - 2), low),
        ],
        axis=1,
    )
    shared_all = in_order(gather_blocks(shared))
    key_all = shared_all[:, :kv_width]
    value_all = shared_all[:, kv_width : 2 * kv_width]
    member_all = shared_all[:, 2 * kv_width : 2 * kv_width + experts_total]
    rank_parts = shared_all[:, 2 * kv_width + experts_total :][:, :2].astype(jnp.float32)
    rank_all = (rank_parts[:, 0] * 32 + rank_parts[:, 1]).astype(jnp.int32)
    earlier = (rank_all[None, :] < rank_rows[:, None]).astype(low)
    before = product(earlier, member_all)
    capacity = 5 * group_rows * route_rows.shape[1] // (4 * experts_total)
    kept = member & (before < capacity)

    query_heads = queries.reshape(local_rows, KV_HEADS, repeat, HEAD_DIM).transpose(1, 2, 0, 3)
    key_heads = key_all.reshape(group_rows, KV_HEADS, HEAD_DIM).transpose(1, 0, 2)
    value_heads = value_all.reshape(group_rows, KV_HEADS, HEAD_DIM).transpose(1, 0, 2)
    visible_mask = visible(row_ids, group_ids)
    head_out, log_totals = lax.map(
        partial(head_forward, visible_mask), (query_heads, key_heads, value_heads)
    )
    attended = head_out.transpose(2, 0, 1, 3).reshape(local_rows, query_width).astype(low)
    residual = inputs + product(attended, out_full)
    scale_two = rms_scale(residual)
    normed_two = (residual * scale_two * gain_second).astype(low)
    logits = product(normed_two, router_full)
    chosen = jnp.sum(jnp.where(picked, logits[:, None, :], 0.0), axis=-1)
    gate_probs = jax.nn.softmax(chosen, axis=-1)
    gate_rows = jnp.sum(jnp.where(picked, gate_probs[:, :, None], 0.0), axis=1)
    sent = jnp.concatenate(
        [
            normed_two,
            jnp.where(kept, gate_rows, 0.0).astype(low),
            jnp.zeros((local_rows, extra - experts_total), low),
        ],
        axis=1,
    )
    sent_all = jnp.concatenate(gather_blocks(sent), axis=0)
    rows_all = sent_all[:, :width]
    own_gates = lax.dynamic_slice_in_dim(
        sent_all[:, width : width + experts_total], member_id * local_experts, local_experts, axis=1
    ).astype(jnp.float32)
    grad_all = jnp.concatenate(grad_blocks, axis=0)

    slope = product(grad_all, down_full.T)
    pair_pre = product(rows_all, pair_full)
    gate_pre = pair_pre[:, :hidden_all]
    up_pre = pair_pre[:, hidden_all:]
    sigmoid_gate = jax.nn.sigmoid(gate_pre)
    activated = gate_pre * sigmoid_gate
    hidden = (activated * up_pre).astype(low).astype(jnp.float32)
    gate_wide = jnp.repeat(own_gates, hidden_width, axis=1)
    gate_grads = jnp.sum((hidden * slope).reshape(group_rows, local_experts, hidden_width), axis=-1)
    weighted = (hidden * gate_wide).astype(low)
    hidden_grad = slope * gate_wide
    gate_side = hidden_grad * up_pre * sigmoid_gate * (1.0 + gate_pre * (1.0 - sigmoid_gate))
    up_side = hidden_grad * activated
    sides = jnp.concatenate([gate_side.astype(low), up_side.astype(low)], axis=1)

    down_wgrad = product(weighted.T, grad_all).astype(low)
    pair_wgrad = product(rows_all.T, sides).astype(low)
    down_total = lax.psum_scatter(
        down_wgrad.reshape(local_experts, hidden_width, width),
        "batch",
        scatter_dimension=1,
        tiled=True,
    ).astype(jnp.float32)
    pair_total = lax.psum_scatter(pair_wgrad, "batch", scatter_dimension=0, tiled=True)
    pair_total = pair_total.astype(jnp.float32).reshape(
        model_part, 2, local_experts, hidden_width
    )
    gate_total = pair_total[:, 0].transpose(1, 0, 2)
    up_total = pair_total[:, 1].transpose(1, 0, 2)

    row_grad = product(sides, pair_full.T)
    gate_grads = lax.dynamic_update_slice_in_dim(
        jnp.zeros((group_rows, extra), jnp.float32), gate_grads, member_id * local_experts, axis=1
    )
    mixture_all = product(weighted, down_full)

    def blocks_of(values):
        return [values[r * local_rows : (r + 1) * local_rows] for r in range(member_count)]

    normed_grad = scatter_blocks(blocks_of(jnp.concatenate([row_grad, gate_grads], axis=1)))
    gate_grad_rows = jnp.where(kept, normed_grad[:, width : width + experts_total], 0.0)
    normed_grad = normed_grad[:, :width]
    mixture = scatter_blocks(blocks_of(mixture_all))
    result = (residual + mixture).astype(low)

    chosen_grad = gate_rows * (
        gate_grad_rows - jnp.sum(gate_rows * gate_grad_rows, axis=-1, keepdims=True)
    )
    logit_grad = jnp.where(member, chosen_grad, 0.0).astype(low)
    router_wgrad = product(normed_two.T, logit_grad)
    normed_grad = normed_grad + product(logit_grad, router_full.T)
    gain_two_grad = jnp.sum(normed_grad * residual * scale_two, axis=0)
    scaled_two = normed_grad * gain_second
    resid_grad = (
        grad_out.astype(jnp.float32)
        + scale_two * scaled_two
        - residual * scale_two**3 * jnp.mean(scaled_two * residual, axis=-1, keepdims=True)
    )
    attn_grad = resid_grad.astype(low)
    out_wgrad = product(attended.T, attn_grad)
    attended_grad = product(attn_grad, out_full.T).astype(low)
    grad_heads = attended_grad.reshape(local_rows, KV_HEADS, repeat, HEAD_DIM).transpose(1, 2, 0, 3)
    query_head_grad, key_head_grad, value_head_grad = lax.map(
        partial(head_backward, visible_mask),
        (query_heads, key_heads, value_heads, grad_heads, log_totals),
    )
    key_value_grad = jnp.concatenate(
        [
            key_head_grad.transpose(1, 0, 2).reshape(group_rows, kv_width),
            value_head_grad.transpose(1, 0, 2).reshape(group_rows, kv_width),
        ],
        axis=1,
    )
    key_value_sum = scatter_blocks(from_order(key_value_grad, member_count))
    query_rot_grad = query_head_grad.transpose(2, 0, 1, 3).reshape(local_rows, HEADS, HEAD_DIM)
    key_rot_grad = key_value_sum[:, :kv_width].reshape(local_rows, KV_HEADS, HEAD_DIM)
    qkv_grad = jnp.concatenate(
        [
            unrotate(query_rot_grad, cosine, sine_part).reshape(local_rows, -1).astype(low),
            unrotate(key_rot_grad, cosine, sine_part).reshape(local_rows, -1).astype(low),
            key_value_sum[:, kv_width:].astype(low),
        ],
        axis=1,
    )
    qkv_wgrad = product(normed.T, qkv_grad)
    first_grad = product(qkv_grad, qkv_full.T)
    gain_one_grad = jnp.sum(first_grad * inputs * scale_one, axis=0)
    scaled_one = first_grad * gain_first
    input_grad = (
        resid_grad
        + scale_one * scaled_one
        - inputs * scale_one**3 * jnp.mean(scaled_one * inputs, axis=-1, keepdims=True)
    )
    dense_sum = lax.psum_scatter(
        jnp.concatenate(
            [
                qkv_wgrad.astype(low),
                out_wgrad.astype(low),
                router_wgrad.astype(low),
                gain_one_grad.astype(low)[:, None],
                gain_two_grad.astype(low)[:, None],
                jnp.zeros((width, extra - experts_total - 2), low),
            ],
            axis=1,
        ),
        both,
        scatter_dimension=0,
        tiled=True,
    ).astype(jnp.float32)
    tail = dense_sum[:, qkv_width + width :]
    return (
        result[None],
        input_grad[None],
        tail[:, experts_total],
        dense_sum[:, :query_width],
        dense_sum[:, query_width : query_width + kv_width],
        dense_sum[:, query_width + kv_width : qkv_width],
        dense_sum[:, qkv_width : qkv_width + width],
        tail[:, experts_total + 1],
        tail[:, :experts_total],
        gate_total,
        up_total,
        down_total,
    )


def solution(mesh):
    return jax.shard_map(
        local,
        mesh=mesh,
        in_specs=(
            P("batch", "expert", None),
            P("batch", "expert", None),
            P(("batch", "expert")),
            P(("batch", "expert"), None),
            P(("batch", "expert"), None),
            P(("batch", "expert"), None),
            P(("batch", "expert"), None),
            P(("batch", "expert")),
            P(("batch", "expert"), None),
            P("expert", "batch", None),
            P("expert", "batch", None),
            P("expert", "batch", None),
            P("batch", "expert", None),
            P("batch", "expert"),
        ),
        out_specs=(
            P("batch", "expert", None),
            P("batch", "expert", None),
            P(("batch", "expert")),
            P(("batch", "expert"), None),
            P(("batch", "expert"), None),
            P(("batch", "expert"), None),
            P(("batch", "expert"), None),
            P(("batch", "expert")),
            P(("batch", "expert"), None),
            P("expert", "batch", None),
            P("expert", "batch", None),
            P("expert", "batch", None),
        ),
        check_vma=False,
    )
```

```python
from functools import partial

import jax
import jax.numpy as jnp
from jax import lax
from jax.experimental import pallas as pl
from jax.experimental.pallas import tpu as pltpu
from jax.sharding import PartitionSpec as P

HEADS = 24
KV_HEADS = 8
HEAD_DIM = 64
PROMPT = 512
CLEN = 256


EPS = 1e-06
THETA = 10000.0


def product(left, right):
    return jnp.dot(left, right, preferred_element_type=jnp.float32)


def rms_scale(values):
    return lax.rsqrt(jnp.mean(values * values, axis=-1, keepdims=True) + EPS)


def place_of(row_ids):
    return jnp.where(row_ids < PROMPT, row_ids, PROMPT + (row_ids - PROMPT) % CLEN)


def rotary_tables(rotary_place):
    half_dim = HEAD_DIM // 2
    frequency = THETA ** (-jnp.arange(half_dim, dtype=jnp.float32) / half_dim)
    angles = rotary_place.astype(jnp.float32)[:, None] * frequency[None, :]
    return (jnp.cos(angles)[:, None, :], jnp.sin(angles)[:, None, :])


def rotate(values, cosine, sine_part):
    half_dim = values.shape[-1] // 2
    front_half = values[..., :half_dim]
    back_half = values[..., half_dim:]
    return jnp.concatenate(
        [front_half * cosine - back_half * sine_part, back_half * cosine + front_half * sine_part],
        axis=-1,
    )


def unrotate(gradients, cosine, sine_part):
    half_dim = gradients.shape[-1] // 2
    front_half = gradients[..., :half_dim]
    back_half = gradients[..., half_dim:]
    return jnp.concatenate(
        [front_half * cosine + back_half * sine_part, back_half * cosine - front_half * sine_part],
        axis=-1,
    )


def visible(query_ids, key_ids):
    causal = key_ids[None, :] <= query_ids[:, None]
    same_run = (key_ids[None, :] - PROMPT) // CLEN == (query_ids[:, None] - PROMPT) // CLEN
    return causal & ((key_ids[None, :] < PROMPT) | same_run)


def head_scores(visible_mask, query_block, key_block):
    scores = jnp.einsum("rqd,kd->rqk", query_block, key_block, preferred_element_type=jnp.float32)
    scores = scores * query_block.shape[-1] ** (-0.5)
    return jnp.where(visible_mask[None], scores, -jnp.inf)


def head_forward(visible_mask, operands):
    query_block, key_block, value_block = operands
    scores = head_scores(visible_mask, query_block, key_block)
    row_peak = jnp.max(scores, axis=-1, keepdims=True)
    lifted = jnp.exp(scores - row_peak)
    row_total = jnp.sum(lifted, axis=-1, keepdims=True)
    weights_low = (lifted / row_total).astype(jnp.bfloat16)
    attended = jnp.einsum(
        "rqk,kd->rqd", weights_low, value_block, preferred_element_type=jnp.float32
    )
    return (attended, row_peak + jnp.log(row_total))


def head_backward(visible_mask, operands):
    query_block, key_block, value_block, grad_block, log_total = operands
    scale_factor = query_block.shape[-1] ** (-0.5)
    scores = head_scores(visible_mask, query_block, key_block)
    weights_full = jnp.exp(scores - log_total)
    grad_values = jnp.einsum(
        "rqk,rqd->kd",
        weights_full.astype(jnp.bfloat16),
        grad_block,
        preferred_element_type=jnp.float32,
    )
    grad_weights = jnp.einsum(
        "rqd,kd->rqk", grad_block, value_block, preferred_element_type=jnp.float32
    )
    grad_scores = weights_full * (
        grad_weights - jnp.sum(weights_full * grad_weights, axis=-1, keepdims=True)
    )
    grad_scores = grad_scores.astype(jnp.bfloat16)
    grad_queries = (
        jnp.einsum("rqk,kd->rqd", grad_scores, key_block, preferred_element_type=jnp.float32)
        * scale_factor
    )
    grad_keys = (
        jnp.einsum("rqk,rqd->kd", grad_scores, query_block, preferred_element_type=jnp.float32)
        * scale_factor
    )
    return (grad_queries, grad_keys, grad_values)


def weave_kernel(spots, *refs):
    pieces, out, sems = refs[:-2], refs[-2], refs[-1]
    copies = []
    for p, piece in enumerate(pieces):
        blocks, rows = piece.shape[0], piece.shape[1]
        for k in range(blocks):
            place = pl.multiple_of(spots[p, k] * rows, rows)
            copy = pltpu.make_async_copy(
                piece.at[k], out.at[pl.ds(place, rows)], sems.at[p * blocks + k]
            )
            copy.start()
            copies.append(copy)
    for copy in copies:
        copy.wait()


def weave(pieces, spots):
    blocks, rows, columns = pieces[0].shape
    count = len(pieces) * blocks
    return pl.pallas_call(
        weave_kernel,
        grid_spec=pltpu.PrefetchScalarGridSpec(
            num_scalar_prefetch=1,
            grid=(),
            in_specs=[pl.BlockSpec(memory_space=pl.ANY)] * len(pieces),
            out_specs=pl.BlockSpec(memory_space=pl.ANY),
            scratch_shapes=[pltpu.SemaphoreType.DMA((count,))],
        ),
        out_shape=jax.ShapeDtypeStruct((count * rows, columns), pieces[0].dtype),
        cost_estimate=pl.CostEstimate(
            flops=0, bytes_accessed=4 * count * rows * columns, transcendentals=0
        ),
        name="weave",
    )(spots, *pieces)


def dot_plain(left, right):
    return lax.dot_general(left, right, (((1,), (0,)), ((), ())), preferred_element_type=jnp.float32)


def dot_right(left, right):
    return lax.dot_general(left, right, (((1,), (1,)), ((), ())), preferred_element_type=jnp.float32)


def dot_left(left, right):
    return lax.dot_general(left, right, (((0,), (0,)), ((), ())), preferred_element_type=jnp.float32)


def expert_kernel(
    carried,
    row_tile,
    gates,
    rows,
    grads,
    packed,
    *refs,
):
    if carried:
        mix_in, turn_in = refs[:2]
        refs = refs[2:]
    (
        packed_grad,
        mix,
        turn,
        gate_grads,
        gate_w,
        up_w,
        down_w,
        gate_g,
        up_g,
        down_g,
        weighted,
        gate_side,
        up_side,
        load_sems,
        save_sems,
        carry_sems,
    ) = refs
    count = packed.shape[1]
    hidden_width = gate_w.shape[-1]
    width = rows.shape[1]
    total_rows = rows.shape[0]
    low = jnp.bfloat16

    def loads(e):
        slot = e % 2
        found = []
        for side, target in ((0, gate_w), (1, up_w)):
            for j in range(3):
                found.append(
                    pltpu.make_async_copy(
                        packed.at[:, e, side, :, pl.ds(j * hidden_width, hidden_width)],
                        target.at[slot, :, j],
                        load_sems.at[slot, 3 * side + j],
                    )
                )
        found.append(
            pltpu.make_async_copy(packed.at[:, e, 2], down_w.at[slot], load_sems.at[slot, 6])
        )
        return found

    def saves(e):
        slot = e % 2
        found = []
        for side, source in ((0, gate_g), (1, up_g)):
            for j in range(3):
                found.append(
                    pltpu.make_async_copy(
                        source.at[slot, :, j],
                        packed_grad.at[:, e, side, :, pl.ds(j * hidden_width, hidden_width)],
                        save_sems.at[slot, 3 * side + j],
                    )
                )
        found.append(
            pltpu.make_async_copy(down_g.at[slot], packed_grad.at[:, e, 2], save_sems.at[slot, 6])
        )
        return found

    for copy in loads(0):
        copy.start()
    if carried:
        carries = [
            pltpu.make_async_copy(mix_in, mix, carry_sems.at[0]),
            pltpu.make_async_copy(turn_in, turn, carry_sems.at[1]),
        ]
        for copy in carries:
            copy.start()
    gate_grads[...] = jnp.zeros_like(gate_grads)
    for e in range(count):
        slot = e % 2
        if e + 1 < count:
            for copy in loads(e + 1):
                copy.start()
        for copy in loads(e):
            copy.wait()
        if e == 0 and carried:
            for copy in carries:
                copy.wait()

        @pl.loop(0, total_rows // row_tile)
        def _(tile):
            span = pl.ds(pl.multiple_of(tile * row_tile, row_tile), row_tile)
            gate_full = gate_w[slot].reshape(width, hidden_width)
            up_full = up_w[slot].reshape(width, hidden_width)
            down_full = down_w[slot].reshape(hidden_width, width)
            here = rows[span, :]
            slope = dot_right(grads[span, :], down_full)
            gate_pre = dot_plain(here, gate_full)
            up_pre = dot_plain(here, up_full)
            gate_column = gates[span, e : e + 1]
            sigmoid_gate = jax.nn.sigmoid(gate_pre)
            activated = gate_pre * sigmoid_gate
            hidden = (activated * up_pre).astype(low).astype(jnp.float32)
            lane = lax.broadcasted_iota(jnp.int32, (row_tile, gate_grads.shape[1]), 1)
            share = jnp.sum(hidden * slope, axis=1, keepdims=True)
            gate_grads[span, :] = jnp.where(lane == e, share, gate_grads[span, :])
            part_weighted = (hidden * gate_column).astype(low)
            hidden_grad = slope * gate_column
            part_gate = (
                hidden_grad * up_pre * (sigmoid_gate + activated * (1.0 - sigmoid_gate))
            ).astype(low)
            part_up = (hidden_grad * activated).astype(low)
            weighted[span, :] = part_weighted
            gate_side[span, :] = part_gate
            up_side[span, :] = part_up
            mix_part = dot_plain(part_weighted, down_full)
            turn_part = dot_right(part_gate, gate_full) + dot_right(part_up, up_full)
            if e == 0 and not carried:
                mix[span, :] = mix_part
                turn[span, :] = turn_part
            else:
                mix[span, :] += mix_part
                turn[span, :] += turn_part

        if e >= 2:
            for copy in saves(e - 2):
                copy.wait()
        down_g[slot] = dot_left(weighted[...], grads[...]).astype(low).reshape(down_g.shape[1:])
        gate_g[slot] = dot_left(rows[...], gate_side[...]).astype(low).reshape(gate_g.shape[1:])
        up_g[slot] = dot_left(rows[...], up_side[...]).astype(low).reshape(up_g.shape[1:])
        for copy in saves(e):
            copy.start()
    for e in range(max(0, count - 2), count):
        for copy in saves(e):
            copy.wait()


def expert_pass(gates, rows, grads, packed, carry=None):
    blocks, count, _, part, width = packed.shape
    hidden_width = blocks * part
    total_rows = rows.shape[0]
    low = jnp.bfloat16
    anywhere = pl.BlockSpec(memory_space=pl.ANY)
    inside = pl.BlockSpec(memory_space=pltpu.VMEM)
    carried = carry is not None
    flops = 18 * total_rows * count * hidden_width * width
    return pl.pallas_call(
        partial(expert_kernel, carried, min(512, total_rows)),
        in_specs=[inside, inside, inside, anywhere] + [anywhere] * (2 if carried else 0),
        out_specs=[anywhere, inside, inside, inside],
        out_shape=[
            jax.ShapeDtypeStruct(packed.shape, low),
            jax.ShapeDtypeStruct((total_rows, width), jnp.float32),
            jax.ShapeDtypeStruct((total_rows, width), jnp.float32),
            jax.ShapeDtypeStruct((total_rows, 128), jnp.float32),
        ],
        scratch_shapes=[
            pltpu.VMEM((2, blocks, 3, part, hidden_width), low),
            pltpu.VMEM((2, blocks, 3, part, hidden_width), low),
            pltpu.VMEM((2, blocks, part, width), low),
            pltpu.VMEM((2, blocks, 3, part, hidden_width), low),
            pltpu.VMEM((2, blocks, 3, part, hidden_width), low),
            pltpu.VMEM((2, blocks, part, width), low),
            pltpu.VMEM((total_rows, hidden_width), low),
            pltpu.VMEM((total_rows, hidden_width), low),
            pltpu.VMEM((total_rows, hidden_width), low),
            pltpu.SemaphoreType.DMA((2, 7)),
            pltpu.SemaphoreType.DMA((2, 7)),
            pltpu.SemaphoreType.DMA((2,)),
        ],
        compiler_params=pltpu.CompilerParams(vmem_limit_bytes=60 * 1024 * 1024),
        cost_estimate=pl.CostEstimate(
            flops=flops,
            bytes_accessed=4 * packed.size + 12 * rows.size,
            transcendentals=total_rows * count * hidden_width,
        ),
        name="experts",
    )(gates, rows, grads, packed, *(carry or ()))


def pair_moves(size, flip):
    return [(i, i ^ flip) for i in range(size)]


def gather_blocks(rows):
    size = lax.axis_size("expert")
    if size != 4:
        stacked = lax.all_gather(rows, "expert", axis=0)
        own = lax.axis_index("expert")
        return [
            lax.dynamic_index_in_dim(stacked, own ^ r, axis=0, keepdims=False) for r in range(size)
        ]
    across, along = pair_moves(size, 1), pair_moves(size, 2)
    half = rows.shape[0] // 2
    first = lax.ppermute(rows, "expert", across)
    second = lax.ppermute(rows, "expert", along)
    top = lax.ppermute(second[:half], "expert", across)
    bottom = lax.ppermute(first[half:], "expert", along)
    return [rows, first, second, jnp.concatenate([top, bottom], axis=0)]


def scatter_blocks(parts):
    size = lax.axis_size("expert")
    low = jnp.bfloat16
    if size != 4:
        own = lax.axis_index("expert")
        order = jnp.arange(size, dtype=jnp.int32) ^ own
        stacked = jnp.take(jnp.stack(parts), order, axis=0).astype(low)
        return lax.psum_scatter(stacked, "expert", scatter_dimension=0).astype(jnp.float32)
    across, along = pair_moves(size, 1), pair_moves(size, 2)
    half = parts[0].shape[0] // 2
    far = parts[3].astype(low)
    top = lax.ppermute(far[:half], "expert", across).astype(jnp.float32)
    bottom = lax.ppermute(far[half:], "expert", along).astype(jnp.float32)
    for_second = jnp.concatenate([parts[2][:half] + top, parts[2][half:]], axis=0)
    for_first = jnp.concatenate([parts[1][:half], parts[1][half:] + bottom], axis=0)
    from_first = lax.ppermute(for_first.astype(low), "expert", across)
    from_second = lax.ppermute(for_second.astype(low), "expert", along)
    return parts[0] + from_first.astype(jnp.float32) + from_second.astype(jnp.float32)


def in_order(blocks):
    own = lax.axis_index("expert")
    return jnp.concatenate(
        [lax.select_n(own ^ k, *blocks) if len(blocks) > 1 else blocks[0] for k in range(len(blocks))],
        axis=0,
    )


def from_order(values, count):
    own = lax.axis_index("expert")
    rows = values.shape[0] // count
    return [
        lax.dynamic_slice_in_dim(values, (own ^ r) * rows, rows, axis=0) for r in range(count)
    ]


def cube():
    return lax.axis_size("batch") == 8 and lax.axis_size("expert") == 4


def shift_moves(step):
    return [(2 * z + c, 2 * ((z + step) % 4) + c) for z in range(4) for c in range(2)]


def gather_dense(rows):
    if not cube():
        return lax.all_gather(rows, ("batch", "expert"), axis=0, tiled=True)
    place = lax.axis_index("batch")
    level, core = place // 2, place % 2
    member = lax.axis_index("expert")
    line = [rows] + [lax.ppermute(rows, "batch", shift_moves(r)) for r in range(1, 4)]
    mine = gather_blocks(jnp.stack(line))
    other = [lax.ppermute(block, "batch", pair_moves(8, 1)) for block in mine]
    levels = [(level + 4 - r) % 4 for r in range(4)]
    spots = [
        [(levels[k] * 2 + (core ^ c)) * 4 + (member ^ r) for k in range(4)]
        for c in range(2)
        for r in range(4)
    ]
    return weave(mine + other, jnp.array(spots, jnp.int32))


def scatter_dense(values):
    low = jnp.bfloat16
    if not cube():
        total = lax.psum_scatter(values, ("batch", "expert"), scatter_dimension=0, tiled=True)
        return total.astype(jnp.float32)
    place = lax.axis_index("batch")
    level, core = place // 2, place % 2
    member = lax.axis_index("expert")
    rows = values.shape[0] // 32
    cut = values.reshape(4, 2, 4, rows, values.shape[1])

    def side(index):
        return lax.dynamic_index_in_dim(cut, index, axis=1, keepdims=False)

    received = lax.ppermute(side(1 - core), "batch", pair_moves(8, 1))
    chip = side(core).astype(jnp.float32) + received.astype(jnp.float32)
    parts = [
        lax.dynamic_index_in_dim(chip, member ^ r, axis=1, keepdims=False) for r in range(4)
    ]
    plane = scatter_blocks(parts)
    total = lax.dynamic_index_in_dim(plane, level, axis=0, keepdims=False)
    for r in range(1, 4):
        sent = lax.dynamic_index_in_dim(plane, (level + r) % 4, axis=0, keepdims=False)
        total += lax.ppermute(sent.astype(low), "batch", shift_moves(r)).astype(jnp.float32)
    return total


def pack_sides(gate, up, down):
    def fold(values):
        count, depth, width = values.shape
        return values.reshape(count, 3, depth // 3, width).transpose(0, 2, 1, 3).reshape(down.shape)

    return jnp.stack([fold(gate), fold(up), down], axis=1)


def unpack_side(values):
    count, part, width = values.shape
    return values.reshape(count, part, 3, width // 3).transpose(0, 2, 1, 3).reshape(
        count, 3 * part, width // 3
    )


def local(
    tokens,
    cotangent,
    attn_gain,
    query_weight,
    key_weight,
    value_weight,
    out_weight,
    ffn_gain,
    router_weight,
    gate_weight,
    up_weight,
    down_weight,
    routes,
    ranking,
):
    low = jnp.bfloat16
    query_width = HEADS * HEAD_DIM
    kv_width = KV_HEADS * HEAD_DIM
    qkv_width = query_width + 2 * kv_width
    width = tokens.shape[2]
    experts_total = router_weight.shape[1]
    extra = -(-(experts_total + 2) // 128) * 128
    local_experts = gate_weight.shape[0]
    member_count = lax.axis_size("expert")
    member_id = lax.axis_index("expert")
    local_rows = tokens.shape[1]
    group_rows = local_rows * member_count
    chunks = (0, 3, local_experts)
    packed_all = [
        lax.all_gather(
            pack_sides(gate_weight[a:b], up_weight[a:b], down_weight[a:b]), "batch", axis=0
        )
        for a, b in zip(chunks[:-1], chunks[1:])
    ]
    dense = gather_dense(
        jnp.concatenate(
            [
                query_weight,
                key_weight,
                value_weight,
                router_weight,
                attn_gain[:, None],
                ffn_gain[:, None],
                jnp.zeros((query_weight.shape[0], extra - experts_total - 2), low),
            ],
            axis=1,
        )
    )
    out_full = gather_dense(out_weight)
    qkv_full = dense[:, :qkv_width]
    small = dense[:, qkv_width:]
    router_full = small[:, :experts_total]
    gain_first = small[:, experts_total].astype(jnp.float32)
    gain_second = small[:, experts_total + 1].astype(jnp.float32)

    inputs = tokens[0].astype(jnp.float32)
    row_ids = member_id * local_rows + jnp.arange(local_rows, dtype=jnp.int32)
    group_ids = jnp.arange(group_rows, dtype=jnp.int32)
    cosine, sine_part = rotary_tables(place_of(row_ids))
    repeat = HEADS // KV_HEADS
    grad_out = cotangent[0]
    grad_blocks = gather_blocks(grad_out)

    scale_one = rms_scale(inputs)
    normed = (inputs * scale_one * gain_first).astype(low)
    qkv = product(normed, qkv_full)
    query_pre = qkv[:, :query_width].reshape(local_rows, HEADS, HEAD_DIM)
    queries = rotate(query_pre, cosine, sine_part).astype(low)
    key_pre = qkv[:, query_width : query_width + kv_width].reshape(local_rows, KV_HEADS, HEAD_DIM)
    key_rows = rotate(key_pre, cosine, sine_part).astype(low).reshape(local_rows, kv_width)
    value_rows = qkv[:, query_width + kv_width :].astype(low)

    route_rows = routes[0]
    rank_rows = ranking[0]
    picked = route_rows[:, :, None] == jnp.arange(experts_total, dtype=jnp.int32)[None, None, :]
    member = jnp.any(picked, axis=1)
    shared = jnp.concatenate(
        [
            key_rows,
            value_rows,
            member.astype(low),
            (rank_rows // 32).astype(low)[:, None],
            (rank_rows % 32).astype(low)[:, None],
            jnp.zeros((local_rows, extra - experts_total - 2), low),
        ],
        axis=1,
    )
    shared_all = in_order(gather_blocks(shared))
    key_all = shared_all[:, :kv_width]
    value_all = shared_all[:, kv_width : 2 * kv_width]
    member_all = shared_all[:, 2 * kv_width : 2 * kv_width + experts_total]
    rank_parts = shared_all[:, 2 * kv_width + experts_total :][:, :2].astype(jnp.float32)
    rank_all = (rank_parts[:, 0] * 32 + rank_parts[:, 1]).astype(jnp.int32)
    earlier = (rank_all[None, :] < rank_rows[:, None]).astype(low)
    before = product(earlier, member_all)
    capacity = 5 * group_rows * route_rows.shape[1] // (4 * experts_total)
    kept = member & (before < capacity)

    query_heads = queries.reshape(local_rows, KV_HEADS, repeat, HEAD_DIM).transpose(1, 2, 0, 3)
    key_heads = key_all.reshape(group_rows, KV_HEADS, HEAD_DIM).transpose(1, 0, 2)
    value_heads = value_all.reshape(group_rows, KV_HEADS, HEAD_DIM).transpose(1, 0, 2)
    visible_mask = visible(row_ids, group_ids)
    head_out, log_totals = lax.map(
        partial(head_forward, visible_mask), (query_heads, key_heads, value_heads)
    )
    attended = head_out.transpose(2, 0, 1, 3).reshape(local_rows, query_width).astype(low)
    residual = inputs + product(attended, out_full)
    scale_two = rms_scale(residual)
    normed_two = (residual * scale_two * gain_second).astype(low)
    logits = product(normed_two, router_full)
    chosen = jnp.sum(jnp.where(picked, logits[:, None, :], 0.0), axis=-1)
    gate_probs = jax.nn.softmax(chosen, axis=-1)
    gate_rows = jnp.sum(jnp.where(picked, gate_probs[:, :, None], 0.0), axis=1)
    sent = jnp.concatenate(
        [
            normed_two,
            jnp.where(kept, gate_rows, 0.0).astype(low),
            jnp.zeros((local_rows, extra - experts_total), low),
        ],
        axis=1,
    )
    sent_all = jnp.concatenate(gather_blocks(sent), axis=0)
    rows_all = sent_all[:, :width]
    own_gates = lax.dynamic_slice_in_dim(
        sent_all[:, width : width + experts_total], member_id * local_experts, local_experts, axis=1
    ).astype(jnp.float32)
    grad_all = jnp.concatenate(grad_blocks, axis=0)

    carry, gate_parts, totals = None, [], []
    for packed, a, b in zip(packed_all, chunks[:-1], chunks[1:]):
        chunk_gates = jnp.pad(own_gates[:, a:b], ((0, 0), (0, 128 - (b - a))))
        packed_grad, mixture_all, row_grad, gate_part = expert_pass(
            chunk_gates, rows_all, grad_all, packed, carry
        )
        carry = (mixture_all, row_grad)
        gate_parts.append(gate_part[:, : b - a])
        totals.append(lax.psum_scatter(packed_grad, "batch", scatter_dimension=0))
    weight_total = jnp.concatenate(totals, axis=0).astype(jnp.float32)
    gate_total = unpack_side(weight_total[:, 0])
    up_total = unpack_side(weight_total[:, 1])
    down_total = weight_total[:, 2]

    gate_grads = lax.dynamic_update_slice_in_dim(
        jnp.zeros((group_rows, extra), jnp.float32),
        jnp.concatenate(gate_parts, axis=1),
        member_id * local_experts,
        axis=1,
    )

    def blocks_of(values):
        return [values[r * local_rows : (r + 1) * local_rows] for r in range(member_count)]

    normed_grad = scatter_blocks(blocks_of(jnp.concatenate([row_grad, gate_grads], axis=1)))
    gate_grad_rows = jnp.where(kept, normed_grad[:, width : width + experts_total], 0.0)
    normed_grad = normed_grad[:, :width]
    mixture = scatter_blocks(blocks_of(mixture_all))
    result = (residual + mixture).astype(low)

    chosen_grad = gate_rows * (
        gate_grad_rows - jnp.sum(gate_rows * gate_grad_rows, axis=-1, keepdims=True)
    )
    logit_grad = jnp.where(member, chosen_grad, 0.0).astype(low)
    router_wgrad = product(normed_two.T, logit_grad)
    normed_grad = normed_grad + product(logit_grad, router_full.T)
    gain_two_grad = jnp.sum(normed_grad * residual * scale_two, axis=0)
    scaled_two = normed_grad * gain_second
    resid_grad = (
        grad_out.astype(jnp.float32)
        + scale_two * scaled_two
        - residual * scale_two**3 * jnp.mean(scaled_two * residual, axis=-1, keepdims=True)
    )
    attn_grad = resid_grad.astype(low)
    out_wgrad = product(attended.T, attn_grad)
    out_sum = scatter_dense(
        jnp.concatenate(
            [
                out_wgrad.astype(low),
                router_wgrad.astype(low),
                gain_two_grad.astype(low)[:, None],
                jnp.zeros((width, extra - experts_total - 1), low),
            ],
            axis=1,
        )
    )
    attended_grad = product(attn_grad, out_full.T).astype(low)
    grad_heads = attended_grad.reshape(local_rows, KV_HEADS, repeat, HEAD_DIM).transpose(1, 2, 0, 3)
    query_head_grad, key_head_grad, value_head_grad = lax.map(
        partial(head_backward, visible_mask),
        (query_heads, key_heads, value_heads, grad_heads, log_totals),
    )
    key_value_grad = jnp.concatenate(
        [
            key_head_grad.transpose(1, 0, 2).reshape(group_rows, kv_width),
            value_head_grad.transpose(1, 0, 2).reshape(group_rows, kv_width),
        ],
        axis=1,
    )
    key_value_sum = scatter_blocks(from_order(key_value_grad, member_count))
    query_rot_grad = query_head_grad.transpose(2, 0, 1, 3).reshape(local_rows, HEADS, HEAD_DIM)
    key_rot_grad = key_value_sum[:, :kv_width].reshape(local_rows, KV_HEADS, HEAD_DIM)
    qkv_grad = jnp.concatenate(
        [
            unrotate(query_rot_grad, cosine, sine_part).reshape(local_rows, -1).astype(low),
            unrotate(key_rot_grad, cosine, sine_part).reshape(local_rows, -1).astype(low),
            key_value_sum[:, kv_width:].astype(low),
        ],
        axis=1,
    )
    qkv_wgrad = product(normed.T, qkv_grad)
    first_grad = product(qkv_grad, qkv_full.T)
    gain_one_grad = jnp.sum(first_grad * inputs * scale_one, axis=0)
    scaled_one = first_grad * gain_first
    input_grad = (
        resid_grad
        + scale_one * scaled_one
        - inputs * scale_one**3 * jnp.mean(scaled_one * inputs, axis=-1, keepdims=True)
    )
    qkv_sum = scatter_dense(
        jnp.concatenate(
            [
                qkv_wgrad.astype(low),
                gain_one_grad.astype(low)[:, None],
                jnp.zeros((width, 127), low),
            ],
            axis=1,
        )
    )
    return (
        result[None],
        input_grad[None],
        qkv_sum[:, qkv_width],
        qkv_sum[:, :query_width],
        qkv_sum[:, query_width : query_width + kv_width],
        qkv_sum[:, query_width + kv_width : qkv_width],
        out_sum[:, :width],
        out_sum[:, width + experts_total],
        out_sum[:, width : width + experts_total],
        gate_total,
        up_total,
        down_total,
    )


def solution(mesh):
    return jax.shard_map(
        local,
        mesh=mesh,
        in_specs=(
            P("batch", "expert", None),
            P("batch", "expert", None),
            P(("batch", "expert")),
            P(("batch", "expert"), None),
            P(("batch", "expert"), None),
            P(("batch", "expert"), None),
            P(("batch", "expert"), None),
            P(("batch", "expert")),
            P(("batch", "expert"), None),
            P("expert", "batch", None),
            P("expert", "batch", None),
            P("expert", "batch", None),
            P("batch", "expert", None),
            P("batch", "expert"),
        ),
        out_specs=(
            P("batch", "expert", None),
            P("batch", "expert", None),
            P(("batch", "expert")),
            P(("batch", "expert"), None),
            P(("batch", "expert"), None),
            P(("batch", "expert"), None),
            P(("batch", "expert"), None),
            P(("batch", "expert")),
            P(("batch", "expert"), None),
            P("expert", "batch", None),
            P("expert", "batch", None),
            P("expert", "batch", None),
        ),
        check_vma=False,
    )
```

```python
from functools import partial

import jax
import jax.numpy as jnp
from jax import lax
from jax.experimental import pallas as pl
from jax.experimental.pallas import tpu as pltpu
from jax.sharding import PartitionSpec as P

HEADS = 24
KV_HEADS = 8
HEAD_DIM = 64
PROMPT = 512
CLEN = 256


EPS = 1e-06
THETA = 10000.0


def product(left, right):
    return jnp.dot(left, right, preferred_element_type=jnp.float32)


def place_of(row_ids):
    return jnp.where(row_ids < PROMPT, row_ids, PROMPT + (row_ids - PROMPT) % CLEN)


def visible(query_ids, key_ids):
    causal = key_ids[None, :] <= query_ids[:, None]
    same_run = (key_ids[None, :] - PROMPT) // CLEN == (query_ids[:, None] - PROMPT) // CLEN
    return causal & ((key_ids[None, :] < PROMPT) | same_run)


def dot_plain(left, right):
    return lax.dot_general(left, right, (((1,), (0,)), ((), ())), preferred_element_type=jnp.float32)


def dot_right(left, right):
    return lax.dot_general(left, right, (((1,), (1,)), ((), ())), preferred_element_type=jnp.float32)


def dot_left(left, right):
    return lax.dot_general(left, right, (((0,), (0,)), ((), ())), preferred_element_type=jnp.float32)


ANYWHERE = pl.BlockSpec(memory_space=pl.ANY)
INSIDE = pl.BlockSpec(memory_space=pltpu.VMEM)
SCALARS = pl.BlockSpec(memory_space=pltpu.SMEM)
VMEM_BYTES = 60 * 1024 * 1024


def cost(flops, *arrays):
    return pl.CostEstimate(
        flops=int(flops),
        bytes_accessed=int(sum(a.size * a.dtype.itemsize for a in arrays)),
        transcendentals=0,
    )


def weight_copies(spots, pieces, target, sems):
    copies = []
    for p, piece in enumerate(pieces):
        blocks, rows = piece.shape[0], piece.shape[1]
        for k in range(blocks):
            place = pl.multiple_of(spots[p, k] * rows, rows)
            copies.append(
                pltpu.make_async_copy(
                    piece.at[k], target.at[pl.ds(place, rows)], sems.at[p * blocks + k]
                )
            )
    return copies


def block_copies(blocks, target, sems, first, columns=None):
    copies = []
    start = 0
    for i, block in enumerate(blocks):
        rows = block.shape[0]
        source = block if columns is None else block.at[:, columns]
        copies.append(
            pltpu.make_async_copy(source, target.at[pl.ds(start, rows)], sems.at[first + i])
        )
        start += rows
    return copies


def swap_halves(values):
    half = HEAD_DIM // 2
    lane = lax.broadcasted_iota(jnp.int32, values.shape, 1)
    return jnp.where(
        lane % HEAD_DIM < half,
        pltpu.roll(values, 2 * HEAD_DIM - half, 1),
        pltpu.roll(values, half, 1),
    )


def mean_square_scale(values):
    return lax.rsqrt(jnp.mean(values * values, axis=-1, keepdims=True) + EPS)


def enter_kernel(count, gain_at, spots, tokens, cosine, sine, *refs):
    pieces = refs[:count]
    normed, query, keyval, small, weight, sems = refs[count:]
    low = jnp.bfloat16
    copies = weight_copies(spots, pieces, weight, sems)
    for copy in copies:
        copy.start()
    inputs = tokens[...].astype(jnp.float32)
    scaled = inputs * mean_square_scale(inputs)
    for copy in copies:
        copy.wait()
    query_width = query.shape[1]
    kv_width = keyval.shape[1] // 2
    qkv_width = query_width + 2 * kv_width
    turned = weight[:, qkv_width:].astype(jnp.float32).T
    small[...] = turned
    rows = (scaled * turned[gain_at : gain_at + 1]).astype(low)
    normed[...] = rows
    pair = 2 * HEAD_DIM
    scale = HEAD_DIM**-0.5
    for start in range(0, query_width + kv_width, 512):
        product_part = dot_plain(rows, weight[:, start : start + 512])
        for offset in range(0, 512, pair):
            part = product_part[:, offset : offset + pair]
            part = part * cosine[...] + swap_halves(part) * sine[...]
            at = start + offset
            if at < query_width:
                query[:, at : at + pair] = (part * scale).astype(low)
            else:
                keyval[:, at - query_width : at - query_width + pair] = part.astype(low)
    keyval[:, kv_width:] = dot_plain(
        rows, weight[:, query_width + kv_width : qkv_width]
    ).astype(low)


def enter(tokens, cosine, sine, pieces, spots, gain_at, query_width, kv_width):
    rows, width = tokens.shape
    columns = pieces[0].shape[2]
    low = jnp.bfloat16
    return pl.pallas_call(
        partial(enter_kernel, len(pieces), gain_at),
        in_specs=[SCALARS, INSIDE, INSIDE, INSIDE] + [ANYWHERE] * len(pieces),
        out_specs=[INSIDE] * 4,
        out_shape=[
            jax.ShapeDtypeStruct((rows, width), low),
            jax.ShapeDtypeStruct((rows, query_width), low),
            jax.ShapeDtypeStruct((rows, 2 * kv_width), low),
            jax.ShapeDtypeStruct((columns - query_width - 2 * kv_width, width), jnp.float32),
        ],
        scratch_shapes=[
            pltpu.VMEM((width, columns), low),
            pltpu.SemaphoreType.DMA((len(pieces) * pieces[0].shape[0],)),
        ],
        compiler_params=pltpu.CompilerParams(vmem_limit_bytes=VMEM_BYTES),
        cost_estimate=cost(2 * rows * width * columns, *pieces),
        name="enter",
    )(spots, tokens, cosine, sine, *pieces)


def both_places(values):
    wide = values.astype(jnp.float32)
    low_lane = lax.broadcasted_iota(jnp.int32, values.shape, 1) < HEAD_DIM
    moved = pltpu.roll(wide, HEAD_DIM, 1)
    kind = values.dtype
    return [
        [jnp.where(low_lane, wide, 0.0).astype(kind), jnp.where(low_lane, 0.0, moved).astype(kind)],
        [jnp.where(low_lane, moved, 0.0).astype(kind), jnp.where(low_lane, 0.0, wide).astype(kind)],
    ]


def attend_kernel(
    count, query, keyval, bias, tokens, small, member, kept, gain_at, spots, *refs
):
    pieces = refs[:count]
    attended, log_totals, residual, sent, gate_rows, weight, sems = refs[count:]
    low = jnp.bfloat16
    rows = query.shape[0]
    width = tokens.shape[1]
    kv_width = keyval.shape[1] // 2
    pair_lanes = 2 * HEAD_DIM
    repeat = HEADS // KV_HEADS
    copies = weight_copies(spots, pieces, weight, sems)
    for copy in copies:
        copy.start()
    log_totals[...] = jnp.zeros_like(log_totals)
    lane = lax.broadcasted_iota(jnp.int32, log_totals.shape, 1)

    @pl.loop(0, KV_HEADS // 2)
    def _(pair):
        at = pl.ds(pl.multiple_of(pair * pair_lanes, pair_lanes), pair_lanes)
        keys = both_places(keyval[:, at])
        at = pl.ds(pl.multiple_of(kv_width + pair * pair_lanes, pair_lanes), pair_lanes)
        values = both_places(keyval[:, at])
        for i in range(repeat):
            at = pl.ds(pl.multiple_of((pair * repeat + i) * pair_lanes, pair_lanes), pair_lanes)
            queries = query[:, at]
            total = jnp.zeros((rows, pair_lanes), jnp.float32)
            for a in range(2):
                head = 2 * i + a
                scores = dot_right(queries, keys[head // repeat][a]) + bias[...]
                peak = jnp.max(scores, axis=-1, keepdims=True)
                lifted = jnp.exp(scores - peak)
                row_total = jnp.sum(lifted, axis=-1, keepdims=True)
                weights_low = (lifted * (1.0 / row_total)).astype(low)
                total += dot_plain(weights_low, values[head // repeat][a])
                log_totals[...] = jnp.where(
                    lane == pair * (2 * repeat) + head, peak + jnp.log(row_total), log_totals[...]
                )
            attended[:, at] = total.astype(low)

    for copy in copies:
        copy.wait()
    hidden = tokens[...].astype(jnp.float32) + dot_plain(attended[...], weight[...])
    residual[...] = hidden
    gain = small[gain_at : gain_at + 1, :]
    normed = (hidden * mean_square_scale(hidden) * gain).astype(low)
    logits = dot_right(normed, small[...].astype(low))
    chosen = member[...] > 0.0
    logits = jnp.where(chosen, logits, -1e30)
    lifted = jnp.where(chosen, jnp.exp(logits - jnp.max(logits, axis=-1, keepdims=True)), 0.0)
    gates = lifted / jnp.sum(lifted, axis=-1, keepdims=True)
    gate_rows[...] = gates
    sent[:, :width] = normed
    sent[:, width:] = (gates * kept[...]).astype(low)


def attend(query, keyval, bias, tokens, small, member, kept, gain_at, pieces, spots):
    rows, width = tokens.shape
    query_width = query.shape[1]
    lanes = small.shape[0]
    low = jnp.bfloat16

    def kernel(*refs):
        attend_kernel(len(pieces), *refs[:7], gain_at, *refs[7:])

    return pl.pallas_call(
        kernel,
        in_specs=[INSIDE] * 7 + [SCALARS] + [ANYWHERE] * len(pieces),
        out_specs=[INSIDE] * 5,
        out_shape=[
            jax.ShapeDtypeStruct((rows, query_width), low),
            jax.ShapeDtypeStruct((rows, 128), jnp.float32),
            jax.ShapeDtypeStruct((rows, width), jnp.float32),
            jax.ShapeDtypeStruct((rows, width + lanes), low),
            jax.ShapeDtypeStruct((rows, lanes), jnp.float32),
        ],
        scratch_shapes=[
            pltpu.VMEM((query_width, width), low),
            pltpu.SemaphoreType.DMA((len(pieces) * pieces[0].shape[0],)),
        ],
        compiler_params=pltpu.CompilerParams(vmem_limit_bytes=VMEM_BYTES),
        cost_estimate=cost(2 * rows * width * width + 8 * rows * query_width * bias.shape[1], *pieces),
        name="attend",
    )(query, keyval, bias, tokens, small, member, kept, spots, *pieces)


def sorted_copies(place, source, others, own, sems):
    core, member = place[0], place[1]
    copies = []
    for r, (other, mine) in enumerate(zip(others, own)):
        copies.append(
            pltpu.make_async_copy(source.at[:, 1 - core, member ^ r], other, sems.at[2 * r])
        )
        copies.append(
            pltpu.make_async_copy(source.at[:, core, member ^ r], mine, sems.at[2 * r + 1])
        )
    return copies


def grad_shapes(cut, rows, columns):
    low = jnp.bfloat16
    if cut:
        block = rows // 32
        return (
            [jax.ShapeDtypeStruct((4, block, columns), low)] * 8,
            pltpu.VMEM((4, 2, 4, block, columns), low),
        )
    return (
        [jax.ShapeDtypeStruct((1, 1, 1, rows, columns), low)],
        pltpu.VMEM((1, 1, 1, rows, columns), low),
    )


def grad_copies(cut, place, source, outs, sems):
    if cut:
        return sorted_copies(place, source, outs[:4], outs[4:], sems)
    return [pltpu.make_async_copy(source, outs[0], sems.at[0])]


def turn_kernel(
    count,
    cut,
    gain_at,
    place,
    spots,
    normed_grad,
    residual,
    grad_out,
    small,
    gate_rows,
    member,
    kept,
    normed,
    attended,
    query,
    keyval,
    bias,
    log_totals,
    cosine,
    sine,
    *refs,
):
    pieces = refs[:count]
    refs = refs[count:]
    outs = refs[: (8 if cut else 1)]
    refs = refs[len(outs) :]
    resid_grad, query_grad, keyval_grad, weight, weight_grad, head_grad, totals, sems, out_sems = refs
    low = jnp.bfloat16
    rows, width = residual.shape
    lanes = gate_rows.shape[1]
    kv_width = keyval.shape[1] // 2
    pair_lanes = 2 * HEAD_DIM
    repeat = HEADS // KV_HEADS
    copies = weight_copies(spots, pieces, weight, sems)
    for copy in copies:
        copy.start()
    lane = lax.broadcasted_iota(jnp.int32, (rows, lanes), 1)
    gates = gate_rows[...]
    gate_grads = normed_grad[:, width:] * kept[...]
    chosen_grad = gates * (gate_grads - jnp.sum(gates * gate_grads, axis=-1, keepdims=True))
    logit_grad = (chosen_grad * member[...]).astype(low)
    hidden = residual[...]
    scale = mean_square_scale(hidden)
    row_grad = normed_grad[:, :width] + dot_plain(logit_grad, small[...].astype(low))
    gain = small[gain_at : gain_at + 1, :]
    scaled = row_grad * gain
    total_grad = (
        grad_out[...].astype(jnp.float32)
        + scale * scaled
        - hidden * (scale * scale * scale) * jnp.mean(scaled * hidden, axis=-1, keepdims=True)
    )
    resid_grad[...] = total_grad
    attn_grad = total_grad.astype(low)
    shape = weight_grad.shape[:-1]
    gain_grad = (row_grad * hidden * scale).astype(low)
    picks = jnp.where(lane == gain_at, 1.0, 0.0).astype(low)
    weight_grad[..., width:] = (
        (dot_left(normed[...][:, :width], logit_grad) + dot_left(gain_grad, picks))
        .astype(low)
        .reshape(shape + (lanes,))
    )
    for start in range(0, width, 512):
        weight_grad[..., start : start + 512] = (
            dot_left(attended[...], attn_grad[:, start : start + 512])
            .astype(low)
            .reshape(shape + (512,))
        )
    out_copies = grad_copies(cut, place, weight_grad, outs, out_sems)
    for copy in out_copies:
        copy.start()
    for copy in copies:
        copy.wait()
    head_grad[...] = dot_right(attn_grad, weight[...]).astype(low)
    totals[...] = log_totals[...].T

    @pl.loop(0, KV_HEADS // 2)
    def _(pair):
        key_at = pl.ds(pl.multiple_of(pair * pair_lanes, pair_lanes), pair_lanes)
        value_at = pl.ds(pl.multiple_of(kv_width + pair * pair_lanes, pair_lanes), pair_lanes)
        keys = both_places(keyval[:, key_at])
        values = both_places(keyval[:, value_at])
        key_grads = [[None, None], [None, None]]
        value_grads = [[None, None], [None, None]]
        for i in range(repeat):
            at = pl.ds(pl.multiple_of((pair * repeat + i) * pair_lanes, pair_lanes), pair_lanes)
            queries = query[:, at]
            grads = head_grad[:, at]
            query_part = jnp.zeros((rows, pair_lanes), jnp.float32)
            for a in range(2):
                head = 2 * i + a
                g = head // repeat
                total = totals[pl.ds(pair * (2 * repeat) + head, 1), :]
                weights = jnp.exp(dot_right(keys[g][a], queries) + bias[...] - total)
                weight_grads = dot_right(values[g][a], grads)
                delta = jnp.sum(weights * weight_grads, axis=0, keepdims=True)
                score_grads = (weights * (weight_grads - delta)).astype(low)
                value_part = dot_plain(weights.astype(low), grads)
                key_part = dot_plain(score_grads, queries)
                query_part += dot_left(score_grads, keys[g][a])
                if key_grads[g][a] is None:
                    key_grads[g][a], value_grads[g][a] = key_part, value_part
                else:
                    key_grads[g][a] += key_part
                    value_grads[g][a] += value_part
            query_part = query_part * (HEAD_DIM**-0.5)
            query_part = query_part * cosine[...] - swap_halves(query_part) * sine[...]
            query_grad[:, at] = query_part.astype(low)
        low_lane = lax.broadcasted_iota(jnp.int32, (keyval.shape[0], pair_lanes), 1) < HEAD_DIM
        for at, found in ((key_at, key_grads), (value_at, value_grads)):
            keyval_grad[:, at] = jnp.where(
                low_lane,
                found[0][0] + pltpu.roll(found[0][1], HEAD_DIM, 1),
                pltpu.roll(found[1][0], HEAD_DIM, 1) + found[1][1],
            ).astype(low)

    for copy in out_copies:
        copy.wait()


def turn(place, spots, operands, pieces, cut, gain_at):
    residual, gate_rows, query, keyval = operands[1], operands[4], operands[9], operands[10]
    rows, width = residual.shape
    query_width = query.shape[1]
    low = jnp.bfloat16
    grads, held = grad_shapes(cut, query_width, width + gate_rows.shape[1])
    keys = keyval.shape[0]
    return pl.pallas_call(
        partial(turn_kernel, len(pieces), cut, gain_at),
        in_specs=[SCALARS, SCALARS] + [INSIDE] * len(operands) + [ANYWHERE] * len(pieces),
        out_specs=[ANYWHERE] * len(grads) + [INSIDE] * 3,
        out_shape=grads
        + [
            jax.ShapeDtypeStruct((rows, width), jnp.float32),
            jax.ShapeDtypeStruct((rows, query_width), low),
            jax.ShapeDtypeStruct(keyval.shape, low),
        ],
        scratch_shapes=[
            pltpu.VMEM((query_width, width), low),
            held,
            pltpu.VMEM((rows, query_width), low),
            pltpu.VMEM((128, rows), jnp.float32),
            pltpu.SemaphoreType.DMA((len(pieces) * pieces[0].shape[0],)),
            pltpu.SemaphoreType.DMA((8,)),
        ],
        compiler_params=pltpu.CompilerParams(vmem_limit_bytes=VMEM_BYTES),
        cost_estimate=cost(4 * rows * width * width + 20 * rows * query_width * keys, *pieces, *pieces),
        name="turn",
    )(place, spots, *operands, *pieces)


def leave_kernel(
    count,
    cut,
    gain_at,
    place,
    spots,
    keyval_sum,
    query_grad,
    normed,
    tokens,
    resid_grad,
    small,
    cosine,
    sine,
    *refs,
):
    pieces = refs[:count]
    refs = refs[count:]
    outs = refs[: (8 if cut else 1)]
    input_grad, weight, weight_grad, joined, sems, out_sems = refs[len(outs) :]
    low = jnp.bfloat16
    rows, width = tokens.shape
    query_width = query_grad.shape[1]
    kv_width = keyval_sum.shape[1] // 2
    qkv_width = query_width + 2 * kv_width
    pair = 2 * HEAD_DIM
    copies = weight_copies(spots, pieces, weight, sems)
    for copy in copies:
        copy.start()
    joined[:, :query_width] = query_grad[...]
    for start in range(0, kv_width, pair):
        part = keyval_sum[:, start : start + pair]
        part = part * cosine[...] - swap_halves(part) * sine[...]
        joined[:, query_width + start : query_width + start + pair] = part.astype(low)
    joined[:, query_width + kv_width :] = keyval_sum[:, kv_width:].astype(low)
    shape = weight_grad.shape[:-1]
    for start in range(0, qkv_width, 512):
        weight_grad[..., start : start + 512] = (
            dot_left(normed[...], joined[:, start : start + 512]).astype(low).reshape(shape + (512,))
        )
    for copy in copies:
        copy.wait()
    row_grad = dot_right(joined[...], weight[:, :qkv_width])
    inputs = tokens[...].astype(jnp.float32)
    scale = mean_square_scale(inputs)
    lanes = weight_grad.shape[-1] - qkv_width
    lane = lax.broadcasted_iota(jnp.int32, (rows, lanes), 1)
    picks = jnp.where(lane == gain_at, 1.0, 0.0).astype(low)
    weight_grad[..., qkv_width:] = (
        dot_left((row_grad * inputs * scale).astype(low), picks).astype(low).reshape(shape + (lanes,))
    )
    out_copies = grad_copies(cut, place, weight_grad, outs, out_sems)
    for copy in out_copies:
        copy.start()
    scaled = row_grad * small[gain_at : gain_at + 1, :]
    input_grad[...] = (
        resid_grad[...]
        + scale * scaled
        - inputs * (scale * scale * scale) * jnp.mean(scaled * inputs, axis=-1, keepdims=True)
    )
    for copy in out_copies:
        copy.wait()


def leave(place, spots, operands, pieces, cut, gain_at):
    tokens, query_grad, keyval_sum = operands[3], operands[1], operands[0]
    rows, width = tokens.shape
    columns = pieces[0].shape[2]
    low = jnp.bfloat16
    grads, held = grad_shapes(cut, width, columns)
    return pl.pallas_call(
        partial(leave_kernel, len(pieces), cut, gain_at),
        in_specs=[SCALARS, SCALARS] + [INSIDE] * len(operands) + [ANYWHERE] * len(pieces),
        out_specs=[ANYWHERE] * len(grads) + [INSIDE],
        out_shape=grads + [jax.ShapeDtypeStruct((rows, width), jnp.float32)],
        scratch_shapes=[
            pltpu.VMEM((width, columns), low),
            held,
            pltpu.VMEM((rows, query_grad.shape[1] + keyval_sum.shape[1]), low),
            pltpu.SemaphoreType.DMA((len(pieces) * pieces[0].shape[0],)),
            pltpu.SemaphoreType.DMA((8,)),
        ],
        compiler_params=pltpu.CompilerParams(vmem_limit_bytes=VMEM_BYTES),
        cost_estimate=cost(4 * rows * width * columns, *pieces, *pieces),
        name="leave",
    )(place, spots, *operands, *pieces)


def expert_kernel(carried, row_blocks, grad_blocks, row_tile, first, packed, *refs):
    blocks_in = refs[:row_blocks]
    grads_in = refs[row_blocks : row_blocks + grad_blocks]
    refs = refs[row_blocks + grad_blocks :]
    if carried:
        mix_in, turn_in = refs[:2]
        refs = refs[2:]
    (
        packed_grad,
        mix,
        turned,
        rows,
        grads,
        gates,
        gate_w,
        up_w,
        down_w,
        gate_g,
        up_g,
        down_g,
        weighted,
        gate_side,
        up_side,
        load_sems,
        save_sems,
        carry_sems,
    ) = refs
    count = packed.shape[2]
    hidden_width = gate_w.shape[-1]
    total_rows, width = rows.shape
    lanes = gates.shape[1]
    low = jnp.bfloat16

    def loads(e):
        slot = e % 2
        found = []
        for side, target in ((0, gate_w), (1, up_w)):
            for j in range(3):
                found.append(
                    pltpu.make_async_copy(
                        packed.at[:, side, e, :, pl.ds(j * hidden_width, hidden_width)],
                        target.at[slot, :, j],
                        load_sems.at[slot, 3 * side + j],
                    )
                )
        found.append(
            pltpu.make_async_copy(packed.at[:, 2, e], down_w.at[slot], load_sems.at[slot, 6])
        )
        return found

    def saves(e):
        slot = e % 2
        found = []
        for side, source in ((0, gate_g), (1, up_g)):
            for j in range(3):
                found.append(
                    pltpu.make_async_copy(
                        source.at[slot, :, j],
                        packed_grad.at[:, side, e, :, pl.ds(j * hidden_width, hidden_width)],
                        save_sems.at[slot, 3 * side + j],
                    )
                )
        found.append(
            pltpu.make_async_copy(down_g.at[slot], packed_grad.at[:, 2, e], save_sems.at[slot, 6])
        )
        return found

    carries = (
        block_copies(grads_in, grads, carry_sems, 0)
        + block_copies(blocks_in, rows, carry_sems, grad_blocks, pl.ds(0, width))
        + block_copies(
            blocks_in, gates, carry_sems, grad_blocks + row_blocks, pl.ds(width, lanes)
        )
    )
    if carried:
        at = grad_blocks + 2 * row_blocks
        carries += [
            pltpu.make_async_copy(mix_in, mix, carry_sems.at[at]),
            pltpu.make_async_copy(turn_in, turned, carry_sems.at[at + 1]),
        ]
    for copy in loads(0) + carries:
        copy.start()
    for e in range(count):
        slot = e % 2
        if e + 1 < count:
            for copy in loads(e + 1):
                copy.start()
        for copy in loads(e):
            copy.wait()
        if e == 0:
            for copy in carries:
                copy.wait()
            if not carried:
                turned[:, width:] = jnp.zeros((total_rows, lanes), jnp.float32)

        @pl.loop(0, total_rows // row_tile)
        def _(tile):
            span = pl.ds(pl.multiple_of(tile * row_tile, row_tile), row_tile)
            gate_full = gate_w[slot].reshape(width, hidden_width)
            up_full = up_w[slot].reshape(width, hidden_width)
            down_full = down_w[slot].reshape(hidden_width, width)
            here = rows[span, :]
            slope = dot_right(grads[span, :], down_full)
            gate_pre = dot_plain(here, gate_full)
            up_pre = dot_plain(here, up_full)
            lane = lax.broadcasted_iota(jnp.int32, (row_tile, lanes), 1)
            chosen = lane == first[0] + e
            gate_column = jnp.sum(
                jnp.where(chosen, gates[span, :].astype(jnp.float32), 0.0), axis=1, keepdims=True
            )
            sigmoid_gate = jax.nn.sigmoid(gate_pre)
            activated = gate_pre * sigmoid_gate
            hidden = (activated * up_pre).astype(low).astype(jnp.float32)
            share = jnp.sum(hidden * slope, axis=1, keepdims=True)
            turned[span, width:] = jnp.where(chosen, share, turned[span, width:])
            part_weighted = (hidden * gate_column).astype(low)
            hidden_grad = slope * gate_column
            part_gate = (
                hidden_grad * up_pre * (sigmoid_gate + activated * (1.0 - sigmoid_gate))
            ).astype(low)
            part_up = (hidden_grad * activated).astype(low)
            weighted[span, :] = part_weighted
            gate_side[span, :] = part_gate
            up_side[span, :] = part_up
            mix_part = dot_plain(part_weighted, down_full)
            turn_part = dot_right(part_gate, gate_full) + dot_right(part_up, up_full)
            if e == 0 and not carried:
                mix[span, :] = mix_part
                turned[span, :width] = turn_part
            else:
                mix[span, :] += mix_part
                turned[span, :width] += turn_part

        if e >= 2:
            for copy in saves(e - 2):
                copy.wait()
        down_g[slot] = dot_left(weighted[...], grads[...]).astype(low).reshape(down_g.shape[1:])
        gate_g[slot] = dot_left(rows[...], gate_side[...]).astype(low).reshape(gate_g.shape[1:])
        up_g[slot] = dot_left(rows[...], up_side[...]).astype(low).reshape(up_g.shape[1:])
        for copy in saves(e):
            copy.start()
    for e in range(max(0, count - 2), count):
        for copy in saves(e):
            copy.wait()


def expert_pass(first, rows, grads, packed, carry=None):
    blocks, _, count, part, width = packed.shape
    hidden_width = blocks * part
    total_rows = sum(block.shape[0] for block in rows)
    lanes = rows[0].shape[1] - width
    low = jnp.bfloat16
    carried = carry is not None
    flops = 18 * total_rows * count * hidden_width * width
    sides = [
        pltpu.VMEM((2, blocks, 3, part, hidden_width), low),
        pltpu.VMEM((2, blocks, 3, part, hidden_width), low),
        pltpu.VMEM((2, blocks, part, width), low),
    ]
    return pl.pallas_call(
        partial(expert_kernel, carried, len(rows), len(grads), min(512, total_rows)),
        in_specs=[SCALARS] + [ANYWHERE] * (1 + len(rows) + len(grads) + (2 if carried else 0)),
        out_specs=[ANYWHERE, INSIDE, INSIDE],
        out_shape=[
            jax.ShapeDtypeStruct(packed.shape, low),
            jax.ShapeDtypeStruct((total_rows, width), jnp.float32),
            jax.ShapeDtypeStruct((total_rows, width + lanes), jnp.float32),
        ],
        scratch_shapes=[
            pltpu.VMEM((total_rows, width), low),
            pltpu.VMEM((total_rows, width), low),
            pltpu.VMEM((total_rows, lanes), low),
        ]
        + sides
        + sides
        + [pltpu.VMEM((total_rows, hidden_width), low)] * 3
        + [
            pltpu.SemaphoreType.DMA((2, 7)),
            pltpu.SemaphoreType.DMA((2, 7)),
            pltpu.SemaphoreType.DMA((2 * len(rows) + len(grads) + 2,)),
        ],
        compiler_params=pltpu.CompilerParams(vmem_limit_bytes=VMEM_BYTES),
        cost_estimate=cost(flops, packed, packed, *rows, *grads),
        name="experts",
    )(first, packed, *rows, *grads, *(carry or ()))


def unpack_kernel(chunks, *refs):
    found, (gate, up, down) = refs[:chunks], refs[chunks:]
    hidden_width = gate.shape[2]
    base = 0
    for chunk in found:
        count, part = chunk.shape[1], chunk.shape[2]
        for e in range(count):
            for side, target in ((0, gate), (1, up)):
                for j in range(3):
                    target[base + e, j * part : (j + 1) * part, :] = chunk[
                        side, e, :, j * hidden_width : (j + 1) * hidden_width
                    ].astype(jnp.float32)
            down[base + e] = chunk[2, e].astype(jnp.float32)
        base += count


def unpack(chunks, gate_shape, down_shape):
    return pl.pallas_call(
        partial(unpack_kernel, len(chunks)),
        in_specs=[INSIDE] * len(chunks),
        out_specs=[INSIDE] * 3,
        out_shape=[
            jax.ShapeDtypeStruct(gate_shape, jnp.float32),
            jax.ShapeDtypeStruct(gate_shape, jnp.float32),
            jax.ShapeDtypeStruct(down_shape, jnp.float32),
        ],
        compiler_params=pltpu.CompilerParams(vmem_limit_bytes=VMEM_BYTES),
        cost_estimate=cost(0, *chunks, *chunks, *chunks),
        name="unpack",
    )(*chunks)


def cube():
    return lax.axis_size("batch") == 8 and lax.axis_size("expert") == 4


def pair_moves(size, flip):
    return [(i, i ^ flip) for i in range(size)]


def shift_moves(step):
    return [(2 * z + c, 2 * ((z + step) % 4) + c) for z in range(4) for c in range(2)]


def gather_blocks(rows):
    size = lax.axis_size("expert")
    if size != 4:
        stacked = lax.all_gather(rows, "expert", axis=0)
        own = lax.axis_index("expert")
        return [
            lax.dynamic_index_in_dim(stacked, own ^ r, axis=0, keepdims=False) for r in range(size)
        ]
    across, along = pair_moves(size, 1), pair_moves(size, 2)
    half = rows.shape[0] // 2
    first = lax.ppermute(rows, "expert", across)
    second = lax.ppermute(rows, "expert", along)
    top = lax.ppermute(second[:half], "expert", across)
    bottom = lax.ppermute(first[half:], "expert", along)
    return [rows, first, second, top, bottom]


def scatter_blocks(parts):
    size = lax.axis_size("expert")
    low = jnp.bfloat16
    wide = jnp.float32
    if size != 4:
        own = lax.axis_index("expert")
        order = jnp.arange(size, dtype=jnp.int32) ^ own
        stacked = jnp.take(jnp.stack(parts), order, axis=0).astype(low)
        return lax.psum_scatter(stacked, "expert", scatter_dimension=0).astype(wide)
    across, along = pair_moves(size, 1), pair_moves(size, 2)
    half = parts[0].shape[0] // 2
    top = lax.ppermute(parts[3][:half].astype(low), "expert", across)
    bottom = lax.ppermute(parts[3][half:].astype(low), "expert", along)
    first_top = lax.ppermute(parts[1][:half].astype(low), "expert", across)
    second_bottom = lax.ppermute(parts[2][half:].astype(low), "expert", along)
    for_second = (parts[2][:half].astype(wide) + top.astype(wide)).astype(low)
    for_first = (parts[1][half:].astype(wide) + bottom.astype(wide)).astype(low)
    second_top = lax.ppermute(for_second, "expert", along)
    first_bottom = lax.ppermute(for_first, "expert", across)
    own = parts[0].astype(wide)
    return jnp.concatenate(
        [
            own[:half] + first_top.astype(wide) + second_top.astype(wide),
            own[half:] + first_bottom.astype(wide) + second_bottom.astype(wide),
        ],
        axis=0,
    )


def gather_dense(rows):
    if not cube():
        whole = lax.all_gather(rows, ("batch", "expert"), axis=0, tiled=True)
        return [whole[None]], jnp.zeros((1, 1), jnp.int32), None
    place = lax.axis_index("batch")
    level, core = place // 2, place % 2
    member = lax.axis_index("expert")
    line = [rows] + [lax.ppermute(rows, "batch", shift_moves(r)) for r in range(1, 4)]
    mine = gather_blocks(jnp.stack(line))
    mine = mine[:3] + [jnp.concatenate(mine[3:], axis=0)]
    other = [lax.ppermute(block, "batch", pair_moves(8, 1)) for block in mine]
    spots = [
        [(((level + 4 - k) % 4) * 2 + (core ^ c)) * 4 + (member ^ r) for k in range(4)]
        for c in range(2)
        for r in range(4)
    ]
    return mine + other, jnp.array(spots, jnp.int32), line[1]


def scatter_dense(found):
    low = jnp.bfloat16
    wide = jnp.float32
    if not cube():
        values = found[0].reshape(found[0].shape[3:])
        total = lax.psum_scatter(values, ("batch", "expert"), scatter_dimension=0, tiled=True)
        return total.astype(wide)
    level = lax.axis_index("batch") // 2
    received = {r: lax.ppermute(found[r], "batch", pair_moves(8, 1)) for r in (3, 1, 2, 0)}
    parts = [found[4 + r].astype(wide) + received[r].astype(wide) for r in range(4)]
    plane = scatter_blocks(parts)
    total = lax.dynamic_index_in_dim(plane, level, axis=0, keepdims=False)
    for r in range(1, 4):
        sent = lax.dynamic_index_in_dim(plane, (level + r) % 4, axis=0, keepdims=False)
        total += lax.ppermute(sent.astype(low), "batch", shift_moves(r)).astype(wide)
    return total


def pack_sides(gate, up, down):
    def fold(values):
        count, depth, width = values.shape
        return values.reshape(count, 3, depth // 3, width).transpose(0, 2, 1, 3).reshape(down.shape)

    return jnp.stack([fold(gate), fold(up), down], axis=0)


def local(
    tokens,
    cotangent,
    attn_gain,
    query_weight,
    key_weight,
    value_weight,
    out_weight,
    ffn_gain,
    router_weight,
    gate_weight,
    up_weight,
    down_weight,
    routes,
    ranking,
):
    low = jnp.bfloat16
    wide = jnp.float32
    query_width = HEADS * HEAD_DIM
    kv_width = KV_HEADS * HEAD_DIM
    qkv_width = query_width + 2 * kv_width
    width = tokens.shape[2]
    experts_total = router_weight.shape[1]
    extra = -(-(experts_total + 2) // 128) * 128
    first_gain, second_gain = experts_total, experts_total + 1
    local_experts = gate_weight.shape[0]
    member_count = lax.axis_size("expert")
    member_id = lax.axis_index("expert")
    local_rows = tokens.shape[1]
    group_rows = local_rows * member_count
    cut = cube()
    place = jnp.stack([lax.axis_index("batch") % 2, member_id]).astype(jnp.int32)

    qkv_pieces, qkv_spots, early = gather_dense(
        jnp.concatenate(
            [
                query_weight,
                key_weight,
                value_weight,
                router_weight,
                attn_gain[:, None],
                ffn_gain[:, None],
                jnp.zeros((query_weight.shape[0], extra - experts_total - 2), low),
            ],
            axis=1,
        )
    )
    out_pieces, out_spots, _ = gather_dense(out_weight)
    chunks = (0, 3, local_experts)
    packed_all = []
    for a, b in zip(chunks[:-1], chunks[1:]):
        sides = (gate_weight[a:b], up_weight[a:b], down_weight[a:b])
        if a > 0 and early is not None:
            sides = lax.optimization_barrier((early, sides))[1]
        packed_all.append(lax.all_gather(pack_sides(*sides), "batch", axis=0))

    row_ids = member_id * local_rows + jnp.arange(local_rows, dtype=jnp.int32)
    half_dim = HEAD_DIM // 2
    frequency = THETA ** (-jnp.arange(half_dim, dtype=wide) / half_dim)
    angles = place_of(row_ids).astype(wide)[:, None] * frequency[None, :]
    cosine = jnp.tile(jnp.cos(angles), (1, 4))
    sine_part = jnp.tile(jnp.concatenate([-jnp.sin(angles), jnp.sin(angles)], axis=1), (1, 2))
    grad_out = cotangent[0]
    grad_blocks = gather_blocks(grad_out)

    normed, query, keyval, small = enter(
        tokens[0], cosine, sine_part, qkv_pieces, qkv_spots, first_gain, query_width, kv_width
    )

    route_rows = routes[0]
    rank_rows = ranking[0]
    expert_lanes = jnp.arange(extra, dtype=jnp.int32)
    member = jnp.any(route_rows[:, :, None] == expert_lanes[None, None, :], axis=1)
    marks = jnp.where(
        expert_lanes[None, :] == experts_total,
        (rank_rows // 32)[:, None],
        jnp.where(expert_lanes[None, :] == experts_total + 1, (rank_rows % 32)[:, None], member),
    ).astype(low)
    marks_all = jnp.concatenate(gather_blocks(marks), axis=0)
    rank_all = (
        marks_all[:, experts_total].astype(wide) * 32 + marks_all[:, experts_total + 1].astype(wide)
    )
    earlier = (rank_all[None, :] < rank_rows.astype(wide)[:, None]).astype(low)
    before = product(earlier, marks_all)
    capacity = 5 * group_rows * route_rows.shape[1] // (4 * experts_total)
    member = member.astype(wide)
    kept = jnp.where(before < capacity, member, 0.0)

    keyval_blocks = gather_blocks(keyval)
    if member_count == 4:
        ordered = keyval_blocks[:3] + [jnp.concatenate(keyval_blocks[3:], axis=0)]
        away = 1 << 20
        keys = jnp.concatenate(
            [
                lax.select_n(member_id, *ordered),
                lax.select_n(member_id ^ 1, *ordered),
                keyval,
            ],
            axis=0,
        )
        starts = [
            jnp.where(member_id >= 1, 0, away),
            jnp.where(member_id >= 2, local_rows, away),
            member_id * local_rows,
        ]
    else:
        keys = jnp.concatenate(keyval_blocks, axis=0)
        starts = [(member_id ^ r) * local_rows for r in range(member_count)]
    key_ids = jnp.concatenate([s + jnp.arange(local_rows, dtype=jnp.int32) for s in starts])
    bias = jnp.where(visible(row_ids, key_ids), 0.0, -1e30).astype(wide)
    attended, log_totals, residual, sent, gate_rows = attend(
        query, keys, bias, tokens[0], small, member, kept, second_gain, out_pieces, out_spots
    )
    sent_blocks = gather_blocks(sent)

    carry, totals = None, []
    for packed, a in zip(packed_all, chunks):
        first = (member_id * local_experts + a).astype(jnp.int32).reshape(1)
        packed_grad, mixture_all, row_grad = expert_pass(
            first, sent_blocks, grad_blocks, packed, carry
        )
        carry = (mixture_all, row_grad)
        if totals:
            packed_grad, totals[-1] = lax.optimization_barrier((packed_grad, totals[-1]))
        totals.append(lax.psum_scatter(packed_grad, "batch", scatter_dimension=0))

    def blocks_of(values):
        return [values[r * local_rows : (r + 1) * local_rows] for r in range(member_count)]

    normed_grad = scatter_blocks(blocks_of(row_grad))
    turned = turn(
        place,
        out_spots,
        (
            normed_grad,
            residual,
            grad_out,
            small,
            gate_rows,
            member,
            kept,
            sent,
            attended,
            query,
            keys,
            bias.T,
            log_totals,
            cosine,
            sine_part,
        ),
        out_pieces,
        cut,
        second_gain,
    )
    out_found = turned[:-3]
    resid_grad, query_grad, key_grads = turned[-3:]
    if member_count == 4:
        zero = jnp.zeros((), low)
        for_first, for_second, for_own = blocks_of(key_grads)[:3]
        key_parts = []
        for r in range(4):
            part = jnp.where(member_id == r, for_first, zero)
            part += jnp.where(member_id ^ 1 == r, for_second, zero)
            key_parts.append(part + for_own if r == 0 else part)
    else:
        key_parts = blocks_of(key_grads)
    keyval_sum = scatter_blocks(key_parts)
    left = leave(
        place,
        qkv_spots,
        (
            keyval_sum,
            query_grad,
            normed,
            tokens[0],
            resid_grad,
            small,
            cosine,
            sine_part,
        ),
        qkv_pieces,
        cut,
        first_gain,
    )
    qkv_found, input_grad = left[:-1], left[-1]
    mixture = scatter_blocks(blocks_of(mixture_all))
    result = (residual + mixture).astype(low)
    out_sum = scatter_dense(out_found)
    qkv_sum = scatter_dense(qkv_found)
    gate_total, up_total, down_total = unpack(totals, gate_weight.shape, down_weight.shape)
    return (
        result[None],
        input_grad[None],
        qkv_sum[:, qkv_width + first_gain],
        qkv_sum[:, :query_width],
        qkv_sum[:, query_width : query_width + kv_width],
        qkv_sum[:, query_width + kv_width : qkv_width],
        out_sum[:, :width],
        out_sum[:, width + second_gain],
        out_sum[:, width : width + experts_total],
        gate_total,
        up_total,
        down_total,
    )


def solution(mesh):
    return jax.shard_map(
        local,
        mesh=mesh,
        in_specs=(
            P("batch", "expert", None),
            P("batch", "expert", None),
            P(("batch", "expert")),
            P(("batch", "expert"), None),
            P(("batch", "expert"), None),
            P(("batch", "expert"), None),
            P(("batch", "expert"), None),
            P(("batch", "expert")),
            P(("batch", "expert"), None),
            P("expert", "batch", None),
            P("expert", "batch", None),
            P("expert", "batch", None),
            P("batch", "expert", None),
            P("batch", "expert"),
        ),
        out_specs=(
            P("batch", "expert", None),
            P("batch", "expert", None),
            P(("batch", "expert")),
            P(("batch", "expert"), None),
            P(("batch", "expert"), None),
            P(("batch", "expert"), None),
            P(("batch", "expert"), None),
            P(("batch", "expert")),
            P(("batch", "expert"), None),
            P("expert", "batch", None),
            P("expert", "batch", None),
            P("expert", "batch", None),
        ),
        check_vma=False,
    )
```

```python
from functools import partial

import jax
import jax.numpy as jnp
from jax import lax
from jax.experimental import pallas as pl
from jax.experimental.pallas import tpu as pltpu
from jax.sharding import PartitionSpec as P

HEADS = 24
KV_HEADS = 8
HEAD_DIM = 64
PROMPT = 512
CLEN = 256


EPS = 1e-06
THETA = 10000.0


def product(left, right):
    return jnp.dot(left, right, preferred_element_type=jnp.float32)


def place_of(row_ids):
    return jnp.where(row_ids < PROMPT, row_ids, PROMPT + (row_ids - PROMPT) % CLEN)


def visible(query_ids, key_ids):
    causal = key_ids[None, :] <= query_ids[:, None]
    same_run = (key_ids[None, :] - PROMPT) // CLEN == (query_ids[:, None] - PROMPT) // CLEN
    return causal & ((key_ids[None, :] < PROMPT) | same_run)


def dot_plain(left, right):
    return lax.dot_general(left, right, (((1,), (0,)), ((), ())), preferred_element_type=jnp.float32)


def dot_right(left, right):
    return lax.dot_general(left, right, (((1,), (1,)), ((), ())), preferred_element_type=jnp.float32)


def dot_left(left, right):
    return lax.dot_general(left, right, (((0,), (0,)), ((), ())), preferred_element_type=jnp.float32)


ANYWHERE = pl.BlockSpec(memory_space=pl.ANY)
INSIDE = pl.BlockSpec(memory_space=pltpu.VMEM)
SCALARS = pl.BlockSpec(memory_space=pltpu.SMEM)
VMEM_BYTES = 60 * 1024 * 1024


def cost(flops, *arrays):
    return pl.CostEstimate(
        flops=int(flops),
        bytes_accessed=int(sum(a.size * a.dtype.itemsize for a in arrays)),
        transcendentals=0,
    )


def weight_copies(spots, pieces, target, sems):
    copies = []
    for p, piece in enumerate(pieces):
        blocks, rows = piece.shape[0], piece.shape[1]
        for k in range(blocks):
            place = pl.multiple_of(spots[p, k] * rows, rows)
            copies.append(
                pltpu.make_async_copy(
                    piece.at[k], target.at[pl.ds(place, rows)], sems.at[p * blocks + k]
                )
            )
    return copies


def block_copies(blocks, target, sems, first, columns=None):
    copies = []
    start = 0
    for i, block in enumerate(blocks):
        rows = block.shape[0]
        source = block if columns is None else block.at[:, columns]
        copies.append(
            pltpu.make_async_copy(source, target.at[pl.ds(start, rows)], sems.at[first + i])
        )
        start += rows
    return copies


def swap_halves(values):
    half = HEAD_DIM // 2
    lane = lax.broadcasted_iota(jnp.int32, values.shape, 1)
    return jnp.where(
        lane % HEAD_DIM < half,
        pltpu.roll(values, 2 * HEAD_DIM - half, 1),
        pltpu.roll(values, half, 1),
    )


def mean_square_scale(values):
    return lax.rsqrt(jnp.mean(values * values, axis=-1, keepdims=True) + EPS)


def enter_kernel(count, gain_at, spots, tokens, cosine, sine, *refs):
    pieces = refs[:count]
    normed, query, keyval, small, weight, sems = refs[count:]
    low = jnp.bfloat16
    copies = weight_copies(spots, pieces, weight, sems)
    for copy in copies:
        copy.start()
    inputs = tokens[...].astype(jnp.float32)
    scaled = inputs * mean_square_scale(inputs)
    for copy in copies:
        copy.wait()
    query_width = query.shape[1]
    kv_width = keyval.shape[1] // 2
    qkv_width = query_width + 2 * kv_width
    turned = weight[:, qkv_width:].astype(jnp.float32).T
    small[...] = turned
    rows = (scaled * turned[gain_at : gain_at + 1]).astype(low)
    normed[...] = rows
    pair = 2 * HEAD_DIM
    scale = HEAD_DIM**-0.5
    for start in range(0, query_width + kv_width, 512):
        product_part = dot_plain(rows, weight[:, start : start + 512])
        for offset in range(0, 512, pair):
            part = product_part[:, offset : offset + pair]
            part = part * cosine[...] + swap_halves(part) * sine[...]
            at = start + offset
            if at < query_width:
                query[:, at : at + pair] = (part * scale).astype(low)
            else:
                keyval[:, at - query_width : at - query_width + pair] = part.astype(low)
    keyval[:, kv_width:] = dot_plain(
        rows, weight[:, query_width + kv_width : qkv_width]
    ).astype(low)


def enter(tokens, cosine, sine, pieces, spots, gain_at, query_width, kv_width):
    rows, width = tokens.shape
    columns = pieces[0].shape[2]
    low = jnp.bfloat16
    return pl.pallas_call(
        partial(enter_kernel, len(pieces), gain_at),
        in_specs=[SCALARS, INSIDE, INSIDE, INSIDE] + [ANYWHERE] * len(pieces),
        out_specs=[INSIDE] * 4,
        out_shape=[
            jax.ShapeDtypeStruct((rows, width), low),
            jax.ShapeDtypeStruct((rows, query_width), low),
            jax.ShapeDtypeStruct((rows, 2 * kv_width), low),
            jax.ShapeDtypeStruct((columns - query_width - 2 * kv_width, width), jnp.float32),
        ],
        scratch_shapes=[
            pltpu.VMEM((width, columns), low),
            pltpu.SemaphoreType.DMA((len(pieces) * pieces[0].shape[0],)),
        ],
        compiler_params=pltpu.CompilerParams(vmem_limit_bytes=VMEM_BYTES),
        cost_estimate=cost(2 * rows * width * columns, *pieces),
        name="enter",
    )(spots, tokens, cosine, sine, *pieces)


def both_places(values):
    wide = values.astype(jnp.float32)
    low_lane = lax.broadcasted_iota(jnp.int32, values.shape, 1) < HEAD_DIM
    moved = pltpu.roll(wide, HEAD_DIM, 1)
    kind = values.dtype
    return [
        [jnp.where(low_lane, wide, 0.0).astype(kind), jnp.where(low_lane, 0.0, moved).astype(kind)],
        [jnp.where(low_lane, moved, 0.0).astype(kind), jnp.where(low_lane, 0.0, wide).astype(kind)],
    ]


def attend_kernel(
    count, query, keyval, bias, tokens, small, member, kept, gain_at, spots, *refs
):
    pieces = refs[:count]
    attended, log_totals, residual, sent, gate_rows, weight, sems = refs[count:]
    low = jnp.bfloat16
    rows = query.shape[0]
    width = tokens.shape[1]
    kv_width = keyval.shape[1] // 2
    pair_lanes = 2 * HEAD_DIM
    repeat = HEADS // KV_HEADS
    copies = weight_copies(spots, pieces, weight, sems)
    for copy in copies:
        copy.start()
    log_totals[...] = jnp.zeros_like(log_totals)
    lane = lax.broadcasted_iota(jnp.int32, log_totals.shape, 1)

    @pl.loop(0, KV_HEADS // 2)
    def _(pair):
        at = pl.ds(pl.multiple_of(pair * pair_lanes, pair_lanes), pair_lanes)
        keys = both_places(keyval[:, at])
        at = pl.ds(pl.multiple_of(kv_width + pair * pair_lanes, pair_lanes), pair_lanes)
        values = both_places(keyval[:, at])
        for i in range(repeat):
            at = pl.ds(pl.multiple_of((pair * repeat + i) * pair_lanes, pair_lanes), pair_lanes)
            queries = query[:, at]
            total = jnp.zeros((rows, pair_lanes), jnp.float32)
            for a in range(2):
                head = 2 * i + a
                scores = dot_right(queries, keys[head // repeat][a]) + bias[...]
                peak = jnp.max(scores, axis=-1, keepdims=True)
                lifted = jnp.exp(scores - peak)
                row_total = jnp.sum(lifted, axis=-1, keepdims=True)
                weights_low = (lifted * (1.0 / row_total)).astype(low)
                total += dot_plain(weights_low, values[head // repeat][a])
                log_totals[...] = jnp.where(
                    lane == pair * (2 * repeat) + head, peak + jnp.log(row_total), log_totals[...]
                )
            attended[:, at] = total.astype(low)

    for copy in copies:
        copy.wait()
    hidden = tokens[...].astype(jnp.float32) + dot_plain(attended[...], weight[...])
    residual[...] = hidden
    gain = small[gain_at : gain_at + 1, :]
    normed = (hidden * mean_square_scale(hidden) * gain).astype(low)
    logits = dot_right(normed, small[...].astype(low))
    chosen = member[...] > 0.0
    logits = jnp.where(chosen, logits, -1e30)
    lifted = jnp.where(chosen, jnp.exp(logits - jnp.max(logits, axis=-1, keepdims=True)), 0.0)
    gates = lifted / jnp.sum(lifted, axis=-1, keepdims=True)
    gate_rows[...] = gates
    sent[:, :width] = normed
    sent[:, width:] = (gates * kept[...]).astype(low)


def attend(query, keyval, bias, tokens, small, member, kept, gain_at, pieces, spots):
    rows, width = tokens.shape
    query_width = query.shape[1]
    lanes = small.shape[0]
    low = jnp.bfloat16

    def kernel(*refs):
        attend_kernel(len(pieces), *refs[:7], gain_at, *refs[7:])

    return pl.pallas_call(
        kernel,
        in_specs=[INSIDE] * 7 + [SCALARS] + [ANYWHERE] * len(pieces),
        out_specs=[INSIDE] * 5,
        out_shape=[
            jax.ShapeDtypeStruct((rows, query_width), low),
            jax.ShapeDtypeStruct((rows, 128), jnp.float32),
            jax.ShapeDtypeStruct((rows, width), jnp.float32),
            jax.ShapeDtypeStruct((rows, width + lanes), low),
            jax.ShapeDtypeStruct((rows, lanes), jnp.float32),
        ],
        scratch_shapes=[
            pltpu.VMEM((query_width, width), low),
            pltpu.SemaphoreType.DMA((len(pieces) * pieces[0].shape[0],)),
        ],
        compiler_params=pltpu.CompilerParams(vmem_limit_bytes=VMEM_BYTES),
        cost_estimate=cost(2 * rows * width * width + 8 * rows * query_width * bias.shape[1], *pieces),
        name="attend",
    )(query, keyval, bias, tokens, small, member, kept, spots, *pieces)


def sorted_copies(place, source, others, own, sems):
    core, member = place[0], place[1]
    copies = []
    for r, (other, mine) in enumerate(zip(others, own)):
        copies.append(
            pltpu.make_async_copy(source.at[:, 1 - core, member ^ r], other, sems.at[2 * r])
        )
        copies.append(
            pltpu.make_async_copy(source.at[:, core, member ^ r], mine, sems.at[2 * r + 1])
        )
    return copies


def grad_shapes(cut, rows, columns):
    low = jnp.bfloat16
    if cut:
        block = rows // 32
        return (
            [jax.ShapeDtypeStruct((4, block, columns), low)] * 8,
            pltpu.VMEM((4, 2, 4, block, columns), low),
        )
    return (
        [jax.ShapeDtypeStruct((1, 1, 1, rows, columns), low)],
        pltpu.VMEM((1, 1, 1, rows, columns), low),
    )


def grad_copies(cut, place, source, outs, sems):
    if cut:
        return sorted_copies(place, source, outs[:4], outs[4:], sems)
    return [pltpu.make_async_copy(source, outs[0], sems.at[0])]


def turn_kernel(
    count,
    cut,
    gain_at,
    place,
    spots,
    normed_grad,
    residual,
    grad_out,
    small,
    gate_rows,
    member,
    kept,
    normed,
    attended,
    query,
    keyval,
    bias,
    log_totals,
    cosine,
    sine,
    *refs,
):
    pieces = refs[:count]
    refs = refs[count:]
    outs = refs[: (8 if cut else 1)]
    refs = refs[len(outs) :]
    resid_grad, query_grad, keyval_grad, weight, weight_grad, head_grad, totals, sems, out_sems = refs
    low = jnp.bfloat16
    rows, width = residual.shape
    lanes = gate_rows.shape[1]
    kv_width = keyval.shape[1] // 2
    pair_lanes = 2 * HEAD_DIM
    repeat = HEADS // KV_HEADS
    copies = weight_copies(spots, pieces, weight, sems)
    for copy in copies:
        copy.start()
    lane = lax.broadcasted_iota(jnp.int32, (rows, lanes), 1)
    gates = gate_rows[...]
    gate_grads = normed_grad[:, width:] * kept[...]
    chosen_grad = gates * (gate_grads - jnp.sum(gates * gate_grads, axis=-1, keepdims=True))
    logit_grad = (chosen_grad * member[...]).astype(low)
    hidden = residual[...]
    scale = mean_square_scale(hidden)
    row_grad = normed_grad[:, :width] + dot_plain(logit_grad, small[...].astype(low))
    gain = small[gain_at : gain_at + 1, :]
    scaled = row_grad * gain
    total_grad = (
        grad_out[...].astype(jnp.float32)
        + scale * scaled
        - hidden * (scale * scale * scale) * jnp.mean(scaled * hidden, axis=-1, keepdims=True)
    )
    resid_grad[...] = total_grad
    attn_grad = total_grad.astype(low)
    shape = weight_grad.shape[:-1]
    gain_grad = (row_grad * hidden * scale).astype(low)
    picks = jnp.where(lane == gain_at, 1.0, 0.0).astype(low)
    weight_grad[..., width:] = (
        (dot_left(normed[...][:, :width], logit_grad) + dot_left(gain_grad, picks))
        .astype(low)
        .reshape(shape + (lanes,))
    )
    for start in range(0, width, 512):
        weight_grad[..., start : start + 512] = (
            dot_left(attended[...], attn_grad[:, start : start + 512])
            .astype(low)
            .reshape(shape + (512,))
        )
    out_copies = grad_copies(cut, place, weight_grad, outs, out_sems)
    for copy in out_copies:
        copy.start()
    for copy in copies:
        copy.wait()
    head_grad[...] = dot_right(attn_grad, weight[...]).astype(low)
    totals[...] = log_totals[...].T

    @pl.loop(0, KV_HEADS // 2)
    def _(pair):
        key_at = pl.ds(pl.multiple_of(pair * pair_lanes, pair_lanes), pair_lanes)
        value_at = pl.ds(pl.multiple_of(kv_width + pair * pair_lanes, pair_lanes), pair_lanes)
        keys = both_places(keyval[:, key_at])
        values = both_places(keyval[:, value_at])
        key_grads = [[None, None], [None, None]]
        value_grads = [[None, None], [None, None]]
        for i in range(repeat):
            at = pl.ds(pl.multiple_of((pair * repeat + i) * pair_lanes, pair_lanes), pair_lanes)
            queries = query[:, at]
            grads = head_grad[:, at]
            query_part = jnp.zeros((rows, pair_lanes), jnp.float32)
            for a in range(2):
                head = 2 * i + a
                g = head // repeat
                total = totals[pl.ds(pair * (2 * repeat) + head, 1), :]
                weights = jnp.exp(dot_right(keys[g][a], queries) + bias[...] - total)
                weight_grads = dot_right(values[g][a], grads)
                delta = jnp.sum(weights * weight_grads, axis=0, keepdims=True)
                score_grads = (weights * (weight_grads - delta)).astype(low)
                value_part = dot_plain(weights.astype(low), grads)
                key_part = dot_plain(score_grads, queries)
                query_part += dot_left(score_grads, keys[g][a])
                if key_grads[g][a] is None:
                    key_grads[g][a], value_grads[g][a] = key_part, value_part
                else:
                    key_grads[g][a] += key_part
                    value_grads[g][a] += value_part
            query_part = query_part * (HEAD_DIM**-0.5)
            query_part = query_part * cosine[...] - swap_halves(query_part) * sine[...]
            query_grad[:, at] = query_part.astype(low)
        low_lane = lax.broadcasted_iota(jnp.int32, (keyval.shape[0], pair_lanes), 1) < HEAD_DIM
        for at, found in ((key_at, key_grads), (value_at, value_grads)):
            keyval_grad[:, at] = jnp.where(
                low_lane,
                found[0][0] + pltpu.roll(found[0][1], HEAD_DIM, 1),
                pltpu.roll(found[1][0], HEAD_DIM, 1) + found[1][1],
            ).astype(low)

    for copy in out_copies:
        copy.wait()


def turn(place, spots, operands, pieces, cut, gain_at):
    residual, gate_rows, query, keyval = operands[1], operands[4], operands[9], operands[10]
    rows, width = residual.shape
    query_width = query.shape[1]
    low = jnp.bfloat16
    grads, held = grad_shapes(cut, query_width, width + gate_rows.shape[1])
    keys = keyval.shape[0]
    return pl.pallas_call(
        partial(turn_kernel, len(pieces), cut, gain_at),
        in_specs=[SCALARS, SCALARS] + [INSIDE] * len(operands) + [ANYWHERE] * len(pieces),
        out_specs=[ANYWHERE] * len(grads) + [INSIDE] * 3,
        out_shape=grads
        + [
            jax.ShapeDtypeStruct((rows, width), jnp.float32),
            jax.ShapeDtypeStruct((rows, query_width), low),
            jax.ShapeDtypeStruct(keyval.shape, low),
        ],
        scratch_shapes=[
            pltpu.VMEM((query_width, width), low),
            held,
            pltpu.VMEM((rows, query_width), low),
            pltpu.VMEM((128, rows), jnp.float32),
            pltpu.SemaphoreType.DMA((len(pieces) * pieces[0].shape[0],)),
            pltpu.SemaphoreType.DMA((8,)),
        ],
        compiler_params=pltpu.CompilerParams(vmem_limit_bytes=VMEM_BYTES),
        cost_estimate=cost(4 * rows * width * width + 20 * rows * query_width * keys, *pieces, *pieces),
        name="turn",
    )(place, spots, *operands, *pieces)


def leave_kernel(
    count,
    cut,
    gain_at,
    place,
    spots,
    keyval_sum,
    query_grad,
    normed,
    tokens,
    resid_grad,
    small,
    cosine,
    sine,
    *refs,
):
    pieces = refs[:count]
    refs = refs[count:]
    outs = refs[: (8 if cut else 1)]
    input_grad, weight, weight_grad, joined, sems, out_sems = refs[len(outs) :]
    low = jnp.bfloat16
    rows, width = tokens.shape
    query_width = query_grad.shape[1]
    kv_width = keyval_sum.shape[1] // 2
    qkv_width = query_width + 2 * kv_width
    pair = 2 * HEAD_DIM
    copies = weight_copies(spots, pieces, weight, sems)
    for copy in copies:
        copy.start()
    joined[:, :query_width] = query_grad[...]
    for start in range(0, kv_width, pair):
        part = keyval_sum[:, start : start + pair]
        part = part * cosine[...] - swap_halves(part) * sine[...]
        joined[:, query_width + start : query_width + start + pair] = part.astype(low)
    joined[:, query_width + kv_width :] = keyval_sum[:, kv_width:].astype(low)
    shape = weight_grad.shape[:-1]
    for start in range(0, qkv_width, 512):
        weight_grad[..., start : start + 512] = (
            dot_left(normed[...], joined[:, start : start + 512]).astype(low).reshape(shape + (512,))
        )
    for copy in copies:
        copy.wait()
    row_grad = dot_right(joined[...], weight[:, :qkv_width])
    inputs = tokens[...].astype(jnp.float32)
    scale = mean_square_scale(inputs)
    lanes = weight_grad.shape[-1] - qkv_width
    lane = lax.broadcasted_iota(jnp.int32, (rows, lanes), 1)
    picks = jnp.where(lane == gain_at, 1.0, 0.0).astype(low)
    weight_grad[..., qkv_width:] = (
        dot_left((row_grad * inputs * scale).astype(low), picks).astype(low).reshape(shape + (lanes,))
    )
    out_copies = grad_copies(cut, place, weight_grad, outs, out_sems)
    for copy in out_copies:
        copy.start()
    scaled = row_grad * small[gain_at : gain_at + 1, :]
    input_grad[...] = (
        resid_grad[...]
        + scale * scaled
        - inputs * (scale * scale * scale) * jnp.mean(scaled * inputs, axis=-1, keepdims=True)
    )
    for copy in out_copies:
        copy.wait()


def leave(place, spots, operands, pieces, cut, gain_at):
    tokens, query_grad, keyval_sum = operands[3], operands[1], operands[0]
    rows, width = tokens.shape
    columns = pieces[0].shape[2]
    low = jnp.bfloat16
    grads, held = grad_shapes(cut, width, columns)
    return pl.pallas_call(
        partial(leave_kernel, len(pieces), cut, gain_at),
        in_specs=[SCALARS, SCALARS] + [INSIDE] * len(operands) + [ANYWHERE] * len(pieces),
        out_specs=[ANYWHERE] * len(grads) + [INSIDE],
        out_shape=grads + [jax.ShapeDtypeStruct((rows, width), jnp.float32)],
        scratch_shapes=[
            pltpu.VMEM((width, columns), low),
            held,
            pltpu.VMEM((rows, query_grad.shape[1] + keyval_sum.shape[1]), low),
            pltpu.SemaphoreType.DMA((len(pieces) * pieces[0].shape[0],)),
            pltpu.SemaphoreType.DMA((8,)),
        ],
        compiler_params=pltpu.CompilerParams(vmem_limit_bytes=VMEM_BYTES),
        cost_estimate=cost(4 * rows * width * columns, *pieces, *pieces),
        name="leave",
    )(place, spots, *operands, *pieces)


def expert_kernel(carried, row_blocks, grad_blocks, row_tile, first, packed, *refs):
    blocks_in = refs[:row_blocks]
    grads_in = refs[row_blocks : row_blocks + grad_blocks]
    refs = refs[row_blocks + grad_blocks :]
    if carried:
        mix_in, turn_in = refs[:2]
        refs = refs[2:]
    (
        packed_grad,
        mix,
        turned,
        rows,
        grads,
        gates,
        gate_w,
        up_w,
        down_w,
        gate_g,
        up_g,
        down_g,
        weighted,
        gate_side,
        up_side,
        load_sems,
        save_sems,
        carry_sems,
    ) = refs
    count = packed.shape[2]
    hidden_width = gate_w.shape[-1]
    total_rows, width = rows.shape
    lanes = gates.shape[1]
    low = jnp.bfloat16

    def loads(e):
        slot = e % 2
        found = []
        for side, target in ((0, gate_w), (1, up_w)):
            for j in range(3):
                found.append(
                    pltpu.make_async_copy(
                        packed.at[:, side, e, :, pl.ds(j * hidden_width, hidden_width)],
                        target.at[slot, :, j],
                        load_sems.at[slot, 3 * side + j],
                    )
                )
        found.append(
            pltpu.make_async_copy(packed.at[:, 2, e], down_w.at[slot], load_sems.at[slot, 6])
        )
        return found

    def saves(e):
        slot = e % 2
        found = []
        for side, source in ((0, gate_g), (1, up_g)):
            for j in range(3):
                found.append(
                    pltpu.make_async_copy(
                        source.at[slot, :, j],
                        packed_grad.at[:, side, e, :, pl.ds(j * hidden_width, hidden_width)],
                        save_sems.at[slot, 3 * side + j],
                    )
                )
        found.append(
            pltpu.make_async_copy(down_g.at[slot], packed_grad.at[:, 2, e], save_sems.at[slot, 6])
        )
        return found

    carries = (
        block_copies(grads_in, grads, carry_sems, 0, pl.ds(0, width))
        + block_copies(blocks_in, rows, carry_sems, grad_blocks, pl.ds(0, width))
        + block_copies(
            blocks_in, gates, carry_sems, grad_blocks + row_blocks, pl.ds(width, lanes)
        )
    )
    sums = []
    if carried:
        at = grad_blocks + 2 * row_blocks
        sums = [
            pltpu.make_async_copy(mix_in, mix, carry_sems.at[at]),
            pltpu.make_async_copy(turn_in, turned, carry_sems.at[at + 1]),
        ]
    for copy in loads(0) + carries + sums:
        copy.start()
    for e in range(count):
        slot = e % 2
        if e + 1 < count:
            for copy in loads(e + 1):
                copy.start()
        for copy in loads(e):
            copy.wait()
        if e == 0:
            for copy in carries:
                copy.wait()
            if not carried:
                turned[:, width:] = jnp.zeros((total_rows, lanes), jnp.float32)

        @pl.loop(0, total_rows // row_tile)
        def _(tile):
            span = pl.ds(pl.multiple_of(tile * row_tile, row_tile), row_tile)
            gate_full = gate_w[slot].reshape(width, hidden_width)
            up_full = up_w[slot].reshape(width, hidden_width)
            down_full = down_w[slot].reshape(hidden_width, width)
            here = rows[span, :]
            slope = dot_right(grads[span, :], down_full)
            gate_pre = dot_plain(here, gate_full)
            up_pre = dot_plain(here, up_full)
            lane = lax.broadcasted_iota(jnp.int32, (row_tile, lanes), 1)
            chosen = lane == first[0] + e
            gate_column = jnp.sum(
                jnp.where(chosen, gates[span, :].astype(jnp.float32), 0.0), axis=1, keepdims=True
            )
            sigmoid_gate = jax.nn.sigmoid(gate_pre)
            activated = gate_pre * sigmoid_gate
            hidden = (activated * up_pre).astype(low).astype(jnp.float32)
            share = jnp.sum(hidden * slope, axis=1, keepdims=True)
            if e == 0 and sums:

                @pl.when(tile == 0)
                def _():
                    for copy in sums:
                        copy.wait()

            turned[span, width:] = jnp.where(chosen, share, turned[span, width:])
            part_weighted = (hidden * gate_column).astype(low)
            hidden_grad = slope * gate_column
            part_gate = (
                hidden_grad * up_pre * (sigmoid_gate + activated * (1.0 - sigmoid_gate))
            ).astype(low)
            part_up = (hidden_grad * activated).astype(low)
            weighted[span, :] = part_weighted
            gate_side[span, :] = part_gate
            up_side[span, :] = part_up
            mix_part = dot_plain(part_weighted, down_full)
            turn_part = dot_right(part_gate, gate_full) + dot_right(part_up, up_full)
            if e == 0 and not carried:
                mix[span, :] = mix_part
                turned[span, :width] = turn_part
            else:
                mix[span, :] += mix_part
                turned[span, :width] += turn_part

        if e >= 2:
            for copy in saves(e - 2):
                copy.wait()
        down_g[slot] = dot_left(weighted[...], grads[...]).astype(low).reshape(down_g.shape[1:])
        gate_g[slot] = dot_left(rows[...], gate_side[...]).astype(low).reshape(gate_g.shape[1:])
        up_g[slot] = dot_left(rows[...], up_side[...]).astype(low).reshape(up_g.shape[1:])
        for copy in saves(e):
            copy.start()
    for e in range(max(0, count - 2), count):
        for copy in saves(e):
            copy.wait()


def expert_pass(first, rows, grads, packed, carry=None):
    blocks, _, count, part, width = packed.shape
    hidden_width = blocks * part
    total_rows = sum(block.shape[0] for block in rows)
    lanes = rows[0].shape[1] - width
    low = jnp.bfloat16
    carried = carry is not None
    flops = 18 * total_rows * count * hidden_width * width
    sides = [
        pltpu.VMEM((2, blocks, 3, part, hidden_width), low),
        pltpu.VMEM((2, blocks, 3, part, hidden_width), low),
        pltpu.VMEM((2, blocks, part, width), low),
    ]
    return pl.pallas_call(
        partial(expert_kernel, carried, len(rows), len(grads), min(512, total_rows)),
        in_specs=[SCALARS] + [ANYWHERE] * (1 + len(rows) + len(grads) + (2 if carried else 0)),
        out_specs=[ANYWHERE, INSIDE, INSIDE],
        out_shape=[
            jax.ShapeDtypeStruct(packed.shape, low),
            jax.ShapeDtypeStruct((total_rows, width), jnp.float32),
            jax.ShapeDtypeStruct((total_rows, width + lanes), jnp.float32),
        ],
        scratch_shapes=[
            pltpu.VMEM((total_rows, width), low),
            pltpu.VMEM((total_rows, width), low),
            pltpu.VMEM((total_rows, lanes), low),
        ]
        + sides
        + sides
        + [pltpu.VMEM((total_rows, hidden_width), low)] * 3
        + [
            pltpu.SemaphoreType.DMA((2, 7)),
            pltpu.SemaphoreType.DMA((2, 7)),
            pltpu.SemaphoreType.DMA((2 * len(rows) + len(grads) + 2,)),
        ],
        compiler_params=pltpu.CompilerParams(vmem_limit_bytes=VMEM_BYTES),
        cost_estimate=cost(flops, packed, packed, *rows, *grads),
        name="experts",
    )(first, packed, *rows, *grads, *(carry or ()))


def unpack_kernel(chunks, *refs):
    found, (gate, up, down) = refs[:chunks], refs[chunks:]
    hidden_width = gate.shape[2]
    base = 0
    for chunk in found:
        count, part = chunk.shape[1], chunk.shape[2]
        for e in range(count):
            for side, target in ((0, gate), (1, up)):
                for j in range(3):
                    target[base + e, j * part : (j + 1) * part, :] = chunk[
                        side, e, :, j * hidden_width : (j + 1) * hidden_width
                    ].astype(jnp.float32)
            down[base + e] = chunk[2, e].astype(jnp.float32)
        base += count


def unpack(chunks, gate_shape, down_shape):
    return pl.pallas_call(
        partial(unpack_kernel, len(chunks)),
        in_specs=[INSIDE] * len(chunks),
        out_specs=[INSIDE] * 3,
        out_shape=[
            jax.ShapeDtypeStruct(gate_shape, jnp.float32),
            jax.ShapeDtypeStruct(gate_shape, jnp.float32),
            jax.ShapeDtypeStruct(down_shape, jnp.float32),
        ],
        compiler_params=pltpu.CompilerParams(vmem_limit_bytes=VMEM_BYTES),
        cost_estimate=cost(0, *chunks, *chunks, *chunks),
        name="unpack",
    )(*chunks)


def cube():
    return lax.axis_size("batch") == 8 and lax.axis_size("expert") == 4


def pair_moves(size, flip):
    return [(i, i ^ flip) for i in range(size)]


def shift_moves(step):
    return [(2 * z + c, 2 * ((z + step) % 4) + c) for z in range(4) for c in range(2)]


def gather_blocks(rows):
    size = lax.axis_size("expert")
    if size != 4:
        stacked = lax.all_gather(rows, "expert", axis=0)
        own = lax.axis_index("expert")
        return [
            lax.dynamic_index_in_dim(stacked, own ^ r, axis=0, keepdims=False) for r in range(size)
        ]
    across, along = pair_moves(size, 1), pair_moves(size, 2)
    half = rows.shape[0] // 2
    first = lax.ppermute(rows, "expert", across)
    second = lax.ppermute(rows, "expert", along)
    top = lax.ppermute(second[:half], "expert", across)
    bottom = lax.ppermute(first[half:], "expert", along)
    return [rows, first, second, top, bottom]


def scatter_blocks(parts):
    size = lax.axis_size("expert")
    low = jnp.bfloat16
    wide = jnp.float32
    if size != 4:
        own = lax.axis_index("expert")
        order = jnp.arange(size, dtype=jnp.int32) ^ own
        stacked = jnp.take(jnp.stack(parts), order, axis=0).astype(low)
        return lax.psum_scatter(stacked, "expert", scatter_dimension=0).astype(wide)
    across, along = pair_moves(size, 1), pair_moves(size, 2)
    half = parts[0].shape[0] // 2
    top = lax.ppermute(parts[3][:half].astype(low), "expert", across)
    bottom = lax.ppermute(parts[3][half:].astype(low), "expert", along)
    first_top = lax.ppermute(parts[1][:half].astype(low), "expert", across)
    second_bottom = lax.ppermute(parts[2][half:].astype(low), "expert", along)
    for_second = (parts[2][:half].astype(wide) + top.astype(wide)).astype(low)
    for_first = (parts[1][half:].astype(wide) + bottom.astype(wide)).astype(low)
    second_top = lax.ppermute(for_second, "expert", along)
    first_bottom = lax.ppermute(for_first, "expert", across)
    own = parts[0].astype(wide)
    return jnp.concatenate(
        [
            own[:half] + first_top.astype(wide) + second_top.astype(wide),
            own[half:] + first_bottom.astype(wide) + second_bottom.astype(wide),
        ],
        axis=0,
    )


def after(values, events):
    return lax.optimization_barrier((values, events))[0]


def gather_dense(rows, events):
    if not cube():
        whole = lax.all_gather(rows, ("batch", "expert"), axis=0, tiled=True)
        return [whole[None]], jnp.zeros((1, 1), jnp.int32), [whole], [whole]
    place = lax.axis_index("batch")
    level, core = place // 2, place % 2
    member = lax.axis_index("expert")
    line = [rows] + [lax.ppermute(rows, "batch", shift_moves(r)) for r in range(1, 4)]
    mine = gather_blocks(after(jnp.stack(line), events))
    plane = mine[1:3]
    mine = mine[:3] + [jnp.concatenate(mine[3:], axis=0)]
    other = [lax.ppermute(block, "batch", pair_moves(8, 1)) for block in mine]
    spots = [
        [(((level + 4 - k) % 4) * 2 + (core ^ c)) * 4 + (member ^ r) for k in range(4)]
        for c in range(2)
        for r in range(4)
    ]
    return mine + other, jnp.array(spots, jnp.int32), line[1:], plane


def scatter_dense(found):
    low = jnp.bfloat16
    wide = jnp.float32
    if not cube():
        values = found[0].reshape(found[0].shape[3:])
        total = lax.psum_scatter(values, ("batch", "expert"), scatter_dimension=0, tiled=True)
        return total.astype(wide)
    level = lax.axis_index("batch") // 2
    received = {r: lax.ppermute(found[r], "batch", pair_moves(8, 1)) for r in (3, 1, 2, 0)}
    parts = [found[4 + r].astype(wide) + received[r].astype(wide) for r in range(4)]
    plane = scatter_blocks(parts)
    total = lax.dynamic_index_in_dim(plane, level, axis=0, keepdims=False)
    for r in range(1, 4):
        sent = lax.dynamic_index_in_dim(plane, (level + r) % 4, axis=0, keepdims=False)
        total += lax.ppermute(sent.astype(low), "batch", shift_moves(r)).astype(wide)
    return total


def pack_sides(gate, up, down):
    def fold(values):
        count, depth, width = values.shape
        return values.reshape(count, 3, depth // 3, width).transpose(0, 2, 1, 3).reshape(down.shape)

    return jnp.stack([fold(gate), fold(up), down], axis=0)


def local(
    tokens,
    cotangent,
    attn_gain,
    query_weight,
    key_weight,
    value_weight,
    out_weight,
    ffn_gain,
    router_weight,
    gate_weight,
    up_weight,
    down_weight,
    routes,
    ranking,
):
    low = jnp.bfloat16
    wide = jnp.float32
    query_width = HEADS * HEAD_DIM
    kv_width = KV_HEADS * HEAD_DIM
    qkv_width = query_width + 2 * kv_width
    width = tokens.shape[2]
    experts_total = router_weight.shape[1]
    extra = -(-(experts_total + 2) // 128) * 128
    first_gain, second_gain = experts_total, experts_total + 1
    local_experts = gate_weight.shape[0]
    member_count = lax.axis_size("expert")
    member_id = lax.axis_index("expert")
    local_rows = tokens.shape[1]
    group_rows = local_rows * member_count
    cut = cube()
    place = jnp.stack([lax.axis_index("batch") % 2, member_id]).astype(jnp.int32)

    route_rows = routes[0]
    rank_rows = ranking[0]
    expert_lanes = jnp.arange(extra, dtype=jnp.int32)
    member = jnp.any(route_rows[:, :, None] == expert_lanes[None, None, :], axis=1)
    marks = jnp.where(
        expert_lanes[None, :] == experts_total,
        (rank_rows // 32)[:, None],
        jnp.where(expert_lanes[None, :] == experts_total + 1, (rank_rows % 32)[:, None], member),
    ).astype(low)
    grad_out = cotangent[0]
    grad_blocks = gather_blocks(jnp.concatenate([grad_out, marks], axis=1))
    marks_all = jnp.concatenate([block[:, width:] for block in grad_blocks], axis=0)

    qkv_pieces, qkv_spots, line, _ = gather_dense(
        jnp.concatenate(
            [
                query_weight,
                key_weight,
                value_weight,
                router_weight,
                attn_gain[:, None],
                ffn_gain[:, None],
                jnp.zeros((query_weight.shape[0], extra - experts_total - 2), low),
            ],
            axis=1,
        ),
        grad_blocks[3:],
    )
    out_pieces, out_spots, out_line, out_plane = gather_dense(after(out_weight, line), ())
    chunks = (0, 2, local_experts)
    packed_all = []
    for a, b in zip(chunks[:-1], chunks[1:]):
        sides = (gate_weight[a:b], up_weight[a:b], down_weight[a:b])
        if a > 0 and cut:
            sides = after(sides, line[0])
        packed_all.append(lax.all_gather(pack_sides(*sides), "batch", axis=0))

    row_ids = member_id * local_rows + jnp.arange(local_rows, dtype=jnp.int32)
    half_dim = HEAD_DIM // 2
    frequency = THETA ** (-jnp.arange(half_dim, dtype=wide) / half_dim)
    angles = place_of(row_ids).astype(wide)[:, None] * frequency[None, :]
    cosine = jnp.tile(jnp.cos(angles), (1, 4))
    sine_part = jnp.tile(jnp.concatenate([-jnp.sin(angles), jnp.sin(angles)], axis=1), (1, 2))
    first_rows = after(tokens[0], out_line)
    normed, query, keyval, small = enter(
        first_rows, cosine, sine_part, qkv_pieces, qkv_spots, first_gain, query_width, kv_width
    )

    rank_all = (
        marks_all[:, experts_total].astype(wide) * 32 + marks_all[:, experts_total + 1].astype(wide)
    )
    earlier = (rank_all[None, :] < rank_rows.astype(wide)[:, None]).astype(low)
    before = product(earlier, marks_all)
    capacity = 5 * group_rows * route_rows.shape[1] // (4 * experts_total)
    member = member.astype(wide)
    kept = jnp.where(before < capacity, member, 0.0)

    keyval_blocks = gather_blocks(after(keyval, out_plane))
    if member_count == 4:
        ordered = keyval_blocks[:3] + [jnp.concatenate(keyval_blocks[3:], axis=0)]
        away = 1 << 20
        keys = jnp.concatenate(
            [
                lax.select_n(member_id, *ordered),
                lax.select_n(member_id ^ 1, *ordered),
                keyval,
            ],
            axis=0,
        )
        starts = [
            jnp.where(member_id >= 1, 0, away),
            jnp.where(member_id >= 2, local_rows, away),
            member_id * local_rows,
        ]
    else:
        keys = jnp.concatenate(keyval_blocks, axis=0)
        starts = [(member_id ^ r) * local_rows for r in range(member_count)]
    key_ids = jnp.concatenate([s + jnp.arange(local_rows, dtype=jnp.int32) for s in starts])
    bias = jnp.where(visible(row_ids, key_ids), 0.0, -1e30).astype(wide)
    attended, log_totals, residual, sent, gate_rows = attend(
        query, keys, bias, tokens[0], small, member, kept, second_gain, out_pieces, out_spots
    )
    sent_blocks = gather_blocks(sent)

    carry, chunk_grads = None, []
    for packed, a in zip(packed_all, chunks):
        first = (member_id * local_experts + a).astype(jnp.int32).reshape(1)
        packed_grad, mixture_all, row_grad = expert_pass(
            first, sent_blocks, grad_blocks, packed, carry
        )
        carry = (mixture_all, row_grad)
        chunk_grads.append(packed_grad)

    def blocks_of(values):
        return [values[r * local_rows : (r + 1) * local_rows] for r in range(member_count)]

    normed_grad = scatter_blocks(blocks_of(row_grad))
    turned = turn(
        place,
        out_spots,
        (
            normed_grad,
            residual,
            grad_out,
            small,
            gate_rows,
            member,
            kept,
            sent,
            attended,
            query,
            keys,
            bias.T,
            log_totals,
            cosine,
            sine_part,
        ),
        out_pieces,
        cut,
        second_gain,
    )
    out_found = turned[:-3]
    resid_grad, query_grad, key_grads = turned[-3:]
    totals = [lax.psum_scatter(chunk_grads[0], "batch", scatter_dimension=0)]
    for packed_grad in chunk_grads[1:]:
        packed_grad = after(packed_grad, (totals[-1], resid_grad))
        totals.append(lax.psum_scatter(packed_grad, "batch", scatter_dimension=0))
    if member_count == 4:
        zero = jnp.zeros((), low)
        for_first, for_second, for_own = blocks_of(key_grads)[:3]
        key_parts = []
        for r in range(4):
            part = jnp.where(member_id == r, for_first, zero)
            part += jnp.where(member_id ^ 1 == r, for_second, zero)
            key_parts.append(part + for_own if r == 0 else part)
    else:
        key_parts = blocks_of(key_grads)
    keyval_sum = scatter_blocks(key_parts)
    left = leave(
        place,
        qkv_spots,
        (
            keyval_sum,
            query_grad,
            normed,
            tokens[0],
            resid_grad,
            small,
            cosine,
            sine_part,
        ),
        qkv_pieces,
        cut,
        first_gain,
    )
    qkv_found, input_grad = left[:-1], left[-1]
    mixture = scatter_blocks(blocks_of(after(mixture_all, keyval_sum)))
    result = (residual + mixture).astype(low)
    out_sum = scatter_dense(out_found)
    qkv_sum = scatter_dense(qkv_found)
    gate_total, up_total, down_total = unpack(totals, gate_weight.shape, down_weight.shape)
    return (
        result[None],
        input_grad[None],
        qkv_sum[:, qkv_width + first_gain],
        qkv_sum[:, :query_width],
        qkv_sum[:, query_width : query_width + kv_width],
        qkv_sum[:, query_width + kv_width : qkv_width],
        out_sum[:, :width],
        out_sum[:, width + second_gain],
        out_sum[:, width : width + experts_total],
        gate_total,
        up_total,
        down_total,
    )


def solution(mesh):
    return jax.shard_map(
        local,
        mesh=mesh,
        in_specs=(
            P("batch", "expert", None),
            P("batch", "expert", None),
            P(("batch", "expert")),
            P(("batch", "expert"), None),
            P(("batch", "expert"), None),
            P(("batch", "expert"), None),
            P(("batch", "expert"), None),
            P(("batch", "expert")),
            P(("batch", "expert"), None),
            P("expert", "batch", None),
            P("expert", "batch", None),
            P("expert", "batch", None),
            P("batch", "expert", None),
            P("batch", "expert"),
        ),
        out_specs=(
            P("batch", "expert", None),
            P("batch", "expert", None),
            P(("batch", "expert")),
            P(("batch", "expert"), None),
            P(("batch", "expert"), None),
            P(("batch", "expert"), None),
            P(("batch", "expert"), None),
            P(("batch", "expert")),
            P(("batch", "expert"), None),
            P("expert", "batch", None),
            P("expert", "batch", None),
            P("expert", "batch", None),
        ),
        check_vma=False,
    )
```

```python
from functools import partial

import jax
import jax.numpy as jnp
from jax import lax
from jax.experimental import pallas as pl
from jax.experimental.pallas import tpu as pltpu
from jax.sharding import PartitionSpec as P

HEADS = 24
KV_HEADS = 8
HEAD_DIM = 64
PROMPT = 512
CLEN = 256


EPS = 1e-06
THETA = 10000.0


def product(left, right):
    return jnp.dot(left, right, preferred_element_type=jnp.float32)


def place_of(row_ids):
    return jnp.where(row_ids < PROMPT, row_ids, PROMPT + (row_ids - PROMPT) % CLEN)


def visible(query_ids, key_ids):
    causal = key_ids[None, :] <= query_ids[:, None]
    same_run = (key_ids[None, :] - PROMPT) // CLEN == (query_ids[:, None] - PROMPT) // CLEN
    return causal & ((key_ids[None, :] < PROMPT) | same_run)


def dot_plain(left, right):
    return lax.dot_general(left, right, (((1,), (0,)), ((), ())), preferred_element_type=jnp.float32)


def dot_right(left, right):
    return lax.dot_general(left, right, (((1,), (1,)), ((), ())), preferred_element_type=jnp.float32)


def dot_left(left, right):
    return lax.dot_general(left, right, (((0,), (0,)), ((), ())), preferred_element_type=jnp.float32)


ANYWHERE = pl.BlockSpec(memory_space=pl.ANY)
INSIDE = pl.BlockSpec(memory_space=pltpu.VMEM)
SCALARS = pl.BlockSpec(memory_space=pltpu.SMEM)
VMEM_BYTES = 60 * 1024 * 1024


def cost(flops, *arrays):
    return pl.CostEstimate(flops=1, bytes_accessed=1, transcendentals=0)


def weight_copies(spots, pieces, target, sems):
    copies = []
    for p, piece in enumerate(pieces):
        blocks, rows = piece.shape[0], piece.shape[1]
        for k in range(blocks):
            place = pl.multiple_of(spots[p, k] * rows, rows)
            copies.append(
                pltpu.make_async_copy(
                    piece.at[k], target.at[pl.ds(place, rows)], sems.at[p * blocks + k]
                )
            )
    return copies


def block_copies(blocks, target, sems, first, columns=None):
    copies = []
    start = 0
    for i, block in enumerate(blocks):
        rows = block.shape[0]
        source = block if columns is None else block.at[:, columns]
        copies.append(
            pltpu.make_async_copy(source, target.at[pl.ds(start, rows)], sems.at[first + i])
        )
        start += rows
    return copies


def swap_halves(values):
    half = HEAD_DIM // 2
    lane = lax.broadcasted_iota(jnp.int32, values.shape, 1)
    return jnp.where(
        lane % HEAD_DIM < half,
        pltpu.roll(values, 2 * HEAD_DIM - half, 1),
        pltpu.roll(values, half, 1),
    )


def mean_square_scale(values):
    return lax.rsqrt(jnp.mean(values * values, axis=-1, keepdims=True) + EPS)


def enter_kernel(count, gain_at, spots, tokens, cosine, sine, *refs):
    pieces = refs[:count]
    normed, query, keyval, small, weight, sems = refs[count:]
    low = jnp.bfloat16
    copies = weight_copies(spots, pieces, weight, sems)
    for copy in copies:
        copy.start()
    inputs = tokens[...].astype(jnp.float32)
    scaled = inputs * mean_square_scale(inputs)
    for copy in copies:
        copy.wait()
    query_width = query.shape[1]
    kv_width = keyval.shape[1] // 2
    qkv_width = query_width + 2 * kv_width
    turned = weight[:, qkv_width:].astype(jnp.float32).T
    small[...] = turned
    rows = (scaled * turned[gain_at : gain_at + 1]).astype(low)
    normed[...] = rows
    pair = 2 * HEAD_DIM
    scale = HEAD_DIM**-0.5
    for start in range(0, query_width + kv_width, 512):
        product_part = dot_plain(rows, weight[:, start : start + 512])
        for offset in range(0, 512, pair):
            part = product_part[:, offset : offset + pair]
            part = part * cosine[...] + swap_halves(part) * sine[...]
            at = start + offset
            if at < query_width:
                query[:, at : at + pair] = (part * scale).astype(low)
            else:
                keyval[:, at - query_width : at - query_width + pair] = part.astype(low)
    keyval[:, kv_width:] = dot_plain(
        rows, weight[:, query_width + kv_width : qkv_width]
    ).astype(low)


def enter(tokens, cosine, sine, pieces, spots, gain_at, query_width, kv_width):
    rows, width = tokens.shape
    columns = pieces[0].shape[2]
    low = jnp.bfloat16
    return pl.pallas_call(
        partial(enter_kernel, len(pieces), gain_at),
        in_specs=[SCALARS, INSIDE, INSIDE, INSIDE] + [ANYWHERE] * len(pieces),
        out_specs=[INSIDE] * 4,
        out_shape=[
            jax.ShapeDtypeStruct((rows, width), low),
            jax.ShapeDtypeStruct((rows, query_width), low),
            jax.ShapeDtypeStruct((rows, 2 * kv_width), low),
            jax.ShapeDtypeStruct((columns - query_width - 2 * kv_width, width), jnp.float32),
        ],
        scratch_shapes=[
            pltpu.VMEM((width, columns), low),
            pltpu.SemaphoreType.DMA((len(pieces) * pieces[0].shape[0],)),
        ],
        compiler_params=pltpu.CompilerParams(vmem_limit_bytes=VMEM_BYTES),
        cost_estimate=cost(2 * rows * width * columns, *pieces),
        name="enter",
    )(spots, tokens, cosine, sine, *pieces)


def both_places(values):
    wide = values.astype(jnp.float32)
    low_lane = lax.broadcasted_iota(jnp.int32, values.shape, 1) < HEAD_DIM
    moved = pltpu.roll(wide, HEAD_DIM, 1)
    kind = values.dtype
    return [
        [jnp.where(low_lane, wide, 0.0).astype(kind), jnp.where(low_lane, 0.0, moved).astype(kind)],
        [jnp.where(low_lane, moved, 0.0).astype(kind), jnp.where(low_lane, 0.0, wide).astype(kind)],
    ]


def attend_kernel(
    count, query, keyval, bias, tokens, small, member, kept, gain_at, spots, *refs
):
    pieces = refs[:count]
    attended, log_totals, residual, sent, gate_rows, weight, sems = refs[count:]
    low = jnp.bfloat16
    rows = query.shape[0]
    width = tokens.shape[1]
    kv_width = keyval.shape[1] // 2
    pair_lanes = 2 * HEAD_DIM
    repeat = HEADS // KV_HEADS
    copies = weight_copies(spots, pieces, weight, sems)
    for copy in copies:
        copy.start()
    log_totals[...] = jnp.zeros_like(log_totals)
    lane = lax.broadcasted_iota(jnp.int32, log_totals.shape, 1)

    @pl.loop(0, KV_HEADS // 2)
    def _(pair):
        at = pl.ds(pl.multiple_of(pair * pair_lanes, pair_lanes), pair_lanes)
        keys = both_places(keyval[:, at])
        at = pl.ds(pl.multiple_of(kv_width + pair * pair_lanes, pair_lanes), pair_lanes)
        values = both_places(keyval[:, at])
        for i in range(repeat):
            at = pl.ds(pl.multiple_of((pair * repeat + i) * pair_lanes, pair_lanes), pair_lanes)
            queries = query[:, at]
            total = jnp.zeros((rows, pair_lanes), jnp.float32)
            for a in range(2):
                head = 2 * i + a
                scores = dot_right(queries, keys[head // repeat][a]) + bias[...]
                peak = jnp.max(scores, axis=-1, keepdims=True)
                lifted = jnp.exp(scores - peak)
                row_total = jnp.sum(lifted, axis=-1, keepdims=True)
                weights_low = (lifted * (1.0 / row_total)).astype(low)
                total += dot_plain(weights_low, values[head // repeat][a])
                log_totals[...] = jnp.where(
                    lane == pair * (2 * repeat) + head, peak + jnp.log(row_total), log_totals[...]
                )
            attended[:, at] = total.astype(low)

    for copy in copies:
        copy.wait()
    hidden = tokens[...].astype(jnp.float32) + dot_plain(attended[...], weight[...])
    residual[...] = hidden
    gain = small[gain_at : gain_at + 1, :]
    normed = (hidden * mean_square_scale(hidden) * gain).astype(low)
    logits = dot_right(normed, small[...].astype(low))
    chosen = member[...] > 0.0
    logits = jnp.where(chosen, logits, -1e30)
    lifted = jnp.where(chosen, jnp.exp(logits - jnp.max(logits, axis=-1, keepdims=True)), 0.0)
    gates = lifted / jnp.sum(lifted, axis=-1, keepdims=True)
    gate_rows[...] = gates
    sent[:, :width] = normed
    sent[:, width:] = (gates * kept[...]).astype(low)


def attend(query, keyval, bias, tokens, small, member, kept, gain_at, pieces, spots):
    rows, width = tokens.shape
    query_width = query.shape[1]
    lanes = small.shape[0]
    low = jnp.bfloat16

    def kernel(*refs):
        attend_kernel(len(pieces), *refs[:7], gain_at, *refs[7:])

    return pl.pallas_call(
        kernel,
        in_specs=[INSIDE] * 7 + [SCALARS] + [ANYWHERE] * len(pieces),
        out_specs=[INSIDE] * 5,
        out_shape=[
            jax.ShapeDtypeStruct((rows, query_width), low),
            jax.ShapeDtypeStruct((rows, 128), jnp.float32),
            jax.ShapeDtypeStruct((rows, width), jnp.float32),
            jax.ShapeDtypeStruct((rows, width + lanes), low),
            jax.ShapeDtypeStruct((rows, lanes), jnp.float32),
        ],
        scratch_shapes=[
            pltpu.VMEM((query_width, width), low),
            pltpu.SemaphoreType.DMA((len(pieces) * pieces[0].shape[0],)),
        ],
        compiler_params=pltpu.CompilerParams(vmem_limit_bytes=VMEM_BYTES),
        cost_estimate=cost(2 * rows * width * width + 8 * rows * query_width * bias.shape[1], *pieces),
        name="attend",
    )(query, keyval, bias, tokens, small, member, kept, spots, *pieces)


def sorted_copies(place, source, others, own, sems):
    core, member = place[0], place[1]
    copies = []
    for r, (other, mine) in enumerate(zip(others, own)):
        copies.append(
            pltpu.make_async_copy(source.at[:, 1 - core, member ^ r], other, sems.at[2 * r])
        )
        copies.append(
            pltpu.make_async_copy(source.at[:, core, member ^ r], mine, sems.at[2 * r + 1])
        )
    return copies


def grad_shapes(cut, rows, columns):
    low = jnp.bfloat16
    if cut:
        block = rows // 32
        return (
            [jax.ShapeDtypeStruct((4, block, columns), low)] * 8,
            pltpu.VMEM((4, 2, 4, block, columns), low),
        )
    return (
        [jax.ShapeDtypeStruct((1, 1, 1, rows, columns), low)],
        pltpu.VMEM((1, 1, 1, rows, columns), low),
    )


def grad_copies(cut, place, source, outs, sems):
    if cut:
        return sorted_copies(place, source, outs[:4], outs[4:], sems)
    return [pltpu.make_async_copy(source, outs[0], sems.at[0])]


def turn_kernel(
    count,
    cut,
    gain_at,
    place,
    spots,
    normed_grad,
    residual,
    grad_out,
    small,
    gate_rows,
    member,
    kept,
    normed,
    attended,
    *refs,
):
    pieces = refs[:count]
    refs = refs[count:]
    outs = refs[: (8 if cut else 1)]
    resid_grad, head_grad, weight, weight_grad, sems, out_sems = refs[len(outs) :]
    low = jnp.bfloat16
    rows, width = residual.shape
    lanes = gate_rows.shape[1]
    copies = weight_copies(spots, pieces, weight, sems)
    for copy in copies:
        copy.start()
    lane = lax.broadcasted_iota(jnp.int32, (rows, lanes), 1)
    gates = gate_rows[...]
    gate_grads = normed_grad[:, width:] * kept[...]
    chosen_grad = gates * (gate_grads - jnp.sum(gates * gate_grads, axis=-1, keepdims=True))
    logit_grad = (chosen_grad * member[...]).astype(low)
    hidden = residual[...]
    scale = mean_square_scale(hidden)
    row_grad = normed_grad[:, :width] + dot_plain(logit_grad, small[...].astype(low))
    gain = small[gain_at : gain_at + 1, :]
    scaled = row_grad * gain
    total_grad = (
        grad_out[...].astype(jnp.float32)
        + scale * scaled
        - hidden * (scale * scale * scale) * jnp.mean(scaled * hidden, axis=-1, keepdims=True)
    )
    resid_grad[...] = total_grad
    attn_grad = total_grad.astype(low)
    shape = weight_grad.shape[:-1]
    gain_grad = (row_grad * hidden * scale).astype(low)
    picks = jnp.where(lane == gain_at, 1.0, 0.0).astype(low)
    weight_grad[..., width:] = (
        (dot_left(normed[...][:, :width], logit_grad) + dot_left(gain_grad, picks))
        .astype(low)
        .reshape(shape + (lanes,))
    )
    for start in range(0, width, 512):
        weight_grad[..., start : start + 512] = (
            dot_left(attended[...], attn_grad[:, start : start + 512])
            .astype(low)
            .reshape(shape + (512,))
        )
    out_copies = grad_copies(cut, place, weight_grad, outs, out_sems)
    for copy in out_copies:
        copy.start()
    for copy in copies:
        copy.wait()
    head_grad[...] = dot_right(attn_grad, weight[...]).astype(low)
    for copy in out_copies:
        copy.wait()


def turn(place, spots, operands, pieces, cut, gain_at):
    residual, gate_rows, attended = operands[1], operands[4], operands[8]
    rows, width = residual.shape
    query_width = attended.shape[1]
    low = jnp.bfloat16
    grads, held = grad_shapes(cut, query_width, width + gate_rows.shape[1])
    return pl.pallas_call(
        partial(turn_kernel, len(pieces), cut, gain_at),
        in_specs=[SCALARS, SCALARS] + [INSIDE] * len(operands) + [ANYWHERE] * len(pieces),
        out_specs=[ANYWHERE] * len(grads) + [INSIDE] * 2,
        out_shape=grads
        + [
            jax.ShapeDtypeStruct((rows, width), jnp.float32),
            jax.ShapeDtypeStruct((rows, query_width), low),
        ],
        scratch_shapes=[
            pltpu.VMEM((query_width, width), low),
            held,
            pltpu.SemaphoreType.DMA((len(pieces) * pieces[0].shape[0],)),
            pltpu.SemaphoreType.DMA((8,)),
        ],
        compiler_params=pltpu.CompilerParams(vmem_limit_bytes=VMEM_BYTES),
        cost_estimate=cost(4 * rows * width * width, *pieces, *pieces),
        name="turn",
    )(place, spots, *operands, *pieces)


def attend_back_kernel(
    head_grad, query, keyval, bias, log_totals, cosine, sine, query_grad, keyval_grad, totals
):
    low = jnp.bfloat16
    rows = query.shape[0]
    kv_width = keyval.shape[1] // 2
    pair_lanes = 2 * HEAD_DIM
    repeat = HEADS // KV_HEADS
    totals[...] = log_totals[...].T

    @pl.loop(0, KV_HEADS // 2)
    def _(pair):
        key_at = pl.ds(pl.multiple_of(pair * pair_lanes, pair_lanes), pair_lanes)
        value_at = pl.ds(pl.multiple_of(kv_width + pair * pair_lanes, pair_lanes), pair_lanes)
        keys = both_places(keyval[:, key_at])
        values = both_places(keyval[:, value_at])
        key_grads = [[None, None], [None, None]]
        value_grads = [[None, None], [None, None]]
        for i in range(repeat):
            at = pl.ds(pl.multiple_of((pair * repeat + i) * pair_lanes, pair_lanes), pair_lanes)
            queries = query[:, at]
            grads = head_grad[:, at]
            query_part = jnp.zeros((rows, pair_lanes), jnp.float32)
            for a in range(2):
                head = 2 * i + a
                g = head // repeat
                total = totals[pl.ds(pair * (2 * repeat) + head, 1), :]
                weights = jnp.exp(dot_right(keys[g][a], queries) + bias[...] - total)
                weight_grads = dot_right(values[g][a], grads)
                delta = jnp.sum(weights * weight_grads, axis=0, keepdims=True)
                score_grads = (weights * (weight_grads - delta)).astype(low)
                value_part = dot_plain(weights.astype(low), grads)
                key_part = dot_plain(score_grads, queries)
                query_part += dot_left(score_grads, keys[g][a])
                if key_grads[g][a] is None:
                    key_grads[g][a], value_grads[g][a] = key_part, value_part
                else:
                    key_grads[g][a] += key_part
                    value_grads[g][a] += value_part
            query_part = query_part * (HEAD_DIM**-0.5)
            query_part = query_part * cosine[...] - swap_halves(query_part) * sine[...]
            query_grad[:, at] = query_part.astype(low)
        low_lane = lax.broadcasted_iota(jnp.int32, (keyval.shape[0], pair_lanes), 1) < HEAD_DIM
        for at, found in ((key_at, key_grads), (value_at, value_grads)):
            keyval_grad[:, at] = jnp.where(
                low_lane,
                found[0][0] + pltpu.roll(found[0][1], HEAD_DIM, 1),
                pltpu.roll(found[1][0], HEAD_DIM, 1) + found[1][1],
            ).astype(low)


def attend_back(head_grad, query, keyval, bias, log_totals, cosine, sine):
    rows, query_width = query.shape
    low = jnp.bfloat16
    return pl.pallas_call(
        attend_back_kernel,
        in_specs=[INSIDE] * 7,
        out_specs=[INSIDE] * 2,
        out_shape=[
            jax.ShapeDtypeStruct((rows, query_width), low),
            jax.ShapeDtypeStruct(keyval.shape, low),
        ],
        scratch_shapes=[pltpu.VMEM((128, rows), jnp.float32)],
        compiler_params=pltpu.CompilerParams(vmem_limit_bytes=VMEM_BYTES),
        cost_estimate=cost(20 * rows * query_width * keyval.shape[0], query, keyval, bias),
        name="attend_back",
    )(head_grad, query, keyval, bias, log_totals, cosine, sine)


def leave_kernel(
    count,
    cut,
    gain_at,
    place,
    spots,
    keyval_sum,
    query_grad,
    normed,
    tokens,
    resid_grad,
    small,
    cosine,
    sine,
    *refs,
):
    pieces = refs[:count]
    refs = refs[count:]
    outs = refs[: (8 if cut else 1)]
    input_grad, weight, weight_grad, joined, sems, out_sems = refs[len(outs) :]
    low = jnp.bfloat16
    rows, width = tokens.shape
    query_width = query_grad.shape[1]
    kv_width = keyval_sum.shape[1] // 2
    qkv_width = query_width + 2 * kv_width
    pair = 2 * HEAD_DIM
    copies = weight_copies(spots, pieces, weight, sems)
    for copy in copies:
        copy.start()
    joined[:, :query_width] = query_grad[...]
    for start in range(0, kv_width, pair):
        part = keyval_sum[:, start : start + pair]
        part = part * cosine[...] - swap_halves(part) * sine[...]
        joined[:, query_width + start : query_width + start + pair] = part.astype(low)
    joined[:, query_width + kv_width :] = keyval_sum[:, kv_width:].astype(low)
    shape = weight_grad.shape[:-1]
    for start in range(0, qkv_width, 512):
        weight_grad[..., start : start + 512] = (
            dot_left(normed[...], joined[:, start : start + 512]).astype(low).reshape(shape + (512,))
        )
    for copy in copies:
        copy.wait()
    row_grad = dot_right(joined[...], weight[:, :qkv_width])
    inputs = tokens[...].astype(jnp.float32)
    scale = mean_square_scale(inputs)
    lanes = weight_grad.shape[-1] - qkv_width
    lane = lax.broadcasted_iota(jnp.int32, (rows, lanes), 1)
    picks = jnp.where(lane == gain_at, 1.0, 0.0).astype(low)
    weight_grad[..., qkv_width:] = (
        dot_left((row_grad * inputs * scale).astype(low), picks).astype(low).reshape(shape + (lanes,))
    )
    out_copies = grad_copies(cut, place, weight_grad, outs, out_sems)
    for copy in out_copies:
        copy.start()
    scaled = row_grad * small[gain_at : gain_at + 1, :]
    input_grad[...] = (
        resid_grad[...]
        + scale * scaled
        - inputs * (scale * scale * scale) * jnp.mean(scaled * inputs, axis=-1, keepdims=True)
    )
    for copy in out_copies:
        copy.wait()


def leave(place, spots, operands, pieces, cut, gain_at):
    tokens, query_grad, keyval_sum = operands[3], operands[1], operands[0]
    rows, width = tokens.shape
    columns = pieces[0].shape[2]
    low = jnp.bfloat16
    grads, held = grad_shapes(cut, width, columns)
    return pl.pallas_call(
        partial(leave_kernel, len(pieces), cut, gain_at),
        in_specs=[SCALARS, SCALARS] + [INSIDE] * len(operands) + [ANYWHERE] * len(pieces),
        out_specs=[ANYWHERE] * len(grads) + [INSIDE],
        out_shape=grads + [jax.ShapeDtypeStruct((rows, width), jnp.float32)],
        scratch_shapes=[
            pltpu.VMEM((width, columns), low),
            held,
            pltpu.VMEM((rows, query_grad.shape[1] + keyval_sum.shape[1]), low),
            pltpu.SemaphoreType.DMA((len(pieces) * pieces[0].shape[0],)),
            pltpu.SemaphoreType.DMA((8,)),
        ],
        compiler_params=pltpu.CompilerParams(vmem_limit_bytes=VMEM_BYTES),
        cost_estimate=cost(4 * rows * width * columns, *pieces, *pieces),
        name="leave",
    )(place, spots, *operands, *pieces)


def expert_kernel(sources, carried, last, row_blocks, grad_blocks, row_tile, first, place, *refs):
    packed = refs[:sources]
    refs = refs[sources:]
    blocks_in = refs[:row_blocks]
    grads_in = refs[row_blocks : row_blocks + grad_blocks]
    refs = refs[row_blocks + grad_blocks :]
    if carried:
        mix_in, turn_in = refs[:2]
        refs = refs[2:]
    packed_grads = refs[:sources]
    mix_out, turn_out = refs[sources : sources + 2]
    refs = refs[sources + 2 :]
    if last:
        mix, turned = refs[:2]
        refs = refs[2:]
    else:
        mix, turned = mix_out, turn_out
    (
        rows,
        grads,
        gates,
        gate_w,
        up_w,
        down_w,
        gate_g,
        up_g,
        down_g,
        weighted,
        gate_side,
        up_side,
        load_sems,
        save_sems,
        carry_sems,
    ) = refs
    count = packed[0].shape[2]
    hidden_width = gate_w.shape[-1]
    total_rows, width = rows.shape
    lanes = gates.shape[1]
    low = jnp.bfloat16

    def moves(e, outside, gate, up, down, sems, inward):
        slot = e % 2
        found = []
        for n, array in enumerate(outside):
            core = place[0] ^ n if sources > 1 else 0
            ends = []
            for side, inner in ((0, gate), (1, up)):
                for j in range(3):
                    columns = pl.ds(j * hidden_width, hidden_width)
                    ends.append((array.at[:, side, e, :, columns], inner.at[slot, :, core, j]))
            ends.append((array.at[:, 2, e], down.at[slot, :, core]))
            for i, (outer, inner) in enumerate(ends):
                ends_now = (outer, inner) if inward else (inner, outer)
                found.append(pltpu.make_async_copy(*ends_now, sems.at[slot, 7 * n + i]))
        return found

    def loads(e):
        return moves(e, packed, gate_w, up_w, down_w, load_sems, True)

    def saves(e):
        return moves(e, packed_grads, gate_g, up_g, down_g, save_sems, False)

    carries = (
        block_copies(grads_in, grads, carry_sems, 0, pl.ds(0, width))
        + block_copies(blocks_in, rows, carry_sems, grad_blocks, pl.ds(0, width))
        + block_copies(
            blocks_in, gates, carry_sems, grad_blocks + row_blocks, pl.ds(width, lanes)
        )
    )
    sums = []
    if carried:
        at = grad_blocks + 2 * row_blocks
        sums = [
            pltpu.make_async_copy(mix_in, mix, carry_sems.at[at]),
            pltpu.make_async_copy(turn_in, turned, carry_sems.at[at + 1]),
        ]
    for copy in loads(0) + carries + sums:
        copy.start()
    for e in range(count):
        slot = e % 2
        if e + 1 < count:
            for copy in loads(e + 1):
                copy.start()
        for copy in loads(e):
            copy.wait()
        if e == 0:
            for copy in carries:
                copy.wait()
            if not carried:
                turned[:, width:] = jnp.zeros((total_rows, lanes), jnp.float32)

        @pl.loop(0, total_rows // row_tile)
        def _(tile):
            span = pl.ds(pl.multiple_of(tile * row_tile, row_tile), row_tile)
            gate_full = gate_w[slot].reshape(width, hidden_width)
            up_full = up_w[slot].reshape(width, hidden_width)
            down_full = down_w[slot].reshape(hidden_width, width)
            here = rows[span, :]
            slope = dot_right(grads[span, :], down_full)
            gate_pre = dot_plain(here, gate_full)
            up_pre = dot_plain(here, up_full)
            lane = lax.broadcasted_iota(jnp.int32, (row_tile, lanes), 1)
            chosen = lane == first[0] + e
            gate_column = jnp.sum(
                jnp.where(chosen, gates[span, :].astype(jnp.float32), 0.0), axis=1, keepdims=True
            )
            sigmoid_gate = jax.nn.sigmoid(gate_pre)
            activated = gate_pre * sigmoid_gate
            hidden = (activated * up_pre).astype(low).astype(jnp.float32)
            share = jnp.sum(hidden * slope, axis=1, keepdims=True)
            if e == 0 and sums:

                @pl.when(tile == 0)
                def _():
                    for copy in sums:
                        copy.wait()

            turned[span, width:] = jnp.where(chosen, share, turned[span, width:])
            part_weighted = (hidden * gate_column).astype(low)
            hidden_grad = slope * gate_column
            part_gate = (
                hidden_grad * up_pre * (sigmoid_gate + activated * (1.0 - sigmoid_gate))
            ).astype(low)
            part_up = (hidden_grad * activated).astype(low)
            weighted[span, :] = part_weighted
            gate_side[span, :] = part_gate
            up_side[span, :] = part_up
            mix_part = dot_plain(part_weighted, down_full)
            turn_part = dot_right(part_gate, gate_full) + dot_right(part_up, up_full)
            if e == 0 and not carried:
                mix[span, :] = mix_part
                turned[span, :width] = turn_part
            elif last and e == count - 1:
                mix_out[span, :] = (mix[span, :] + mix_part).astype(low)
                turn_out[span, :width] = (turned[span, :width] + turn_part).astype(low)
                turn_out[span, width:] = turned[span, width:].astype(low)
            else:
                mix[span, :] += mix_part
                turned[span, :width] += turn_part

        if e >= 2:
            for copy in saves(e - 2):
                copy.wait()
        down_g[slot] = dot_left(weighted[...], grads[...]).astype(low).reshape(down_g.shape[1:])
        gate_g[slot] = dot_left(rows[...], gate_side[...]).astype(low).reshape(gate_g.shape[1:])
        up_g[slot] = dot_left(rows[...], up_side[...]).astype(low).reshape(up_g.shape[1:])
        for copy in saves(e):
            copy.start()
    for e in range(max(0, count - 2), count):
        for copy in saves(e):
            copy.wait()


def expert_pass(first, place, rows, grads, packed, carry, last):
    sources = len(packed)
    levels, _, count, part, width = packed[0].shape
    hidden_width = levels * sources * part
    total_rows = sum(block.shape[0] for block in rows)
    lanes = rows[0].shape[1] - width
    low = jnp.bfloat16
    wide = jnp.float32
    carried = carry is not None
    flops = 18 * total_rows * count * hidden_width * width
    side = pltpu.VMEM((2, levels, sources, 3, part, hidden_width), low)
    sides = [side, side, pltpu.VMEM((2, levels, sources, part, width), low)]
    sums = [(total_rows, width), (total_rows, width + lanes)]
    return pl.pallas_call(
        partial(
            expert_kernel, sources, carried, last, len(rows), len(grads), min(512, total_rows)
        ),
        in_specs=[SCALARS, SCALARS]
        + [ANYWHERE] * (sources + len(rows) + len(grads) + (2 if carried else 0)),
        out_specs=[ANYWHERE] * sources + [INSIDE, INSIDE],
        out_shape=[jax.ShapeDtypeStruct(packed[0].shape, low)] * sources
        + [jax.ShapeDtypeStruct(shape, low if last else wide) for shape in sums],
        scratch_shapes=([pltpu.VMEM(shape, wide) for shape in sums] if last else [])
        + [
            pltpu.VMEM((total_rows, width), low),
            pltpu.VMEM((total_rows, width), low),
            pltpu.VMEM((total_rows, lanes), low),
        ]
        + sides
        + sides
        + [pltpu.VMEM((total_rows, hidden_width), low)] * 3
        + [
            pltpu.SemaphoreType.DMA((2, 7 * sources)),
            pltpu.SemaphoreType.DMA((2, 7 * sources)),
            pltpu.SemaphoreType.DMA((2 * len(rows) + len(grads) + 2,)),
        ],
        compiler_params=pltpu.CompilerParams(vmem_limit_bytes=VMEM_BYTES),
        cost_estimate=cost(flops, *packed, *packed, *rows, *grads),
        name="experts",
    )(first, place, *packed, *rows, *grads, *(carry or ()))


def unpack_kernel(chunks, *refs):
    found, (gate, up, down) = refs[:chunks], refs[chunks:]
    hidden_width = gate.shape[2]
    base = 0
    for chunk in found:
        count, part = chunk.shape[1], chunk.shape[2]
        for e in range(count):
            for side, target in ((0, gate), (1, up)):
                for j in range(3):
                    target[base + e, j * part : (j + 1) * part, :] = chunk[
                        side, e, :, j * hidden_width : (j + 1) * hidden_width
                    ].astype(jnp.float32)
            down[base + e] = chunk[2, e].astype(jnp.float32)
        base += count


def unpack(chunks, gate_shape, down_shape):
    return pl.pallas_call(
        partial(unpack_kernel, len(chunks)),
        in_specs=[INSIDE] * len(chunks),
        out_specs=[INSIDE] * 3,
        out_shape=[
            jax.ShapeDtypeStruct(gate_shape, jnp.float32),
            jax.ShapeDtypeStruct(gate_shape, jnp.float32),
            jax.ShapeDtypeStruct(down_shape, jnp.float32),
        ],
        compiler_params=pltpu.CompilerParams(vmem_limit_bytes=VMEM_BYTES),
        cost_estimate=cost(0, *chunks, *chunks, *chunks),
        name="unpack",
    )(*chunks)


def cube():
    return lax.axis_size("batch") == 8 and lax.axis_size("expert") == 4


def pair_moves(size, flip):
    return [(i, i ^ flip) for i in range(size)]


def shift_moves(step):
    return [(2 * z + c, 2 * ((z + step) % 4) + c) for z in range(4) for c in range(2)]


def gather_blocks(rows):
    size = lax.axis_size("expert")
    if size != 4:
        stacked = lax.all_gather(rows, "expert", axis=0)
        own = lax.axis_index("expert")
        return [
            lax.dynamic_index_in_dim(stacked, own ^ r, axis=0, keepdims=False) for r in range(size)
        ]
    across, along = pair_moves(size, 1), pair_moves(size, 2)
    half = rows.shape[0] // 2
    first = lax.ppermute(rows, "expert", across)
    second = lax.ppermute(rows, "expert", along)
    top = lax.ppermute(second[:half], "expert", across)
    bottom = lax.ppermute(first[half:], "expert", along)
    return [rows, first, second, top, bottom]


def scatter_blocks(parts):
    size = lax.axis_size("expert")
    low = jnp.bfloat16
    wide = jnp.float32
    if size != 4:
        own = lax.axis_index("expert")
        order = jnp.arange(size, dtype=jnp.int32) ^ own
        stacked = jnp.take(jnp.stack(parts), order, axis=0).astype(low)
        return lax.psum_scatter(stacked, "expert", scatter_dimension=0).astype(wide)
    across, along = pair_moves(size, 1), pair_moves(size, 2)
    half = parts[0].shape[0] // 2
    top = lax.ppermute(parts[3][:half].astype(low), "expert", across)
    bottom = lax.ppermute(parts[3][half:].astype(low), "expert", along)
    first_top = lax.ppermute(parts[1][:half].astype(low), "expert", across)
    second_bottom = lax.ppermute(parts[2][half:].astype(low), "expert", along)
    for_second = (parts[2][:half].astype(wide) + top.astype(wide)).astype(low)
    for_first = (parts[1][half:].astype(wide) + bottom.astype(wide)).astype(low)
    second_top = lax.ppermute(for_second, "expert", along)
    first_bottom = lax.ppermute(for_first, "expert", across)
    own = parts[0].astype(wide)
    return jnp.concatenate(
        [
            own[:half] + first_top.astype(wide) + second_top.astype(wide),
            own[half:] + first_bottom.astype(wide) + second_bottom.astype(wide),
        ],
        axis=0,
    )


def after(values, events):
    return lax.optimization_barrier((values, events))[0]


def shift_dense(rows):
    if not cube():
        return [lax.all_gather(rows, ("batch", "expert"), axis=0, tiled=True)]
    return [rows] + [lax.ppermute(rows, "batch", shift_moves(r)) for r in range(1, 4)]


def gather_dense(line, columns, events):
    found = [rows[:, columns] for rows in line]
    if not cube():
        return [found[0][None]], jnp.zeros((1, 1), jnp.int32), (), ()
    place = lax.axis_index("batch")
    level, core = place // 2, place % 2
    member = lax.axis_index("expert")
    mine = gather_blocks(after(jnp.stack(found), events))
    plane, far = mine[1:3], mine[3:]
    mine = mine[:3] + [jnp.concatenate(far, axis=0)]
    other = [lax.ppermute(block, "batch", pair_moves(8, 1)) for block in mine]
    spots = [
        [(((level + 4 - k) % 4) * 2 + (core ^ c)) * 4 + (member ^ r) for k in range(4)]
        for c in range(2)
        for r in range(4)
    ]
    return mine + other, jnp.array(spots, jnp.int32), plane, far


LINES = [[2 * z + c for z in range(4)] for c in range(2)]


def gather_experts(packed):
    groups = LINES if cube() else None
    return lax.all_gather(packed, "batch", axis=0, axis_index_groups=groups)


def with_other_core(own, events):
    if not cube():
        return [own]
    return [own, lax.ppermute(after(own, events), "batch", pair_moves(8, 1))]


def join_cores(found):
    if not cube():
        return found[0]
    return found[0] + lax.ppermute(found[1], "batch", pair_moves(8, 1))


def scatter_experts(values):
    groups = LINES if cube() else None
    return lax.psum_scatter(values, "batch", scatter_dimension=0, axis_index_groups=groups)


def scatter_dense(found, events, late):
    low = jnp.bfloat16
    wide = jnp.float32
    if not cube():
        values = found[0].reshape(found[0].shape[3:])
        total = lax.psum_scatter(values, ("batch", "expert"), scatter_dimension=0, tiled=True)
        return total.astype(wide)
    level = lax.axis_index("batch") // 2
    received = {r: lax.ppermute(found[r], "batch", pair_moves(8, 1)) for r in (3, 1, 2, 0)}
    received = after(received, events)
    parts = [found[4 + r].astype(wide) + received[r].astype(wide) for r in range(4)]
    plane = after(scatter_blocks(parts), late)
    total = lax.dynamic_index_in_dim(plane, level, axis=0, keepdims=False)
    for r in range(1, 4):
        sent = lax.dynamic_index_in_dim(plane, (level + r) % 4, axis=0, keepdims=False)
        total += lax.ppermute(sent.astype(low), "batch", shift_moves(r)).astype(wide)
    return total


def pack_sides(gate, up, down):
    def fold(values):
        count, depth, width = values.shape
        return values.reshape(count, 3, depth // 3, width).transpose(0, 2, 1, 3).reshape(down.shape)

    return jnp.stack([fold(gate), fold(up), down], axis=0)


def local(
    tokens,
    cotangent,
    attn_gain,
    query_weight,
    key_weight,
    value_weight,
    out_weight,
    ffn_gain,
    router_weight,
    gate_weight,
    up_weight,
    down_weight,
    routes,
    ranking,
):
    low = jnp.bfloat16
    wide = jnp.float32
    query_width = HEADS * HEAD_DIM
    kv_width = KV_HEADS * HEAD_DIM
    qkv_width = query_width + 2 * kv_width
    width = tokens.shape[2]
    experts_total = router_weight.shape[1]
    extra = -(-(experts_total + 2) // 128) * 128
    first_gain, second_gain = experts_total, experts_total + 1
    local_experts = gate_weight.shape[0]
    member_count = lax.axis_size("expert")
    member_id = lax.axis_index("expert")
    local_rows = tokens.shape[1]
    group_rows = local_rows * member_count
    cut = cube()
    place = jnp.stack([lax.axis_index("batch") % 2, member_id]).astype(jnp.int32)

    route_rows = routes[0]
    rank_rows = ranking[0]
    expert_lanes = jnp.arange(extra, dtype=jnp.int32)
    member = jnp.any(route_rows[:, :, None] == expert_lanes[None, None, :], axis=1)
    marks = jnp.where(
        expert_lanes[None, :] == experts_total,
        (rank_rows // 32)[:, None],
        jnp.where(expert_lanes[None, :] == experts_total + 1, (rank_rows % 32)[:, None], member),
    ).astype(low)
    grad_out = cotangent[0]
    grad_blocks = gather_blocks(jnp.concatenate([grad_out, marks], axis=1))
    marks_all = jnp.concatenate([block[:, width:] for block in grad_blocks], axis=0)

    small_width = qkv_width + extra
    line = shift_dense(
        jnp.concatenate(
            [
                query_weight,
                key_weight,
                value_weight,
                router_weight,
                attn_gain[:, None],
                ffn_gain[:, None],
                jnp.zeros((query_weight.shape[0], extra - experts_total - 2), low),
                out_weight,
            ],
            axis=1,
        )
    )
    qkv_pieces, qkv_spots, plane, far = gather_dense(
        line, slice(0, small_width), grad_blocks[3:]
    )
    out_pieces, out_spots, out_plane, _ = gather_dense(line, slice(small_width, None), far)
    chunks = (0, 3, local_experts)
    packed_all = []
    for a, b in zip(chunks[:-1], chunks[1:]):
        sides = (gate_weight[a:b], up_weight[a:b], down_weight[a:b])
        if cut:
            sides = after(sides, line[1:] if a == 0 else plane)
        packed_all.append(gather_experts(pack_sides(*sides)))

    row_ids = member_id * local_rows + jnp.arange(local_rows, dtype=jnp.int32)
    half_dim = HEAD_DIM // 2
    frequency = THETA ** (-jnp.arange(half_dim, dtype=wide) / half_dim)
    angles = place_of(row_ids).astype(wide)[:, None] * frequency[None, :]
    cosine = jnp.tile(jnp.cos(angles), (1, 4))
    sine_part = jnp.tile(jnp.concatenate([-jnp.sin(angles), jnp.sin(angles)], axis=1), (1, 2))
    normed, query, keyval, small = enter(
        tokens[0], cosine, sine_part, qkv_pieces, qkv_spots, first_gain, query_width, kv_width
    )

    rank_all = (
        marks_all[:, experts_total].astype(wide) * 32 + marks_all[:, experts_total + 1].astype(wide)
    )
    earlier = (rank_all[None, :] < rank_rows.astype(wide)[:, None]).astype(low)
    before = product(earlier, marks_all)
    capacity = 5 * group_rows * route_rows.shape[1] // (4 * experts_total)
    member = member.astype(wide)
    kept = jnp.where(before < capacity, member, 0.0)

    keyval_blocks = gather_blocks(after(keyval, out_plane))
    if member_count == 4:
        ordered = keyval_blocks[:3] + [jnp.concatenate(keyval_blocks[3:], axis=0)]
        away = 1 << 20
        keys = jnp.concatenate(
            [
                lax.select_n(member_id, *ordered),
                lax.select_n(member_id ^ 1, *ordered),
                keyval,
            ],
            axis=0,
        )
        starts = [
            jnp.where(member_id >= 1, 0, away),
            jnp.where(member_id >= 2, local_rows, away),
            member_id * local_rows,
        ]
    else:
        keys = jnp.concatenate(keyval_blocks, axis=0)
        starts = [(member_id ^ r) * local_rows for r in range(member_count)]
    key_ids = jnp.concatenate([s + jnp.arange(local_rows, dtype=jnp.int32) for s in starts])
    bias = jnp.where(visible(row_ids, key_ids), 0.0, -1e30).astype(wide)
    attended, log_totals, residual, sent, gate_rows = attend(
        query, keys, bias, tokens[0], small, member, kept, second_gain, out_pieces, out_spots
    )
    sent_blocks = gather_blocks(sent)

    carry, chunk_grads = None, []
    for packed, a, b in zip(packed_all, chunks[:-1], chunks[1:]):
        first = (member_id * local_experts + a).astype(jnp.int32).reshape(1)
        packed = with_other_core(packed, sent if carry is None else carry)
        if chunk_grads:
            first = after(first, chunk_grads[-1])
        *packed_grads, mixture_all, row_grad = expert_pass(
            first, place, sent_blocks, grad_blocks, packed, carry, b == local_experts
        )
        carry = (mixture_all, row_grad)
        chunk_grads.append(join_cores(packed_grads))

    def blocks_of(values):
        return [values[r * local_rows : (r + 1) * local_rows] for r in range(member_count)]

    normed_grad = scatter_blocks(blocks_of(row_grad))
    turned = turn(
        place,
        out_spots,
        (
            normed_grad,
            residual,
            grad_out,
            small,
            gate_rows,
            member,
            kept,
            sent,
            attended,
        ),
        out_pieces,
        cut,
        second_gain,
    )
    out_found = turned[:-2]
    resid_grad, head_grad = turned[-2:]
    query_grad, key_grads = attend_back(
        head_grad, query, keys, bias.T, log_totals, cosine, sine_part
    )
    totals = [scatter_experts(chunk_grads[0])]
    for chunk_grad in chunk_grads[1:]:
        totals.append(scatter_experts(after(chunk_grad, (totals[-1], query_grad))))
    if member_count == 4:
        zero = jnp.zeros((), low)
        for_first, for_second, for_own = blocks_of(key_grads)[:3]
        key_parts = []
        for r in range(4):
            part = jnp.where(member_id == r, for_first, zero)
            part += jnp.where(member_id ^ 1 == r, for_second, zero)
            key_parts.append(part + for_own if r == 0 else part)
    else:
        key_parts = blocks_of(key_grads)
    keyval_sum = scatter_blocks(key_parts)
    left = leave(
        place,
        qkv_spots,
        (
            keyval_sum,
            query_grad,
            normed,
            tokens[0],
            resid_grad,
            small,
            cosine,
            sine_part,
        ),
        qkv_pieces,
        cut,
        first_gain,
    )
    qkv_found, input_grad = left[:-1], left[-1]
    mixture = scatter_blocks(blocks_of(after(mixture_all, resid_grad)))
    result = (residual + mixture).astype(low)
    out_sum = scatter_dense(out_found, keyval_sum, ())
    qkv_sum = scatter_dense(qkv_found, (), totals)
    gate_total, up_total, down_total = unpack(totals, gate_weight.shape, down_weight.shape)
    return (
        result[None],
        input_grad[None],
        qkv_sum[:, qkv_width + first_gain],
        qkv_sum[:, :query_width],
        qkv_sum[:, query_width : query_width + kv_width],
        qkv_sum[:, query_width + kv_width : qkv_width],
        out_sum[:, :width],
        out_sum[:, width + second_gain],
        out_sum[:, width : width + experts_total],
        gate_total,
        up_total,
        down_total,
    )


def solution(mesh):
    return jax.shard_map(
        local,
        mesh=mesh,
        in_specs=(
            P("batch", "expert", None),
            P("batch", "expert", None),
            P(("batch", "expert")),
            P(("batch", "expert"), None),
            P(("batch", "expert"), None),
            P(("batch", "expert"), None),
            P(("batch", "expert"), None),
            P(("batch", "expert")),
            P(("batch", "expert"), None),
            P("expert", "batch", None),
            P("expert", "batch", None),
            P("expert", "batch", None),
            P("batch", "expert", None),
            P("batch", "expert"),
        ),
        out_specs=(
            P("batch", "expert", None),
            P("batch", "expert", None),
            P(("batch", "expert")),
            P(("batch", "expert"), None),
            P(("batch", "expert"), None),
            P(("batch", "expert"), None),
            P(("batch", "expert"), None),
            P(("batch", "expert")),
            P(("batch", "expert"), None),
            P("expert", "batch", None),
            P("expert", "batch", None),
            P("expert", "batch", None),
        ),
        check_vma=False,
    )
```

```python
from functools import partial

import jax
import jax.numpy as jnp
from jax import lax
from jax.experimental import pallas as pl
from jax.experimental.pallas import tpu as pltpu
from jax.sharding import PartitionSpec as P

HEADS = 24
KV_HEADS = 8
HEAD_DIM = 64
PROMPT = 512
CLEN = 256


EPS = 1e-06
THETA = 10000.0


def product(left, right):
    return jnp.dot(left, right, preferred_element_type=jnp.float32)


def place_of(row_ids):
    return jnp.where(row_ids < PROMPT, row_ids, PROMPT + (row_ids - PROMPT) % CLEN)


def visible(query_ids, key_ids):
    causal = key_ids[None, :] <= query_ids[:, None]
    same_run = (key_ids[None, :] - PROMPT) // CLEN == (query_ids[:, None] - PROMPT) // CLEN
    return causal & ((key_ids[None, :] < PROMPT) | same_run)


def dot_plain(left, right):
    return lax.dot_general(left, right, (((1,), (0,)), ((), ())), preferred_element_type=jnp.float32)


def dot_right(left, right):
    return lax.dot_general(left, right, (((1,), (1,)), ((), ())), preferred_element_type=jnp.float32)


def dot_left(left, right):
    return lax.dot_general(left, right, (((0,), (0,)), ((), ())), preferred_element_type=jnp.float32)


ANYWHERE = pl.BlockSpec(memory_space=pl.ANY)
INSIDE = pl.BlockSpec(memory_space=pltpu.VMEM)
SCALARS = pl.BlockSpec(memory_space=pltpu.SMEM)
VMEM_BYTES = 60 * 1024 * 1024


def cost(flops, *arrays):
    return pl.CostEstimate(flops=1, bytes_accessed=1, transcendentals=0)


def weight_copies(spots, pieces, target, sems):
    copies = []
    for p, piece in enumerate(pieces):
        blocks, rows = piece.shape[0], piece.shape[1]
        for k in range(blocks):
            place = pl.multiple_of(spots[p, k] * rows, rows)
            copies.append(
                pltpu.make_async_copy(
                    piece.at[k], target.at[pl.ds(place, rows)], sems.at[p * blocks + k]
                )
            )
    return copies


def block_copies(blocks, target, sems, first, columns=None):
    copies = []
    start = 0
    for i, block in enumerate(blocks):
        rows = block.shape[0]
        source = block if columns is None else block.at[:, columns]
        copies.append(
            pltpu.make_async_copy(source, target.at[pl.ds(start, rows)], sems.at[first + i])
        )
        start += rows
    return copies


def swap_halves(values):
    half = HEAD_DIM // 2
    lane = lax.broadcasted_iota(jnp.int32, values.shape, 1)
    return jnp.where(
        lane % HEAD_DIM < half,
        pltpu.roll(values, 2 * HEAD_DIM - half, 1),
        pltpu.roll(values, half, 1),
    )


def mean_square_scale(values):
    return lax.rsqrt(jnp.mean(values * values, axis=-1, keepdims=True) + EPS)


def enter_kernel(count, gain_at, spots, tokens, cosine, sine, *refs):
    pieces = refs[:count]
    normed, query, keyval, small, weight, sems = refs[count:]
    low = jnp.bfloat16
    copies = weight_copies(spots, pieces, weight, sems)
    for copy in copies:
        copy.start()
    inputs = tokens[...].astype(jnp.float32)
    scaled = inputs * mean_square_scale(inputs)
    for copy in copies:
        copy.wait()
    query_width = query.shape[1]
    kv_width = keyval.shape[1] // 2
    qkv_width = query_width + 2 * kv_width
    turned = weight[:, qkv_width:].astype(jnp.float32).T
    small[...] = turned
    rows = (scaled * turned[gain_at : gain_at + 1]).astype(low)
    normed[...] = rows
    pair = 2 * HEAD_DIM
    scale = HEAD_DIM**-0.5
    for start in range(0, query_width + kv_width, 512):
        product_part = dot_plain(rows, weight[:, start : start + 512])
        for offset in range(0, 512, pair):
            part = product_part[:, offset : offset + pair]
            part = part * cosine[...] + swap_halves(part) * sine[...]
            at = start + offset
            if at < query_width:
                query[:, at : at + pair] = (part * scale).astype(low)
            else:
                keyval[:, at - query_width : at - query_width + pair] = part.astype(low)
    keyval[:, kv_width:] = dot_plain(
        rows, weight[:, query_width + kv_width : qkv_width]
    ).astype(low)


def enter(tokens, cosine, sine, pieces, spots, gain_at, query_width, kv_width):
    rows, width = tokens.shape
    columns = pieces[0].shape[2]
    low = jnp.bfloat16
    return pl.pallas_call(
        partial(enter_kernel, len(pieces), gain_at),
        in_specs=[SCALARS, INSIDE, INSIDE, INSIDE] + [ANYWHERE] * len(pieces),
        out_specs=[INSIDE] * 4,
        out_shape=[
            jax.ShapeDtypeStruct((rows, width), low),
            jax.ShapeDtypeStruct((rows, query_width), low),
            jax.ShapeDtypeStruct((rows, 2 * kv_width), low),
            jax.ShapeDtypeStruct((columns - query_width - 2 * kv_width, width), jnp.float32),
        ],
        scratch_shapes=[
            pltpu.VMEM((width, columns), low),
            pltpu.SemaphoreType.DMA((len(pieces) * pieces[0].shape[0],)),
        ],
        compiler_params=pltpu.CompilerParams(vmem_limit_bytes=VMEM_BYTES),
        cost_estimate=cost(2 * rows * width * columns, *pieces),
        name="enter",
    )(spots, tokens, cosine, sine, *pieces)


def both_places(values):
    wide = values.astype(jnp.float32)
    low_lane = lax.broadcasted_iota(jnp.int32, values.shape, 1) < HEAD_DIM
    moved = pltpu.roll(wide, HEAD_DIM, 1)
    kind = values.dtype
    return [
        [jnp.where(low_lane, wide, 0.0).astype(kind), jnp.where(low_lane, 0.0, moved).astype(kind)],
        [jnp.where(low_lane, moved, 0.0).astype(kind), jnp.where(low_lane, 0.0, wide).astype(kind)],
    ]


def attend_kernel(
    count, query, keyval, bias, tokens, small, member, kept, gain_at, spots, *refs
):
    pieces = refs[:count]
    attended, log_totals, residual, sent, gate_rows, weight, sems = refs[count:]
    low = jnp.bfloat16
    rows = query.shape[0]
    width = tokens.shape[1]
    kv_width = keyval.shape[1] // 2
    pair_lanes = 2 * HEAD_DIM
    repeat = HEADS // KV_HEADS
    copies = weight_copies(spots, pieces, weight, sems)
    for copy in copies:
        copy.start()
    log_totals[...] = jnp.zeros_like(log_totals)
    lane = lax.broadcasted_iota(jnp.int32, log_totals.shape, 1)

    @pl.loop(0, KV_HEADS // 2)
    def _(pair):
        at = pl.ds(pl.multiple_of(pair * pair_lanes, pair_lanes), pair_lanes)
        keys = both_places(keyval[:, at])
        at = pl.ds(pl.multiple_of(kv_width + pair * pair_lanes, pair_lanes), pair_lanes)
        values = both_places(keyval[:, at])
        for i in range(repeat):
            at = pl.ds(pl.multiple_of((pair * repeat + i) * pair_lanes, pair_lanes), pair_lanes)
            queries = query[:, at]
            total = jnp.zeros((rows, pair_lanes), jnp.float32)
            for a in range(2):
                head = 2 * i + a
                scores = dot_right(queries, keys[head // repeat][a]) + bias[...]
                peak = jnp.max(scores, axis=-1, keepdims=True)
                lifted = jnp.exp(scores - peak)
                row_total = jnp.sum(lifted, axis=-1, keepdims=True)
                weights_low = (lifted * (1.0 / row_total)).astype(low)
                total += dot_plain(weights_low, values[head // repeat][a])
                log_totals[...] = jnp.where(
                    lane == pair * (2 * repeat) + head, peak + jnp.log(row_total), log_totals[...]
                )
            attended[:, at] = total.astype(low)

    for copy in copies:
        copy.wait()
    hidden = tokens[...].astype(jnp.float32) + dot_plain(attended[...], weight[...])
    residual[...] = hidden
    gain = small[gain_at : gain_at + 1, :]
    normed = (hidden * mean_square_scale(hidden) * gain).astype(low)
    logits = dot_right(normed, small[...].astype(low))
    chosen = member[...] > 0.0
    logits = jnp.where(chosen, logits, -1e30)
    lifted = jnp.where(chosen, jnp.exp(logits - jnp.max(logits, axis=-1, keepdims=True)), 0.0)
    gates = lifted / jnp.sum(lifted, axis=-1, keepdims=True)
    gate_rows[...] = gates
    sent[:, :width] = normed
    sent[:, width:] = (gates * kept[...]).astype(low)


def attend(query, keyval, bias, tokens, small, member, kept, gain_at, pieces, spots):
    rows, width = tokens.shape
    query_width = query.shape[1]
    lanes = small.shape[0]
    low = jnp.bfloat16

    def kernel(*refs):
        attend_kernel(len(pieces), *refs[:7], gain_at, *refs[7:])

    return pl.pallas_call(
        kernel,
        in_specs=[INSIDE] * 7 + [SCALARS] + [ANYWHERE] * len(pieces),
        out_specs=[INSIDE] * 5,
        out_shape=[
            jax.ShapeDtypeStruct((rows, query_width), low),
            jax.ShapeDtypeStruct((rows, 128), jnp.float32),
            jax.ShapeDtypeStruct((rows, width), jnp.float32),
            jax.ShapeDtypeStruct((rows, width + lanes), low),
            jax.ShapeDtypeStruct((rows, lanes), jnp.float32),
        ],
        scratch_shapes=[
            pltpu.VMEM((query_width, width), low),
            pltpu.SemaphoreType.DMA((len(pieces) * pieces[0].shape[0],)),
        ],
        compiler_params=pltpu.CompilerParams(vmem_limit_bytes=VMEM_BYTES),
        cost_estimate=cost(2 * rows * width * width + 8 * rows * query_width * bias.shape[1], *pieces),
        name="attend",
    )(query, keyval, bias, tokens, small, member, kept, spots, *pieces)


def sorted_copies(place, source, others, own, sems):
    core, member = place[0], place[1]
    copies = []
    for r, (other, mine) in enumerate(zip(others, own)):
        copies.append(
            pltpu.make_async_copy(source.at[:, 1 - core, member ^ r], other, sems.at[2 * r])
        )
        copies.append(
            pltpu.make_async_copy(source.at[:, core, member ^ r], mine, sems.at[2 * r + 1])
        )
    return copies


def grad_shapes(cut, rows, columns):
    low = jnp.bfloat16
    if cut:
        block = rows // 32
        return (
            [jax.ShapeDtypeStruct((4, block, columns), low)] * 8,
            pltpu.VMEM((4, 2, 4, block, columns), low),
        )
    return (
        [jax.ShapeDtypeStruct((1, 1, 1, rows, columns), low)],
        pltpu.VMEM((1, 1, 1, rows, columns), low),
    )


def grad_copies(cut, place, source, outs, sems):
    if cut:
        return sorted_copies(place, source, outs[:4], outs[4:], sems)
    return [pltpu.make_async_copy(source, outs[0], sems.at[0])]


def turn_kernel(
    count,
    cut,
    gain_at,
    place,
    spots,
    normed_grad,
    residual,
    grad_out,
    small,
    gate_rows,
    member,
    kept,
    normed,
    attended,
    *refs,
):
    pieces = refs[:count]
    refs = refs[count:]
    outs = refs[: (8 if cut else 1)]
    resid_grad, head_grad, weight, weight_grad, sems, out_sems = refs[len(outs) :]
    low = jnp.bfloat16
    rows, width = residual.shape
    lanes = gate_rows.shape[1]
    copies = weight_copies(spots, pieces, weight, sems)
    for copy in copies:
        copy.start()
    lane = lax.broadcasted_iota(jnp.int32, (rows, lanes), 1)
    gates = gate_rows[...]
    gate_grads = normed_grad[:, width:] * kept[...]
    chosen_grad = gates * (gate_grads - jnp.sum(gates * gate_grads, axis=-1, keepdims=True))
    logit_grad = (chosen_grad * member[...]).astype(low)
    hidden = residual[...]
    scale = mean_square_scale(hidden)
    row_grad = normed_grad[:, :width] + dot_plain(logit_grad, small[...].astype(low))
    gain = small[gain_at : gain_at + 1, :]
    scaled = row_grad * gain
    total_grad = (
        grad_out[...].astype(jnp.float32)
        + scale * scaled
        - hidden * (scale * scale * scale) * jnp.mean(scaled * hidden, axis=-1, keepdims=True)
    )
    resid_grad[...] = total_grad
    attn_grad = total_grad.astype(low)
    shape = weight_grad.shape[:-1]
    gain_grad = (row_grad * hidden * scale).astype(low)
    picks = jnp.where(lane == gain_at, 1.0, 0.0).astype(low)
    weight_grad[..., width:] = (
        (dot_left(normed[...][:, :width], logit_grad) + dot_left(gain_grad, picks))
        .astype(low)
        .reshape(shape + (lanes,))
    )
    for start in range(0, width, 512):
        weight_grad[..., start : start + 512] = (
            dot_left(attended[...], attn_grad[:, start : start + 512])
            .astype(low)
            .reshape(shape + (512,))
        )
    out_copies = grad_copies(cut, place, weight_grad, outs, out_sems)
    for copy in out_copies:
        copy.start()
    for copy in copies:
        copy.wait()
    head_grad[...] = dot_right(attn_grad, weight[...]).astype(low)
    for copy in out_copies:
        copy.wait()


def turn(place, spots, operands, pieces, cut, gain_at):
    residual, gate_rows, attended = operands[1], operands[4], operands[8]
    rows, width = residual.shape
    query_width = attended.shape[1]
    low = jnp.bfloat16
    grads, held = grad_shapes(cut, query_width, width + gate_rows.shape[1])
    return pl.pallas_call(
        partial(turn_kernel, len(pieces), cut, gain_at),
        in_specs=[SCALARS, SCALARS] + [INSIDE] * len(operands) + [ANYWHERE] * len(pieces),
        out_specs=[ANYWHERE] * len(grads) + [INSIDE] * 2,
        out_shape=grads
        + [
            jax.ShapeDtypeStruct((rows, width), jnp.float32),
            jax.ShapeDtypeStruct((rows, query_width), low),
        ],
        scratch_shapes=[
            pltpu.VMEM((query_width, width), low),
            held,
            pltpu.SemaphoreType.DMA((len(pieces) * pieces[0].shape[0],)),
            pltpu.SemaphoreType.DMA((8,)),
        ],
        compiler_params=pltpu.CompilerParams(vmem_limit_bytes=VMEM_BYTES),
        cost_estimate=cost(4 * rows * width * width, *pieces, *pieces),
        name="turn",
    )(place, spots, *operands, *pieces)


def attend_back_kernel(
    head_grad, query, keyval, bias, log_totals, cosine, sine, query_grad, keyval_grad, totals
):
    low = jnp.bfloat16
    rows = query.shape[0]
    kv_width = keyval.shape[1] // 2
    pair_lanes = 2 * HEAD_DIM
    repeat = HEADS // KV_HEADS
    totals[...] = log_totals[...].T

    @pl.loop(0, KV_HEADS // 2)
    def _(pair):
        key_at = pl.ds(pl.multiple_of(pair * pair_lanes, pair_lanes), pair_lanes)
        value_at = pl.ds(pl.multiple_of(kv_width + pair * pair_lanes, pair_lanes), pair_lanes)
        keys = both_places(keyval[:, key_at])
        values = both_places(keyval[:, value_at])
        key_grads = [[None, None], [None, None]]
        value_grads = [[None, None], [None, None]]
        for i in range(repeat):
            at = pl.ds(pl.multiple_of((pair * repeat + i) * pair_lanes, pair_lanes), pair_lanes)
            queries = query[:, at]
            grads = head_grad[:, at]
            query_part = jnp.zeros((rows, pair_lanes), jnp.float32)
            for a in range(2):
                head = 2 * i + a
                g = head // repeat
                total = totals[pl.ds(pair * (2 * repeat) + head, 1), :]
                weights = jnp.exp(dot_right(keys[g][a], queries) + bias[...] - total)
                weight_grads = dot_right(values[g][a], grads)
                delta = jnp.sum(weights * weight_grads, axis=0, keepdims=True)
                score_grads = (weights * (weight_grads - delta)).astype(low)
                value_part = dot_plain(weights.astype(low), grads)
                key_part = dot_plain(score_grads, queries)
                query_part += dot_left(score_grads, keys[g][a])
                if key_grads[g][a] is None:
                    key_grads[g][a], value_grads[g][a] = key_part, value_part
                else:
                    key_grads[g][a] += key_part
                    value_grads[g][a] += value_part
            query_part = query_part * (HEAD_DIM**-0.5)
            query_part = query_part * cosine[...] - swap_halves(query_part) * sine[...]
            query_grad[:, at] = query_part.astype(low)
        low_lane = lax.broadcasted_iota(jnp.int32, (keyval.shape[0], pair_lanes), 1) < HEAD_DIM
        for at, found in ((key_at, key_grads), (value_at, value_grads)):
            keyval_grad[:, at] = jnp.where(
                low_lane,
                found[0][0] + pltpu.roll(found[0][1], HEAD_DIM, 1),
                pltpu.roll(found[1][0], HEAD_DIM, 1) + found[1][1],
            ).astype(low)


def attend_back(head_grad, query, keyval, bias, log_totals, cosine, sine):
    rows, query_width = query.shape
    low = jnp.bfloat16
    return pl.pallas_call(
        attend_back_kernel,
        in_specs=[INSIDE] * 7,
        out_specs=[INSIDE] * 2,
        out_shape=[
            jax.ShapeDtypeStruct((rows, query_width), low),
            jax.ShapeDtypeStruct(keyval.shape, low),
        ],
        scratch_shapes=[pltpu.VMEM((128, rows), jnp.float32)],
        compiler_params=pltpu.CompilerParams(vmem_limit_bytes=VMEM_BYTES),
        cost_estimate=cost(20 * rows * query_width * keyval.shape[0], query, keyval, bias),
        name="attend_back",
    )(head_grad, query, keyval, bias, log_totals, cosine, sine)


def leave_kernel(
    count,
    cut,
    gain_at,
    place,
    spots,
    keyval_sum,
    query_grad,
    normed,
    tokens,
    resid_grad,
    small,
    cosine,
    sine,
    *refs,
):
    pieces = refs[:count]
    refs = refs[count:]
    outs = refs[: (8 if cut else 1)]
    input_grad, weight, weight_grad, joined, sems, out_sems = refs[len(outs) :]
    low = jnp.bfloat16
    rows, width = tokens.shape
    query_width = query_grad.shape[1]
    kv_width = keyval_sum.shape[1] // 2
    qkv_width = query_width + 2 * kv_width
    pair = 2 * HEAD_DIM
    copies = weight_copies(spots, pieces, weight, sems)
    for copy in copies:
        copy.start()
    joined[:, :query_width] = query_grad[...]
    for start in range(0, kv_width, pair):
        part = keyval_sum[:, start : start + pair]
        part = part * cosine[...] - swap_halves(part) * sine[...]
        joined[:, query_width + start : query_width + start + pair] = part.astype(low)
    joined[:, query_width + kv_width :] = keyval_sum[:, kv_width:].astype(low)
    shape = weight_grad.shape[:-1]
    for start in range(0, qkv_width, 512):
        weight_grad[..., start : start + 512] = (
            dot_left(normed[...], joined[:, start : start + 512]).astype(low).reshape(shape + (512,))
        )
    for copy in copies:
        copy.wait()
    row_grad = dot_right(joined[...], weight[:, :qkv_width])
    inputs = tokens[...].astype(jnp.float32)
    scale = mean_square_scale(inputs)
    lanes = weight_grad.shape[-1] - qkv_width
    lane = lax.broadcasted_iota(jnp.int32, (rows, lanes), 1)
    picks = jnp.where(lane == gain_at, 1.0, 0.0).astype(low)
    weight_grad[..., qkv_width:] = (
        dot_left((row_grad * inputs * scale).astype(low), picks).astype(low).reshape(shape + (lanes,))
    )
    out_copies = grad_copies(cut, place, weight_grad, outs, out_sems)
    for copy in out_copies:
        copy.start()
    scaled = row_grad * small[gain_at : gain_at + 1, :]
    input_grad[...] = (
        resid_grad[...]
        + scale * scaled
        - inputs * (scale * scale * scale) * jnp.mean(scaled * inputs, axis=-1, keepdims=True)
    )
    for copy in out_copies:
        copy.wait()


def leave(place, spots, operands, pieces, cut, gain_at):
    tokens, query_grad, keyval_sum = operands[3], operands[1], operands[0]
    rows, width = tokens.shape
    columns = pieces[0].shape[2]
    low = jnp.bfloat16
    grads, held = grad_shapes(cut, width, columns)
    return pl.pallas_call(
        partial(leave_kernel, len(pieces), cut, gain_at),
        in_specs=[SCALARS, SCALARS] + [INSIDE] * len(operands) + [ANYWHERE] * len(pieces),
        out_specs=[ANYWHERE] * len(grads) + [INSIDE],
        out_shape=grads + [jax.ShapeDtypeStruct((rows, width), jnp.float32)],
        scratch_shapes=[
            pltpu.VMEM((width, columns), low),
            held,
            pltpu.VMEM((rows, query_grad.shape[1] + keyval_sum.shape[1]), low),
            pltpu.SemaphoreType.DMA((len(pieces) * pieces[0].shape[0],)),
            pltpu.SemaphoreType.DMA((8,)),
        ],
        compiler_params=pltpu.CompilerParams(vmem_limit_bytes=VMEM_BYTES),
        cost_estimate=cost(4 * rows * width * columns, *pieces, *pieces),
        name="leave",
    )(place, spots, *operands, *pieces)


def expert_kernel(sources, carried, last, row_blocks, grad_blocks, row_tile, first, place, *refs):
    packed = refs[:sources]
    refs = refs[sources:]
    blocks_in = refs[:row_blocks]
    grads_in = refs[row_blocks : row_blocks + grad_blocks]
    refs = refs[row_blocks + grad_blocks :]
    if carried:
        mix_in, turn_in = refs[:2]
        refs = refs[2:]
    packed_grads = refs[:sources]
    mix_out, turn_out = refs[sources : sources + 2]
    refs = refs[sources + 2 :]
    if last:
        mix, turned = refs[:2]
        refs = refs[2:]
    else:
        mix, turned = mix_out, turn_out
    (
        rows,
        grads,
        gates,
        gate_w,
        up_w,
        down_w,
        gate_g,
        up_g,
        down_g,
        weighted,
        gate_side,
        up_side,
        load_sems,
        save_sems,
        carry_sems,
    ) = refs
    count = packed[0].shape[2]
    hidden_width = gate_w.shape[-1]
    total_rows, width = rows.shape
    lanes = gates.shape[1]
    low = jnp.bfloat16

    def moves(e, outside, gate, up, down, sems, inward):
        slot = e % 2
        found = []
        for n, array in enumerate(outside):
            core = place[0] ^ n if sources > 1 else 0
            ends = []
            for side, inner in ((0, gate), (1, up)):
                for j in range(3):
                    columns = pl.ds(j * hidden_width, hidden_width)
                    ends.append((array.at[:, side, e, :, columns], inner.at[slot, :, core, j]))
            ends.append((array.at[:, 2, e], down.at[slot, :, core]))
            for i, (outer, inner) in enumerate(ends):
                ends_now = (outer, inner) if inward else (inner, outer)
                found.append(pltpu.make_async_copy(*ends_now, sems.at[slot, 7 * n + i]))
        return found

    def loads(e):
        return moves(e, packed, gate_w, up_w, down_w, load_sems, True)

    def saves(e):
        return moves(e, packed_grads, gate_g, up_g, down_g, save_sems, False)

    carries = (
        block_copies(grads_in, grads, carry_sems, 0, pl.ds(0, width))
        + block_copies(blocks_in, rows, carry_sems, grad_blocks, pl.ds(0, width))
        + block_copies(
            blocks_in, gates, carry_sems, grad_blocks + row_blocks, pl.ds(width, lanes)
        )
    )
    sums = []
    if carried:
        at = grad_blocks + 2 * row_blocks
        sums = [
            pltpu.make_async_copy(mix_in, mix, carry_sems.at[at]),
            pltpu.make_async_copy(turn_in, turned, carry_sems.at[at + 1]),
        ]
    for copy in loads(0) + carries + sums:
        copy.start()
    for e in range(count):
        slot = e % 2
        if e + 1 < count:
            for copy in loads(e + 1):
                copy.start()
        for copy in loads(e):
            copy.wait()
        if e == 0:
            for copy in carries:
                copy.wait()
            if not carried:
                turned[:, width:] = jnp.zeros((total_rows, lanes), jnp.float32)

        @pl.loop(0, total_rows // row_tile)
        def _(tile):
            span = pl.ds(pl.multiple_of(tile * row_tile, row_tile), row_tile)
            gate_full = gate_w[slot].reshape(width, hidden_width)
            up_full = up_w[slot].reshape(width, hidden_width)
            down_full = down_w[slot].reshape(hidden_width, width)
            here = rows[span, :]
            slope = dot_right(grads[span, :], down_full)
            gate_pre = dot_plain(here, gate_full)
            up_pre = dot_plain(here, up_full)
            lane = lax.broadcasted_iota(jnp.int32, (row_tile, lanes), 1)
            chosen = lane == first[0] + e
            gate_column = jnp.sum(
                jnp.where(chosen, gates[span, :].astype(jnp.float32), 0.0), axis=1, keepdims=True
            )
            sigmoid_gate = jax.nn.sigmoid(gate_pre)
            activated = gate_pre * sigmoid_gate
            hidden = (activated * up_pre).astype(low).astype(jnp.float32)
            share = jnp.sum(hidden * slope, axis=1, keepdims=True)
            if e == 0 and sums:

                @pl.when(tile == 0)
                def _():
                    for copy in sums:
                        copy.wait()

            turned[span, width:] = jnp.where(chosen, share, turned[span, width:])
            part_weighted = (hidden * gate_column).astype(low)
            hidden_grad = slope * gate_column
            part_gate = (
                hidden_grad * up_pre * (sigmoid_gate + activated * (1.0 - sigmoid_gate))
            ).astype(low)
            part_up = (hidden_grad * activated).astype(low)
            weighted[span, :] = part_weighted
            gate_side[span, :] = part_gate
            up_side[span, :] = part_up
            mix_part = dot_plain(part_weighted, down_full)
            turn_part = dot_right(part_gate, gate_full) + dot_right(part_up, up_full)
            if e == 0 and not carried:
                mix[span, :] = mix_part
                turned[span, :width] = turn_part
            elif last and e == count - 1:
                mix_out[span, :] = (mix[span, :] + mix_part).astype(low)
                turn_out[span, :width] = (turned[span, :width] + turn_part).astype(low)
                turn_out[span, width:] = turned[span, width:].astype(low)
            else:
                mix[span, :] += mix_part
                turned[span, :width] += turn_part

        if e >= 2:
            for copy in saves(e - 2):
                copy.wait()
        down_g[slot] = dot_left(weighted[...], grads[...]).astype(low).reshape(down_g.shape[1:])
        gate_g[slot] = dot_left(rows[...], gate_side[...]).astype(low).reshape(gate_g.shape[1:])
        up_g[slot] = dot_left(rows[...], up_side[...]).astype(low).reshape(up_g.shape[1:])
        for copy in saves(e):
            copy.start()
    for e in range(max(0, count - 2), count):
        for copy in saves(e):
            copy.wait()


def expert_pass(first, place, rows, grads, packed, carry, last):
    sources = len(packed)
    levels, _, count, part, width = packed[0].shape
    hidden_width = levels * sources * part
    total_rows = sum(block.shape[0] for block in rows)
    lanes = rows[0].shape[1] - width
    low = jnp.bfloat16
    wide = jnp.float32
    carried = carry is not None
    flops = 18 * total_rows * count * hidden_width * width
    side = pltpu.VMEM((2, levels, sources, 3, part, hidden_width), low)
    sides = [side, side, pltpu.VMEM((2, levels, sources, part, width), low)]
    sums = [(total_rows, width), (total_rows, width + lanes)]
    return pl.pallas_call(
        partial(
            expert_kernel, sources, carried, last, len(rows), len(grads), min(512, total_rows)
        ),
        in_specs=[SCALARS, SCALARS]
        + [ANYWHERE] * (sources + len(rows) + len(grads) + (2 if carried else 0)),
        out_specs=[ANYWHERE] * sources + [INSIDE, INSIDE],
        out_shape=[jax.ShapeDtypeStruct(packed[0].shape, low)] * sources
        + [jax.ShapeDtypeStruct(shape, low if last else wide) for shape in sums],
        scratch_shapes=([pltpu.VMEM(shape, wide) for shape in sums] if last else [])
        + [
            pltpu.VMEM((total_rows, width), low),
            pltpu.VMEM((total_rows, width), low),
            pltpu.VMEM((total_rows, lanes), low),
        ]
        + sides
        + sides
        + [pltpu.VMEM((total_rows, hidden_width), low)] * 3
        + [
            pltpu.SemaphoreType.DMA((2, 7 * sources)),
            pltpu.SemaphoreType.DMA((2, 7 * sources)),
            pltpu.SemaphoreType.DMA((2 * len(rows) + len(grads) + 2,)),
        ],
        compiler_params=pltpu.CompilerParams(vmem_limit_bytes=VMEM_BYTES),
        cost_estimate=cost(flops, *packed, *packed, *rows, *grads),
        name="experts",
    )(first, place, *packed, *rows, *grads, *(carry or ()))


def unpack_kernel(chunks, *refs):
    found, (gate, up, down) = refs[:chunks], refs[chunks:]
    hidden_width = gate.shape[2]
    base = 0
    for chunk in found:
        count, part = chunk.shape[1], chunk.shape[2]
        for e in range(count):
            for side, target in ((0, gate), (1, up)):
                for j in range(3):
                    target[base + e, j * part : (j + 1) * part, :] = chunk[
                        side, e, :, j * hidden_width : (j + 1) * hidden_width
                    ].astype(jnp.float32)
            down[base + e] = chunk[2, e].astype(jnp.float32)
        base += count


def unpack(chunks, gate_shape, down_shape):
    return pl.pallas_call(
        partial(unpack_kernel, len(chunks)),
        in_specs=[INSIDE] * len(chunks),
        out_specs=[INSIDE] * 3,
        out_shape=[
            jax.ShapeDtypeStruct(gate_shape, jnp.float32),
            jax.ShapeDtypeStruct(gate_shape, jnp.float32),
            jax.ShapeDtypeStruct(down_shape, jnp.float32),
        ],
        compiler_params=pltpu.CompilerParams(vmem_limit_bytes=VMEM_BYTES),
        cost_estimate=cost(0, *chunks, *chunks, *chunks),
        name="unpack",
    )(*chunks)


def cube():
    return lax.axis_size("batch") == 8 and lax.axis_size("expert") == 4


def pair_moves(size, flip):
    return [(i, i ^ flip) for i in range(size)]


def shift_moves(step):
    return [(2 * z + c, 2 * ((z + step) % 4) + c) for z in range(4) for c in range(2)]


def gather_blocks(rows, at_once=False):
    size = lax.axis_size("expert")
    if size != 4:
        stacked = lax.all_gather(rows, "expert", axis=0)
        own = lax.axis_index("expert")
        return [
            lax.dynamic_index_in_dim(stacked, own ^ r, axis=0, keepdims=False) for r in range(size)
        ]
    across, along = pair_moves(size, 1), pair_moves(size, 2)
    if at_once:
        return [rows] + [lax.ppermute(rows, "expert", pair_moves(size, r)) for r in range(1, 4)]
    half = rows.shape[0] // 2
    first = lax.ppermute(rows, "expert", across)
    second = lax.ppermute(rows, "expert", along)
    top = lax.ppermute(second[:half], "expert", across)
    bottom = lax.ppermute(first[half:], "expert", along)
    return [rows, first, second, top, bottom]


def scatter_blocks(parts):
    size = lax.axis_size("expert")
    low = jnp.bfloat16
    wide = jnp.float32
    if size != 4:
        own = lax.axis_index("expert")
        order = jnp.arange(size, dtype=jnp.int32) ^ own
        stacked = jnp.take(jnp.stack(parts), order, axis=0).astype(low)
        return lax.psum_scatter(stacked, "expert", scatter_dimension=0).astype(wide)
    across, along = pair_moves(size, 1), pair_moves(size, 2)
    half = parts[0].shape[0] // 2
    top = lax.ppermute(parts[3][:half].astype(low), "expert", across)
    bottom = lax.ppermute(parts[3][half:].astype(low), "expert", along)
    first_top = lax.ppermute(parts[1][:half].astype(low), "expert", across)
    second_bottom = lax.ppermute(parts[2][half:].astype(low), "expert", along)
    for_second = (parts[2][:half].astype(wide) + top.astype(wide)).astype(low)
    for_first = (parts[1][half:].astype(wide) + bottom.astype(wide)).astype(low)
    second_top = lax.ppermute(for_second, "expert", along)
    first_bottom = lax.ppermute(for_first, "expert", across)
    own = parts[0].astype(wide)
    return jnp.concatenate(
        [
            own[:half] + first_top.astype(wide) + second_top.astype(wide),
            own[half:] + first_bottom.astype(wide) + second_bottom.astype(wide),
        ],
        axis=0,
    )


def after(values, events):
    return lax.optimization_barrier((values, events))[0]


def shift_dense(rows):
    if not cube():
        return [lax.all_gather(rows, ("batch", "expert"), axis=0, tiled=True)]
    return [rows] + [lax.ppermute(rows, "batch", shift_moves(r)) for r in range(1, 4)]


def gather_dense(line, columns, events):
    found = [rows[:, columns] for rows in line]
    if not cube():
        return [found[0][None]], jnp.zeros((1, 1), jnp.int32), (), ()
    place = lax.axis_index("batch")
    level, core = place // 2, place % 2
    member = lax.axis_index("expert")
    mine = gather_blocks(after(jnp.stack(found), events))
    plane, far = mine[1:3], mine[3:]
    mine = mine[:3] + [jnp.concatenate(far, axis=0)]
    other = [lax.ppermute(block, "batch", pair_moves(8, 1)) for block in mine]
    spots = [
        [(((level + 4 - k) % 4) * 2 + (core ^ c)) * 4 + (member ^ r) for k in range(4)]
        for c in range(2)
        for r in range(4)
    ]
    return mine + other, jnp.array(spots, jnp.int32), plane, far


def scatter_dense(found, events, late):
    low = jnp.bfloat16
    wide = jnp.float32
    if not cube():
        values = found[0].reshape(found[0].shape[3:])
        total = lax.psum_scatter(values, ("batch", "expert"), scatter_dimension=0, tiled=True)
        return total.astype(wide)
    level = lax.axis_index("batch") // 2
    received = {r: lax.ppermute(found[r], "batch", pair_moves(8, 1)) for r in (3, 1, 2, 0)}
    received = after(received, events)
    parts = [found[4 + r].astype(wide) + received[r].astype(wide) for r in range(4)]
    plane = after(scatter_blocks(parts), late)
    total = lax.dynamic_index_in_dim(plane, level, axis=0, keepdims=False)
    for r in range(1, 4):
        sent = lax.dynamic_index_in_dim(plane, (level + r) % 4, axis=0, keepdims=False)
        total += lax.ppermute(sent.astype(low), "batch", shift_moves(r)).astype(wide)
    return total


def pack_sides(gate, up, down):
    def fold(values):
        count, depth, width = values.shape
        return values.reshape(count, 3, depth // 3, width).transpose(0, 2, 1, 3).reshape(down.shape)

    return jnp.stack([fold(gate), fold(up), down], axis=0)


def local(
    tokens,
    cotangent,
    attn_gain,
    query_weight,
    key_weight,
    value_weight,
    out_weight,
    ffn_gain,
    router_weight,
    gate_weight,
    up_weight,
    down_weight,
    routes,
    ranking,
):
    low = jnp.bfloat16
    wide = jnp.float32
    query_width = HEADS * HEAD_DIM
    kv_width = KV_HEADS * HEAD_DIM
    qkv_width = query_width + 2 * kv_width
    width = tokens.shape[2]
    experts_total = router_weight.shape[1]
    extra = -(-(experts_total + 2) // 128) * 128
    first_gain, second_gain = experts_total, experts_total + 1
    local_experts = gate_weight.shape[0]
    member_count = lax.axis_size("expert")
    member_id = lax.axis_index("expert")
    local_rows = tokens.shape[1]
    group_rows = local_rows * member_count
    cut = cube()
    place = jnp.stack([lax.axis_index("batch") % 2, member_id]).astype(jnp.int32)

    route_rows = routes[0]
    rank_rows = ranking[0]
    expert_lanes = jnp.arange(extra, dtype=jnp.int32)
    member = jnp.any(route_rows[:, :, None] == expert_lanes[None, None, :], axis=1)
    marks = jnp.where(
        expert_lanes[None, :] == experts_total,
        (rank_rows // 32)[:, None],
        jnp.where(expert_lanes[None, :] == experts_total + 1, (rank_rows % 32)[:, None], member),
    ).astype(low)
    grad_out = cotangent[0]
    grad_blocks = gather_blocks(jnp.concatenate([grad_out, marks], axis=1), True)
    marks_all = jnp.concatenate([block[:, width:] for block in grad_blocks], axis=0)

    small_width = qkv_width + extra
    line = shift_dense(
        jnp.concatenate(
            [
                query_weight,
                key_weight,
                value_weight,
                router_weight,
                attn_gain[:, None],
                ffn_gain[:, None],
                jnp.zeros((query_weight.shape[0], extra - experts_total - 2), low),
                out_weight,
            ],
            axis=1,
        )
    )
    qkv_pieces, qkv_spots, plane, far = gather_dense(
        line, slice(0, small_width), grad_blocks
    )
    out_pieces, out_spots, out_plane, _ = gather_dense(line, slice(small_width, None), far)
    chunks = (0, 3, local_experts)
    packed_all = []
    for a, b in zip(chunks[:-1], chunks[1:]):
        sides = (gate_weight[a:b], up_weight[a:b], down_weight[a:b])
        if cut:
            sides = after(sides, (line[1:], grad_blocks) if a == 0 else plane)
        packed_all.append(lax.all_gather(pack_sides(*sides), "batch", axis=0))

    row_ids = member_id * local_rows + jnp.arange(local_rows, dtype=jnp.int32)
    half_dim = HEAD_DIM // 2
    frequency = THETA ** (-jnp.arange(half_dim, dtype=wide) / half_dim)
    angles = place_of(row_ids).astype(wide)[:, None] * frequency[None, :]
    cosine = jnp.tile(jnp.cos(angles), (1, 4))
    sine_part = jnp.tile(jnp.concatenate([-jnp.sin(angles), jnp.sin(angles)], axis=1), (1, 2))
    normed, query, keyval, small = enter(
        tokens[0], cosine, sine_part, qkv_pieces, qkv_spots, first_gain, query_width, kv_width
    )

    rank_all = (
        marks_all[:, experts_total].astype(wide) * 32 + marks_all[:, experts_total + 1].astype(wide)
    )
    earlier = (rank_all[None, :] < rank_rows.astype(wide)[:, None]).astype(low)
    before = product(earlier, marks_all)
    capacity = 5 * group_rows * route_rows.shape[1] // (4 * experts_total)
    member = member.astype(wide)
    kept = jnp.where(before < capacity, member, 0.0)

    keyval_blocks = gather_blocks(after(keyval, out_plane))
    if member_count == 4:
        ordered = keyval_blocks[:3] + [jnp.concatenate(keyval_blocks[3:], axis=0)]
        away = 1 << 20
        keys = jnp.concatenate(
            [
                lax.select_n(member_id, *ordered),
                lax.select_n(member_id ^ 1, *ordered),
                keyval,
            ],
            axis=0,
        )
        starts = [
            jnp.where(member_id >= 1, 0, away),
            jnp.where(member_id >= 2, local_rows, away),
            member_id * local_rows,
        ]
    else:
        keys = jnp.concatenate(keyval_blocks, axis=0)
        starts = [(member_id ^ r) * local_rows for r in range(member_count)]
    key_ids = jnp.concatenate([s + jnp.arange(local_rows, dtype=jnp.int32) for s in starts])
    bias = jnp.where(visible(row_ids, key_ids), 0.0, -1e30).astype(wide)
    attended, log_totals, residual, sent, gate_rows = attend(
        query, keys, bias, tokens[0], small, member, kept, second_gain, out_pieces, out_spots
    )
    sent_blocks = gather_blocks(sent)

    carry, chunk_grads = None, []
    for packed, a, b in zip(packed_all, chunks[:-1], chunks[1:]):
        first = (member_id * local_experts + a).astype(jnp.int32).reshape(1)
        packed_grad, mixture_all, row_grad = expert_pass(
            first, place, sent_blocks, grad_blocks, [packed], carry, b == local_experts
        )
        carry = (mixture_all, row_grad)
        chunk_grads.append(packed_grad)

    def blocks_of(values):
        return [values[r * local_rows : (r + 1) * local_rows] for r in range(member_count)]

    normed_grad = scatter_blocks(blocks_of(row_grad))
    turned = turn(
        place,
        out_spots,
        (
            normed_grad,
            residual,
            grad_out,
            small,
            gate_rows,
            member,
            kept,
            sent,
            attended,
        ),
        out_pieces,
        cut,
        second_gain,
    )
    out_found = turned[:-2]
    resid_grad, head_grad = turned[-2:]
    query_grad, key_grads = attend_back(
        head_grad, query, keys, bias.T, log_totals, cosine, sine_part
    )
    totals = [lax.psum_scatter(chunk_grads[0], "batch", scatter_dimension=0)]
    for packed_grad in chunk_grads[1:]:
        packed_grad = after(packed_grad, (totals[-1], query_grad))
        totals.append(lax.psum_scatter(packed_grad, "batch", scatter_dimension=0))
    if member_count == 4:
        zero = jnp.zeros((), low)
        for_first, for_second, for_own = blocks_of(key_grads)[:3]
        key_parts = []
        for r in range(4):
            part = jnp.where(member_id == r, for_first, zero)
            part += jnp.where(member_id ^ 1 == r, for_second, zero)
            key_parts.append(part + for_own if r == 0 else part)
    else:
        key_parts = blocks_of(key_grads)
    keyval_sum = after(scatter_blocks(key_parts), totals[0])
    left = leave(
        place,
        qkv_spots,
        (
            keyval_sum,
            query_grad,
            normed,
            tokens[0],
            resid_grad,
            small,
            cosine,
            sine_part,
        ),
        qkv_pieces,
        cut,
        first_gain,
    )
    qkv_found, input_grad = left[:-1], left[-1]
    mixture = scatter_blocks(blocks_of(after(mixture_all, resid_grad)))
    result = (residual + mixture).astype(low)
    out_sum = scatter_dense(out_found, keyval_sum, ())
    qkv_sum = scatter_dense(qkv_found, (), totals)
    gate_total, up_total, down_total = unpack(totals, gate_weight.shape, down_weight.shape)
    return (
        result[None],
        input_grad[None],
        qkv_sum[:, qkv_width + first_gain],
        qkv_sum[:, :query_width],
        qkv_sum[:, query_width : query_width + kv_width],
        qkv_sum[:, query_width + kv_width : qkv_width],
        out_sum[:, :width],
        out_sum[:, width + second_gain],
        out_sum[:, width : width + experts_total],
        gate_total,
        up_total,
        down_total,
    )


def solution(mesh):
    return jax.shard_map(
        local,
        mesh=mesh,
        in_specs=(
            P("batch", "expert", None),
            P("batch", "expert", None),
            P(("batch", "expert")),
            P(("batch", "expert"), None),
            P(("batch", "expert"), None),
            P(("batch", "expert"), None),
            P(("batch", "expert"), None),
            P(("batch", "expert")),
            P(("batch", "expert"), None),
            P("expert", "batch", None),
            P("expert", "batch", None),
            P("expert", "batch", None),
            P("batch", "expert", None),
            P("batch", "expert"),
        ),
        out_specs=(
            P("batch", "expert", None),
            P("batch", "expert", None),
            P(("batch", "expert")),
            P(("batch", "expert"), None),
            P(("batch", "expert"), None),
            P(("batch", "expert"), None),
            P(("batch", "expert"), None),
            P(("batch", "expert")),
            P(("batch", "expert"), None),
            P("expert", "batch", None),
            P("expert", "batch", None),
            P("expert", "batch", None),
        ),
        check_vma=False,
    )
```

```python
from functools import partial

import jax
import jax.numpy as jnp
from jax import lax
from jax.experimental import pallas as pl
from jax.experimental.pallas import tpu as pltpu
from jax.sharding import PartitionSpec as P

HEADS = 24
KV_HEADS = 8
HEAD_DIM = 64
PROMPT = 512
CLEN = 256


EPS = 1e-06
THETA = 10000.0


def product(left, right):
    return jnp.dot(left, right, preferred_element_type=jnp.float32)


def place_of(row_ids):
    return jnp.where(row_ids < PROMPT, row_ids, PROMPT + (row_ids - PROMPT) % CLEN)


def visible(query_ids, key_ids):
    causal = key_ids[None, :] <= query_ids[:, None]
    same_run = (key_ids[None, :] - PROMPT) // CLEN == (query_ids[:, None] - PROMPT) // CLEN
    return causal & ((key_ids[None, :] < PROMPT) | same_run)


def dot_plain(left, right):
    return lax.dot_general(left, right, (((1,), (0,)), ((), ())), preferred_element_type=jnp.float32)


def dot_right(left, right):
    return lax.dot_general(left, right, (((1,), (1,)), ((), ())), preferred_element_type=jnp.float32)


def dot_left(left, right):
    return lax.dot_general(left, right, (((0,), (0,)), ((), ())), preferred_element_type=jnp.float32)


ANYWHERE = pl.BlockSpec(memory_space=pl.ANY)
INSIDE = pl.BlockSpec(memory_space=pltpu.VMEM)
SCALARS = pl.BlockSpec(memory_space=pltpu.SMEM)
VMEM_BYTES = 60 * 1024 * 1024


def cost(flops, *arrays):
    return pl.CostEstimate(flops=1, bytes_accessed=1, transcendentals=0)


def weight_copies(spots, pieces, target, sems):
    copies = []
    for p, piece in enumerate(pieces):
        blocks, rows = piece.shape[0], piece.shape[1]
        for k in range(blocks):
            place = pl.multiple_of(spots[p, k] * rows, rows)
            copies.append(
                pltpu.make_async_copy(
                    piece.at[k], target.at[pl.ds(place, rows)], sems.at[p * blocks + k]
                )
            )
    return copies


def block_copies(blocks, target, sems, first, columns=None):
    copies = []
    start = 0
    for i, block in enumerate(blocks):
        rows = block.shape[0]
        source = block if columns is None else block.at[:, columns]
        copies.append(
            pltpu.make_async_copy(source, target.at[pl.ds(start, rows)], sems.at[first + i])
        )
        start += rows
    return copies


def swap_halves(values):
    half = HEAD_DIM // 2
    lane = lax.broadcasted_iota(jnp.int32, values.shape, 1)
    return jnp.where(
        lane % HEAD_DIM < half,
        pltpu.roll(values, 2 * HEAD_DIM - half, 1),
        pltpu.roll(values, half, 1),
    )


def mean_square_scale(values):
    return lax.rsqrt(jnp.mean(values * values, axis=-1, keepdims=True) + EPS)


def enter_kernel(count, gain_at, spots, tokens, cosine, sine, *refs):
    pieces = refs[:count]
    normed, query, keyval, small, weight, sems = refs[count:]
    low = jnp.bfloat16
    copies = weight_copies(spots, pieces, weight, sems)
    for copy in copies:
        copy.start()
    inputs = tokens[...].astype(jnp.float32)
    scaled = inputs * mean_square_scale(inputs)
    for copy in copies:
        copy.wait()
    query_width = query.shape[1]
    kv_width = keyval.shape[1] // 2
    qkv_width = query_width + 2 * kv_width
    turned = weight[:, qkv_width:].astype(jnp.float32).T
    small[...] = turned
    rows = (scaled * turned[gain_at : gain_at + 1]).astype(low)
    normed[...] = rows
    pair = 2 * HEAD_DIM
    scale = HEAD_DIM**-0.5
    for start in range(0, query_width + kv_width, 512):
        product_part = dot_plain(rows, weight[:, start : start + 512])
        for offset in range(0, 512, pair):
            part = product_part[:, offset : offset + pair]
            part = part * cosine[...] + swap_halves(part) * sine[...]
            at = start + offset
            if at < query_width:
                query[:, at : at + pair] = (part * scale).astype(low)
            else:
                keyval[:, at - query_width : at - query_width + pair] = part.astype(low)
    keyval[:, kv_width:] = dot_plain(
        rows, weight[:, query_width + kv_width : qkv_width]
    ).astype(low)


def enter(tokens, cosine, sine, pieces, spots, gain_at, query_width, kv_width):
    rows, width = tokens.shape
    columns = pieces[0].shape[2]
    low = jnp.bfloat16
    return pl.pallas_call(
        partial(enter_kernel, len(pieces), gain_at),
        in_specs=[SCALARS, INSIDE, INSIDE, INSIDE] + [ANYWHERE] * len(pieces),
        out_specs=[INSIDE] * 4,
        out_shape=[
            jax.ShapeDtypeStruct((rows, width), low),
            jax.ShapeDtypeStruct((rows, query_width), low),
            jax.ShapeDtypeStruct((rows, 2 * kv_width), low),
            jax.ShapeDtypeStruct((columns - query_width - 2 * kv_width, width), jnp.float32),
        ],
        scratch_shapes=[
            pltpu.VMEM((width, columns), low),
            pltpu.SemaphoreType.DMA((len(pieces) * pieces[0].shape[0],)),
        ],
        compiler_params=pltpu.CompilerParams(vmem_limit_bytes=VMEM_BYTES),
        cost_estimate=cost(2 * rows * width * columns, *pieces),
        name="enter",
    )(spots, tokens, cosine, sine, *pieces)


def both_places(values):
    wide = values.astype(jnp.float32)
    low_lane = lax.broadcasted_iota(jnp.int32, values.shape, 1) < HEAD_DIM
    moved = pltpu.roll(wide, HEAD_DIM, 1)
    kind = values.dtype
    return [
        [jnp.where(low_lane, wide, 0.0).astype(kind), jnp.where(low_lane, 0.0, moved).astype(kind)],
        [jnp.where(low_lane, moved, 0.0).astype(kind), jnp.where(low_lane, 0.0, wide).astype(kind)],
    ]


def attend_kernel(
    count, query, keyval, bias, tokens, small, member, kept, gain_at, spots, *refs
):
    pieces = refs[:count]
    attended, log_totals, residual, sent, gate_rows, weight, sems = refs[count:]
    low = jnp.bfloat16
    rows = query.shape[0]
    width = tokens.shape[1]
    kv_width = keyval.shape[1] // 2
    pair_lanes = 2 * HEAD_DIM
    repeat = HEADS // KV_HEADS
    copies = weight_copies(spots, pieces, weight, sems)
    for copy in copies:
        copy.start()
    log_totals[...] = jnp.zeros_like(log_totals)
    lane = lax.broadcasted_iota(jnp.int32, log_totals.shape, 1)

    @pl.loop(0, KV_HEADS // 2)
    def _(pair):
        at = pl.ds(pl.multiple_of(pair * pair_lanes, pair_lanes), pair_lanes)
        keys = both_places(keyval[:, at])
        at = pl.ds(pl.multiple_of(kv_width + pair * pair_lanes, pair_lanes), pair_lanes)
        values = both_places(keyval[:, at])
        for i in range(repeat):
            at = pl.ds(pl.multiple_of((pair * repeat + i) * pair_lanes, pair_lanes), pair_lanes)
            queries = query[:, at]
            total = jnp.zeros((rows, pair_lanes), jnp.float32)
            for a in range(2):
                head = 2 * i + a
                scores = dot_right(queries, keys[head // repeat][a]) + bias[...]
                peak = jnp.max(scores, axis=-1, keepdims=True)
                lifted = jnp.exp(scores - peak)
                row_total = jnp.sum(lifted, axis=-1, keepdims=True)
                weights_low = (lifted * (1.0 / row_total)).astype(low)
                total += dot_plain(weights_low, values[head // repeat][a])
                log_totals[...] = jnp.where(
                    lane == pair * (2 * repeat) + head, peak + jnp.log(row_total), log_totals[...]
                )
            attended[:, at] = total.astype(low)

    for copy in copies:
        copy.wait()
    hidden = tokens[...].astype(jnp.float32) + dot_plain(attended[...], weight[...])
    residual[...] = hidden
    gain = small[gain_at : gain_at + 1, :]
    normed = (hidden * mean_square_scale(hidden) * gain).astype(low)
    logits = dot_right(normed, small[...].astype(low))
    chosen = member[...] > 0.0
    logits = jnp.where(chosen, logits, -1e30)
    lifted = jnp.where(chosen, jnp.exp(logits - jnp.max(logits, axis=-1, keepdims=True)), 0.0)
    gates = lifted / jnp.sum(lifted, axis=-1, keepdims=True)
    gate_rows[...] = gates
    sent[:, :width] = normed
    sent[:, width:] = (gates * kept[...]).astype(low)


def attend(query, keyval, bias, tokens, small, member, kept, gain_at, pieces, spots):
    rows, width = tokens.shape
    query_width = query.shape[1]
    lanes = small.shape[0]
    low = jnp.bfloat16

    def kernel(*refs):
        attend_kernel(len(pieces), *refs[:7], gain_at, *refs[7:])

    return pl.pallas_call(
        kernel,
        in_specs=[INSIDE] * 7 + [SCALARS] + [ANYWHERE] * len(pieces),
        out_specs=[INSIDE] * 5,
        out_shape=[
            jax.ShapeDtypeStruct((rows, query_width), low),
            jax.ShapeDtypeStruct((rows, 128), jnp.float32),
            jax.ShapeDtypeStruct((rows, width), jnp.float32),
            jax.ShapeDtypeStruct((rows, width + lanes), low),
            jax.ShapeDtypeStruct((rows, lanes), jnp.float32),
        ],
        scratch_shapes=[
            pltpu.VMEM((query_width, width), low),
            pltpu.SemaphoreType.DMA((len(pieces) * pieces[0].shape[0],)),
        ],
        compiler_params=pltpu.CompilerParams(vmem_limit_bytes=VMEM_BYTES),
        cost_estimate=cost(2 * rows * width * width + 8 * rows * query_width * bias.shape[1], *pieces),
        name="attend",
    )(query, keyval, bias, tokens, small, member, kept, spots, *pieces)


def sorted_copies(place, source, others, own, sems):
    core, member = place[0], place[1]
    copies = []
    for r, (other, mine) in enumerate(zip(others, own)):
        copies.append(
            pltpu.make_async_copy(source.at[:, 1 - core, member ^ r], other, sems.at[2 * r])
        )
        copies.append(
            pltpu.make_async_copy(source.at[:, core, member ^ r], mine, sems.at[2 * r + 1])
        )
    return copies


def grad_shapes(cut, rows, columns):
    low = jnp.bfloat16
    if cut:
        block = rows // 32
        return (
            [jax.ShapeDtypeStruct((4, block, columns), low)] * 8,
            pltpu.VMEM((4, 2, 4, block, columns), low),
        )
    return (
        [jax.ShapeDtypeStruct((1, 1, 1, rows, columns), low)],
        pltpu.VMEM((1, 1, 1, rows, columns), low),
    )


def grad_copies(cut, place, source, outs, sems):
    if cut:
        return sorted_copies(place, source, outs[:4], outs[4:], sems)
    return [pltpu.make_async_copy(source, outs[0], sems.at[0])]


def turn_kernel(
    count,
    cut,
    gain_at,
    place,
    spots,
    normed_grad,
    residual,
    grad_out,
    small,
    gate_rows,
    member,
    kept,
    normed,
    attended,
    *refs,
):
    pieces = refs[:count]
    refs = refs[count:]
    outs = refs[: (8 if cut else 1)]
    resid_grad, head_grad, weight, weight_grad, sems, out_sems = refs[len(outs) :]
    low = jnp.bfloat16
    rows, width = residual.shape
    lanes = gate_rows.shape[1]
    copies = weight_copies(spots, pieces, weight, sems)
    for copy in copies:
        copy.start()
    lane = lax.broadcasted_iota(jnp.int32, (rows, lanes), 1)
    gates = gate_rows[...]
    gate_grads = normed_grad[:, width:] * kept[...]
    chosen_grad = gates * (gate_grads - jnp.sum(gates * gate_grads, axis=-1, keepdims=True))
    logit_grad = (chosen_grad * member[...]).astype(low)
    hidden = residual[...]
    scale = mean_square_scale(hidden)
    row_grad = normed_grad[:, :width] + dot_plain(logit_grad, small[...].astype(low))
    gain = small[gain_at : gain_at + 1, :]
    scaled = row_grad * gain
    total_grad = (
        grad_out[...].astype(jnp.float32)
        + scale * scaled
        - hidden * (scale * scale * scale) * jnp.mean(scaled * hidden, axis=-1, keepdims=True)
    )
    resid_grad[...] = total_grad
    attn_grad = total_grad.astype(low)
    shape = weight_grad.shape[:-1]
    gain_grad = (row_grad * hidden * scale).astype(low)
    picks = jnp.where(lane == gain_at, 1.0, 0.0).astype(low)
    weight_grad[..., width:] = (
        (dot_left(normed[...][:, :width], logit_grad) + dot_left(gain_grad, picks))
        .astype(low)
        .reshape(shape + (lanes,))
    )
    for start in range(0, width, 512):
        weight_grad[..., start : start + 512] = (
            dot_left(attended[...], attn_grad[:, start : start + 512])
            .astype(low)
            .reshape(shape + (512,))
        )
    out_copies = grad_copies(cut, place, weight_grad, outs, out_sems)
    for copy in out_copies:
        copy.start()
    for copy in copies:
        copy.wait()
    head_grad[...] = dot_right(attn_grad, weight[...]).astype(low)
    for copy in out_copies:
        copy.wait()


def turn(place, spots, operands, pieces, cut, gain_at):
    residual, gate_rows, attended = operands[1], operands[4], operands[8]
    rows, width = residual.shape
    query_width = attended.shape[1]
    low = jnp.bfloat16
    grads, held = grad_shapes(cut, query_width, width + gate_rows.shape[1])
    return pl.pallas_call(
        partial(turn_kernel, len(pieces), cut, gain_at),
        in_specs=[SCALARS, SCALARS] + [INSIDE] * len(operands) + [ANYWHERE] * len(pieces),
        out_specs=[ANYWHERE] * len(grads) + [INSIDE] * 2,
        out_shape=grads
        + [
            jax.ShapeDtypeStruct((rows, width), jnp.float32),
            jax.ShapeDtypeStruct((rows, query_width), low),
        ],
        scratch_shapes=[
            pltpu.VMEM((query_width, width), low),
            held,
            pltpu.SemaphoreType.DMA((len(pieces) * pieces[0].shape[0],)),
            pltpu.SemaphoreType.DMA((8,)),
        ],
        compiler_params=pltpu.CompilerParams(vmem_limit_bytes=VMEM_BYTES),
        cost_estimate=cost(4 * rows * width * width, *pieces, *pieces),
        name="turn",
    )(place, spots, *operands, *pieces)


def attend_back_kernel(
    head_grad, query, keyval, bias, log_totals, cosine, sine, query_grad, keyval_grad, totals
):
    low = jnp.bfloat16
    rows = query.shape[0]
    kv_width = keyval.shape[1] // 2
    pair_lanes = 2 * HEAD_DIM
    repeat = HEADS // KV_HEADS
    totals[...] = log_totals[...].T

    @pl.loop(0, KV_HEADS // 2)
    def _(pair):
        key_at = pl.ds(pl.multiple_of(pair * pair_lanes, pair_lanes), pair_lanes)
        value_at = pl.ds(pl.multiple_of(kv_width + pair * pair_lanes, pair_lanes), pair_lanes)
        keys = both_places(keyval[:, key_at])
        values = both_places(keyval[:, value_at])
        key_grads = [[None, None], [None, None]]
        value_grads = [[None, None], [None, None]]
        for i in range(repeat):
            at = pl.ds(pl.multiple_of((pair * repeat + i) * pair_lanes, pair_lanes), pair_lanes)
            queries = query[:, at]
            grads = head_grad[:, at]
            query_part = jnp.zeros((rows, pair_lanes), jnp.float32)
            for a in range(2):
                head = 2 * i + a
                g = head // repeat
                total = totals[pl.ds(pair * (2 * repeat) + head, 1), :]
                weights = jnp.exp(dot_right(keys[g][a], queries) + bias[...] - total)
                weight_grads = dot_right(values[g][a], grads)
                delta = jnp.sum(weights * weight_grads, axis=0, keepdims=True)
                score_grads = (weights * (weight_grads - delta)).astype(low)
                value_part = dot_plain(weights.astype(low), grads)
                key_part = dot_plain(score_grads, queries)
                query_part += dot_left(score_grads, keys[g][a])
                if key_grads[g][a] is None:
                    key_grads[g][a], value_grads[g][a] = key_part, value_part
                else:
                    key_grads[g][a] += key_part
                    value_grads[g][a] += value_part
            query_part = query_part * (HEAD_DIM**-0.5)
            query_part = query_part * cosine[...] - swap_halves(query_part) * sine[...]
            query_grad[:, at] = query_part.astype(low)
        low_lane = lax.broadcasted_iota(jnp.int32, (keyval.shape[0], pair_lanes), 1) < HEAD_DIM
        for at, found in ((key_at, key_grads), (value_at, value_grads)):
            keyval_grad[:, at] = jnp.where(
                low_lane,
                found[0][0] + pltpu.roll(found[0][1], HEAD_DIM, 1),
                pltpu.roll(found[1][0], HEAD_DIM, 1) + found[1][1],
            ).astype(low)


def attend_back(head_grad, query, keyval, bias, log_totals, cosine, sine):
    rows, query_width = query.shape
    low = jnp.bfloat16
    return pl.pallas_call(
        attend_back_kernel,
        in_specs=[INSIDE] * 7,
        out_specs=[INSIDE] * 2,
        out_shape=[
            jax.ShapeDtypeStruct((rows, query_width), low),
            jax.ShapeDtypeStruct(keyval.shape, low),
        ],
        scratch_shapes=[pltpu.VMEM((128, rows), jnp.float32)],
        compiler_params=pltpu.CompilerParams(vmem_limit_bytes=VMEM_BYTES),
        cost_estimate=cost(20 * rows * query_width * keyval.shape[0], query, keyval, bias),
        name="attend_back",
    )(head_grad, query, keyval, bias, log_totals, cosine, sine)


def leave_kernel(
    count,
    cut,
    gain_at,
    place,
    spots,
    keyval_sum,
    query_grad,
    normed,
    tokens,
    resid_grad,
    small,
    cosine,
    sine,
    *refs,
):
    pieces = refs[:count]
    refs = refs[count:]
    outs = refs[: (8 if cut else 1)]
    input_grad, weight, weight_grad, joined, sems, out_sems = refs[len(outs) :]
    low = jnp.bfloat16
    rows, width = tokens.shape
    query_width = query_grad.shape[1]
    kv_width = keyval_sum.shape[1] // 2
    qkv_width = query_width + 2 * kv_width
    pair = 2 * HEAD_DIM
    copies = weight_copies(spots, pieces, weight, sems)
    for copy in copies:
        copy.start()
    joined[:, :query_width] = query_grad[...]
    for start in range(0, kv_width, pair):
        part = keyval_sum[:, start : start + pair]
        part = part * cosine[...] - swap_halves(part) * sine[...]
        joined[:, query_width + start : query_width + start + pair] = part.astype(low)
    joined[:, query_width + kv_width :] = keyval_sum[:, kv_width:].astype(low)
    shape = weight_grad.shape[:-1]
    for start in range(0, qkv_width, 512):
        weight_grad[..., start : start + 512] = (
            dot_left(normed[...], joined[:, start : start + 512]).astype(low).reshape(shape + (512,))
        )
    for copy in copies:
        copy.wait()
    row_grad = dot_right(joined[...], weight[:, :qkv_width])
    inputs = tokens[...].astype(jnp.float32)
    scale = mean_square_scale(inputs)
    lanes = weight_grad.shape[-1] - qkv_width
    lane = lax.broadcasted_iota(jnp.int32, (rows, lanes), 1)
    picks = jnp.where(lane == gain_at, 1.0, 0.0).astype(low)
    weight_grad[..., qkv_width:] = (
        dot_left((row_grad * inputs * scale).astype(low), picks).astype(low).reshape(shape + (lanes,))
    )
    out_copies = grad_copies(cut, place, weight_grad, outs, out_sems)
    for copy in out_copies:
        copy.start()
    scaled = row_grad * small[gain_at : gain_at + 1, :]
    input_grad[...] = (
        resid_grad[...]
        + scale * scaled
        - inputs * (scale * scale * scale) * jnp.mean(scaled * inputs, axis=-1, keepdims=True)
    )
    for copy in out_copies:
        copy.wait()


def leave(place, spots, operands, pieces, cut, gain_at):
    tokens, query_grad, keyval_sum = operands[3], operands[1], operands[0]
    rows, width = tokens.shape
    columns = pieces[0].shape[2]
    low = jnp.bfloat16
    grads, held = grad_shapes(cut, width, columns)
    return pl.pallas_call(
        partial(leave_kernel, len(pieces), cut, gain_at),
        in_specs=[SCALARS, SCALARS] + [INSIDE] * len(operands) + [ANYWHERE] * len(pieces),
        out_specs=[ANYWHERE] * len(grads) + [INSIDE],
        out_shape=grads + [jax.ShapeDtypeStruct((rows, width), jnp.float32)],
        scratch_shapes=[
            pltpu.VMEM((width, columns), low),
            held,
            pltpu.VMEM((rows, query_grad.shape[1] + keyval_sum.shape[1]), low),
            pltpu.SemaphoreType.DMA((len(pieces) * pieces[0].shape[0],)),
            pltpu.SemaphoreType.DMA((8,)),
        ],
        compiler_params=pltpu.CompilerParams(vmem_limit_bytes=VMEM_BYTES),
        cost_estimate=cost(4 * rows * width * columns, *pieces, *pieces),
        name="leave",
    )(place, spots, *operands, *pieces)


def expert_kernel(sources, carried, last, row_blocks, grad_blocks, row_tile, first, place, *refs):
    packed = refs[:sources]
    refs = refs[sources:]
    blocks_in = refs[:row_blocks]
    grads_in = refs[row_blocks : row_blocks + grad_blocks]
    refs = refs[row_blocks + grad_blocks :]
    if carried:
        mix_in, turn_in = refs[:2]
        refs = refs[2:]
    packed_grads = refs[:sources]
    mix_out, turn_out = refs[sources : sources + 2]
    refs = refs[sources + 2 :]
    if last:
        mix, turned = refs[:2]
        refs = refs[2:]
    else:
        mix, turned = mix_out, turn_out
    (
        rows,
        grads,
        gates,
        gate_w,
        up_w,
        down_w,
        gate_g,
        up_g,
        down_g,
        weighted,
        gate_side,
        up_side,
        load_sems,
        save_sems,
        carry_sems,
    ) = refs
    count = packed[0].shape[2]
    hidden_width = gate_w.shape[-1]
    total_rows, width = rows.shape
    lanes = gates.shape[1]
    low = jnp.bfloat16

    def moves(e, outside, gate, up, down, sems, inward):
        slot = e % 2
        found = []
        for n, array in enumerate(outside):
            core = place[0] ^ n if sources > 1 else 0
            ends = []
            for side, inner in ((0, gate), (1, up)):
                for j in range(3):
                    columns = pl.ds(j * hidden_width, hidden_width)
                    ends.append((array.at[:, side, e, :, columns], inner.at[slot, :, core, j]))
            ends.append((array.at[:, 2, e], down.at[slot, :, core]))
            for i, (outer, inner) in enumerate(ends):
                ends_now = (outer, inner) if inward else (inner, outer)
                found.append(pltpu.make_async_copy(*ends_now, sems.at[slot, 7 * n + i]))
        return found

    def loads(e):
        return moves(e, packed, gate_w, up_w, down_w, load_sems, True)

    def saves(e):
        return moves(e, packed_grads, gate_g, up_g, down_g, save_sems, False)

    carries = (
        block_copies(grads_in, grads, carry_sems, 0, pl.ds(0, width))
        + block_copies(blocks_in, rows, carry_sems, grad_blocks, pl.ds(0, width))
        + block_copies(
            blocks_in, gates, carry_sems, grad_blocks + row_blocks, pl.ds(width, lanes)
        )
    )
    sums = []
    if carried:
        at = grad_blocks + 2 * row_blocks
        sums = [
            pltpu.make_async_copy(mix_in, mix, carry_sems.at[at]),
            pltpu.make_async_copy(turn_in, turned, carry_sems.at[at + 1]),
        ]
    for copy in loads(0) + carries + sums:
        copy.start()
    for e in range(count):
        slot = e % 2
        if e + 1 < count:
            for copy in loads(e + 1):
                copy.start()
        for copy in loads(e):
            copy.wait()
        if e == 0:
            for copy in carries:
                copy.wait()
            if not carried:
                turned[:, width:] = jnp.zeros((total_rows, lanes), jnp.float32)

        @pl.loop(0, total_rows // row_tile)
        def _(tile):
            span = pl.ds(pl.multiple_of(tile * row_tile, row_tile), row_tile)
            gate_full = gate_w[slot].reshape(width, hidden_width)
            up_full = up_w[slot].reshape(width, hidden_width)
            down_full = down_w[slot].reshape(hidden_width, width)
            here = rows[span, :]
            slope = dot_right(grads[span, :], down_full)
            gate_pre = dot_plain(here, gate_full)
            up_pre = dot_plain(here, up_full)
            lane = lax.broadcasted_iota(jnp.int32, (row_tile, lanes), 1)
            chosen = lane == first[0] + e
            gate_column = jnp.sum(
                jnp.where(chosen, gates[span, :].astype(jnp.float32), 0.0), axis=1, keepdims=True
            )
            sigmoid_gate = jax.nn.sigmoid(gate_pre)
            activated = gate_pre * sigmoid_gate
            hidden = (activated * up_pre).astype(low).astype(jnp.float32)
            share = jnp.sum(hidden * slope, axis=1, keepdims=True)
            if e == 0 and sums:

                @pl.when(tile == 0)
                def _():
                    for copy in sums:
                        copy.wait()

            turned[span, width:] = jnp.where(chosen, share, turned[span, width:])
            part_weighted = (hidden * gate_column).astype(low)
            hidden_grad = slope * gate_column
            part_gate = (
                hidden_grad * up_pre * (sigmoid_gate + activated * (1.0 - sigmoid_gate))
            ).astype(low)
            part_up = (hidden_grad * activated).astype(low)
            weighted[span, :] = part_weighted
            gate_side[span, :] = part_gate
            up_side[span, :] = part_up
            mix_part = dot_plain(part_weighted, down_full)
            turn_part = dot_right(part_gate, gate_full) + dot_right(part_up, up_full)
            if e == 0 and not carried:
                mix[span, :] = mix_part
                turned[span, :width] = turn_part
            elif last and e == count - 1:
                mix_out[span, :] = (mix[span, :] + mix_part).astype(low)
                turn_out[span, :width] = (turned[span, :width] + turn_part).astype(low)
                turn_out[span, width:] = turned[span, width:].astype(low)
            else:
                mix[span, :] += mix_part
                turned[span, :width] += turn_part

        if e >= 2:
            for copy in saves(e - 2):
                copy.wait()
        down_g[slot] = dot_left(weighted[...], grads[...]).astype(low).reshape(down_g.shape[1:])
        gate_g[slot] = dot_left(rows[...], gate_side[...]).astype(low).reshape(gate_g.shape[1:])
        up_g[slot] = dot_left(rows[...], up_side[...]).astype(low).reshape(up_g.shape[1:])
        for copy in saves(e):
            copy.start()
    for e in range(max(0, count - 2), count):
        for copy in saves(e):
            copy.wait()


def expert_pass(first, place, rows, grads, packed, carry, last):
    sources = len(packed)
    levels, _, count, part, width = packed[0].shape
    hidden_width = levels * sources * part
    total_rows = sum(block.shape[0] for block in rows)
    lanes = rows[0].shape[1] - width
    low = jnp.bfloat16
    wide = jnp.float32
    carried = carry is not None
    flops = 18 * total_rows * count * hidden_width * width
    side = pltpu.VMEM((2, levels, sources, 3, part, hidden_width), low)
    sides = [side, side, pltpu.VMEM((2, levels, sources, part, width), low)]
    sums = [(total_rows, width), (total_rows, width + lanes)]
    return pl.pallas_call(
        partial(
            expert_kernel, sources, carried, last, len(rows), len(grads), min(512, total_rows)
        ),
        in_specs=[SCALARS, SCALARS]
        + [ANYWHERE] * (sources + len(rows) + len(grads) + (2 if carried else 0)),
        out_specs=[ANYWHERE] * sources + [INSIDE, INSIDE],
        out_shape=[jax.ShapeDtypeStruct(packed[0].shape, low)] * sources
        + [jax.ShapeDtypeStruct(shape, low if last else wide) for shape in sums],
        scratch_shapes=([pltpu.VMEM(shape, wide) for shape in sums] if last else [])
        + [
            pltpu.VMEM((total_rows, width), low),
            pltpu.VMEM((total_rows, width), low),
            pltpu.VMEM((total_rows, lanes), low),
        ]
        + sides
        + sides
        + [pltpu.VMEM((total_rows, hidden_width), low)] * 3
        + [
            pltpu.SemaphoreType.DMA((2, 7 * sources)),
            pltpu.SemaphoreType.DMA((2, 7 * sources)),
            pltpu.SemaphoreType.DMA((2 * len(rows) + len(grads) + 2,)),
        ],
        compiler_params=pltpu.CompilerParams(vmem_limit_bytes=VMEM_BYTES),
        cost_estimate=cost(flops, *packed, *packed, *rows, *grads),
        name="experts",
    )(first, place, *packed, *rows, *grads, *(carry or ()))


def unpack_kernel(chunks, *refs):
    found, (gate, up, down) = refs[:chunks], refs[chunks:]
    hidden_width = gate.shape[2]
    base = 0
    for chunk in found:
        count, part = chunk.shape[1], chunk.shape[2]
        for e in range(count):
            for side, target in ((0, gate), (1, up)):
                for j in range(3):
                    target[base + e, j * part : (j + 1) * part, :] = chunk[
                        side, e, :, j * hidden_width : (j + 1) * hidden_width
                    ].astype(jnp.float32)
            down[base + e] = chunk[2, e].astype(jnp.float32)
        base += count


def unpack(chunks, gate_shape, down_shape):
    return pl.pallas_call(
        partial(unpack_kernel, len(chunks)),
        in_specs=[INSIDE] * len(chunks),
        out_specs=[INSIDE] * 3,
        out_shape=[
            jax.ShapeDtypeStruct(gate_shape, jnp.float32),
            jax.ShapeDtypeStruct(gate_shape, jnp.float32),
            jax.ShapeDtypeStruct(down_shape, jnp.float32),
        ],
        compiler_params=pltpu.CompilerParams(vmem_limit_bytes=VMEM_BYTES),
        cost_estimate=pl.CostEstimate(flops=12 * 10**9, bytes_accessed=1, transcendentals=0),
        name="unpack",
    )(*chunks)


def cube():
    return lax.axis_size("batch") == 8 and lax.axis_size("expert") == 4


def pair_moves(size, flip):
    return [(i, i ^ flip) for i in range(size)]


def shift_moves(step):
    return [(2 * z + c, 2 * ((z + step) % 4) + c) for z in range(4) for c in range(2)]


def gather_blocks(rows, at_once=False):
    size = lax.axis_size("expert")
    if size != 4:
        stacked = lax.all_gather(rows, "expert", axis=0)
        own = lax.axis_index("expert")
        return [
            lax.dynamic_index_in_dim(stacked, own ^ r, axis=0, keepdims=False) for r in range(size)
        ]
    across, along = pair_moves(size, 1), pair_moves(size, 2)
    if at_once:
        return [rows] + [lax.ppermute(rows, "expert", pair_moves(size, r)) for r in range(1, 4)]
    half = rows.shape[0] // 2
    first = lax.ppermute(rows, "expert", across)
    second = lax.ppermute(rows, "expert", along)
    top = lax.ppermute(second[:half], "expert", across)
    bottom = lax.ppermute(first[half:], "expert", along)
    return [rows, first, second, top, bottom]


def scatter_blocks(parts):
    size = lax.axis_size("expert")
    low = jnp.bfloat16
    wide = jnp.float32
    if size != 4:
        own = lax.axis_index("expert")
        order = jnp.arange(size, dtype=jnp.int32) ^ own
        stacked = jnp.take(jnp.stack(parts), order, axis=0).astype(low)
        return lax.psum_scatter(stacked, "expert", scatter_dimension=0).astype(wide)
    across, along = pair_moves(size, 1), pair_moves(size, 2)
    half = parts[0].shape[0] // 2
    top = lax.ppermute(parts[3][:half].astype(low), "expert", across)
    bottom = lax.ppermute(parts[3][half:].astype(low), "expert", along)
    first_top = lax.ppermute(parts[1][:half].astype(low), "expert", across)
    second_bottom = lax.ppermute(parts[2][half:].astype(low), "expert", along)
    for_second = (parts[2][:half].astype(wide) + top.astype(wide)).astype(low)
    for_first = (parts[1][half:].astype(wide) + bottom.astype(wide)).astype(low)
    second_top = lax.ppermute(for_second, "expert", along)
    first_bottom = lax.ppermute(for_first, "expert", across)
    own = parts[0].astype(wide)
    return jnp.concatenate(
        [
            own[:half] + first_top.astype(wide) + second_top.astype(wide),
            own[half:] + first_bottom.astype(wide) + second_bottom.astype(wide),
        ],
        axis=0,
    )


def after(values, events):
    return lax.optimization_barrier((values, events))[0]


def shift_dense(rows):
    if not cube():
        return [lax.all_gather(rows, ("batch", "expert"), axis=0, tiled=True)]
    return [rows] + [lax.ppermute(rows, "batch", shift_moves(r)) for r in range(1, 4)]


def gather_dense(line, columns, events):
    found = [rows[:, columns] for rows in line]
    if not cube():
        return [found[0][None]], jnp.zeros((1, 1), jnp.int32), (), ()
    place = lax.axis_index("batch")
    level, core = place // 2, place % 2
    member = lax.axis_index("expert")
    mine = gather_blocks(after(jnp.stack(found), events))
    plane, far = mine[1:3], mine[3:]
    mine = mine[:3] + [jnp.concatenate(far, axis=0)]
    other = [lax.ppermute(block, "batch", pair_moves(8, 1)) for block in mine]
    spots = [
        [(((level + 4 - k) % 4) * 2 + (core ^ c)) * 4 + (member ^ r) for k in range(4)]
        for c in range(2)
        for r in range(4)
    ]
    return mine + other, jnp.array(spots, jnp.int32), plane, far


def scatter_dense(found, events, late):
    low = jnp.bfloat16
    wide = jnp.float32
    if not cube():
        values = found[0].reshape(found[0].shape[3:])
        total = lax.psum_scatter(values, ("batch", "expert"), scatter_dimension=0, tiled=True)
        return total.astype(wide)
    level = lax.axis_index("batch") // 2
    received = {r: lax.ppermute(found[r], "batch", pair_moves(8, 1)) for r in (3, 1, 2, 0)}
    received = after(received, events)
    parts = [found[4 + r].astype(wide) + received[r].astype(wide) for r in range(4)]
    plane = after(scatter_blocks(parts), late)
    total = lax.dynamic_index_in_dim(plane, level, axis=0, keepdims=False)
    for r in range(1, 4):
        sent = lax.dynamic_index_in_dim(plane, (level + r) % 4, axis=0, keepdims=False)
        total += lax.ppermute(sent.astype(low), "batch", shift_moves(r)).astype(wide)
    return total


def pack_sides(gate, up, down):
    def fold(values):
        count, depth, width = values.shape
        return values.reshape(count, 3, depth // 3, width).transpose(0, 2, 1, 3).reshape(down.shape)

    return jnp.stack([fold(gate), fold(up), down], axis=0)


def local(
    tokens,
    cotangent,
    attn_gain,
    query_weight,
    key_weight,
    value_weight,
    out_weight,
    ffn_gain,
    router_weight,
    gate_weight,
    up_weight,
    down_weight,
    routes,
    ranking,
):
    low = jnp.bfloat16
    wide = jnp.float32
    query_width = HEADS * HEAD_DIM
    kv_width = KV_HEADS * HEAD_DIM
    qkv_width = query_width + 2 * kv_width
    width = tokens.shape[2]
    experts_total = router_weight.shape[1]
    extra = -(-(experts_total + 2) // 128) * 128
    first_gain, second_gain = experts_total, experts_total + 1
    local_experts = gate_weight.shape[0]
    member_count = lax.axis_size("expert")
    member_id = lax.axis_index("expert")
    local_rows = tokens.shape[1]
    group_rows = local_rows * member_count
    cut = cube()
    place = jnp.stack([lax.axis_index("batch") % 2, member_id]).astype(jnp.int32)

    route_rows = routes[0]
    rank_rows = ranking[0]
    expert_lanes = jnp.arange(extra, dtype=jnp.int32)
    member = jnp.any(route_rows[:, :, None] == expert_lanes[None, None, :], axis=1)
    marks = jnp.where(
        expert_lanes[None, :] == experts_total,
        (rank_rows // 32)[:, None],
        jnp.where(expert_lanes[None, :] == experts_total + 1, (rank_rows % 32)[:, None], member),
    ).astype(low)
    grad_out = cotangent[0]
    grad_blocks = gather_blocks(jnp.concatenate([grad_out, marks], axis=1), True)
    marks_all = jnp.concatenate([block[:, width:] for block in grad_blocks], axis=0)

    small_width = qkv_width + extra
    line = shift_dense(
        jnp.concatenate(
            [
                query_weight,
                key_weight,
                value_weight,
                router_weight,
                attn_gain[:, None],
                ffn_gain[:, None],
                jnp.zeros((query_weight.shape[0], extra - experts_total - 2), low),
                out_weight,
            ],
            axis=1,
        )
    )
    qkv_pieces, qkv_spots, plane, far = gather_dense(
        line, slice(0, small_width), grad_blocks
    )
    out_pieces, out_spots, out_plane, _ = gather_dense(line, slice(small_width, None), far)
    chunks = (0, 3, local_experts)
    packed_all = []
    for a, b in zip(chunks[:-1], chunks[1:]):
        packed = pack_sides(gate_weight[a:b], up_weight[a:b], down_weight[a:b])
        if a > 0 and cut:
            packed = after(packed, line[1:])
        packed_all.append(lax.all_gather(packed, "batch", axis=0))

    row_ids = member_id * local_rows + jnp.arange(local_rows, dtype=jnp.int32)
    half_dim = HEAD_DIM // 2
    frequency = THETA ** (-jnp.arange(half_dim, dtype=wide) / half_dim)
    angles = place_of(row_ids).astype(wide)[:, None] * frequency[None, :]
    cosine = jnp.tile(jnp.cos(angles), (1, 4))
    sine_part = jnp.tile(jnp.concatenate([-jnp.sin(angles), jnp.sin(angles)], axis=1), (1, 2))
    normed, query, keyval, small = enter(
        tokens[0], cosine, sine_part, qkv_pieces, qkv_spots, first_gain, query_width, kv_width
    )

    rank_all = (
        marks_all[:, experts_total].astype(wide) * 32 + marks_all[:, experts_total + 1].astype(wide)
    )
    earlier = (rank_all[None, :] < rank_rows.astype(wide)[:, None]).astype(low)
    before = product(earlier, marks_all)
    capacity = 5 * group_rows * route_rows.shape[1] // (4 * experts_total)
    member = member.astype(wide)
    kept = jnp.where(before < capacity, member, 0.0)

    keyval_blocks = gather_blocks(after(keyval, out_plane))
    if member_count == 4:
        ordered = keyval_blocks[:3] + [jnp.concatenate(keyval_blocks[3:], axis=0)]
        away = 1 << 20
        keys = jnp.concatenate(
            [
                lax.select_n(member_id, *ordered),
                lax.select_n(member_id ^ 1, *ordered),
                keyval,
            ],
            axis=0,
        )
        starts = [
            jnp.where(member_id >= 1, 0, away),
            jnp.where(member_id >= 2, local_rows, away),
            member_id * local_rows,
        ]
    else:
        keys = jnp.concatenate(keyval_blocks, axis=0)
        starts = [(member_id ^ r) * local_rows for r in range(member_count)]
    key_ids = jnp.concatenate([s + jnp.arange(local_rows, dtype=jnp.int32) for s in starts])
    bias = jnp.where(visible(row_ids, key_ids), 0.0, -1e30).astype(wide)
    attended, log_totals, residual, sent, gate_rows = attend(
        query, keys, bias, tokens[0], small, member, kept, second_gain, out_pieces, out_spots
    )
    sent_blocks = gather_blocks(sent)

    carry, chunk_grads = None, []
    for packed, a, b in zip(packed_all, chunks[:-1], chunks[1:]):
        first = (member_id * local_experts + a).astype(jnp.int32).reshape(1)
        packed_grad, mixture_all, row_grad = expert_pass(
            first, place, sent_blocks, grad_blocks, [packed], carry, b == local_experts
        )
        carry = (mixture_all, row_grad)
        chunk_grads.append(packed_grad)

    def blocks_of(values):
        return [values[r * local_rows : (r + 1) * local_rows] for r in range(member_count)]

    normed_grad = scatter_blocks(blocks_of(row_grad))
    turned = turn(
        place,
        out_spots,
        (
            normed_grad,
            residual,
            grad_out,
            small,
            gate_rows,
            member,
            kept,
            sent,
            attended,
        ),
        out_pieces,
        cut,
        second_gain,
    )
    out_found = turned[:-2]
    resid_grad, head_grad = turned[-2:]
    query_grad, key_grads = attend_back(
        head_grad, query, keys, bias.T, log_totals, cosine, sine_part
    )
    totals = [lax.psum_scatter(chunk_grads[0], "batch", scatter_dimension=0)]
    if member_count == 4:
        zero = jnp.zeros((), low)
        for_first, for_second, for_own = blocks_of(key_grads)[:3]
        key_parts = []
        for r in range(4):
            part = jnp.where(member_id == r, for_first, zero)
            part += jnp.where(member_id ^ 1 == r, for_second, zero)
            key_parts.append(part + for_own if r == 0 else part)
    else:
        key_parts = blocks_of(key_grads)
    keyval_sum = scatter_blocks(key_parts)
    for packed_grad in chunk_grads[1:]:
        packed_grad = after(packed_grad, (totals[-1], keyval_sum))
        totals.append(lax.psum_scatter(packed_grad, "batch", scatter_dimension=0))
    keyval_sum = after(keyval_sum, totals[0])
    left = leave(
        place,
        qkv_spots,
        (
            keyval_sum,
            query_grad,
            normed,
            tokens[0],
            resid_grad,
            small,
            cosine,
            sine_part,
        ),
        qkv_pieces,
        cut,
        first_gain,
    )
    qkv_found, input_grad = left[:-1], left[-1]
    mixture = scatter_blocks(blocks_of(after(mixture_all, resid_grad)))
    result = (residual + mixture).astype(low)
    out_sum = scatter_dense(out_found, keyval_sum, ())
    qkv_sum = scatter_dense(qkv_found, (), ())
    gate_total, up_total, down_total = unpack(totals, gate_weight.shape, down_weight.shape)
    return (
        result[None],
        input_grad[None],
        qkv_sum[:, qkv_width + first_gain],
        qkv_sum[:, :query_width],
        qkv_sum[:, query_width : query_width + kv_width],
        qkv_sum[:, query_width + kv_width : qkv_width],
        out_sum[:, :width],
        out_sum[:, width + second_gain],
        out_sum[:, width : width + experts_total],
        gate_total,
        up_total,
        down_total,
    )


def solution(mesh):
    return jax.shard_map(
        local,
        mesh=mesh,
        in_specs=(
            P("batch", "expert", None),
            P("batch", "expert", None),
            P(("batch", "expert")),
            P(("batch", "expert"), None),
            P(("batch", "expert"), None),
            P(("batch", "expert"), None),
            P(("batch", "expert"), None),
            P(("batch", "expert")),
            P(("batch", "expert"), None),
            P("expert", "batch", None),
            P("expert", "batch", None),
            P("expert", "batch", None),
            P("batch", "expert", None),
            P("batch", "expert"),
        ),
        out_specs=(
            P("batch", "expert", None),
            P("batch", "expert", None),
            P(("batch", "expert")),
            P(("batch", "expert"), None),
            P(("batch", "expert"), None),
            P(("batch", "expert"), None),
            P(("batch", "expert"), None),
            P(("batch", "expert")),
            P(("batch", "expert"), None),
            P("expert", "batch", None),
            P("expert", "batch", None),
            P("expert", "batch", None),
        ),
        check_vma=False,
    )
```

```python
from functools import partial

import jax
import jax.numpy as jnp
from jax import lax
from jax.experimental import pallas as pl
from jax.experimental.pallas import tpu as pltpu
from jax.sharding import PartitionSpec as P

HEADS = 24
KV_HEADS = 8
HEAD_DIM = 64
PROMPT = 512
CLEN = 256


EPS = 1e-06
THETA = 10000.0


def product(left, right):
    return jnp.dot(left, right, preferred_element_type=jnp.float32)


def place_of(row_ids):
    return jnp.where(row_ids < PROMPT, row_ids, PROMPT + (row_ids - PROMPT) % CLEN)


def visible(query_ids, key_ids):
    causal = key_ids[None, :] <= query_ids[:, None]
    same_run = (key_ids[None, :] - PROMPT) // CLEN == (query_ids[:, None] - PROMPT) // CLEN
    return causal & ((key_ids[None, :] < PROMPT) | same_run)


def dot_plain(left, right):
    return lax.dot_general(left, right, (((1,), (0,)), ((), ())), preferred_element_type=jnp.float32)


def dot_right(left, right):
    return lax.dot_general(left, right, (((1,), (1,)), ((), ())), preferred_element_type=jnp.float32)


def dot_left(left, right):
    return lax.dot_general(left, right, (((0,), (0,)), ((), ())), preferred_element_type=jnp.float32)


ANYWHERE = pl.BlockSpec(memory_space=pl.ANY)
INSIDE = pl.BlockSpec(memory_space=pltpu.VMEM)
SCALARS = pl.BlockSpec(memory_space=pltpu.SMEM)
VMEM_BYTES = 60 * 1024 * 1024


def cost(flops, *arrays):
    return pl.CostEstimate(flops=1, bytes_accessed=1, transcendentals=0)


def weight_copies(spots, pieces, target, sems):
    copies = []
    for p, piece in enumerate(pieces):
        blocks, rows = piece.shape[0], piece.shape[1]
        for k in range(blocks):
            place = pl.multiple_of(spots[p, k] * rows, rows)
            copies.append(
                pltpu.make_async_copy(
                    piece.at[k], target.at[pl.ds(place, rows)], sems.at[p * blocks + k]
                )
            )
    return copies


def block_copies(blocks, target, sems, first, columns=None):
    copies = []
    start = 0
    for i, block in enumerate(blocks):
        rows = block.shape[0]
        source = block if columns is None else block.at[:, columns]
        copies.append(
            pltpu.make_async_copy(source, target.at[pl.ds(start, rows)], sems.at[first + i])
        )
        start += rows
    return copies


def swap_halves(values):
    half = HEAD_DIM // 2
    lane = lax.broadcasted_iota(jnp.int32, values.shape, 1)
    return jnp.where(
        lane % HEAD_DIM < half,
        pltpu.roll(values, 2 * HEAD_DIM - half, 1),
        pltpu.roll(values, half, 1),
    )


def mean_square_scale(values):
    return lax.rsqrt(jnp.mean(values * values, axis=-1, keepdims=True) + EPS)


def enter_kernel(count, gain_at, spots, tokens, cosine, sine, *refs):
    pieces = refs[:count]
    normed, query, keyval, small, weight, sems = refs[count:]
    low = jnp.bfloat16
    copies = weight_copies(spots, pieces, weight, sems)
    for copy in copies:
        copy.start()
    inputs = tokens[...].astype(jnp.float32)
    scaled = inputs * mean_square_scale(inputs)
    for copy in copies:
        copy.wait()
    query_width = query.shape[1]
    kv_width = keyval.shape[1] // 2
    qkv_width = query_width + 2 * kv_width
    turned = weight[:, qkv_width:].astype(jnp.float32).T
    small[...] = turned
    rows = (scaled * turned[gain_at : gain_at + 1]).astype(low)
    normed[...] = rows
    pair = 2 * HEAD_DIM
    scale = HEAD_DIM**-0.5
    for start in range(0, query_width + kv_width, 512):
        product_part = dot_plain(rows, weight[:, start : start + 512])
        for offset in range(0, 512, pair):
            part = product_part[:, offset : offset + pair]
            part = part * cosine[...] + swap_halves(part) * sine[...]
            at = start + offset
            if at < query_width:
                query[:, at : at + pair] = (part * scale).astype(low)
            else:
                keyval[:, at - query_width : at - query_width + pair] = part.astype(low)
    keyval[:, kv_width:] = dot_plain(
        rows, weight[:, query_width + kv_width : qkv_width]
    ).astype(low)


def enter(tokens, cosine, sine, pieces, spots, gain_at, query_width, kv_width):
    rows, width = tokens.shape
    columns = pieces[0].shape[2]
    low = jnp.bfloat16
    return pl.pallas_call(
        partial(enter_kernel, len(pieces), gain_at),
        in_specs=[SCALARS, INSIDE, INSIDE, INSIDE] + [ANYWHERE] * len(pieces),
        out_specs=[INSIDE] * 4,
        out_shape=[
            jax.ShapeDtypeStruct((rows, width), low),
            jax.ShapeDtypeStruct((rows, query_width), low),
            jax.ShapeDtypeStruct((rows, 2 * kv_width), low),
            jax.ShapeDtypeStruct((columns - query_width - 2 * kv_width, width), jnp.float32),
        ],
        scratch_shapes=[
            pltpu.VMEM((width, columns), low),
            pltpu.SemaphoreType.DMA((len(pieces) * pieces[0].shape[0],)),
        ],
        compiler_params=pltpu.CompilerParams(vmem_limit_bytes=VMEM_BYTES),
        cost_estimate=cost(2 * rows * width * columns, *pieces),
        name="enter",
    )(spots, tokens, cosine, sine, *pieces)


def both_places(values):
    wide = values.astype(jnp.float32)
    low_lane = lax.broadcasted_iota(jnp.int32, values.shape, 1) < HEAD_DIM
    moved = pltpu.roll(wide, HEAD_DIM, 1)
    kind = values.dtype
    return [
        [jnp.where(low_lane, wide, 0.0).astype(kind), jnp.where(low_lane, 0.0, moved).astype(kind)],
        [jnp.where(low_lane, moved, 0.0).astype(kind), jnp.where(low_lane, 0.0, wide).astype(kind)],
    ]


def attend_kernel(
    count, query, keyval, bias, tokens, small, member, kept, gain_at, spots, *refs
):
    pieces = refs[:count]
    attended, log_totals, residual, sent, gate_rows, weight, sems = refs[count:]
    low = jnp.bfloat16
    rows = query.shape[0]
    width = tokens.shape[1]
    kv_width = keyval.shape[1] // 2
    pair_lanes = 2 * HEAD_DIM
    repeat = HEADS // KV_HEADS
    copies = weight_copies(spots, pieces, weight, sems)
    for copy in copies:
        copy.start()
    log_totals[...] = jnp.zeros_like(log_totals)
    lane = lax.broadcasted_iota(jnp.int32, log_totals.shape, 1)

    @pl.loop(0, KV_HEADS // 2)
    def _(pair):
        at = pl.ds(pl.multiple_of(pair * pair_lanes, pair_lanes), pair_lanes)
        keys = both_places(keyval[:, at])
        at = pl.ds(pl.multiple_of(kv_width + pair * pair_lanes, pair_lanes), pair_lanes)
        values = both_places(keyval[:, at])
        for i in range(repeat):
            at = pl.ds(pl.multiple_of((pair * repeat + i) * pair_lanes, pair_lanes), pair_lanes)
            queries = query[:, at]
            total = jnp.zeros((rows, pair_lanes), jnp.float32)
            for a in range(2):
                head = 2 * i + a
                scores = dot_right(queries, keys[head // repeat][a]) + bias[...]
                peak = jnp.max(scores, axis=-1, keepdims=True)
                lifted = jnp.exp(scores - peak)
                row_total = jnp.sum(lifted, axis=-1, keepdims=True)
                weights_low = (lifted * (1.0 / row_total)).astype(low)
                total += dot_plain(weights_low, values[head // repeat][a])
                log_totals[...] = jnp.where(
                    lane == pair * (2 * repeat) + head, peak + jnp.log(row_total), log_totals[...]
                )
            attended[:, at] = total.astype(low)

    for copy in copies:
        copy.wait()
    hidden = tokens[...].astype(jnp.float32) + dot_plain(attended[...], weight[...])
    residual[...] = hidden
    gain = small[gain_at : gain_at + 1, :]
    normed = (hidden * mean_square_scale(hidden) * gain).astype(low)
    logits = dot_right(normed, small[...].astype(low))
    chosen = member[...] > 0.0
    logits = jnp.where(chosen, logits, -1e30)
    lifted = jnp.where(chosen, jnp.exp(logits - jnp.max(logits, axis=-1, keepdims=True)), 0.0)
    gates = lifted / jnp.sum(lifted, axis=-1, keepdims=True)
    gate_rows[...] = gates
    sent[:, :width] = normed
    sent[:, width:] = (gates * kept[...]).astype(low)


def attend(query, keyval, bias, tokens, small, member, kept, gain_at, pieces, spots):
    rows, width = tokens.shape
    query_width = query.shape[1]
    lanes = small.shape[0]
    low = jnp.bfloat16

    def kernel(*refs):
        attend_kernel(len(pieces), *refs[:7], gain_at, *refs[7:])

    return pl.pallas_call(
        kernel,
        in_specs=[INSIDE] * 7 + [SCALARS] + [ANYWHERE] * len(pieces),
        out_specs=[INSIDE] * 5,
        out_shape=[
            jax.ShapeDtypeStruct((rows, query_width), low),
            jax.ShapeDtypeStruct((rows, 128), jnp.float32),
            jax.ShapeDtypeStruct((rows, width), jnp.float32),
            jax.ShapeDtypeStruct((rows, width + lanes), low),
            jax.ShapeDtypeStruct((rows, lanes), jnp.float32),
        ],
        scratch_shapes=[
            pltpu.VMEM((query_width, width), low),
            pltpu.SemaphoreType.DMA((len(pieces) * pieces[0].shape[0],)),
        ],
        compiler_params=pltpu.CompilerParams(vmem_limit_bytes=VMEM_BYTES),
        cost_estimate=cost(2 * rows * width * width + 8 * rows * query_width * bias.shape[1], *pieces),
        name="attend",
    )(query, keyval, bias, tokens, small, member, kept, spots, *pieces)


def sorted_copies(place, source, others, own, sems):
    core, member = place[0], place[1]
    copies = []
    for r, (other, mine) in enumerate(zip(others, own)):
        copies.append(
            pltpu.make_async_copy(source.at[:, 1 - core, member ^ r], other, sems.at[2 * r])
        )
        copies.append(
            pltpu.make_async_copy(source.at[:, core, member ^ r], mine, sems.at[2 * r + 1])
        )
    return copies


def grad_shapes(cut, rows, columns):
    low = jnp.bfloat16
    if cut:
        block = rows // 32
        return (
            [jax.ShapeDtypeStruct((4, block, columns), low)] * 8,
            pltpu.VMEM((4, 2, 4, block, columns), low),
        )
    return (
        [jax.ShapeDtypeStruct((1, 1, 1, rows, columns), low)],
        pltpu.VMEM((1, 1, 1, rows, columns), low),
    )


def grad_copies(cut, place, source, outs, sems):
    if cut:
        return sorted_copies(place, source, outs[:4], outs[4:], sems)
    return [pltpu.make_async_copy(source, outs[0], sems.at[0])]


def turn_kernel(
    count,
    cut,
    gain_at,
    place,
    spots,
    normed_grad,
    residual,
    grad_out,
    small,
    gate_rows,
    member,
    kept,
    normed,
    attended,
    *refs,
):
    pieces = refs[:count]
    refs = refs[count:]
    outs = refs[: (8 if cut else 1)]
    resid_grad, head_grad, weight, weight_grad, sems, out_sems = refs[len(outs) :]
    low = jnp.bfloat16
    rows, width = residual.shape
    lanes = gate_rows.shape[1]
    copies = weight_copies(spots, pieces, weight, sems)
    for copy in copies:
        copy.start()
    lane = lax.broadcasted_iota(jnp.int32, (rows, lanes), 1)
    gates = gate_rows[...]
    gate_grads = normed_grad[:, width:] * kept[...]
    chosen_grad = gates * (gate_grads - jnp.sum(gates * gate_grads, axis=-1, keepdims=True))
    logit_grad = (chosen_grad * member[...]).astype(low)
    hidden = residual[...]
    scale = mean_square_scale(hidden)
    row_grad = normed_grad[:, :width] + dot_plain(logit_grad, small[...].astype(low))
    gain = small[gain_at : gain_at + 1, :]
    scaled = row_grad * gain
    total_grad = (
        grad_out[...].astype(jnp.float32)
        + scale * scaled
        - hidden * (scale * scale * scale) * jnp.mean(scaled * hidden, axis=-1, keepdims=True)
    )
    resid_grad[...] = total_grad
    attn_grad = total_grad.astype(low)
    shape = weight_grad.shape[:-1]
    gain_grad = (row_grad * hidden * scale).astype(low)
    picks = jnp.where(lane == gain_at, 1.0, 0.0).astype(low)
    weight_grad[..., width:] = (
        (dot_left(normed[...][:, :width], logit_grad) + dot_left(gain_grad, picks))
        .astype(low)
        .reshape(shape + (lanes,))
    )
    for start in range(0, width, 512):
        weight_grad[..., start : start + 512] = (
            dot_left(attended[...], attn_grad[:, start : start + 512])
            .astype(low)
            .reshape(shape + (512,))
        )
    out_copies = grad_copies(cut, place, weight_grad, outs, out_sems)
    for copy in out_copies:
        copy.start()
    for copy in copies:
        copy.wait()
    head_grad[...] = dot_right(attn_grad, weight[...]).astype(low)
    for copy in out_copies:
        copy.wait()


def turn(place, spots, operands, pieces, cut, gain_at):
    residual, gate_rows, attended = operands[1], operands[4], operands[8]
    rows, width = residual.shape
    query_width = attended.shape[1]
    low = jnp.bfloat16
    grads, held = grad_shapes(cut, query_width, width + gate_rows.shape[1])
    return pl.pallas_call(
        partial(turn_kernel, len(pieces), cut, gain_at),
        in_specs=[SCALARS, SCALARS] + [INSIDE] * len(operands) + [ANYWHERE] * len(pieces),
        out_specs=[ANYWHERE] * len(grads) + [INSIDE] * 2,
        out_shape=grads
        + [
            jax.ShapeDtypeStruct((rows, width), jnp.float32),
            jax.ShapeDtypeStruct((rows, query_width), low),
        ],
        scratch_shapes=[
            pltpu.VMEM((query_width, width), low),
            held,
            pltpu.SemaphoreType.DMA((len(pieces) * pieces[0].shape[0],)),
            pltpu.SemaphoreType.DMA((8,)),
        ],
        compiler_params=pltpu.CompilerParams(vmem_limit_bytes=VMEM_BYTES),
        cost_estimate=cost(4 * rows * width * width, *pieces, *pieces),
        name="turn",
    )(place, spots, *operands, *pieces)


def attend_back_kernel(
    head_grad, query, keyval, bias, log_totals, cosine, sine, query_grad, keyval_grad, totals
):
    low = jnp.bfloat16
    rows = query.shape[0]
    kv_width = keyval.shape[1] // 2
    pair_lanes = 2 * HEAD_DIM
    repeat = HEADS // KV_HEADS
    totals[...] = log_totals[...].T

    @pl.loop(0, KV_HEADS // 2)
    def _(pair):
        key_at = pl.ds(pl.multiple_of(pair * pair_lanes, pair_lanes), pair_lanes)
        value_at = pl.ds(pl.multiple_of(kv_width + pair * pair_lanes, pair_lanes), pair_lanes)
        keys = both_places(keyval[:, key_at])
        values = both_places(keyval[:, value_at])
        key_grads = [[None, None], [None, None]]
        value_grads = [[None, None], [None, None]]
        for i in range(repeat):
            at = pl.ds(pl.multiple_of((pair * repeat + i) * pair_lanes, pair_lanes), pair_lanes)
            queries = query[:, at]
            grads = head_grad[:, at]
            query_part = jnp.zeros((rows, pair_lanes), jnp.float32)
            for a in range(2):
                head = 2 * i + a
                g = head // repeat
                total = totals[pl.ds(pair * (2 * repeat) + head, 1), :]
                weights = jnp.exp(dot_right(keys[g][a], queries) + bias[...] - total)
                weight_grads = dot_right(values[g][a], grads)
                delta = jnp.sum(weights * weight_grads, axis=0, keepdims=True)
                score_grads = (weights * (weight_grads - delta)).astype(low)
                value_part = dot_plain(weights.astype(low), grads)
                key_part = dot_plain(score_grads, queries)
                query_part += dot_left(score_grads, keys[g][a])
                if key_grads[g][a] is None:
                    key_grads[g][a], value_grads[g][a] = key_part, value_part
                else:
                    key_grads[g][a] += key_part
                    value_grads[g][a] += value_part
            query_part = query_part * (HEAD_DIM**-0.5)
            query_part = query_part * cosine[...] - swap_halves(query_part) * sine[...]
            query_grad[:, at] = query_part.astype(low)
        low_lane = lax.broadcasted_iota(jnp.int32, (keyval.shape[0], pair_lanes), 1) < HEAD_DIM
        for at, found in ((key_at, key_grads), (value_at, value_grads)):
            keyval_grad[:, at] = jnp.where(
                low_lane,
                found[0][0] + pltpu.roll(found[0][1], HEAD_DIM, 1),
                pltpu.roll(found[1][0], HEAD_DIM, 1) + found[1][1],
            ).astype(low)


def attend_back(head_grad, query, keyval, bias, log_totals, cosine, sine):
    rows, query_width = query.shape
    low = jnp.bfloat16
    return pl.pallas_call(
        attend_back_kernel,
        in_specs=[INSIDE] * 7,
        out_specs=[INSIDE] * 2,
        out_shape=[
            jax.ShapeDtypeStruct((rows, query_width), low),
            jax.ShapeDtypeStruct(keyval.shape, low),
        ],
        scratch_shapes=[pltpu.VMEM((128, rows), jnp.float32)],
        compiler_params=pltpu.CompilerParams(vmem_limit_bytes=VMEM_BYTES),
        cost_estimate=cost(20 * rows * query_width * keyval.shape[0], query, keyval, bias),
        name="attend_back",
    )(head_grad, query, keyval, bias, log_totals, cosine, sine)


def leave_kernel(
    count,
    cut,
    gain_at,
    place,
    spots,
    keyval_sum,
    query_grad,
    normed,
    tokens,
    resid_grad,
    small,
    cosine,
    sine,
    *refs,
):
    pieces = refs[:count]
    refs = refs[count:]
    outs = refs[: (8 if cut else 1)]
    input_grad, weight, weight_grad, joined, sems, out_sems = refs[len(outs) :]
    low = jnp.bfloat16
    rows, width = tokens.shape
    query_width = query_grad.shape[1]
    kv_width = keyval_sum.shape[1] // 2
    qkv_width = query_width + 2 * kv_width
    pair = 2 * HEAD_DIM
    copies = weight_copies(spots, pieces, weight, sems)
    for copy in copies:
        copy.start()
    joined[:, :query_width] = query_grad[...]
    for start in range(0, kv_width, pair):
        part = keyval_sum[:, start : start + pair]
        part = part * cosine[...] - swap_halves(part) * sine[...]
        joined[:, query_width + start : query_width + start + pair] = part.astype(low)
    joined[:, query_width + kv_width :] = keyval_sum[:, kv_width:].astype(low)
    shape = weight_grad.shape[:-1]
    for start in range(0, qkv_width, 512):
        weight_grad[..., start : start + 512] = (
            dot_left(normed[...], joined[:, start : start + 512]).astype(low).reshape(shape + (512,))
        )
    for copy in copies:
        copy.wait()
    row_grad = dot_right(joined[...], weight[:, :qkv_width])
    inputs = tokens[...].astype(jnp.float32)
    scale = mean_square_scale(inputs)
    lanes = weight_grad.shape[-1] - qkv_width
    lane = lax.broadcasted_iota(jnp.int32, (rows, lanes), 1)
    picks = jnp.where(lane == gain_at, 1.0, 0.0).astype(low)
    weight_grad[..., qkv_width:] = (
        dot_left((row_grad * inputs * scale).astype(low), picks).astype(low).reshape(shape + (lanes,))
    )
    out_copies = grad_copies(cut, place, weight_grad, outs, out_sems)
    for copy in out_copies:
        copy.start()
    scaled = row_grad * small[gain_at : gain_at + 1, :]
    input_grad[...] = (
        resid_grad[...]
        + scale * scaled
        - inputs * (scale * scale * scale) * jnp.mean(scaled * inputs, axis=-1, keepdims=True)
    )
    for copy in out_copies:
        copy.wait()


def leave(place, spots, operands, pieces, cut, gain_at):
    tokens, query_grad, keyval_sum = operands[3], operands[1], operands[0]
    rows, width = tokens.shape
    columns = pieces[0].shape[2]
    low = jnp.bfloat16
    grads, held = grad_shapes(cut, width, columns)
    return pl.pallas_call(
        partial(leave_kernel, len(pieces), cut, gain_at),
        in_specs=[SCALARS, SCALARS] + [INSIDE] * len(operands) + [ANYWHERE] * len(pieces),
        out_specs=[ANYWHERE] * len(grads) + [INSIDE],
        out_shape=grads + [jax.ShapeDtypeStruct((rows, width), jnp.float32)],
        scratch_shapes=[
            pltpu.VMEM((width, columns), low),
            held,
            pltpu.VMEM((rows, query_grad.shape[1] + keyval_sum.shape[1]), low),
            pltpu.SemaphoreType.DMA((len(pieces) * pieces[0].shape[0],)),
            pltpu.SemaphoreType.DMA((8,)),
        ],
        compiler_params=pltpu.CompilerParams(vmem_limit_bytes=VMEM_BYTES),
        cost_estimate=cost(4 * rows * width * columns, *pieces, *pieces),
        name="leave",
    )(place, spots, *operands, *pieces)


def expert_kernel(sources, carried, last, row_blocks, grad_blocks, row_tile, first, place, *refs):
    packed = refs[:sources]
    refs = refs[sources:]
    blocks_in = refs[:row_blocks]
    grads_in = refs[row_blocks : row_blocks + grad_blocks]
    refs = refs[row_blocks + grad_blocks :]
    if carried:
        mix_in, turn_in = refs[:2]
        refs = refs[2:]
    packed_grads = refs[:sources]
    mix_out, turn_out = refs[sources : sources + 2]
    refs = refs[sources + 2 :]
    if last:
        mix, turned = refs[:2]
        refs = refs[2:]
    else:
        mix, turned = mix_out, turn_out
    (
        rows,
        grads,
        gates,
        gate_w,
        up_w,
        down_w,
        gate_g,
        up_g,
        down_g,
        weighted,
        gate_side,
        up_side,
        load_sems,
        save_sems,
        carry_sems,
    ) = refs
    count = packed[0].shape[2]
    hidden_width = gate_w.shape[-1]
    total_rows, width = rows.shape
    lanes = gates.shape[1]
    low = jnp.bfloat16

    def moves(e, outside, gate, up, down, sems, inward):
        slot = e % 2
        found = []
        for n, array in enumerate(outside):
            core = place[0] ^ n if sources > 1 else 0
            ends = []
            for side, inner in ((0, gate), (1, up)):
                for j in range(3):
                    columns = pl.ds(j * hidden_width, hidden_width)
                    ends.append((array.at[:, side, e, :, columns], inner.at[slot, :, core, j]))
            ends.append((array.at[:, 2, e], down.at[slot, :, core]))
            for i, (outer, inner) in enumerate(ends):
                ends_now = (outer, inner) if inward else (inner, outer)
                found.append(pltpu.make_async_copy(*ends_now, sems.at[slot, 7 * n + i]))
        return found

    def loads(e):
        return moves(e, packed, gate_w, up_w, down_w, load_sems, True)

    def saves(e):
        return moves(e, packed_grads, gate_g, up_g, down_g, save_sems, False)

    carries = (
        block_copies(grads_in, grads, carry_sems, 0, pl.ds(0, width))
        + block_copies(blocks_in, rows, carry_sems, grad_blocks, pl.ds(0, width))
        + block_copies(
            blocks_in, gates, carry_sems, grad_blocks + row_blocks, pl.ds(width, lanes)
        )
    )
    sums = []
    if carried:
        at = grad_blocks + 2 * row_blocks
        sums = [
            pltpu.make_async_copy(mix_in, mix, carry_sems.at[at]),
            pltpu.make_async_copy(turn_in, turned, carry_sems.at[at + 1]),
        ]
    for copy in loads(0) + carries + sums:
        copy.start()
    for e in range(count):
        slot = e % 2
        if e + 1 < count:
            for copy in loads(e + 1):
                copy.start()
        for copy in loads(e):
            copy.wait()
        if e == 0:
            for copy in carries:
                copy.wait()
            if not carried:
                turned[:, width:] = jnp.zeros((total_rows, lanes), jnp.float32)

        @pl.loop(0, total_rows // row_tile)
        def _(tile):
            span = pl.ds(pl.multiple_of(tile * row_tile, row_tile), row_tile)
            gate_full = gate_w[slot].reshape(width, hidden_width)
            up_full = up_w[slot].reshape(width, hidden_width)
            down_full = down_w[slot].reshape(hidden_width, width)
            here = rows[span, :]
            slope = dot_right(grads[span, :], down_full)
            gate_pre = dot_plain(here, gate_full)
            up_pre = dot_plain(here, up_full)
            lane = lax.broadcasted_iota(jnp.int32, (row_tile, lanes), 1)
            chosen = lane == first[0] + e
            gate_column = jnp.sum(
                jnp.where(chosen, gates[span, :].astype(jnp.float32), 0.0), axis=1, keepdims=True
            )
            sigmoid_gate = jax.nn.sigmoid(gate_pre)
            activated = gate_pre * sigmoid_gate
            hidden = (activated * up_pre).astype(low).astype(jnp.float32)
            share = jnp.sum(hidden * slope, axis=1, keepdims=True)
            if e == 0 and sums:

                @pl.when(tile == 0)
                def _():
                    for copy in sums:
                        copy.wait()

            turned[span, width:] = jnp.where(chosen, share, turned[span, width:])
            part_weighted = (hidden * gate_column).astype(low)
            hidden_grad = slope * gate_column
            part_gate = (
                hidden_grad * up_pre * (sigmoid_gate + activated * (1.0 - sigmoid_gate))
            ).astype(low)
            part_up = (hidden_grad * activated).astype(low)
            weighted[span, :] = part_weighted
            gate_side[span, :] = part_gate
            up_side[span, :] = part_up
            mix_part = dot_plain(part_weighted, down_full)
            turn_part = dot_right(part_gate, gate_full) + dot_right(part_up, up_full)
            if e == 0 and not carried:
                mix[span, :] = mix_part
                turned[span, :width] = turn_part
            elif last and e == count - 1:
                mix_out[span, :] = (mix[span, :] + mix_part).astype(low)
                turn_out[span, :width] = (turned[span, :width] + turn_part).astype(low)
                turn_out[span, width:] = turned[span, width:].astype(low)
            else:
                mix[span, :] += mix_part
                turned[span, :width] += turn_part

        if e >= 2:
            for copy in saves(e - 2):
                copy.wait()
        down_g[slot] = dot_left(weighted[...], grads[...]).astype(low).reshape(down_g.shape[1:])
        gate_g[slot] = dot_left(rows[...], gate_side[...]).astype(low).reshape(gate_g.shape[1:])
        up_g[slot] = dot_left(rows[...], up_side[...]).astype(low).reshape(up_g.shape[1:])
        for copy in saves(e):
            copy.start()
    for e in range(max(0, count - 2), count):
        for copy in saves(e):
            copy.wait()


def expert_pass(first, place, rows, grads, packed, carry, last):
    sources = len(packed)
    levels, _, count, part, width = packed[0].shape
    hidden_width = levels * sources * part
    total_rows = sum(block.shape[0] for block in rows)
    lanes = rows[0].shape[1] - width
    low = jnp.bfloat16
    wide = jnp.float32
    carried = carry is not None
    flops = 18 * total_rows * count * hidden_width * width
    side = pltpu.VMEM((2, levels, sources, 3, part, hidden_width), low)
    sides = [side, side, pltpu.VMEM((2, levels, sources, part, width), low)]
    sums = [(total_rows, width), (total_rows, width + lanes)]
    return pl.pallas_call(
        partial(
            expert_kernel, sources, carried, last, len(rows), len(grads), min(512, total_rows)
        ),
        in_specs=[SCALARS, SCALARS]
        + [ANYWHERE] * (sources + len(rows) + len(grads) + (2 if carried else 0)),
        out_specs=[ANYWHERE] * sources + [INSIDE, INSIDE],
        out_shape=[jax.ShapeDtypeStruct(packed[0].shape, low)] * sources
        + [jax.ShapeDtypeStruct(shape, low if last else wide) for shape in sums],
        scratch_shapes=([pltpu.VMEM(shape, wide) for shape in sums] if last else [])
        + [
            pltpu.VMEM((total_rows, width), low),
            pltpu.VMEM((total_rows, width), low),
            pltpu.VMEM((total_rows, lanes), low),
        ]
        + sides
        + sides
        + [pltpu.VMEM((total_rows, hidden_width), low)] * 3
        + [
            pltpu.SemaphoreType.DMA((2, 7 * sources)),
            pltpu.SemaphoreType.DMA((2, 7 * sources)),
            pltpu.SemaphoreType.DMA((2 * len(rows) + len(grads) + 2,)),
        ],
        compiler_params=pltpu.CompilerParams(vmem_limit_bytes=VMEM_BYTES),
        cost_estimate=cost(flops, *packed, *packed, *rows, *grads),
        name="experts",
    )(first, place, *packed, *rows, *grads, *(carry or ()))


def unpack_kernel(chunks, *refs):
    found, (gate, up, down) = refs[:chunks], refs[chunks:]
    hidden_width = gate.shape[2]
    base = 0
    for chunk in found:
        count, part = chunk.shape[1], chunk.shape[2]
        for e in range(count):
            for side, target in ((0, gate), (1, up)):
                for j in range(3):
                    target[base + e, j * part : (j + 1) * part, :] = chunk[
                        side, e, :, j * hidden_width : (j + 1) * hidden_width
                    ].astype(jnp.float32)
            down[base + e] = chunk[2, e].astype(jnp.float32)
        base += count


def unpack(chunks, gate_shape, down_shape):
    return pl.pallas_call(
        partial(unpack_kernel, len(chunks)),
        in_specs=[INSIDE] * len(chunks),
        out_specs=[INSIDE] * 3,
        out_shape=[
            jax.ShapeDtypeStruct(gate_shape, jnp.float32),
            jax.ShapeDtypeStruct(gate_shape, jnp.float32),
            jax.ShapeDtypeStruct(down_shape, jnp.float32),
        ],
        compiler_params=pltpu.CompilerParams(vmem_limit_bytes=VMEM_BYTES),
        cost_estimate=pl.CostEstimate(flops=12 * 10**9, bytes_accessed=1, transcendentals=0),
        name="unpack",
    )(*chunks)


def cube():
    return lax.axis_size("batch") == 8 and lax.axis_size("expert") == 4


def pair_moves(size, flip):
    return [(i, i ^ flip) for i in range(size)]


def shift_moves(step):
    return [(2 * z + c, 2 * ((z + step) % 4) + c) for z in range(4) for c in range(2)]


def gather_blocks(rows, at_once=False):
    size = lax.axis_size("expert")
    if size != 4:
        stacked = lax.all_gather(rows, "expert", axis=0)
        own = lax.axis_index("expert")
        return [
            lax.dynamic_index_in_dim(stacked, own ^ r, axis=0, keepdims=False) for r in range(size)
        ]
    across, along = pair_moves(size, 1), pair_moves(size, 2)
    if at_once:
        return [rows] + [lax.ppermute(rows, "expert", pair_moves(size, r)) for r in range(1, 4)]
    half = rows.shape[0] // 2
    first = lax.ppermute(rows, "expert", across)
    second = lax.ppermute(rows, "expert", along)
    top = lax.ppermute(second[:half], "expert", across)
    bottom = lax.ppermute(first[half:], "expert", along)
    return [rows, first, second, top, bottom]


def scatter_blocks(parts):
    size = lax.axis_size("expert")
    low = jnp.bfloat16
    wide = jnp.float32
    if size != 4:
        own = lax.axis_index("expert")
        order = jnp.arange(size, dtype=jnp.int32) ^ own
        stacked = jnp.take(jnp.stack(parts), order, axis=0).astype(low)
        return lax.psum_scatter(stacked, "expert", scatter_dimension=0).astype(wide)
    across, along = pair_moves(size, 1), pair_moves(size, 2)
    half = parts[0].shape[0] // 2
    top = lax.ppermute(parts[3][:half].astype(low), "expert", across)
    bottom = lax.ppermute(parts[3][half:].astype(low), "expert", along)
    first_top = lax.ppermute(parts[1][:half].astype(low), "expert", across)
    second_bottom = lax.ppermute(parts[2][half:].astype(low), "expert", along)
    for_second = (parts[2][:half].astype(wide) + top.astype(wide)).astype(low)
    for_first = (parts[1][half:].astype(wide) + bottom.astype(wide)).astype(low)
    second_top = lax.ppermute(for_second, "expert", along)
    first_bottom = lax.ppermute(for_first, "expert", across)
    own = parts[0].astype(wide)
    return jnp.concatenate(
        [
            own[:half] + first_top.astype(wide) + second_top.astype(wide),
            own[half:] + first_bottom.astype(wide) + second_bottom.astype(wide),
        ],
        axis=0,
    )


def after(values, events):
    return lax.optimization_barrier((values, events))[0]


def send_parts(parts):
    if lax.axis_size("expert") != 4:
        return [scatter_blocks(parts)]
    low = jnp.bfloat16
    return [parts[0]] + [
        lax.ppermute(parts[r].astype(low), "expert", pair_moves(4, r)) for r in range(1, 4)
    ]


def total_of(parts):
    total = parts[0].astype(jnp.float32)
    for part in parts[1:]:
        total += part.astype(jnp.float32)
    return total


def shift_dense(rows):
    if not cube():
        return [lax.all_gather(rows, ("batch", "expert"), axis=0, tiled=True)]
    return [rows] + [lax.ppermute(rows, "batch", shift_moves(r)) for r in range(1, 4)]


def gather_dense(line, columns, events):
    found = [rows[:, columns] for rows in line]
    if not cube():
        return [found[0][None]], jnp.zeros((1, 1), jnp.int32), (), ()
    place = lax.axis_index("batch")
    level, core = place // 2, place % 2
    member = lax.axis_index("expert")
    mine = gather_blocks(after(jnp.stack(found), events))
    plane, far = mine[1:3], mine[3:]
    mine = mine[:3] + [jnp.concatenate(far, axis=0)]
    other = [lax.ppermute(block, "batch", pair_moves(8, 1)) for block in mine]
    spots = [
        [(((level + 4 - k) % 4) * 2 + (core ^ c)) * 4 + (member ^ r) for k in range(4)]
        for c in range(2)
        for r in range(4)
    ]
    return mine + other, jnp.array(spots, jnp.int32), plane, far


def join_cores(found, events):
    low = jnp.bfloat16
    wide = jnp.float32
    received = {r: lax.ppermute(found[r], "batch", pair_moves(8, 1)) for r in (3, 1, 2, 0)}
    received = after(received, events)
    return [(found[4 + r].astype(wide) + received[r].astype(wide)).astype(low) for r in range(4)]


def scatter_line(plane):
    low = jnp.bfloat16
    wide = jnp.float32
    level = lax.axis_index("batch") // 2
    total = lax.dynamic_index_in_dim(plane, level, axis=0, keepdims=False)
    for r in range(1, 4):
        sent = lax.dynamic_index_in_dim(plane, (level + r) % 4, axis=0, keepdims=False)
        total += lax.ppermute(sent.astype(low), "batch", shift_moves(r)).astype(wide)
    return total


def scatter_whole(found):
    values = found[0].reshape(found[0].shape[3:])
    total = lax.psum_scatter(values, ("batch", "expert"), scatter_dimension=0, tiled=True)
    return total.astype(jnp.float32)


def pack_sides(gate, up, down):
    def fold(values):
        count, depth, width = values.shape
        return values.reshape(count, 3, depth // 3, width).transpose(0, 2, 1, 3).reshape(down.shape)

    return jnp.stack([fold(gate), fold(up), down], axis=0)


def local(
    tokens,
    cotangent,
    attn_gain,
    query_weight,
    key_weight,
    value_weight,
    out_weight,
    ffn_gain,
    router_weight,
    gate_weight,
    up_weight,
    down_weight,
    routes,
    ranking,
):
    low = jnp.bfloat16
    wide = jnp.float32
    query_width = HEADS * HEAD_DIM
    kv_width = KV_HEADS * HEAD_DIM
    qkv_width = query_width + 2 * kv_width
    width = tokens.shape[2]
    experts_total = router_weight.shape[1]
    extra = -(-(experts_total + 2) // 128) * 128
    first_gain, second_gain = experts_total, experts_total + 1
    local_experts = gate_weight.shape[0]
    member_count = lax.axis_size("expert")
    member_id = lax.axis_index("expert")
    local_rows = tokens.shape[1]
    group_rows = local_rows * member_count
    cut = cube()
    place = jnp.stack([lax.axis_index("batch") % 2, member_id]).astype(jnp.int32)

    route_rows = routes[0]
    rank_rows = ranking[0]
    expert_lanes = jnp.arange(extra, dtype=jnp.int32)
    member = jnp.any(route_rows[:, :, None] == expert_lanes[None, None, :], axis=1)
    marks = jnp.where(
        expert_lanes[None, :] == experts_total,
        (rank_rows // 32)[:, None],
        jnp.where(expert_lanes[None, :] == experts_total + 1, (rank_rows % 32)[:, None], member),
    ).astype(low)
    grad_out = cotangent[0]
    grad_blocks = gather_blocks(jnp.concatenate([grad_out, marks], axis=1), True)
    marks_all = jnp.concatenate([block[:, width:] for block in grad_blocks], axis=0)

    small_width = qkv_width + extra
    line = shift_dense(
        jnp.concatenate(
            [
                query_weight,
                key_weight,
                value_weight,
                router_weight,
                attn_gain[:, None],
                ffn_gain[:, None],
                jnp.zeros((query_weight.shape[0], extra - experts_total - 2), low),
                out_weight,
            ],
            axis=1,
        )
    )
    qkv_pieces, qkv_spots, plane, far = gather_dense(
        line, slice(0, small_width), grad_blocks
    )
    out_pieces, out_spots, out_plane, _ = gather_dense(line, slice(small_width, None), far)
    chunks = (0, 3, local_experts)
    packed_all = []
    for a, b in zip(chunks[:-1], chunks[1:]):
        sides = (gate_weight[a:b], up_weight[a:b], down_weight[a:b])
        packed = after(pack_sides(*after(sides, line[0])), (line, grad_blocks) if a == 0 else plane)
        packed_all.append(lax.all_gather(packed, "batch", axis=0))

    row_ids = member_id * local_rows + jnp.arange(local_rows, dtype=jnp.int32)
    half_dim = HEAD_DIM // 2
    frequency = THETA ** (-jnp.arange(half_dim, dtype=wide) / half_dim)
    angles = place_of(row_ids).astype(wide)[:, None] * frequency[None, :]
    cosine = jnp.tile(jnp.cos(angles), (1, 4))
    sine_part = jnp.tile(jnp.concatenate([-jnp.sin(angles), jnp.sin(angles)], axis=1), (1, 2))
    normed, query, keyval, small = enter(
        tokens[0], cosine, sine_part, qkv_pieces, qkv_spots, first_gain, query_width, kv_width
    )

    rank_all = (
        marks_all[:, experts_total].astype(wide) * 32 + marks_all[:, experts_total + 1].astype(wide)
    )
    earlier = (rank_all[None, :] < rank_rows.astype(wide)[:, None]).astype(low)
    before = product(earlier, marks_all)
    capacity = 5 * group_rows * route_rows.shape[1] // (4 * experts_total)
    member = member.astype(wide)
    kept = jnp.where(before < capacity, member, 0.0)

    keyval_blocks = gather_blocks(after(keyval, out_plane))
    if member_count == 4:
        ordered = keyval_blocks[:3] + [jnp.concatenate(keyval_blocks[3:], axis=0)]
        away = 1 << 20
        keys = jnp.concatenate(
            [
                lax.select_n(member_id, *ordered),
                lax.select_n(member_id ^ 1, *ordered),
                keyval,
            ],
            axis=0,
        )
        starts = [
            jnp.where(member_id >= 1, 0, away),
            jnp.where(member_id >= 2, local_rows, away),
            member_id * local_rows,
        ]
    else:
        keys = jnp.concatenate(keyval_blocks, axis=0)
        starts = [(member_id ^ r) * local_rows for r in range(member_count)]
    key_ids = jnp.concatenate([s + jnp.arange(local_rows, dtype=jnp.int32) for s in starts])
    bias = jnp.where(visible(row_ids, key_ids), 0.0, -1e30).astype(wide)
    attended, log_totals, residual, sent, gate_rows = attend(
        query, keys, bias, tokens[0], small, member, kept, second_gain, out_pieces, out_spots
    )
    sent_blocks = gather_blocks(sent)

    carry, chunk_grads = None, []
    for packed, a, b in zip(packed_all, chunks[:-1], chunks[1:]):
        first = (member_id * local_experts + a).astype(jnp.int32).reshape(1)
        packed_grad, mixture_all, row_grad = expert_pass(
            first, place, sent_blocks, grad_blocks, [packed], carry, b == local_experts
        )
        carry = (mixture_all, row_grad)
        chunk_grads.append(packed_grad)

    def blocks_of(values):
        return [values[r * local_rows : (r + 1) * local_rows] for r in range(member_count)]

    normed_grad = scatter_blocks(blocks_of(row_grad))
    turned = turn(
        place,
        out_spots,
        (
            normed_grad,
            residual,
            grad_out,
            small,
            gate_rows,
            member,
            kept,
            sent,
            attended,
        ),
        out_pieces,
        cut,
        second_gain,
    )
    out_found = turned[:-2]
    resid_grad, head_grad = turned[-2:]
    mixture_parts = send_parts(blocks_of(after(mixture_all, normed_grad)))
    query_grad, key_grads = attend_back(
        head_grad, query, keys, bias.T, log_totals, cosine, sine_part
    )
    totals = [lax.psum_scatter(chunk_grads[0], "batch", scatter_dimension=0)]
    if member_count == 4:
        zero = jnp.zeros((), low)
        for_first, for_second, for_own = blocks_of(key_grads)[:3]
        key_parts = []
        for r in range(4):
            part = jnp.where(member_id == r, for_first, zero)
            part += jnp.where(member_id ^ 1 == r, for_second, zero)
            key_parts.append(part + for_own if r == 0 else part)
    else:
        key_parts = blocks_of(key_grads)
    keyval_sum = scatter_blocks(after(key_parts, mixture_parts[1:]))
    if cut:
        out_parts = send_parts(join_cores(out_found, keyval_sum))
    for packed_grad in chunk_grads[1:]:
        packed_grad = after(packed_grad, (totals[-1], keyval_sum))
        totals.append(lax.psum_scatter(packed_grad, "batch", scatter_dimension=0))
    keyval_sum = after(keyval_sum, totals[0])
    left = leave(
        place,
        qkv_spots,
        (
            keyval_sum,
            query_grad,
            normed,
            tokens[0],
            resid_grad,
            small,
            cosine,
            sine_part,
        ),
        qkv_pieces,
        cut,
        first_gain,
    )
    qkv_found, input_grad = left[:-1], left[-1]
    result = (residual + total_of(mixture_parts)).astype(low)
    if cut:
        qkv_parts = join_cores(qkv_found, ())
        qkv_plane = scatter_blocks(after(qkv_parts, out_parts[1:]))
        out_sum = scatter_line(total_of(out_parts))
        qkv_sum = scatter_line(qkv_plane)
    else:
        out_sum = scatter_whole(out_found)
        qkv_sum = scatter_whole(qkv_found)
    gate_total, up_total, down_total = unpack(totals, gate_weight.shape, down_weight.shape)
    return (
        result[None],
        input_grad[None],
        qkv_sum[:, qkv_width + first_gain],
        qkv_sum[:, :query_width],
        qkv_sum[:, query_width : query_width + kv_width],
        qkv_sum[:, query_width + kv_width : qkv_width],
        out_sum[:, :width],
        out_sum[:, width + second_gain],
        out_sum[:, width : width + experts_total],
        gate_total,
        up_total,
        down_total,
    )


def solution(mesh):
    return jax.shard_map(
        local,
        mesh=mesh,
        in_specs=(
            P("batch", "expert", None),
            P("batch", "expert", None),
            P(("batch", "expert")),
            P(("batch", "expert"), None),
            P(("batch", "expert"), None),
            P(("batch", "expert"), None),
            P(("batch", "expert"), None),
            P(("batch", "expert")),
            P(("batch", "expert"), None),
            P("expert", "batch", None),
            P("expert", "batch", None),
            P("expert", "batch", None),
            P("batch", "expert", None),
            P("batch", "expert"),
        ),
        out_specs=(
            P("batch", "expert", None),
            P("batch", "expert", None),
            P(("batch", "expert")),
            P(("batch", "expert"), None),
            P(("batch", "expert"), None),
            P(("batch", "expert"), None),
            P(("batch", "expert"), None),
            P(("batch", "expert")),
            P(("batch", "expert"), None),
            P("expert", "batch", None),
            P("expert", "batch", None),
            P("expert", "batch", None),
        ),
        check_vma=False,
    )
```

```python
from functools import partial

import jax
import jax.numpy as jnp
from jax import lax
from jax.experimental import pallas as pl
from jax.experimental.pallas import tpu as pltpu
from jax.sharding import PartitionSpec as P

HEADS = 24
KV_HEADS = 8
HEAD_DIM = 64
PROMPT = 512
CLEN = 256


EPS = 1e-06
THETA = 10000.0


def product(left, right):
    return jnp.dot(left, right, preferred_element_type=jnp.float32)


def place_of(row_ids):
    return jnp.where(row_ids < PROMPT, row_ids, PROMPT + (row_ids - PROMPT) % CLEN)


def visible(query_ids, key_ids):
    causal = key_ids[None, :] <= query_ids[:, None]
    same_run = (key_ids[None, :] - PROMPT) // CLEN == (query_ids[:, None] - PROMPT) // CLEN
    return causal & ((key_ids[None, :] < PROMPT) | same_run)


def dot_plain(left, right):
    return lax.dot_general(left, right, (((1,), (0,)), ((), ())), preferred_element_type=jnp.float32)


def dot_right(left, right):
    return lax.dot_general(left, right, (((1,), (1,)), ((), ())), preferred_element_type=jnp.float32)


def dot_left(left, right):
    return lax.dot_general(left, right, (((0,), (0,)), ((), ())), preferred_element_type=jnp.float32)


ANYWHERE = pl.BlockSpec(memory_space=pl.ANY)
INSIDE = pl.BlockSpec(memory_space=pltpu.VMEM)
SCALARS = pl.BlockSpec(memory_space=pltpu.SMEM)
VMEM_BYTES = 60 * 1024 * 1024


def cost(flops, *arrays):
    return pl.CostEstimate(flops=1, bytes_accessed=1, transcendentals=0)


def weight_copies(spots, pieces, target, sems):
    copies = []
    for p, piece in enumerate(pieces):
        blocks, rows = piece.shape[0], piece.shape[1]
        for k in range(blocks):
            place = pl.multiple_of(spots[p, k] * rows, rows)
            copies.append(
                pltpu.make_async_copy(
                    piece.at[k], target.at[pl.ds(place, rows)], sems.at[p * blocks + k]
                )
            )
    return copies


def block_copies(blocks, target, sems, first, columns=None):
    copies = []
    start = 0
    for i, block in enumerate(blocks):
        rows = block.shape[0]
        source = block if columns is None else block.at[:, columns]
        copies.append(
            pltpu.make_async_copy(source, target.at[pl.ds(start, rows)], sems.at[first + i])
        )
        start += rows
    return copies


def swap_halves(values):
    half = HEAD_DIM // 2
    lane = lax.broadcasted_iota(jnp.int32, values.shape, 1)
    return jnp.where(
        lane % HEAD_DIM < half,
        pltpu.roll(values, 2 * HEAD_DIM - half, 1),
        pltpu.roll(values, half, 1),
    )


def mean_square_scale(values):
    return lax.rsqrt(jnp.mean(values * values, axis=-1, keepdims=True) + EPS)


def enter_kernel(count, gain_at, spots, tokens, cosine, sine, *refs):
    pieces = refs[:count]
    normed, query, keyval, small, weight, sems = refs[count:]
    low = jnp.bfloat16
    copies = weight_copies(spots, pieces, weight, sems)
    for copy in copies:
        copy.start()
    inputs = tokens[...].astype(jnp.float32)
    scaled = inputs * mean_square_scale(inputs)
    for copy in copies:
        copy.wait()
    query_width = query.shape[1]
    kv_width = keyval.shape[1] // 2
    qkv_width = query_width + 2 * kv_width
    turned = weight[:, qkv_width:].astype(jnp.float32).T
    small[...] = turned
    rows = (scaled * turned[gain_at : gain_at + 1]).astype(low)
    normed[...] = rows
    pair = 2 * HEAD_DIM
    scale = HEAD_DIM**-0.5
    for start in range(0, query_width + kv_width, 512):
        product_part = dot_plain(rows, weight[:, start : start + 512])
        for offset in range(0, 512, pair):
            part = product_part[:, offset : offset + pair]
            part = part * cosine[...] + swap_halves(part) * sine[...]
            at = start + offset
            if at < query_width:
                query[:, at : at + pair] = (part * scale).astype(low)
            else:
                keyval[:, at - query_width : at - query_width + pair] = part.astype(low)
    keyval[:, kv_width:] = dot_plain(
        rows, weight[:, query_width + kv_width : qkv_width]
    ).astype(low)


def enter(tokens, cosine, sine, pieces, spots, gain_at, query_width, kv_width):
    rows, width = tokens.shape
    columns = pieces[0].shape[2]
    low = jnp.bfloat16
    return pl.pallas_call(
        partial(enter_kernel, len(pieces), gain_at),
        in_specs=[SCALARS, INSIDE, INSIDE, INSIDE] + [ANYWHERE] * len(pieces),
        out_specs=[INSIDE] * 4,
        out_shape=[
            jax.ShapeDtypeStruct((rows, width), low),
            jax.ShapeDtypeStruct((rows, query_width), low),
            jax.ShapeDtypeStruct((rows, 2 * kv_width), low),
            jax.ShapeDtypeStruct((columns - query_width - 2 * kv_width, width), jnp.float32),
        ],
        scratch_shapes=[
            pltpu.VMEM((width, columns), low),
            pltpu.SemaphoreType.DMA((len(pieces) * pieces[0].shape[0],)),
        ],
        compiler_params=pltpu.CompilerParams(vmem_limit_bytes=VMEM_BYTES),
        cost_estimate=cost(2 * rows * width * columns, *pieces),
        name="enter",
    )(spots, tokens, cosine, sine, *pieces)


def both_places(values):
    wide = values.astype(jnp.float32)
    low_lane = lax.broadcasted_iota(jnp.int32, values.shape, 1) < HEAD_DIM
    moved = pltpu.roll(wide, HEAD_DIM, 1)
    kind = values.dtype
    return [
        [jnp.where(low_lane, wide, 0.0).astype(kind), jnp.where(low_lane, 0.0, moved).astype(kind)],
        [jnp.where(low_lane, moved, 0.0).astype(kind), jnp.where(low_lane, 0.0, wide).astype(kind)],
    ]


def attend_kernel(
    count, query, keyval, bias, tokens, small, member, kept, gain_at, spots, *refs
):
    pieces = refs[:count]
    attended, log_totals, residual, sent, gate_rows, weight, sems = refs[count:]
    low = jnp.bfloat16
    rows = query.shape[0]
    width = tokens.shape[1]
    kv_width = keyval.shape[1] // 2
    pair_lanes = 2 * HEAD_DIM
    repeat = HEADS // KV_HEADS
    copies = weight_copies(spots, pieces, weight, sems)
    for copy in copies:
        copy.start()
    log_totals[...] = jnp.zeros_like(log_totals)
    lane = lax.broadcasted_iota(jnp.int32, log_totals.shape, 1)

    @pl.loop(0, KV_HEADS // 2)
    def _(pair):
        at = pl.ds(pl.multiple_of(pair * pair_lanes, pair_lanes), pair_lanes)
        keys = both_places(keyval[:, at])
        at = pl.ds(pl.multiple_of(kv_width + pair * pair_lanes, pair_lanes), pair_lanes)
        values = both_places(keyval[:, at])
        for i in range(repeat):
            at = pl.ds(pl.multiple_of((pair * repeat + i) * pair_lanes, pair_lanes), pair_lanes)
            queries = query[:, at]
            total = jnp.zeros((rows, pair_lanes), jnp.float32)
            for a in range(2):
                head = 2 * i + a
                scores = dot_right(queries, keys[head // repeat][a]) + bias[...]
                peak = jnp.max(scores, axis=-1, keepdims=True)
                lifted = jnp.exp(scores - peak)
                row_total = jnp.sum(lifted, axis=-1, keepdims=True)
                weights_low = (lifted * (1.0 / row_total)).astype(low)
                total += dot_plain(weights_low, values[head // repeat][a])
                log_totals[...] = jnp.where(
                    lane == pair * (2 * repeat) + head, peak + jnp.log(row_total), log_totals[...]
                )
            attended[:, at] = total.astype(low)

    for copy in copies:
        copy.wait()
    hidden = tokens[...].astype(jnp.float32) + dot_plain(attended[...], weight[...])
    residual[...] = hidden
    gain = small[gain_at : gain_at + 1, :]
    normed = (hidden * mean_square_scale(hidden) * gain).astype(low)
    logits = dot_right(normed, small[...].astype(low))
    chosen = member[...] > 0.0
    logits = jnp.where(chosen, logits, -1e30)
    lifted = jnp.where(chosen, jnp.exp(logits - jnp.max(logits, axis=-1, keepdims=True)), 0.0)
    gates = lifted / jnp.sum(lifted, axis=-1, keepdims=True)
    gate_rows[...] = gates
    sent[:, :width] = normed
    sent[:, width:] = (gates * kept[...]).astype(low)


def attend(query, keyval, bias, tokens, small, member, kept, gain_at, pieces, spots):
    rows, width = tokens.shape
    query_width = query.shape[1]
    lanes = small.shape[0]
    low = jnp.bfloat16

    def kernel(*refs):
        attend_kernel(len(pieces), *refs[:7], gain_at, *refs[7:])

    return pl.pallas_call(
        kernel,
        in_specs=[INSIDE] * 7 + [SCALARS] + [ANYWHERE] * len(pieces),
        out_specs=[INSIDE] * 5,
        out_shape=[
            jax.ShapeDtypeStruct((rows, query_width), low),
            jax.ShapeDtypeStruct((rows, 128), jnp.float32),
            jax.ShapeDtypeStruct((rows, width), jnp.float32),
            jax.ShapeDtypeStruct((rows, width + lanes), low),
            jax.ShapeDtypeStruct((rows, lanes), jnp.float32),
        ],
        scratch_shapes=[
            pltpu.VMEM((query_width, width), low),
            pltpu.SemaphoreType.DMA((len(pieces) * pieces[0].shape[0],)),
        ],
        compiler_params=pltpu.CompilerParams(vmem_limit_bytes=VMEM_BYTES),
        cost_estimate=cost(2 * rows * width * width + 8 * rows * query_width * bias.shape[1], *pieces),
        name="attend",
    )(query, keyval, bias, tokens, small, member, kept, spots, *pieces)


def grad_shapes(cut, rows, columns):
    low = jnp.bfloat16
    if cut:
        block = rows // 32
        return (
            [jax.ShapeDtypeStruct((4, 4, block, columns), low)] * 2,
            pltpu.VMEM((4, 2, 4, block, columns), low),
        )
    return (
        [jax.ShapeDtypeStruct((1, 1, 1, rows, columns), low)],
        pltpu.VMEM((1, 1, 1, rows, columns), low),
    )


def grad_copies(cut, place, source, outs, sems):
    if not cut:
        return [pltpu.make_async_copy(source, outs[0], sems.at[0])]
    core, member = place[0], place[1]
    other, own = outs
    copies = []
    for r in range(4):
        copies.append(
            pltpu.make_async_copy(
                source.at[:, 1 - core, member ^ r], other.at[r], sems.at[2 * r]
            )
        )
        copies.append(
            pltpu.make_async_copy(source.at[:, core, member ^ r], own.at[r], sems.at[2 * r + 1])
        )
    return copies


def turn_kernel(
    count,
    cut,
    gain_at,
    place,
    spots,
    normed_grad,
    residual,
    grad_out,
    small,
    gate_rows,
    member,
    kept,
    normed,
    attended,
    *refs,
):
    pieces = refs[:count]
    refs = refs[count:]
    outs = refs[: (2 if cut else 1)]
    resid_grad, head_grad, weight, weight_grad, sems, out_sems = refs[len(outs) :]
    low = jnp.bfloat16
    rows, width = residual.shape
    lanes = gate_rows.shape[1]
    copies = weight_copies(spots, pieces, weight, sems)
    for copy in copies:
        copy.start()
    lane = lax.broadcasted_iota(jnp.int32, (rows, lanes), 1)
    gates = gate_rows[...]
    gate_grads = normed_grad[:, width:] * kept[...]
    chosen_grad = gates * (gate_grads - jnp.sum(gates * gate_grads, axis=-1, keepdims=True))
    logit_grad = (chosen_grad * member[...]).astype(low)
    hidden = residual[...]
    scale = mean_square_scale(hidden)
    row_grad = normed_grad[:, :width] + dot_plain(logit_grad, small[...].astype(low))
    gain = small[gain_at : gain_at + 1, :]
    scaled = row_grad * gain
    total_grad = (
        grad_out[...].astype(jnp.float32)
        + scale * scaled
        - hidden * (scale * scale * scale) * jnp.mean(scaled * hidden, axis=-1, keepdims=True)
    )
    resid_grad[...] = total_grad
    attn_grad = total_grad.astype(low)
    shape = weight_grad.shape[:-1]
    gain_grad = (row_grad * hidden * scale).astype(low)
    picks = jnp.where(lane == gain_at, 1.0, 0.0).astype(low)
    weight_grad[..., width:] = (
        (dot_left(normed[...][:, :width], logit_grad) + dot_left(gain_grad, picks))
        .astype(low)
        .reshape(shape + (lanes,))
    )
    for start in range(0, width, 512):
        weight_grad[..., start : start + 512] = (
            dot_left(attended[...], attn_grad[:, start : start + 512])
            .astype(low)
            .reshape(shape + (512,))
        )
    out_copies = grad_copies(cut, place, weight_grad, outs, out_sems)
    for copy in out_copies:
        copy.start()
    for copy in copies:
        copy.wait()
    head_grad[...] = dot_right(attn_grad, weight[...]).astype(low)
    for copy in out_copies:
        copy.wait()


def turn(place, spots, operands, pieces, cut, gain_at):
    residual, gate_rows, attended = operands[1], operands[4], operands[8]
    rows, width = residual.shape
    query_width = attended.shape[1]
    low = jnp.bfloat16
    grads, held = grad_shapes(cut, query_width, width + gate_rows.shape[1])
    return pl.pallas_call(
        partial(turn_kernel, len(pieces), cut, gain_at),
        in_specs=[SCALARS, SCALARS] + [INSIDE] * len(operands) + [ANYWHERE] * len(pieces),
        out_specs=[ANYWHERE] * len(grads) + [INSIDE] * 2,
        out_shape=grads
        + [
            jax.ShapeDtypeStruct((rows, width), jnp.float32),
            jax.ShapeDtypeStruct((rows, query_width), low),
        ],
        scratch_shapes=[
            pltpu.VMEM((query_width, width), low),
            held,
            pltpu.SemaphoreType.DMA((len(pieces) * pieces[0].shape[0],)),
            pltpu.SemaphoreType.DMA((8,)),
        ],
        compiler_params=pltpu.CompilerParams(vmem_limit_bytes=VMEM_BYTES),
        cost_estimate=cost(0),
        name="turn",
    )(place, spots, *operands, *pieces)


def attend_back_kernel(
    head_grad, query, keyval, bias, log_totals, cosine, sine, query_grad, keyval_grad, totals
):
    low = jnp.bfloat16
    rows = query.shape[0]
    kv_width = keyval.shape[1] // 2
    pair_lanes = 2 * HEAD_DIM
    repeat = HEADS // KV_HEADS
    totals[...] = log_totals[...].T

    @pl.loop(0, KV_HEADS // 2)
    def _(pair):
        key_at = pl.ds(pl.multiple_of(pair * pair_lanes, pair_lanes), pair_lanes)
        value_at = pl.ds(pl.multiple_of(kv_width + pair * pair_lanes, pair_lanes), pair_lanes)
        keys = both_places(keyval[:, key_at])
        values = both_places(keyval[:, value_at])
        key_grads = [[None, None], [None, None]]
        value_grads = [[None, None], [None, None]]
        for i in range(repeat):
            at = pl.ds(pl.multiple_of((pair * repeat + i) * pair_lanes, pair_lanes), pair_lanes)
            queries = query[:, at]
            grads = head_grad[:, at]
            query_part = jnp.zeros((rows, pair_lanes), jnp.float32)
            for a in range(2):
                head = 2 * i + a
                g = head // repeat
                total = totals[pl.ds(pair * (2 * repeat) + head, 1), :]
                weights = jnp.exp(dot_right(keys[g][a], queries) + bias[...] - total)
                weight_grads = dot_right(values[g][a], grads)
                delta = jnp.sum(weights * weight_grads, axis=0, keepdims=True)
                score_grads = (weights * (weight_grads - delta)).astype(low)
                value_part = dot_plain(weights.astype(low), grads)
                key_part = dot_plain(score_grads, queries)
                query_part += dot_left(score_grads, keys[g][a])
                if key_grads[g][a] is None:
                    key_grads[g][a], value_grads[g][a] = key_part, value_part
                else:
                    key_grads[g][a] += key_part
                    value_grads[g][a] += value_part
            query_part = query_part * (HEAD_DIM**-0.5)
            query_part = query_part * cosine[...] - swap_halves(query_part) * sine[...]
            query_grad[:, at] = query_part.astype(low)
        low_lane = lax.broadcasted_iota(jnp.int32, (keyval.shape[0], pair_lanes), 1) < HEAD_DIM
        for at, found in ((key_at, key_grads), (value_at, value_grads)):
            keyval_grad[:, at] = jnp.where(
                low_lane,
                found[0][0] + pltpu.roll(found[0][1], HEAD_DIM, 1),
                pltpu.roll(found[1][0], HEAD_DIM, 1) + found[1][1],
            ).astype(low)


def attend_back(head_grad, query, keyval, bias, log_totals, cosine, sine):
    rows, query_width = query.shape
    low = jnp.bfloat16
    return pl.pallas_call(
        attend_back_kernel,
        in_specs=[INSIDE] * 7,
        out_specs=[INSIDE] * 2,
        out_shape=[
            jax.ShapeDtypeStruct((rows, query_width), low),
            jax.ShapeDtypeStruct(keyval.shape, low),
        ],
        scratch_shapes=[pltpu.VMEM((128, rows), jnp.float32)],
        compiler_params=pltpu.CompilerParams(vmem_limit_bytes=VMEM_BYTES),
        cost_estimate=cost(0),
        name="attend_back",
    )(head_grad, query, keyval, bias, log_totals, cosine, sine)


def leave_kernel(
    count,
    cut,
    gain_at,
    place,
    spots,
    keyval_sum,
    query_grad,
    normed,
    tokens,
    resid_grad,
    small,
    cosine,
    sine,
    *refs,
):
    pieces = refs[:count]
    refs = refs[count:]
    outs = refs[: (2 if cut else 1)]
    input_grad, weight, weight_grad, joined, sems, out_sems = refs[len(outs) :]
    low = jnp.bfloat16
    rows, width = tokens.shape
    query_width = query_grad.shape[1]
    kv_width = keyval_sum.shape[1] // 2
    qkv_width = query_width + 2 * kv_width
    pair = 2 * HEAD_DIM
    copies = weight_copies(spots, pieces, weight, sems)
    for copy in copies:
        copy.start()
    joined[:, :query_width] = query_grad[...]
    for start in range(0, kv_width, pair):
        part = keyval_sum[:, start : start + pair]
        part = part * cosine[...] - swap_halves(part) * sine[...]
        joined[:, query_width + start : query_width + start + pair] = part.astype(low)
    joined[:, query_width + kv_width :] = keyval_sum[:, kv_width:].astype(low)
    shape = weight_grad.shape[:-1]
    for start in range(0, qkv_width, 512):
        weight_grad[..., start : start + 512] = (
            dot_left(normed[...], joined[:, start : start + 512]).astype(low).reshape(shape + (512,))
        )
    for copy in copies:
        copy.wait()
    row_grad = dot_right(joined[...], weight[:, :qkv_width])
    inputs = tokens[...].astype(jnp.float32)
    scale = mean_square_scale(inputs)
    lanes = weight_grad.shape[-1] - qkv_width
    lane = lax.broadcasted_iota(jnp.int32, (rows, lanes), 1)
    picks = jnp.where(lane == gain_at, 1.0, 0.0).astype(low)
    weight_grad[..., qkv_width:] = (
        dot_left((row_grad * inputs * scale).astype(low), picks).astype(low).reshape(shape + (lanes,))
    )
    out_copies = grad_copies(cut, place, weight_grad, outs, out_sems)
    for copy in out_copies:
        copy.start()
    scaled = row_grad * small[gain_at : gain_at + 1, :]
    input_grad[...] = (
        resid_grad[...]
        + scale * scaled
        - inputs * (scale * scale * scale) * jnp.mean(scaled * inputs, axis=-1, keepdims=True)
    )
    for copy in out_copies:
        copy.wait()


def leave(place, spots, operands, pieces, cut, gain_at):
    tokens, query_grad, keyval_sum = operands[3], operands[1], operands[0]
    rows, width = tokens.shape
    columns = pieces[0].shape[2]
    low = jnp.bfloat16
    grads, held = grad_shapes(cut, width, columns)
    return pl.pallas_call(
        partial(leave_kernel, len(pieces), cut, gain_at),
        in_specs=[SCALARS, SCALARS] + [INSIDE] * len(operands) + [ANYWHERE] * len(pieces),
        out_specs=[ANYWHERE] * len(grads) + [INSIDE],
        out_shape=grads + [jax.ShapeDtypeStruct((rows, width), jnp.float32)],
        scratch_shapes=[
            pltpu.VMEM((width, columns), low),
            held,
            pltpu.VMEM((rows, query_grad.shape[1] + keyval_sum.shape[1]), low),
            pltpu.SemaphoreType.DMA((len(pieces) * pieces[0].shape[0],)),
            pltpu.SemaphoreType.DMA((8,)),
        ],
        compiler_params=pltpu.CompilerParams(vmem_limit_bytes=VMEM_BYTES),
        cost_estimate=cost(0),
        name="leave",
    )(place, spots, *operands, *pieces)


def expert_kernel(carried, last, row_blocks, grad_blocks, row_tile, first, packed, *refs):
    blocks_in = refs[:row_blocks]
    grads_in = refs[row_blocks : row_blocks + grad_blocks]
    refs = refs[row_blocks + grad_blocks :]
    if carried:
        mix_in, turn_in = refs[:2]
        refs = refs[2:]
    count = packed.shape[2]
    grads_each = count if last else 1
    packed_grads = refs[:grads_each]
    mix_out, turn_out = refs[grads_each : grads_each + 2]
    refs = refs[grads_each + 2 :]
    if last:
        mix, turned = refs[:2]
        refs = refs[2:]
    else:
        mix, turned = mix_out, turn_out
    (
        rows,
        grads,
        gates,
        gate_w,
        up_w,
        down_w,
        gate_g,
        up_g,
        down_g,
        weighted,
        gate_side,
        up_side,
        load_sems,
        save_sems,
        carry_sems,
    ) = refs
    hidden_width = gate_w.shape[-1]
    total_rows, width = rows.shape
    lanes = gates.shape[1]
    low = jnp.bfloat16

    def moves(outside, slot, gate, up, down, sems):
        ends = []
        for side, inner in ((0, gate), (1, up)):
            for j in range(3):
                columns = pl.ds(j * hidden_width, hidden_width)
                ends.append((outside.at[:, side, :, columns], inner.at[slot, :, j]))
        ends.append((outside.at[:, 2], down.at[slot]))
        return [(outer, inner, sems.at[slot, i]) for i, (outer, inner) in enumerate(ends)]

    def loads(e):
        ends = moves(packed.at[:, :, e], e % 2, gate_w, up_w, down_w, load_sems)
        return [pltpu.make_async_copy(outer, inner, sem) for outer, inner, sem in ends]

    def saves(e):
        outside = packed_grads[e].at[:, :, 0] if last else packed_grads[0].at[:, :, e]
        ends = moves(outside, e % 2, gate_g, up_g, down_g, save_sems)
        return [pltpu.make_async_copy(inner, outer, sem) for outer, inner, sem in ends]

    carries = (
        block_copies(grads_in, grads, carry_sems, 0, pl.ds(0, width))
        + block_copies(blocks_in, rows, carry_sems, grad_blocks, pl.ds(0, width))
        + block_copies(
            blocks_in, gates, carry_sems, grad_blocks + row_blocks, pl.ds(width, lanes)
        )
    )
    sums = []
    if carried:
        at = grad_blocks + 2 * row_blocks
        sums = [
            pltpu.make_async_copy(mix_in, mix, carry_sems.at[at]),
            pltpu.make_async_copy(turn_in, turned, carry_sems.at[at + 1]),
        ]
    for copy in loads(0) + carries + sums:
        copy.start()
    for e in range(count):
        slot = e % 2
        if e + 1 < count:
            for copy in loads(e + 1):
                copy.start()
        for copy in loads(e):
            copy.wait()
        if e == 0:
            for copy in carries:
                copy.wait()
            if not carried:
                turned[:, width:] = jnp.zeros((total_rows, lanes), jnp.float32)

        @pl.loop(0, total_rows // row_tile)
        def _(tile):
            span = pl.ds(pl.multiple_of(tile * row_tile, row_tile), row_tile)
            gate_full = gate_w[slot].reshape(width, hidden_width)
            up_full = up_w[slot].reshape(width, hidden_width)
            down_full = down_w[slot].reshape(hidden_width, width)
            here = rows[span, :]
            slope = dot_right(grads[span, :], down_full)
            gate_pre = dot_plain(here, gate_full)
            up_pre = dot_plain(here, up_full)
            lane = lax.broadcasted_iota(jnp.int32, (row_tile, lanes), 1)
            chosen = lane == first[0] + e
            gate_column = jnp.sum(
                jnp.where(chosen, gates[span, :].astype(jnp.float32), 0.0), axis=1, keepdims=True
            )
            sigmoid_gate = jax.nn.sigmoid(gate_pre)
            activated = gate_pre * sigmoid_gate
            hidden = (activated * up_pre).astype(low).astype(jnp.float32)
            share = jnp.sum(hidden * slope, axis=1, keepdims=True)
            if e == 0 and sums:

                @pl.when(tile == 0)
                def _():
                    for copy in sums:
                        copy.wait()

            turned[span, width:] = jnp.where(chosen, share, turned[span, width:])
            part_weighted = (hidden * gate_column).astype(low)
            hidden_grad = slope * gate_column
            part_gate = (
                hidden_grad * up_pre * (sigmoid_gate + activated * (1.0 - sigmoid_gate))
            ).astype(low)
            part_up = (hidden_grad * activated).astype(low)
            weighted[span, :] = part_weighted
            gate_side[span, :] = part_gate
            up_side[span, :] = part_up
            mix_part = dot_plain(part_weighted, down_full)
            turn_part = dot_right(part_gate, gate_full) + dot_right(part_up, up_full)
            if e == 0 and not carried:
                mix[span, :] = mix_part
                turned[span, :width] = turn_part
            elif last and e == count - 1:
                mix_out[span, :] = (mix[span, :] + mix_part).astype(low)
                turn_out[span, :width] = (turned[span, :width] + turn_part).astype(low)
                turn_out[span, width:] = turned[span, width:].astype(low)
            else:
                mix[span, :] += mix_part
                turned[span, :width] += turn_part

        if e >= 2:
            for copy in saves(e - 2):
                copy.wait()
        down_g[slot] = dot_left(weighted[...], grads[...]).astype(low).reshape(down_g.shape[1:])
        gate_g[slot] = dot_left(rows[...], gate_side[...]).astype(low).reshape(gate_g.shape[1:])
        up_g[slot] = dot_left(rows[...], up_side[...]).astype(low).reshape(up_g.shape[1:])
        for copy in saves(e):
            copy.start()
    for e in range(max(0, count - 2), count):
        for copy in saves(e):
            copy.wait()


def expert_pass(first, rows, grads, packed, carry, last):
    blocks, _, count, part, width = packed.shape
    hidden_width = blocks * part
    total_rows = sum(block.shape[0] for block in rows)
    lanes = rows[0].shape[1] - width
    low = jnp.bfloat16
    wide = jnp.float32
    carried = carry is not None
    flops = 18 * total_rows * count * hidden_width * width
    side = pltpu.VMEM((2, blocks, 3, part, hidden_width), low)
    sides = [side, side, pltpu.VMEM((2, blocks, part, width), low)]
    sums = [(total_rows, width), (total_rows, width + lanes)]
    grad_shape = (blocks, 3, 1, part, width) if last else packed.shape
    outs = count if last else 1
    found = pl.pallas_call(
        partial(expert_kernel, carried, last, len(rows), len(grads), min(512, total_rows)),
        in_specs=[SCALARS] + [ANYWHERE] * (1 + len(rows) + len(grads) + (2 if carried else 0)),
        out_specs=[ANYWHERE] * outs + [INSIDE, INSIDE],
        out_shape=[jax.ShapeDtypeStruct(grad_shape, low)] * outs
        + [jax.ShapeDtypeStruct(shape, low if last else wide) for shape in sums],
        scratch_shapes=([pltpu.VMEM(shape, wide) for shape in sums] if last else [])
        + [
            pltpu.VMEM((total_rows, width), low),
            pltpu.VMEM((total_rows, width), low),
            pltpu.VMEM((total_rows, lanes), low),
        ]
        + sides
        + sides
        + [pltpu.VMEM((total_rows, hidden_width), low)] * 3
        + [
            pltpu.SemaphoreType.DMA((2, 7)),
            pltpu.SemaphoreType.DMA((2, 7)),
            pltpu.SemaphoreType.DMA((2 * len(rows) + len(grads) + 2,)),
        ],
        compiler_params=pltpu.CompilerParams(vmem_limit_bytes=VMEM_BYTES),
        cost_estimate=cost(flops, packed, packed, *rows, *grads),
        name="experts",
    )(first, packed, *rows, *grads, *(carry or ()))
    return found[:outs], found[outs], found[outs + 1]


def unpack_kernel(chunks, *refs):
    found, (gate, up, down) = refs[:chunks], refs[chunks:]
    hidden_width = gate.shape[2]
    base = 0
    for chunk in found:
        count, part = chunk.shape[1], chunk.shape[2]
        for e in range(count):
            for side, target in ((0, gate), (1, up)):
                for j in range(3):
                    target[base + e, j * part : (j + 1) * part, :] = chunk[
                        side, e, :, j * hidden_width : (j + 1) * hidden_width
                    ].astype(jnp.float32)
            down[base + e] = chunk[2, e].astype(jnp.float32)
        base += count


def unpack(chunks, gate_shape, down_shape):
    return pl.pallas_call(
        partial(unpack_kernel, len(chunks)),
        in_specs=[INSIDE] * len(chunks),
        out_specs=[INSIDE] * 3,
        out_shape=[
            jax.ShapeDtypeStruct(gate_shape, jnp.float32),
            jax.ShapeDtypeStruct(gate_shape, jnp.float32),
            jax.ShapeDtypeStruct(down_shape, jnp.float32),
        ],
        compiler_params=pltpu.CompilerParams(vmem_limit_bytes=VMEM_BYTES),
        cost_estimate=pl.CostEstimate(flops=12 * 10**9, bytes_accessed=1, transcendentals=0),
        name="unpack",
    )(*chunks)


def cube():
    return lax.axis_size("batch") == 8 and lax.axis_size("expert") == 4


def pair_moves(size, flip):
    return [(i, i ^ flip) for i in range(size)]


def shift_moves(step):
    return [(2 * z + c, 2 * ((z + step) % 4) + c) for z in range(4) for c in range(2)]


def gather_blocks(rows, at_once=False):
    size = lax.axis_size("expert")
    if size != 4:
        stacked = lax.all_gather(rows, "expert", axis=0)
        own = lax.axis_index("expert")
        return [
            lax.dynamic_index_in_dim(stacked, own ^ r, axis=0, keepdims=False) for r in range(size)
        ]
    across, along = pair_moves(size, 1), pair_moves(size, 2)
    if at_once:
        return [rows] + [lax.ppermute(rows, "expert", pair_moves(size, r)) for r in range(1, 4)]
    half = rows.shape[0] // 2
    first = lax.ppermute(rows, "expert", across)
    second = lax.ppermute(rows, "expert", along)
    top = lax.ppermute(second[:half], "expert", across)
    bottom = lax.ppermute(first[half:], "expert", along)
    return [rows, first, second, top, bottom]


def scatter_blocks(parts):
    size = lax.axis_size("expert")
    low = jnp.bfloat16
    wide = jnp.float32
    if size != 4:
        own = lax.axis_index("expert")
        order = jnp.arange(size, dtype=jnp.int32) ^ own
        stacked = jnp.take(jnp.stack(parts), order, axis=0).astype(low)
        return lax.psum_scatter(stacked, "expert", scatter_dimension=0).astype(wide)
    across, along = pair_moves(size, 1), pair_moves(size, 2)
    half = parts[0].shape[0] // 2
    top = lax.ppermute(parts[3][:half].astype(low), "expert", across)
    bottom = lax.ppermute(parts[3][half:].astype(low), "expert", along)
    first_top = lax.ppermute(parts[1][:half].astype(low), "expert", across)
    second_bottom = lax.ppermute(parts[2][half:].astype(low), "expert", along)
    for_second = (parts[2][:half].astype(wide) + top.astype(wide)).astype(low)
    for_first = (parts[1][half:].astype(wide) + bottom.astype(wide)).astype(low)
    second_top = lax.ppermute(for_second, "expert", along)
    first_bottom = lax.ppermute(for_first, "expert", across)
    own = parts[0].astype(wide)
    return jnp.concatenate(
        [
            own[:half] + first_top.astype(wide) + second_top.astype(wide),
            own[half:] + first_bottom.astype(wide) + second_bottom.astype(wide),
        ],
        axis=0,
    )


def after(values, events):
    return lax.optimization_barrier((values, events))[0]


def send_parts(parts):
    if lax.axis_size("expert") != 4:
        return [scatter_blocks(parts)]
    low = jnp.bfloat16
    return [parts[0]] + [
        lax.ppermute(parts[r].astype(low), "expert", pair_moves(4, r)) for r in range(1, 4)
    ]


def total_of(parts):
    total = parts[0].astype(jnp.float32)
    for part in parts[1:]:
        total += part.astype(jnp.float32)
    return total


def shift_dense(rows):
    if not cube():
        return [lax.all_gather(rows, ("batch", "expert"), axis=0, tiled=True)]
    return [rows] + [lax.ppermute(rows, "batch", shift_moves(r)) for r in range(1, 4)]


def gather_dense(line, columns, events):
    found = [rows[:, columns] for rows in line]
    if not cube():
        return [found[0][None]], jnp.zeros((1, 1), jnp.int32), (), ()
    place = lax.axis_index("batch")
    level, core = place // 2, place % 2
    member = lax.axis_index("expert")
    mine = gather_blocks(after(jnp.stack(found), events))
    plane, far = mine[1:3], mine[3:]
    mine = mine[:3] + [jnp.concatenate(far, axis=0)]
    other = [lax.ppermute(block, "batch", pair_moves(8, 1)) for block in mine]
    spots = [
        [(((level + 4 - k) % 4) * 2 + (core ^ c)) * 4 + (member ^ r) for k in range(4)]
        for c in range(2)
        for r in range(4)
    ]
    return mine + other, jnp.array(spots, jnp.int32), plane, far


def sum_chunk(packed_grad):
    return lax.psum_scatter(packed_grad, "batch", scatter_dimension=0)


def exchange_cores(values):
    return lax.ppermute(values, "batch", pair_moves(8, 1))


def join_cores(own, received):
    wide = jnp.float32
    return [(own[r].astype(wide) + received[r].astype(wide)).astype(own.dtype) for r in range(4)]


def scatter_line(plane):
    low = jnp.bfloat16
    wide = jnp.float32
    level = lax.axis_index("batch") // 2
    total = lax.dynamic_index_in_dim(plane, level, axis=0, keepdims=False)
    for r in range(1, 4):
        sent = lax.dynamic_index_in_dim(plane, (level + r) % 4, axis=0, keepdims=False)
        total += lax.ppermute(sent.astype(low), "batch", shift_moves(r)).astype(wide)
    return total


def scatter_whole(found):
    values = found[0].reshape(found[0].shape[3:])
    total = lax.psum_scatter(values, ("batch", "expert"), scatter_dimension=0, tiled=True)
    return total.astype(jnp.float32)


def pack_kernel(chunks, query, key, value, small, out, gate, up, down, dense, *packed):
    start = 0
    for part in (query, key, value, small, out):
        dense[:, start : start + part.shape[1]] = part[...]
        start += part.shape[1]
    part, hidden_width = down.shape[1], gate.shape[2]
    for n, target in enumerate(packed):
        for e in range(chunks[n], chunks[n + 1]):
            for side, source in ((0, gate), (1, up)):
                for j in range(3):
                    target[side, e - chunks[n], :, j * hidden_width : (j + 1) * hidden_width] = (
                        source[e, j * part : (j + 1) * part, :]
                    )
            target[2, e - chunks[n]] = down[e]


def pack(chunks, query, key, value, small, out, gate, up, down):
    low = jnp.bfloat16
    columns = sum(part.shape[1] for part in (query, key, value, small, out))
    return pl.pallas_call(
        partial(pack_kernel, chunks),
        in_specs=[INSIDE] * 8,
        out_specs=[INSIDE] * len(chunks),
        out_shape=[jax.ShapeDtypeStruct((query.shape[0], columns), low)]
        + [
            jax.ShapeDtypeStruct((3, b - a) + down.shape[1:], low)
            for a, b in zip(chunks[:-1], chunks[1:])
        ],
        compiler_params=pltpu.CompilerParams(vmem_limit_bytes=VMEM_BYTES),
        cost_estimate=cost(0),
        name="pack",
    )(query, key, value, small, out, gate, up, down)


def local(
    tokens,
    cotangent,
    attn_gain,
    query_weight,
    key_weight,
    value_weight,
    out_weight,
    ffn_gain,
    router_weight,
    gate_weight,
    up_weight,
    down_weight,
    routes,
    ranking,
):
    low = jnp.bfloat16
    wide = jnp.float32
    query_width = HEADS * HEAD_DIM
    kv_width = KV_HEADS * HEAD_DIM
    qkv_width = query_width + 2 * kv_width
    width = tokens.shape[2]
    experts_total = router_weight.shape[1]
    extra = -(-(experts_total + 2) // 128) * 128
    first_gain, second_gain = experts_total, experts_total + 1
    local_experts = gate_weight.shape[0]
    member_count = lax.axis_size("expert")
    member_id = lax.axis_index("expert")
    local_rows = tokens.shape[1]
    group_rows = local_rows * member_count
    cut = cube()
    place = jnp.stack([lax.axis_index("batch") % 2, member_id]).astype(jnp.int32)

    route_rows = routes[0]
    rank_rows = ranking[0]
    expert_lanes = jnp.arange(extra, dtype=jnp.int32)
    member = jnp.any(route_rows[:, :, None] == expert_lanes[None, None, :], axis=1)
    marks = jnp.where(
        expert_lanes[None, :] == experts_total,
        (rank_rows // 32)[:, None],
        jnp.where(expert_lanes[None, :] == experts_total + 1, (rank_rows % 32)[:, None], member),
    ).astype(low)
    grad_out = cotangent[0]
    small_width = qkv_width + extra
    chunks = (0, 3, local_experts)
    dense_rows, *packed_own = pack(
        chunks,
        query_weight,
        key_weight,
        value_weight,
        jnp.concatenate(
            [
                router_weight,
                attn_gain[:, None],
                ffn_gain[:, None],
                jnp.zeros((query_weight.shape[0], extra - experts_total - 2), low),
            ],
            axis=1,
        ),
        out_weight,
        gate_weight,
        up_weight,
        down_weight,
    )
    line = shift_dense(dense_rows)
    grad_blocks = gather_blocks(
        after(jnp.concatenate([grad_out, marks], axis=1), dense_rows), True
    )
    marks_all = jnp.concatenate([block[:, width:] for block in grad_blocks], axis=0)
    qkv_pieces, qkv_spots, plane, far = gather_dense(line, slice(0, small_width), grad_blocks)
    out_pieces, out_spots, out_plane, _ = gather_dense(line, slice(small_width, None), far)
    packed_all = [
        lax.all_gather(after(packed, events), "batch", axis=0)
        for packed, events in zip(packed_own, ((line, grad_blocks), plane))
    ]

    row_ids = member_id * local_rows + jnp.arange(local_rows, dtype=jnp.int32)
    half_dim = HEAD_DIM // 2
    frequency = THETA ** (-jnp.arange(half_dim, dtype=wide) / half_dim)
    angles = place_of(row_ids).astype(wide)[:, None] * frequency[None, :]
    cosine = jnp.tile(jnp.cos(angles), (1, 4))
    sine_part = jnp.tile(jnp.concatenate([-jnp.sin(angles), jnp.sin(angles)], axis=1), (1, 2))
    normed, query, keyval, small = enter(
        tokens[0], cosine, sine_part, qkv_pieces, qkv_spots, first_gain, query_width, kv_width
    )

    rank_all = (
        marks_all[:, experts_total].astype(wide) * 32 + marks_all[:, experts_total + 1].astype(wide)
    )
    earlier = (rank_all[None, :] < rank_rows.astype(wide)[:, None]).astype(low)
    before = product(earlier, marks_all)
    capacity = 5 * group_rows * route_rows.shape[1] // (4 * experts_total)
    member = member.astype(wide)
    kept = jnp.where(before < capacity, member, 0.0)

    keyval_blocks = gather_blocks(after(keyval, out_plane))
    if member_count == 4:
        ordered = keyval_blocks[:3] + [jnp.concatenate(keyval_blocks[3:], axis=0)]
        away = 1 << 20
        keys = jnp.concatenate(
            [
                lax.select_n(member_id, *ordered),
                lax.select_n(member_id ^ 1, *ordered),
                keyval,
            ],
            axis=0,
        )
        starts = [
            jnp.where(member_id >= 1, 0, away),
            jnp.where(member_id >= 2, local_rows, away),
            member_id * local_rows,
        ]
    else:
        keys = jnp.concatenate(keyval_blocks, axis=0)
        starts = [(member_id ^ r) * local_rows for r in range(member_count)]
    key_ids = jnp.concatenate([s + jnp.arange(local_rows, dtype=jnp.int32) for s in starts])
    bias = jnp.where(visible(row_ids, key_ids), 0.0, -1e30).astype(wide)
    attended, log_totals, residual, sent, gate_rows = attend(
        query, keys, bias, tokens[0], small, member, kept, second_gain, out_pieces, out_spots
    )
    sent_blocks = gather_blocks(sent)

    carry, chunk_grads = None, []
    for packed, a, b in zip(packed_all, chunks[:-1], chunks[1:]):
        first = (member_id * local_experts + a).astype(jnp.int32).reshape(1)
        packed_grads, mixture_all, row_grad = expert_pass(
            first, sent_blocks, grad_blocks, packed, carry, b == local_experts
        )
        carry = (mixture_all, row_grad)
        chunk_grads += packed_grads

    def blocks_of(values):
        return [values[r * local_rows : (r + 1) * local_rows] for r in range(member_count)]

    normed_grad = scatter_blocks(blocks_of(row_grad))
    turned = turn(
        place,
        out_spots,
        (
            normed_grad,
            residual,
            grad_out,
            small,
            gate_rows,
            member,
            kept,
            sent,
            attended,
        ),
        out_pieces,
        cut,
        second_gain,
    )
    out_found = turned[:-2]
    resid_grad, head_grad = turned[-2:]
    mixture_parts = send_parts(blocks_of(after(mixture_all, normed_grad)))
    query_grad, key_grads = attend_back(
        head_grad, query, keys, bias.T, log_totals, cosine, sine_part
    )
    totals = [sum_chunk(chunk_grads[0])]
    if member_count == 4:
        zero = jnp.zeros((), low)
        for_first, for_second, for_own = blocks_of(key_grads)[:3]
        key_parts = []
        for r in range(4):
            part = jnp.where(member_id == r, for_first, zero)
            part += jnp.where(member_id ^ 1 == r, for_second, zero)
            key_parts.append(part + for_own if r == 0 else part)
    else:
        key_parts = blocks_of(key_grads)
    if cut:
        out_found = out_found[1], exchange_cores(out_found[0])
        key_parts = after(key_parts, mixture_parts[1:])
    keyval_sum = scatter_blocks(key_parts)
    if cut:
        out_parts = send_parts(join_cores(*out_found))
    totals.append(sum_chunk(after(chunk_grads[1], (totals[-1], keyval_sum))))
    keyval_sum = after(keyval_sum, (totals[0], out_found))
    left = leave(
        place,
        qkv_spots,
        (
            keyval_sum,
            query_grad,
            normed,
            tokens[0],
            resid_grad,
            small,
            cosine,
            sine_part,
        ),
        qkv_pieces,
        cut,
        first_gain,
    )
    qkv_found, input_grad = left[:-1], left[-1]
    result = (residual + total_of(mixture_parts)).astype(low)
    if cut:
        qkv_found = after(qkv_found, out_parts[1:])
        qkv_parts = join_cores(qkv_found[1], exchange_cores(qkv_found[0]))
        qkv_plane = after(scatter_blocks(qkv_parts), totals[1])
        out_sum = scatter_line(total_of(out_parts))
        qkv_sum = scatter_line(qkv_plane)
    else:
        out_sum = scatter_whole(out_found)
        qkv_sum = scatter_whole(qkv_found)
    for packed_grad in chunk_grads[2:]:
        totals.append(sum_chunk(after(packed_grad, totals[-1])))
    gate_total, up_total, down_total = unpack(totals, gate_weight.shape, down_weight.shape)
    return (
        result[None],
        input_grad[None],
        qkv_sum[:, qkv_width + first_gain],
        qkv_sum[:, :query_width],
        qkv_sum[:, query_width : query_width + kv_width],
        qkv_sum[:, query_width + kv_width : qkv_width],
        out_sum[:, :width],
        out_sum[:, width + second_gain],
        out_sum[:, width : width + experts_total],
        gate_total,
        up_total,
        down_total,
    )


def solution(mesh):
    return jax.shard_map(
        local,
        mesh=mesh,
        in_specs=(
            P("batch", "expert", None),
            P("batch", "expert", None),
            P(("batch", "expert")),
            P(("batch", "expert"), None),
            P(("batch", "expert"), None),
            P(("batch", "expert"), None),
            P(("batch", "expert"), None),
            P(("batch", "expert")),
            P(("batch", "expert"), None),
            P("expert", "batch", None),
            P("expert", "batch", None),
            P("expert", "batch", None),
            P("batch", "expert", None),
            P("batch", "expert"),
        ),
        out_specs=(
            P("batch", "expert", None),
            P("batch", "expert", None),
            P(("batch", "expert")),
            P(("batch", "expert"), None),
            P(("batch", "expert"), None),
            P(("batch", "expert"), None),
            P(("batch", "expert"), None),
            P(("batch", "expert")),
            P(("batch", "expert"), None),
            P("expert", "batch", None),
            P("expert", "batch", None),
            P("expert", "batch", None),
        ),
        check_vma=False,
    )
```

```python
from functools import partial

import jax
import jax.numpy as jnp
from jax import lax
from jax.experimental import pallas as pl
from jax.experimental.pallas import tpu as pltpu
from jax.sharding import PartitionSpec as P

HEADS = 24
KV_HEADS = 8
HEAD_DIM = 64
PROMPT = 512
CLEN = 256


EPS = 1e-06
THETA = 10000.0


def product(left, right):
    return jnp.dot(left, right, preferred_element_type=jnp.float32)


def place_of(row_ids):
    return jnp.where(row_ids < PROMPT, row_ids, PROMPT + (row_ids - PROMPT) % CLEN)


def visible(query_ids, key_ids):
    causal = key_ids[None, :] <= query_ids[:, None]
    same_run = (key_ids[None, :] - PROMPT) // CLEN == (query_ids[:, None] - PROMPT) // CLEN
    return causal & ((key_ids[None, :] < PROMPT) | same_run)


def dot_plain(left, right):
    return lax.dot_general(left, right, (((1,), (0,)), ((), ())), preferred_element_type=jnp.float32)


def dot_right(left, right):
    return lax.dot_general(left, right, (((1,), (1,)), ((), ())), preferred_element_type=jnp.float32)


def dot_left(left, right):
    return lax.dot_general(left, right, (((0,), (0,)), ((), ())), preferred_element_type=jnp.float32)


ANYWHERE = pl.BlockSpec(memory_space=pl.ANY)
INSIDE = pl.BlockSpec(memory_space=pltpu.VMEM)
SCALARS = pl.BlockSpec(memory_space=pltpu.SMEM)
VMEM_BYTES = 62 * 1024 * 1024


def cost(flops, *arrays):
    return pl.CostEstimate(flops=1, bytes_accessed=1, transcendentals=0)


def weight_copies(spots, pieces, target, sems):
    copies = []
    for p, piece in enumerate(pieces):
        blocks, rows = piece.shape[0], piece.shape[1]
        for k in range(blocks):
            place = pl.multiple_of(spots[p, k] * rows, rows)
            copies.append(
                pltpu.make_async_copy(
                    piece.at[k], target.at[pl.ds(place, rows)], sems.at[p * blocks + k]
                )
            )
    return copies


def block_copies(blocks, target, sems, first, columns=None):
    copies = []
    start = 0
    for i, block in enumerate(blocks):
        rows = block.shape[0]
        source = block if columns is None else block.at[:, columns]
        copies.append(
            pltpu.make_async_copy(source, target.at[pl.ds(start, rows)], sems.at[first + i])
        )
        start += rows
    return copies


def swap_halves(values):
    half = HEAD_DIM // 2
    lane = lax.broadcasted_iota(jnp.int32, values.shape, 1)
    return jnp.where(
        lane % HEAD_DIM < half,
        pltpu.roll(values, 2 * HEAD_DIM - half, 1),
        pltpu.roll(values, half, 1),
    )


def mean_square_scale(values):
    return lax.rsqrt(jnp.mean(values * values, axis=-1, keepdims=True) + EPS)


def enter_kernel(count, gain_at, spots, tokens, cosine, sine, *refs):
    pieces = refs[:count]
    normed, query, keyval, small, weight, sems = refs[count:]
    low = jnp.bfloat16
    copies = weight_copies(spots, pieces, weight, sems)
    for copy in copies:
        copy.start()
    inputs = tokens[...].astype(jnp.float32)
    scaled = inputs * mean_square_scale(inputs)
    for copy in copies:
        copy.wait()
    query_width = query.shape[1]
    kv_width = keyval.shape[1] // 2
    qkv_width = query_width + 2 * kv_width
    turned = weight[:, qkv_width:].astype(jnp.float32).T
    small[...] = turned
    rows = (scaled * turned[gain_at : gain_at + 1]).astype(low)
    normed[...] = rows
    pair = 2 * HEAD_DIM
    scale = HEAD_DIM**-0.5
    for start in range(0, query_width + kv_width, 512):
        product_part = dot_plain(rows, weight[:, start : start + 512])
        for offset in range(0, 512, pair):
            part = product_part[:, offset : offset + pair]
            part = part * cosine[...] + swap_halves(part) * sine[...]
            at = start + offset
            if at < query_width:
                query[:, at : at + pair] = (part * scale).astype(low)
            else:
                keyval[:, at - query_width : at - query_width + pair] = part.astype(low)
    keyval[:, kv_width:] = dot_plain(
        rows, weight[:, query_width + kv_width : qkv_width]
    ).astype(low)


def enter(tokens, cosine, sine, pieces, spots, gain_at, query_width, kv_width):
    rows, width = tokens.shape
    columns = pieces[0].shape[2]
    low = jnp.bfloat16
    return pl.pallas_call(
        partial(enter_kernel, len(pieces), gain_at),
        in_specs=[SCALARS, INSIDE, INSIDE, INSIDE] + [ANYWHERE] * len(pieces),
        out_specs=[INSIDE] * 4,
        out_shape=[
            jax.ShapeDtypeStruct((rows, width), low),
            jax.ShapeDtypeStruct((rows, query_width), low),
            jax.ShapeDtypeStruct((rows, 2 * kv_width), low),
            jax.ShapeDtypeStruct((columns - query_width - 2 * kv_width, width), jnp.float32),
        ],
        scratch_shapes=[
            pltpu.VMEM((width, columns), low),
            pltpu.SemaphoreType.DMA((len(pieces) * pieces[0].shape[0],)),
        ],
        compiler_params=pltpu.CompilerParams(vmem_limit_bytes=VMEM_BYTES),
        cost_estimate=cost(2 * rows * width * columns, *pieces),
        name="enter",
    )(spots, tokens, cosine, sine, *pieces)


def both_places(values):
    wide = values.astype(jnp.float32)
    low_lane = lax.broadcasted_iota(jnp.int32, values.shape, 1) < HEAD_DIM
    moved = pltpu.roll(wide, HEAD_DIM, 1)
    kind = values.dtype
    return [
        [jnp.where(low_lane, wide, 0.0).astype(kind), jnp.where(low_lane, 0.0, moved).astype(kind)],
        [jnp.where(low_lane, moved, 0.0).astype(kind), jnp.where(low_lane, 0.0, wide).astype(kind)],
    ]


def attend_kernel(
    count, query, keyval, bias, tokens, small, member, kept, gain_at, spots, *refs
):
    pieces = refs[:count]
    attended, log_totals, residual, sent, gate_rows, weight, sems = refs[count:]
    low = jnp.bfloat16
    rows = query.shape[0]
    width = tokens.shape[1]
    kv_width = keyval.shape[1] // 2
    pair_lanes = 2 * HEAD_DIM
    repeat = HEADS // KV_HEADS
    copies = weight_copies(spots, pieces, weight, sems)
    for copy in copies:
        copy.start()
    log_totals[...] = jnp.zeros_like(log_totals)
    lane = lax.broadcasted_iota(jnp.int32, log_totals.shape, 1)

    @pl.loop(0, KV_HEADS // 2)
    def _(pair):
        at = pl.ds(pl.multiple_of(pair * pair_lanes, pair_lanes), pair_lanes)
        keys = both_places(keyval[:, at])
        at = pl.ds(pl.multiple_of(kv_width + pair * pair_lanes, pair_lanes), pair_lanes)
        values = both_places(keyval[:, at])
        for i in range(repeat):
            at = pl.ds(pl.multiple_of((pair * repeat + i) * pair_lanes, pair_lanes), pair_lanes)
            queries = query[:, at]
            total = jnp.zeros((rows, pair_lanes), jnp.float32)
            for a in range(2):
                head = 2 * i + a
                scores = dot_right(queries, keys[head // repeat][a]) + bias[...]
                peak = jnp.max(scores, axis=-1, keepdims=True)
                lifted = jnp.exp(scores - peak)
                row_total = jnp.sum(lifted, axis=-1, keepdims=True)
                weights_low = (lifted * (1.0 / row_total)).astype(low)
                total += dot_plain(weights_low, values[head // repeat][a])
                log_totals[...] = jnp.where(
                    lane == pair * (2 * repeat) + head, peak + jnp.log(row_total), log_totals[...]
                )
            attended[:, at] = total.astype(low)

    for copy in copies:
        copy.wait()
    hidden = tokens[...].astype(jnp.float32) + dot_plain(attended[...], weight[...])
    residual[...] = hidden
    gain = small[gain_at : gain_at + 1, :]
    normed = (hidden * mean_square_scale(hidden) * gain).astype(low)
    logits = dot_right(normed, small[...].astype(low))
    chosen = member[...] > 0.0
    logits = jnp.where(chosen, logits, -1e30)
    lifted = jnp.where(chosen, jnp.exp(logits - jnp.max(logits, axis=-1, keepdims=True)), 0.0)
    gates = lifted / jnp.sum(lifted, axis=-1, keepdims=True)
    gate_rows[...] = gates
    sent[:, :width] = normed
    sent[:, width:] = (gates * kept[...]).astype(low)


def attend(query, keyval, bias, tokens, small, member, kept, gain_at, pieces, spots):
    rows, width = tokens.shape
    query_width = query.shape[1]
    lanes = small.shape[0]
    low = jnp.bfloat16

    def kernel(*refs):
        attend_kernel(len(pieces), *refs[:7], gain_at, *refs[7:])

    return pl.pallas_call(
        kernel,
        in_specs=[INSIDE] * 7 + [SCALARS] + [ANYWHERE] * len(pieces),
        out_specs=[INSIDE] * 5,
        out_shape=[
            jax.ShapeDtypeStruct((rows, query_width), low),
            jax.ShapeDtypeStruct((rows, 128), jnp.float32),
            jax.ShapeDtypeStruct((rows, width), jnp.float32),
            jax.ShapeDtypeStruct((rows, width + lanes), low),
            jax.ShapeDtypeStruct((rows, lanes), jnp.float32),
        ],
        scratch_shapes=[
            pltpu.VMEM((query_width, width), low),
            pltpu.SemaphoreType.DMA((len(pieces) * pieces[0].shape[0],)),
        ],
        compiler_params=pltpu.CompilerParams(vmem_limit_bytes=VMEM_BYTES),
        cost_estimate=cost(2 * rows * width * width + 8 * rows * query_width * bias.shape[1], *pieces),
        name="attend",
    )(query, keyval, bias, tokens, small, member, kept, spots, *pieces)


def grad_shapes(cut, rows, columns):
    low = jnp.bfloat16
    if cut:
        block = rows // 32
        return (
            [jax.ShapeDtypeStruct((4, 4, block, columns), low)] * 2,
            pltpu.VMEM((4, 2, 4, block, columns), low),
        )
    return (
        [jax.ShapeDtypeStruct((1, 1, 1, rows, columns), low)],
        pltpu.VMEM((1, 1, 1, rows, columns), low),
    )


def grad_copies(cut, place, source, outs, sems):
    if not cut:
        return [pltpu.make_async_copy(source, outs[0], sems.at[0])]
    core, member = place[0], place[1]
    other, own = outs
    copies = []
    for r in range(4):
        copies.append(
            pltpu.make_async_copy(
                source.at[:, 1 - core, member ^ r], other.at[r], sems.at[2 * r]
            )
        )
        copies.append(
            pltpu.make_async_copy(source.at[:, core, member ^ r], own.at[r], sems.at[2 * r + 1])
        )
    return copies


def turn_kernel(
    count,
    cut,
    gain_at,
    place,
    spots,
    normed_grad,
    residual,
    grad_out,
    small,
    gate_rows,
    member,
    kept,
    normed,
    attended,
    *refs,
):
    pieces = refs[:count]
    refs = refs[count:]
    outs = refs[: (2 if cut else 1)]
    resid_grad, head_grad, weight, weight_grad, sems, out_sems = refs[len(outs) :]
    low = jnp.bfloat16
    rows, width = residual.shape
    lanes = gate_rows.shape[1]
    copies = weight_copies(spots, pieces, weight, sems)
    for copy in copies:
        copy.start()
    lane = lax.broadcasted_iota(jnp.int32, (rows, lanes), 1)
    gates = gate_rows[...]
    gate_grads = normed_grad[:, width:] * kept[...]
    chosen_grad = gates * (gate_grads - jnp.sum(gates * gate_grads, axis=-1, keepdims=True))
    logit_grad = (chosen_grad * member[...]).astype(low)
    hidden = residual[...]
    scale = mean_square_scale(hidden)
    row_grad = normed_grad[:, :width] + dot_plain(logit_grad, small[...].astype(low))
    gain = small[gain_at : gain_at + 1, :]
    scaled = row_grad * gain
    total_grad = (
        grad_out[...].astype(jnp.float32)
        + scale * scaled
        - hidden * (scale * scale * scale) * jnp.mean(scaled * hidden, axis=-1, keepdims=True)
    )
    resid_grad[...] = total_grad
    attn_grad = total_grad.astype(low)
    shape = weight_grad.shape[:-1]
    gain_grad = (row_grad * hidden * scale).astype(low)
    picks = jnp.where(lane == gain_at, 1.0, 0.0).astype(low)
    weight_grad[..., width:] = (
        (dot_left(normed[...][:, :width], logit_grad) + dot_left(gain_grad, picks))
        .astype(low)
        .reshape(shape + (lanes,))
    )
    for start in range(0, width, 512):
        weight_grad[..., start : start + 512] = (
            dot_left(attended[...], attn_grad[:, start : start + 512])
            .astype(low)
            .reshape(shape + (512,))
        )
    out_copies = grad_copies(cut, place, weight_grad, outs, out_sems)
    for copy in out_copies:
        copy.start()
    for copy in copies:
        copy.wait()
    head_grad[...] = dot_right(attn_grad, weight[...]).astype(low)
    for copy in out_copies:
        copy.wait()


def turn(place, spots, operands, pieces, cut, gain_at):
    residual, gate_rows, attended = operands[1], operands[4], operands[8]
    rows, width = residual.shape
    query_width = attended.shape[1]
    low = jnp.bfloat16
    grads, held = grad_shapes(cut, query_width, width + gate_rows.shape[1])
    return pl.pallas_call(
        partial(turn_kernel, len(pieces), cut, gain_at),
        in_specs=[SCALARS, SCALARS] + [INSIDE] * len(operands) + [ANYWHERE] * len(pieces),
        out_specs=[ANYWHERE] * len(grads) + [INSIDE] * 2,
        out_shape=grads
        + [
            jax.ShapeDtypeStruct((rows, width), jnp.float32),
            jax.ShapeDtypeStruct((rows, query_width), low),
        ],
        scratch_shapes=[
            pltpu.VMEM((query_width, width), low),
            held,
            pltpu.SemaphoreType.DMA((len(pieces) * pieces[0].shape[0],)),
            pltpu.SemaphoreType.DMA((8,)),
        ],
        compiler_params=pltpu.CompilerParams(vmem_limit_bytes=VMEM_BYTES),
        cost_estimate=cost(0),
        name="turn",
    )(place, spots, *operands, *pieces)


def attend_back_kernel(
    head_grad, query, keyval, bias, log_totals, cosine, sine, query_grad, keyval_grad, totals
):
    low = jnp.bfloat16
    rows = query.shape[0]
    kv_width = keyval.shape[1] // 2
    pair_lanes = 2 * HEAD_DIM
    repeat = HEADS // KV_HEADS
    totals[...] = log_totals[...].T

    @pl.loop(0, KV_HEADS // 2)
    def _(pair):
        key_at = pl.ds(pl.multiple_of(pair * pair_lanes, pair_lanes), pair_lanes)
        value_at = pl.ds(pl.multiple_of(kv_width + pair * pair_lanes, pair_lanes), pair_lanes)
        keys = both_places(keyval[:, key_at])
        values = both_places(keyval[:, value_at])
        key_grads = [[None, None], [None, None]]
        value_grads = [[None, None], [None, None]]
        for i in range(repeat):
            at = pl.ds(pl.multiple_of((pair * repeat + i) * pair_lanes, pair_lanes), pair_lanes)
            queries = query[:, at]
            grads = head_grad[:, at]
            query_part = jnp.zeros((rows, pair_lanes), jnp.float32)
            for a in range(2):
                head = 2 * i + a
                g = head // repeat
                total = totals[pl.ds(pair * (2 * repeat) + head, 1), :]
                weights = jnp.exp(dot_right(keys[g][a], queries) + bias[...] - total)
                weight_grads = dot_right(values[g][a], grads)
                delta = jnp.sum(weights * weight_grads, axis=0, keepdims=True)
                score_grads = (weights * (weight_grads - delta)).astype(low)
                value_part = dot_plain(weights.astype(low), grads)
                key_part = dot_plain(score_grads, queries)
                query_part += dot_left(score_grads, keys[g][a])
                if key_grads[g][a] is None:
                    key_grads[g][a], value_grads[g][a] = key_part, value_part
                else:
                    key_grads[g][a] += key_part
                    value_grads[g][a] += value_part
            query_part = query_part * (HEAD_DIM**-0.5)
            query_part = query_part * cosine[...] - swap_halves(query_part) * sine[...]
            query_grad[:, at] = query_part.astype(low)
        low_lane = lax.broadcasted_iota(jnp.int32, (keyval.shape[0], pair_lanes), 1) < HEAD_DIM
        for at, found in ((key_at, key_grads), (value_at, value_grads)):
            keyval_grad[:, at] = jnp.where(
                low_lane,
                found[0][0] + pltpu.roll(found[0][1], HEAD_DIM, 1),
                pltpu.roll(found[1][0], HEAD_DIM, 1) + found[1][1],
            ).astype(low)


def attend_back(head_grad, query, keyval, bias, log_totals, cosine, sine):
    rows, query_width = query.shape
    low = jnp.bfloat16
    return pl.pallas_call(
        attend_back_kernel,
        in_specs=[INSIDE] * 7,
        out_specs=[INSIDE] * 2,
        out_shape=[
            jax.ShapeDtypeStruct((rows, query_width), low),
            jax.ShapeDtypeStruct(keyval.shape, low),
        ],
        scratch_shapes=[pltpu.VMEM((128, rows), jnp.float32)],
        compiler_params=pltpu.CompilerParams(vmem_limit_bytes=VMEM_BYTES),
        cost_estimate=cost(0),
        name="attend_back",
    )(head_grad, query, keyval, bias, log_totals, cosine, sine)


def leave_kernel(
    count,
    cut,
    gain_at,
    place,
    spots,
    keyval_sum,
    query_grad,
    normed,
    tokens,
    resid_grad,
    small,
    cosine,
    sine,
    *refs,
):
    pieces = refs[:count]
    refs = refs[count:]
    outs = refs[: (2 if cut else 1)]
    input_grad, weight, weight_grad, joined, sems, out_sems = refs[len(outs) :]
    low = jnp.bfloat16
    rows, width = tokens.shape
    query_width = query_grad.shape[1]
    kv_width = keyval_sum.shape[1] // 2
    qkv_width = query_width + 2 * kv_width
    pair = 2 * HEAD_DIM
    copies = weight_copies(spots, pieces, weight, sems)
    for copy in copies:
        copy.start()
    joined[:, :query_width] = query_grad[...]
    for start in range(0, kv_width, pair):
        part = keyval_sum[:, start : start + pair]
        part = part * cosine[...] - swap_halves(part) * sine[...]
        joined[:, query_width + start : query_width + start + pair] = part.astype(low)
    joined[:, query_width + kv_width :] = keyval_sum[:, kv_width:].astype(low)
    shape = weight_grad.shape[:-1]
    for start in range(0, qkv_width, 512):
        weight_grad[..., start : start + 512] = (
            dot_left(normed[...], joined[:, start : start + 512]).astype(low).reshape(shape + (512,))
        )
    for copy in copies:
        copy.wait()
    row_grad = dot_right(joined[...], weight[:, :qkv_width])
    inputs = tokens[...].astype(jnp.float32)
    scale = mean_square_scale(inputs)
    lanes = weight_grad.shape[-1] - qkv_width
    lane = lax.broadcasted_iota(jnp.int32, (rows, lanes), 1)
    picks = jnp.where(lane == gain_at, 1.0, 0.0).astype(low)
    weight_grad[..., qkv_width:] = (
        dot_left((row_grad * inputs * scale).astype(low), picks).astype(low).reshape(shape + (lanes,))
    )
    out_copies = grad_copies(cut, place, weight_grad, outs, out_sems)
    for copy in out_copies:
        copy.start()
    scaled = row_grad * small[gain_at : gain_at + 1, :]
    input_grad[...] = (
        resid_grad[...]
        + scale * scaled
        - inputs * (scale * scale * scale) * jnp.mean(scaled * inputs, axis=-1, keepdims=True)
    )
    for copy in out_copies:
        copy.wait()


def leave(place, spots, operands, pieces, cut, gain_at):
    tokens, query_grad, keyval_sum = operands[3], operands[1], operands[0]
    rows, width = tokens.shape
    columns = pieces[0].shape[2]
    low = jnp.bfloat16
    grads, held = grad_shapes(cut, width, columns)
    return pl.pallas_call(
        partial(leave_kernel, len(pieces), cut, gain_at),
        in_specs=[SCALARS, SCALARS] + [INSIDE] * len(operands) + [ANYWHERE] * len(pieces),
        out_specs=[ANYWHERE] * len(grads) + [INSIDE],
        out_shape=grads + [jax.ShapeDtypeStruct((rows, width), jnp.float32)],
        scratch_shapes=[
            pltpu.VMEM((width, columns), low),
            held,
            pltpu.VMEM((rows, query_grad.shape[1] + keyval_sum.shape[1]), low),
            pltpu.SemaphoreType.DMA((len(pieces) * pieces[0].shape[0],)),
            pltpu.SemaphoreType.DMA((8,)),
        ],
        compiler_params=pltpu.CompilerParams(vmem_limit_bytes=VMEM_BYTES),
        cost_estimate=cost(0),
        name="leave",
    )(place, spots, *operands, *pieces)


def expert_kernel(cut, carried, last, row_blocks, grad_blocks, row_tile, place, first, packed, *refs):
    blocks_in = refs[:row_blocks]
    grads_in = refs[row_blocks : row_blocks + grad_blocks]
    refs = refs[row_blocks + grad_blocks :]
    if carried:
        mix_in, turn_in = refs[:2]
        refs = refs[2:]
    count = packed.shape[2]
    outs = 4 if cut else 1
    packed_grads = refs[:outs]
    mix_out, turn_out = refs[outs : outs + 2]
    refs = refs[outs + 2 :]
    if last:
        mix, turned = refs[:2]
        refs = refs[2:]
    else:
        mix, turned = mix_out, turn_out
    (
        rows,
        rows_turned,
        grads,
        gates,
        gate_w,
        up_w,
        down_w,
        gate_g,
        up_g,
        down_g,
        weighted,
        gate_side,
        up_side,
        load_sems,
        save_sems,
        carry_sems,
    ) = refs
    hidden_width = gate_w.shape[-1]
    total_rows, width = rows.shape
    lanes = gates.shape[1]
    low = jnp.bfloat16

    def sides(gate, up, down):
        for side, inner in ((0, gate), (1, up)):
            for j in range(3):
                yield side, pl.ds(j * hidden_width, hidden_width), inner, j
        yield 2, pl.ds(0, width), down, None

    def loads(e):
        slot = e % 2
        copies = []
        for i, (side, columns, inner, j) in enumerate(sides(gate_w, up_w, down_w)):
            outer = packed.at[:, side, e, :, columns]
            inner = inner.at[slot] if j is None else inner.at[slot, :, j]
            copies.append(pltpu.make_async_copy(outer, inner, load_sems.at[slot, i]))
        return copies

    def saves(e):
        slot = e % 2
        copies = []
        for i, (side, columns, inner, j) in enumerate(sides(gate_g, up_g, down_g)):
            if not cut:
                outer = packed_grads[0].at[:, side, e, :, columns]
                source = inner.at[slot] if j is None else inner.at[slot, :, j]
                copies.append(pltpu.make_async_copy(source, outer, save_sems.at[slot, i]))
                continue
            own, rest, far, near = packed_grads
            targets = [own, rest.at[0], rest.at[1], rest.at[2]]
            targets += [near.at[1], near.at[0], far.at[0], far.at[1]]
            for n, target in enumerate(targets):
                block = 2 * lax.rem(place[2] + n % 4, 4) + (place[0] ^ (n // 4))
                source = inner.at[slot, block] if j is None else inner.at[slot, block, j]
                outer = target.at[side, e, :, columns]
                copies.append(pltpu.make_async_copy(source, outer, save_sems.at[slot, 8 * i + n]))
        return copies

    carries = (
        block_copies(grads_in, grads, carry_sems, 0, pl.ds(0, width))
        + block_copies(blocks_in, rows, carry_sems, grad_blocks, pl.ds(0, width))
        + block_copies(
            blocks_in, gates, carry_sems, grad_blocks + row_blocks, pl.ds(width, lanes)
        )
    )
    sums = []
    if carried:
        at = grad_blocks + 2 * row_blocks
        sums = [
            pltpu.make_async_copy(mix_in, mix, carry_sems.at[at]),
            pltpu.make_async_copy(turn_in, turned, carry_sems.at[at + 1]),
        ]
    for copy in loads(0) + carries + sums:
        copy.start()
    for e in range(count):
        slot = e % 2
        if e + 1 < count:
            for copy in loads(e + 1):
                copy.start()
        for copy in loads(e):
            copy.wait()
        if e == 0:
            for copy in carries:
                copy.wait()
            rows_turned[...] = rows[...].T
            if not carried:
                turned[:, width:] = jnp.zeros((total_rows, lanes), jnp.float32)

        @pl.loop(0, total_rows // row_tile)
        def _(tile):
            span = pl.ds(pl.multiple_of(tile * row_tile, row_tile), row_tile)
            gate_full = gate_w[slot].reshape(width, hidden_width)
            up_full = up_w[slot].reshape(width, hidden_width)
            down_full = down_w[slot].reshape(hidden_width, width)
            here = rows[span, :]
            slope = dot_right(grads[span, :], down_full)
            gate_pre = dot_plain(here, gate_full)
            up_pre = dot_plain(here, up_full)
            lane = lax.broadcasted_iota(jnp.int32, (row_tile, lanes), 1)
            chosen = lane == first[0] + e
            gate_column = jnp.sum(
                jnp.where(chosen, gates[span, :].astype(jnp.float32), 0.0), axis=1, keepdims=True
            )
            sigmoid_gate = jax.nn.sigmoid(gate_pre)
            activated = gate_pre * sigmoid_gate
            hidden = (activated * up_pre).astype(low).astype(jnp.float32)
            share = jnp.sum(hidden * slope, axis=1, keepdims=True)
            if e == 0 and sums:

                @pl.when(tile == 0)
                def _():
                    for copy in sums:
                        copy.wait()

            turned[span, width:] = jnp.where(chosen, share, turned[span, width:])
            part_weighted = (hidden * gate_column).astype(low)
            hidden_grad = slope * gate_column
            part_gate = (
                hidden_grad * up_pre * (sigmoid_gate + activated * (1.0 - sigmoid_gate))
            ).astype(low)
            part_up = (hidden_grad * activated).astype(low)
            weighted[span, :] = part_weighted
            gate_side[span, :] = part_gate
            up_side[span, :] = part_up
            mix_part = dot_plain(part_weighted, down_full)
            turn_part = dot_right(part_gate, gate_full) + dot_right(part_up, up_full)
            if e == 0 and not carried:
                mix[span, :] = mix_part
                turned[span, :width] = turn_part
            elif last and e == count - 1:
                mix_out[span, :] = (mix[span, :] + mix_part).astype(low)
                turn_out[span, :width] = (turned[span, :width] + turn_part).astype(low)
                turn_out[span, width:] = turned[span, width:].astype(low)
            else:
                mix[span, :] += mix_part
                turned[span, :width] += turn_part

        if e >= 2:
            for copy in saves(e - 2):
                copy.wait()
        down_g[slot] = dot_left(weighted[...], grads[...]).astype(low).reshape(down_g.shape[1:])
        gate_g[slot] = dot_plain(rows_turned[...], gate_side[...]).astype(low).reshape(gate_g.shape[1:])
        up_g[slot] = dot_plain(rows_turned[...], up_side[...]).astype(low).reshape(up_g.shape[1:])
        for copy in saves(e):
            copy.start()
    for e in range(max(0, count - 2), count):
        for copy in saves(e):
            copy.wait()


def expert_pass(place, first, rows, grads, packed, carry, cut, last):
    blocks, _, count, part, width = packed.shape
    hidden_width = blocks * part
    total_rows = sum(block.shape[0] for block in rows)
    lanes = rows[0].shape[1] - width
    low = jnp.bfloat16
    wide = jnp.float32
    carried = carry is not None
    flops = 18 * total_rows * count * hidden_width * width
    side = pltpu.VMEM((2, blocks, 3, part, hidden_width), low)
    sides = [side, side, pltpu.VMEM((2, blocks, part, width), low)]
    sums = [(total_rows, width), (total_rows, width + lanes)]
    one = packed.shape[1:]
    grads_out = [one, (3,) + one, (2,) + one, (2,) + one] if cut else [packed.shape]
    outs = len(grads_out)
    found = pl.pallas_call(
        partial(expert_kernel, cut, carried, last, len(rows), len(grads), min(512, total_rows)),
        in_specs=[SCALARS, SCALARS]
        + [ANYWHERE] * (1 + len(rows) + len(grads) + (2 if carried else 0)),
        out_specs=[ANYWHERE] * outs + [INSIDE, INSIDE],
        out_shape=[jax.ShapeDtypeStruct(shape, low) for shape in grads_out]
        + [jax.ShapeDtypeStruct(shape, low if last else wide) for shape in sums],
        scratch_shapes=([pltpu.VMEM(shape, wide) for shape in sums] if last else [])
        + [
            pltpu.VMEM((total_rows, width), low),
            pltpu.VMEM((width, total_rows), low),
            pltpu.VMEM((total_rows, width), low),
            pltpu.VMEM((total_rows, lanes), low),
        ]
        + sides
        + sides
        + [pltpu.VMEM((total_rows, hidden_width), low)] * 3
        + [
            pltpu.SemaphoreType.DMA((2, 7)),
            pltpu.SemaphoreType.DMA((2, 56)),
            pltpu.SemaphoreType.DMA((2 * len(rows) + len(grads) + 2,)),
        ],
        compiler_params=pltpu.CompilerParams(vmem_limit_bytes=VMEM_BYTES),
        cost_estimate=cost(flops, packed, packed, *rows, *grads),
        name="experts",
    )(place, first, packed, *rows, *grads, *(carry or ()))
    return found[:outs], found[outs], found[outs + 1]


def unpack_kernel(terms, *refs):
    found, (gate, up, down) = refs[:-3], refs[-3:]
    hidden_width = gate.shape[2]
    base = 0
    for n in range(0, len(found), terms):
        parts = found[n : n + terms]
        count, part = parts[0].shape[1], parts[0].shape[2]
        for e in range(count):
            for side in range(3):
                total = parts[0][side, e].astype(jnp.float32)
                for other in parts[1:]:
                    total += other[side, e].astype(jnp.float32)
                if side == 2:
                    down[base + e] = total
                    continue
                for j in range(3):
                    (gate, up)[side][base + e, j * part : (j + 1) * part, :] = total[
                        :, j * hidden_width : (j + 1) * hidden_width
                    ]
        base += count


def unpack(chunks, gate_shape, down_shape):
    arrays = [term for terms in chunks for term in terms]
    return pl.pallas_call(
        partial(unpack_kernel, len(chunks[0])),
        in_specs=[INSIDE] * len(arrays),
        out_specs=[INSIDE] * 3,
        out_shape=[
            jax.ShapeDtypeStruct(gate_shape, jnp.float32),
            jax.ShapeDtypeStruct(gate_shape, jnp.float32),
            jax.ShapeDtypeStruct(down_shape, jnp.float32),
        ],
        compiler_params=pltpu.CompilerParams(vmem_limit_bytes=VMEM_BYTES),
        cost_estimate=cost(0),
        name="unpack",
    )(*arrays)


def cube():
    return lax.axis_size("batch") == 8 and lax.axis_size("expert") == 4


def pair_moves(size, flip):
    return [(i, i ^ flip) for i in range(size)]


def shift_moves(step):
    return [(2 * z + c, 2 * ((z + step) % 4) + c) for z in range(4) for c in range(2)]


def gather_blocks(rows, at_once=False):
    size = lax.axis_size("expert")
    if size != 4:
        stacked = lax.all_gather(rows, "expert", axis=0)
        own = lax.axis_index("expert")
        return [
            lax.dynamic_index_in_dim(stacked, own ^ r, axis=0, keepdims=False) for r in range(size)
        ]
    across, along = pair_moves(size, 1), pair_moves(size, 2)
    if at_once:
        return [rows] + [lax.ppermute(rows, "expert", pair_moves(size, r)) for r in range(1, 4)]
    half = rows.shape[0] // 2
    first = lax.ppermute(rows, "expert", across)
    second = lax.ppermute(rows, "expert", along)
    top = lax.ppermute(second[:half], "expert", across)
    bottom = lax.ppermute(first[half:], "expert", along)
    return [rows, first, second, top, bottom]


def scatter_blocks(parts, events=()):
    size = lax.axis_size("expert")
    low = jnp.bfloat16
    wide = jnp.float32
    if size != 4:
        own = lax.axis_index("expert")
        order = jnp.arange(size, dtype=jnp.int32) ^ own
        stacked = jnp.take(jnp.stack(parts), order, axis=0).astype(low)
        return lax.psum_scatter(stacked, "expert", scatter_dimension=0).astype(wide)
    across, along = pair_moves(size, 1), pair_moves(size, 2)
    half = parts[0].shape[0] // 2
    top = lax.ppermute(parts[3][:half].astype(low), "expert", across)
    bottom = lax.ppermute(parts[3][half:].astype(low), "expert", along)
    first_top = lax.ppermute(parts[1][:half].astype(low), "expert", across)
    second_bottom = lax.ppermute(parts[2][half:].astype(low), "expert", along)
    for_second = (parts[2][:half].astype(wide) + top.astype(wide)).astype(low)
    for_first = (parts[1][half:].astype(wide) + bottom.astype(wide)).astype(low)
    for_first, for_second = after((for_first, for_second), events)
    second_top = lax.ppermute(for_second, "expert", along)
    first_bottom = lax.ppermute(for_first, "expert", across)
    own = parts[0].astype(wide)
    return jnp.concatenate(
        [
            own[:half] + first_top.astype(wide) + second_top.astype(wide),
            own[half:] + first_bottom.astype(wide) + second_bottom.astype(wide),
        ],
        axis=0,
    )


def after(values, events):
    return lax.optimization_barrier((values, events))[0]


def send_parts(parts):
    if lax.axis_size("expert") != 4:
        return [scatter_blocks(parts)]
    low = jnp.bfloat16
    return [parts[0]] + [
        lax.ppermute(parts[r].astype(low), "expert", pair_moves(4, r)) for r in range(1, 4)
    ]


def total_of(parts):
    total = parts[0].astype(jnp.float32)
    for part in parts[1:]:
        total += part.astype(jnp.float32)
    return total


def shift_dense(rows):
    if not cube():
        return [lax.all_gather(rows, ("batch", "expert"), axis=0, tiled=True)]
    below = lax.ppermute(rows, "batch", shift_moves(1))
    above = lax.ppermute(rows, "batch", shift_moves(3))
    return [rows, below, lax.ppermute(below, "batch", shift_moves(1)), above]


def gather_dense(line, columns, events):
    found = [rows[:, columns] for rows in line]
    if not cube():
        return [found[0][None]], jnp.zeros((1, 1), jnp.int32), (), ()
    place = lax.axis_index("batch")
    level, core = place // 2, place % 2
    member = lax.axis_index("expert")
    mine = gather_blocks(after(jnp.stack(found), events))
    plane, far = mine[1:3], mine[3:]
    mine = mine[:3] + [jnp.concatenate(far, axis=0)]
    other = [lax.ppermute(block, "batch", pair_moves(8, 1)) for block in mine]
    spots = [
        [(((level + 4 - k) % 4) * 2 + (core ^ c)) * 4 + (member ^ r) for k in range(4)]
        for c in range(2)
        for r in range(4)
    ]
    return mine + other, jnp.array(spots, jnp.int32), plane, far


def sum_chunk(packed_grad):
    return lax.psum_scatter(packed_grad, "batch", scatter_dimension=0)


def exchange_cores(values):
    return lax.ppermute(values, "batch", pair_moves(8, 1))


def step_up(values):
    return lax.ppermute(values, "batch", shift_moves(1))


def step_down(values):
    return lax.ppermute(values, "batch", shift_moves(3))


def add_low(*parts):
    total = parts[0].astype(jnp.float32)
    for part in parts[1:]:
        total += part.astype(jnp.float32)
    return total.astype(jnp.bfloat16)


def join_cores(own, received):
    return [add_low(own[r], received[r]) for r in range(4)]


def scatter_line(plane):
    level = lax.axis_index("batch") // 2
    own, up, far, down = (
        lax.dynamic_index_in_dim(plane, (level + r) % 4, axis=0, keepdims=False) for r in range(4)
    )
    forwarded = step_up(add_low(up, step_up(add_low(far))))
    return total_of([own, forwarded, step_down(add_low(down))])


def scatter_whole(found):
    values = found[0].reshape(found[0].shape[3:])
    total = lax.psum_scatter(values, ("batch", "expert"), scatter_dimension=0, tiled=True)
    return total.astype(jnp.float32)


def pack_kernel(chunks, query, key, value, small, out, gate, up, down, dense, *packed):
    start = 0
    for part in (query, key, value, small, out):
        dense[:, start : start + part.shape[1]] = part[...]
        start += part.shape[1]
    part, hidden_width = down.shape[1], gate.shape[2]
    for n, target in enumerate(packed):
        for e in range(chunks[n], chunks[n + 1]):
            for side, source in ((0, gate), (1, up)):
                for j in range(3):
                    target[side, e - chunks[n], :, j * hidden_width : (j + 1) * hidden_width] = (
                        source[e, j * part : (j + 1) * part, :]
                    )
            target[2, e - chunks[n]] = down[e]


def pack(chunks, query, key, value, small, out, gate, up, down):
    low = jnp.bfloat16
    columns = sum(part.shape[1] for part in (query, key, value, small, out))
    return pl.pallas_call(
        partial(pack_kernel, chunks),
        in_specs=[INSIDE] * 8,
        out_specs=[INSIDE] * len(chunks),
        out_shape=[jax.ShapeDtypeStruct((query.shape[0], columns), low)]
        + [
            jax.ShapeDtypeStruct((3, b - a) + down.shape[1:], low)
            for a, b in zip(chunks[:-1], chunks[1:])
        ],
        compiler_params=pltpu.CompilerParams(vmem_limit_bytes=VMEM_BYTES),
        cost_estimate=cost(0),
        name="pack",
    )(query, key, value, small, out, gate, up, down)


def local(
    tokens,
    cotangent,
    attn_gain,
    query_weight,
    key_weight,
    value_weight,
    out_weight,
    ffn_gain,
    router_weight,
    gate_weight,
    up_weight,
    down_weight,
    routes,
    ranking,
):
    low = jnp.bfloat16
    wide = jnp.float32
    query_width = HEADS * HEAD_DIM
    kv_width = KV_HEADS * HEAD_DIM
    qkv_width = query_width + 2 * kv_width
    width = tokens.shape[2]
    experts_total = router_weight.shape[1]
    extra = -(-(experts_total + 2) // 128) * 128
    first_gain, second_gain = experts_total, experts_total + 1
    local_experts = gate_weight.shape[0]
    member_count = lax.axis_size("expert")
    member_id = lax.axis_index("expert")
    local_rows = tokens.shape[1]
    group_rows = local_rows * member_count
    cut = cube()
    line_place = lax.axis_index("batch")
    place = jnp.stack([line_place % 2, member_id, line_place // 2]).astype(jnp.int32)

    route_rows = routes[0]
    rank_rows = ranking[0]
    expert_lanes = jnp.arange(extra, dtype=jnp.int32)
    member = jnp.any(route_rows[:, :, None] == expert_lanes[None, None, :], axis=1)
    marks = jnp.where(
        expert_lanes[None, :] == experts_total,
        (rank_rows // 32)[:, None],
        jnp.where(expert_lanes[None, :] == experts_total + 1, (rank_rows % 32)[:, None], member),
    ).astype(low)
    grad_out = cotangent[0]
    small_width = qkv_width + extra
    chunks = (0, 3, local_experts)
    dense_rows, *packed_own = pack(
        chunks,
        query_weight,
        key_weight,
        value_weight,
        jnp.concatenate(
            [
                router_weight,
                attn_gain[:, None],
                ffn_gain[:, None],
                jnp.zeros((query_weight.shape[0], extra - experts_total - 2), low),
            ],
            axis=1,
        ),
        out_weight,
        gate_weight,
        up_weight,
        down_weight,
    )
    line = shift_dense(dense_rows)
    grad_blocks = gather_blocks(
        after(jnp.concatenate([grad_out, marks], axis=1), dense_rows), True
    )
    marks_all = jnp.concatenate([block[:, width:] for block in grad_blocks], axis=0)
    qkv_pieces, qkv_spots, plane, far = gather_dense(line, slice(0, small_width), grad_blocks)
    out_pieces, out_spots, out_plane, _ = gather_dense(line, slice(small_width, None), far)
    packed_all = [
        lax.all_gather(after(packed, events), "batch", axis=0)
        for packed, events in zip(packed_own, ((line, grad_blocks), plane))
    ]

    row_ids = member_id * local_rows + jnp.arange(local_rows, dtype=jnp.int32)
    half_dim = HEAD_DIM // 2
    frequency = THETA ** (-jnp.arange(half_dim, dtype=wide) / half_dim)
    angles = place_of(row_ids).astype(wide)[:, None] * frequency[None, :]
    cosine = jnp.tile(jnp.cos(angles), (1, 4))
    sine_part = jnp.tile(jnp.concatenate([-jnp.sin(angles), jnp.sin(angles)], axis=1), (1, 2))
    normed, query, keyval, small = enter(
        tokens[0], cosine, sine_part, qkv_pieces, qkv_spots, first_gain, query_width, kv_width
    )

    rank_all = (
        marks_all[:, experts_total].astype(wide) * 32 + marks_all[:, experts_total + 1].astype(wide)
    )
    earlier = (rank_all[None, :] < rank_rows.astype(wide)[:, None]).astype(low)
    before = product(earlier, marks_all)
    capacity = 5 * group_rows * route_rows.shape[1] // (4 * experts_total)
    member = member.astype(wide)
    kept = jnp.where(before < capacity, member, 0.0)

    keyval_blocks = gather_blocks(after(keyval, out_plane))
    if member_count == 4:
        ordered = keyval_blocks[:3] + [jnp.concatenate(keyval_blocks[3:], axis=0)]
        away = 1 << 20
        keys = jnp.concatenate(
            [
                lax.select_n(member_id, *ordered),
                lax.select_n(member_id ^ 1, *ordered),
                keyval,
            ],
            axis=0,
        )
        starts = [
            jnp.where(member_id >= 1, 0, away),
            jnp.where(member_id >= 2, local_rows, away),
            member_id * local_rows,
        ]
    else:
        keys = jnp.concatenate(keyval_blocks, axis=0)
        starts = [(member_id ^ r) * local_rows for r in range(member_count)]
    key_ids = jnp.concatenate([s + jnp.arange(local_rows, dtype=jnp.int32) for s in starts])
    bias = jnp.where(visible(row_ids, key_ids), 0.0, -1e30).astype(wide)
    attended, log_totals, residual, sent, gate_rows = attend(
        query, keys, bias, tokens[0], small, member, kept, second_gain, out_pieces, out_spots
    )
    sent_blocks = gather_blocks(sent)

    carry, chunk_grads = None, []
    for packed, a, b in zip(packed_all, chunks[:-1], chunks[1:]):
        first = (member_id * local_experts + a).astype(jnp.int32).reshape(1)
        if carry is not None and cut:
            own, rest, far, near = chunk_grads[0]
            far, near = exchange_cores(far), exchange_cores(near)
            far_sum, down_sum = add_low(rest[1], far[0]), add_low(rest[2], far[1])
            first = after(first, (far_sum, down_sum))
            up_sum = add_low(rest[0], near[0], step_up(far_sum))
        packed_grads, mixture_all, row_grad = expert_pass(
            place, first, sent_blocks, grad_blocks, packed, carry, cut, b == local_experts
        )
        carry = (mixture_all, row_grad)
        chunk_grads.append(packed_grads)

    def blocks_of(values):
        return [values[r * local_rows : (r + 1) * local_rows] for r in range(member_count)]

    if cut:
        row_grad = after(row_grad, up_sum)
        down_term = step_down(after(down_sum, up_sum))
        early_own, early_near = own, near[1]
        own, rest, far, near = chunk_grads[1]
        far, near = exchange_cores(far), exchange_cores(near)
        far_sum, late_down_sum = add_low(rest[1], far[0]), add_low(rest[2], far[1])
    normed_grad = scatter_blocks(blocks_of(row_grad))
    if cut:
        normed_grad = after(normed_grad, (far_sum, late_down_sum))
    turned = turn(
        place,
        out_spots,
        (
            normed_grad,
            residual,
            grad_out,
            small,
            gate_rows,
            member,
            kept,
            sent,
            attended,
        ),
        out_pieces,
        cut,
        second_gain,
    )
    out_found = turned[:-2]
    resid_grad, head_grad = turned[-2:]
    mixture_parts = send_parts(blocks_of(after(mixture_all, normed_grad)))
    if cut:
        head_grad = after(head_grad, down_term)
        up_term = step_up(up_sum)
        terms = [[early_own, early_near, down_term, up_term]]
        late_up_sum = add_low(rest[0], near[0], step_up(far_sum))
    query_grad, key_grads = attend_back(
        head_grad, query, keys, bias.T, log_totals, cosine, sine_part
    )
    if member_count == 4:
        zero = jnp.zeros((), low)
        for_first, for_second, for_own = blocks_of(key_grads)[:3]
        key_parts = []
        for r in range(4):
            part = jnp.where(member_id == r, for_first, zero)
            part += jnp.where(member_id ^ 1 == r, for_second, zero)
            key_parts.append(part + for_own if r == 0 else part)
    else:
        key_parts = blocks_of(key_grads)
    if cut:
        out_found = out_found[1], exchange_cores(out_found[0])
        key_parts = after(key_parts, (mixture_parts[1:], late_up_sum))
    keyval_sum = scatter_blocks(key_parts)
    if cut:
        out_parts = send_parts(join_cores(*out_found))
    if cut:
        keyval_sum = after(keyval_sum, out_found)
    left = leave(
        place,
        qkv_spots,
        (
            keyval_sum,
            query_grad,
            normed,
            tokens[0],
            resid_grad,
            small,
            cosine,
            sine_part,
        ),
        qkv_pieces,
        cut,
        first_gain,
    )
    qkv_found, input_grad = left[:-1], left[-1]
    result = (residual + total_of(mixture_parts)).astype(low)
    if cut:
        qkv_found = after(qkv_found, (out_parts[1:], up_term))
        qkv_parts = join_cores(qkv_found[1], exchange_cores(qkv_found[0]))
        late_down_term = step_down(after(late_down_sum, up_term))
        late_up_term = step_up(after(late_up_sum, up_term))
        terms.append([own, near[1], late_down_term, late_up_term])
        qkv_plane = after(scatter_blocks(qkv_parts, late_down_term), late_up_term)
        out_sum = scatter_line(total_of(out_parts))
        qkv_sum = scatter_line(qkv_plane)
        terms = after(terms, qkv_plane)
    else:
        out_sum = scatter_whole(out_found)
        qkv_sum = scatter_whole(qkv_found)
        terms = [[sum_chunk(found[0])] for found in chunk_grads]
    gate_total, up_total, down_total = unpack(terms, gate_weight.shape, down_weight.shape)
    return (
        result[None],
        input_grad[None],
        qkv_sum[:, qkv_width + first_gain],
        qkv_sum[:, :query_width],
        qkv_sum[:, query_width : query_width + kv_width],
        qkv_sum[:, query_width + kv_width : qkv_width],
        out_sum[:, :width],
        out_sum[:, width + second_gain],
        out_sum[:, width : width + experts_total],
        gate_total,
        up_total,
        down_total,
    )


def solution(mesh):
    return jax.shard_map(
        local,
        mesh=mesh,
        in_specs=(
            P("batch", "expert", None),
            P("batch", "expert", None),
            P(("batch", "expert")),
            P(("batch", "expert"), None),
            P(("batch", "expert"), None),
            P(("batch", "expert"), None),
            P(("batch", "expert"), None),
            P(("batch", "expert")),
            P(("batch", "expert"), None),
            P("expert", "batch", None),
            P("expert", "batch", None),
            P("expert", "batch", None),
            P("batch", "expert", None),
            P("batch", "expert"),
        ),
        out_specs=(
            P("batch", "expert", None),
            P("batch", "expert", None),
            P(("batch", "expert")),
            P(("batch", "expert"), None),
            P(("batch", "expert"), None),
            P(("batch", "expert"), None),
            P(("batch", "expert"), None),
            P(("batch", "expert")),
            P(("batch", "expert"), None),
            P("expert", "batch", None),
            P("expert", "batch", None),
            P("expert", "batch", None),
        ),
        check_vma=False,
    )
```

```python
from functools import partial

import jax
import jax.numpy as jnp
from jax import lax
from jax.experimental import pallas as pl
from jax.experimental.pallas import tpu as pltpu
from jax.sharding import PartitionSpec as P

HEADS = 24
KV_HEADS = 8
HEAD_DIM = 64
PROMPT = 512
CLEN = 256


EPS = 1e-06
THETA = 10000.0


def product(left, right):
    return jnp.dot(left, right, preferred_element_type=jnp.float32)


def place_of(row_ids):
    return jnp.where(row_ids < PROMPT, row_ids, PROMPT + (row_ids - PROMPT) % CLEN)


def visible(query_ids, key_ids):
    causal = key_ids[None, :] <= query_ids[:, None]
    same_run = (key_ids[None, :] - PROMPT) // CLEN == (query_ids[:, None] - PROMPT) // CLEN
    return causal & ((key_ids[None, :] < PROMPT) | same_run)


def dot_plain(left, right):
    return lax.dot_general(left, right, (((1,), (0,)), ((), ())), preferred_element_type=jnp.float32)


def dot_right(left, right):
    return lax.dot_general(left, right, (((1,), (1,)), ((), ())), preferred_element_type=jnp.float32)


def dot_left(left, right):
    return lax.dot_general(left, right, (((0,), (0,)), ((), ())), preferred_element_type=jnp.float32)


ANYWHERE = pl.BlockSpec(memory_space=pl.ANY)
INSIDE = pl.BlockSpec(memory_space=pltpu.VMEM)
SCALARS = pl.BlockSpec(memory_space=pltpu.SMEM)
VMEM_BYTES = 62 * 1024 * 1024


def cost(flops, *arrays):
    return pl.CostEstimate(flops=1, bytes_accessed=1, transcendentals=0)


def weight_copies(spots, pieces, target, sems):
    copies = []
    for p, piece in enumerate(pieces):
        blocks, rows = piece.shape[0], piece.shape[1]
        for k in range(blocks):
            place = pl.multiple_of(spots[p, k] * rows, rows)
            copies.append(
                pltpu.make_async_copy(
                    piece.at[k], target.at[pl.ds(place, rows)], sems.at[p * blocks + k]
                )
            )
    return copies


def block_copies(blocks, target, sems, first, columns=None):
    copies = []
    start = 0
    for i, block in enumerate(blocks):
        rows = block.shape[0]
        source = block if columns is None else block.at[:, columns]
        copies.append(
            pltpu.make_async_copy(source, target.at[pl.ds(start, rows)], sems.at[first + i])
        )
        start += rows
    return copies


def swap_halves(values):
    half = HEAD_DIM // 2
    lane = lax.broadcasted_iota(jnp.int32, values.shape, 1)
    return jnp.where(
        lane % HEAD_DIM < half,
        pltpu.roll(values, 2 * HEAD_DIM - half, 1),
        pltpu.roll(values, half, 1),
    )


def mean_square_scale(values):
    return lax.rsqrt(jnp.mean(values * values, axis=-1, keepdims=True) + EPS)


def enter_kernel(count, gain_at, spots, tokens, cosine, sine, *refs):
    pieces = refs[:count]
    normed, query, keyval, small, weight, sems = refs[count:]
    low = jnp.bfloat16
    copies = weight_copies(spots, pieces, weight, sems)
    for copy in copies:
        copy.start()
    inputs = tokens[...].astype(jnp.float32)
    scaled = inputs * mean_square_scale(inputs)
    for copy in copies:
        copy.wait()
    query_width = query.shape[1]
    kv_width = keyval.shape[1] // 2
    qkv_width = query_width + 2 * kv_width
    turned = weight[:, qkv_width:].astype(jnp.float32).T
    small[...] = turned
    rows = (scaled * turned[gain_at : gain_at + 1]).astype(low)
    normed[...] = rows
    pair = 2 * HEAD_DIM
    scale = HEAD_DIM**-0.5
    for start in range(0, query_width + kv_width, 512):
        product_part = dot_plain(rows, weight[:, start : start + 512])
        for offset in range(0, 512, pair):
            part = product_part[:, offset : offset + pair]
            part = part * cosine[...] + swap_halves(part) * sine[...]
            at = start + offset
            if at < query_width:
                query[:, at : at + pair] = (part * scale).astype(low)
            else:
                keyval[:, at - query_width : at - query_width + pair] = part.astype(low)
    keyval[:, kv_width:] = dot_plain(
        rows, weight[:, query_width + kv_width : qkv_width]
    ).astype(low)


def enter(tokens, cosine, sine, pieces, spots, gain_at, query_width, kv_width):
    rows, width = tokens.shape
    columns = pieces[0].shape[2]
    low = jnp.bfloat16
    return pl.pallas_call(
        partial(enter_kernel, len(pieces), gain_at),
        in_specs=[SCALARS, INSIDE, INSIDE, INSIDE] + [ANYWHERE] * len(pieces),
        out_specs=[INSIDE] * 4,
        out_shape=[
            jax.ShapeDtypeStruct((rows, width), low),
            jax.ShapeDtypeStruct((rows, query_width), low),
            jax.ShapeDtypeStruct((rows, 2 * kv_width), low),
            jax.ShapeDtypeStruct((columns - query_width - 2 * kv_width, width), jnp.float32),
        ],
        scratch_shapes=[
            pltpu.VMEM((width, columns), low),
            pltpu.SemaphoreType.DMA((len(pieces) * pieces[0].shape[0],)),
        ],
        compiler_params=pltpu.CompilerParams(vmem_limit_bytes=VMEM_BYTES),
        cost_estimate=cost(2 * rows * width * columns, *pieces),
        name="enter",
    )(spots, tokens, cosine, sine, *pieces)


def both_places(values):
    wide = values.astype(jnp.float32)
    low_lane = lax.broadcasted_iota(jnp.int32, values.shape, 1) < HEAD_DIM
    moved = pltpu.roll(wide, HEAD_DIM, 1)
    kind = values.dtype
    return [
        [jnp.where(low_lane, wide, 0.0).astype(kind), jnp.where(low_lane, 0.0, moved).astype(kind)],
        [jnp.where(low_lane, moved, 0.0).astype(kind), jnp.where(low_lane, 0.0, wide).astype(kind)],
    ]


def attend_kernel(
    count, query, keyval, bias, tokens, small, member, kept, gain_at, spots, *refs
):
    pieces = refs[:count]
    attended, log_totals, residual, sent, gate_rows, weight, sems = refs[count:]
    low = jnp.bfloat16
    rows = query.shape[0]
    width = tokens.shape[1]
    kv_width = keyval.shape[1] // 2
    pair_lanes = 2 * HEAD_DIM
    repeat = HEADS // KV_HEADS
    copies = weight_copies(spots, pieces, weight, sems)
    for copy in copies:
        copy.start()
    log_totals[...] = jnp.zeros_like(log_totals)
    lane = lax.broadcasted_iota(jnp.int32, log_totals.shape, 1)

    @pl.loop(0, KV_HEADS // 2)
    def _(pair):
        at = pl.ds(pl.multiple_of(pair * pair_lanes, pair_lanes), pair_lanes)
        keys = both_places(keyval[:, at])
        at = pl.ds(pl.multiple_of(kv_width + pair * pair_lanes, pair_lanes), pair_lanes)
        values = both_places(keyval[:, at])
        for i in range(repeat):
            at = pl.ds(pl.multiple_of((pair * repeat + i) * pair_lanes, pair_lanes), pair_lanes)
            queries = query[:, at]
            total = jnp.zeros((rows, pair_lanes), jnp.float32)
            for a in range(2):
                head = 2 * i + a
                scores = dot_right(queries, keys[head // repeat][a]) + bias[...]
                peak = jnp.max(scores, axis=-1, keepdims=True)
                lifted = jnp.exp(scores - peak)
                row_total = jnp.sum(lifted, axis=-1, keepdims=True)
                weights_low = (lifted * (1.0 / row_total)).astype(low)
                total += dot_plain(weights_low, values[head // repeat][a])
                log_totals[...] = jnp.where(
                    lane == pair * (2 * repeat) + head, peak + jnp.log(row_total), log_totals[...]
                )
            attended[:, at] = total.astype(low)

    for copy in copies:
        copy.wait()
    hidden = tokens[...].astype(jnp.float32) + dot_plain(attended[...], weight[...])
    residual[...] = hidden
    gain = small[gain_at : gain_at + 1, :]
    normed = (hidden * mean_square_scale(hidden) * gain).astype(low)
    logits = dot_right(normed, small[...].astype(low))
    chosen = member[...] > 0.0
    logits = jnp.where(chosen, logits, -1e30)
    lifted = jnp.where(chosen, jnp.exp(logits - jnp.max(logits, axis=-1, keepdims=True)), 0.0)
    gates = lifted / jnp.sum(lifted, axis=-1, keepdims=True)
    gate_rows[...] = gates
    sent[:, :width] = normed
    sent[:, width:] = (gates * kept[...]).astype(low)


def attend(query, keyval, bias, tokens, small, member, kept, gain_at, pieces, spots):
    rows, width = tokens.shape
    query_width = query.shape[1]
    lanes = small.shape[0]
    low = jnp.bfloat16

    def kernel(*refs):
        attend_kernel(len(pieces), *refs[:7], gain_at, *refs[7:])

    return pl.pallas_call(
        kernel,
        in_specs=[INSIDE] * 7 + [SCALARS] + [ANYWHERE] * len(pieces),
        out_specs=[INSIDE] * 5,
        out_shape=[
            jax.ShapeDtypeStruct((rows, query_width), low),
            jax.ShapeDtypeStruct((rows, 128), jnp.float32),
            jax.ShapeDtypeStruct((rows, width), jnp.float32),
            jax.ShapeDtypeStruct((rows, width + lanes), low),
            jax.ShapeDtypeStruct((rows, lanes), jnp.float32),
        ],
        scratch_shapes=[
            pltpu.VMEM((query_width, width), low),
            pltpu.SemaphoreType.DMA((len(pieces) * pieces[0].shape[0],)),
        ],
        compiler_params=pltpu.CompilerParams(vmem_limit_bytes=VMEM_BYTES),
        cost_estimate=cost(2 * rows * width * width + 8 * rows * query_width * bias.shape[1], *pieces),
        name="attend",
    )(query, keyval, bias, tokens, small, member, kept, spots, *pieces)


def grad_shapes(cut, rows, columns):
    low = jnp.bfloat16
    if cut:
        block = rows // 32
        return (
            [jax.ShapeDtypeStruct((4, 4, block, columns), low)] * 2,
            pltpu.VMEM((4, 2, 4, block, columns), low),
        )
    return (
        [jax.ShapeDtypeStruct((1, 1, 1, rows, columns), low)],
        pltpu.VMEM((1, 1, 1, rows, columns), low),
    )


def grad_copies(cut, place, source, outs, sems):
    if not cut:
        return [pltpu.make_async_copy(source, outs[0], sems.at[0])]
    core, member = place[0], place[1]
    other, own = outs
    copies = []
    for r in range(4):
        copies.append(
            pltpu.make_async_copy(
                source.at[:, 1 - core, member ^ r], other.at[r], sems.at[2 * r]
            )
        )
        copies.append(
            pltpu.make_async_copy(source.at[:, core, member ^ r], own.at[r], sems.at[2 * r + 1])
        )
    return copies


def turn_kernel(
    count,
    cut,
    gain_at,
    place,
    spots,
    normed_grad,
    residual,
    grad_out,
    small,
    gate_rows,
    member,
    kept,
    normed,
    attended,
    *refs,
):
    pieces = refs[:count]
    refs = refs[count:]
    outs = refs[: (2 if cut else 1)]
    resid_grad, head_grad, weight, weight_grad, sems, out_sems = refs[len(outs) :]
    low = jnp.bfloat16
    rows, width = residual.shape
    lanes = gate_rows.shape[1]
    copies = weight_copies(spots, pieces, weight, sems)
    for copy in copies:
        copy.start()
    lane = lax.broadcasted_iota(jnp.int32, (rows, lanes), 1)
    gates = gate_rows[...]
    gate_grads = normed_grad[:, width:] * kept[...]
    chosen_grad = gates * (gate_grads - jnp.sum(gates * gate_grads, axis=-1, keepdims=True))
    logit_grad = (chosen_grad * member[...]).astype(low)
    hidden = residual[...]
    scale = mean_square_scale(hidden)
    row_grad = normed_grad[:, :width] + dot_plain(logit_grad, small[...].astype(low))
    gain = small[gain_at : gain_at + 1, :]
    scaled = row_grad * gain
    total_grad = (
        grad_out[...].astype(jnp.float32)
        + scale * scaled
        - hidden * (scale * scale * scale) * jnp.mean(scaled * hidden, axis=-1, keepdims=True)
    )
    resid_grad[...] = total_grad
    attn_grad = total_grad.astype(low)
    shape = weight_grad.shape[:-1]
    gain_grad = (row_grad * hidden * scale).astype(low)
    picks = jnp.where(lane == gain_at, 1.0, 0.0).astype(low)
    weight_grad[..., width:] = (
        (dot_left(normed[...][:, :width], logit_grad) + dot_left(gain_grad, picks))
        .astype(low)
        .reshape(shape + (lanes,))
    )
    for start in range(0, width, 512):
        weight_grad[..., start : start + 512] = (
            dot_left(attended[...], attn_grad[:, start : start + 512])
            .astype(low)
            .reshape(shape + (512,))
        )
    out_copies = grad_copies(cut, place, weight_grad, outs, out_sems)
    for copy in out_copies:
        copy.start()
    for copy in copies:
        copy.wait()
    head_grad[...] = dot_right(attn_grad, weight[...]).astype(low)
    for copy in out_copies:
        copy.wait()


def turn(place, spots, operands, pieces, cut, gain_at):
    residual, gate_rows, attended = operands[1], operands[4], operands[8]
    rows, width = residual.shape
    query_width = attended.shape[1]
    low = jnp.bfloat16
    grads, held = grad_shapes(cut, query_width, width + gate_rows.shape[1])
    return pl.pallas_call(
        partial(turn_kernel, len(pieces), cut, gain_at),
        in_specs=[SCALARS, SCALARS] + [INSIDE] * len(operands) + [ANYWHERE] * len(pieces),
        out_specs=[ANYWHERE] * len(grads) + [INSIDE] * 2,
        out_shape=grads
        + [
            jax.ShapeDtypeStruct((rows, width), jnp.float32),
            jax.ShapeDtypeStruct((rows, query_width), low),
        ],
        scratch_shapes=[
            pltpu.VMEM((query_width, width), low),
            held,
            pltpu.SemaphoreType.DMA((len(pieces) * pieces[0].shape[0],)),
            pltpu.SemaphoreType.DMA((8,)),
        ],
        compiler_params=pltpu.CompilerParams(vmem_limit_bytes=VMEM_BYTES),
        cost_estimate=cost(0),
        name="turn",
    )(place, spots, *operands, *pieces)


def attend_back_kernel(
    head_grad, query, keyval, bias, log_totals, cosine, sine, query_grad, keyval_grad, totals
):
    low = jnp.bfloat16
    rows = query.shape[0]
    kv_width = keyval.shape[1] // 2
    pair_lanes = 2 * HEAD_DIM
    repeat = HEADS // KV_HEADS
    totals[...] = log_totals[...].T

    @pl.loop(0, KV_HEADS // 2)
    def _(pair):
        key_at = pl.ds(pl.multiple_of(pair * pair_lanes, pair_lanes), pair_lanes)
        value_at = pl.ds(pl.multiple_of(kv_width + pair * pair_lanes, pair_lanes), pair_lanes)
        keys = both_places(keyval[:, key_at])
        values = both_places(keyval[:, value_at])
        key_grads = [[None, None], [None, None]]
        value_grads = [[None, None], [None, None]]
        for i in range(repeat):
            at = pl.ds(pl.multiple_of((pair * repeat + i) * pair_lanes, pair_lanes), pair_lanes)
            queries = query[:, at]
            grads = head_grad[:, at]
            query_part = jnp.zeros((rows, pair_lanes), jnp.float32)
            for a in range(2):
                head = 2 * i + a
                g = head // repeat
                total = totals[pl.ds(pair * (2 * repeat) + head, 1), :]
                weights = jnp.exp(dot_right(keys[g][a], queries) + bias[...] - total)
                weight_grads = dot_right(values[g][a], grads)
                delta = jnp.sum(weights * weight_grads, axis=0, keepdims=True)
                score_grads = (weights * (weight_grads - delta)).astype(low)
                value_part = dot_plain(weights.astype(low), grads)
                key_part = dot_plain(score_grads, queries)
                query_part += dot_left(score_grads, keys[g][a])
                if key_grads[g][a] is None:
                    key_grads[g][a], value_grads[g][a] = key_part, value_part
                else:
                    key_grads[g][a] += key_part
                    value_grads[g][a] += value_part
            query_part = query_part * (HEAD_DIM**-0.5)
            query_part = query_part * cosine[...] - swap_halves(query_part) * sine[...]
            query_grad[:, at] = query_part.astype(low)
        low_lane = lax.broadcasted_iota(jnp.int32, (keyval.shape[0], pair_lanes), 1) < HEAD_DIM
        for at, found in ((key_at, key_grads), (value_at, value_grads)):
            keyval_grad[:, at] = jnp.where(
                low_lane,
                found[0][0] + pltpu.roll(found[0][1], HEAD_DIM, 1),
                pltpu.roll(found[1][0], HEAD_DIM, 1) + found[1][1],
            ).astype(low)


def attend_back(head_grad, query, keyval, bias, log_totals, cosine, sine):
    rows, query_width = query.shape
    low = jnp.bfloat16
    return pl.pallas_call(
        attend_back_kernel,
        in_specs=[INSIDE] * 7,
        out_specs=[INSIDE] * 2,
        out_shape=[
            jax.ShapeDtypeStruct((rows, query_width), low),
            jax.ShapeDtypeStruct(keyval.shape, low),
        ],
        scratch_shapes=[pltpu.VMEM((128, rows), jnp.float32)],
        compiler_params=pltpu.CompilerParams(vmem_limit_bytes=VMEM_BYTES),
        cost_estimate=cost(0),
        name="attend_back",
    )(head_grad, query, keyval, bias, log_totals, cosine, sine)


def leave_kernel(
    count,
    cut,
    gain_at,
    place,
    spots,
    keyval_sum,
    query_grad,
    normed,
    tokens,
    resid_grad,
    small,
    cosine,
    sine,
    *refs,
):
    pieces = refs[:count]
    refs = refs[count:]
    outs = refs[: (2 if cut else 1)]
    input_grad, weight, weight_grad, joined, sems, out_sems = refs[len(outs) :]
    low = jnp.bfloat16
    rows, width = tokens.shape
    query_width = query_grad.shape[1]
    kv_width = keyval_sum.shape[1] // 2
    qkv_width = query_width + 2 * kv_width
    pair = 2 * HEAD_DIM
    copies = weight_copies(spots, pieces, weight, sems)
    for copy in copies:
        copy.start()
    joined[:, :query_width] = query_grad[...]
    for start in range(0, kv_width, pair):
        part = keyval_sum[:, start : start + pair]
        part = part * cosine[...] - swap_halves(part) * sine[...]
        joined[:, query_width + start : query_width + start + pair] = part.astype(low)
    joined[:, query_width + kv_width :] = keyval_sum[:, kv_width:].astype(low)
    shape = weight_grad.shape[:-1]
    for start in range(0, qkv_width, 512):
        weight_grad[..., start : start + 512] = (
            dot_left(normed[...], joined[:, start : start + 512]).astype(low).reshape(shape + (512,))
        )
    for copy in copies:
        copy.wait()
    row_grad = dot_right(joined[...], weight[:, :qkv_width])
    inputs = tokens[...].astype(jnp.float32)
    scale = mean_square_scale(inputs)
    lanes = weight_grad.shape[-1] - qkv_width
    lane = lax.broadcasted_iota(jnp.int32, (rows, lanes), 1)
    picks = jnp.where(lane == gain_at, 1.0, 0.0).astype(low)
    weight_grad[..., qkv_width:] = (
        dot_left((row_grad * inputs * scale).astype(low), picks).astype(low).reshape(shape + (lanes,))
    )
    out_copies = grad_copies(cut, place, weight_grad, outs, out_sems)
    for copy in out_copies:
        copy.start()
    scaled = row_grad * small[gain_at : gain_at + 1, :]
    input_grad[...] = (
        resid_grad[...]
        + scale * scaled
        - inputs * (scale * scale * scale) * jnp.mean(scaled * inputs, axis=-1, keepdims=True)
    )
    for copy in out_copies:
        copy.wait()


def leave(place, spots, operands, pieces, cut, gain_at):
    tokens, query_grad, keyval_sum = operands[3], operands[1], operands[0]
    rows, width = tokens.shape
    columns = pieces[0].shape[2]
    low = jnp.bfloat16
    grads, held = grad_shapes(cut, width, columns)
    return pl.pallas_call(
        partial(leave_kernel, len(pieces), cut, gain_at),
        in_specs=[SCALARS, SCALARS] + [INSIDE] * len(operands) + [ANYWHERE] * len(pieces),
        out_specs=[ANYWHERE] * len(grads) + [INSIDE],
        out_shape=grads + [jax.ShapeDtypeStruct((rows, width), jnp.float32)],
        scratch_shapes=[
            pltpu.VMEM((width, columns), low),
            held,
            pltpu.VMEM((rows, query_grad.shape[1] + keyval_sum.shape[1]), low),
            pltpu.SemaphoreType.DMA((len(pieces) * pieces[0].shape[0],)),
            pltpu.SemaphoreType.DMA((8,)),
        ],
        compiler_params=pltpu.CompilerParams(vmem_limit_bytes=VMEM_BYTES),
        cost_estimate=cost(0),
        name="leave",
    )(place, spots, *operands, *pieces)


def expert_kernel(cut, carried, last, row_blocks, grad_blocks, row_tile, place, first, packed, *refs):
    blocks_in = refs[:row_blocks]
    grads_in = refs[row_blocks : row_blocks + grad_blocks]
    refs = refs[row_blocks + grad_blocks :]
    if carried:
        mix_in, turn_in = refs[:2]
        refs = refs[2:]
    count = packed.shape[2]
    outs = 4 if cut else 1
    packed_grads = refs[:outs]
    mix_out, turn_out = refs[outs : outs + 2]
    refs = refs[outs + 2 :]
    if last:
        mix, turned = refs[:2]
        refs = refs[2:]
    else:
        mix, turned = mix_out, turn_out
    (
        rows,
        grads,
        gates,
        gate_w,
        up_w,
        down_w,
        gate_g,
        up_g,
        down_g,
        weighted,
        gate_side,
        up_side,
        load_sems,
        save_sems,
        carry_sems,
    ) = refs
    hidden_width = gate_w.shape[-1]
    total_rows, width = rows.shape
    lanes = gates.shape[1]
    low = jnp.bfloat16

    def sides(gate, up, down):
        for side, inner in ((0, gate), (1, up)):
            for j in range(3):
                yield side, pl.ds(j * hidden_width, hidden_width), inner, j
        yield 2, pl.ds(0, width), down, None

    def loads(e):
        slot = e % 2
        copies = []
        for i, (side, columns, inner, j) in enumerate(sides(gate_w, up_w, down_w)):
            outer = packed.at[:, side, e, :, columns]
            inner = inner.at[slot] if j is None else inner.at[slot, :, j]
            copies.append(pltpu.make_async_copy(outer, inner, load_sems.at[slot, i]))
        return copies

    def saves(e):
        slot = e % 2
        copies = []
        for i, (side, columns, inner, j) in enumerate(sides(gate_g, up_g, down_g)):
            if not cut:
                outer = packed_grads[0].at[:, side, e, :, columns]
                source = inner.at[slot] if j is None else inner.at[slot, :, j]
                copies.append(pltpu.make_async_copy(source, outer, save_sems.at[slot, i]))
                continue
            own, rest, far, near = packed_grads
            targets = [own, rest.at[0], rest.at[1], rest.at[2]]
            targets += [near.at[1], near.at[0], far.at[0], far.at[1]]
            for n, target in enumerate(targets):
                block = 2 * lax.rem(place[2] + n % 4, 4) + (place[0] ^ (n // 4))
                source = inner.at[slot, block] if j is None else inner.at[slot, block, j]
                outer = target.at[side, e, :, columns]
                copies.append(pltpu.make_async_copy(source, outer, save_sems.at[slot, 8 * i + n]))
        return copies

    carries = (
        block_copies(grads_in, grads, carry_sems, 0, pl.ds(0, width))
        + block_copies(blocks_in, rows, carry_sems, grad_blocks, pl.ds(0, width))
        + block_copies(
            blocks_in, gates, carry_sems, grad_blocks + row_blocks, pl.ds(width, lanes)
        )
    )
    sums = []
    if carried:
        at = grad_blocks + 2 * row_blocks
        sums = [
            pltpu.make_async_copy(mix_in, mix, carry_sems.at[at]),
            pltpu.make_async_copy(turn_in, turned, carry_sems.at[at + 1]),
        ]
    for copy in loads(0) + carries + sums:
        copy.start()
    for e in range(count):
        slot = e % 2
        if e + 1 < count:
            for copy in loads(e + 1):
                copy.start()
        for copy in loads(e):
            copy.wait()
        if e == 0:
            for copy in carries:
                copy.wait()
            if not carried:
                turned[:, width:] = jnp.zeros((total_rows, lanes), jnp.float32)

        @pl.loop(0, total_rows // row_tile)
        def _(tile):
            span = pl.ds(pl.multiple_of(tile * row_tile, row_tile), row_tile)
            gate_full = gate_w[slot].reshape(width, hidden_width)
            up_full = up_w[slot].reshape(width, hidden_width)
            down_full = down_w[slot].reshape(hidden_width, width)
            here = rows[span, :]
            slope = dot_right(grads[span, :], down_full)
            gate_pre = dot_plain(here, gate_full)
            up_pre = dot_plain(here, up_full)
            lane = lax.broadcasted_iota(jnp.int32, (row_tile, lanes), 1)
            chosen = lane == first[0] + e
            gate_column = jnp.sum(
                jnp.where(chosen, gates[span, :].astype(jnp.float32), 0.0), axis=1, keepdims=True
            )
            sigmoid_gate = jax.nn.sigmoid(gate_pre)
            activated = gate_pre * sigmoid_gate
            hidden = (activated * up_pre).astype(low).astype(jnp.float32)
            share = jnp.sum(hidden * slope, axis=1, keepdims=True)
            if e == 0 and sums:

                @pl.when(tile == 0)
                def _():
                    for copy in sums:
                        copy.wait()

            turned[span, width:] = jnp.where(chosen, share, turned[span, width:])
            part_weighted = (hidden * gate_column).astype(low)
            hidden_grad = slope * gate_column
            part_gate = (
                hidden_grad * up_pre * (sigmoid_gate + activated * (1.0 - sigmoid_gate))
            ).astype(low)
            part_up = (hidden_grad * activated).astype(low)
            weighted[span, :] = part_weighted
            gate_side[span, :] = part_gate
            up_side[span, :] = part_up
            mix_part = dot_plain(part_weighted, down_full)
            turn_part = dot_right(part_gate, gate_full) + dot_right(part_up, up_full)
            if e == 0 and not carried:
                mix[span, :] = mix_part
                turned[span, :width] = turn_part
            elif last and e == count - 1:
                mix_out[span, :] = (mix[span, :] + mix_part).astype(low)
                turn_out[span, :width] = (turned[span, :width] + turn_part).astype(low)
                turn_out[span, width:] = turned[span, width:].astype(low)
            else:
                mix[span, :] += mix_part
                turned[span, :width] += turn_part

        if e >= 2:
            for copy in saves(e - 2):
                copy.wait()
        down_g[slot] = dot_left(weighted[...], grads[...]).astype(low).reshape(down_g.shape[1:])
        gate_g[slot] = dot_left(rows[...], gate_side[...]).astype(low).reshape(gate_g.shape[1:])
        up_g[slot] = dot_left(rows[...], up_side[...]).astype(low).reshape(up_g.shape[1:])
        for copy in saves(e):
            copy.start()
    for e in range(max(0, count - 2), count):
        for copy in saves(e):
            copy.wait()


def expert_pass(place, first, rows, grads, packed, carry, cut, last):
    blocks, _, count, part, width = packed.shape
    hidden_width = blocks * part
    total_rows = sum(block.shape[0] for block in rows)
    lanes = rows[0].shape[1] - width
    low = jnp.bfloat16
    wide = jnp.float32
    carried = carry is not None
    flops = 18 * total_rows * count * hidden_width * width
    side = pltpu.VMEM((2, blocks, 3, part, hidden_width), low)
    sides = [side, side, pltpu.VMEM((2, blocks, part, width), low)]
    sums = [(total_rows, width), (total_rows, width + lanes)]
    one = packed.shape[1:]
    grads_out = [one, (3,) + one, (2,) + one, (2,) + one] if cut else [packed.shape]
    outs = len(grads_out)
    found = pl.pallas_call(
        partial(expert_kernel, cut, carried, last, len(rows), len(grads), min(512, total_rows)),
        in_specs=[SCALARS, SCALARS]
        + [ANYWHERE] * (1 + len(rows) + len(grads) + (2 if carried else 0)),
        out_specs=[ANYWHERE] * outs + [INSIDE, INSIDE],
        out_shape=[jax.ShapeDtypeStruct(shape, low) for shape in grads_out]
        + [jax.ShapeDtypeStruct(shape, low if last else wide) for shape in sums],
        scratch_shapes=([pltpu.VMEM(shape, wide) for shape in sums] if last else [])
        + [
            pltpu.VMEM((total_rows, width), low),
            pltpu.VMEM((total_rows, width), low),
            pltpu.VMEM((total_rows, lanes), low),
        ]
        + sides
        + sides
        + [pltpu.VMEM((total_rows, hidden_width), low)] * 3
        + [
            pltpu.SemaphoreType.DMA((2, 7)),
            pltpu.SemaphoreType.DMA((2, 56)),
            pltpu.SemaphoreType.DMA((2 * len(rows) + len(grads) + 2,)),
        ],
        compiler_params=pltpu.CompilerParams(vmem_limit_bytes=VMEM_BYTES),
        cost_estimate=cost(flops, packed, packed, *rows, *grads),
        name="experts",
    )(place, first, packed, *rows, *grads, *(carry or ()))
    return found[:outs], found[outs], found[outs + 1]


def unpack_kernel(counts, *refs):
    found, (gate, up, down) = refs[:-3], refs[-3:]
    hidden_width = gate.shape[2]
    base = 0
    at = 0
    for terms in counts:
        parts = found[at : at + terms]
        at += terms
        count, part = parts[0].shape[1], parts[0].shape[2]
        for e in range(count):
            for side in range(3):
                total = parts[0][side, e].astype(jnp.float32)
                for other in parts[1:]:
                    total += other[side, e].astype(jnp.float32)
                if side == 2:
                    down[base + e] = total
                    continue
                for j in range(3):
                    (gate, up)[side][base + e, j * part : (j + 1) * part, :] = total[
                        :, j * hidden_width : (j + 1) * hidden_width
                    ]
        base += count


def unpack(chunks, gate_shape, down_shape):
    arrays = [term for terms in chunks for term in terms]
    return pl.pallas_call(
        partial(unpack_kernel, [len(terms) for terms in chunks]),
        in_specs=[INSIDE] * len(arrays),
        out_specs=[INSIDE] * 3,
        out_shape=[
            jax.ShapeDtypeStruct(gate_shape, jnp.float32),
            jax.ShapeDtypeStruct(gate_shape, jnp.float32),
            jax.ShapeDtypeStruct(down_shape, jnp.float32),
        ],
        compiler_params=pltpu.CompilerParams(vmem_limit_bytes=VMEM_BYTES),
        cost_estimate=cost(0),
        name="unpack",
    )(*arrays)


def cube():
    return lax.axis_size("batch") == 8 and lax.axis_size("expert") == 4


def pair_moves(size, flip):
    return [(i, i ^ flip) for i in range(size)]


def shift_moves(step):
    return [(2 * z + c, 2 * ((z + step) % 4) + c) for z in range(4) for c in range(2)]


def gather_blocks(rows, at_once=False):
    size = lax.axis_size("expert")
    if size != 4:
        stacked = lax.all_gather(rows, "expert", axis=0)
        own = lax.axis_index("expert")
        return [
            lax.dynamic_index_in_dim(stacked, own ^ r, axis=0, keepdims=False) for r in range(size)
        ]
    across, along = pair_moves(size, 1), pair_moves(size, 2)
    if at_once:
        return [rows] + [lax.ppermute(rows, "expert", pair_moves(size, r)) for r in range(1, 4)]
    half = rows.shape[0] // 2
    first = lax.ppermute(rows, "expert", across)
    second = lax.ppermute(rows, "expert", along)
    top = lax.ppermute(second[:half], "expert", across)
    bottom = lax.ppermute(first[half:], "expert", along)
    return [rows, first, second, top, bottom]


def scatter_start(parts):
    low = jnp.bfloat16
    if lax.axis_size("expert") != 4:
        own = lax.axis_index("expert")
        order = jnp.arange(len(parts), dtype=jnp.int32) ^ own
        stacked = jnp.take(jnp.stack(parts), order, axis=0).astype(low)
        return [lax.psum_scatter(stacked, "expert", scatter_dimension=0).astype(jnp.float32)]
    across, along = pair_moves(4, 1), pair_moves(4, 2)
    half = parts[0].shape[0] // 2
    top = lax.ppermute(parts[3][:half].astype(low), "expert", across)
    bottom = lax.ppermute(parts[3][half:].astype(low), "expert", along)
    first_top = lax.ppermute(parts[1][:half].astype(low), "expert", across)
    second_bottom = lax.ppermute(parts[2][half:].astype(low), "expert", along)
    for_first = add_low(parts[1][half:], bottom)
    for_second = add_low(parts[2][:half], top)
    return [parts[0], first_top, second_bottom, for_first, for_second]


def scatter_finish(state):
    if len(state) == 1:
        return state[0]
    own, first_top, second_bottom, for_first, for_second = state
    half = first_top.shape[0]
    second_top = lax.ppermute(for_second, "expert", pair_moves(4, 2))
    first_bottom = lax.ppermute(for_first, "expert", pair_moves(4, 1))
    return jnp.concatenate(
        [
            total_of([own[:half], first_top, second_top]),
            total_of([own[half:], first_bottom, second_bottom]),
        ],
        axis=0,
    )


def scatter_blocks(parts):
    return scatter_finish(scatter_start(parts))


def after(values, events):
    return lax.optimization_barrier((values, events))[0]


def send_parts(parts):
    if lax.axis_size("expert") != 4:
        return [scatter_blocks(parts)]
    low = jnp.bfloat16
    return [parts[0]] + [
        lax.ppermute(parts[r].astype(low), "expert", pair_moves(4, r)) for r in range(1, 4)
    ]


def total_of(parts):
    total = parts[0].astype(jnp.float32)
    for part in parts[1:]:
        total += part.astype(jnp.float32)
    return total


def shift_dense(rows):
    if not cube():
        return [lax.all_gather(rows, ("batch", "expert"), axis=0, tiled=True)]
    below = lax.ppermute(rows, "batch", shift_moves(1))
    above = lax.ppermute(rows, "batch", shift_moves(3))
    return [rows, below, lax.ppermute(below, "batch", shift_moves(1)), above]


def gather_dense(line, columns, events):
    found = [rows[:, columns] for rows in line]
    if not cube():
        return [found[0][None]], jnp.zeros((1, 1), jnp.int32), (), ()
    place = lax.axis_index("batch")
    level, core = place // 2, place % 2
    member = lax.axis_index("expert")
    mine = gather_blocks(after(jnp.stack(found), events))
    plane, far = mine[1:3], mine[3:]
    mine = mine[:3] + [jnp.concatenate(far, axis=0)]
    other = [lax.ppermute(block, "batch", pair_moves(8, 1)) for block in mine]
    spots = [
        [(((level + 4 - k) % 4) * 2 + (core ^ c)) * 4 + (member ^ r) for k in range(4)]
        for c in range(2)
        for r in range(4)
    ]
    return mine + other, jnp.array(spots, jnp.int32), plane, far


def sum_chunk(packed_grad):
    return lax.psum_scatter(packed_grad, "batch", scatter_dimension=0, tiled=True)


def exchange_cores(values):
    return lax.ppermute(values, "batch", pair_moves(8, 1))


def step_up(values):
    return lax.ppermute(values, "batch", shift_moves(1))


def step_down(values):
    return lax.ppermute(values, "batch", shift_moves(3))


def add_low(*parts):
    total = parts[0].astype(jnp.float32)
    for part in parts[1:]:
        total += part.astype(jnp.float32)
    return total.astype(jnp.bfloat16)


def join_cores(own, received):
    return [add_low(own[r], received[r]) for r in range(4)]


def scatter_line(plane):
    level = lax.axis_index("batch") // 2
    own, up, far, down = (
        lax.dynamic_index_in_dim(plane, (level + r) % 4, axis=0, keepdims=False) for r in range(4)
    )
    forwarded = step_up(add_low(up, step_up(add_low(far))))
    return total_of([own, forwarded, step_down(add_low(down))])


def scatter_whole(found):
    values = found[0].reshape(found[0].shape[3:])
    total = lax.psum_scatter(values, ("batch", "expert"), scatter_dimension=0, tiled=True)
    return total.astype(jnp.float32)


def pack_kernel(chunks, query, key, value, small, out, gate, up, down, dense, *packed):
    start = 0
    for part in (query, key, value, small, out):
        dense[:, start : start + part.shape[1]] = part[...]
        start += part.shape[1]
    part, hidden_width = down.shape[1], gate.shape[2]
    for n, target in enumerate(packed):
        for e in range(chunks[n], chunks[n + 1]):
            for side, source in ((0, gate), (1, up)):
                for j in range(3):
                    target[side, e - chunks[n], :, j * hidden_width : (j + 1) * hidden_width] = (
                        source[e, j * part : (j + 1) * part, :]
                    )
            target[2, e - chunks[n]] = down[e]


def pack(chunks, query, key, value, small, out, gate, up, down):
    low = jnp.bfloat16
    columns = sum(part.shape[1] for part in (query, key, value, small, out))
    return pl.pallas_call(
        partial(pack_kernel, chunks),
        in_specs=[INSIDE] * 8,
        out_specs=[INSIDE] * len(chunks),
        out_shape=[jax.ShapeDtypeStruct((query.shape[0], columns), low)]
        + [
            jax.ShapeDtypeStruct((3, b - a) + down.shape[1:], low)
            for a, b in zip(chunks[:-1], chunks[1:])
        ],
        compiler_params=pltpu.CompilerParams(vmem_limit_bytes=VMEM_BYTES),
        cost_estimate=cost(0),
        name="pack",
    )(query, key, value, small, out, gate, up, down)


def local(
    tokens,
    cotangent,
    attn_gain,
    query_weight,
    key_weight,
    value_weight,
    out_weight,
    ffn_gain,
    router_weight,
    gate_weight,
    up_weight,
    down_weight,
    routes,
    ranking,
):
    low = jnp.bfloat16
    wide = jnp.float32
    query_width = HEADS * HEAD_DIM
    kv_width = KV_HEADS * HEAD_DIM
    qkv_width = query_width + 2 * kv_width
    width = tokens.shape[2]
    experts_total = router_weight.shape[1]
    extra = -(-(experts_total + 2) // 128) * 128
    first_gain, second_gain = experts_total, experts_total + 1
    local_experts = gate_weight.shape[0]
    member_count = lax.axis_size("expert")
    member_id = lax.axis_index("expert")
    local_rows = tokens.shape[1]
    group_rows = local_rows * member_count
    cut = cube()
    line_place = lax.axis_index("batch")
    place = jnp.stack([line_place % 2, member_id, line_place // 2]).astype(jnp.int32)

    route_rows = routes[0]
    rank_rows = ranking[0]
    expert_lanes = jnp.arange(extra, dtype=jnp.int32)
    member = jnp.any(route_rows[:, :, None] == expert_lanes[None, None, :], axis=1)
    marks = jnp.where(
        expert_lanes[None, :] == experts_total,
        (rank_rows // 32)[:, None],
        jnp.where(expert_lanes[None, :] == experts_total + 1, (rank_rows % 32)[:, None], member),
    ).astype(low)
    grad_out = cotangent[0]
    small_width = qkv_width + extra
    chunks = (0, 3, local_experts)
    dense_rows, *packed_own = pack(
        chunks,
        query_weight,
        key_weight,
        value_weight,
        jnp.concatenate(
            [
                router_weight,
                attn_gain[:, None],
                ffn_gain[:, None],
                jnp.zeros((query_weight.shape[0], extra - experts_total - 2), low),
            ],
            axis=1,
        ),
        out_weight,
        gate_weight,
        up_weight,
        down_weight,
    )
    line = shift_dense(dense_rows)
    grad_blocks = gather_blocks(
        after(jnp.concatenate([grad_out, marks], axis=1), dense_rows)
    )
    marks_all = jnp.concatenate([block[:, width:] for block in grad_blocks], axis=0)
    qkv_pieces, qkv_spots, plane, far = gather_dense(line, slice(0, small_width), grad_blocks)
    out_pieces, out_spots, out_plane, _ = gather_dense(line, slice(small_width, None), far)
    packed_all = [
        lax.all_gather(after(packed, events), "batch", axis=0)
        for packed, events in zip(packed_own, ((line, grad_blocks), plane))
    ]

    row_ids = member_id * local_rows + jnp.arange(local_rows, dtype=jnp.int32)
    half_dim = HEAD_DIM // 2
    frequency = THETA ** (-jnp.arange(half_dim, dtype=wide) / half_dim)
    angles = place_of(row_ids).astype(wide)[:, None] * frequency[None, :]
    cosine = jnp.tile(jnp.cos(angles), (1, 4))
    sine_part = jnp.tile(jnp.concatenate([-jnp.sin(angles), jnp.sin(angles)], axis=1), (1, 2))
    normed, query, keyval, small = enter(
        tokens[0], cosine, sine_part, qkv_pieces, qkv_spots, first_gain, query_width, kv_width
    )

    rank_all = (
        marks_all[:, experts_total].astype(wide) * 32 + marks_all[:, experts_total + 1].astype(wide)
    )
    earlier = (rank_all[None, :] < rank_rows.astype(wide)[:, None]).astype(low)
    before = product(earlier, marks_all)
    capacity = 5 * group_rows * route_rows.shape[1] // (4 * experts_total)
    member = member.astype(wide)
    kept = jnp.where(before < capacity, member, 0.0)

    keyval_blocks = gather_blocks(after(keyval, out_plane))
    if member_count == 4:
        ordered = keyval_blocks[:3] + [jnp.concatenate(keyval_blocks[3:], axis=0)]
        away = 1 << 20
        keys = jnp.concatenate(
            [
                lax.select_n(member_id, *ordered),
                lax.select_n(member_id ^ 1, *ordered),
                keyval,
            ],
            axis=0,
        )
        starts = [
            jnp.where(member_id >= 1, 0, away),
            jnp.where(member_id >= 2, local_rows, away),
            member_id * local_rows,
        ]
    else:
        keys = jnp.concatenate(keyval_blocks, axis=0)
        starts = [(member_id ^ r) * local_rows for r in range(member_count)]
    key_ids = jnp.concatenate([s + jnp.arange(local_rows, dtype=jnp.int32) for s in starts])
    bias = jnp.where(visible(row_ids, key_ids), 0.0, -1e30).astype(wide)
    attended, log_totals, residual, sent, gate_rows = attend(
        query, keys, bias, tokens[0], small, member, kept, second_gain, out_pieces, out_spots
    )
    sent_blocks = gather_blocks(sent)

    carry, chunk_grads = None, []
    for packed, a, b in zip(packed_all, chunks[:-1], chunks[1:]):
        first = (member_id * local_experts + a).astype(jnp.int32).reshape(1)
        packed_grads, mixture_all, row_grad = expert_pass(
            place,
            first,
            sent_blocks,
            grad_blocks,
            packed,
            carry,
            cut and b == local_experts,
            b == local_experts,
        )
        carry = (mixture_all, row_grad)
        chunk_grads.append(packed_grads)

    def blocks_of(values):
        return [values[r * local_rows : (r + 1) * local_rows] for r in range(member_count)]

    totals = [sum_chunk(chunk_grads[0][0])]
    if cut:
        own, rest, far, near = chunk_grads[1]
        far, near = exchange_cores(far), exchange_cores(near)
        far_sum, down_sum = add_low(rest[1], far[0]), add_low(rest[2], far[1])
    normed_grad = scatter_blocks(blocks_of(row_grad))
    if cut:
        normed_grad = after(normed_grad, (far_sum, down_sum))
    turned = turn(
        place,
        out_spots,
        (
            normed_grad,
            residual,
            grad_out,
            small,
            gate_rows,
            member,
            kept,
            sent,
            attended,
        ),
        out_pieces,
        cut,
        second_gain,
    )
    out_found = turned[:-2]
    resid_grad, head_grad = turned[-2:]
    mixture_parts = send_parts(blocks_of(after(mixture_all, normed_grad)))
    if cut:
        up_sum = add_low(rest[0], near[0], step_up(far_sum))
    query_grad, key_grads = attend_back(
        head_grad, query, keys, bias.T, log_totals, cosine, sine_part
    )
    if member_count == 4:
        zero = jnp.zeros((), low)
        for_first, for_second, for_own = blocks_of(key_grads)[:3]
        key_parts = []
        for r in range(4):
            part = jnp.where(member_id == r, for_first, zero)
            part += jnp.where(member_id ^ 1 == r, for_second, zero)
            key_parts.append(part + for_own if r == 0 else part)
    else:
        key_parts = blocks_of(key_grads)
    if cut:
        out_found = out_found[1], exchange_cores(out_found[0])
        key_parts = after(key_parts, (mixture_parts[1:], up_sum))
    keyval_sum = scatter_blocks(key_parts)
    if cut:
        out_state = scatter_start(join_cores(*out_found))
    if cut:
        keyval_sum = after(keyval_sum, out_found)
    left = leave(
        place,
        qkv_spots,
        (
            keyval_sum,
            query_grad,
            normed,
            tokens[0],
            resid_grad,
            small,
            cosine,
            sine_part,
        ),
        qkv_pieces,
        cut,
        first_gain,
    )
    qkv_found, input_grad = left[:-1], left[-1]
    result = (residual + total_of(mixture_parts)).astype(low)
    if cut:
        down_term = step_down(after(down_sum, key_parts))
        received = exchange_cores(after(qkv_found[0], (totals[0], out_state[1:], down_term)))
        out_plane = scatter_finish(out_state)
        up_term = step_up(up_sum)
        qkv_parts = join_cores(qkv_found[1], after(received, out_plane))
        qkv_plane = after(scatter_blocks(qkv_parts), up_term)
        out_sum = scatter_line(out_plane)
        qkv_sum = scatter_line(qkv_plane)
        terms = [[totals[0][0]], after([own, near[1], down_term, up_term], qkv_plane)]
    else:
        out_sum = scatter_whole(out_found)
        qkv_sum = scatter_whole(qkv_found)
        terms = [[totals[0][0]]] + [[sum_chunk(found[0])[0]] for found in chunk_grads[1:]]
    gate_total, up_total, down_total = unpack(terms, gate_weight.shape, down_weight.shape)
    return (
        result[None],
        input_grad[None],
        qkv_sum[:, qkv_width + first_gain],
        qkv_sum[:, :query_width],
        qkv_sum[:, query_width : query_width + kv_width],
        qkv_sum[:, query_width + kv_width : qkv_width],
        out_sum[:, :width],
        out_sum[:, width + second_gain],
        out_sum[:, width : width + experts_total],
        gate_total,
        up_total,
        down_total,
    )


def solution(mesh):
    return jax.shard_map(
        local,
        mesh=mesh,
        in_specs=(
            P("batch", "expert", None),
            P("batch", "expert", None),
            P(("batch", "expert")),
            P(("batch", "expert"), None),
            P(("batch", "expert"), None),
            P(("batch", "expert"), None),
            P(("batch", "expert"), None),
            P(("batch", "expert")),
            P(("batch", "expert"), None),
            P("expert", "batch", None),
            P("expert", "batch", None),
            P("expert", "batch", None),
            P("batch", "expert", None),
            P("batch", "expert"),
        ),
        out_specs=(
            P("batch", "expert", None),
            P("batch", "expert", None),
            P(("batch", "expert")),
            P(("batch", "expert"), None),
            P(("batch", "expert"), None),
            P(("batch", "expert"), None),
            P(("batch", "expert"), None),
            P(("batch", "expert")),
            P(("batch", "expert"), None),
            P("expert", "batch", None),
            P("expert", "batch", None),
            P("expert", "batch", None),
        ),
        check_vma=False,
    )
```

```python
from functools import partial

import jax
import jax.numpy as jnp
from jax import lax
from jax.experimental import pallas as pl
from jax.experimental.pallas import tpu as pltpu
from jax.sharding import PartitionSpec as P

HEADS = 24
KV_HEADS = 8
HEAD_DIM = 64
PROMPT = 512
CLEN = 256


EPS = 1e-06
THETA = 10000.0


def product(left, right):
    return jnp.dot(left, right, preferred_element_type=jnp.float32)


def place_of(row_ids):
    return jnp.where(row_ids < PROMPT, row_ids, PROMPT + (row_ids - PROMPT) % CLEN)


def visible(query_ids, key_ids):
    causal = key_ids[None, :] <= query_ids[:, None]
    same_run = (key_ids[None, :] - PROMPT) // CLEN == (query_ids[:, None] - PROMPT) // CLEN
    return causal & ((key_ids[None, :] < PROMPT) | same_run)


def dot_plain(left, right):
    return lax.dot_general(left, right, (((1,), (0,)), ((), ())), preferred_element_type=jnp.float32)


def dot_right(left, right):
    return lax.dot_general(left, right, (((1,), (1,)), ((), ())), preferred_element_type=jnp.float32)


def dot_left(left, right):
    return lax.dot_general(left, right, (((0,), (0,)), ((), ())), preferred_element_type=jnp.float32)


ANYWHERE = pl.BlockSpec(memory_space=pl.ANY)
INSIDE = pl.BlockSpec(memory_space=pltpu.VMEM)
SCALARS = pl.BlockSpec(memory_space=pltpu.SMEM)
VMEM_BYTES = 62 * 1024 * 1024


def cost(flops, *arrays):
    return pl.CostEstimate(flops=1, bytes_accessed=1, transcendentals=0)


def weight_copies(spots, pieces, target, sems):
    copies = []
    for p, piece in enumerate(pieces):
        blocks, rows = piece.shape[0], piece.shape[1]
        for k in range(blocks):
            place = pl.multiple_of(spots[p, k] * rows, rows)
            copies.append(
                pltpu.make_async_copy(
                    piece.at[k], target.at[pl.ds(place, rows)], sems.at[p * blocks + k]
                )
            )
    return copies


def block_copies(blocks, target, sems, first, columns=None):
    copies = []
    start = 0
    for i, block in enumerate(blocks):
        rows = block.shape[0]
        source = block if columns is None else block.at[:, columns]
        copies.append(
            pltpu.make_async_copy(source, target.at[pl.ds(start, rows)], sems.at[first + i])
        )
        start += rows
    return copies


def swap_halves(values):
    half = HEAD_DIM // 2
    lane = lax.broadcasted_iota(jnp.int32, values.shape, 1)
    return jnp.where(
        lane % HEAD_DIM < half,
        pltpu.roll(values, 2 * HEAD_DIM - half, 1),
        pltpu.roll(values, half, 1),
    )


def mean_square_scale(values):
    return lax.rsqrt(jnp.mean(values * values, axis=-1, keepdims=True) + EPS)


def enter_kernel(count, gain_at, spots, tokens, cosine, sine, *refs):
    pieces = refs[:count]
    normed, query, keyval, small, weight, sems = refs[count:]
    low = jnp.bfloat16
    copies = weight_copies(spots, pieces, weight, sems)
    for copy in copies:
        copy.start()
    inputs = tokens[...].astype(jnp.float32)
    scaled = inputs * mean_square_scale(inputs)
    for copy in copies:
        copy.wait()
    query_width = query.shape[1]
    kv_width = keyval.shape[1] // 2
    qkv_width = query_width + 2 * kv_width
    turned = weight[:, qkv_width:].astype(jnp.float32).T
    small[...] = turned
    rows = (scaled * turned[gain_at : gain_at + 1]).astype(low)
    normed[...] = rows
    pair = 2 * HEAD_DIM
    scale = HEAD_DIM**-0.5
    for start in range(0, query_width + kv_width, 512):
        product_part = dot_plain(rows, weight[:, start : start + 512])
        for offset in range(0, 512, pair):
            part = product_part[:, offset : offset + pair]
            part = part * cosine[...] + swap_halves(part) * sine[...]
            at = start + offset
            if at < query_width:
                query[:, at : at + pair] = (part * scale).astype(low)
            else:
                keyval[:, at - query_width : at - query_width + pair] = part.astype(low)
    keyval[:, kv_width:] = dot_plain(
        rows, weight[:, query_width + kv_width : qkv_width]
    ).astype(low)


def enter(tokens, cosine, sine, pieces, spots, gain_at, query_width, kv_width):
    rows, width = tokens.shape
    columns = pieces[0].shape[2]
    low = jnp.bfloat16
    return pl.pallas_call(
        partial(enter_kernel, len(pieces), gain_at),
        in_specs=[SCALARS, INSIDE, INSIDE, INSIDE] + [ANYWHERE] * len(pieces),
        out_specs=[INSIDE] * 4,
        out_shape=[
            jax.ShapeDtypeStruct((rows, width), low),
            jax.ShapeDtypeStruct((rows, query_width), low),
            jax.ShapeDtypeStruct((rows, 2 * kv_width), low),
            jax.ShapeDtypeStruct((columns - query_width - 2 * kv_width, width), jnp.float32),
        ],
        scratch_shapes=[
            pltpu.VMEM((width, columns), low),
            pltpu.SemaphoreType.DMA((len(pieces) * pieces[0].shape[0],)),
        ],
        compiler_params=pltpu.CompilerParams(vmem_limit_bytes=VMEM_BYTES),
        cost_estimate=cost(2 * rows * width * columns, *pieces),
        name="enter",
    )(spots, tokens, cosine, sine, *pieces)


def both_places(values):
    wide = values.astype(jnp.float32)
    low_lane = lax.broadcasted_iota(jnp.int32, values.shape, 1) < HEAD_DIM
    moved = pltpu.roll(wide, HEAD_DIM, 1)
    kind = values.dtype
    return [
        [jnp.where(low_lane, wide, 0.0).astype(kind), jnp.where(low_lane, 0.0, moved).astype(kind)],
        [jnp.where(low_lane, moved, 0.0).astype(kind), jnp.where(low_lane, 0.0, wide).astype(kind)],
    ]


def attend_kernel(query, keyval, bias, attended, log_totals):
    low = jnp.bfloat16
    rows = query.shape[0]
    kv_width = keyval.shape[1] // 2
    pair_lanes = 2 * HEAD_DIM
    repeat = HEADS // KV_HEADS
    log_totals[...] = jnp.zeros_like(log_totals)
    lane = lax.broadcasted_iota(jnp.int32, log_totals.shape, 1)

    @pl.loop(0, KV_HEADS // 2)
    def _(pair):
        at = pl.ds(pl.multiple_of(pair * pair_lanes, pair_lanes), pair_lanes)
        keys = both_places(keyval[:, at])
        at = pl.ds(pl.multiple_of(kv_width + pair * pair_lanes, pair_lanes), pair_lanes)
        values = both_places(keyval[:, at])
        for i in range(repeat):
            at = pl.ds(pl.multiple_of((pair * repeat + i) * pair_lanes, pair_lanes), pair_lanes)
            queries = query[:, at]
            total = jnp.zeros((rows, pair_lanes), jnp.float32)
            for a in range(2):
                head = 2 * i + a
                scores = dot_right(queries, keys[head // repeat][a]) + bias[...]
                peak = jnp.max(scores, axis=-1, keepdims=True)
                lifted = jnp.exp(scores - peak)
                row_total = jnp.sum(lifted, axis=-1, keepdims=True)
                weights_low = (lifted * (1.0 / row_total)).astype(low)
                total += dot_plain(weights_low, values[head // repeat][a])
                log_totals[...] = jnp.where(
                    lane == pair * (2 * repeat) + head, peak + jnp.log(row_total), log_totals[...]
                )
            attended[:, at] = total.astype(low)


def attend(query, keyval, bias):
    rows, query_width = query.shape
    return pl.pallas_call(
        attend_kernel,
        in_specs=[INSIDE] * 3,
        out_specs=[INSIDE] * 2,
        out_shape=[
            jax.ShapeDtypeStruct((rows, query_width), jnp.bfloat16),
            jax.ShapeDtypeStruct((rows, 128), jnp.float32),
        ],
        compiler_params=pltpu.CompilerParams(vmem_limit_bytes=VMEM_BYTES),
        cost_estimate=cost(8 * rows * query_width * bias.shape[1], query, keyval, bias),
        name="attend",
    )(query, keyval, bias)


def project_kernel(count, gain_at, spots, attended, tokens, small, member, kept, *refs):
    pieces = refs[:count]
    residual, sent, gate_rows, weight, sems = refs[count:]
    low = jnp.bfloat16
    width = tokens.shape[1]
    copies = weight_copies(spots, pieces, weight, sems)
    for copy in copies:
        copy.start()
    for copy in copies:
        copy.wait()
    hidden = tokens[...].astype(jnp.float32) + dot_plain(attended[...], weight[...])
    residual[...] = hidden
    gain = small[gain_at : gain_at + 1, :]
    normed = (hidden * mean_square_scale(hidden) * gain).astype(low)
    logits = dot_right(normed, small[...].astype(low))
    chosen = member[...] > 0.0
    logits = jnp.where(chosen, logits, -1e30)
    lifted = jnp.where(chosen, jnp.exp(logits - jnp.max(logits, axis=-1, keepdims=True)), 0.0)
    gates = lifted / jnp.sum(lifted, axis=-1, keepdims=True)
    gate_rows[...] = gates
    sent[:, :width] = normed
    sent[:, width:] = (gates * kept[...]).astype(low)


def project(attended, tokens, small, member, kept, gain_at, pieces, spots):
    rows, width = tokens.shape
    lanes = small.shape[0]
    low = jnp.bfloat16
    return pl.pallas_call(
        partial(project_kernel, len(pieces), gain_at),
        in_specs=[SCALARS] + [INSIDE] * 5 + [ANYWHERE] * len(pieces),
        out_specs=[INSIDE] * 3,
        out_shape=[
            jax.ShapeDtypeStruct((rows, width), jnp.float32),
            jax.ShapeDtypeStruct((rows, width + lanes), low),
            jax.ShapeDtypeStruct((rows, lanes), jnp.float32),
        ],
        scratch_shapes=[
            pltpu.VMEM((attended.shape[1], width), low),
            pltpu.SemaphoreType.DMA((len(pieces) * pieces[0].shape[0],)),
        ],
        compiler_params=pltpu.CompilerParams(vmem_limit_bytes=VMEM_BYTES),
        cost_estimate=cost(2 * rows * width * width, *pieces),
        name="project",
    )(spots, attended, tokens, small, member, kept, *pieces)


def grad_shapes(cut, rows, columns):
    low = jnp.bfloat16
    if cut:
        block = rows // 32
        return (
            [jax.ShapeDtypeStruct((4, 4, block, columns), low)] * 2,
            pltpu.VMEM((4, 2, 4, block, columns), low),
        )
    return (
        [jax.ShapeDtypeStruct((1, 1, 1, rows, columns), low)],
        pltpu.VMEM((1, 1, 1, rows, columns), low),
    )


def grad_copies(cut, place, source, outs, sems):
    if not cut:
        return [pltpu.make_async_copy(source, outs[0], sems.at[0])]
    core, member = place[0], place[1]
    other, own = outs
    copies = []
    for r in range(4):
        copies.append(
            pltpu.make_async_copy(
                source.at[:, 1 - core, member ^ r], other.at[r], sems.at[2 * r]
            )
        )
        copies.append(
            pltpu.make_async_copy(source.at[:, core, member ^ r], own.at[r], sems.at[2 * r + 1])
        )
    return copies


def turn_kernel(
    count,
    cut,
    gain_at,
    place,
    spots,
    normed_grad,
    residual,
    grad_out,
    small,
    gate_rows,
    member,
    kept,
    normed,
    attended,
    *refs,
):
    pieces = refs[:count]
    refs = refs[count:]
    outs = refs[: (2 if cut else 1)]
    resid_grad, head_grad, weight, weight_grad, sems, out_sems = refs[len(outs) :]
    low = jnp.bfloat16
    rows, width = residual.shape
    lanes = gate_rows.shape[1]
    copies = weight_copies(spots, pieces, weight, sems)
    for copy in copies:
        copy.start()
    lane = lax.broadcasted_iota(jnp.int32, (rows, lanes), 1)
    gates = gate_rows[...]
    gate_grads = normed_grad[:, width:] * kept[...]
    chosen_grad = gates * (gate_grads - jnp.sum(gates * gate_grads, axis=-1, keepdims=True))
    logit_grad = (chosen_grad * member[...]).astype(low)
    hidden = residual[...]
    scale = mean_square_scale(hidden)
    row_grad = normed_grad[:, :width] + dot_plain(logit_grad, small[...].astype(low))
    gain = small[gain_at : gain_at + 1, :]
    scaled = row_grad * gain
    total_grad = (
        grad_out[...].astype(jnp.float32)
        + scale * scaled
        - hidden * (scale * scale * scale) * jnp.mean(scaled * hidden, axis=-1, keepdims=True)
    )
    resid_grad[...] = total_grad
    attn_grad = total_grad.astype(low)
    shape = weight_grad.shape[:-1]
    gain_grad = (row_grad * hidden * scale).astype(low)
    picks = jnp.where(lane == gain_at, 1.0, 0.0).astype(low)
    weight_grad[..., width:] = (
        (dot_left(normed[...][:, :width], logit_grad) + dot_left(gain_grad, picks))
        .astype(low)
        .reshape(shape + (lanes,))
    )
    for start in range(0, width, 512):
        weight_grad[..., start : start + 512] = (
            dot_left(attended[...], attn_grad[:, start : start + 512])
            .astype(low)
            .reshape(shape + (512,))
        )
    out_copies = grad_copies(cut, place, weight_grad, outs, out_sems)
    for copy in out_copies:
        copy.start()
    for copy in copies:
        copy.wait()
    head_grad[...] = dot_right(attn_grad, weight[...]).astype(low)
    for copy in out_copies:
        copy.wait()


def turn(place, spots, operands, pieces, cut, gain_at):
    residual, gate_rows, attended = operands[1], operands[4], operands[8]
    rows, width = residual.shape
    query_width = attended.shape[1]
    low = jnp.bfloat16
    grads, held = grad_shapes(cut, query_width, width + gate_rows.shape[1])
    return pl.pallas_call(
        partial(turn_kernel, len(pieces), cut, gain_at),
        in_specs=[SCALARS, SCALARS] + [INSIDE] * len(operands) + [ANYWHERE] * len(pieces),
        out_specs=[ANYWHERE] * len(grads) + [INSIDE] * 2,
        out_shape=grads
        + [
            jax.ShapeDtypeStruct((rows, width), jnp.float32),
            jax.ShapeDtypeStruct((rows, query_width), low),
        ],
        scratch_shapes=[
            pltpu.VMEM((query_width, width), low),
            held,
            pltpu.SemaphoreType.DMA((len(pieces) * pieces[0].shape[0],)),
            pltpu.SemaphoreType.DMA((8,)),
        ],
        compiler_params=pltpu.CompilerParams(vmem_limit_bytes=VMEM_BYTES),
        cost_estimate=cost(0),
        name="turn",
    )(place, spots, *operands, *pieces)


def attend_back_kernel(
    head_grad, query, keyval, bias, log_totals, cosine, sine, query_grad, keyval_grad, totals
):
    low = jnp.bfloat16
    rows = query.shape[0]
    kv_width = keyval.shape[1] // 2
    pair_lanes = 2 * HEAD_DIM
    repeat = HEADS // KV_HEADS
    totals[...] = log_totals[...].T

    @pl.loop(0, KV_HEADS // 2)
    def _(pair):
        key_at = pl.ds(pl.multiple_of(pair * pair_lanes, pair_lanes), pair_lanes)
        value_at = pl.ds(pl.multiple_of(kv_width + pair * pair_lanes, pair_lanes), pair_lanes)
        keys = both_places(keyval[:, key_at])
        values = both_places(keyval[:, value_at])
        key_grads = [[None, None], [None, None]]
        value_grads = [[None, None], [None, None]]
        for i in range(repeat):
            at = pl.ds(pl.multiple_of((pair * repeat + i) * pair_lanes, pair_lanes), pair_lanes)
            queries = query[:, at]
            grads = head_grad[:, at]
            query_part = jnp.zeros((rows, pair_lanes), jnp.float32)
            for a in range(2):
                head = 2 * i + a
                g = head // repeat
                total = totals[pl.ds(pair * (2 * repeat) + head, 1), :]
                weights = jnp.exp(dot_right(keys[g][a], queries) + bias[...] - total)
                weight_grads = dot_right(values[g][a], grads)
                delta = jnp.sum(weights * weight_grads, axis=0, keepdims=True)
                score_grads = (weights * (weight_grads - delta)).astype(low)
                value_part = dot_plain(weights.astype(low), grads)
                key_part = dot_plain(score_grads, queries)
                query_part += dot_left(score_grads, keys[g][a])
                if key_grads[g][a] is None:
                    key_grads[g][a], value_grads[g][a] = key_part, value_part
                else:
                    key_grads[g][a] += key_part
                    value_grads[g][a] += value_part
            query_part = query_part * (HEAD_DIM**-0.5)
            query_part = query_part * cosine[...] - swap_halves(query_part) * sine[...]
            query_grad[:, at] = query_part.astype(low)
        low_lane = lax.broadcasted_iota(jnp.int32, (keyval.shape[0], pair_lanes), 1) < HEAD_DIM
        for at, found in ((key_at, key_grads), (value_at, value_grads)):
            keyval_grad[:, at] = jnp.where(
                low_lane,
                found[0][0] + pltpu.roll(found[0][1], HEAD_DIM, 1),
                pltpu.roll(found[1][0], HEAD_DIM, 1) + found[1][1],
            ).astype(low)


def attend_back(head_grad, query, keyval, bias, log_totals, cosine, sine):
    rows, query_width = query.shape
    low = jnp.bfloat16
    return pl.pallas_call(
        attend_back_kernel,
        in_specs=[INSIDE] * 7,
        out_specs=[INSIDE] * 2,
        out_shape=[
            jax.ShapeDtypeStruct((rows, query_width), low),
            jax.ShapeDtypeStruct(keyval.shape, low),
        ],
        scratch_shapes=[pltpu.VMEM((128, rows), jnp.float32)],
        compiler_params=pltpu.CompilerParams(vmem_limit_bytes=VMEM_BYTES),
        cost_estimate=cost(0),
        name="attend_back",
    )(head_grad, query, keyval, bias, log_totals, cosine, sine)


def leave_kernel(
    count,
    cut,
    gain_at,
    place,
    spots,
    keyval_sum,
    query_grad,
    normed,
    tokens,
    resid_grad,
    small,
    cosine,
    sine,
    *refs,
):
    pieces = refs[:count]
    refs = refs[count:]
    outs = refs[: (2 if cut else 1)]
    input_grad, weight, weight_grad, joined, sems, out_sems = refs[len(outs) :]
    low = jnp.bfloat16
    rows, width = tokens.shape
    query_width = query_grad.shape[1]
    kv_width = keyval_sum.shape[1] // 2
    qkv_width = query_width + 2 * kv_width
    pair = 2 * HEAD_DIM
    copies = weight_copies(spots, pieces, weight, sems)
    for copy in copies:
        copy.start()
    joined[:, :query_width] = query_grad[...]
    for start in range(0, kv_width, pair):
        part = keyval_sum[:, start : start + pair]
        part = part * cosine[...] - swap_halves(part) * sine[...]
        joined[:, query_width + start : query_width + start + pair] = part.astype(low)
    joined[:, query_width + kv_width :] = keyval_sum[:, kv_width:].astype(low)
    shape = weight_grad.shape[:-1]
    for start in range(0, qkv_width, 512):
        weight_grad[..., start : start + 512] = (
            dot_left(normed[...], joined[:, start : start + 512]).astype(low).reshape(shape + (512,))
        )
    for copy in copies:
        copy.wait()
    row_grad = dot_right(joined[...], weight[:, :qkv_width])
    inputs = tokens[...].astype(jnp.float32)
    scale = mean_square_scale(inputs)
    lanes = weight_grad.shape[-1] - qkv_width
    lane = lax.broadcasted_iota(jnp.int32, (rows, lanes), 1)
    picks = jnp.where(lane == gain_at, 1.0, 0.0).astype(low)
    weight_grad[..., qkv_width:] = (
        dot_left((row_grad * inputs * scale).astype(low), picks).astype(low).reshape(shape + (lanes,))
    )
    out_copies = grad_copies(cut, place, weight_grad, outs, out_sems)
    for copy in out_copies:
        copy.start()
    scaled = row_grad * small[gain_at : gain_at + 1, :]
    input_grad[...] = (
        resid_grad[...]
        + scale * scaled
        - inputs * (scale * scale * scale) * jnp.mean(scaled * inputs, axis=-1, keepdims=True)
    )
    for copy in out_copies:
        copy.wait()


def leave(place, spots, operands, pieces, cut, gain_at):
    tokens, query_grad, keyval_sum = operands[3], operands[1], operands[0]
    rows, width = tokens.shape
    columns = pieces[0].shape[2]
    low = jnp.bfloat16
    grads, held = grad_shapes(cut, width, columns)
    return pl.pallas_call(
        partial(leave_kernel, len(pieces), cut, gain_at),
        in_specs=[SCALARS, SCALARS] + [INSIDE] * len(operands) + [ANYWHERE] * len(pieces),
        out_specs=[ANYWHERE] * len(grads) + [INSIDE],
        out_shape=grads + [jax.ShapeDtypeStruct((rows, width), jnp.float32)],
        scratch_shapes=[
            pltpu.VMEM((width, columns), low),
            held,
            pltpu.VMEM((rows, query_grad.shape[1] + keyval_sum.shape[1]), low),
            pltpu.SemaphoreType.DMA((len(pieces) * pieces[0].shape[0],)),
            pltpu.SemaphoreType.DMA((8,)),
        ],
        compiler_params=pltpu.CompilerParams(vmem_limit_bytes=VMEM_BYTES),
        cost_estimate=cost(0),
        name="leave",
    )(place, spots, *operands, *pieces)


def expert_kernel(cut, carried, last, row_blocks, grad_blocks, row_tile, place, first, packed, *refs):
    blocks_in = refs[:row_blocks]
    grads_in = refs[row_blocks : row_blocks + grad_blocks]
    refs = refs[row_blocks + grad_blocks :]
    if carried:
        mix_in, turn_in = refs[:2]
        refs = refs[2:]
    count = packed.shape[2]
    outs = 4 if cut else 1
    packed_grads = refs[:outs]
    mix_out, turn_out = refs[outs : outs + 2]
    refs = refs[outs + 2 :]
    if last:
        mix, turned = refs[:2]
        refs = refs[2:]
    else:
        mix, turned = mix_out, turn_out
    (
        rows,
        grads,
        gates,
        gate_w,
        up_w,
        down_w,
        gate_g,
        up_g,
        down_g,
        weighted,
        gate_side,
        up_side,
        load_sems,
        save_sems,
        carry_sems,
    ) = refs
    hidden_width = gate_w.shape[-1]
    total_rows, width = rows.shape
    lanes = gates.shape[1]
    low = jnp.bfloat16

    def sides(gate, up, down):
        for side, inner in ((0, gate), (1, up)):
            for j in range(3):
                yield side, pl.ds(j * hidden_width, hidden_width), inner, j
        yield 2, pl.ds(0, width), down, None

    def loads(e):
        slot = e % 2
        copies = []
        for i, (side, columns, inner, j) in enumerate(sides(gate_w, up_w, down_w)):
            outer = packed.at[:, side, e, :, columns]
            inner = inner.at[slot] if j is None else inner.at[slot, :, j]
            copies.append(pltpu.make_async_copy(outer, inner, load_sems.at[slot, i]))
        return copies

    def saves(e):
        slot = e % 2
        copies = []
        for i, (side, columns, inner, j) in enumerate(sides(gate_g, up_g, down_g)):
            if not cut:
                outer = packed_grads[0].at[:, side, e, :, columns]
                source = inner.at[slot] if j is None else inner.at[slot, :, j]
                copies.append(pltpu.make_async_copy(source, outer, save_sems.at[slot, i]))
                continue
            own, rest, far, near = packed_grads
            targets = [own, rest.at[0], rest.at[1], rest.at[2]]
            targets += [near.at[1], near.at[0], far.at[0], far.at[1]]
            for n, target in enumerate(targets):
                block = 2 * lax.rem(place[2] + n % 4, 4) + (place[0] ^ (n // 4))
                source = inner.at[slot, block] if j is None else inner.at[slot, block, j]
                outer = target.at[side, e, :, columns]
                copies.append(pltpu.make_async_copy(source, outer, save_sems.at[slot, 8 * i + n]))
        return copies

    carries = (
        block_copies(grads_in, grads, carry_sems, 0, pl.ds(0, width))
        + block_copies(blocks_in, rows, carry_sems, grad_blocks, pl.ds(0, width))
        + block_copies(
            blocks_in, gates, carry_sems, grad_blocks + row_blocks, pl.ds(width, lanes)
        )
    )
    sums = []
    if carried:
        at = grad_blocks + 2 * row_blocks
        sums = [
            pltpu.make_async_copy(mix_in, mix, carry_sems.at[at]),
            pltpu.make_async_copy(turn_in, turned, carry_sems.at[at + 1]),
        ]
    for copy in loads(0) + carries + sums:
        copy.start()
    for e in range(count):
        slot = e % 2
        if e + 1 < count:
            for copy in loads(e + 1):
                copy.start()
        for copy in loads(e):
            copy.wait()
        if e == 0:
            for copy in carries:
                copy.wait()
            if not carried:
                turned[:, width:] = jnp.zeros((total_rows, lanes), jnp.float32)

        @pl.loop(0, total_rows // row_tile)
        def _(tile):
            span = pl.ds(pl.multiple_of(tile * row_tile, row_tile), row_tile)
            gate_full = gate_w[slot].reshape(width, hidden_width)
            up_full = up_w[slot].reshape(width, hidden_width)
            down_full = down_w[slot].reshape(hidden_width, width)
            here = rows[span, :]
            slope = dot_right(grads[span, :], down_full)
            gate_pre = dot_plain(here, gate_full)
            up_pre = dot_plain(here, up_full)
            lane = lax.broadcasted_iota(jnp.int32, (row_tile, lanes), 1)
            chosen = lane == first[0] + e
            gate_column = jnp.sum(
                jnp.where(chosen, gates[span, :].astype(jnp.float32), 0.0), axis=1, keepdims=True
            )
            sigmoid_gate = jax.nn.sigmoid(gate_pre)
            activated = gate_pre * sigmoid_gate
            hidden = (activated * up_pre).astype(low).astype(jnp.float32)
            share = jnp.sum(hidden * slope, axis=1, keepdims=True)
            if e == 0 and sums:

                @pl.when(tile == 0)
                def _():
                    for copy in sums:
                        copy.wait()

            turned[span, width:] = jnp.where(chosen, share, turned[span, width:])
            part_weighted = (hidden * gate_column).astype(low)
            hidden_grad = slope * gate_column
            part_gate = (
                hidden_grad * up_pre * (sigmoid_gate + activated * (1.0 - sigmoid_gate))
            ).astype(low)
            part_up = (hidden_grad * activated).astype(low)
            weighted[span, :] = part_weighted
            gate_side[span, :] = part_gate
            up_side[span, :] = part_up
            mix_part = dot_plain(part_weighted, down_full)
            turn_part = dot_right(part_gate, gate_full) + dot_right(part_up, up_full)
            if e == 0 and not carried:
                mix[span, :] = mix_part
                turned[span, :width] = turn_part
            elif last and e == count - 1:
                mix_out[span, :] = (mix[span, :] + mix_part).astype(low)
                turn_out[span, :width] = (turned[span, :width] + turn_part).astype(low)
                turn_out[span, width:] = turned[span, width:].astype(low)
            else:
                mix[span, :] += mix_part
                turned[span, :width] += turn_part

        if e >= 2:
            for copy in saves(e - 2):
                copy.wait()
        down_g[slot] = dot_left(weighted[...], grads[...]).astype(low).reshape(down_g.shape[1:])
        gate_g[slot] = dot_left(rows[...], gate_side[...]).astype(low).reshape(gate_g.shape[1:])
        up_g[slot] = dot_left(rows[...], up_side[...]).astype(low).reshape(up_g.shape[1:])
        for copy in saves(e):
            copy.start()
    for e in range(max(0, count - 2), count):
        for copy in saves(e):
            copy.wait()


def expert_pass(place, first, rows, grads, packed, carry, cut, last):
    blocks, _, count, part, width = packed.shape
    hidden_width = blocks * part
    total_rows = sum(block.shape[0] for block in rows)
    lanes = rows[0].shape[1] - width
    low = jnp.bfloat16
    wide = jnp.float32
    carried = carry is not None
    flops = 18 * total_rows * count * hidden_width * width
    side = pltpu.VMEM((2, blocks, 3, part, hidden_width), low)
    sides = [side, side, pltpu.VMEM((2, blocks, part, width), low)]
    sums = [(total_rows, width), (total_rows, width + lanes)]
    one = packed.shape[1:]
    grads_out = [one, (3,) + one, (2,) + one, (2,) + one] if cut else [packed.shape]
    outs = len(grads_out)
    found = pl.pallas_call(
        partial(expert_kernel, cut, carried, last, len(rows), len(grads), min(512, total_rows)),
        in_specs=[SCALARS, SCALARS]
        + [ANYWHERE] * (1 + len(rows) + len(grads) + (2 if carried else 0)),
        out_specs=[ANYWHERE] * outs + [INSIDE, INSIDE],
        out_shape=[jax.ShapeDtypeStruct(shape, low) for shape in grads_out]
        + [jax.ShapeDtypeStruct(shape, low if last else wide) for shape in sums],
        scratch_shapes=([pltpu.VMEM(shape, wide) for shape in sums] if last else [])
        + [
            pltpu.VMEM((total_rows, width), low),
            pltpu.VMEM((total_rows, width), low),
            pltpu.VMEM((total_rows, lanes), low),
        ]
        + sides
        + sides
        + [pltpu.VMEM((total_rows, hidden_width), low)] * 3
        + [
            pltpu.SemaphoreType.DMA((2, 7)),
            pltpu.SemaphoreType.DMA((2, 56)),
            pltpu.SemaphoreType.DMA((2 * len(rows) + len(grads) + 2,)),
        ],
        compiler_params=pltpu.CompilerParams(vmem_limit_bytes=VMEM_BYTES),
        cost_estimate=cost(flops, packed, packed, *rows, *grads),
        name="experts",
    )(place, first, packed, *rows, *grads, *(carry or ()))
    return found[:outs], found[outs], found[outs + 1]


def unpack_kernel(counts, *refs):
    found, (gate, up, down) = refs[:-3], refs[-3:]
    hidden_width = gate.shape[2]
    base = 0
    at = 0
    for terms in counts:
        parts = found[at : at + terms]
        at += terms
        count, part = parts[0].shape[1], parts[0].shape[2]
        for e in range(count):
            for side in range(3):
                total = parts[0][side, e].astype(jnp.float32)
                for other in parts[1:]:
                    total += other[side, e].astype(jnp.float32)
                if side == 2:
                    down[base + e] = total
                    continue
                for j in range(3):
                    (gate, up)[side][base + e, j * part : (j + 1) * part, :] = total[
                        :, j * hidden_width : (j + 1) * hidden_width
                    ]
        base += count


def unpack(chunks, gate_shape, down_shape):
    arrays = [term for terms in chunks for term in terms]
    return pl.pallas_call(
        partial(unpack_kernel, [len(terms) for terms in chunks]),
        in_specs=[INSIDE] * len(arrays),
        out_specs=[INSIDE] * 3,
        out_shape=[
            jax.ShapeDtypeStruct(gate_shape, jnp.float32),
            jax.ShapeDtypeStruct(gate_shape, jnp.float32),
            jax.ShapeDtypeStruct(down_shape, jnp.float32),
        ],
        compiler_params=pltpu.CompilerParams(vmem_limit_bytes=VMEM_BYTES),
        cost_estimate=cost(0),
        name="unpack",
    )(*arrays)


def cube():
    return lax.axis_size("batch") == 8 and lax.axis_size("expert") == 4


def pair_moves(size, flip):
    return [(i, i ^ flip) for i in range(size)]


def shift_moves(step):
    return [(2 * z + c, 2 * ((z + step) % 4) + c) for z in range(4) for c in range(2)]


def gather_start(rows):
    size = lax.axis_size("expert")
    if size != 4:
        stacked = lax.all_gather(rows, "expert", axis=0)
        own = lax.axis_index("expert")
        return [
            lax.dynamic_index_in_dim(stacked, own ^ r, axis=0, keepdims=False) for r in range(size)
        ]
    return [rows] + [lax.ppermute(rows, "expert", pair_moves(4, r)) for r in (1, 2)]


def gather_finish(state, events=()):
    if lax.axis_size("expert") != 4:
        return state
    first, second = after(state[1:], events)
    half = first.shape[0] // 2
    top = lax.ppermute(second[:half], "expert", pair_moves(4, 1))
    bottom = lax.ppermute(first[half:], "expert", pair_moves(4, 2))
    return state + [top, bottom]


def gather_blocks(rows):
    return gather_finish(gather_start(rows))


def scatter_start(parts):
    low = jnp.bfloat16
    if lax.axis_size("expert") != 4:
        own = lax.axis_index("expert")
        order = jnp.arange(len(parts), dtype=jnp.int32) ^ own
        stacked = jnp.take(jnp.stack(parts), order, axis=0).astype(low)
        return [lax.psum_scatter(stacked, "expert", scatter_dimension=0).astype(jnp.float32)]
    across, along = pair_moves(4, 1), pair_moves(4, 2)
    half = parts[0].shape[0] // 2
    top = lax.ppermute(parts[3][:half].astype(low), "expert", across)
    bottom = lax.ppermute(parts[3][half:].astype(low), "expert", along)
    first_top = lax.ppermute(parts[1][:half].astype(low), "expert", across)
    second_bottom = lax.ppermute(parts[2][half:].astype(low), "expert", along)
    for_first = add_low(parts[1][half:], bottom)
    for_second = add_low(parts[2][:half], top)
    return [parts[0], first_top, second_bottom, for_first, for_second]


def scatter_finish(state):
    if len(state) == 1:
        return state[0]
    own, first_top, second_bottom, for_first, for_second = state
    half = first_top.shape[0]
    second_top = lax.ppermute(for_second, "expert", pair_moves(4, 2))
    first_bottom = lax.ppermute(for_first, "expert", pair_moves(4, 1))
    return jnp.concatenate(
        [
            total_of([own[:half], first_top, second_top]),
            total_of([own[half:], first_bottom, second_bottom]),
        ],
        axis=0,
    )


def scatter_blocks(parts):
    return scatter_finish(scatter_start(parts))


def after(values, events):
    return lax.optimization_barrier((values, events))[0]


def send_parts(parts):
    if lax.axis_size("expert") != 4:
        return [scatter_blocks(parts)]
    low = jnp.bfloat16
    return [parts[0]] + [
        lax.ppermute(parts[r].astype(low), "expert", pair_moves(4, r)) for r in range(1, 4)
    ]


def total_of(parts):
    total = parts[0].astype(jnp.float32)
    for part in parts[1:]:
        total += part.astype(jnp.float32)
    return total


def shift_dense(rows, events):
    if not cube():
        return [lax.all_gather(rows, ("batch", "expert"), axis=0, tiled=True)]
    below, above = step_up(rows), step_down(rows)
    return [rows, below, step_up(after(below, (above, events))), above]


def dense_start(line, columns, events):
    found = [rows[:, columns] for rows in line]
    if not cube():
        return [found[0][None]]
    return gather_start(after(jnp.stack(found), events))


def dense_finish(state, events=()):
    if not cube():
        return state, jnp.zeros((1, 1), jnp.int32), ()
    place = lax.axis_index("batch")
    level, core = place // 2, place % 2
    member = lax.axis_index("expert")
    mine = gather_finish(state, events)
    far = mine[3:]
    mine = mine[:3] + [jnp.concatenate(far, axis=0)]
    other = [exchange_cores(block) for block in mine]
    spots = [
        [(((level + 4 - k) % 4) * 2 + (core ^ c)) * 4 + (member ^ r) for k in range(4)]
        for c in range(2)
        for r in range(4)
    ]
    return mine + other, jnp.array(spots, jnp.int32), far


def sum_chunk(packed_grad):
    return lax.psum_scatter(packed_grad, "batch", scatter_dimension=0, tiled=True)


def exchange_cores(values):
    return lax.ppermute(values, "batch", pair_moves(8, 1))


def step_up(values):
    return lax.ppermute(values, "batch", shift_moves(1))


def step_down(values):
    return lax.ppermute(values, "batch", shift_moves(3))


def add_low(*parts):
    total = parts[0].astype(jnp.float32)
    for part in parts[1:]:
        total += part.astype(jnp.float32)
    return total.astype(jnp.bfloat16)


def join_cores(own, received):
    return [add_low(own[r], received[r]) for r in range(4)]


def line_start(plane):
    level = lax.axis_index("batch") // 2
    own, up, far, down = (
        lax.dynamic_index_in_dim(plane, (level + r) % 4, axis=0, keepdims=False) for r in range(4)
    )
    return own, step_down(add_low(down)), add_low(up, step_up(add_low(far)))


def line_finish(state, events=()):
    own, down, up = state
    return total_of([own, down, step_up(after(up, events))])


def scatter_whole(found):
    values = found[0].reshape(found[0].shape[3:])
    total = lax.psum_scatter(values, ("batch", "expert"), scatter_dimension=0, tiled=True)
    return total.astype(jnp.float32)


def pack_kernel(chunks, query, key, value, small, out, gate, up, down, dense, *packed):
    start = 0
    for part in (query, key, value, small, out):
        dense[:, start : start + part.shape[1]] = part[...]
        start += part.shape[1]
    part, hidden_width = down.shape[1], gate.shape[2]
    for n, target in enumerate(packed):
        for e in range(chunks[n], chunks[n + 1]):
            for side, source in ((0, gate), (1, up)):
                for j in range(3):
                    target[side, e - chunks[n], :, j * hidden_width : (j + 1) * hidden_width] = (
                        source[e, j * part : (j + 1) * part, :]
                    )
            target[2, e - chunks[n]] = down[e]


def pack(chunks, query, key, value, small, out, gate, up, down):
    low = jnp.bfloat16
    columns = sum(part.shape[1] for part in (query, key, value, small, out))
    return pl.pallas_call(
        partial(pack_kernel, chunks),
        in_specs=[INSIDE] * 8,
        out_specs=[INSIDE] * len(chunks),
        out_shape=[jax.ShapeDtypeStruct((query.shape[0], columns), low)]
        + [
            jax.ShapeDtypeStruct((3, b - a) + down.shape[1:], low)
            for a, b in zip(chunks[:-1], chunks[1:])
        ],
        compiler_params=pltpu.CompilerParams(vmem_limit_bytes=VMEM_BYTES),
        cost_estimate=cost(0),
        name="pack",
    )(query, key, value, small, out, gate, up, down)


def local(
    tokens,
    cotangent,
    attn_gain,
    query_weight,
    key_weight,
    value_weight,
    out_weight,
    ffn_gain,
    router_weight,
    gate_weight,
    up_weight,
    down_weight,
    routes,
    ranking,
):
    low = jnp.bfloat16
    wide = jnp.float32
    query_width = HEADS * HEAD_DIM
    kv_width = KV_HEADS * HEAD_DIM
    qkv_width = query_width + 2 * kv_width
    width = tokens.shape[2]
    experts_total = router_weight.shape[1]
    extra = -(-(experts_total + 2) // 128) * 128
    first_gain, second_gain = experts_total, experts_total + 1
    local_experts = gate_weight.shape[0]
    member_count = lax.axis_size("expert")
    member_id = lax.axis_index("expert")
    local_rows = tokens.shape[1]
    group_rows = local_rows * member_count
    cut = cube()
    line_place = lax.axis_index("batch")
    place = jnp.stack([line_place % 2, member_id, line_place // 2]).astype(jnp.int32)

    route_rows = routes[0]
    rank_rows = ranking[0]
    expert_lanes = jnp.arange(extra, dtype=jnp.int32)
    member = jnp.any(route_rows[:, :, None] == expert_lanes[None, None, :], axis=1)
    marks = jnp.where(
        expert_lanes[None, :] == experts_total,
        (rank_rows // 32)[:, None],
        jnp.where(expert_lanes[None, :] == experts_total + 1, (rank_rows % 32)[:, None], member),
    ).astype(low)
    grad_out = cotangent[0]
    small_width = qkv_width + extra
    chunks = (0, 3, local_experts)
    dense_rows, *packed_own = pack(
        chunks,
        query_weight,
        key_weight,
        value_weight,
        jnp.concatenate(
            [
                router_weight,
                attn_gain[:, None],
                ffn_gain[:, None],
                jnp.zeros((query_weight.shape[0], extra - experts_total - 2), low),
            ],
            axis=1,
        ),
        out_weight,
        gate_weight,
        up_weight,
        down_weight,
    )
    row_ids = member_id * local_rows + jnp.arange(local_rows, dtype=jnp.int32)
    half_dim = HEAD_DIM // 2
    frequency = THETA ** (-jnp.arange(half_dim, dtype=wide) / half_dim)
    angles = place_of(row_ids).astype(wide)[:, None] * frequency[None, :]
    cosine = jnp.tile(jnp.cos(angles), (1, 4))
    sine_part = jnp.tile(jnp.concatenate([-jnp.sin(angles), jnp.sin(angles)], axis=1), (1, 2))
    if member_count == 4:
        away = 1 << 20
        starts = [
            jnp.where(member_id >= 1, 0, away),
            jnp.where(member_id >= 2, local_rows, away),
            member_id * local_rows,
        ]
    else:
        starts = [(member_id ^ r) * local_rows for r in range(member_count)]
    key_ids = jnp.concatenate([s + jnp.arange(local_rows, dtype=jnp.int32) for s in starts])
    bias = jnp.where(visible(row_ids, key_ids), 0.0, -1e30).astype(wide)
    bias_turned = bias.T
    tables = (cosine, sine_part, bias, bias_turned)

    line = shift_dense(dense_rows, tables)
    grad_blocks = gather_blocks(after(jnp.concatenate([grad_out, marks], axis=1), dense_rows))
    marks_all = jnp.concatenate([block[:, width:] for block in grad_blocks], axis=0)
    qkv_state = dense_start(line, slice(0, small_width), grad_blocks)
    plane = qkv_state[1:]
    qkv_pieces, qkv_spots, far = dense_finish(qkv_state)
    out_state = dense_start(line, slice(small_width, None), far)
    packed_all = [
        lax.all_gather(after(packed, events), "batch", axis=0)
        for packed, events in zip(packed_own, ((line, grad_blocks), plane))
    ]

    normed, query, keyval, small = enter(
        tokens[0], cosine, sine_part, qkv_pieces, qkv_spots, first_gain, query_width, kv_width
    )

    rank_all = (
        marks_all[:, experts_total].astype(wide) * 32 + marks_all[:, experts_total + 1].astype(wide)
    )
    earlier = (rank_all[None, :] < rank_rows.astype(wide)[:, None]).astype(low)
    before = product(earlier, marks_all)
    capacity = 5 * group_rows * route_rows.shape[1] // (4 * experts_total)
    member = member.astype(wide)
    kept = jnp.where(before < capacity, member, 0.0)

    keyval_blocks = gather_blocks(after(keyval, out_state[1:]))
    if member_count == 4:
        ordered = keyval_blocks[:3] + [jnp.concatenate(keyval_blocks[3:], axis=0)]
        keys = jnp.concatenate(
            [
                lax.select_n(member_id, *ordered),
                lax.select_n(member_id ^ 1, *ordered),
                keyval,
            ],
            axis=0,
        )
    else:
        keys = jnp.concatenate(keyval_blocks, axis=0)
    attended, log_totals = attend(query, keys, bias)
    out_pieces, out_spots, _ = dense_finish(out_state, keyval_blocks[3:])
    residual, sent, gate_rows = project(
        attended, tokens[0], small, member, kept, second_gain, out_pieces, out_spots
    )
    sent_blocks = gather_blocks(sent)

    carry, chunk_grads = None, []
    for packed, a, b in zip(packed_all, chunks[:-1], chunks[1:]):
        first = (member_id * local_experts + a).astype(jnp.int32).reshape(1)
        packed_grads, mixture_all, row_grad = expert_pass(
            place,
            first,
            sent_blocks,
            grad_blocks,
            packed,
            carry,
            cut and b == local_experts,
            b == local_experts,
        )
        carry = (mixture_all, row_grad)
        chunk_grads.append(packed_grads)

    def blocks_of(values):
        return [values[r * local_rows : (r + 1) * local_rows] for r in range(member_count)]

    totals = [sum_chunk(chunk_grads[0][0])]
    if cut:
        own, rest, far, near = chunk_grads[1]
        far, near = exchange_cores(far), exchange_cores(near)
        far_sum, down_sum = add_low(rest[1], far[0]), add_low(rest[2], far[1])
    turn_state = scatter_start(blocks_of(row_grad))
    if cut:
        turn_state = after(turn_state, (far_sum, down_sum))
    normed_grad = scatter_finish(turn_state)
    turned = turn(
        place,
        out_spots,
        (
            normed_grad,
            residual,
            grad_out,
            small,
            gate_rows,
            member,
            kept,
            sent,
            attended,
        ),
        out_pieces,
        cut,
        second_gain,
    )
    out_found = turned[:-2]
    resid_grad, head_grad = turned[-2:]
    mixture_parts = send_parts(blocks_of(after(mixture_all, normed_grad)))
    if cut:
        up_sum = add_low(rest[0], near[0], step_up(far_sum))
    query_grad, key_grads = attend_back(
        head_grad, query, keys, bias_turned, log_totals, cosine, sine_part
    )
    if member_count == 4:
        zero = jnp.zeros((), low)
        for_first, for_second, for_own = blocks_of(key_grads)[:3]
        key_parts = []
        for r in range(4):
            part = jnp.where(member_id == r, for_first, zero)
            part += jnp.where(member_id ^ 1 == r, for_second, zero)
            key_parts.append(part + for_own if r == 0 else part)
    else:
        key_parts = blocks_of(key_grads)
    if cut:
        out_found = out_found[1], exchange_cores(out_found[0])
        key_parts = after(key_parts, (mixture_parts[1:], up_sum))
    keyval_sum = scatter_blocks(key_parts)
    if cut:
        out_state = scatter_start(join_cores(*out_found))
    if cut:
        keyval_sum = after(keyval_sum, out_found)
    left = leave(
        place,
        qkv_spots,
        (
            keyval_sum,
            query_grad,
            normed,
            tokens[0],
            resid_grad,
            small,
            cosine,
            sine_part,
        ),
        qkv_pieces,
        cut,
        first_gain,
    )
    qkv_found, input_grad = left[:-1], left[-1]
    result = (residual + total_of(mixture_parts)).astype(low)
    if cut:
        down_term = step_down(after(down_sum, key_parts))
        received = exchange_cores(after(qkv_found[0], (totals[0], out_state[1:], down_term)))
        out_plane = scatter_finish(out_state)
        up_term = step_up(up_sum)
        qkv_parts = join_cores(qkv_found[1], after(received, out_plane))
        qkv_plane = after(scatter_blocks(qkv_parts), up_term)
        out_sum = line_finish(line_start(out_plane))
        qkv_state = line_start(qkv_plane)
        terms = [[totals[0][0]], after([own, near[1], down_term, up_term], qkv_plane)]
        expert_totals = unpack(terms, gate_weight.shape, down_weight.shape)
        qkv_sum = line_finish(qkv_state, expert_totals)
    else:
        out_sum = scatter_whole(out_found)
        qkv_sum = scatter_whole(qkv_found)
        terms = [[totals[0][0]]] + [[sum_chunk(found[0])[0]] for found in chunk_grads[1:]]
        expert_totals = unpack(terms, gate_weight.shape, down_weight.shape)
    gate_total, up_total, down_total = expert_totals
    return (
        result[None],
        input_grad[None],
        qkv_sum[:, qkv_width + first_gain],
        qkv_sum[:, :query_width],
        qkv_sum[:, query_width : query_width + kv_width],
        qkv_sum[:, query_width + kv_width : qkv_width],
        out_sum[:, :width],
        out_sum[:, width + second_gain],
        out_sum[:, width : width + experts_total],
        gate_total,
        up_total,
        down_total,
    )


def solution(mesh):
    return jax.shard_map(
        local,
        mesh=mesh,
        in_specs=(
            P("batch", "expert", None),
            P("batch", "expert", None),
            P(("batch", "expert")),
            P(("batch", "expert"), None),
            P(("batch", "expert"), None),
            P(("batch", "expert"), None),
            P(("batch", "expert"), None),
            P(("batch", "expert")),
            P(("batch", "expert"), None),
            P("expert", "batch", None),
            P("expert", "batch", None),
            P("expert", "batch", None),
            P("batch", "expert", None),
            P("batch", "expert"),
        ),
        out_specs=(
            P("batch", "expert", None),
            P("batch", "expert", None),
            P(("batch", "expert")),
            P(("batch", "expert"), None),
            P(("batch", "expert"), None),
            P(("batch", "expert"), None),
            P(("batch", "expert"), None),
            P(("batch", "expert")),
            P(("batch", "expert"), None),
            P("expert", "batch", None),
            P("expert", "batch", None),
            P("expert", "batch", None),
        ),
        check_vma=False,
    )
```

```python
from functools import partial

import jax
import jax.numpy as jnp
from jax import lax
from jax.experimental import pallas as pl
from jax.experimental.pallas import tpu as pltpu
from jax.sharding import PartitionSpec as P

HEADS = 24
KV_HEADS = 8
HEAD_DIM = 64
PROMPT = 512
CLEN = 256


EPS = 1e-06
THETA = 10000.0


def product(left, right):
    return jnp.dot(left, right, preferred_element_type=jnp.float32)


def place_of(row_ids):
    return jnp.where(row_ids < PROMPT, row_ids, PROMPT + (row_ids - PROMPT) % CLEN)


def visible(query_ids, key_ids):
    causal = key_ids[None, :] <= query_ids[:, None]
    same_run = (key_ids[None, :] - PROMPT) // CLEN == (query_ids[:, None] - PROMPT) // CLEN
    return causal & ((key_ids[None, :] < PROMPT) | same_run)


def dot_plain(left, right):
    return lax.dot_general(left, right, (((1,), (0,)), ((), ())), preferred_element_type=jnp.float32)


def dot_right(left, right):
    return lax.dot_general(left, right, (((1,), (1,)), ((), ())), preferred_element_type=jnp.float32)


def dot_left(left, right):
    return lax.dot_general(left, right, (((0,), (0,)), ((), ())), preferred_element_type=jnp.float32)


ANYWHERE = pl.BlockSpec(memory_space=pl.ANY)
INSIDE = pl.BlockSpec(memory_space=pltpu.VMEM)
SCALARS = pl.BlockSpec(memory_space=pltpu.SMEM)
VMEM_BYTES = 62 * 1024 * 1024


def cost(flops, *arrays):
    return pl.CostEstimate(flops=1, bytes_accessed=1, transcendentals=0)


def weight_copies(spots, pieces, target, sems):
    copies = []
    for p, piece in enumerate(pieces):
        blocks, rows = piece.shape[0], piece.shape[1]
        for k in range(blocks):
            place = pl.multiple_of(spots[p, k] * rows, rows)
            copies.append(
                pltpu.make_async_copy(
                    piece.at[k], target.at[pl.ds(place, rows)], sems.at[p * blocks + k]
                )
            )
    return copies


def block_copies(blocks, target, sems, first, columns=None):
    copies = []
    start = 0
    for i, block in enumerate(blocks):
        rows = block.shape[0]
        source = block if columns is None else block.at[:, columns]
        copies.append(
            pltpu.make_async_copy(source, target.at[pl.ds(start, rows)], sems.at[first + i])
        )
        start += rows
    return copies


def swap_halves(values):
    half = HEAD_DIM // 2
    lane = lax.broadcasted_iota(jnp.int32, values.shape, 1)
    return jnp.where(
        lane % HEAD_DIM < half,
        pltpu.roll(values, 2 * HEAD_DIM - half, 1),
        pltpu.roll(values, half, 1),
    )


def mean_square_scale(values):
    return lax.rsqrt(jnp.mean(values * values, axis=-1, keepdims=True) + EPS)


def enter_kernel(count, gain_at, spots, tokens, cosine, sine, *refs):
    pieces = refs[:count]
    normed, query, keyval, small, weight, sems = refs[count:]
    low = jnp.bfloat16
    copies = weight_copies(spots, pieces, weight, sems)
    for copy in copies:
        copy.start()
    inputs = tokens[...].astype(jnp.float32)
    scaled = inputs * mean_square_scale(inputs)
    for copy in copies:
        copy.wait()
    query_width = query.shape[1]
    kv_width = keyval.shape[1] // 2
    qkv_width = query_width + 2 * kv_width
    turned = weight[:, qkv_width:].astype(jnp.float32).T
    small[...] = turned
    rows = (scaled * turned[gain_at : gain_at + 1]).astype(low)
    normed[...] = rows
    pair = 2 * HEAD_DIM
    scale = HEAD_DIM**-0.5
    for start in range(0, query_width + kv_width, 512):
        product_part = dot_plain(rows, weight[:, start : start + 512])
        for offset in range(0, 512, pair):
            part = product_part[:, offset : offset + pair]
            part = part * cosine[...] + swap_halves(part) * sine[...]
            at = start + offset
            if at < query_width:
                query[:, at : at + pair] = (part * scale).astype(low)
            else:
                keyval[:, at - query_width : at - query_width + pair] = part.astype(low)
    keyval[:, kv_width:] = dot_plain(
        rows, weight[:, query_width + kv_width : qkv_width]
    ).astype(low)


def enter(tokens, cosine, sine, pieces, spots, gain_at, query_width, kv_width):
    rows, width = tokens.shape
    columns = pieces[0].shape[2]
    low = jnp.bfloat16
    return pl.pallas_call(
        partial(enter_kernel, len(pieces), gain_at),
        in_specs=[SCALARS, INSIDE, INSIDE, INSIDE] + [ANYWHERE] * len(pieces),
        out_specs=[INSIDE] * 4,
        out_shape=[
            jax.ShapeDtypeStruct((rows, width), low),
            jax.ShapeDtypeStruct((rows, query_width), low),
            jax.ShapeDtypeStruct((rows, 2 * kv_width), low),
            jax.ShapeDtypeStruct((columns - query_width - 2 * kv_width, width), jnp.float32),
        ],
        scratch_shapes=[
            pltpu.VMEM((width, columns), low),
            pltpu.SemaphoreType.DMA((len(pieces) * pieces[0].shape[0],)),
        ],
        compiler_params=pltpu.CompilerParams(vmem_limit_bytes=VMEM_BYTES),
        cost_estimate=cost(2 * rows * width * columns, *pieces),
        name="enter",
    )(spots, tokens, cosine, sine, *pieces)


def both_places(values):
    wide = values.astype(jnp.float32)
    low_lane = lax.broadcasted_iota(jnp.int32, values.shape, 1) < HEAD_DIM
    moved = pltpu.roll(wide, HEAD_DIM, 1)
    kind = values.dtype
    return [
        [jnp.where(low_lane, wide, 0.0).astype(kind), jnp.where(low_lane, 0.0, moved).astype(kind)],
        [jnp.where(low_lane, moved, 0.0).astype(kind), jnp.where(low_lane, 0.0, wide).astype(kind)],
    ]


def attend_kernel(query, keyval, bias, attended, log_totals):
    low = jnp.bfloat16
    rows = query.shape[0]
    kv_width = keyval.shape[1] // 2
    pair_lanes = 2 * HEAD_DIM
    repeat = HEADS // KV_HEADS
    log_totals[...] = jnp.zeros_like(log_totals)
    lane = lax.broadcasted_iota(jnp.int32, log_totals.shape, 1)

    @pl.loop(0, KV_HEADS // 2)
    def _(pair):
        at = pl.ds(pl.multiple_of(pair * pair_lanes, pair_lanes), pair_lanes)
        keys = both_places(keyval[:, at])
        at = pl.ds(pl.multiple_of(kv_width + pair * pair_lanes, pair_lanes), pair_lanes)
        values = both_places(keyval[:, at])
        for i in range(repeat):
            at = pl.ds(pl.multiple_of((pair * repeat + i) * pair_lanes, pair_lanes), pair_lanes)
            queries = query[:, at]
            total = jnp.zeros((rows, pair_lanes), jnp.float32)
            for a in range(2):
                head = 2 * i + a
                scores = dot_right(queries, keys[head // repeat][a]) + bias[...]
                peak = jnp.max(scores, axis=-1, keepdims=True)
                lifted = jnp.exp(scores - peak)
                row_total = jnp.sum(lifted, axis=-1, keepdims=True)
                weights_low = (lifted * (1.0 / row_total)).astype(low)
                total += dot_plain(weights_low, values[head // repeat][a])
                log_totals[...] = jnp.where(
                    lane == pair * (2 * repeat) + head, peak + jnp.log(row_total), log_totals[...]
                )
            attended[:, at] = total.astype(low)


def attend(query, keyval, bias):
    rows, query_width = query.shape
    return pl.pallas_call(
        attend_kernel,
        in_specs=[INSIDE] * 3,
        out_specs=[INSIDE] * 2,
        out_shape=[
            jax.ShapeDtypeStruct((rows, query_width), jnp.bfloat16),
            jax.ShapeDtypeStruct((rows, 128), jnp.float32),
        ],
        compiler_params=pltpu.CompilerParams(vmem_limit_bytes=VMEM_BYTES),
        cost_estimate=cost(8 * rows * query_width * bias.shape[1], query, keyval, bias),
        name="attend",
    )(query, keyval, bias)


def project_kernel(count, gain_at, spots, attended, tokens, small, member, kept, *refs):
    pieces = refs[:count]
    residual, sent, gate_rows, weight, sems = refs[count:]
    low = jnp.bfloat16
    width = tokens.shape[1]
    copies = weight_copies(spots, pieces, weight, sems)
    for copy in copies:
        copy.start()
    for copy in copies:
        copy.wait()
    hidden = tokens[...].astype(jnp.float32) + dot_plain(attended[...], weight[...])
    residual[...] = hidden
    gain = small[gain_at : gain_at + 1, :]
    normed = (hidden * mean_square_scale(hidden) * gain).astype(low)
    logits = dot_right(normed, small[...].astype(low))
    chosen = member[...] > 0.0
    logits = jnp.where(chosen, logits, -1e30)
    lifted = jnp.where(chosen, jnp.exp(logits - jnp.max(logits, axis=-1, keepdims=True)), 0.0)
    gates = lifted / jnp.sum(lifted, axis=-1, keepdims=True)
    gate_rows[...] = gates
    sent[:, :width] = normed
    sent[:, width:] = (gates * kept[...]).astype(low)


def project(attended, tokens, small, member, kept, gain_at, pieces, spots):
    rows, width = tokens.shape
    lanes = small.shape[0]
    low = jnp.bfloat16
    return pl.pallas_call(
        partial(project_kernel, len(pieces), gain_at),
        in_specs=[SCALARS] + [INSIDE] * 5 + [ANYWHERE] * len(pieces),
        out_specs=[INSIDE] * 3,
        out_shape=[
            jax.ShapeDtypeStruct((rows, width), jnp.float32),
            jax.ShapeDtypeStruct((rows, width + lanes), low),
            jax.ShapeDtypeStruct((rows, lanes), jnp.float32),
        ],
        scratch_shapes=[
            pltpu.VMEM((attended.shape[1], width), low),
            pltpu.SemaphoreType.DMA((len(pieces) * pieces[0].shape[0],)),
        ],
        compiler_params=pltpu.CompilerParams(vmem_limit_bytes=VMEM_BYTES),
        cost_estimate=cost(2 * rows * width * width, *pieces),
        name="project",
    )(spots, attended, tokens, small, member, kept, *pieces)


def grad_shapes(cut, rows, columns):
    low = jnp.bfloat16
    if cut:
        block = rows // 32
        return (
            [jax.ShapeDtypeStruct((4, 4, block, columns), low)] * 2,
            pltpu.VMEM((4, 2, 4, block, columns), low),
        )
    return (
        [jax.ShapeDtypeStruct((1, 1, 1, rows, columns), low)],
        pltpu.VMEM((1, 1, 1, rows, columns), low),
    )


def grad_copies(cut, place, source, outs, sems):
    if not cut:
        return [pltpu.make_async_copy(source, outs[0], sems.at[0])]
    core, member = place[0], place[1]
    other, own = outs
    copies = []
    for r in range(4):
        copies.append(
            pltpu.make_async_copy(
                source.at[:, 1 - core, member ^ r], other.at[r], sems.at[2 * r]
            )
        )
        copies.append(
            pltpu.make_async_copy(source.at[:, core, member ^ r], own.at[r], sems.at[2 * r + 1])
        )
    return copies


def turn_kernel(
    count,
    cut,
    gain_at,
    place,
    spots,
    normed_grad,
    residual,
    grad_out,
    small,
    gate_rows,
    member,
    kept,
    normed,
    attended,
    *refs,
):
    pieces = refs[:count]
    refs = refs[count:]
    outs = refs[: (2 if cut else 1)]
    resid_grad, head_grad, weight, weight_grad, sems, out_sems = refs[len(outs) :]
    low = jnp.bfloat16
    rows, width = residual.shape
    lanes = gate_rows.shape[1]
    copies = weight_copies(spots, pieces, weight, sems)
    for copy in copies:
        copy.start()
    lane = lax.broadcasted_iota(jnp.int32, (rows, lanes), 1)
    gates = gate_rows[...]
    gate_grads = normed_grad[:, width:] * kept[...]
    chosen_grad = gates * (gate_grads - jnp.sum(gates * gate_grads, axis=-1, keepdims=True))
    logit_grad = (chosen_grad * member[...]).astype(low)
    hidden = residual[...]
    scale = mean_square_scale(hidden)
    row_grad = normed_grad[:, :width] + dot_plain(logit_grad, small[...].astype(low))
    gain = small[gain_at : gain_at + 1, :]
    scaled = row_grad * gain
    total_grad = (
        grad_out[...].astype(jnp.float32)
        + scale * scaled
        - hidden * (scale * scale * scale) * jnp.mean(scaled * hidden, axis=-1, keepdims=True)
    )
    resid_grad[...] = total_grad
    attn_grad = total_grad.astype(low)
    shape = weight_grad.shape[:-1]
    gain_grad = (row_grad * hidden * scale).astype(low)
    picks = jnp.where(lane == gain_at, 1.0, 0.0).astype(low)
    weight_grad[..., width:] = (
        (dot_left(normed[...][:, :width], logit_grad) + dot_left(gain_grad, picks))
        .astype(low)
        .reshape(shape + (lanes,))
    )
    for start in range(0, width, 512):
        weight_grad[..., start : start + 512] = (
            dot_left(attended[...], attn_grad[:, start : start + 512])
            .astype(low)
            .reshape(shape + (512,))
        )
    out_copies = grad_copies(cut, place, weight_grad, outs, out_sems)
    for copy in out_copies:
        copy.start()
    for copy in copies:
        copy.wait()
    head_grad[...] = dot_right(attn_grad, weight[...]).astype(low)
    for copy in out_copies:
        copy.wait()


def turn(place, spots, operands, pieces, cut, gain_at):
    residual, gate_rows, attended = operands[1], operands[4], operands[8]
    rows, width = residual.shape
    query_width = attended.shape[1]
    low = jnp.bfloat16
    grads, held = grad_shapes(cut, query_width, width + gate_rows.shape[1])
    return pl.pallas_call(
        partial(turn_kernel, len(pieces), cut, gain_at),
        in_specs=[SCALARS, SCALARS] + [INSIDE] * len(operands) + [ANYWHERE] * len(pieces),
        out_specs=[ANYWHERE] * len(grads) + [INSIDE] * 2,
        out_shape=grads
        + [
            jax.ShapeDtypeStruct((rows, width), jnp.float32),
            jax.ShapeDtypeStruct((rows, query_width), low),
        ],
        scratch_shapes=[
            pltpu.VMEM((query_width, width), low),
            held,
            pltpu.SemaphoreType.DMA((len(pieces) * pieces[0].shape[0],)),
            pltpu.SemaphoreType.DMA((8,)),
        ],
        compiler_params=pltpu.CompilerParams(vmem_limit_bytes=VMEM_BYTES),
        cost_estimate=cost(0),
        name="turn",
    )(place, spots, *operands, *pieces)


def attend_back_kernel(
    head_grad, query, keyval, bias, log_totals, cosine, sine, query_grad, keyval_grad, totals
):
    low = jnp.bfloat16
    rows = query.shape[0]
    kv_width = keyval.shape[1] // 2
    pair_lanes = 2 * HEAD_DIM
    repeat = HEADS // KV_HEADS
    totals[...] = log_totals[...].T

    @pl.loop(0, KV_HEADS // 2)
    def _(pair):
        key_at = pl.ds(pl.multiple_of(pair * pair_lanes, pair_lanes), pair_lanes)
        value_at = pl.ds(pl.multiple_of(kv_width + pair * pair_lanes, pair_lanes), pair_lanes)
        keys = both_places(keyval[:, key_at])
        values = both_places(keyval[:, value_at])
        key_grads = [[None, None], [None, None]]
        value_grads = [[None, None], [None, None]]
        for i in range(repeat):
            at = pl.ds(pl.multiple_of((pair * repeat + i) * pair_lanes, pair_lanes), pair_lanes)
            queries = query[:, at]
            grads = head_grad[:, at]
            query_part = jnp.zeros((rows, pair_lanes), jnp.float32)
            for a in range(2):
                head = 2 * i + a
                g = head // repeat
                total = totals[pl.ds(pair * (2 * repeat) + head, 1), :]
                weights = jnp.exp(dot_right(keys[g][a], queries) + bias[...] - total)
                weight_grads = dot_right(values[g][a], grads)
                delta = jnp.sum(weights * weight_grads, axis=0, keepdims=True)
                score_grads = (weights * (weight_grads - delta)).astype(low)
                value_part = dot_plain(weights.astype(low), grads)
                key_part = dot_plain(score_grads, queries)
                query_part += dot_left(score_grads, keys[g][a])
                if key_grads[g][a] is None:
                    key_grads[g][a], value_grads[g][a] = key_part, value_part
                else:
                    key_grads[g][a] += key_part
                    value_grads[g][a] += value_part
            query_part = query_part * (HEAD_DIM**-0.5)
            query_part = query_part * cosine[...] - swap_halves(query_part) * sine[...]
            query_grad[:, at] = query_part.astype(low)
        low_lane = lax.broadcasted_iota(jnp.int32, (keyval.shape[0], pair_lanes), 1) < HEAD_DIM
        for at, found in ((key_at, key_grads), (value_at, value_grads)):
            keyval_grad[:, at] = jnp.where(
                low_lane,
                found[0][0] + pltpu.roll(found[0][1], HEAD_DIM, 1),
                pltpu.roll(found[1][0], HEAD_DIM, 1) + found[1][1],
            ).astype(low)


def attend_back(head_grad, query, keyval, bias, log_totals, cosine, sine):
    rows, query_width = query.shape
    low = jnp.bfloat16
    return pl.pallas_call(
        attend_back_kernel,
        in_specs=[INSIDE] * 7,
        out_specs=[INSIDE] * 2,
        out_shape=[
            jax.ShapeDtypeStruct((rows, query_width), low),
            jax.ShapeDtypeStruct(keyval.shape, low),
        ],
        scratch_shapes=[pltpu.VMEM((128, rows), jnp.float32)],
        compiler_params=pltpu.CompilerParams(vmem_limit_bytes=VMEM_BYTES),
        cost_estimate=cost(0),
        name="attend_back",
    )(head_grad, query, keyval, bias, log_totals, cosine, sine)


def leave_kernel(
    count,
    cut,
    gain_at,
    place,
    spots,
    keyval_sum,
    query_grad,
    normed,
    tokens,
    resid_grad,
    small,
    cosine,
    sine,
    *refs,
):
    pieces = refs[:count]
    refs = refs[count:]
    outs = refs[: (2 if cut else 1)]
    input_grad, weight, weight_grad, joined, sems, out_sems = refs[len(outs) :]
    low = jnp.bfloat16
    rows, width = tokens.shape
    query_width = query_grad.shape[1]
    kv_width = keyval_sum.shape[1] // 2
    qkv_width = query_width + 2 * kv_width
    pair = 2 * HEAD_DIM
    copies = weight_copies(spots, pieces, weight, sems)
    for copy in copies:
        copy.start()
    joined[:, :query_width] = query_grad[...]
    for start in range(0, kv_width, pair):
        part = keyval_sum[:, start : start + pair]
        part = part * cosine[...] - swap_halves(part) * sine[...]
        joined[:, query_width + start : query_width + start + pair] = part.astype(low)
    joined[:, query_width + kv_width :] = keyval_sum[:, kv_width:].astype(low)
    shape = weight_grad.shape[:-1]
    for start in range(0, qkv_width, 512):
        weight_grad[..., start : start + 512] = (
            dot_left(normed[...], joined[:, start : start + 512]).astype(low).reshape(shape + (512,))
        )
    for copy in copies:
        copy.wait()
    row_grad = dot_right(joined[...], weight[:, :qkv_width])
    inputs = tokens[...].astype(jnp.float32)
    scale = mean_square_scale(inputs)
    lanes = weight_grad.shape[-1] - qkv_width
    lane = lax.broadcasted_iota(jnp.int32, (rows, lanes), 1)
    picks = jnp.where(lane == gain_at, 1.0, 0.0).astype(low)
    weight_grad[..., qkv_width:] = (
        dot_left((row_grad * inputs * scale).astype(low), picks).astype(low).reshape(shape + (lanes,))
    )
    out_copies = grad_copies(cut, place, weight_grad, outs, out_sems)
    for copy in out_copies:
        copy.start()
    scaled = row_grad * small[gain_at : gain_at + 1, :]
    input_grad[...] = (
        resid_grad[...]
        + scale * scaled
        - inputs * (scale * scale * scale) * jnp.mean(scaled * inputs, axis=-1, keepdims=True)
    )
    for copy in out_copies:
        copy.wait()


def leave(place, spots, operands, pieces, cut, gain_at):
    tokens, query_grad, keyval_sum = operands[3], operands[1], operands[0]
    rows, width = tokens.shape
    columns = pieces[0].shape[2]
    low = jnp.bfloat16
    grads, held = grad_shapes(cut, width, columns)
    return pl.pallas_call(
        partial(leave_kernel, len(pieces), cut, gain_at),
        in_specs=[SCALARS, SCALARS] + [INSIDE] * len(operands) + [ANYWHERE] * len(pieces),
        out_specs=[ANYWHERE] * len(grads) + [INSIDE],
        out_shape=grads + [jax.ShapeDtypeStruct((rows, width), jnp.float32)],
        scratch_shapes=[
            pltpu.VMEM((width, columns), low),
            held,
            pltpu.VMEM((rows, query_grad.shape[1] + keyval_sum.shape[1]), low),
            pltpu.SemaphoreType.DMA((len(pieces) * pieces[0].shape[0],)),
            pltpu.SemaphoreType.DMA((8,)),
        ],
        compiler_params=pltpu.CompilerParams(vmem_limit_bytes=VMEM_BYTES),
        cost_estimate=cost(0),
        name="leave",
    )(place, spots, *operands, *pieces)


def expert_kernel(cut, carried, last, row_blocks, grad_blocks, row_tile, place, first, packed, *refs):
    blocks_in = refs[:row_blocks]
    grads_in = refs[row_blocks : row_blocks + grad_blocks]
    refs = refs[row_blocks + grad_blocks :]
    if carried:
        mix_in, turn_in = refs[:2]
        refs = refs[2:]
    count = packed.shape[2]
    outs = 4 if cut else 1
    packed_grads = refs[:outs]
    mix_out, turn_out = refs[outs : outs + 2]
    refs = refs[outs + 2 :]
    if last:
        mix, turned = refs[:2]
        refs = refs[2:]
    else:
        mix, turned = mix_out, turn_out
    (
        rows,
        grads,
        gates,
        gate_w,
        up_w,
        down_w,
        gate_g,
        up_g,
        down_g,
        weighted,
        gate_side,
        up_side,
        load_sems,
        save_sems,
        carry_sems,
    ) = refs
    hidden_width = gate_w.shape[-1]
    total_rows, width = rows.shape
    lanes = gates.shape[1]
    low = jnp.bfloat16

    def sides(gate, up, down):
        for side, inner in ((0, gate), (1, up)):
            for j in range(3):
                yield side, pl.ds(j * hidden_width, hidden_width), inner, j
        yield 2, pl.ds(0, width), down, None

    def loads(e):
        slot = e % 2
        copies = []
        for i, (side, columns, inner, j) in enumerate(sides(gate_w, up_w, down_w)):
            outer = packed.at[:, side, e, :, columns]
            inner = inner.at[slot] if j is None else inner.at[slot, :, j]
            copies.append(pltpu.make_async_copy(outer, inner, load_sems.at[slot, i]))
        return copies

    def saves(e):
        slot = e % 2
        copies = []
        for i, (side, columns, inner, j) in enumerate(sides(gate_g, up_g, down_g)):
            if not cut:
                outer = packed_grads[0].at[:, side, e, :, columns]
                source = inner.at[slot] if j is None else inner.at[slot, :, j]
                copies.append(pltpu.make_async_copy(source, outer, save_sems.at[slot, i]))
                continue
            own, rest, far, near = packed_grads
            targets = [own, rest.at[0], rest.at[1], rest.at[2]]
            targets += [near.at[1], near.at[0], far.at[0], far.at[1]]
            for n, target in enumerate(targets):
                block = 2 * lax.rem(place[2] + n % 4, 4) + (place[0] ^ (n // 4))
                source = inner.at[slot, block] if j is None else inner.at[slot, block, j]
                outer = target.at[side, e, :, columns]
                copies.append(pltpu.make_async_copy(source, outer, save_sems.at[slot, 8 * i + n]))
        return copies

    carries = (
        block_copies(grads_in, grads, carry_sems, 0, pl.ds(0, width))
        + block_copies(blocks_in, rows, carry_sems, grad_blocks, pl.ds(0, width))
        + block_copies(
            blocks_in, gates, carry_sems, grad_blocks + row_blocks, pl.ds(width, lanes)
        )
    )
    sums = []
    if carried:
        at = grad_blocks + 2 * row_blocks
        sums = [
            pltpu.make_async_copy(mix_in, mix, carry_sems.at[at]),
            pltpu.make_async_copy(turn_in, turned, carry_sems.at[at + 1]),
        ]
    for copy in loads(0) + carries + sums:
        copy.start()
    for e in range(count):
        slot = e % 2
        if e + 1 < count:
            for copy in loads(e + 1):
                copy.start()
        for copy in loads(e):
            copy.wait()
        if e == 0:
            for copy in carries:
                copy.wait()
            if not carried:
                turned[:, width:] = jnp.zeros((total_rows, lanes), jnp.float32)

        @pl.loop(0, total_rows // row_tile)
        def _(tile):
            span = pl.ds(pl.multiple_of(tile * row_tile, row_tile), row_tile)
            gate_full = gate_w[slot].reshape(width, hidden_width)
            up_full = up_w[slot].reshape(width, hidden_width)
            down_full = down_w[slot].reshape(hidden_width, width)
            here = rows[span, :]
            slope = dot_right(grads[span, :], down_full)
            gate_pre = dot_plain(here, gate_full)
            up_pre = dot_plain(here, up_full)
            lane = lax.broadcasted_iota(jnp.int32, (row_tile, lanes), 1)
            chosen = lane == first[0] + e
            gate_column = jnp.sum(
                jnp.where(chosen, gates[span, :].astype(jnp.float32), 0.0), axis=1, keepdims=True
            )
            sigmoid_gate = jax.nn.sigmoid(gate_pre)
            activated = gate_pre * sigmoid_gate
            hidden = (activated * up_pre).astype(low).astype(jnp.float32)
            share = jnp.sum(hidden * slope, axis=1, keepdims=True)
            if e == 0 and sums:

                @pl.when(tile == 0)
                def _():
                    for copy in sums:
                        copy.wait()

            turned[span, width:] = jnp.where(chosen, share, turned[span, width:])
            part_weighted = (hidden * gate_column).astype(low)
            hidden_grad = slope * gate_column
            part_gate = (
                hidden_grad * up_pre * (sigmoid_gate + activated * (1.0 - sigmoid_gate))
            ).astype(low)
            part_up = (hidden_grad * activated).astype(low)
            weighted[span, :] = part_weighted
            gate_side[span, :] = part_gate
            up_side[span, :] = part_up
            mix_part = dot_plain(part_weighted, down_full)
            turn_part = dot_right(part_gate, gate_full) + dot_right(part_up, up_full)
            if e == 0 and not carried:
                mix[span, :] = mix_part
                turned[span, :width] = turn_part
            elif last and e == count - 1:
                mix_out[span, :] = (mix[span, :] + mix_part).astype(low)
                turn_out[span, :width] = (turned[span, :width] + turn_part).astype(low)
                turn_out[span, width:] = turned[span, width:].astype(low)
            else:
                mix[span, :] += mix_part
                turned[span, :width] += turn_part

        if e >= 2:
            for copy in saves(e - 2):
                copy.wait()
        down_g[slot] = dot_left(weighted[...], grads[...]).astype(low).reshape(down_g.shape[1:])
        gate_g[slot] = dot_left(rows[...], gate_side[...]).astype(low).reshape(gate_g.shape[1:])
        up_g[slot] = dot_left(rows[...], up_side[...]).astype(low).reshape(up_g.shape[1:])
        for copy in saves(e):
            copy.start()
    for e in range(max(0, count - 2), count):
        for copy in saves(e):
            copy.wait()


def expert_pass(place, first, rows, grads, packed, carry, cut, last):
    blocks, _, count, part, width = packed.shape
    hidden_width = blocks * part
    total_rows = sum(block.shape[0] for block in rows)
    lanes = rows[0].shape[1] - width
    low = jnp.bfloat16
    wide = jnp.float32
    carried = carry is not None
    flops = 18 * total_rows * count * hidden_width * width
    side = pltpu.VMEM((2, blocks, 3, part, hidden_width), low)
    sides = [side, side, pltpu.VMEM((2, blocks, part, width), low)]
    sums = [(total_rows, width), (total_rows, width + lanes)]
    one = packed.shape[1:]
    grads_out = [one, (3,) + one, (2,) + one, (2,) + one] if cut else [packed.shape]
    outs = len(grads_out)
    found = pl.pallas_call(
        partial(expert_kernel, cut, carried, last, len(rows), len(grads), min(512, total_rows)),
        in_specs=[SCALARS, SCALARS]
        + [ANYWHERE] * (1 + len(rows) + len(grads) + (2 if carried else 0)),
        out_specs=[ANYWHERE] * outs + [INSIDE, INSIDE],
        out_shape=[jax.ShapeDtypeStruct(shape, low) for shape in grads_out]
        + [jax.ShapeDtypeStruct(shape, low if last else wide) for shape in sums],
        scratch_shapes=([pltpu.VMEM(shape, wide) for shape in sums] if last else [])
        + [
            pltpu.VMEM((total_rows, width), low),
            pltpu.VMEM((total_rows, width), low),
            pltpu.VMEM((total_rows, lanes), low),
        ]
        + sides
        + sides
        + [pltpu.VMEM((total_rows, hidden_width), low)] * 3
        + [
            pltpu.SemaphoreType.DMA((2, 7)),
            pltpu.SemaphoreType.DMA((2, 56)),
            pltpu.SemaphoreType.DMA((2 * len(rows) + len(grads) + 2,)),
        ],
        compiler_params=pltpu.CompilerParams(vmem_limit_bytes=VMEM_BYTES),
        cost_estimate=cost(flops, packed, packed, *rows, *grads),
        name="experts",
    )(place, first, packed, *rows, *grads, *(carry or ()))
    return found[:outs], found[outs], found[outs + 1]


def unpack_kernel(counts, places, *refs):
    found, (gate, up, down) = refs[:-3], refs[-3:]
    found = [array if place is None else array.at[place] for array, place in zip(found, places)]
    hidden_width = gate.shape[2]
    base = 0
    at = 0
    for terms in counts:
        parts = found[at : at + terms]
        at += terms
        count, part = parts[0].shape[1], parts[0].shape[2]
        for e in range(count):
            for side in range(3):
                total = parts[0][side, e].astype(jnp.float32)
                for other in parts[1:]:
                    total += other[side, e].astype(jnp.float32)
                if side == 2:
                    down[base + e] = total
                    continue
                for j in range(3):
                    (gate, up)[side][base + e, j * part : (j + 1) * part, :] = total[
                        :, j * hidden_width : (j + 1) * hidden_width
                    ]
        base += count


def unpack(chunks, gate_shape, down_shape):
    arrays = [array for terms in chunks for array, _ in terms]
    places = [place for terms in chunks for _, place in terms]
    return pl.pallas_call(
        partial(unpack_kernel, [len(terms) for terms in chunks], places),
        in_specs=[INSIDE] * len(arrays),
        out_specs=[INSIDE] * 3,
        out_shape=[
            jax.ShapeDtypeStruct(gate_shape, jnp.float32),
            jax.ShapeDtypeStruct(gate_shape, jnp.float32),
            jax.ShapeDtypeStruct(down_shape, jnp.float32),
        ],
        compiler_params=pltpu.CompilerParams(vmem_limit_bytes=VMEM_BYTES),
        cost_estimate=cost(0),
        name="unpack",
    )(*arrays)


def cube():
    return lax.axis_size("batch") == 8 and lax.axis_size("expert") == 4


def pair_moves(size, flip):
    return [(i, i ^ flip) for i in range(size)]


def shift_moves(step):
    return [(2 * z + c, 2 * ((z + step) % 4) + c) for z in range(4) for c in range(2)]


def gather_start(rows):
    size = lax.axis_size("expert")
    if size != 4:
        stacked = lax.all_gather(rows, "expert", axis=0)
        own = lax.axis_index("expert")
        return [
            lax.dynamic_index_in_dim(stacked, own ^ r, axis=0, keepdims=False) for r in range(size)
        ]
    return [rows] + [lax.ppermute(rows, "expert", pair_moves(4, r)) for r in (1, 2)]


def gather_finish(state, events=()):
    if lax.axis_size("expert") != 4:
        return state
    first, second = after(state[1:], events)
    half = first.shape[0] // 2
    top = lax.ppermute(second[:half], "expert", pair_moves(4, 1))
    bottom = lax.ppermute(first[half:], "expert", pair_moves(4, 2))
    return state + [top, bottom]


def gather_blocks(rows):
    return gather_finish(gather_start(rows))


def scatter_start(parts):
    low = jnp.bfloat16
    if lax.axis_size("expert") != 4:
        own = lax.axis_index("expert")
        order = jnp.arange(len(parts), dtype=jnp.int32) ^ own
        stacked = jnp.take(jnp.stack(parts), order, axis=0).astype(low)
        return [lax.psum_scatter(stacked, "expert", scatter_dimension=0).astype(jnp.float32)]
    across, along = pair_moves(4, 1), pair_moves(4, 2)
    half = parts[0].shape[0] // 2
    top = lax.ppermute(parts[3][:half].astype(low), "expert", across)
    bottom = lax.ppermute(parts[3][half:].astype(low), "expert", along)
    first_top = lax.ppermute(parts[1][:half].astype(low), "expert", across)
    second_bottom = lax.ppermute(parts[2][half:].astype(low), "expert", along)
    for_first = add_low(parts[1][half:], bottom)
    for_second = add_low(parts[2][:half], top)
    return [parts[0], first_top, second_bottom, for_first, for_second]


def scatter_finish(state):
    if len(state) == 1:
        return state[0]
    own, first_top, second_bottom, for_first, for_second = state
    half = first_top.shape[0]
    second_top = lax.ppermute(for_second, "expert", pair_moves(4, 2))
    first_bottom = lax.ppermute(for_first, "expert", pair_moves(4, 1))
    return jnp.concatenate(
        [
            total_of([own[:half], first_top, second_top]),
            total_of([own[half:], first_bottom, second_bottom]),
        ],
        axis=0,
    )


def scatter_blocks(parts):
    return scatter_finish(scatter_start(parts))


def after(values, events):
    return lax.optimization_barrier((values, events))[0]


def send_parts(parts):
    if lax.axis_size("expert") != 4:
        return [scatter_blocks(parts)]
    low = jnp.bfloat16
    return [parts[0]] + [
        lax.ppermute(parts[r].astype(low), "expert", pair_moves(4, r)) for r in range(1, 4)
    ]


def total_of(parts):
    total = parts[0].astype(jnp.float32)
    for part in parts[1:]:
        total += part.astype(jnp.float32)
    return total


def shift_dense(rows, events):
    if not cube():
        return [lax.all_gather(rows, ("batch", "expert"), axis=0, tiled=True)]
    below, above = step_up(rows), step_down(rows)
    return [rows, below, step_up(after(below, (above, events))), above]


def dense_start(line, columns, events):
    found = [rows[:, columns] for rows in line]
    if not cube():
        return [found[0][None]]
    return gather_start(after(jnp.stack(found), events))


def dense_finish(state, events=(), late=()):
    if not cube():
        return state, jnp.zeros((1, 1), jnp.int32), ()
    place = lax.axis_index("batch")
    level, core = place // 2, place % 2
    member = lax.axis_index("expert")
    mine = gather_finish(state, events)
    far = mine[3:]
    mine = mine[:3] + [after(jnp.concatenate(far, axis=0), late)]
    other = [exchange_cores(block) for block in mine]
    spots = [
        [(((level + 4 - k) % 4) * 2 + (core ^ c)) * 4 + (member ^ r) for k in range(4)]
        for c in range(2)
        for r in range(4)
    ]
    return mine + other, jnp.array(spots, jnp.int32), far


def sum_chunk(packed_grad):
    return lax.psum_scatter(packed_grad, "batch", scatter_dimension=0, tiled=True)


def exchange_cores(values):
    return lax.ppermute(values, "batch", pair_moves(8, 1))


def step_up(values):
    return lax.ppermute(values, "batch", shift_moves(1))


def step_down(values):
    return lax.ppermute(values, "batch", shift_moves(3))


def add_low(*parts):
    total = parts[0].astype(jnp.float32)
    for part in parts[1:]:
        total += part.astype(jnp.float32)
    return total.astype(jnp.bfloat16)


def join_cores(own, received):
    return [add_low(own[r], received[r]) for r in range(4)]


def line_start(plane):
    level = lax.axis_index("batch") // 2
    own, up, far, down = (
        lax.dynamic_index_in_dim(plane, (level + r) % 4, axis=0, keepdims=False) for r in range(4)
    )
    return own, step_down(add_low(down)), add_low(up, step_up(add_low(far)))


def line_finish(state, events=()):
    own, down, up = state
    return total_of([own, down, step_up(after(up, events))])


def scatter_whole(found):
    values = found[0].reshape(found[0].shape[3:])
    total = lax.psum_scatter(values, ("batch", "expert"), scatter_dimension=0, tiled=True)
    return total.astype(jnp.float32)


def pack_kernel(chunks, query, key, value, small, out, gate, up, down, dense, *packed):
    start = 0
    for part in (query, key, value, small, out):
        dense[:, start : start + part.shape[1]] = part[...]
        start += part.shape[1]
    part, hidden_width = down.shape[1], gate.shape[2]
    for n, target in enumerate(packed):
        for e in range(chunks[n], chunks[n + 1]):
            for side, source in ((0, gate), (1, up)):
                for j in range(3):
                    target[side, e - chunks[n], :, j * hidden_width : (j + 1) * hidden_width] = (
                        source[e, j * part : (j + 1) * part, :]
                    )
            target[2, e - chunks[n]] = down[e]


def pack(chunks, query, key, value, small, out, gate, up, down):
    low = jnp.bfloat16
    columns = sum(part.shape[1] for part in (query, key, value, small, out))
    return pl.pallas_call(
        partial(pack_kernel, chunks),
        in_specs=[INSIDE] * 8,
        out_specs=[INSIDE] * len(chunks),
        out_shape=[jax.ShapeDtypeStruct((query.shape[0], columns), low)]
        + [
            jax.ShapeDtypeStruct((3, b - a) + down.shape[1:], low)
            for a, b in zip(chunks[:-1], chunks[1:])
        ],
        compiler_params=pltpu.CompilerParams(vmem_limit_bytes=VMEM_BYTES),
        cost_estimate=cost(0),
        name="pack",
    )(query, key, value, small, out, gate, up, down)


def local(
    tokens,
    cotangent,
    attn_gain,
    query_weight,
    key_weight,
    value_weight,
    out_weight,
    ffn_gain,
    router_weight,
    gate_weight,
    up_weight,
    down_weight,
    routes,
    ranking,
):
    low = jnp.bfloat16
    wide = jnp.float32
    query_width = HEADS * HEAD_DIM
    kv_width = KV_HEADS * HEAD_DIM
    qkv_width = query_width + 2 * kv_width
    width = tokens.shape[2]
    experts_total = router_weight.shape[1]
    extra = -(-(experts_total + 2) // 128) * 128
    first_gain, second_gain = experts_total, experts_total + 1
    local_experts = gate_weight.shape[0]
    member_count = lax.axis_size("expert")
    member_id = lax.axis_index("expert")
    local_rows = tokens.shape[1]
    group_rows = local_rows * member_count
    cut = cube()
    line_place = lax.axis_index("batch")
    place = jnp.stack([line_place % 2, member_id, line_place // 2]).astype(jnp.int32)

    route_rows = routes[0]
    rank_rows = ranking[0]
    expert_lanes = jnp.arange(extra, dtype=jnp.int32)
    member = jnp.any(route_rows[:, :, None] == expert_lanes[None, None, :], axis=1)
    marks = jnp.where(
        expert_lanes[None, :] == experts_total,
        (rank_rows // 32)[:, None],
        jnp.where(expert_lanes[None, :] == experts_total + 1, (rank_rows % 32)[:, None], member),
    ).astype(low)
    grad_out = cotangent[0]
    small_width = qkv_width + extra
    chunks = (0, 3, local_experts)
    dense_rows, *packed_own = pack(
        chunks,
        query_weight,
        key_weight,
        value_weight,
        jnp.concatenate(
            [
                router_weight,
                attn_gain[:, None],
                ffn_gain[:, None],
                jnp.zeros((query_weight.shape[0], extra - experts_total - 2), low),
            ],
            axis=1,
        ),
        out_weight,
        gate_weight,
        up_weight,
        down_weight,
    )
    row_ids = member_id * local_rows + jnp.arange(local_rows, dtype=jnp.int32)
    half_dim = HEAD_DIM // 2
    frequency = THETA ** (-jnp.arange(half_dim, dtype=wide) / half_dim)
    angles = place_of(row_ids).astype(wide)[:, None] * frequency[None, :]
    cosine = jnp.tile(jnp.cos(angles), (1, 4))
    sine_part = jnp.tile(jnp.concatenate([-jnp.sin(angles), jnp.sin(angles)], axis=1), (1, 2))
    if member_count == 4:
        away = 1 << 20
        starts = [
            jnp.where(member_id >= 1, 0, away),
            jnp.where(member_id >= 2, local_rows, away),
            member_id * local_rows,
        ]
    else:
        starts = [(member_id ^ r) * local_rows for r in range(member_count)]
    key_ids = jnp.concatenate([s + jnp.arange(local_rows, dtype=jnp.int32) for s in starts])
    bias = jnp.where(visible(row_ids, key_ids), 0.0, -1e30).astype(wide)
    bias_turned = bias.T
    tables = (cosine, sine_part, bias, bias_turned)

    line = shift_dense(dense_rows, tables)
    grad_state = gather_start(jnp.concatenate([grad_out, marks], axis=1))
    grad_blocks = gather_finish(grad_state, line[1::2])
    marks_all = jnp.concatenate([block[:, width:] for block in grad_blocks], axis=0)
    qkv_state = dense_start(line, slice(0, small_width), ())
    plane = qkv_state[1:]
    qkv_pieces, qkv_spots, far = dense_finish(qkv_state)
    out_state = dense_start(line, slice(small_width, None), far)
    packed_all = [
        lax.all_gather(after(packed, events), "batch", axis=0)
        for packed, events in zip(packed_own, ((line, grad_blocks), plane))
    ]

    normed, query, keyval, small = enter(
        tokens[0], cosine, sine_part, qkv_pieces, qkv_spots, first_gain, query_width, kv_width
    )

    rank_all = (
        marks_all[:, experts_total].astype(wide) * 32 + marks_all[:, experts_total + 1].astype(wide)
    )
    earlier = (rank_all[None, :] < rank_rows.astype(wide)[:, None]).astype(low)
    before = product(earlier, marks_all)
    capacity = 5 * group_rows * route_rows.shape[1] // (4 * experts_total)
    member = member.astype(wide)
    kept = jnp.where(before < capacity, member, 0.0)

    keyval_blocks = gather_blocks(after(keyval, out_state[1:]))
    if member_count == 4:
        ordered = keyval_blocks[:3] + [jnp.concatenate(keyval_blocks[3:], axis=0)]
        keys = jnp.concatenate(
            [
                lax.select_n(member_id, *ordered),
                lax.select_n(member_id ^ 1, *ordered),
                keyval,
            ],
            axis=0,
        )
    else:
        keys = jnp.concatenate(keyval_blocks, axis=0)
    attended, log_totals = attend(query, keys, bias)
    out_pieces, out_spots, _ = dense_finish(out_state, keyval_blocks[3:], attended)
    residual, sent, gate_rows = project(
        attended, tokens[0], small, member, kept, second_gain, out_pieces, out_spots
    )
    sent_blocks = gather_blocks(sent)

    carry, chunk_grads = None, []
    for packed, a, b in zip(packed_all, chunks[:-1], chunks[1:]):
        first = (member_id * local_experts + a).astype(jnp.int32).reshape(1)
        packed_grads, mixture_all, row_grad = expert_pass(
            place,
            first,
            sent_blocks,
            grad_blocks,
            packed,
            carry,
            cut and b == local_experts,
            b == local_experts,
        )
        carry = (mixture_all, row_grad)
        chunk_grads.append(packed_grads)

    def blocks_of(values):
        return [values[r * local_rows : (r + 1) * local_rows] for r in range(member_count)]

    totals = [sum_chunk(chunk_grads[0][0])]
    if cut:
        own, rest, far, near = chunk_grads[1]
        far, near = exchange_cores(far), exchange_cores(near)
        far_sum, down_sum = add_low(rest[1], far[0]), add_low(rest[2], far[1])
    turn_state = scatter_start(blocks_of(row_grad))
    if cut:
        turn_state = after(turn_state, (far_sum, down_sum))
    normed_grad = scatter_finish(turn_state)
    turned = turn(
        place,
        out_spots,
        (
            normed_grad,
            residual,
            grad_out,
            small,
            gate_rows,
            member,
            kept,
            sent,
            attended,
        ),
        out_pieces,
        cut,
        second_gain,
    )
    out_found = turned[:-2]
    resid_grad, head_grad = turned[-2:]
    mixture_parts = send_parts(blocks_of(after(mixture_all, normed_grad)))
    if cut:
        head_grad = after(head_grad, mixture_parts[1:3])
        up_part = step_up(far_sum)
    query_grad, key_grads = attend_back(
        head_grad, query, keys, bias_turned, log_totals, cosine, sine_part
    )
    if member_count == 4:
        zero = jnp.zeros((), low)
        for_first, for_second, for_own = blocks_of(key_grads)[:3]
        key_parts = []
        for r in range(4):
            part = jnp.where(member_id == r, for_first, zero)
            part += jnp.where(member_id ^ 1 == r, for_second, zero)
            key_parts.append(part + for_own if r == 0 else part)
    else:
        key_parts = blocks_of(key_grads)
    if cut:
        out_found = out_found[1], exchange_cores(out_found[0])
        key_parts = after(key_parts, (mixture_parts[3], up_part))
    keyval_sum = scatter_blocks(key_parts)
    if cut:
        out_state = scatter_start(join_cores(*out_found))
    if cut:
        up_sum = add_low(rest[0], near[0], up_part)
        down_term = step_down(after(down_sum, key_parts))
        keyval_sum = after(keyval_sum, (out_found, up_sum, down_term))
    left = leave(
        place,
        qkv_spots,
        (
            keyval_sum,
            query_grad,
            normed,
            tokens[0],
            resid_grad,
            small,
            cosine,
            sine_part,
        ),
        qkv_pieces,
        cut,
        first_gain,
    )
    qkv_found, input_grad = left[:-1], left[-1]
    result = (residual + total_of(mixture_parts)).astype(low)
    if cut:
        received = exchange_cores(after(qkv_found[0], (totals[0], out_state[1:])))
        out_plane = scatter_finish(out_state)
        up_term = step_up(up_sum)
        qkv_parts = join_cores(qkv_found[1], after(received, out_plane))
        qkv_plane = after(scatter_blocks(qkv_parts), up_term)
        out_sum = line_finish(line_start(out_plane))
        qkv_state = line_start(qkv_plane)
        near, down_term, up_term = after((near, down_term, up_term), qkv_plane)
        terms = [[(totals[0], 0)], [(own, None), (near, 1), (down_term, None), (up_term, None)]]
        expert_totals = unpack(terms, gate_weight.shape, down_weight.shape)
        qkv_sum = line_finish(qkv_state, expert_totals)
    else:
        out_sum = scatter_whole(out_found)
        qkv_sum = scatter_whole(qkv_found)
        totals += [sum_chunk(found[0]) for found in chunk_grads[1:]]
        terms = [[(total, 0)] for total in totals]
        expert_totals = unpack(terms, gate_weight.shape, down_weight.shape)
    gate_total, up_total, down_total = expert_totals
    return (
        result[None],
        input_grad[None],
        qkv_sum[:, qkv_width + first_gain],
        qkv_sum[:, :query_width],
        qkv_sum[:, query_width : query_width + kv_width],
        qkv_sum[:, query_width + kv_width : qkv_width],
        out_sum[:, :width],
        out_sum[:, width + second_gain],
        out_sum[:, width : width + experts_total],
        gate_total,
        up_total,
        down_total,
    )


def solution(mesh):
    return jax.shard_map(
        local,
        mesh=mesh,
        in_specs=(
            P("batch", "expert", None),
            P("batch", "expert", None),
            P(("batch", "expert")),
            P(("batch", "expert"), None),
            P(("batch", "expert"), None),
            P(("batch", "expert"), None),
            P(("batch", "expert"), None),
            P(("batch", "expert")),
            P(("batch", "expert"), None),
            P("expert", "batch", None),
            P("expert", "batch", None),
            P("expert", "batch", None),
            P("batch", "expert", None),
            P("batch", "expert"),
        ),
        out_specs=(
            P("batch", "expert", None),
            P("batch", "expert", None),
            P(("batch", "expert")),
            P(("batch", "expert"), None),
            P(("batch", "expert"), None),
            P(("batch", "expert"), None),
            P(("batch", "expert"), None),
            P(("batch", "expert")),
            P(("batch", "expert"), None),
            P("expert", "batch", None),
            P("expert", "batch", None),
            P("expert", "batch", None),
        ),
        check_vma=False,
    )
```

```python
from functools import partial

import jax
import jax.numpy as jnp
from jax import lax
from jax.experimental import pallas as pl
from jax.experimental.pallas import tpu as pltpu
from jax.sharding import PartitionSpec as P

HEADS = 24
KV_HEADS = 8
HEAD_DIM = 64
PROMPT = 512
CLEN = 256


EPS = 1e-06
THETA = 10000.0


def product(left, right):
    return jnp.dot(left, right, preferred_element_type=jnp.float32)


def place_of(row_ids):
    return jnp.where(row_ids < PROMPT, row_ids, PROMPT + (row_ids - PROMPT) % CLEN)


def visible(query_ids, key_ids):
    causal = key_ids[None, :] <= query_ids[:, None]
    same_run = (key_ids[None, :] - PROMPT) // CLEN == (query_ids[:, None] - PROMPT) // CLEN
    return causal & ((key_ids[None, :] < PROMPT) | same_run)


def dot_plain(left, right):
    return lax.dot_general(left, right, (((1,), (0,)), ((), ())), preferred_element_type=jnp.float32)


def dot_right(left, right):
    return lax.dot_general(left, right, (((1,), (1,)), ((), ())), preferred_element_type=jnp.float32)


def dot_left(left, right):
    return lax.dot_general(left, right, (((0,), (0,)), ((), ())), preferred_element_type=jnp.float32)


ANYWHERE = pl.BlockSpec(memory_space=pl.ANY)
INSIDE = pl.BlockSpec(memory_space=pltpu.VMEM)
SCALARS = pl.BlockSpec(memory_space=pltpu.SMEM)
VMEM_BYTES = 62 * 1024 * 1024


def cost(flops, *arrays):
    return pl.CostEstimate(flops=1, bytes_accessed=1, transcendentals=0)


def weight_copies(spots, pieces, target, sems):
    copies = []
    for p, piece in enumerate(pieces):
        blocks, rows = piece.shape[0], piece.shape[1]
        for k in range(blocks):
            place = pl.multiple_of(spots[p, k] * rows, rows)
            copies.append(
                pltpu.make_async_copy(
                    piece.at[k], target.at[pl.ds(place, rows)], sems.at[p * blocks + k]
                )
            )
    return copies


def block_copies(blocks, target, sems, first, columns=None):
    copies = []
    start = 0
    for i, block in enumerate(blocks):
        rows = block.shape[0]
        source = block if columns is None else block.at[:, columns]
        copies.append(
            pltpu.make_async_copy(source, target.at[pl.ds(start, rows)], sems.at[first + i])
        )
        start += rows
    return copies


def swap_halves(values):
    half = HEAD_DIM // 2
    lane = lax.broadcasted_iota(jnp.int32, values.shape, 1)
    return jnp.where(
        lane % HEAD_DIM < half,
        pltpu.roll(values, 2 * HEAD_DIM - half, 1),
        pltpu.roll(values, half, 1),
    )


def mean_square_scale(values):
    return lax.rsqrt(jnp.mean(values * values, axis=-1, keepdims=True) + EPS)


def enter_kernel(count, gain_at, spots, tokens, cosine, sine, *refs):
    pieces = refs[:count]
    normed, query, keyval, small, weight, sems = refs[count:]
    low = jnp.bfloat16
    copies = weight_copies(spots, pieces, weight, sems)
    for copy in copies:
        copy.start()
    inputs = tokens[...].astype(jnp.float32)
    scaled = inputs * mean_square_scale(inputs)
    for copy in copies:
        copy.wait()
    query_width = query.shape[1]
    kv_width = keyval.shape[1] // 2
    qkv_width = query_width + 2 * kv_width
    turned = weight[:, qkv_width:].astype(jnp.float32).T
    small[...] = turned
    rows = (scaled * turned[gain_at : gain_at + 1]).astype(low)
    normed[...] = rows
    pair = 2 * HEAD_DIM
    scale = HEAD_DIM**-0.5
    for start in range(0, query_width + kv_width, 512):
        product_part = dot_plain(rows, weight[:, start : start + 512])
        for offset in range(0, 512, pair):
            part = product_part[:, offset : offset + pair]
            part = part * cosine[...] + swap_halves(part) * sine[...]
            at = start + offset
            if at < query_width:
                query[:, at : at + pair] = (part * scale).astype(low)
            else:
                keyval[:, at - query_width : at - query_width + pair] = part.astype(low)
    keyval[:, kv_width:] = dot_plain(
        rows, weight[:, query_width + kv_width : qkv_width]
    ).astype(low)


def enter(tokens, cosine, sine, pieces, spots, gain_at, query_width, kv_width):
    rows, width = tokens.shape
    columns = pieces[0].shape[2]
    low = jnp.bfloat16
    return pl.pallas_call(
        partial(enter_kernel, len(pieces), gain_at),
        in_specs=[SCALARS, INSIDE, INSIDE, INSIDE] + [ANYWHERE] * len(pieces),
        out_specs=[INSIDE] * 4,
        out_shape=[
            jax.ShapeDtypeStruct((rows, width), low),
            jax.ShapeDtypeStruct((rows, query_width), low),
            jax.ShapeDtypeStruct((rows, 2 * kv_width), low),
            jax.ShapeDtypeStruct((columns - query_width - 2 * kv_width, width), jnp.float32),
        ],
        scratch_shapes=[
            pltpu.VMEM((width, columns), low),
            pltpu.SemaphoreType.DMA((len(pieces) * pieces[0].shape[0],)),
        ],
        compiler_params=pltpu.CompilerParams(vmem_limit_bytes=VMEM_BYTES),
        cost_estimate=cost(2 * rows * width * columns, *pieces),
        name="enter",
    )(spots, tokens, cosine, sine, *pieces)


def both_places(values):
    wide = values.astype(jnp.float32)
    low_lane = lax.broadcasted_iota(jnp.int32, values.shape, 1) < HEAD_DIM
    moved = pltpu.roll(wide, HEAD_DIM, 1)
    kind = values.dtype
    return [
        [jnp.where(low_lane, wide, 0.0).astype(kind), jnp.where(low_lane, 0.0, moved).astype(kind)],
        [jnp.where(low_lane, moved, 0.0).astype(kind), jnp.where(low_lane, 0.0, wide).astype(kind)],
    ]


def attend_kernel(query, keyval, bias, attended, log_totals):
    low = jnp.bfloat16
    rows = query.shape[0]
    kv_width = keyval.shape[1] // 2
    pair_lanes = 2 * HEAD_DIM
    repeat = HEADS // KV_HEADS
    log_totals[...] = jnp.zeros_like(log_totals)
    lane = lax.broadcasted_iota(jnp.int32, log_totals.shape, 1)

    @pl.loop(0, KV_HEADS // 2)
    def _(pair):
        at = pl.ds(pl.multiple_of(pair * pair_lanes, pair_lanes), pair_lanes)
        keys = both_places(keyval[:, at])
        at = pl.ds(pl.multiple_of(kv_width + pair * pair_lanes, pair_lanes), pair_lanes)
        values = both_places(keyval[:, at])
        for i in range(repeat):
            at = pl.ds(pl.multiple_of((pair * repeat + i) * pair_lanes, pair_lanes), pair_lanes)
            queries = query[:, at]
            total = jnp.zeros((rows, pair_lanes), jnp.float32)
            for a in range(2):
                head = 2 * i + a
                scores = dot_right(queries, keys[head // repeat][a]) + bias[...]
                peak = jnp.max(scores, axis=-1, keepdims=True)
                lifted = jnp.exp(scores - peak)
                row_total = jnp.sum(lifted, axis=-1, keepdims=True)
                weights_low = (lifted * (1.0 / row_total)).astype(low)
                total += dot_plain(weights_low, values[head // repeat][a])
                log_totals[...] = jnp.where(
                    lane == pair * (2 * repeat) + head, peak + jnp.log(row_total), log_totals[...]
                )
            attended[:, at] = total.astype(low)


def attend(query, keyval, bias):
    rows, query_width = query.shape
    return pl.pallas_call(
        attend_kernel,
        in_specs=[INSIDE] * 3,
        out_specs=[INSIDE] * 2,
        out_shape=[
            jax.ShapeDtypeStruct((rows, query_width), jnp.bfloat16),
            jax.ShapeDtypeStruct((rows, 128), jnp.float32),
        ],
        compiler_params=pltpu.CompilerParams(vmem_limit_bytes=VMEM_BYTES),
        cost_estimate=cost(8 * rows * query_width * bias.shape[1], query, keyval, bias),
        name="attend",
    )(query, keyval, bias)


def project_kernel(count, gain_at, spots, attended, tokens, small, member, kept, *refs):
    pieces = refs[:count]
    residual, sent, gate_rows, weight, sems = refs[count:]
    low = jnp.bfloat16
    width = tokens.shape[1]
    copies = weight_copies(spots, pieces, weight, sems)
    for copy in copies:
        copy.start()
    for copy in copies:
        copy.wait()
    hidden = tokens[...].astype(jnp.float32) + dot_plain(attended[...], weight[...])
    residual[...] = hidden
    gain = small[gain_at : gain_at + 1, :]
    normed = (hidden * mean_square_scale(hidden) * gain).astype(low)
    logits = dot_right(normed, small[...].astype(low))
    chosen = member[...] > 0.0
    logits = jnp.where(chosen, logits, -1e30)
    lifted = jnp.where(chosen, jnp.exp(logits - jnp.max(logits, axis=-1, keepdims=True)), 0.0)
    gates = lifted / jnp.sum(lifted, axis=-1, keepdims=True)
    gate_rows[...] = gates
    sent[:, :width] = normed
    sent[:, width:] = (gates * kept[...]).astype(low)


def project(attended, tokens, small, member, kept, gain_at, pieces, spots):
    rows, width = tokens.shape
    lanes = small.shape[0]
    low = jnp.bfloat16
    return pl.pallas_call(
        partial(project_kernel, len(pieces), gain_at),
        in_specs=[SCALARS] + [INSIDE] * 5 + [ANYWHERE] * len(pieces),
        out_specs=[INSIDE] * 3,
        out_shape=[
            jax.ShapeDtypeStruct((rows, width), jnp.float32),
            jax.ShapeDtypeStruct((rows, width + lanes), low),
            jax.ShapeDtypeStruct((rows, lanes), jnp.float32),
        ],
        scratch_shapes=[
            pltpu.VMEM((attended.shape[1], width), low),
            pltpu.SemaphoreType.DMA((len(pieces) * pieces[0].shape[0],)),
        ],
        compiler_params=pltpu.CompilerParams(vmem_limit_bytes=VMEM_BYTES),
        cost_estimate=cost(2 * rows * width * width, *pieces),
        name="project",
    )(spots, attended, tokens, small, member, kept, *pieces)


def grad_shapes(cut, rows, columns):
    low = jnp.bfloat16
    if cut:
        block = rows // 32
        return (
            [jax.ShapeDtypeStruct((4, 4, block, columns), low)] * 2,
            pltpu.VMEM((4, 2, 4, block, columns), low),
        )
    return (
        [jax.ShapeDtypeStruct((1, 1, 1, rows, columns), low)],
        pltpu.VMEM((1, 1, 1, rows, columns), low),
    )


def grad_copies(cut, place, source, outs, sems):
    if not cut:
        return [pltpu.make_async_copy(source, outs[0], sems.at[0])]
    core, member = place[0], place[1]
    other, own = outs
    copies = []
    for r in range(4):
        copies.append(
            pltpu.make_async_copy(
                source.at[:, 1 - core, member ^ r], other.at[r], sems.at[2 * r]
            )
        )
        copies.append(
            pltpu.make_async_copy(source.at[:, core, member ^ r], own.at[r], sems.at[2 * r + 1])
        )
    return copies


def turn_kernel(
    count,
    cut,
    gain_at,
    place,
    spots,
    normed_grad,
    residual,
    grad_out,
    small,
    gate_rows,
    member,
    kept,
    normed,
    attended,
    *refs,
):
    pieces = refs[:count]
    refs = refs[count:]
    outs = refs[: (2 if cut else 1)]
    resid_grad, head_grad, weight, weight_grad, sems, out_sems = refs[len(outs) :]
    low = jnp.bfloat16
    rows, width = residual.shape
    lanes = gate_rows.shape[1]
    copies = weight_copies(spots, pieces, weight, sems)
    for copy in copies:
        copy.start()
    lane = lax.broadcasted_iota(jnp.int32, (rows, lanes), 1)
    gates = gate_rows[...]
    gate_grads = normed_grad[:, width:] * kept[...]
    chosen_grad = gates * (gate_grads - jnp.sum(gates * gate_grads, axis=-1, keepdims=True))
    logit_grad = (chosen_grad * member[...]).astype(low)
    hidden = residual[...]
    scale = mean_square_scale(hidden)
    row_grad = normed_grad[:, :width] + dot_plain(logit_grad, small[...].astype(low))
    gain = small[gain_at : gain_at + 1, :]
    scaled = row_grad * gain
    total_grad = (
        grad_out[...].astype(jnp.float32)
        + scale * scaled
        - hidden * (scale * scale * scale) * jnp.mean(scaled * hidden, axis=-1, keepdims=True)
    )
    resid_grad[...] = total_grad
    attn_grad = total_grad.astype(low)
    shape = weight_grad.shape[:-1]
    gain_grad = (row_grad * hidden * scale).astype(low)
    picks = jnp.where(lane == gain_at, 1.0, 0.0).astype(low)
    weight_grad[..., width:] = (
        (dot_left(normed[...][:, :width], logit_grad) + dot_left(gain_grad, picks))
        .astype(low)
        .reshape(shape + (lanes,))
    )
    for start in range(0, width, 512):
        weight_grad[..., start : start + 512] = (
            dot_left(attended[...], attn_grad[:, start : start + 512])
            .astype(low)
            .reshape(shape + (512,))
        )
    out_copies = grad_copies(cut, place, weight_grad, outs, out_sems)
    for copy in out_copies:
        copy.start()
    for copy in copies:
        copy.wait()
    head_grad[...] = dot_right(attn_grad, weight[...]).astype(low)
    for copy in out_copies:
        copy.wait()


def turn(place, spots, operands, pieces, cut, gain_at):
    residual, gate_rows, attended = operands[1], operands[4], operands[8]
    rows, width = residual.shape
    query_width = attended.shape[1]
    low = jnp.bfloat16
    grads, held = grad_shapes(cut, query_width, width + gate_rows.shape[1])
    return pl.pallas_call(
        partial(turn_kernel, len(pieces), cut, gain_at),
        in_specs=[SCALARS, SCALARS] + [INSIDE] * len(operands) + [ANYWHERE] * len(pieces),
        out_specs=[ANYWHERE] * len(grads) + [INSIDE] * 2,
        out_shape=grads
        + [
            jax.ShapeDtypeStruct((rows, width), jnp.float32),
            jax.ShapeDtypeStruct((rows, query_width), low),
        ],
        scratch_shapes=[
            pltpu.VMEM((query_width, width), low),
            held,
            pltpu.SemaphoreType.DMA((len(pieces) * pieces[0].shape[0],)),
            pltpu.SemaphoreType.DMA((8,)),
        ],
        compiler_params=pltpu.CompilerParams(vmem_limit_bytes=VMEM_BYTES),
        cost_estimate=cost(0),
        name="turn",
    )(place, spots, *operands, *pieces)


def attend_back_kernel(
    head_grad, query, keyval, bias, log_totals, cosine, sine, query_grad, keyval_grad, totals
):
    low = jnp.bfloat16
    rows = query.shape[0]
    kv_width = keyval.shape[1] // 2
    pair_lanes = 2 * HEAD_DIM
    repeat = HEADS // KV_HEADS
    totals[...] = log_totals[...].T

    @pl.loop(0, KV_HEADS // 2)
    def _(pair):
        key_at = pl.ds(pl.multiple_of(pair * pair_lanes, pair_lanes), pair_lanes)
        value_at = pl.ds(pl.multiple_of(kv_width + pair * pair_lanes, pair_lanes), pair_lanes)
        keys = both_places(keyval[:, key_at])
        values = both_places(keyval[:, value_at])
        key_grads = [[None, None], [None, None]]
        value_grads = [[None, None], [None, None]]
        for i in range(repeat):
            at = pl.ds(pl.multiple_of((pair * repeat + i) * pair_lanes, pair_lanes), pair_lanes)
            queries = query[:, at]
            grads = head_grad[:, at]
            query_part = jnp.zeros((rows, pair_lanes), jnp.float32)
            for a in range(2):
                head = 2 * i + a
                g = head // repeat
                total = totals[pl.ds(pair * (2 * repeat) + head, 1), :]
                weights = jnp.exp(dot_right(keys[g][a], queries) + bias[...] - total)
                weight_grads = dot_right(values[g][a], grads)
                delta = jnp.sum(weights * weight_grads, axis=0, keepdims=True)
                score_grads = (weights * (weight_grads - delta)).astype(low)
                value_part = dot_plain(weights.astype(low), grads)
                key_part = dot_plain(score_grads, queries)
                query_part += dot_left(score_grads, keys[g][a])
                if key_grads[g][a] is None:
                    key_grads[g][a], value_grads[g][a] = key_part, value_part
                else:
                    key_grads[g][a] += key_part
                    value_grads[g][a] += value_part
            query_part = query_part * (HEAD_DIM**-0.5)
            query_part = query_part * cosine[...] - swap_halves(query_part) * sine[...]
            query_grad[:, at] = query_part.astype(low)
        low_lane = lax.broadcasted_iota(jnp.int32, (keyval.shape[0], pair_lanes), 1) < HEAD_DIM
        for at, found in ((key_at, key_grads), (value_at, value_grads)):
            keyval_grad[:, at] = jnp.where(
                low_lane,
                found[0][0] + pltpu.roll(found[0][1], HEAD_DIM, 1),
                pltpu.roll(found[1][0], HEAD_DIM, 1) + found[1][1],
            ).astype(low)


def attend_back(head_grad, query, keyval, bias, log_totals, cosine, sine):
    rows, query_width = query.shape
    low = jnp.bfloat16
    return pl.pallas_call(
        attend_back_kernel,
        in_specs=[INSIDE] * 7,
        out_specs=[INSIDE] * 2,
        out_shape=[
            jax.ShapeDtypeStruct((rows, query_width), low),
            jax.ShapeDtypeStruct(keyval.shape, low),
        ],
        scratch_shapes=[pltpu.VMEM((128, rows), jnp.float32)],
        compiler_params=pltpu.CompilerParams(vmem_limit_bytes=VMEM_BYTES),
        cost_estimate=cost(0),
        name="attend_back",
    )(head_grad, query, keyval, bias, log_totals, cosine, sine)


def leave_kernel(
    count,
    cut,
    gain_at,
    place,
    spots,
    keyval_sum,
    query_grad,
    normed,
    tokens,
    resid_grad,
    small,
    cosine,
    sine,
    *refs,
):
    pieces = refs[:count]
    refs = refs[count:]
    outs = refs[: (2 if cut else 1)]
    input_grad, weight, weight_grad, joined, sems, out_sems = refs[len(outs) :]
    low = jnp.bfloat16
    rows, width = tokens.shape
    query_width = query_grad.shape[1]
    kv_width = keyval_sum.shape[1] // 2
    qkv_width = query_width + 2 * kv_width
    pair = 2 * HEAD_DIM
    copies = weight_copies(spots, pieces, weight, sems)
    for copy in copies:
        copy.start()
    joined[:, :query_width] = query_grad[...]
    for start in range(0, kv_width, pair):
        part = keyval_sum[:, start : start + pair]
        part = part * cosine[...] - swap_halves(part) * sine[...]
        joined[:, query_width + start : query_width + start + pair] = part.astype(low)
    joined[:, query_width + kv_width :] = keyval_sum[:, kv_width:].astype(low)
    shape = weight_grad.shape[:-1]
    for start in range(0, qkv_width, 512):
        weight_grad[..., start : start + 512] = (
            dot_left(normed[...], joined[:, start : start + 512]).astype(low).reshape(shape + (512,))
        )
    for copy in copies:
        copy.wait()
    row_grad = dot_right(joined[...], weight[:, :qkv_width])
    inputs = tokens[...].astype(jnp.float32)
    scale = mean_square_scale(inputs)
    lanes = weight_grad.shape[-1] - qkv_width
    lane = lax.broadcasted_iota(jnp.int32, (rows, lanes), 1)
    picks = jnp.where(lane == gain_at, 1.0, 0.0).astype(low)
    weight_grad[..., qkv_width:] = (
        dot_left((row_grad * inputs * scale).astype(low), picks).astype(low).reshape(shape + (lanes,))
    )
    out_copies = grad_copies(cut, place, weight_grad, outs, out_sems)
    for copy in out_copies:
        copy.start()
    scaled = row_grad * small[gain_at : gain_at + 1, :]
    input_grad[...] = (
        resid_grad[...]
        + scale * scaled
        - inputs * (scale * scale * scale) * jnp.mean(scaled * inputs, axis=-1, keepdims=True)
    )
    for copy in out_copies:
        copy.wait()


def leave(place, spots, operands, pieces, cut, gain_at):
    tokens, query_grad, keyval_sum = operands[3], operands[1], operands[0]
    rows, width = tokens.shape
    columns = pieces[0].shape[2]
    low = jnp.bfloat16
    grads, held = grad_shapes(cut, width, columns)
    return pl.pallas_call(
        partial(leave_kernel, len(pieces), cut, gain_at),
        in_specs=[SCALARS, SCALARS] + [INSIDE] * len(operands) + [ANYWHERE] * len(pieces),
        out_specs=[ANYWHERE] * len(grads) + [INSIDE],
        out_shape=grads + [jax.ShapeDtypeStruct((rows, width), jnp.float32)],
        scratch_shapes=[
            pltpu.VMEM((width, columns), low),
            held,
            pltpu.VMEM((rows, query_grad.shape[1] + keyval_sum.shape[1]), low),
            pltpu.SemaphoreType.DMA((len(pieces) * pieces[0].shape[0],)),
            pltpu.SemaphoreType.DMA((8,)),
        ],
        compiler_params=pltpu.CompilerParams(vmem_limit_bytes=VMEM_BYTES),
        cost_estimate=cost(0),
        name="leave",
    )(place, spots, *operands, *pieces)


def expert_kernel(cut, carried, last, row_blocks, grad_blocks, row_tile, place, first, packed, *refs):
    blocks_in = refs[:row_blocks]
    grads_in = refs[row_blocks : row_blocks + grad_blocks]
    refs = refs[row_blocks + grad_blocks :]
    if carried:
        mix_in, turn_in = refs[:2]
        refs = refs[2:]
    count = packed.shape[2]
    outs = 4 if cut else 1
    packed_grads = refs[:outs]
    mix_out, turn_out = refs[outs : outs + 2]
    refs = refs[outs + 2 :]
    if last:
        mix, turned = refs[:2]
        refs = refs[2:]
    else:
        mix, turned = mix_out, turn_out
    (
        rows,
        grads,
        gates,
        gate_w,
        up_w,
        down_w,
        gate_g,
        up_g,
        down_g,
        weighted,
        gate_side,
        up_side,
        load_sems,
        save_sems,
        carry_sems,
    ) = refs
    hidden_width = gate_w.shape[-1]
    total_rows, width = rows.shape
    lanes = gates.shape[1]
    low = jnp.bfloat16

    def sides(gate, up, down):
        for side, inner in ((0, gate), (1, up)):
            for j in range(3):
                yield side, pl.ds(j * hidden_width, hidden_width), inner, j
        yield 2, pl.ds(0, width), down, None

    def loads(e):
        slot = e % 2
        copies = []
        for i, (side, columns, inner, j) in enumerate(sides(gate_w, up_w, down_w)):
            outer = packed.at[:, side, e, :, columns]
            inner = inner.at[slot] if j is None else inner.at[slot, :, j]
            copies.append(pltpu.make_async_copy(outer, inner, load_sems.at[slot, i]))
        return copies

    def saves(e):
        slot = e % 2
        copies = []
        for i, (side, columns, inner, j) in enumerate(sides(gate_g, up_g, down_g)):
            if not cut:
                outer = packed_grads[0].at[:, side, e, :, columns]
                source = inner.at[slot] if j is None else inner.at[slot, :, j]
                copies.append(pltpu.make_async_copy(source, outer, save_sems.at[slot, i]))
                continue
            own, rest, far, near = packed_grads
            targets = [own, rest.at[0], rest.at[1], rest.at[2]]
            targets += [near.at[1], near.at[0], far.at[0], far.at[1]]
            for n, target in enumerate(targets):
                block = 2 * lax.rem(place[2] + n % 4, 4) + (place[0] ^ (n // 4))
                source = inner.at[slot, block] if j is None else inner.at[slot, block, j]
                outer = target.at[side, e, :, columns]
                copies.append(pltpu.make_async_copy(source, outer, save_sems.at[slot, 8 * i + n]))
        return copies

    carries = (
        block_copies(grads_in, grads, carry_sems, 0, pl.ds(0, width))
        + block_copies(blocks_in, rows, carry_sems, grad_blocks, pl.ds(0, width))
        + block_copies(
            blocks_in, gates, carry_sems, grad_blocks + row_blocks, pl.ds(width, lanes)
        )
    )
    sums = []
    if carried:
        at = grad_blocks + 2 * row_blocks
        sums = [
            pltpu.make_async_copy(mix_in, mix, carry_sems.at[at]),
            pltpu.make_async_copy(turn_in, turned, carry_sems.at[at + 1]),
        ]
    for copy in loads(0) + carries + sums:
        copy.start()
    for e in range(count):
        slot = e % 2
        if e + 1 < count:
            for copy in loads(e + 1):
                copy.start()
        for copy in loads(e):
            copy.wait()
        if e == 0:
            for copy in carries:
                copy.wait()
            if not carried:
                turned[:, width:] = jnp.zeros((total_rows, lanes), jnp.float32)

        @pl.loop(0, total_rows // row_tile)
        def _(tile):
            span = pl.ds(pl.multiple_of(tile * row_tile, row_tile), row_tile)
            gate_full = gate_w[slot].reshape(width, hidden_width)
            up_full = up_w[slot].reshape(width, hidden_width)
            down_full = down_w[slot].reshape(hidden_width, width)
            here = rows[span, :]
            slope = dot_right(grads[span, :], down_full)
            gate_pre = dot_plain(here, gate_full)
            up_pre = dot_plain(here, up_full)
            lane = lax.broadcasted_iota(jnp.int32, (row_tile, lanes), 1)
            chosen = lane == first[0] + e
            gate_column = jnp.sum(
                jnp.where(chosen, gates[span, :].astype(jnp.float32), 0.0), axis=1, keepdims=True
            )
            sigmoid_gate = jax.nn.sigmoid(gate_pre)
            activated = gate_pre * sigmoid_gate
            hidden = (activated * up_pre).astype(low).astype(jnp.float32)
            share = jnp.sum(hidden * slope, axis=1, keepdims=True)
            if e == 0 and sums:

                @pl.when(tile == 0)
                def _():
                    for copy in sums:
                        copy.wait()

            turned[span, width:] = jnp.where(chosen, share, turned[span, width:])
            part_weighted = (hidden * gate_column).astype(low)
            hidden_grad = slope * gate_column
            part_gate = (
                hidden_grad * up_pre * (sigmoid_gate + activated * (1.0 - sigmoid_gate))
            ).astype(low)
            part_up = (hidden_grad * activated).astype(low)
            weighted[span, :] = part_weighted
            gate_side[span, :] = part_gate
            up_side[span, :] = part_up
            mix_part = dot_plain(part_weighted, down_full)
            turn_part = dot_right(part_gate, gate_full) + dot_right(part_up, up_full)
            if e == 0 and not carried:
                mix[span, :] = mix_part
                turned[span, :width] = turn_part
            elif last and e == count - 1:
                mix_out[span, :] = (mix[span, :] + mix_part).astype(low)
                turn_out[span, :width] = (turned[span, :width] + turn_part).astype(low)
                turn_out[span, width:] = turned[span, width:].astype(low)
            else:
                mix[span, :] += mix_part
                turned[span, :width] += turn_part

        if e >= 2:
            for copy in saves(e - 2):
                copy.wait()
        down_g[slot] = dot_left(weighted[...], grads[...]).astype(low).reshape(down_g.shape[1:])
        gate_g[slot] = dot_left(rows[...], gate_side[...]).astype(low).reshape(gate_g.shape[1:])
        up_g[slot] = dot_left(rows[...], up_side[...]).astype(low).reshape(up_g.shape[1:])
        for copy in saves(e):
            copy.start()
    for e in range(max(0, count - 2), count):
        for copy in saves(e):
            copy.wait()


def expert_pass(place, first, rows, grads, packed, carry, cut, last):
    blocks, _, count, part, width = packed.shape
    hidden_width = blocks * part
    total_rows = sum(block.shape[0] for block in rows)
    lanes = rows[0].shape[1] - width
    low = jnp.bfloat16
    wide = jnp.float32
    carried = carry is not None
    flops = 18 * total_rows * count * hidden_width * width
    side = pltpu.VMEM((2, blocks, 3, part, hidden_width), low)
    sides = [side, side, pltpu.VMEM((2, blocks, part, width), low)]
    sums = [(total_rows, width), (total_rows, width + lanes)]
    one = packed.shape[1:]
    grads_out = [one, (3,) + one, (2,) + one, (2,) + one] if cut else [packed.shape]
    outs = len(grads_out)
    found = pl.pallas_call(
        partial(expert_kernel, cut, carried, last, len(rows), len(grads), min(512, total_rows)),
        in_specs=[SCALARS, SCALARS]
        + [ANYWHERE] * (1 + len(rows) + len(grads) + (2 if carried else 0)),
        out_specs=[ANYWHERE] * outs + [INSIDE, INSIDE],
        out_shape=[jax.ShapeDtypeStruct(shape, low) for shape in grads_out]
        + [jax.ShapeDtypeStruct(shape, low if last else wide) for shape in sums],
        scratch_shapes=([pltpu.VMEM(shape, wide) for shape in sums] if last else [])
        + [
            pltpu.VMEM((total_rows, width), low),
            pltpu.VMEM((total_rows, width), low),
            pltpu.VMEM((total_rows, lanes), low),
        ]
        + sides
        + sides
        + [pltpu.VMEM((total_rows, hidden_width), low)] * 3
        + [
            pltpu.SemaphoreType.DMA((2, 7)),
            pltpu.SemaphoreType.DMA((2, 56)),
            pltpu.SemaphoreType.DMA((2 * len(rows) + len(grads) + 2,)),
        ],
        compiler_params=pltpu.CompilerParams(vmem_limit_bytes=VMEM_BYTES),
        cost_estimate=cost(flops, packed, packed, *rows, *grads),
        name="experts",
    )(place, first, packed, *rows, *grads, *(carry or ()))
    return found[:outs], found[outs], found[outs + 1]


def unpack_kernel(counts, places, *refs):
    found, (gate, up, down) = refs[:-3], refs[-3:]
    found = [array if place is None else array.at[place] for array, place in zip(found, places)]
    hidden_width = gate.shape[2]
    base = 0
    at = 0
    for terms in counts:
        parts = found[at : at + terms]
        at += terms
        count, part = parts[0].shape[1], parts[0].shape[2]
        for e in range(count):
            for side in range(3):
                total = parts[0][side, e].astype(jnp.float32)
                for other in parts[1:]:
                    total += other[side, e].astype(jnp.float32)
                if side == 2:
                    down[base + e] = total
                    continue
                for j in range(3):
                    (gate, up)[side][base + e, j * part : (j + 1) * part, :] = total[
                        :, j * hidden_width : (j + 1) * hidden_width
                    ]
        base += count


def unpack(chunks, gate_shape, down_shape):
    arrays = [array for terms in chunks for array, _ in terms]
    places = [place for terms in chunks for _, place in terms]
    return pl.pallas_call(
        partial(unpack_kernel, [len(terms) for terms in chunks], places),
        in_specs=[INSIDE] * len(arrays),
        out_specs=[INSIDE] * 3,
        out_shape=[
            jax.ShapeDtypeStruct(gate_shape, jnp.float32),
            jax.ShapeDtypeStruct(gate_shape, jnp.float32),
            jax.ShapeDtypeStruct(down_shape, jnp.float32),
        ],
        compiler_params=pltpu.CompilerParams(vmem_limit_bytes=VMEM_BYTES),
        cost_estimate=cost(0),
        name="unpack",
    )(*arrays)


def cube():
    return lax.axis_size("batch") == 8 and lax.axis_size("expert") == 4


def pair_moves(size, flip):
    return [(i, i ^ flip) for i in range(size)]


def shift_moves(step):
    return [(2 * z + c, 2 * ((z + step) % 4) + c) for z in range(4) for c in range(2)]


def gather_start(rows):
    size = lax.axis_size("expert")
    if size != 4:
        stacked = lax.all_gather(rows, "expert", axis=0)
        own = lax.axis_index("expert")
        return [
            lax.dynamic_index_in_dim(stacked, own ^ r, axis=0, keepdims=False) for r in range(size)
        ]
    return [rows] + [lax.ppermute(rows, "expert", pair_moves(4, r)) for r in (1, 2)]


def gather_finish(state, events=()):
    if lax.axis_size("expert") != 4:
        return state
    first, second = after(state[1:], events)
    half = first.shape[0] // 2
    top = lax.ppermute(second[:half], "expert", pair_moves(4, 1))
    bottom = lax.ppermute(first[half:], "expert", pair_moves(4, 2))
    return state + [top, bottom]


def gather_blocks(rows):
    return gather_finish(gather_start(rows))


def scatter_start(parts):
    low = jnp.bfloat16
    if lax.axis_size("expert") != 4:
        own = lax.axis_index("expert")
        order = jnp.arange(len(parts), dtype=jnp.int32) ^ own
        stacked = jnp.take(jnp.stack(parts), order, axis=0).astype(low)
        return [lax.psum_scatter(stacked, "expert", scatter_dimension=0).astype(jnp.float32)]
    across, along = pair_moves(4, 1), pair_moves(4, 2)
    half = parts[0].shape[0] // 2
    top = lax.ppermute(parts[3][:half].astype(low), "expert", across)
    bottom = lax.ppermute(parts[3][half:].astype(low), "expert", along)
    first_top = lax.ppermute(parts[1][:half].astype(low), "expert", across)
    second_bottom = lax.ppermute(parts[2][half:].astype(low), "expert", along)
    for_first = add_low(parts[1][half:], bottom)
    for_second = add_low(parts[2][:half], top)
    return [parts[0], first_top, second_bottom, for_first, for_second]


def scatter_finish(state):
    if len(state) == 1:
        return state[0]
    own, first_top, second_bottom, for_first, for_second = state
    half = first_top.shape[0]
    second_top = lax.ppermute(for_second, "expert", pair_moves(4, 2))
    first_bottom = lax.ppermute(for_first, "expert", pair_moves(4, 1))
    return jnp.concatenate(
        [
            total_of([own[:half], first_top, second_top]),
            total_of([own[half:], first_bottom, second_bottom]),
        ],
        axis=0,
    )


def scatter_blocks(parts):
    return scatter_finish(scatter_start(parts))


def after(values, events):
    return lax.optimization_barrier((values, events))[0]


def send_parts(parts, events):
    if lax.axis_size("expert") != 4:
        return [scatter_blocks(parts)]
    low = jnp.bfloat16
    first, second = (
        lax.ppermute(parts[r].astype(low), "expert", pair_moves(4, r)) for r in (1, 2)
    )
    far = lax.ppermute(after(parts[3].astype(low), (first, second, events)), "expert", pair_moves(4, 3))
    return [parts[0], first, second, far]


def total_of(parts):
    total = parts[0].astype(jnp.float32)
    for part in parts[1:]:
        total += part.astype(jnp.float32)
    return total


def shift_dense(rows, events):
    if not cube():
        return [lax.all_gather(rows, ("batch", "expert"), axis=0, tiled=True)]
    below, above = step_up(rows), step_down(rows)
    return [rows, below, step_up(after(below, (above, events))), above]


def dense_start(line, columns, events):
    found = [rows[:, columns] for rows in line]
    if not cube():
        return [found[0][None]]
    return gather_start(after(jnp.stack(found), events))


def dense_finish(state, events=(), late=()):
    if not cube():
        return state, jnp.zeros((1, 1), jnp.int32), ()
    place = lax.axis_index("batch")
    level, core = place // 2, place % 2
    member = lax.axis_index("expert")
    mine = gather_finish(state, events)
    far = mine[3:]
    mine = mine[:3] + [after(jnp.concatenate(far, axis=0), late)]
    other = [exchange_cores(block) for block in mine]
    spots = [
        [(((level + 4 - k) % 4) * 2 + (core ^ c)) * 4 + (member ^ r) for k in range(4)]
        for c in range(2)
        for r in range(4)
    ]
    return mine + other, jnp.array(spots, jnp.int32), far


def sum_chunk(packed_grad):
    return lax.psum_scatter(packed_grad, "batch", scatter_dimension=0, tiled=True)


def exchange_cores(values):
    return lax.ppermute(values, "batch", pair_moves(8, 1))


def step_up(values):
    return lax.ppermute(values, "batch", shift_moves(1))


def step_down(values):
    return lax.ppermute(values, "batch", shift_moves(3))


def add_low(*parts):
    total = parts[0].astype(jnp.float32)
    for part in parts[1:]:
        total += part.astype(jnp.float32)
    return total.astype(jnp.bfloat16)


def join_cores(own, received):
    return [add_low(own[r], received[r]) for r in range(4)]


def line_start(plane):
    level = lax.axis_index("batch") // 2
    own, up, far, down = (
        lax.dynamic_index_in_dim(plane, (level + r) % 4, axis=0, keepdims=False) for r in range(4)
    )
    return own, step_down(add_low(down)), add_low(up, step_up(add_low(far)))


def line_finish(state, events=()):
    own, down, up = state
    return total_of([own, down, step_up(after(up, events))])


def scatter_whole(found):
    values = found[0].reshape(found[0].shape[3:])
    total = lax.psum_scatter(values, ("batch", "expert"), scatter_dimension=0, tiled=True)
    return total.astype(jnp.float32)


def pack_kernel(chunks, query, key, value, small, out, gate, up, down, dense, *packed):
    start = 0
    for part in (query, key, value, small, out):
        dense[:, start : start + part.shape[1]] = part[...]
        start += part.shape[1]
    part, hidden_width = down.shape[1], gate.shape[2]
    for n, target in enumerate(packed):
        for e in range(chunks[n], chunks[n + 1]):
            for side, source in ((0, gate), (1, up)):
                for j in range(3):
                    target[side, e - chunks[n], :, j * hidden_width : (j + 1) * hidden_width] = (
                        source[e, j * part : (j + 1) * part, :]
                    )
            target[2, e - chunks[n]] = down[e]


def pack(chunks, query, key, value, small, out, gate, up, down):
    low = jnp.bfloat16
    columns = sum(part.shape[1] for part in (query, key, value, small, out))
    return pl.pallas_call(
        partial(pack_kernel, chunks),
        in_specs=[INSIDE] * 8,
        out_specs=[INSIDE] * len(chunks),
        out_shape=[jax.ShapeDtypeStruct((query.shape[0], columns), low)]
        + [
            jax.ShapeDtypeStruct((3, b - a) + down.shape[1:], low)
            for a, b in zip(chunks[:-1], chunks[1:])
        ],
        compiler_params=pltpu.CompilerParams(vmem_limit_bytes=VMEM_BYTES),
        cost_estimate=cost(0),
        name="pack",
    )(query, key, value, small, out, gate, up, down)


def local(
    tokens,
    cotangent,
    attn_gain,
    query_weight,
    key_weight,
    value_weight,
    out_weight,
    ffn_gain,
    router_weight,
    gate_weight,
    up_weight,
    down_weight,
    routes,
    ranking,
):
    low = jnp.bfloat16
    wide = jnp.float32
    query_width = HEADS * HEAD_DIM
    kv_width = KV_HEADS * HEAD_DIM
    qkv_width = query_width + 2 * kv_width
    width = tokens.shape[2]
    experts_total = router_weight.shape[1]
    extra = -(-(experts_total + 2) // 128) * 128
    first_gain, second_gain = experts_total, experts_total + 1
    local_experts = gate_weight.shape[0]
    member_count = lax.axis_size("expert")
    member_id = lax.axis_index("expert")
    local_rows = tokens.shape[1]
    group_rows = local_rows * member_count
    cut = cube()
    line_place = lax.axis_index("batch")
    place = jnp.stack([line_place % 2, member_id, line_place // 2]).astype(jnp.int32)

    route_rows = routes[0]
    rank_rows = ranking[0]
    expert_lanes = jnp.arange(extra, dtype=jnp.int32)
    member = jnp.any(route_rows[:, :, None] == expert_lanes[None, None, :], axis=1)
    marks = jnp.where(
        expert_lanes[None, :] == experts_total,
        (rank_rows // 32)[:, None],
        jnp.where(expert_lanes[None, :] == experts_total + 1, (rank_rows % 32)[:, None], member),
    ).astype(low)
    grad_out = cotangent[0]
    small_width = qkv_width + extra
    chunks = (0, 3, local_experts)
    dense_rows, *packed_own = pack(
        chunks,
        query_weight,
        key_weight,
        value_weight,
        jnp.concatenate(
            [
                router_weight,
                attn_gain[:, None],
                ffn_gain[:, None],
                jnp.zeros((query_weight.shape[0], extra - experts_total - 2), low),
            ],
            axis=1,
        ),
        out_weight,
        gate_weight,
        up_weight,
        down_weight,
    )
    row_ids = member_id * local_rows + jnp.arange(local_rows, dtype=jnp.int32)
    half_dim = HEAD_DIM // 2
    frequency = THETA ** (-jnp.arange(half_dim, dtype=wide) / half_dim)
    angles = place_of(row_ids).astype(wide)[:, None] * frequency[None, :]
    cosine = jnp.tile(jnp.cos(angles), (1, 4))
    sine_part = jnp.tile(jnp.concatenate([-jnp.sin(angles), jnp.sin(angles)], axis=1), (1, 2))
    if member_count == 4:
        away = 1 << 20
        starts = [
            jnp.where(member_id >= 1, 0, away),
            jnp.where(member_id >= 2, local_rows, away),
            member_id * local_rows,
        ]
    else:
        starts = [(member_id ^ r) * local_rows for r in range(member_count)]
    key_ids = jnp.concatenate([s + jnp.arange(local_rows, dtype=jnp.int32) for s in starts])
    bias = jnp.where(visible(row_ids, key_ids), 0.0, -1e30).astype(wide)
    bias_turned = bias.T
    tables = (cosine, sine_part, bias, bias_turned)

    line = shift_dense(dense_rows, tables)
    grad_state = gather_start(jnp.concatenate([grad_out, marks], axis=1))
    grad_blocks = gather_finish(grad_state, line[1::2])
    marks_all = jnp.concatenate([block[:, width:] for block in grad_blocks], axis=0)
    qkv_state = dense_start(line, slice(0, small_width), ())
    plane = qkv_state[1:]
    qkv_pieces, qkv_spots, far = dense_finish(qkv_state)
    out_state = dense_start(line, slice(small_width, None), far)
    packed_all = [
        lax.all_gather(after(packed, events), "batch", axis=0)
        for packed, events in zip(packed_own, ((line, grad_blocks), plane))
    ]

    normed, query, keyval, small = enter(
        tokens[0], cosine, sine_part, qkv_pieces, qkv_spots, first_gain, query_width, kv_width
    )

    rank_all = (
        marks_all[:, experts_total].astype(wide) * 32 + marks_all[:, experts_total + 1].astype(wide)
    )
    earlier = (rank_all[None, :] < rank_rows.astype(wide)[:, None]).astype(low)
    before = product(earlier, marks_all)
    capacity = 5 * group_rows * route_rows.shape[1] // (4 * experts_total)
    member = member.astype(wide)
    kept = jnp.where(before < capacity, member, 0.0)

    keyval_blocks = gather_blocks(after(keyval, out_state[1:]))
    if member_count == 4:
        ordered = keyval_blocks[:3] + [jnp.concatenate(keyval_blocks[3:], axis=0)]
        keys = jnp.concatenate(
            [
                lax.select_n(member_id, *ordered),
                lax.select_n(member_id ^ 1, *ordered),
                keyval,
            ],
            axis=0,
        )
    else:
        keys = jnp.concatenate(keyval_blocks, axis=0)
    attended, log_totals = attend(query, keys, bias)
    out_pieces, out_spots, _ = dense_finish(out_state, keyval_blocks[3:], attended)
    residual, sent, gate_rows = project(
        attended, tokens[0], small, member, kept, second_gain, out_pieces, out_spots
    )
    sent_blocks = gather_blocks(sent)

    carry, chunk_grads = None, []
    for packed, a, b in zip(packed_all, chunks[:-1], chunks[1:]):
        first = (member_id * local_experts + a).astype(jnp.int32).reshape(1)
        packed_grads, mixture_all, row_grad = expert_pass(
            place,
            first,
            sent_blocks,
            grad_blocks,
            packed,
            carry,
            cut and b == local_experts,
            b == local_experts,
        )
        carry = (mixture_all, row_grad)
        chunk_grads.append(packed_grads)

    def blocks_of(values):
        return [values[r * local_rows : (r + 1) * local_rows] for r in range(member_count)]

    totals = [sum_chunk(chunk_grads[0][0])]
    if cut:
        own, rest, far, near = chunk_grads[1]
        far, near = exchange_cores(far), exchange_cores(near)
        far_sum, down_sum = add_low(rest[1], far[0]), add_low(rest[2], far[1])
    turn_state = scatter_start(blocks_of(row_grad))
    if cut:
        turn_state = after(turn_state, (far_sum, down_sum))
    normed_grad = scatter_finish(turn_state)
    turned = turn(
        place,
        out_spots,
        (
            normed_grad,
            residual,
            grad_out,
            small,
            gate_rows,
            member,
            kept,
            sent,
            attended,
        ),
        out_pieces,
        cut,
        second_gain,
    )
    out_found = turned[:-2]
    resid_grad, head_grad = turned[-2:]
    mixture_parts = send_parts(blocks_of(after(mixture_all, normed_grad)), resid_grad)
    if cut:
        head_grad = after(head_grad, mixture_parts[1:3])
        up_part = step_up(far_sum)
    query_grad, key_grads = attend_back(
        head_grad, query, keys, bias_turned, log_totals, cosine, sine_part
    )
    if member_count == 4:
        zero = jnp.zeros((), low)
        for_first, for_second, for_own = blocks_of(key_grads)[:3]
        key_parts = []
        for r in range(4):
            part = jnp.where(member_id == r, for_first, zero)
            part += jnp.where(member_id ^ 1 == r, for_second, zero)
            key_parts.append(part + for_own if r == 0 else part)
    else:
        key_parts = blocks_of(key_grads)
    if cut:
        out_found = out_found[1], exchange_cores(out_found[0])
        key_parts = after(key_parts, (mixture_parts[3], up_part))
    keyval_sum = scatter_blocks(key_parts)
    if cut:
        out_state = scatter_start(join_cores(*out_found))
    if cut:
        up_sum = add_low(rest[0], near[0], up_part)
        keyval_sum = after(keyval_sum, (out_found, up_sum))
    left = leave(
        place,
        qkv_spots,
        (
            keyval_sum,
            query_grad,
            normed,
            tokens[0],
            resid_grad,
            small,
            cosine,
            sine_part,
        ),
        qkv_pieces,
        cut,
        first_gain,
    )
    qkv_found, input_grad = left[:-1], left[-1]
    result = (residual + total_of(mixture_parts)).astype(low)
    if cut:
        down_term = step_down(after(down_sum, key_parts))
        received = exchange_cores(after(qkv_found[0], (totals[0], out_state[1:], down_term)))
        out_plane = scatter_finish(out_state)
        up_term = step_up(up_sum)
        qkv_parts = join_cores(qkv_found[1], after(received, out_plane))
        qkv_state = after(scatter_start(qkv_parts), up_term)
        qkv_plane = scatter_finish(qkv_state)
        out_sum = line_finish(line_start(out_plane))
        qkv_state = line_start(qkv_plane)
        near, down_term, up_term = after((near, down_term, up_term), qkv_plane)
        terms = [[(totals[0], 0)], [(own, None), (near, 1), (down_term, None), (up_term, None)]]
        expert_totals = unpack(terms, gate_weight.shape, down_weight.shape)
        qkv_sum = line_finish(qkv_state, expert_totals)
    else:
        out_sum = scatter_whole(out_found)
        qkv_sum = scatter_whole(qkv_found)
        totals += [sum_chunk(found[0]) for found in chunk_grads[1:]]
        terms = [[(total, 0)] for total in totals]
        expert_totals = unpack(terms, gate_weight.shape, down_weight.shape)
    gate_total, up_total, down_total = expert_totals
    return (
        result[None],
        input_grad[None],
        qkv_sum[:, qkv_width + first_gain],
        qkv_sum[:, :query_width],
        qkv_sum[:, query_width : query_width + kv_width],
        qkv_sum[:, query_width + kv_width : qkv_width],
        out_sum[:, :width],
        out_sum[:, width + second_gain],
        out_sum[:, width : width + experts_total],
        gate_total,
        up_total,
        down_total,
    )


def solution(mesh):
    return jax.shard_map(
        local,
        mesh=mesh,
        in_specs=(
            P("batch", "expert", None),
            P("batch", "expert", None),
            P(("batch", "expert")),
            P(("batch", "expert"), None),
            P(("batch", "expert"), None),
            P(("batch", "expert"), None),
            P(("batch", "expert"), None),
            P(("batch", "expert")),
            P(("batch", "expert"), None),
            P("expert", "batch", None),
            P("expert", "batch", None),
            P("expert", "batch", None),
            P("batch", "expert", None),
            P("batch", "expert"),
        ),
        out_specs=(
            P("batch", "expert", None),
            P("batch", "expert", None),
            P(("batch", "expert")),
            P(("batch", "expert"), None),
            P(("batch", "expert"), None),
            P(("batch", "expert"), None),
            P(("batch", "expert"), None),
            P(("batch", "expert")),
            P(("batch", "expert"), None),
            P("expert", "batch", None),
            P("expert", "batch", None),
            P("expert", "batch", None),
        ),
        check_vma=False,
    )
```

```python
from functools import partial

import jax
import jax.numpy as jnp
from jax import lax
from jax.experimental import pallas as pl
from jax.experimental.pallas import tpu as pltpu
from jax.sharding import PartitionSpec as P

HEADS = 24
KV_HEADS = 8
HEAD_DIM = 64
PROMPT = 512
CLEN = 256


EPS = 1e-06
THETA = 10000.0


def product(left, right):
    return jnp.dot(left, right, preferred_element_type=jnp.float32)


def place_of(row_ids):
    return jnp.where(row_ids < PROMPT, row_ids, PROMPT + (row_ids - PROMPT) % CLEN)


def visible(query_ids, key_ids):
    causal = key_ids[None, :] <= query_ids[:, None]
    same_run = (key_ids[None, :] - PROMPT) // CLEN == (query_ids[:, None] - PROMPT) // CLEN
    return causal & ((key_ids[None, :] < PROMPT) | same_run)


def dot_plain(left, right):
    return lax.dot_general(left, right, (((1,), (0,)), ((), ())), preferred_element_type=jnp.float32)


def dot_right(left, right):
    return lax.dot_general(left, right, (((1,), (1,)), ((), ())), preferred_element_type=jnp.float32)


def dot_left(left, right):
    return lax.dot_general(left, right, (((0,), (0,)), ((), ())), preferred_element_type=jnp.float32)


ANYWHERE = pl.BlockSpec(memory_space=pl.ANY)
INSIDE = pl.BlockSpec(memory_space=pltpu.VMEM)
SCALARS = pl.BlockSpec(memory_space=pltpu.SMEM)
VMEM_BYTES = 62 * 1024 * 1024


def cost(flops, *arrays):
    return pl.CostEstimate(flops=1, bytes_accessed=1, transcendentals=0)


def weight_copies(spots, pieces, target, sems):
    copies = []
    for p, piece in enumerate(pieces):
        blocks, rows = piece.shape[0], piece.shape[1]
        for k in range(blocks):
            place = pl.multiple_of(spots[p, k] * rows, rows)
            copies.append(
                pltpu.make_async_copy(
                    piece.at[k], target.at[pl.ds(place, rows)], sems.at[p * blocks + k]
                )
            )
    return copies


def block_copies(blocks, target, sems, first, columns=None):
    copies = []
    start = 0
    for i, block in enumerate(blocks):
        rows = block.shape[0]
        source = block if columns is None else block.at[:, columns]
        copies.append(
            pltpu.make_async_copy(source, target.at[pl.ds(start, rows)], sems.at[first + i])
        )
        start += rows
    return copies


def swap_halves(values):
    half = HEAD_DIM // 2
    lane = lax.broadcasted_iota(jnp.int32, values.shape, 1)
    return jnp.where(
        lane % HEAD_DIM < half,
        pltpu.roll(values, 2 * HEAD_DIM - half, 1),
        pltpu.roll(values, half, 1),
    )


def mean_square_scale(values):
    return lax.rsqrt(jnp.mean(values * values, axis=-1, keepdims=True) + EPS)


def enter_kernel(count, gain_at, spots, tokens, cosine, sine, *refs):
    pieces = refs[:count]
    normed, query, keyval, small, weight, sems = refs[count:]
    low = jnp.bfloat16
    copies = weight_copies(spots, pieces, weight, sems)
    for copy in copies:
        copy.start()
    inputs = tokens[...].astype(jnp.float32)
    scaled = inputs * mean_square_scale(inputs)
    for copy in copies:
        copy.wait()
    query_width = query.shape[1]
    kv_width = keyval.shape[1] // 2
    qkv_width = query_width + 2 * kv_width
    turned = weight[:, qkv_width:].astype(jnp.float32).T
    small[...] = turned
    rows = (scaled * turned[gain_at : gain_at + 1]).astype(low)
    normed[...] = rows
    pair = 2 * HEAD_DIM
    scale = HEAD_DIM**-0.5
    for start in range(0, query_width + kv_width, 512):
        product_part = dot_plain(rows, weight[:, start : start + 512])
        for offset in range(0, 512, pair):
            part = product_part[:, offset : offset + pair]
            part = part * cosine[...] + swap_halves(part) * sine[...]
            at = start + offset
            if at < query_width:
                query[:, at : at + pair] = (part * scale).astype(low)
            else:
                keyval[:, at - query_width : at - query_width + pair] = part.astype(low)
    keyval[:, kv_width:] = dot_plain(
        rows, weight[:, query_width + kv_width : qkv_width]
    ).astype(low)


def enter(tokens, cosine, sine, pieces, spots, gain_at, query_width, kv_width):
    rows, width = tokens.shape
    columns = pieces[0].shape[2]
    low = jnp.bfloat16
    return pl.pallas_call(
        partial(enter_kernel, len(pieces), gain_at),
        in_specs=[SCALARS, INSIDE, INSIDE, INSIDE] + [ANYWHERE] * len(pieces),
        out_specs=[INSIDE] * 4,
        out_shape=[
            jax.ShapeDtypeStruct((rows, width), low),
            jax.ShapeDtypeStruct((rows, query_width), low),
            jax.ShapeDtypeStruct((rows, 2 * kv_width), low),
            jax.ShapeDtypeStruct((columns - query_width - 2 * kv_width, width), jnp.float32),
        ],
        scratch_shapes=[
            pltpu.VMEM((width, columns), low),
            pltpu.SemaphoreType.DMA((len(pieces) * pieces[0].shape[0],)),
        ],
        compiler_params=pltpu.CompilerParams(vmem_limit_bytes=VMEM_BYTES),
        cost_estimate=cost(2 * rows * width * columns, *pieces),
        name="enter",
    )(spots, tokens, cosine, sine, *pieces)


def both_places(values):
    wide = values.astype(jnp.float32)
    low_lane = lax.broadcasted_iota(jnp.int32, values.shape, 1) < HEAD_DIM
    moved = pltpu.roll(wide, HEAD_DIM, 1)
    kind = values.dtype
    return [
        [jnp.where(low_lane, wide, 0.0).astype(kind), jnp.where(low_lane, 0.0, moved).astype(kind)],
        [jnp.where(low_lane, moved, 0.0).astype(kind), jnp.where(low_lane, 0.0, wide).astype(kind)],
    ]


def attend_kernel(query, keyval, bias, attended, log_totals):
    low = jnp.bfloat16
    rows = query.shape[0]
    kv_width = keyval.shape[1] // 2
    pair_lanes = 2 * HEAD_DIM
    repeat = HEADS // KV_HEADS
    log_totals[...] = jnp.zeros_like(log_totals)
    lane = lax.broadcasted_iota(jnp.int32, log_totals.shape, 1)

    @pl.loop(0, KV_HEADS // 2)
    def _(pair):
        at = pl.ds(pl.multiple_of(pair * pair_lanes, pair_lanes), pair_lanes)
        keys = both_places(keyval[:, at])
        at = pl.ds(pl.multiple_of(kv_width + pair * pair_lanes, pair_lanes), pair_lanes)
        values = both_places(keyval[:, at])
        for i in range(repeat):
            at = pl.ds(pl.multiple_of((pair * repeat + i) * pair_lanes, pair_lanes), pair_lanes)
            queries = query[:, at]
            total = jnp.zeros((rows, pair_lanes), jnp.float32)
            for a in range(2):
                head = 2 * i + a
                scores = dot_right(queries, keys[head // repeat][a]) + bias[...]
                peak = jnp.max(scores, axis=-1, keepdims=True)
                lifted = jnp.exp(scores - peak)
                row_total = jnp.sum(lifted, axis=-1, keepdims=True)
                weights_low = (lifted * (1.0 / row_total)).astype(low)
                total += dot_plain(weights_low, values[head // repeat][a])
                log_totals[...] = jnp.where(
                    lane == pair * (2 * repeat) + head, peak + jnp.log(row_total), log_totals[...]
                )
            attended[:, at] = total.astype(low)


def attend(query, keyval, bias):
    rows, query_width = query.shape
    return pl.pallas_call(
        attend_kernel,
        in_specs=[INSIDE] * 3,
        out_specs=[INSIDE] * 2,
        out_shape=[
            jax.ShapeDtypeStruct((rows, query_width), jnp.bfloat16),
            jax.ShapeDtypeStruct((rows, 128), jnp.float32),
        ],
        compiler_params=pltpu.CompilerParams(vmem_limit_bytes=VMEM_BYTES),
        cost_estimate=cost(8 * rows * query_width * bias.shape[1], query, keyval, bias),
        name="attend",
    )(query, keyval, bias)


def project_kernel(count, gain_at, spots, attended, tokens, small, member, kept, *refs):
    pieces = refs[:count]
    residual, sent, gate_rows, weight, sems = refs[count:]
    low = jnp.bfloat16
    width = tokens.shape[1]
    copies = weight_copies(spots, pieces, weight, sems)
    for copy in copies:
        copy.start()
    for copy in copies:
        copy.wait()
    hidden = tokens[...].astype(jnp.float32) + dot_plain(attended[...], weight[...])
    residual[...] = hidden
    gain = small[gain_at : gain_at + 1, :]
    normed = (hidden * mean_square_scale(hidden) * gain).astype(low)
    logits = dot_right(normed, small[...].astype(low))
    chosen = member[...] > 0.0
    logits = jnp.where(chosen, logits, -1e30)
    lifted = jnp.where(chosen, jnp.exp(logits - jnp.max(logits, axis=-1, keepdims=True)), 0.0)
    gates = lifted / jnp.sum(lifted, axis=-1, keepdims=True)
    gate_rows[...] = gates
    sent[:, :width] = normed
    sent[:, width:] = (gates * kept[...]).astype(low)


def project(attended, tokens, small, member, kept, gain_at, pieces, spots):
    rows, width = tokens.shape
    lanes = small.shape[0]
    low = jnp.bfloat16
    return pl.pallas_call(
        partial(project_kernel, len(pieces), gain_at),
        in_specs=[SCALARS] + [INSIDE] * 5 + [ANYWHERE] * len(pieces),
        out_specs=[INSIDE] * 3,
        out_shape=[
            jax.ShapeDtypeStruct((rows, width), jnp.float32),
            jax.ShapeDtypeStruct((rows, width + lanes), low),
            jax.ShapeDtypeStruct((rows, lanes), jnp.float32),
        ],
        scratch_shapes=[
            pltpu.VMEM((attended.shape[1], width), low),
            pltpu.SemaphoreType.DMA((len(pieces) * pieces[0].shape[0],)),
        ],
        compiler_params=pltpu.CompilerParams(vmem_limit_bytes=VMEM_BYTES),
        cost_estimate=cost(2 * rows * width * width, *pieces),
        name="project",
    )(spots, attended, tokens, small, member, kept, *pieces)


def grad_shapes(cut, rows, columns):
    low = jnp.bfloat16
    if cut:
        block = rows // 32
        return (
            [jax.ShapeDtypeStruct((4, 4, block, columns), low)] * 2,
            pltpu.VMEM((4, 2, 4, block, columns), low),
        )
    return (
        [jax.ShapeDtypeStruct((1, 1, 1, rows, columns), low)],
        pltpu.VMEM((1, 1, 1, rows, columns), low),
    )


def grad_copies(cut, place, source, outs, sems):
    if not cut:
        return [pltpu.make_async_copy(source, outs[0], sems.at[0])]
    core, member = place[0], place[1]
    other, own = outs
    copies = []
    for r in range(4):
        copies.append(
            pltpu.make_async_copy(
                source.at[:, 1 - core, member ^ r], other.at[r], sems.at[2 * r]
            )
        )
        copies.append(
            pltpu.make_async_copy(source.at[:, core, member ^ r], own.at[r], sems.at[2 * r + 1])
        )
    return copies


def turn_kernel(
    count,
    cut,
    gain_at,
    place,
    spots,
    normed_grad,
    residual,
    grad_out,
    small,
    gate_rows,
    member,
    kept,
    normed,
    attended,
    *refs,
):
    pieces = refs[:count]
    refs = refs[count:]
    outs = refs[: (2 if cut else 1)]
    resid_grad, head_grad, weight, weight_grad, sems, out_sems = refs[len(outs) :]
    low = jnp.bfloat16
    rows, width = residual.shape
    lanes = gate_rows.shape[1]
    copies = weight_copies(spots, pieces, weight, sems)
    for copy in copies:
        copy.start()
    lane = lax.broadcasted_iota(jnp.int32, (rows, lanes), 1)
    gates = gate_rows[...]
    gate_grads = normed_grad[:, width:] * kept[...]
    chosen_grad = gates * (gate_grads - jnp.sum(gates * gate_grads, axis=-1, keepdims=True))
    logit_grad = (chosen_grad * member[...]).astype(low)
    hidden = residual[...]
    scale = mean_square_scale(hidden)
    row_grad = normed_grad[:, :width] + dot_plain(logit_grad, small[...].astype(low))
    gain = small[gain_at : gain_at + 1, :]
    scaled = row_grad * gain
    total_grad = (
        grad_out[...].astype(jnp.float32)
        + scale * scaled
        - hidden * (scale * scale * scale) * jnp.mean(scaled * hidden, axis=-1, keepdims=True)
    )
    resid_grad[...] = total_grad
    attn_grad = total_grad.astype(low)
    shape = weight_grad.shape[:-1]
    gain_grad = (row_grad * hidden * scale).astype(low)
    picks = jnp.where(lane == gain_at, 1.0, 0.0).astype(low)
    weight_grad[..., width:] = (
        (dot_left(normed[...][:, :width], logit_grad) + dot_left(gain_grad, picks))
        .astype(low)
        .reshape(shape + (lanes,))
    )
    for start in range(0, width, 512):
        weight_grad[..., start : start + 512] = (
            dot_left(attended[...], attn_grad[:, start : start + 512])
            .astype(low)
            .reshape(shape + (512,))
        )
    out_copies = grad_copies(cut, place, weight_grad, outs, out_sems)
    for copy in out_copies:
        copy.start()
    for copy in copies:
        copy.wait()
    head_grad[...] = dot_right(attn_grad, weight[...]).astype(low)
    for copy in out_copies:
        copy.wait()


def turn(place, spots, operands, pieces, cut, gain_at):
    residual, gate_rows, attended = operands[1], operands[4], operands[8]
    rows, width = residual.shape
    query_width = attended.shape[1]
    low = jnp.bfloat16
    grads, held = grad_shapes(cut, query_width, width + gate_rows.shape[1])
    return pl.pallas_call(
        partial(turn_kernel, len(pieces), cut, gain_at),
        in_specs=[SCALARS, SCALARS] + [INSIDE] * len(operands) + [ANYWHERE] * len(pieces),
        out_specs=[ANYWHERE] * len(grads) + [INSIDE] * 2,
        out_shape=grads
        + [
            jax.ShapeDtypeStruct((rows, width), jnp.float32),
            jax.ShapeDtypeStruct((rows, query_width), low),
        ],
        scratch_shapes=[
            pltpu.VMEM((query_width, width), low),
            held,
            pltpu.SemaphoreType.DMA((len(pieces) * pieces[0].shape[0],)),
            pltpu.SemaphoreType.DMA((8,)),
        ],
        compiler_params=pltpu.CompilerParams(vmem_limit_bytes=VMEM_BYTES),
        cost_estimate=cost(0),
        name="turn",
    )(place, spots, *operands, *pieces)


def attend_back_kernel(
    head_grad, query, keyval, bias, log_totals, cosine, sine, query_grad, keyval_grad, totals
):
    low = jnp.bfloat16
    rows = query.shape[0]
    kv_width = keyval.shape[1] // 2
    pair_lanes = 2 * HEAD_DIM
    repeat = HEADS // KV_HEADS
    totals[...] = log_totals[...].T

    @pl.loop(0, KV_HEADS // 2)
    def _(pair):
        key_at = pl.ds(pl.multiple_of(pair * pair_lanes, pair_lanes), pair_lanes)
        value_at = pl.ds(pl.multiple_of(kv_width + pair * pair_lanes, pair_lanes), pair_lanes)
        keys = both_places(keyval[:, key_at])
        values = both_places(keyval[:, value_at])
        key_grads = [[None, None], [None, None]]
        value_grads = [[None, None], [None, None]]
        for i in range(repeat):
            at = pl.ds(pl.multiple_of((pair * repeat + i) * pair_lanes, pair_lanes), pair_lanes)
            queries = query[:, at]
            grads = head_grad[:, at]
            query_part = jnp.zeros((rows, pair_lanes), jnp.float32)
            for a in range(2):
                head = 2 * i + a
                g = head // repeat
                total = totals[pl.ds(pair * (2 * repeat) + head, 1), :]
                weights = jnp.exp(dot_right(keys[g][a], queries) + bias[...] - total)
                weight_grads = dot_right(values[g][a], grads)
                delta = jnp.sum(weights * weight_grads, axis=0, keepdims=True)
                score_grads = (weights * (weight_grads - delta)).astype(low)
                value_part = dot_plain(weights.astype(low), grads)
                key_part = dot_plain(score_grads, queries)
                query_part += dot_left(score_grads, keys[g][a])
                if key_grads[g][a] is None:
                    key_grads[g][a], value_grads[g][a] = key_part, value_part
                else:
                    key_grads[g][a] += key_part
                    value_grads[g][a] += value_part
            query_part = query_part * (HEAD_DIM**-0.5)
            query_part = query_part * cosine[...] - swap_halves(query_part) * sine[...]
            query_grad[:, at] = query_part.astype(low)
        low_lane = lax.broadcasted_iota(jnp.int32, (keyval.shape[0], pair_lanes), 1) < HEAD_DIM
        for at, found in ((key_at, key_grads), (value_at, value_grads)):
            keyval_grad[:, at] = jnp.where(
                low_lane,
                found[0][0] + pltpu.roll(found[0][1], HEAD_DIM, 1),
                pltpu.roll(found[1][0], HEAD_DIM, 1) + found[1][1],
            ).astype(low)


def attend_back(head_grad, query, keyval, bias, log_totals, cosine, sine):
    rows, query_width = query.shape
    low = jnp.bfloat16
    return pl.pallas_call(
        attend_back_kernel,
        in_specs=[INSIDE] * 7,
        out_specs=[INSIDE] * 2,
        out_shape=[
            jax.ShapeDtypeStruct((rows, query_width), low),
            jax.ShapeDtypeStruct(keyval.shape, low),
        ],
        scratch_shapes=[pltpu.VMEM((128, rows), jnp.float32)],
        compiler_params=pltpu.CompilerParams(vmem_limit_bytes=VMEM_BYTES),
        cost_estimate=cost(0),
        name="attend_back",
    )(head_grad, query, keyval, bias, log_totals, cosine, sine)


def leave_kernel(
    count,
    cut,
    gain_at,
    place,
    spots,
    keyval_sum,
    query_grad,
    normed,
    tokens,
    resid_grad,
    small,
    cosine,
    sine,
    *refs,
):
    pieces = refs[:count]
    refs = refs[count:]
    outs = refs[: (2 if cut else 1)]
    input_grad, weight, weight_grad, joined, sems, out_sems = refs[len(outs) :]
    low = jnp.bfloat16
    rows, width = tokens.shape
    query_width = query_grad.shape[1]
    kv_width = keyval_sum.shape[1] // 2
    qkv_width = query_width + 2 * kv_width
    pair = 2 * HEAD_DIM
    copies = weight_copies(spots, pieces, weight, sems)
    for copy in copies:
        copy.start()
    joined[:, :query_width] = query_grad[...]
    for start in range(0, kv_width, pair):
        part = keyval_sum[:, start : start + pair]
        part = part * cosine[...] - swap_halves(part) * sine[...]
        joined[:, query_width + start : query_width + start + pair] = part.astype(low)
    joined[:, query_width + kv_width :] = keyval_sum[:, kv_width:].astype(low)
    shape = weight_grad.shape[:-1]
    for start in range(0, qkv_width, 512):
        weight_grad[..., start : start + 512] = (
            dot_left(normed[...], joined[:, start : start + 512]).astype(low).reshape(shape + (512,))
        )
    for copy in copies:
        copy.wait()
    row_grad = dot_right(joined[...], weight[:, :qkv_width])
    inputs = tokens[...].astype(jnp.float32)
    scale = mean_square_scale(inputs)
    lanes = weight_grad.shape[-1] - qkv_width
    lane = lax.broadcasted_iota(jnp.int32, (rows, lanes), 1)
    picks = jnp.where(lane == gain_at, 1.0, 0.0).astype(low)
    weight_grad[..., qkv_width:] = (
        dot_left((row_grad * inputs * scale).astype(low), picks).astype(low).reshape(shape + (lanes,))
    )
    out_copies = grad_copies(cut, place, weight_grad, outs, out_sems)
    for copy in out_copies:
        copy.start()
    scaled = row_grad * small[gain_at : gain_at + 1, :]
    input_grad[...] = (
        resid_grad[...]
        + scale * scaled
        - inputs * (scale * scale * scale) * jnp.mean(scaled * inputs, axis=-1, keepdims=True)
    )
    for copy in out_copies:
        copy.wait()


def leave(place, spots, operands, pieces, cut, gain_at):
    tokens, query_grad, keyval_sum = operands[3], operands[1], operands[0]
    rows, width = tokens.shape
    columns = pieces[0].shape[2]
    low = jnp.bfloat16
    grads, held = grad_shapes(cut, width, columns)
    return pl.pallas_call(
        partial(leave_kernel, len(pieces), cut, gain_at),
        in_specs=[SCALARS, SCALARS] + [INSIDE] * len(operands) + [ANYWHERE] * len(pieces),
        out_specs=[ANYWHERE] * len(grads) + [INSIDE],
        out_shape=grads + [jax.ShapeDtypeStruct((rows, width), jnp.float32)],
        scratch_shapes=[
            pltpu.VMEM((width, columns), low),
            held,
            pltpu.VMEM((rows, query_grad.shape[1] + keyval_sum.shape[1]), low),
            pltpu.SemaphoreType.DMA((len(pieces) * pieces[0].shape[0],)),
            pltpu.SemaphoreType.DMA((8,)),
        ],
        compiler_params=pltpu.CompilerParams(vmem_limit_bytes=VMEM_BYTES),
        cost_estimate=cost(0),
        name="leave",
    )(place, spots, *operands, *pieces)


def expert_kernel(cut, carried, last, row_blocks, grad_blocks, row_tile, place, first, packed, *refs):
    blocks_in = refs[:row_blocks]
    grads_in = refs[row_blocks : row_blocks + grad_blocks]
    refs = refs[row_blocks + grad_blocks :]
    if carried:
        mix_in, turn_in = refs[:2]
        refs = refs[2:]
    count = packed.shape[2]
    outs = 4 if cut else 1
    packed_grads = refs[:outs]
    mix_out, turn_out = refs[outs : outs + 2]
    refs = refs[outs + 2 :]
    if last:
        mix, turned = refs[:2]
        refs = refs[2:]
    else:
        mix, turned = mix_out, turn_out
    (
        rows,
        grads,
        gates,
        gate_w,
        up_w,
        down_w,
        gate_g,
        up_g,
        down_g,
        weighted,
        gate_side,
        up_side,
        load_sems,
        save_sems,
        carry_sems,
    ) = refs
    hidden_width = gate_w.shape[-1]
    total_rows, width = rows.shape
    lanes = gates.shape[1]
    low = jnp.bfloat16

    def sides(gate, up, down):
        for side, inner in ((0, gate), (1, up)):
            for j in range(3):
                yield side, pl.ds(j * hidden_width, hidden_width), inner, j
        yield 2, pl.ds(0, width), down, None

    def loads(e):
        slot = e % 2
        copies = []
        for i, (side, columns, inner, j) in enumerate(sides(gate_w, up_w, down_w)):
            outer = packed.at[:, side, e, :, columns]
            inner = inner.at[slot] if j is None else inner.at[slot, :, j]
            copies.append(pltpu.make_async_copy(outer, inner, load_sems.at[slot, i]))
        return copies

    def saves(e):
        slot = e % 2
        copies = []
        for i, (side, columns, inner, j) in enumerate(sides(gate_g, up_g, down_g)):
            if not cut:
                outer = packed_grads[0].at[:, side, e, :, columns]
                source = inner.at[slot] if j is None else inner.at[slot, :, j]
                copies.append(pltpu.make_async_copy(source, outer, save_sems.at[slot, i]))
                continue
            own, rest, far, near = packed_grads
            targets = [own, rest.at[0], rest.at[1], rest.at[2]]
            targets += [near.at[1], near.at[0], far.at[0], far.at[1]]
            for n, target in enumerate(targets):
                block = 2 * lax.rem(place[2] + n % 4, 4) + (place[0] ^ (n // 4))
                source = inner.at[slot, block] if j is None else inner.at[slot, block, j]
                outer = target.at[side, e, :, columns]
                copies.append(pltpu.make_async_copy(source, outer, save_sems.at[slot, 8 * i + n]))
        return copies

    carries = (
        block_copies(grads_in, grads, carry_sems, 0, pl.ds(0, width))
        + block_copies(blocks_in, rows, carry_sems, grad_blocks, pl.ds(0, width))
        + block_copies(
            blocks_in, gates, carry_sems, grad_blocks + row_blocks, pl.ds(width, lanes)
        )
    )
    sums = []
    if carried:
        at = grad_blocks + 2 * row_blocks
        sums = [
            pltpu.make_async_copy(mix_in, mix, carry_sems.at[at]),
            pltpu.make_async_copy(turn_in, turned, carry_sems.at[at + 1]),
        ]
    for copy in loads(0) + carries + sums:
        copy.start()
    for e in range(count):
        slot = e % 2
        if e + 1 < count:
            for copy in loads(e + 1):
                copy.start()
        for copy in loads(e):
            copy.wait()
        if e == 0:
            for copy in carries:
                copy.wait()
            if not carried:
                turned[:, width:] = jnp.zeros((total_rows, lanes), jnp.float32)

        @pl.loop(0, total_rows // row_tile)
        def _(tile):
            span = pl.ds(pl.multiple_of(tile * row_tile, row_tile), row_tile)
            gate_full = gate_w[slot].reshape(width, hidden_width)
            up_full = up_w[slot].reshape(width, hidden_width)
            down_full = down_w[slot].reshape(hidden_width, width)
            here = rows[span, :]
            slope = dot_right(grads[span, :], down_full)
            gate_pre = dot_plain(here, gate_full)
            up_pre = dot_plain(here, up_full)
            lane = lax.broadcasted_iota(jnp.int32, (row_tile, lanes), 1)
            chosen = lane == first[0] + e
            gate_column = jnp.sum(
                jnp.where(chosen, gates[span, :].astype(jnp.float32), 0.0), axis=1, keepdims=True
            )
            sigmoid_gate = jax.nn.sigmoid(gate_pre)
            activated = gate_pre * sigmoid_gate
            hidden = (activated * up_pre).astype(low).astype(jnp.float32)
            share = jnp.sum(hidden * slope, axis=1, keepdims=True)
            if e == 0 and sums:

                @pl.when(tile == 0)
                def _():
                    for copy in sums:
                        copy.wait()

            turned[span, width:] = jnp.where(chosen, share, turned[span, width:])
            part_weighted = (hidden * gate_column).astype(low)
            hidden_grad = slope * gate_column
            part_gate = (
                hidden_grad * up_pre * (sigmoid_gate + activated * (1.0 - sigmoid_gate))
            ).astype(low)
            part_up = (hidden_grad * activated).astype(low)
            weighted[span, :] = part_weighted
            gate_side[span, :] = part_gate
            up_side[span, :] = part_up
            mix_part = dot_plain(part_weighted, down_full)
            turn_part = dot_right(part_gate, gate_full) + dot_right(part_up, up_full)
            if e == 0 and not carried:
                mix[span, :] = mix_part
                turned[span, :width] = turn_part
            elif last and e == count - 1:
                mix_out[span, :] = (mix[span, :] + mix_part).astype(low)
                turn_out[span, :width] = (turned[span, :width] + turn_part).astype(low)
                turn_out[span, width:] = turned[span, width:].astype(low)
            else:
                mix[span, :] += mix_part
                turned[span, :width] += turn_part

        if e >= 2:
            for copy in saves(e - 2):
                copy.wait()
        down_g[slot] = dot_left(weighted[...], grads[...]).astype(low).reshape(down_g.shape[1:])
        gate_g[slot] = dot_left(rows[...], gate_side[...]).astype(low).reshape(gate_g.shape[1:])
        up_g[slot] = dot_left(rows[...], up_side[...]).astype(low).reshape(up_g.shape[1:])
        for copy in saves(e):
            copy.start()
    for e in range(max(0, count - 2), count):
        for copy in saves(e):
            copy.wait()


def expert_pass(place, first, rows, grads, packed, carry, cut, last):
    blocks, _, count, part, width = packed.shape
    hidden_width = blocks * part
    total_rows = sum(block.shape[0] for block in rows)
    lanes = rows[0].shape[1] - width
    low = jnp.bfloat16
    wide = jnp.float32
    carried = carry is not None
    flops = 18 * total_rows * count * hidden_width * width
    side = pltpu.VMEM((2, blocks, 3, part, hidden_width), low)
    sides = [side, side, pltpu.VMEM((2, blocks, part, width), low)]
    sums = [(total_rows, width), (total_rows, width + lanes)]
    one = packed.shape[1:]
    grads_out = [one, (3,) + one, (2,) + one, (2,) + one] if cut else [packed.shape]
    outs = len(grads_out)
    found = pl.pallas_call(
        partial(expert_kernel, cut, carried, last, len(rows), len(grads), min(512, total_rows)),
        in_specs=[SCALARS, SCALARS]
        + [ANYWHERE] * (1 + len(rows) + len(grads) + (2 if carried else 0)),
        out_specs=[ANYWHERE] * outs + [INSIDE, INSIDE],
        out_shape=[jax.ShapeDtypeStruct(shape, low) for shape in grads_out]
        + [jax.ShapeDtypeStruct(shape, low if last else wide) for shape in sums],
        scratch_shapes=([pltpu.VMEM(shape, wide) for shape in sums] if last else [])
        + [
            pltpu.VMEM((total_rows, width), low),
            pltpu.VMEM((total_rows, width), low),
            pltpu.VMEM((total_rows, lanes), low),
        ]
        + sides
        + sides
        + [pltpu.VMEM((total_rows, hidden_width), low)] * 3
        + [
            pltpu.SemaphoreType.DMA((2, 7)),
            pltpu.SemaphoreType.DMA((2, 56)),
            pltpu.SemaphoreType.DMA((2 * len(rows) + len(grads) + 2,)),
        ],
        compiler_params=pltpu.CompilerParams(vmem_limit_bytes=VMEM_BYTES),
        cost_estimate=cost(flops, packed, packed, *rows, *grads),
        name="experts",
    )(place, first, packed, *rows, *grads, *(carry or ()))
    return found[:outs], found[outs], found[outs + 1]


def unpack_kernel(counts, places, *refs):
    found, (gate, up, down) = refs[:-3], refs[-3:]
    found = [array if place is None else array.at[place] for array, place in zip(found, places)]
    hidden_width = gate.shape[2]
    base = 0
    at = 0
    for terms in counts:
        parts = found[at : at + terms]
        at += terms
        count, part = parts[0].shape[1], parts[0].shape[2]
        for e in range(count):
            for side in range(3):
                total = parts[0][side, e].astype(jnp.float32)
                for other in parts[1:]:
                    total += other[side, e].astype(jnp.float32)
                if side == 2:
                    down[base + e] = total
                    continue
                for j in range(3):
                    (gate, up)[side][base + e, j * part : (j + 1) * part, :] = total[
                        :, j * hidden_width : (j + 1) * hidden_width
                    ]
        base += count


def unpack(chunks, gate_shape, down_shape):
    arrays = [array for terms in chunks for array, _ in terms]
    places = [place for terms in chunks for _, place in terms]
    return pl.pallas_call(
        partial(unpack_kernel, [len(terms) for terms in chunks], places),
        in_specs=[INSIDE] * len(arrays),
        out_specs=[INSIDE] * 3,
        out_shape=[
            jax.ShapeDtypeStruct(gate_shape, jnp.float32),
            jax.ShapeDtypeStruct(gate_shape, jnp.float32),
            jax.ShapeDtypeStruct(down_shape, jnp.float32),
        ],
        compiler_params=pltpu.CompilerParams(vmem_limit_bytes=VMEM_BYTES),
        cost_estimate=cost(0),
        name="unpack",
    )(*arrays)


def cube():
    return lax.axis_size("batch") == 8 and lax.axis_size("expert") == 4


def pair_moves(size, flip):
    return [(i, i ^ flip) for i in range(size)]


def shift_moves(step):
    return [(2 * z + c, 2 * ((z + step) % 4) + c) for z in range(4) for c in range(2)]


def gather_start(rows):
    size = lax.axis_size("expert")
    if size != 4:
        stacked = lax.all_gather(rows, "expert", axis=0)
        own = lax.axis_index("expert")
        return [
            lax.dynamic_index_in_dim(stacked, own ^ r, axis=0, keepdims=False) for r in range(size)
        ]
    return [rows] + [lax.ppermute(rows, "expert", pair_moves(4, r)) for r in (1, 2)]


def gather_finish(state, events=()):
    if lax.axis_size("expert") != 4:
        return state
    first, second = after(state[1:], events)
    half = first.shape[0] // 2
    top = lax.ppermute(second[:half], "expert", pair_moves(4, 1))
    bottom = lax.ppermute(first[half:], "expert", pair_moves(4, 2))
    return state + [top, bottom]


def gather_blocks(rows):
    return gather_finish(gather_start(rows))


def scatter_start(parts):
    low = jnp.bfloat16
    if lax.axis_size("expert") != 4:
        own = lax.axis_index("expert")
        order = jnp.arange(len(parts), dtype=jnp.int32) ^ own
        stacked = jnp.take(jnp.stack(parts), order, axis=0).astype(low)
        return [lax.psum_scatter(stacked, "expert", scatter_dimension=0).astype(jnp.float32)]
    across, along = pair_moves(4, 1), pair_moves(4, 2)
    half = parts[0].shape[0] // 2
    top = lax.ppermute(parts[3][:half].astype(low), "expert", across)
    bottom = lax.ppermute(parts[3][half:].astype(low), "expert", along)
    first_top = lax.ppermute(parts[1][:half].astype(low), "expert", across)
    second_bottom = lax.ppermute(parts[2][half:].astype(low), "expert", along)
    for_first = add_low(parts[1][half:], bottom)
    for_second = add_low(parts[2][:half], top)
    return [parts[0], first_top, second_bottom, for_first, for_second]


def scatter_finish(state):
    if len(state) == 1:
        return state[0]
    own, first_top, second_bottom, for_first, for_second = state
    half = first_top.shape[0]
    second_top = lax.ppermute(for_second, "expert", pair_moves(4, 2))
    first_bottom = lax.ppermute(for_first, "expert", pair_moves(4, 1))
    return jnp.concatenate(
        [
            total_of([own[:half], first_top, second_top]),
            total_of([own[half:], first_bottom, second_bottom]),
        ],
        axis=0,
    )


def scatter_blocks(parts):
    return scatter_finish(scatter_start(parts))


def after(values, events):
    return lax.optimization_barrier((values, events))[0]


def send_parts(parts, events):
    if lax.axis_size("expert") != 4:
        return [scatter_blocks(parts)]
    low = jnp.bfloat16
    first, second = (
        lax.ppermute(parts[r].astype(low), "expert", pair_moves(4, r)) for r in (1, 2)
    )
    far = lax.ppermute(after(parts[3].astype(low), (first, second, events)), "expert", pair_moves(4, 3))
    return [parts[0], first, second, far]


def total_of(parts):
    total = parts[0].astype(jnp.float32)
    for part in parts[1:]:
        total += part.astype(jnp.float32)
    return total


def shift_dense(rows, events):
    if not cube():
        return [lax.all_gather(rows, ("batch", "expert"), axis=0, tiled=True)]
    below, above = step_up(rows), step_down(rows)
    return [rows, below, step_up(after(below, (above, events))), above]


def dense_start(line, columns, events):
    found = [rows[:, columns] for rows in line]
    if not cube():
        return [found[0][None]]
    return gather_start(after(jnp.stack(found), events))


def dense_finish(state, events=(), late=()):
    if not cube():
        return state, jnp.zeros((1, 1), jnp.int32), ()
    place = lax.axis_index("batch")
    level, core = place // 2, place % 2
    member = lax.axis_index("expert")
    mine = gather_finish(state, events)
    far = mine[3:]
    mine = mine[:3] + [after(jnp.concatenate(far, axis=0), late)]
    other = [exchange_cores(block) for block in mine]
    spots = [
        [(((level + 4 - k) % 4) * 2 + (core ^ c)) * 4 + (member ^ r) for k in range(4)]
        for c in range(2)
        for r in range(4)
    ]
    return mine + other, jnp.array(spots, jnp.int32), far


def sum_chunk(packed_grad):
    return lax.psum_scatter(packed_grad, "batch", scatter_dimension=0, tiled=True)


def exchange_cores(values):
    return lax.ppermute(values, "batch", pair_moves(8, 1))


def step_up(values):
    return lax.ppermute(values, "batch", shift_moves(1))


def step_down(values):
    return lax.ppermute(values, "batch", shift_moves(3))


def add_low(*parts):
    total = parts[0].astype(jnp.float32)
    for part in parts[1:]:
        total += part.astype(jnp.float32)
    return total.astype(jnp.bfloat16)


def join_cores(own, received):
    return [add_low(own[r], received[r]) for r in range(4)]


def line_start(plane):
    level = lax.axis_index("batch") // 2
    own, up, far, down = (
        lax.dynamic_index_in_dim(plane, (level + r) % 4, axis=0, keepdims=False) for r in range(4)
    )
    return own, step_down(add_low(down)), add_low(up, step_up(add_low(far)))


def line_finish(state, events=()):
    own, down, up = state
    return total_of([own, down, step_up(after(up, events))])


def scatter_whole(found):
    values = found[0].reshape(found[0].shape[3:])
    total = lax.psum_scatter(values, ("batch", "expert"), scatter_dimension=0, tiled=True)
    return total.astype(jnp.float32)


def pack_kernel(chunks, query, key, value, small, out, gate, up, down, dense, *packed):
    start = 0
    for part in (query, key, value, small, out):
        dense[:, start : start + part.shape[1]] = part[...]
        start += part.shape[1]
    part, hidden_width = down.shape[1], gate.shape[2]
    for n, target in enumerate(packed):
        for e in range(chunks[n], chunks[n + 1]):
            for side, source in ((0, gate), (1, up)):
                for j in range(3):
                    target[side, e - chunks[n], :, j * hidden_width : (j + 1) * hidden_width] = (
                        source[e, j * part : (j + 1) * part, :]
                    )
            target[2, e - chunks[n]] = down[e]


def pack(chunks, query, key, value, small, out, gate, up, down):
    low = jnp.bfloat16
    columns = sum(part.shape[1] for part in (query, key, value, small, out))
    return pl.pallas_call(
        partial(pack_kernel, chunks),
        in_specs=[INSIDE] * 8,
        out_specs=[INSIDE] * len(chunks),
        out_shape=[jax.ShapeDtypeStruct((query.shape[0], columns), low)]
        + [
            jax.ShapeDtypeStruct((3, b - a) + down.shape[1:], low)
            for a, b in zip(chunks[:-1], chunks[1:])
        ],
        compiler_params=pltpu.CompilerParams(vmem_limit_bytes=VMEM_BYTES),
        cost_estimate=cost(0),
        name="pack",
    )(query, key, value, small, out, gate, up, down)


def local(
    tokens,
    cotangent,
    attn_gain,
    query_weight,
    key_weight,
    value_weight,
    out_weight,
    ffn_gain,
    router_weight,
    gate_weight,
    up_weight,
    down_weight,
    routes,
    ranking,
):
    low = jnp.bfloat16
    wide = jnp.float32
    query_width = HEADS * HEAD_DIM
    kv_width = KV_HEADS * HEAD_DIM
    qkv_width = query_width + 2 * kv_width
    width = tokens.shape[2]
    experts_total = router_weight.shape[1]
    extra = -(-(experts_total + 2) // 128) * 128
    first_gain, second_gain = experts_total, experts_total + 1
    local_experts = gate_weight.shape[0]
    member_count = lax.axis_size("expert")
    member_id = lax.axis_index("expert")
    local_rows = tokens.shape[1]
    group_rows = local_rows * member_count
    cut = cube()
    line_place = lax.axis_index("batch")
    place = jnp.stack([line_place % 2, member_id, line_place // 2]).astype(jnp.int32)

    route_rows = routes[0]
    rank_rows = ranking[0]
    expert_lanes = jnp.arange(extra, dtype=jnp.int32)
    member = jnp.any(route_rows[:, :, None] == expert_lanes[None, None, :], axis=1)
    marks = jnp.where(
        expert_lanes[None, :] == experts_total,
        (rank_rows // 32)[:, None],
        jnp.where(expert_lanes[None, :] == experts_total + 1, (rank_rows % 32)[:, None], member),
    ).astype(low)
    grad_out = cotangent[0]
    small_width = qkv_width + extra
    chunks = (0, 3, local_experts)
    dense_rows, *packed_own = pack(
        chunks,
        query_weight,
        key_weight,
        value_weight,
        jnp.concatenate(
            [
                router_weight,
                attn_gain[:, None],
                ffn_gain[:, None],
                jnp.zeros((query_weight.shape[0], extra - experts_total - 2), low),
            ],
            axis=1,
        ),
        out_weight,
        gate_weight,
        up_weight,
        down_weight,
    )
    row_ids = member_id * local_rows + jnp.arange(local_rows, dtype=jnp.int32)
    half_dim = HEAD_DIM // 2
    frequency = THETA ** (-jnp.arange(half_dim, dtype=wide) / half_dim)
    angles = place_of(row_ids).astype(wide)[:, None] * frequency[None, :]
    cosine = jnp.tile(jnp.cos(angles), (1, 4))
    sine_part = jnp.tile(jnp.concatenate([-jnp.sin(angles), jnp.sin(angles)], axis=1), (1, 2))
    if member_count == 4:
        away = 1 << 20
        starts = [
            jnp.where(member_id >= 1, 0, away),
            jnp.where(member_id >= 2, local_rows, away),
            member_id * local_rows,
        ]
    else:
        starts = [(member_id ^ r) * local_rows for r in range(member_count)]
    key_ids = jnp.concatenate([s + jnp.arange(local_rows, dtype=jnp.int32) for s in starts])
    bias = jnp.where(visible(row_ids, key_ids), 0.0, -1e30).astype(wide)
    bias_turned = bias.T
    tables = (cosine, sine_part, bias, bias_turned)

    line = shift_dense(dense_rows, tables)
    grad_state = gather_start(jnp.concatenate([grad_out, marks], axis=1))
    grad_blocks = gather_finish(grad_state, line[1::2])
    marks_all = jnp.concatenate([block[:, width:] for block in grad_blocks], axis=0)
    qkv_state = dense_start(line, slice(0, small_width), ())
    plane = qkv_state[1:]
    qkv_pieces, qkv_spots, far = dense_finish(qkv_state)
    out_state = dense_start(line, slice(small_width, None), far)
    packed_all = [
        lax.all_gather(after(packed, events), "batch", axis=0)
        for packed, events in zip(packed_own, ((line, grad_blocks), plane))
    ]

    normed, query, keyval, small = enter(
        tokens[0], cosine, sine_part, qkv_pieces, qkv_spots, first_gain, query_width, kv_width
    )

    rank_all = (
        marks_all[:, experts_total].astype(wide) * 32 + marks_all[:, experts_total + 1].astype(wide)
    )
    earlier = (rank_all[None, :] < rank_rows.astype(wide)[:, None]).astype(low)
    before = product(earlier, marks_all)
    capacity = 5 * group_rows * route_rows.shape[1] // (4 * experts_total)
    member = member.astype(wide)
    kept = jnp.where(before < capacity, member, 0.0)

    keyval_blocks = gather_blocks(after(keyval, out_state[1:]))
    if member_count == 4:
        ordered = keyval_blocks[:3] + [jnp.concatenate(keyval_blocks[3:], axis=0)]
        keys = jnp.concatenate(
            [
                lax.select_n(member_id, *ordered),
                lax.select_n(member_id ^ 1, *ordered),
                keyval,
            ],
            axis=0,
        )
    else:
        keys = jnp.concatenate(keyval_blocks, axis=0)
    attended, log_totals = attend(query, keys, bias)
    out_pieces, out_spots, _ = dense_finish(out_state, keyval_blocks[3:], attended)
    residual, sent, gate_rows = project(
        attended, tokens[0], small, member, kept, second_gain, out_pieces, out_spots
    )
    sent_blocks = gather_blocks(sent)

    carry, chunk_grads = None, []
    for packed, a, b in zip(packed_all, chunks[:-1], chunks[1:]):
        first = (member_id * local_experts + a).astype(jnp.int32).reshape(1)
        packed_grads, mixture_all, row_grad = expert_pass(
            place,
            first,
            sent_blocks,
            grad_blocks,
            packed,
            carry,
            cut and b == local_experts,
            b == local_experts,
        )
        carry = (mixture_all, row_grad)
        chunk_grads.append(packed_grads)

    def blocks_of(values):
        return [values[r * local_rows : (r + 1) * local_rows] for r in range(member_count)]

    totals = [sum_chunk(chunk_grads[0][0])]
    if cut:
        own, rest, far, near = chunk_grads[1]
        far, near = exchange_cores(far), exchange_cores(near)
        far_sum, down_sum = add_low(rest[1], far[0]), add_low(rest[2], far[1])
    turn_state = scatter_start(blocks_of(row_grad))
    if cut:
        turn_state = after(turn_state, (far_sum, down_sum))
    normed_grad = scatter_finish(turn_state)
    turned = turn(
        place,
        out_spots,
        (
            normed_grad,
            residual,
            grad_out,
            small,
            gate_rows,
            member,
            kept,
            sent,
            attended,
        ),
        out_pieces,
        cut,
        second_gain,
    )
    out_found = turned[:-2]
    resid_grad, head_grad = turned[-2:]
    mixture_parts = send_parts(blocks_of(after(mixture_all, normed_grad)), resid_grad)
    if cut:
        head_grad = after(head_grad, mixture_parts[1:3])
        up_part = step_up(far_sum)
    query_grad, key_grads = attend_back(
        head_grad, query, keys, bias_turned, log_totals, cosine, sine_part
    )
    if member_count == 4:
        zero = jnp.zeros((), low)
        for_first, for_second, for_own = blocks_of(key_grads)[:3]
        key_parts = []
        for r in range(4):
            part = jnp.where(member_id == r, for_first, zero)
            part += jnp.where(member_id ^ 1 == r, for_second, zero)
            key_parts.append(part + for_own if r == 0 else part)
    else:
        key_parts = blocks_of(key_grads)
    if cut:
        out_found = out_found[1], exchange_cores(out_found[0])
        key_parts = after(key_parts, mixture_parts[3])
    keyval_sum = scatter_blocks(key_parts)
    if cut:
        out_state = scatter_start(join_cores(*out_found))
    if cut:
        keyval_sum = after(keyval_sum, out_found)
    left = leave(
        place,
        qkv_spots,
        (
            keyval_sum,
            query_grad,
            normed,
            tokens[0],
            resid_grad,
            small,
            cosine,
            sine_part,
        ),
        qkv_pieces,
        cut,
        first_gain,
    )
    qkv_found, input_grad = left[:-1], left[-1]
    result = (residual + total_of(mixture_parts)).astype(low)
    if cut:
        received = exchange_cores(after(qkv_found[0], (totals[0], out_state[1:], up_part)))
        out_plane = scatter_finish(out_state)
        up_term = step_up(add_low(rest[0], near[0], after(up_part, received)))
        down_term = step_down(after(down_sum, up_term))
        qkv_parts = join_cores(qkv_found[1], after(received, out_plane))
        qkv_state = after(scatter_start(qkv_parts), up_term)
        qkv_plane = scatter_finish(qkv_state)
        out_sum = line_finish(line_start(out_plane))
        qkv_state = line_start(qkv_plane)
        near, down_term, up_term = after((near, down_term, up_term), qkv_plane)
        terms = [[(totals[0], 0)], [(own, None), (near, 1), (down_term, None), (up_term, None)]]
        expert_totals = unpack(terms, gate_weight.shape, down_weight.shape)
        qkv_sum = line_finish(qkv_state, down_term)
    else:
        out_sum = scatter_whole(out_found)
        qkv_sum = scatter_whole(qkv_found)
        totals += [sum_chunk(found[0]) for found in chunk_grads[1:]]
        terms = [[(total, 0)] for total in totals]
        expert_totals = unpack(terms, gate_weight.shape, down_weight.shape)
    gate_total, up_total, down_total = expert_totals
    return (
        result[None],
        input_grad[None],
        qkv_sum[:, qkv_width + first_gain],
        qkv_sum[:, :query_width],
        qkv_sum[:, query_width : query_width + kv_width],
        qkv_sum[:, query_width + kv_width : qkv_width],
        out_sum[:, :width],
        out_sum[:, width + second_gain],
        out_sum[:, width : width + experts_total],
        gate_total,
        up_total,
        down_total,
    )


def solution(mesh):
    return jax.shard_map(
        local,
        mesh=mesh,
        in_specs=(
            P("batch", "expert", None),
            P("batch", "expert", None),
            P(("batch", "expert")),
            P(("batch", "expert"), None),
            P(("batch", "expert"), None),
            P(("batch", "expert"), None),
            P(("batch", "expert"), None),
            P(("batch", "expert")),
            P(("batch", "expert"), None),
            P("expert", "batch", None),
            P("expert", "batch", None),
            P("expert", "batch", None),
            P("batch", "expert", None),
            P("batch", "expert"),
        ),
        out_specs=(
            P("batch", "expert", None),
            P("batch", "expert", None),
            P(("batch", "expert")),
            P(("batch", "expert"), None),
            P(("batch", "expert"), None),
            P(("batch", "expert"), None),
            P(("batch", "expert"), None),
            P(("batch", "expert")),
            P(("batch", "expert"), None),
            P("expert", "batch", None),
            P("expert", "batch", None),
            P("expert", "batch", None),
        ),
        check_vma=False,
    )
```

```python
from functools import partial

import jax
import jax.numpy as jnp
from jax import lax
from jax.experimental import pallas as pl
from jax.experimental.pallas import tpu as pltpu
from jax.sharding import PartitionSpec as P

HEADS = 24
KV_HEADS = 8
HEAD_DIM = 64
PROMPT = 512
CLEN = 256


EPS = 1e-06
THETA = 10000.0


def product(left, right):
    return jnp.dot(left, right, preferred_element_type=jnp.float32)


def place_of(row_ids):
    return jnp.where(row_ids < PROMPT, row_ids, PROMPT + (row_ids - PROMPT) % CLEN)


def visible(query_ids, key_ids):
    causal = key_ids[None, :] <= query_ids[:, None]
    same_run = (key_ids[None, :] - PROMPT) // CLEN == (query_ids[:, None] - PROMPT) // CLEN
    return causal & ((key_ids[None, :] < PROMPT) | same_run)


def dot_plain(left, right):
    return lax.dot_general(left, right, (((1,), (0,)), ((), ())), preferred_element_type=jnp.float32)


def dot_right(left, right):
    return lax.dot_general(left, right, (((1,), (1,)), ((), ())), preferred_element_type=jnp.float32)


def dot_left(left, right):
    return lax.dot_general(left, right, (((0,), (0,)), ((), ())), preferred_element_type=jnp.float32)


ANYWHERE = pl.BlockSpec(memory_space=pl.ANY)
INSIDE = pl.BlockSpec(memory_space=pltpu.VMEM)
SCALARS = pl.BlockSpec(memory_space=pltpu.SMEM)
VMEM_BYTES = 62 * 1024 * 1024


def cost(flops, *arrays):
    return pl.CostEstimate(flops=1, bytes_accessed=1, transcendentals=0)


def weight_copies(spots, pieces, target, sems):
    copies = []
    for p, piece in enumerate(pieces):
        blocks, rows = piece.shape[0], piece.shape[1]
        for k in range(blocks):
            place = pl.multiple_of(spots[p, k] * rows, rows)
            copies.append(
                pltpu.make_async_copy(
                    piece.at[k], target.at[pl.ds(place, rows)], sems.at[p * blocks + k]
                )
            )
    return copies


def block_copies(blocks, target, sems, first, columns=None):
    copies = []
    start = 0
    for i, block in enumerate(blocks):
        rows = block.shape[0]
        source = block if columns is None else block.at[:, columns]
        copies.append(
            pltpu.make_async_copy(source, target.at[pl.ds(start, rows)], sems.at[first + i])
        )
        start += rows
    return copies


def swap_halves(values):
    half = HEAD_DIM // 2
    lane = lax.broadcasted_iota(jnp.int32, values.shape, 1)
    return jnp.where(
        lane % HEAD_DIM < half,
        pltpu.roll(values, 2 * HEAD_DIM - half, 1),
        pltpu.roll(values, half, 1),
    )


def mean_square_scale(values):
    return lax.rsqrt(jnp.mean(values * values, axis=-1, keepdims=True) + EPS)


def enter_kernel(count, gain_at, spots, tokens, cosine, sine, *refs):
    pieces = refs[:count]
    normed, query, keyval, small, weight, sems = refs[count:]
    low = jnp.bfloat16
    copies = weight_copies(spots, pieces, weight, sems)
    for copy in copies:
        copy.start()
    inputs = tokens[...].astype(jnp.float32)
    scaled = inputs * mean_square_scale(inputs)
    for copy in copies:
        copy.wait()
    query_width = query.shape[1]
    kv_width = keyval.shape[1] // 2
    qkv_width = query_width + 2 * kv_width
    turned = weight[:, qkv_width:].astype(jnp.float32).T
    small[...] = turned
    rows = (scaled * turned[gain_at : gain_at + 1]).astype(low)
    normed[...] = rows
    pair = 2 * HEAD_DIM
    scale = HEAD_DIM**-0.5
    for start in range(0, query_width + kv_width, 512):
        product_part = dot_plain(rows, weight[:, start : start + 512])
        for offset in range(0, 512, pair):
            part = product_part[:, offset : offset + pair]
            part = part * cosine[...] + swap_halves(part) * sine[...]
            at = start + offset
            if at < query_width:
                query[:, at : at + pair] = (part * scale).astype(low)
            else:
                keyval[:, at - query_width : at - query_width + pair] = part.astype(low)
    keyval[:, kv_width:] = dot_plain(
        rows, weight[:, query_width + kv_width : qkv_width]
    ).astype(low)


def enter(tokens, cosine, sine, pieces, spots, gain_at, query_width, kv_width):
    rows, width = tokens.shape
    columns = pieces[0].shape[2]
    low = jnp.bfloat16
    return pl.pallas_call(
        partial(enter_kernel, len(pieces), gain_at),
        in_specs=[SCALARS, INSIDE, INSIDE, INSIDE] + [ANYWHERE] * len(pieces),
        out_specs=[INSIDE] * 4,
        out_shape=[
            jax.ShapeDtypeStruct((rows, width), low),
            jax.ShapeDtypeStruct((rows, query_width), low),
            jax.ShapeDtypeStruct((rows, 2 * kv_width), low),
            jax.ShapeDtypeStruct((columns - query_width - 2 * kv_width, width), jnp.float32),
        ],
        scratch_shapes=[
            pltpu.VMEM((width, columns), low),
            pltpu.SemaphoreType.DMA((len(pieces) * pieces[0].shape[0],)),
        ],
        compiler_params=pltpu.CompilerParams(vmem_limit_bytes=VMEM_BYTES),
        cost_estimate=cost(2 * rows * width * columns, *pieces),
        name="enter",
    )(spots, tokens, cosine, sine, *pieces)


def both_places(values):
    wide = values.astype(jnp.float32)
    low_lane = lax.broadcasted_iota(jnp.int32, values.shape, 1) < HEAD_DIM
    moved = pltpu.roll(wide, HEAD_DIM, 1)
    kind = values.dtype
    return [
        [jnp.where(low_lane, wide, 0.0).astype(kind), jnp.where(low_lane, 0.0, moved).astype(kind)],
        [jnp.where(low_lane, moved, 0.0).astype(kind), jnp.where(low_lane, 0.0, wide).astype(kind)],
    ]


def attend_kernel(query, keyval, bias, attended, log_totals):
    low = jnp.bfloat16
    rows = query.shape[0]
    kv_width = keyval.shape[1] // 2
    pair_lanes = 2 * HEAD_DIM
    repeat = HEADS // KV_HEADS
    log_totals[...] = jnp.zeros_like(log_totals)
    lane = lax.broadcasted_iota(jnp.int32, log_totals.shape, 1)

    @pl.loop(0, KV_HEADS // 2)
    def _(pair):
        at = pl.ds(pl.multiple_of(pair * pair_lanes, pair_lanes), pair_lanes)
        keys = both_places(keyval[:, at])
        at = pl.ds(pl.multiple_of(kv_width + pair * pair_lanes, pair_lanes), pair_lanes)
        values = both_places(keyval[:, at])
        for i in range(repeat):
            at = pl.ds(pl.multiple_of((pair * repeat + i) * pair_lanes, pair_lanes), pair_lanes)
            queries = query[:, at]
            total = jnp.zeros((rows, pair_lanes), jnp.float32)
            for a in range(2):
                head = 2 * i + a
                scores = dot_right(queries, keys[head // repeat][a]) + bias[...]
                peak = jnp.max(scores, axis=-1, keepdims=True)
                lifted = jnp.exp(scores - peak)
                row_total = jnp.sum(lifted, axis=-1, keepdims=True)
                weights_low = (lifted * (1.0 / row_total)).astype(low)
                total += dot_plain(weights_low, values[head // repeat][a])
                log_totals[...] = jnp.where(
                    lane == pair * (2 * repeat) + head, peak + jnp.log(row_total), log_totals[...]
                )
            attended[:, at] = total.astype(low)


def attend(query, keyval, bias):
    rows, query_width = query.shape
    return pl.pallas_call(
        attend_kernel,
        in_specs=[INSIDE] * 3,
        out_specs=[INSIDE] * 2,
        out_shape=[
            jax.ShapeDtypeStruct((rows, query_width), jnp.bfloat16),
            jax.ShapeDtypeStruct((rows, 128), jnp.float32),
        ],
        compiler_params=pltpu.CompilerParams(vmem_limit_bytes=VMEM_BYTES),
        cost_estimate=cost(8 * rows * query_width * bias.shape[1], query, keyval, bias),
        name="attend",
    )(query, keyval, bias)


def project_kernel(count, gain_at, spots, attended, tokens, small, member, kept, *refs):
    pieces = refs[:count]
    residual, sent, gate_rows, weight, sems = refs[count:]
    low = jnp.bfloat16
    width = tokens.shape[1]
    copies = weight_copies(spots, pieces, weight, sems)
    for copy in copies:
        copy.start()
    for copy in copies:
        copy.wait()
    hidden = tokens[...].astype(jnp.float32) + dot_plain(attended[...], weight[...])
    residual[...] = hidden
    gain = small[gain_at : gain_at + 1, :]
    normed = (hidden * mean_square_scale(hidden) * gain).astype(low)
    logits = dot_right(normed, small[...].astype(low))
    chosen = member[...] > 0.0
    logits = jnp.where(chosen, logits, -1e30)
    lifted = jnp.where(chosen, jnp.exp(logits - jnp.max(logits, axis=-1, keepdims=True)), 0.0)
    gates = lifted / jnp.sum(lifted, axis=-1, keepdims=True)
    gate_rows[...] = gates
    sent[:, :width] = normed
    sent[:, width:] = (gates * kept[...]).astype(low)


def project(attended, tokens, small, member, kept, gain_at, pieces, spots):
    rows, width = tokens.shape
    lanes = small.shape[0]
    low = jnp.bfloat16
    return pl.pallas_call(
        partial(project_kernel, len(pieces), gain_at),
        in_specs=[SCALARS] + [INSIDE] * 5 + [ANYWHERE] * len(pieces),
        out_specs=[INSIDE] * 3,
        out_shape=[
            jax.ShapeDtypeStruct((rows, width), jnp.float32),
            jax.ShapeDtypeStruct((rows, width + lanes), low),
            jax.ShapeDtypeStruct((rows, lanes), jnp.float32),
        ],
        scratch_shapes=[
            pltpu.VMEM((attended.shape[1], width), low),
            pltpu.SemaphoreType.DMA((len(pieces) * pieces[0].shape[0],)),
        ],
        compiler_params=pltpu.CompilerParams(vmem_limit_bytes=VMEM_BYTES),
        cost_estimate=cost(2 * rows * width * width, *pieces),
        name="project",
    )(spots, attended, tokens, small, member, kept, *pieces)


def grad_shapes(cut, rows, columns):
    low = jnp.bfloat16
    if cut:
        block = rows // 32
        return (
            [jax.ShapeDtypeStruct((4, 4, block, columns), low)] * 2,
            pltpu.VMEM((4, 2, 4, block, columns), low),
        )
    return (
        [jax.ShapeDtypeStruct((1, 1, 1, rows, columns), low)],
        pltpu.VMEM((1, 1, 1, rows, columns), low),
    )


def grad_copies(cut, place, source, outs, sems):
    if not cut:
        return [pltpu.make_async_copy(source, outs[0], sems.at[0])]
    core, member = place[0], place[1]
    other, own = outs
    copies = []
    for r in range(4):
        copies.append(
            pltpu.make_async_copy(
                source.at[:, 1 - core, member ^ r], other.at[r], sems.at[2 * r]
            )
        )
        copies.append(
            pltpu.make_async_copy(source.at[:, core, member ^ r], own.at[r], sems.at[2 * r + 1])
        )
    return copies


def turn_kernel(
    count,
    cut,
    gain_at,
    place,
    spots,
    normed_grad,
    residual,
    grad_out,
    small,
    gate_rows,
    member,
    kept,
    normed,
    attended,
    *refs,
):
    pieces = refs[:count]
    refs = refs[count:]
    outs = refs[: (2 if cut else 1)]
    resid_grad, head_grad, weight, weight_grad, sems, out_sems = refs[len(outs) :]
    low = jnp.bfloat16
    rows, width = residual.shape
    lanes = gate_rows.shape[1]
    copies = weight_copies(spots, pieces, weight, sems)
    for copy in copies:
        copy.start()
    lane = lax.broadcasted_iota(jnp.int32, (rows, lanes), 1)
    gates = gate_rows[...]
    gate_grads = normed_grad[:, width:] * kept[...]
    chosen_grad = gates * (gate_grads - jnp.sum(gates * gate_grads, axis=-1, keepdims=True))
    logit_grad = (chosen_grad * member[...]).astype(low)
    hidden = residual[...]
    scale = mean_square_scale(hidden)
    row_grad = normed_grad[:, :width] + dot_plain(logit_grad, small[...].astype(low))
    gain = small[gain_at : gain_at + 1, :]
    scaled = row_grad * gain
    total_grad = (
        grad_out[...].astype(jnp.float32)
        + scale * scaled
        - hidden * (scale * scale * scale) * jnp.mean(scaled * hidden, axis=-1, keepdims=True)
    )
    resid_grad[...] = total_grad
    attn_grad = total_grad.astype(low)
    shape = weight_grad.shape[:-1]
    gain_grad = (row_grad * hidden * scale).astype(low)
    picks = jnp.where(lane == gain_at, 1.0, 0.0).astype(low)
    weight_grad[..., width:] = (
        (dot_left(normed[...][:, :width], logit_grad) + dot_left(gain_grad, picks))
        .astype(low)
        .reshape(shape + (lanes,))
    )
    for start in range(0, width, 512):
        weight_grad[..., start : start + 512] = (
            dot_left(attended[...], attn_grad[:, start : start + 512])
            .astype(low)
            .reshape(shape + (512,))
        )
    out_copies = grad_copies(cut, place, weight_grad, outs, out_sems)
    for copy in out_copies:
        copy.start()
    for copy in copies:
        copy.wait()
    head_grad[...] = dot_right(attn_grad, weight[...]).astype(low)
    for copy in out_copies:
        copy.wait()


def turn(place, spots, operands, pieces, cut, gain_at):
    residual, gate_rows, attended = operands[1], operands[4], operands[8]
    rows, width = residual.shape
    query_width = attended.shape[1]
    low = jnp.bfloat16
    grads, held = grad_shapes(cut, query_width, width + gate_rows.shape[1])
    return pl.pallas_call(
        partial(turn_kernel, len(pieces), cut, gain_at),
        in_specs=[SCALARS, SCALARS] + [INSIDE] * len(operands) + [ANYWHERE] * len(pieces),
        out_specs=[ANYWHERE] * len(grads) + [INSIDE] * 2,
        out_shape=grads
        + [
            jax.ShapeDtypeStruct((rows, width), jnp.float32),
            jax.ShapeDtypeStruct((rows, query_width), low),
        ],
        scratch_shapes=[
            pltpu.VMEM((query_width, width), low),
            held,
            pltpu.SemaphoreType.DMA((len(pieces) * pieces[0].shape[0],)),
            pltpu.SemaphoreType.DMA((8,)),
        ],
        compiler_params=pltpu.CompilerParams(vmem_limit_bytes=VMEM_BYTES),
        cost_estimate=cost(0),
        name="turn",
    )(place, spots, *operands, *pieces)


def attend_back_kernel(
    head_grad, query, keyval, bias, log_totals, cosine, sine, query_grad, keyval_grad, totals
):
    low = jnp.bfloat16
    rows = query.shape[0]
    kv_width = keyval.shape[1] // 2
    pair_lanes = 2 * HEAD_DIM
    repeat = HEADS // KV_HEADS
    totals[...] = log_totals[...].T

    @pl.loop(0, KV_HEADS // 2)
    def _(pair):
        key_at = pl.ds(pl.multiple_of(pair * pair_lanes, pair_lanes), pair_lanes)
        value_at = pl.ds(pl.multiple_of(kv_width + pair * pair_lanes, pair_lanes), pair_lanes)
        keys = both_places(keyval[:, key_at])
        values = both_places(keyval[:, value_at])
        key_grads = [[None, None], [None, None]]
        value_grads = [[None, None], [None, None]]
        for i in range(repeat):
            at = pl.ds(pl.multiple_of((pair * repeat + i) * pair_lanes, pair_lanes), pair_lanes)
            queries = query[:, at]
            grads = head_grad[:, at]
            query_part = jnp.zeros((rows, pair_lanes), jnp.float32)
            for a in range(2):
                head = 2 * i + a
                g = head // repeat
                total = totals[pl.ds(pair * (2 * repeat) + head, 1), :]
                weights = jnp.exp(dot_right(keys[g][a], queries) + bias[...] - total)
                weight_grads = dot_right(values[g][a], grads)
                delta = jnp.sum(weights * weight_grads, axis=0, keepdims=True)
                score_grads = (weights * (weight_grads - delta)).astype(low)
                value_part = dot_plain(weights.astype(low), grads)
                key_part = dot_plain(score_grads, queries)
                query_part += dot_left(score_grads, keys[g][a])
                if key_grads[g][a] is None:
                    key_grads[g][a], value_grads[g][a] = key_part, value_part
                else:
                    key_grads[g][a] += key_part
                    value_grads[g][a] += value_part
            query_part = query_part * (HEAD_DIM**-0.5)
            query_part = query_part * cosine[...] - swap_halves(query_part) * sine[...]
            query_grad[:, at] = query_part.astype(low)
        low_lane = lax.broadcasted_iota(jnp.int32, (keyval.shape[0], pair_lanes), 1) < HEAD_DIM
        for at, found in ((key_at, key_grads), (value_at, value_grads)):
            keyval_grad[:, at] = jnp.where(
                low_lane,
                found[0][0] + pltpu.roll(found[0][1], HEAD_DIM, 1),
                pltpu.roll(found[1][0], HEAD_DIM, 1) + found[1][1],
            ).astype(low)


def attend_back(head_grad, query, keyval, bias, log_totals, cosine, sine):
    rows, query_width = query.shape
    low = jnp.bfloat16
    return pl.pallas_call(
        attend_back_kernel,
        in_specs=[INSIDE] * 7,
        out_specs=[INSIDE] * 2,
        out_shape=[
            jax.ShapeDtypeStruct((rows, query_width), low),
            jax.ShapeDtypeStruct(keyval.shape, low),
        ],
        scratch_shapes=[pltpu.VMEM((128, rows), jnp.float32)],
        compiler_params=pltpu.CompilerParams(vmem_limit_bytes=VMEM_BYTES),
        cost_estimate=cost(0),
        name="attend_back",
    )(head_grad, query, keyval, bias, log_totals, cosine, sine)


def leave_kernel(
    count,
    cut,
    gain_at,
    place,
    spots,
    keyval_sum,
    query_grad,
    normed,
    tokens,
    resid_grad,
    small,
    cosine,
    sine,
    *refs,
):
    pieces = refs[:count]
    refs = refs[count:]
    outs = refs[: (2 if cut else 1)]
    input_grad, weight, weight_grad, joined, sems, out_sems = refs[len(outs) :]
    low = jnp.bfloat16
    rows, width = tokens.shape
    query_width = query_grad.shape[1]
    kv_width = keyval_sum.shape[1] // 2
    qkv_width = query_width + 2 * kv_width
    pair = 2 * HEAD_DIM
    copies = weight_copies(spots, pieces, weight, sems)
    for copy in copies:
        copy.start()
    joined[:, :query_width] = query_grad[...]
    for start in range(0, kv_width, pair):
        part = keyval_sum[:, start : start + pair]
        part = part * cosine[...] - swap_halves(part) * sine[...]
        joined[:, query_width + start : query_width + start + pair] = part.astype(low)
    joined[:, query_width + kv_width :] = keyval_sum[:, kv_width:].astype(low)
    shape = weight_grad.shape[:-1]
    for start in range(0, qkv_width, 512):
        weight_grad[..., start : start + 512] = (
            dot_left(normed[...], joined[:, start : start + 512]).astype(low).reshape(shape + (512,))
        )
    for copy in copies:
        copy.wait()
    row_grad = dot_right(joined[...], weight[:, :qkv_width])
    inputs = tokens[...].astype(jnp.float32)
    scale = mean_square_scale(inputs)
    lanes = weight_grad.shape[-1] - qkv_width
    lane = lax.broadcasted_iota(jnp.int32, (rows, lanes), 1)
    picks = jnp.where(lane == gain_at, 1.0, 0.0).astype(low)
    weight_grad[..., qkv_width:] = (
        dot_left((row_grad * inputs * scale).astype(low), picks).astype(low).reshape(shape + (lanes,))
    )
    out_copies = grad_copies(cut, place, weight_grad, outs, out_sems)
    for copy in out_copies:
        copy.start()
    scaled = row_grad * small[gain_at : gain_at + 1, :]
    input_grad[...] = (
        resid_grad[...]
        + scale * scaled
        - inputs * (scale * scale * scale) * jnp.mean(scaled * inputs, axis=-1, keepdims=True)
    )
    for copy in out_copies:
        copy.wait()


def leave(place, spots, operands, pieces, cut, gain_at):
    tokens, query_grad, keyval_sum = operands[3], operands[1], operands[0]
    rows, width = tokens.shape
    columns = pieces[0].shape[2]
    low = jnp.bfloat16
    grads, held = grad_shapes(cut, width, columns)
    return pl.pallas_call(
        partial(leave_kernel, len(pieces), cut, gain_at),
        in_specs=[SCALARS, SCALARS] + [INSIDE] * len(operands) + [ANYWHERE] * len(pieces),
        out_specs=[ANYWHERE] * len(grads) + [INSIDE],
        out_shape=grads + [jax.ShapeDtypeStruct((rows, width), jnp.float32)],
        scratch_shapes=[
            pltpu.VMEM((width, columns), low),
            held,
            pltpu.VMEM((rows, query_grad.shape[1] + keyval_sum.shape[1]), low),
            pltpu.SemaphoreType.DMA((len(pieces) * pieces[0].shape[0],)),
            pltpu.SemaphoreType.DMA((8,)),
        ],
        compiler_params=pltpu.CompilerParams(vmem_limit_bytes=VMEM_BYTES),
        cost_estimate=cost(0),
        name="leave",
    )(place, spots, *operands, *pieces)


def expert_kernel(cut, carried, last, row_blocks, grad_blocks, row_tile, place, first, packed, *refs):
    blocks_in = refs[:row_blocks]
    grads_in = refs[row_blocks : row_blocks + grad_blocks]
    refs = refs[row_blocks + grad_blocks :]
    if carried:
        mix_in, turn_in = refs[:2]
        refs = refs[2:]
    count = packed.shape[2]
    outs = 4 if cut else 1
    packed_grads = refs[:outs]
    mix_out, turn_out = refs[outs : outs + 2]
    refs = refs[outs + 2 :]
    if last:
        mix, turned = refs[:2]
        refs = refs[2:]
    else:
        mix, turned = mix_out, turn_out
    (
        rows,
        grads,
        gates,
        gate_w,
        up_w,
        down_w,
        gate_g,
        up_g,
        down_g,
        weighted,
        gate_side,
        up_side,
        load_sems,
        save_sems,
        carry_sems,
    ) = refs
    hidden_width = gate_w.shape[-1]
    total_rows, width = rows.shape
    lanes = gates.shape[1]
    low = jnp.bfloat16

    def sides(gate, up, down):
        for side, inner in ((0, gate), (1, up)):
            for j in range(3):
                yield side, pl.ds(j * hidden_width, hidden_width), inner, j
        yield 2, pl.ds(0, width), down, None

    def loads(e):
        slot = e % 2
        copies = []
        for i, (side, columns, inner, j) in enumerate(sides(gate_w, up_w, down_w)):
            outer = packed.at[:, side, e, :, columns]
            inner = inner.at[slot] if j is None else inner.at[slot, :, j]
            copies.append(pltpu.make_async_copy(outer, inner, load_sems.at[slot, i]))
        return copies

    def saves(e):
        slot = e % 2
        copies = []
        for i, (side, columns, inner, j) in enumerate(sides(gate_g, up_g, down_g)):
            if not cut:
                outer = packed_grads[0].at[:, side, e, :, columns]
                source = inner.at[slot] if j is None else inner.at[slot, :, j]
                copies.append(pltpu.make_async_copy(source, outer, save_sems.at[slot, i]))
                continue
            own, rest, far, near = packed_grads
            targets = [own, rest.at[0], rest.at[1], rest.at[2]]
            targets += [near.at[1], near.at[0], far.at[0], far.at[1]]
            for n, target in enumerate(targets):
                block = 2 * lax.rem(place[2] + n % 4, 4) + (place[0] ^ (n // 4))
                source = inner.at[slot, block] if j is None else inner.at[slot, block, j]
                outer = target.at[side, e, :, columns]
                copies.append(pltpu.make_async_copy(source, outer, save_sems.at[slot, 8 * i + n]))
        return copies

    carries = (
        block_copies(grads_in, grads, carry_sems, 0, pl.ds(0, width))
        + block_copies(blocks_in, rows, carry_sems, grad_blocks, pl.ds(0, width))
        + block_copies(
            blocks_in, gates, carry_sems, grad_blocks + row_blocks, pl.ds(width, lanes)
        )
    )
    sums = []
    if carried:
        at = grad_blocks + 2 * row_blocks
        sums = [
            pltpu.make_async_copy(mix_in, mix, carry_sems.at[at]),
            pltpu.make_async_copy(turn_in, turned, carry_sems.at[at + 1]),
        ]
    for copy in loads(0) + carries + sums:
        copy.start()
    for e in range(count):
        slot = e % 2
        if e + 1 < count:
            for copy in loads(e + 1):
                copy.start()
        for copy in loads(e):
            copy.wait()
        if e == 0:
            for copy in carries:
                copy.wait()
            if not carried:
                turned[:, width:] = jnp.zeros((total_rows, lanes), jnp.float32)

        @pl.loop(0, total_rows // row_tile)
        def _(tile):
            span = pl.ds(pl.multiple_of(tile * row_tile, row_tile), row_tile)
            gate_full = gate_w[slot].reshape(width, hidden_width)
            up_full = up_w[slot].reshape(width, hidden_width)
            down_full = down_w[slot].reshape(hidden_width, width)
            here = rows[span, :]
            slope = dot_right(grads[span, :], down_full)
            gate_pre = dot_plain(here, gate_full)
            up_pre = dot_plain(here, up_full)
            lane = lax.broadcasted_iota(jnp.int32, (row_tile, lanes), 1)
            chosen = lane == first[0] + e
            gate_column = jnp.sum(
                jnp.where(chosen, gates[span, :].astype(jnp.float32), 0.0), axis=1, keepdims=True
            )
            sigmoid_gate = jax.nn.sigmoid(gate_pre)
            activated = gate_pre * sigmoid_gate
            hidden = (activated * up_pre).astype(low).astype(jnp.float32)
            share = jnp.sum(hidden * slope, axis=1, keepdims=True)
            if e == 0 and sums:

                @pl.when(tile == 0)
                def _():
                    for copy in sums:
                        copy.wait()

            turned[span, width:] = jnp.where(chosen, share, turned[span, width:])
            part_weighted = (hidden * gate_column).astype(low)
            hidden_grad = slope * gate_column
            part_gate = (
                hidden_grad * up_pre * (sigmoid_gate + activated * (1.0 - sigmoid_gate))
            ).astype(low)
            part_up = (hidden_grad * activated).astype(low)
            weighted[span, :] = part_weighted
            gate_side[span, :] = part_gate
            up_side[span, :] = part_up
            mix_part = dot_plain(part_weighted, down_full)
            turn_part = dot_right(part_gate, gate_full) + dot_right(part_up, up_full)
            if e == 0 and not carried:
                mix[span, :] = mix_part
                turned[span, :width] = turn_part
            elif last and e == count - 1:
                mix_out[span, :] = (mix[span, :] + mix_part).astype(low)
                turn_out[span, :width] = (turned[span, :width] + turn_part).astype(low)
                turn_out[span, width:] = turned[span, width:].astype(low)
            else:
                mix[span, :] += mix_part
                turned[span, :width] += turn_part

        if e >= 2:
            for copy in saves(e - 2):
                copy.wait()
        down_g[slot] = dot_left(weighted[...], grads[...]).astype(low).reshape(down_g.shape[1:])
        gate_g[slot] = dot_left(rows[...], gate_side[...]).astype(low).reshape(gate_g.shape[1:])
        up_g[slot] = dot_left(rows[...], up_side[...]).astype(low).reshape(up_g.shape[1:])
        for copy in saves(e):
            copy.start()
    for e in range(max(0, count - 2), count):
        for copy in saves(e):
            copy.wait()


def expert_pass(place, first, rows, grads, packed, carry, cut, last):
    blocks, _, count, part, width = packed.shape
    hidden_width = blocks * part
    total_rows = sum(block.shape[0] for block in rows)
    lanes = rows[0].shape[1] - width
    low = jnp.bfloat16
    wide = jnp.float32
    carried = carry is not None
    flops = 18 * total_rows * count * hidden_width * width
    side = pltpu.VMEM((2, blocks, 3, part, hidden_width), low)
    sides = [side, side, pltpu.VMEM((2, blocks, part, width), low)]
    sums = [(total_rows, width), (total_rows, width + lanes)]
    one = packed.shape[1:]
    grads_out = [one, (3,) + one, (2,) + one, (2,) + one] if cut else [packed.shape]
    outs = len(grads_out)
    found = pl.pallas_call(
        partial(expert_kernel, cut, carried, last, len(rows), len(grads), min(512, total_rows)),
        in_specs=[SCALARS, SCALARS]
        + [ANYWHERE] * (1 + len(rows) + len(grads) + (2 if carried else 0)),
        out_specs=[ANYWHERE] * outs + [INSIDE, INSIDE],
        out_shape=[jax.ShapeDtypeStruct(shape, low) for shape in grads_out]
        + [jax.ShapeDtypeStruct(shape, low if last else wide) for shape in sums],
        scratch_shapes=([pltpu.VMEM(shape, wide) for shape in sums] if last else [])
        + [
            pltpu.VMEM((total_rows, width), low),
            pltpu.VMEM((total_rows, width), low),
            pltpu.VMEM((total_rows, lanes), low),
        ]
        + sides
        + sides
        + [pltpu.VMEM((total_rows, hidden_width), low)] * 3
        + [
            pltpu.SemaphoreType.DMA((2, 7)),
            pltpu.SemaphoreType.DMA((2, 56)),
            pltpu.SemaphoreType.DMA((2 * len(rows) + len(grads) + 2,)),
        ],
        compiler_params=pltpu.CompilerParams(vmem_limit_bytes=VMEM_BYTES),
        cost_estimate=cost(flops, packed, packed, *rows, *grads),
        name="experts",
    )(place, first, packed, *rows, *grads, *(carry or ()))
    return found[:outs], found[outs], found[outs + 1]


def unpack_kernel(counts, places, *refs):
    found, (gate, up, down) = refs[:-3], refs[-3:]
    found = [array if place is None else array.at[place] for array, place in zip(found, places)]
    hidden_width = gate.shape[2]
    base = 0
    at = 0
    for terms in counts:
        parts = found[at : at + terms]
        at += terms
        count, part = parts[0].shape[1], parts[0].shape[2]
        for e in range(count):
            for side in range(3):
                total = parts[0][side, e].astype(jnp.float32)
                for other in parts[1:]:
                    total += other[side, e].astype(jnp.float32)
                if side == 2:
                    down[base + e] = total
                    continue
                for j in range(3):
                    (gate, up)[side][base + e, j * part : (j + 1) * part, :] = total[
                        :, j * hidden_width : (j + 1) * hidden_width
                    ]
        base += count


def unpack(chunks, gate_shape, down_shape):
    arrays = [array for terms in chunks for array, _ in terms]
    places = [place for terms in chunks for _, place in terms]
    return pl.pallas_call(
        partial(unpack_kernel, [len(terms) for terms in chunks], places),
        in_specs=[INSIDE] * len(arrays),
        out_specs=[INSIDE] * 3,
        out_shape=[
            jax.ShapeDtypeStruct(gate_shape, jnp.float32),
            jax.ShapeDtypeStruct(gate_shape, jnp.float32),
            jax.ShapeDtypeStruct(down_shape, jnp.float32),
        ],
        compiler_params=pltpu.CompilerParams(vmem_limit_bytes=VMEM_BYTES),
        cost_estimate=cost(0),
        name="unpack",
    )(*arrays)


def cube():
    return lax.axis_size("batch") == 8 and lax.axis_size("expert") == 4


def pair_moves(size, flip):
    return [(i, i ^ flip) for i in range(size)]


def shift_moves(step):
    return [(2 * z + c, 2 * ((z + step) % 4) + c) for z in range(4) for c in range(2)]


def gather_start(rows):
    size = lax.axis_size("expert")
    if size != 4:
        stacked = lax.all_gather(rows, "expert", axis=0)
        own = lax.axis_index("expert")
        return [
            lax.dynamic_index_in_dim(stacked, own ^ r, axis=0, keepdims=False) for r in range(size)
        ]
    return [rows] + [lax.ppermute(rows, "expert", pair_moves(4, r)) for r in (1, 2)]


def gather_finish(state, events=()):
    if lax.axis_size("expert") != 4:
        return state
    first, second = after(state[1:], events)
    half = first.shape[0] // 2
    top = lax.ppermute(second[:half], "expert", pair_moves(4, 1))
    bottom = lax.ppermute(first[half:], "expert", pair_moves(4, 2))
    return state + [top, bottom]


def gather_blocks(rows):
    return gather_finish(gather_start(rows))


def scatter_start(parts):
    low = jnp.bfloat16
    if lax.axis_size("expert") != 4:
        own = lax.axis_index("expert")
        order = jnp.arange(len(parts), dtype=jnp.int32) ^ own
        stacked = jnp.take(jnp.stack(parts), order, axis=0).astype(low)
        return [lax.psum_scatter(stacked, "expert", scatter_dimension=0).astype(jnp.float32)]
    across, along = pair_moves(4, 1), pair_moves(4, 2)
    half = parts[0].shape[0] // 2
    top = lax.ppermute(parts[3][:half].astype(low), "expert", across)
    bottom = lax.ppermute(parts[3][half:].astype(low), "expert", along)
    first_top = lax.ppermute(parts[1][:half].astype(low), "expert", across)
    second_bottom = lax.ppermute(parts[2][half:].astype(low), "expert", along)
    for_first = add_low(parts[1][half:], bottom)
    for_second = add_low(parts[2][:half], top)
    return [parts[0], first_top, second_bottom, for_first, for_second]


def scatter_finish(state):
    if len(state) == 1:
        return state[0]
    own, first_top, second_bottom, for_first, for_second = state
    half = first_top.shape[0]
    second_top = lax.ppermute(for_second, "expert", pair_moves(4, 2))
    first_bottom = lax.ppermute(for_first, "expert", pair_moves(4, 1))
    return jnp.concatenate(
        [
            total_of([own[:half], first_top, second_top]),
            total_of([own[half:], first_bottom, second_bottom]),
        ],
        axis=0,
    )


def scatter_blocks(parts):
    return scatter_finish(scatter_start(parts))


def after(values, events):
    return lax.optimization_barrier((values, events))[0]


def send_parts(parts, events):
    if lax.axis_size("expert") != 4:
        return [scatter_blocks(parts)]
    low = jnp.bfloat16
    first, second = (
        lax.ppermute(parts[r].astype(low), "expert", pair_moves(4, r)) for r in (1, 2)
    )
    far = lax.ppermute(after(parts[3].astype(low), (first, second, events)), "expert", pair_moves(4, 3))
    return [parts[0], first, second, far]


def total_of(parts):
    total = parts[0].astype(jnp.float32)
    for part in parts[1:]:
        total += part.astype(jnp.float32)
    return total


def shift_dense(rows, events):
    if not cube():
        return [lax.all_gather(rows, ("batch", "expert"), axis=0, tiled=True)]
    below, above = step_up(rows), step_down(rows)
    return [rows, below, step_up(after(below, (above, events))), above]


def dense_start(line, columns, events):
    found = [rows[:, columns] for rows in line]
    if not cube():
        return [found[0][None]]
    return gather_start(after(jnp.stack(found), events))


def dense_finish(state, events=(), late=()):
    if not cube():
        return state, jnp.zeros((1, 1), jnp.int32), ()
    place = lax.axis_index("batch")
    level, core = place // 2, place % 2
    member = lax.axis_index("expert")
    mine = gather_finish(state, events)
    far = mine[3:]
    mine = mine[:3] + [after(jnp.concatenate(far, axis=0), late)]
    other = [exchange_cores(block) for block in mine]
    spots = [
        [(((level + 4 - k) % 4) * 2 + (core ^ c)) * 4 + (member ^ r) for k in range(4)]
        for c in range(2)
        for r in range(4)
    ]
    return mine + other, jnp.array(spots, jnp.int32), far


def sum_chunk(packed_grad):
    return lax.psum_scatter(packed_grad, "batch", scatter_dimension=0, tiled=True)


def exchange_cores(values):
    return lax.ppermute(values, "batch", pair_moves(8, 1))


def step_up(values):
    return lax.ppermute(values, "batch", shift_moves(1))


def step_down(values):
    return lax.ppermute(values, "batch", shift_moves(3))


def add_low(*parts):
    total = parts[0].astype(jnp.float32)
    for part in parts[1:]:
        total += part.astype(jnp.float32)
    return total.astype(jnp.bfloat16)


def join_cores(own, received):
    return [add_low(own[r], received[r]) for r in range(4)]


def line_start(plane):
    level = lax.axis_index("batch") // 2
    own, up, far, down = (
        lax.dynamic_index_in_dim(plane, (level + r) % 4, axis=0, keepdims=False) for r in range(4)
    )
    return own, step_down(add_low(down)), add_low(up, step_up(add_low(far)))


def line_finish(state, events=()):
    own, down, up = state
    return total_of([own, down, step_up(after(up, events))])


def scatter_whole(found):
    values = found[0].reshape(found[0].shape[3:])
    total = lax.psum_scatter(values, ("batch", "expert"), scatter_dimension=0, tiled=True)
    return total.astype(jnp.float32)


def pack_kernel(chunks, query, key, value, small, out, gate, up, down, dense, *packed):
    start = 0
    for part in (query, key, value, small, out):
        dense[:, start : start + part.shape[1]] = part[...]
        start += part.shape[1]
    part, hidden_width = down.shape[1], gate.shape[2]
    for n, target in enumerate(packed):
        for e in range(chunks[n], chunks[n + 1]):
            for side, source in ((0, gate), (1, up)):
                for j in range(3):
                    target[side, e - chunks[n], :, j * hidden_width : (j + 1) * hidden_width] = (
                        source[e, j * part : (j + 1) * part, :]
                    )
            target[2, e - chunks[n]] = down[e]


def pack(chunks, query, key, value, small, out, gate, up, down):
    low = jnp.bfloat16
    columns = sum(part.shape[1] for part in (query, key, value, small, out))
    return pl.pallas_call(
        partial(pack_kernel, chunks),
        in_specs=[INSIDE] * 8,
        out_specs=[INSIDE] * len(chunks),
        out_shape=[jax.ShapeDtypeStruct((query.shape[0], columns), low)]
        + [
            jax.ShapeDtypeStruct((3, b - a) + down.shape[1:], low)
            for a, b in zip(chunks[:-1], chunks[1:])
        ],
        compiler_params=pltpu.CompilerParams(vmem_limit_bytes=VMEM_BYTES),
        cost_estimate=cost(0),
        name="pack",
    )(query, key, value, small, out, gate, up, down)


def local(
    tokens,
    cotangent,
    attn_gain,
    query_weight,
    key_weight,
    value_weight,
    out_weight,
    ffn_gain,
    router_weight,
    gate_weight,
    up_weight,
    down_weight,
    routes,
    ranking,
):
    low = jnp.bfloat16
    wide = jnp.float32
    query_width = HEADS * HEAD_DIM
    kv_width = KV_HEADS * HEAD_DIM
    qkv_width = query_width + 2 * kv_width
    width = tokens.shape[2]
    experts_total = router_weight.shape[1]
    extra = -(-(experts_total + 2) // 128) * 128
    first_gain, second_gain = experts_total, experts_total + 1
    local_experts = gate_weight.shape[0]
    member_count = lax.axis_size("expert")
    member_id = lax.axis_index("expert")
    local_rows = tokens.shape[1]
    group_rows = local_rows * member_count
    cut = cube()
    line_place = lax.axis_index("batch")
    place = jnp.stack([line_place % 2, member_id, line_place // 2]).astype(jnp.int32)

    route_rows = routes[0]
    rank_rows = ranking[0]
    expert_lanes = jnp.arange(extra, dtype=jnp.int32)
    member = jnp.any(route_rows[:, :, None] == expert_lanes[None, None, :], axis=1)
    marks = jnp.where(
        expert_lanes[None, :] == experts_total,
        (rank_rows // 32)[:, None],
        jnp.where(expert_lanes[None, :] == experts_total + 1, (rank_rows % 32)[:, None], member),
    ).astype(low)
    grad_out = cotangent[0]
    small_width = qkv_width + extra
    chunks = (0, 3, local_experts)
    dense_rows, *packed_own = pack(
        chunks,
        query_weight,
        key_weight,
        value_weight,
        jnp.concatenate(
            [
                router_weight,
                attn_gain[:, None],
                ffn_gain[:, None],
                jnp.zeros((query_weight.shape[0], extra - experts_total - 2), low),
            ],
            axis=1,
        ),
        out_weight,
        gate_weight,
        up_weight,
        down_weight,
    )
    row_ids = member_id * local_rows + jnp.arange(local_rows, dtype=jnp.int32)
    half_dim = HEAD_DIM // 2
    frequency = THETA ** (-jnp.arange(half_dim, dtype=wide) / half_dim)
    angles = place_of(row_ids).astype(wide)[:, None] * frequency[None, :]
    cosine = jnp.tile(jnp.cos(angles), (1, 4))
    sine_part = jnp.tile(jnp.concatenate([-jnp.sin(angles), jnp.sin(angles)], axis=1), (1, 2))
    if member_count == 4:
        away = 1 << 20
        starts = [
            jnp.where(member_id >= 1, 0, away),
            jnp.where(member_id >= 2, local_rows, away),
            member_id * local_rows,
        ]
    else:
        starts = [(member_id ^ r) * local_rows for r in range(member_count)]
    key_ids = jnp.concatenate([s + jnp.arange(local_rows, dtype=jnp.int32) for s in starts])
    bias = jnp.where(visible(row_ids, key_ids), 0.0, -1e30).astype(wide)
    bias_turned = bias.T
    tables = (cosine, sine_part, bias, bias_turned)

    line = shift_dense(dense_rows, tables)
    grad_state = gather_start(jnp.concatenate([grad_out, marks], axis=1))
    grad_blocks = gather_finish(grad_state, line[1::2])
    marks_all = jnp.concatenate([block[:, width:] for block in grad_blocks], axis=0)
    qkv_state = dense_start(line, slice(0, small_width), ())
    plane = qkv_state[1:]
    qkv_pieces, qkv_spots, far = dense_finish(qkv_state)
    out_state = dense_start(line, slice(small_width, None), far)
    packed_all = [
        lax.all_gather(after(packed, events), "batch", axis=0)
        for packed, events in zip(packed_own, ((line, grad_blocks), plane))
    ]

    normed, query, keyval, small = enter(
        tokens[0], cosine, sine_part, qkv_pieces, qkv_spots, first_gain, query_width, kv_width
    )

    rank_all = (
        marks_all[:, experts_total].astype(wide) * 32 + marks_all[:, experts_total + 1].astype(wide)
    )
    earlier = (rank_all[None, :] < rank_rows.astype(wide)[:, None]).astype(low)
    before = product(earlier, marks_all)
    capacity = 5 * group_rows * route_rows.shape[1] // (4 * experts_total)
    member = member.astype(wide)
    kept = jnp.where(before < capacity, member, 0.0)

    keyval_blocks = gather_blocks(after(keyval, out_state[1:]))
    if member_count == 4:
        ordered = keyval_blocks[:3] + [jnp.concatenate(keyval_blocks[3:], axis=0)]
        keys = jnp.concatenate(
            [
                lax.select_n(member_id, *ordered),
                lax.select_n(member_id ^ 1, *ordered),
                keyval,
            ],
            axis=0,
        )
    else:
        keys = jnp.concatenate(keyval_blocks, axis=0)
    attended, log_totals = attend(query, keys, bias)
    out_pieces, out_spots, _ = dense_finish(out_state, keyval_blocks[3:], attended)
    residual, sent, gate_rows = project(
        attended, tokens[0], small, member, kept, second_gain, out_pieces, out_spots
    )
    sent_blocks = gather_blocks(sent)

    carry, chunk_grads = None, []
    for packed, a, b in zip(packed_all, chunks[:-1], chunks[1:]):
        first = (member_id * local_experts + a).astype(jnp.int32).reshape(1)
        packed_grads, mixture_all, row_grad = expert_pass(
            place,
            first,
            sent_blocks,
            grad_blocks,
            packed,
            carry,
            cut and b == local_experts,
            b == local_experts,
        )
        carry = (mixture_all, row_grad)
        chunk_grads.append(packed_grads)

    def blocks_of(values):
        return [values[r * local_rows : (r + 1) * local_rows] for r in range(member_count)]

    totals = [sum_chunk(chunk_grads[0][0])]
    if cut:
        own, rest, far, near = chunk_grads[1]
        far, near = exchange_cores(far), exchange_cores(near)
        far_sum, down_sum = add_low(rest[1], far[0]), add_low(rest[2], far[1])
    turn_state = scatter_start(blocks_of(row_grad))
    if cut:
        turn_state = after(turn_state, (far_sum, down_sum))
    normed_grad = scatter_finish(turn_state)
    turned = turn(
        place,
        out_spots,
        (
            normed_grad,
            residual,
            grad_out,
            small,
            gate_rows,
            member,
            kept,
            sent,
            attended,
        ),
        out_pieces,
        cut,
        second_gain,
    )
    out_found = turned[:-2]
    resid_grad, head_grad = turned[-2:]
    mixture_parts = send_parts(blocks_of(after(mixture_all, normed_grad)), resid_grad)
    if cut:
        head_grad = after(head_grad, mixture_parts[1:3])
        up_part = step_up(far_sum)
    query_grad, key_grads = attend_back(
        head_grad, query, keys, bias_turned, log_totals, cosine, sine_part
    )
    if member_count == 4:
        zero = jnp.zeros((), low)
        for_first, for_second, for_own = blocks_of(key_grads)[:3]
        key_parts = []
        for r in range(4):
            part = jnp.where(member_id == r, for_first, zero)
            part += jnp.where(member_id ^ 1 == r, for_second, zero)
            key_parts.append(part + for_own if r == 0 else part)
    else:
        key_parts = blocks_of(key_grads)
    if cut:
        out_found = out_found[1], exchange_cores(out_found[0])
        key_parts = after(key_parts, mixture_parts[3])
    keyval_sum = scatter_blocks(key_parts)
    if cut:
        out_state = scatter_start(join_cores(*out_found))
    if cut:
        keyval_sum = after(keyval_sum, out_found)
    left = leave(
        place,
        qkv_spots,
        (
            keyval_sum,
            query_grad,
            normed,
            tokens[0],
            resid_grad,
            small,
            cosine,
            sine_part,
        ),
        qkv_pieces,
        cut,
        first_gain,
    )
    qkv_found, input_grad = left[:-1], left[-1]
    result = (residual + total_of(mixture_parts)).astype(low)
    if cut:
        received = exchange_cores(after(qkv_found[0], (totals[0], out_state[1:], up_part)))
        out_plane = scatter_finish(out_state)
        down_term = step_down(after(down_sum, up_part))
        qkv_parts = join_cores(qkv_found[1], after(received, out_plane))
        qkv_parts[1:3] = after(qkv_parts[1:3], down_term)
        qkv_state = scatter_start(qkv_parts)
        up_sum = add_low(rest[0], near[0], up_part)
        up_term = step_up(after(up_sum, qkv_state[1:3]))
        out_line = line_start(out_plane)
        qkv_plane = scatter_finish(qkv_state)
        out_sum = line_finish(out_line)
        qkv_state = line_start(qkv_plane)
        near, down_term, up_term = after((near, down_term, up_term), qkv_plane)
        terms = [[(totals[0], 0)], [(own, None), (near, 1), (down_term, None), (up_term, None)]]
        expert_totals = unpack(terms, gate_weight.shape, down_weight.shape)
        qkv_sum = line_finish(qkv_state, up_term)
    else:
        out_sum = scatter_whole(out_found)
        qkv_sum = scatter_whole(qkv_found)
        totals += [sum_chunk(found[0]) for found in chunk_grads[1:]]
        terms = [[(total, 0)] for total in totals]
        expert_totals = unpack(terms, gate_weight.shape, down_weight.shape)
    gate_total, up_total, down_total = expert_totals
    return (
        result[None],
        input_grad[None],
        qkv_sum[:, qkv_width + first_gain],
        qkv_sum[:, :query_width],
        qkv_sum[:, query_width : query_width + kv_width],
        qkv_sum[:, query_width + kv_width : qkv_width],
        out_sum[:, :width],
        out_sum[:, width + second_gain],
        out_sum[:, width : width + experts_total],
        gate_total,
        up_total,
        down_total,
    )


def solution(mesh):
    return jax.shard_map(
        local,
        mesh=mesh,
        in_specs=(
            P("batch", "expert", None),
            P("batch", "expert", None),
            P(("batch", "expert")),
            P(("batch", "expert"), None),
            P(("batch", "expert"), None),
            P(("batch", "expert"), None),
            P(("batch", "expert"), None),
            P(("batch", "expert")),
            P(("batch", "expert"), None),
            P("expert", "batch", None),
            P("expert", "batch", None),
            P("expert", "batch", None),
            P("batch", "expert", None),
            P("batch", "expert"),
        ),
        out_specs=(
            P("batch", "expert", None),
            P("batch", "expert", None),
            P(("batch", "expert")),
            P(("batch", "expert"), None),
            P(("batch", "expert"), None),
            P(("batch", "expert"), None),
            P(("batch", "expert"), None),
            P(("batch", "expert")),
            P(("batch", "expert"), None),
            P("expert", "batch", None),
            P("expert", "batch", None),
            P("expert", "batch", None),
        ),
        check_vma=False,
    )
```

```python
from functools import partial

import jax
import jax.numpy as jnp
from jax import lax
from jax.experimental import pallas as pl
from jax.experimental.pallas import tpu as pltpu
from jax.sharding import PartitionSpec as P

HEADS = 24
KV_HEADS = 8
HEAD_DIM = 64
PROMPT = 512
CLEN = 256


EPS = 1e-06
THETA = 10000.0


def product(left, right):
    return jnp.dot(left, right, preferred_element_type=jnp.float32)


def place_of(row_ids):
    return jnp.where(row_ids < PROMPT, row_ids, PROMPT + (row_ids - PROMPT) % CLEN)


def visible(query_ids, key_ids):
    causal = key_ids[None, :] <= query_ids[:, None]
    same_run = (key_ids[None, :] - PROMPT) // CLEN == (query_ids[:, None] - PROMPT) // CLEN
    return causal & ((key_ids[None, :] < PROMPT) | same_run)


def dot_plain(left, right):
    return lax.dot_general(left, right, (((1,), (0,)), ((), ())), preferred_element_type=jnp.float32)


def dot_right(left, right):
    return lax.dot_general(left, right, (((1,), (1,)), ((), ())), preferred_element_type=jnp.float32)


def dot_left(left, right):
    return lax.dot_general(left, right, (((0,), (0,)), ((), ())), preferred_element_type=jnp.float32)


ANYWHERE = pl.BlockSpec(memory_space=pl.ANY)
INSIDE = pl.BlockSpec(memory_space=pltpu.VMEM)
SCALARS = pl.BlockSpec(memory_space=pltpu.SMEM)
VMEM_BYTES = 62 * 1024 * 1024


def cost(flops, *arrays):
    return pl.CostEstimate(flops=1, bytes_accessed=1, transcendentals=0)


def weight_copies(spots, pieces, target, sems):
    copies = []
    for p, piece in enumerate(pieces):
        blocks, rows = piece.shape[0], piece.shape[1]
        for k in range(blocks):
            place = pl.multiple_of(spots[p, k] * rows, rows)
            copies.append(
                pltpu.make_async_copy(
                    piece.at[k], target.at[pl.ds(place, rows)], sems.at[p * blocks + k]
                )
            )
    return copies


def block_copies(blocks, target, sems, first, columns=None):
    copies = []
    start = 0
    for i, block in enumerate(blocks):
        rows = block.shape[0]
        source = block if columns is None else block.at[:, columns]
        copies.append(
            pltpu.make_async_copy(source, target.at[pl.ds(start, rows)], sems.at[first + i])
        )
        start += rows
    return copies


def swap_halves(values):
    half = HEAD_DIM // 2
    lane = lax.broadcasted_iota(jnp.int32, values.shape, 1)
    return jnp.where(
        lane % HEAD_DIM < half,
        pltpu.roll(values, 2 * HEAD_DIM - half, 1),
        pltpu.roll(values, half, 1),
    )


def mean_square_scale(values):
    return lax.rsqrt(jnp.mean(values * values, axis=-1, keepdims=True) + EPS)


def enter_kernel(count, gain_at, spots, tokens, cosine, sine, *refs):
    pieces = refs[:count]
    normed, query, keyval, small, weight, sems = refs[count:]
    low = jnp.bfloat16
    copies = weight_copies(spots, pieces, weight, sems)
    for copy in copies:
        copy.start()
    inputs = tokens[...].astype(jnp.float32)
    scaled = inputs * mean_square_scale(inputs)
    for copy in copies:
        copy.wait()
    query_width = query.shape[1]
    kv_width = keyval.shape[1] // 2
    qkv_width = query_width + 2 * kv_width
    turned = weight[:, qkv_width:].astype(jnp.float32).T
    small[...] = turned
    rows = (scaled * turned[gain_at : gain_at + 1]).astype(low)
    normed[...] = rows
    pair = 2 * HEAD_DIM
    scale = HEAD_DIM**-0.5
    for start in range(0, query_width + kv_width, 512):
        product_part = dot_plain(rows, weight[:, start : start + 512])
        for offset in range(0, 512, pair):
            part = product_part[:, offset : offset + pair]
            part = part * cosine[...] + swap_halves(part) * sine[...]
            at = start + offset
            if at < query_width:
                query[:, at : at + pair] = (part * scale).astype(low)
            else:
                keyval[:, at - query_width : at - query_width + pair] = part.astype(low)
    keyval[:, kv_width:] = dot_plain(
        rows, weight[:, query_width + kv_width : qkv_width]
    ).astype(low)


def enter(tokens, cosine, sine, pieces, spots, gain_at, query_width, kv_width):
    rows, width = tokens.shape
    columns = pieces[0].shape[2]
    low = jnp.bfloat16
    return pl.pallas_call(
        partial(enter_kernel, len(pieces), gain_at),
        in_specs=[SCALARS, INSIDE, INSIDE, INSIDE] + [ANYWHERE] * len(pieces),
        out_specs=[INSIDE] * 4,
        out_shape=[
            jax.ShapeDtypeStruct((rows, width), low),
            jax.ShapeDtypeStruct((rows, query_width), low),
            jax.ShapeDtypeStruct((rows, 2 * kv_width), low),
            jax.ShapeDtypeStruct((columns - query_width - 2 * kv_width, width), jnp.float32),
        ],
        scratch_shapes=[
            pltpu.VMEM((width, columns), low),
            pltpu.SemaphoreType.DMA((len(pieces) * pieces[0].shape[0],)),
        ],
        compiler_params=pltpu.CompilerParams(vmem_limit_bytes=VMEM_BYTES),
        cost_estimate=cost(2 * rows * width * columns, *pieces),
        name="enter",
    )(spots, tokens, cosine, sine, *pieces)


def both_places(values):
    wide = values.astype(jnp.float32)
    low_lane = lax.broadcasted_iota(jnp.int32, values.shape, 1) < HEAD_DIM
    moved = pltpu.roll(wide, HEAD_DIM, 1)
    kind = values.dtype
    return [
        [jnp.where(low_lane, wide, 0.0).astype(kind), jnp.where(low_lane, 0.0, moved).astype(kind)],
        [jnp.where(low_lane, moved, 0.0).astype(kind), jnp.where(low_lane, 0.0, wide).astype(kind)],
    ]


def attend_kernel(query, keyval, bias, attended, log_totals):
    low = jnp.bfloat16
    rows = query.shape[0]
    kv_width = keyval.shape[1] // 2
    pair_lanes = 2 * HEAD_DIM
    repeat = HEADS // KV_HEADS
    log_totals[...] = jnp.zeros_like(log_totals)
    lane = lax.broadcasted_iota(jnp.int32, log_totals.shape, 1)

    @pl.loop(0, KV_HEADS // 2)
    def _(pair):
        at = pl.ds(pl.multiple_of(pair * pair_lanes, pair_lanes), pair_lanes)
        keys = both_places(keyval[:, at])
        at = pl.ds(pl.multiple_of(kv_width + pair * pair_lanes, pair_lanes), pair_lanes)
        values = both_places(keyval[:, at])
        for i in range(repeat):
            at = pl.ds(pl.multiple_of((pair * repeat + i) * pair_lanes, pair_lanes), pair_lanes)
            queries = query[:, at]
            total = jnp.zeros((rows, pair_lanes), jnp.float32)
            for a in range(2):
                head = 2 * i + a
                scores = dot_right(queries, keys[head // repeat][a]) + bias[...]
                peak = jnp.max(scores, axis=-1, keepdims=True)
                lifted = jnp.exp(scores - peak)
                row_total = jnp.sum(lifted, axis=-1, keepdims=True)
                weights_low = (lifted * (1.0 / row_total)).astype(low)
                total += dot_plain(weights_low, values[head // repeat][a])
                log_totals[...] = jnp.where(
                    lane == pair * (2 * repeat) + head, peak + jnp.log(row_total), log_totals[...]
                )
            attended[:, at] = total.astype(low)


def attend(query, keyval, bias):
    rows, query_width = query.shape
    return pl.pallas_call(
        attend_kernel,
        in_specs=[INSIDE] * 3,
        out_specs=[INSIDE] * 2,
        out_shape=[
            jax.ShapeDtypeStruct((rows, query_width), jnp.bfloat16),
            jax.ShapeDtypeStruct((rows, 128), jnp.float32),
        ],
        compiler_params=pltpu.CompilerParams(vmem_limit_bytes=VMEM_BYTES),
        cost_estimate=cost(8 * rows * query_width * bias.shape[1], query, keyval, bias),
        name="attend",
    )(query, keyval, bias)


def project_kernel(count, gain_at, spots, attended, tokens, small, member, kept, *refs):
    pieces = refs[:count]
    residual, sent, gate_rows, weight, sems = refs[count:]
    low = jnp.bfloat16
    width = tokens.shape[1]
    copies = weight_copies(spots, pieces, weight, sems)
    for copy in copies:
        copy.start()
    for copy in copies:
        copy.wait()
    hidden = tokens[...].astype(jnp.float32) + dot_plain(attended[...], weight[...])
    residual[...] = hidden
    gain = small[gain_at : gain_at + 1, :]
    normed = (hidden * mean_square_scale(hidden) * gain).astype(low)
    logits = dot_right(normed, small[...].astype(low))
    chosen = member[...] > 0.0
    logits = jnp.where(chosen, logits, -1e30)
    lifted = jnp.where(chosen, jnp.exp(logits - jnp.max(logits, axis=-1, keepdims=True)), 0.0)
    gates = lifted / jnp.sum(lifted, axis=-1, keepdims=True)
    gate_rows[...] = gates
    sent[:, :width] = normed
    sent[:, width:] = (gates * kept[...]).astype(low)


def project(attended, tokens, small, member, kept, gain_at, pieces, spots):
    rows, width = tokens.shape
    lanes = small.shape[0]
    low = jnp.bfloat16
    return pl.pallas_call(
        partial(project_kernel, len(pieces), gain_at),
        in_specs=[SCALARS] + [INSIDE] * 5 + [ANYWHERE] * len(pieces),
        out_specs=[INSIDE] * 3,
        out_shape=[
            jax.ShapeDtypeStruct((rows, width), jnp.float32),
            jax.ShapeDtypeStruct((rows, width + lanes), low),
            jax.ShapeDtypeStruct((rows, lanes), jnp.float32),
        ],
        scratch_shapes=[
            pltpu.VMEM((attended.shape[1], width), low),
            pltpu.SemaphoreType.DMA((len(pieces) * pieces[0].shape[0],)),
        ],
        compiler_params=pltpu.CompilerParams(vmem_limit_bytes=VMEM_BYTES),
        cost_estimate=cost(2 * rows * width * width, *pieces),
        name="project",
    )(spots, attended, tokens, small, member, kept, *pieces)


def grad_shapes(cut, rows, columns):
    low = jnp.bfloat16
    if cut:
        block = rows // 32
        return (
            [jax.ShapeDtypeStruct((4, 4, block, columns), low)] * 2,
            pltpu.VMEM((4, 2, 4, block, columns), low),
        )
    return (
        [jax.ShapeDtypeStruct((1, 1, 1, rows, columns), low)],
        pltpu.VMEM((1, 1, 1, rows, columns), low),
    )


def grad_copies(cut, place, source, outs, sems):
    if not cut:
        return [pltpu.make_async_copy(source, outs[0], sems.at[0])]
    core, member = place[0], place[1]
    other, own = outs
    copies = []
    for r in range(4):
        copies.append(
            pltpu.make_async_copy(
                source.at[:, 1 - core, member ^ r], other.at[r], sems.at[2 * r]
            )
        )
        copies.append(
            pltpu.make_async_copy(source.at[:, core, member ^ r], own.at[r], sems.at[2 * r + 1])
        )
    return copies


def turn_kernel(
    count,
    cut,
    gain_at,
    place,
    spots,
    normed_grad,
    residual,
    grad_out,
    small,
    gate_rows,
    member,
    kept,
    normed,
    attended,
    *refs,
):
    pieces = refs[:count]
    refs = refs[count:]
    outs = refs[: (2 if cut else 1)]
    resid_grad, head_grad, weight, weight_grad, sems, out_sems = refs[len(outs) :]
    low = jnp.bfloat16
    rows, width = residual.shape
    lanes = gate_rows.shape[1]
    copies = weight_copies(spots, pieces, weight, sems)
    for copy in copies:
        copy.start()
    lane = lax.broadcasted_iota(jnp.int32, (rows, lanes), 1)
    gates = gate_rows[...]
    gate_grads = normed_grad[:, width:] * kept[...]
    chosen_grad = gates * (gate_grads - jnp.sum(gates * gate_grads, axis=-1, keepdims=True))
    logit_grad = (chosen_grad * member[...]).astype(low)
    hidden = residual[...]
    scale = mean_square_scale(hidden)
    row_grad = normed_grad[:, :width] + dot_plain(logit_grad, small[...].astype(low))
    gain = small[gain_at : gain_at + 1, :]
    scaled = row_grad * gain
    total_grad = (
        grad_out[...].astype(jnp.float32)
        + scale * scaled
        - hidden * (scale * scale * scale) * jnp.mean(scaled * hidden, axis=-1, keepdims=True)
    )
    resid_grad[...] = total_grad
    attn_grad = total_grad.astype(low)
    shape = weight_grad.shape[:-1]
    gain_grad = (row_grad * hidden * scale).astype(low)
    picks = jnp.where(lane == gain_at, 1.0, 0.0).astype(low)
    weight_grad[..., width:] = (
        (dot_left(normed[...][:, :width], logit_grad) + dot_left(gain_grad, picks))
        .astype(low)
        .reshape(shape + (lanes,))
    )
    for start in range(0, width, 512):
        weight_grad[..., start : start + 512] = (
            dot_left(attended[...], attn_grad[:, start : start + 512])
            .astype(low)
            .reshape(shape + (512,))
        )
    out_copies = grad_copies(cut, place, weight_grad, outs, out_sems)
    for copy in out_copies:
        copy.start()
    for copy in copies:
        copy.wait()
    head_grad[...] = dot_right(attn_grad, weight[...]).astype(low)
    for copy in out_copies:
        copy.wait()


def turn(place, spots, operands, pieces, cut, gain_at):
    residual, gate_rows, attended = operands[1], operands[4], operands[8]
    rows, width = residual.shape
    query_width = attended.shape[1]
    low = jnp.bfloat16
    grads, held = grad_shapes(cut, query_width, width + gate_rows.shape[1])
    return pl.pallas_call(
        partial(turn_kernel, len(pieces), cut, gain_at),
        in_specs=[SCALARS, SCALARS] + [INSIDE] * len(operands) + [ANYWHERE] * len(pieces),
        out_specs=[ANYWHERE] * len(grads) + [INSIDE] * 2,
        out_shape=grads
        + [
            jax.ShapeDtypeStruct((rows, width), jnp.float32),
            jax.ShapeDtypeStruct((rows, query_width), low),
        ],
        scratch_shapes=[
            pltpu.VMEM((query_width, width), low),
            held,
            pltpu.SemaphoreType.DMA((len(pieces) * pieces[0].shape[0],)),
            pltpu.SemaphoreType.DMA((8,)),
        ],
        compiler_params=pltpu.CompilerParams(vmem_limit_bytes=VMEM_BYTES),
        cost_estimate=cost(0),
        name="turn",
    )(place, spots, *operands, *pieces)


def attend_back_kernel(
    head_grad, query, keyval, bias, log_totals, cosine, sine, query_grad, keyval_grad, totals
):
    low = jnp.bfloat16
    rows = query.shape[0]
    kv_width = keyval.shape[1] // 2
    pair_lanes = 2 * HEAD_DIM
    repeat = HEADS // KV_HEADS
    totals[...] = log_totals[...].T

    @pl.loop(0, KV_HEADS // 2)
    def _(pair):
        key_at = pl.ds(pl.multiple_of(pair * pair_lanes, pair_lanes), pair_lanes)
        value_at = pl.ds(pl.multiple_of(kv_width + pair * pair_lanes, pair_lanes), pair_lanes)
        keys = both_places(keyval[:, key_at])
        values = both_places(keyval[:, value_at])
        key_grads = [[None, None], [None, None]]
        value_grads = [[None, None], [None, None]]
        for i in range(repeat):
            at = pl.ds(pl.multiple_of((pair * repeat + i) * pair_lanes, pair_lanes), pair_lanes)
            queries = query[:, at]
            grads = head_grad[:, at]
            query_part = jnp.zeros((rows, pair_lanes), jnp.float32)
            for a in range(2):
                head = 2 * i + a
                g = head // repeat
                total = totals[pl.ds(pair * (2 * repeat) + head, 1), :]
                weights = jnp.exp(dot_right(keys[g][a], queries) + bias[...] - total)
                weight_grads = dot_right(values[g][a], grads)
                delta = jnp.sum(weights * weight_grads, axis=0, keepdims=True)
                score_grads = (weights * (weight_grads - delta)).astype(low)
                value_part = dot_plain(weights.astype(low), grads)
                key_part = dot_plain(score_grads, queries)
                query_part += dot_left(score_grads, keys[g][a])
                if key_grads[g][a] is None:
                    key_grads[g][a], value_grads[g][a] = key_part, value_part
                else:
                    key_grads[g][a] += key_part
                    value_grads[g][a] += value_part
            query_part = query_part * (HEAD_DIM**-0.5)
            query_part = query_part * cosine[...] - swap_halves(query_part) * sine[...]
            query_grad[:, at] = query_part.astype(low)
        low_lane = lax.broadcasted_iota(jnp.int32, (keyval.shape[0], pair_lanes), 1) < HEAD_DIM
        for at, found in ((key_at, key_grads), (value_at, value_grads)):
            keyval_grad[:, at] = jnp.where(
                low_lane,
                found[0][0] + pltpu.roll(found[0][1], HEAD_DIM, 1),
                pltpu.roll(found[1][0], HEAD_DIM, 1) + found[1][1],
            ).astype(low)


def attend_back(head_grad, query, keyval, bias, log_totals, cosine, sine):
    rows, query_width = query.shape
    low = jnp.bfloat16
    return pl.pallas_call(
        attend_back_kernel,
        in_specs=[INSIDE] * 7,
        out_specs=[INSIDE] * 2,
        out_shape=[
            jax.ShapeDtypeStruct((rows, query_width), low),
            jax.ShapeDtypeStruct(keyval.shape, low),
        ],
        scratch_shapes=[pltpu.VMEM((128, rows), jnp.float32)],
        compiler_params=pltpu.CompilerParams(vmem_limit_bytes=VMEM_BYTES),
        cost_estimate=cost(0),
        name="attend_back",
    )(head_grad, query, keyval, bias, log_totals, cosine, sine)


def leave_kernel(
    count,
    cut,
    gain_at,
    place,
    spots,
    keyval_sum,
    query_grad,
    normed,
    tokens,
    resid_grad,
    small,
    cosine,
    sine,
    *refs,
):
    pieces = refs[:count]
    refs = refs[count:]
    outs = refs[: (2 if cut else 1)]
    input_grad, weight, weight_grad, joined, sems, out_sems = refs[len(outs) :]
    low = jnp.bfloat16
    rows, width = tokens.shape
    query_width = query_grad.shape[1]
    kv_width = keyval_sum.shape[1] // 2
    qkv_width = query_width + 2 * kv_width
    pair = 2 * HEAD_DIM
    copies = weight_copies(spots, pieces, weight, sems)
    for copy in copies:
        copy.start()
    joined[:, :query_width] = query_grad[...]
    for start in range(0, kv_width, pair):
        part = keyval_sum[:, start : start + pair]
        part = part * cosine[...] - swap_halves(part) * sine[...]
        joined[:, query_width + start : query_width + start + pair] = part.astype(low)
    joined[:, query_width + kv_width :] = keyval_sum[:, kv_width:].astype(low)
    shape = weight_grad.shape[:-1]
    for start in range(0, qkv_width, 512):
        weight_grad[..., start : start + 512] = (
            dot_left(normed[...], joined[:, start : start + 512]).astype(low).reshape(shape + (512,))
        )
    for copy in copies:
        copy.wait()
    row_grad = dot_right(joined[...], weight[:, :qkv_width])
    inputs = tokens[...].astype(jnp.float32)
    scale = mean_square_scale(inputs)
    lanes = weight_grad.shape[-1] - qkv_width
    lane = lax.broadcasted_iota(jnp.int32, (rows, lanes), 1)
    picks = jnp.where(lane == gain_at, 1.0, 0.0).astype(low)
    weight_grad[..., qkv_width:] = (
        dot_left((row_grad * inputs * scale).astype(low), picks).astype(low).reshape(shape + (lanes,))
    )
    out_copies = grad_copies(cut, place, weight_grad, outs, out_sems)
    for copy in out_copies:
        copy.start()
    scaled = row_grad * small[gain_at : gain_at + 1, :]
    input_grad[...] = (
        resid_grad[...]
        + scale * scaled
        - inputs * (scale * scale * scale) * jnp.mean(scaled * inputs, axis=-1, keepdims=True)
    )
    for copy in out_copies:
        copy.wait()


def leave(place, spots, operands, pieces, cut, gain_at):
    tokens, query_grad, keyval_sum = operands[3], operands[1], operands[0]
    rows, width = tokens.shape
    columns = pieces[0].shape[2]
    low = jnp.bfloat16
    grads, held = grad_shapes(cut, width, columns)
    return pl.pallas_call(
        partial(leave_kernel, len(pieces), cut, gain_at),
        in_specs=[SCALARS, SCALARS] + [INSIDE] * len(operands) + [ANYWHERE] * len(pieces),
        out_specs=[ANYWHERE] * len(grads) + [INSIDE],
        out_shape=grads + [jax.ShapeDtypeStruct((rows, width), jnp.float32)],
        scratch_shapes=[
            pltpu.VMEM((width, columns), low),
            held,
            pltpu.VMEM((rows, query_grad.shape[1] + keyval_sum.shape[1]), low),
            pltpu.SemaphoreType.DMA((len(pieces) * pieces[0].shape[0],)),
            pltpu.SemaphoreType.DMA((8,)),
        ],
        compiler_params=pltpu.CompilerParams(vmem_limit_bytes=VMEM_BYTES),
        cost_estimate=cost(0),
        name="leave",
    )(place, spots, *operands, *pieces)


def expert_kernel(cut, carried, last, row_blocks, grad_blocks, row_tile, place, first, packed, *refs):
    blocks_in = refs[:row_blocks]
    grads_in = refs[row_blocks : row_blocks + grad_blocks]
    refs = refs[row_blocks + grad_blocks :]
    if carried:
        mix_in, turn_in = refs[:2]
        refs = refs[2:]
    count = packed.shape[2]
    outs = 4 if cut else 1
    packed_grads = refs[:outs]
    mix_out, turn_out = refs[outs : outs + 2]
    refs = refs[outs + 2 :]
    if last:
        mix, turned = refs[:2]
        refs = refs[2:]
    else:
        mix, turned = mix_out, turn_out
    (
        rows,
        grads,
        gates,
        gate_w,
        up_w,
        down_w,
        gate_g,
        up_g,
        down_g,
        weighted,
        gate_side,
        up_side,
        load_sems,
        save_sems,
        carry_sems,
    ) = refs
    hidden_width = gate_w.shape[-1]
    total_rows, width = rows.shape
    lanes = gates.shape[1]
    low = jnp.bfloat16

    def sides(gate, up, down):
        for side, inner in ((0, gate), (1, up)):
            for j in range(3):
                yield side, pl.ds(j * hidden_width, hidden_width), inner, j
        yield 2, pl.ds(0, width), down, None

    def loads(e):
        slot = e % 2
        copies = []
        for i, (side, columns, inner, j) in enumerate(sides(gate_w, up_w, down_w)):
            outer = packed.at[:, side, e, :, columns]
            inner = inner.at[slot] if j is None else inner.at[slot, :, j]
            copies.append(pltpu.make_async_copy(outer, inner, load_sems.at[slot, i]))
        return copies

    def saves(e):
        slot = e % 2
        copies = []
        for i, (side, columns, inner, j) in enumerate(sides(gate_g, up_g, down_g)):
            if not cut:
                outer = packed_grads[0].at[:, side, e, :, columns]
                source = inner.at[slot] if j is None else inner.at[slot, :, j]
                copies.append(pltpu.make_async_copy(source, outer, save_sems.at[slot, i]))
                continue
            own, rest, far, near = packed_grads
            targets = [own, rest.at[0], rest.at[1], rest.at[2]]
            targets += [near.at[1], near.at[0], far.at[0], far.at[1]]
            for n, target in enumerate(targets):
                block = 2 * lax.rem(place[2] + n % 4, 4) + (place[0] ^ (n // 4))
                source = inner.at[slot, block] if j is None else inner.at[slot, block, j]
                outer = target.at[side, e, :, columns]
                copies.append(pltpu.make_async_copy(source, outer, save_sems.at[slot, 8 * i + n]))
        return copies

    carries = (
        block_copies(grads_in, grads, carry_sems, 0, pl.ds(0, width))
        + block_copies(blocks_in, rows, carry_sems, grad_blocks, pl.ds(0, width))
        + block_copies(
            blocks_in, gates, carry_sems, grad_blocks + row_blocks, pl.ds(width, lanes)
        )
    )
    sums = []
    if carried:
        at = grad_blocks + 2 * row_blocks
        sums = [
            pltpu.make_async_copy(mix_in, mix, carry_sems.at[at]),
            pltpu.make_async_copy(turn_in, turned, carry_sems.at[at + 1]),
        ]
    for copy in loads(0) + carries + sums:
        copy.start()
    for e in range(count):
        slot = e % 2
        if e + 1 < count:
            for copy in loads(e + 1):
                copy.start()
        for copy in loads(e):
            copy.wait()
        if e == 0:
            for copy in carries:
                copy.wait()
            if not carried:
                turned[:, width:] = jnp.zeros((total_rows, lanes), jnp.float32)

        @pl.loop(0, total_rows // row_tile)
        def _(tile):
            span = pl.ds(pl.multiple_of(tile * row_tile, row_tile), row_tile)
            gate_full = gate_w[slot].reshape(width, hidden_width)
            up_full = up_w[slot].reshape(width, hidden_width)
            down_full = down_w[slot].reshape(hidden_width, width)
            here = rows[span, :]
            slope = dot_right(grads[span, :], down_full)
            gate_pre = dot_plain(here, gate_full)
            up_pre = dot_plain(here, up_full)
            lane = lax.broadcasted_iota(jnp.int32, (row_tile, lanes), 1)
            chosen = lane == first[0] + e
            gate_column = jnp.sum(
                jnp.where(chosen, gates[span, :].astype(jnp.float32), 0.0), axis=1, keepdims=True
            )
            sigmoid_gate = jax.nn.sigmoid(gate_pre)
            activated = gate_pre * sigmoid_gate
            hidden = (activated * up_pre).astype(low).astype(jnp.float32)
            share = jnp.sum(hidden * slope, axis=1, keepdims=True)
            if e == 0 and sums:

                @pl.when(tile == 0)
                def _():
                    for copy in sums:
                        copy.wait()

            turned[span, width:] = jnp.where(chosen, share, turned[span, width:])
            part_weighted = (hidden * gate_column).astype(low)
            hidden_grad = slope * gate_column
            part_gate = (
                hidden_grad * up_pre * (sigmoid_gate + activated * (1.0 - sigmoid_gate))
            ).astype(low)
            part_up = (hidden_grad * activated).astype(low)
            weighted[span, :] = part_weighted
            gate_side[span, :] = part_gate
            up_side[span, :] = part_up
            mix_part = dot_plain(part_weighted, down_full)
            turn_part = dot_right(part_gate, gate_full) + dot_right(part_up, up_full)
            if e == 0 and not carried:
                mix[span, :] = mix_part
                turned[span, :width] = turn_part
            elif last and e == count - 1:
                mix_out[span, :] = (mix[span, :] + mix_part).astype(low)
                turn_out[span, :width] = (turned[span, :width] + turn_part).astype(low)
                turn_out[span, width:] = turned[span, width:].astype(low)
            else:
                mix[span, :] += mix_part
                turned[span, :width] += turn_part

        if e >= 2:
            for copy in saves(e - 2):
                copy.wait()
        down_g[slot] = dot_left(weighted[...], grads[...]).astype(low).reshape(down_g.shape[1:])
        gate_g[slot] = dot_left(rows[...], gate_side[...]).astype(low).reshape(gate_g.shape[1:])
        up_g[slot] = dot_left(rows[...], up_side[...]).astype(low).reshape(up_g.shape[1:])
        for copy in saves(e):
            copy.start()
    for e in range(max(0, count - 2), count):
        for copy in saves(e):
            copy.wait()


def expert_pass(place, first, rows, grads, packed, carry, cut, last):
    blocks, _, count, part, width = packed.shape
    hidden_width = blocks * part
    total_rows = sum(block.shape[0] for block in rows)
    lanes = rows[0].shape[1] - width
    low = jnp.bfloat16
    wide = jnp.float32
    carried = carry is not None
    flops = 18 * total_rows * count * hidden_width * width
    side = pltpu.VMEM((2, blocks, 3, part, hidden_width), low)
    sides = [side, side, pltpu.VMEM((2, blocks, part, width), low)]
    sums = [(total_rows, width), (total_rows, width + lanes)]
    one = packed.shape[1:]
    grads_out = [one, (3,) + one, (2,) + one, (2,) + one] if cut else [packed.shape]
    outs = len(grads_out)
    found = pl.pallas_call(
        partial(expert_kernel, cut, carried, last, len(rows), len(grads), min(512, total_rows)),
        in_specs=[SCALARS, SCALARS]
        + [ANYWHERE] * (1 + len(rows) + len(grads) + (2 if carried else 0)),
        out_specs=[ANYWHERE] * outs + [INSIDE, INSIDE],
        out_shape=[jax.ShapeDtypeStruct(shape, low) for shape in grads_out]
        + [jax.ShapeDtypeStruct(shape, low if last else wide) for shape in sums],
        scratch_shapes=([pltpu.VMEM(shape, wide) for shape in sums] if last else [])
        + [
            pltpu.VMEM((total_rows, width), low),
            pltpu.VMEM((total_rows, width), low),
            pltpu.VMEM((total_rows, lanes), low),
        ]
        + sides
        + sides
        + [pltpu.VMEM((total_rows, hidden_width), low)] * 3
        + [
            pltpu.SemaphoreType.DMA((2, 7)),
            pltpu.SemaphoreType.DMA((2, 56)),
            pltpu.SemaphoreType.DMA((2 * len(rows) + len(grads) + 2,)),
        ],
        compiler_params=pltpu.CompilerParams(vmem_limit_bytes=VMEM_BYTES),
        cost_estimate=cost(flops, packed, packed, *rows, *grads),
        name="experts",
    )(place, first, packed, *rows, *grads, *(carry or ()))
    return found[:outs], found[outs], found[outs + 1]


def unpack_kernel(counts, places, *refs):
    found, (gate, up, down) = refs[:-3], refs[-3:]
    found = [array if place is None else array.at[place] for array, place in zip(found, places)]
    hidden_width = gate.shape[2]
    base = 0
    at = 0
    for terms in counts:
        parts = found[at : at + terms]
        at += terms
        count, part = parts[0].shape[1], parts[0].shape[2]
        for e in range(count):
            for side in range(3):
                total = parts[0][side, e].astype(jnp.float32)
                for other in parts[1:]:
                    total += other[side, e].astype(jnp.float32)
                if side == 2:
                    down[base + e] = total
                    continue
                for j in range(3):
                    (gate, up)[side][base + e, j * part : (j + 1) * part, :] = total[
                        :, j * hidden_width : (j + 1) * hidden_width
                    ]
        base += count


def unpack(chunks, gate_shape, down_shape):
    arrays = [array for terms in chunks for array, _ in terms]
    places = [place for terms in chunks for _, place in terms]
    return pl.pallas_call(
        partial(unpack_kernel, [len(terms) for terms in chunks], places),
        in_specs=[INSIDE] * len(arrays),
        out_specs=[INSIDE] * 3,
        out_shape=[
            jax.ShapeDtypeStruct(gate_shape, jnp.float32),
            jax.ShapeDtypeStruct(gate_shape, jnp.float32),
            jax.ShapeDtypeStruct(down_shape, jnp.float32),
        ],
        compiler_params=pltpu.CompilerParams(vmem_limit_bytes=VMEM_BYTES),
        cost_estimate=cost(0),
        name="unpack",
    )(*arrays)


def cube():
    return lax.axis_size("batch") == 8 and lax.axis_size("expert") == 4


def pair_moves(size, flip):
    return [(i, i ^ flip) for i in range(size)]


def shift_moves(step):
    return [(2 * z + c, 2 * ((z + step) % 4) + c) for z in range(4) for c in range(2)]


def gather_start(rows):
    size = lax.axis_size("expert")
    if size != 4:
        stacked = lax.all_gather(rows, "expert", axis=0)
        own = lax.axis_index("expert")
        return [
            lax.dynamic_index_in_dim(stacked, own ^ r, axis=0, keepdims=False) for r in range(size)
        ]
    return [rows] + [lax.ppermute(rows, "expert", pair_moves(4, r)) for r in (1, 2)]


def gather_finish(state, events=()):
    if lax.axis_size("expert") != 4:
        return state
    first, second = after(state[1:], events)
    half = first.shape[0] // 2
    top = lax.ppermute(second[:half], "expert", pair_moves(4, 1))
    bottom = lax.ppermute(first[half:], "expert", pair_moves(4, 2))
    return state + [top, bottom]


def gather_blocks(rows):
    return gather_finish(gather_start(rows))


def scatter_start(parts):
    low = jnp.bfloat16
    if lax.axis_size("expert") != 4:
        own = lax.axis_index("expert")
        order = jnp.arange(len(parts), dtype=jnp.int32) ^ own
        stacked = jnp.take(jnp.stack(parts), order, axis=0).astype(low)
        return [lax.psum_scatter(stacked, "expert", scatter_dimension=0).astype(jnp.float32)]
    across, along = pair_moves(4, 1), pair_moves(4, 2)
    half = parts[0].shape[0] // 2
    top = lax.ppermute(parts[3][:half].astype(low), "expert", across)
    bottom = lax.ppermute(parts[3][half:].astype(low), "expert", along)
    first_top = lax.ppermute(parts[1][:half].astype(low), "expert", across)
    second_bottom = lax.ppermute(parts[2][half:].astype(low), "expert", along)
    for_first = add_low(parts[1][half:], bottom)
    for_second = add_low(parts[2][:half], top)
    return [parts[0], first_top, second_bottom, for_first, for_second]


def scatter_finish(state):
    if len(state) == 1:
        return state[0]
    own, first_top, second_bottom, for_first, for_second = state
    half = first_top.shape[0]
    second_top = lax.ppermute(for_second, "expert", pair_moves(4, 2))
    first_bottom = lax.ppermute(for_first, "expert", pair_moves(4, 1))
    return jnp.concatenate(
        [
            total_of([own[:half], first_top, second_top]),
            total_of([own[half:], first_bottom, second_bottom]),
        ],
        axis=0,
    )


def scatter_blocks(parts):
    return scatter_finish(scatter_start(parts))


def after(values, events):
    return lax.optimization_barrier((values, events))[0]


def send_part(parts, r, events=()):
    part = after(parts[r].astype(jnp.bfloat16), events)
    return lax.ppermute(part, "expert", pair_moves(4, r))


def total_of(parts):
    total = parts[0].astype(jnp.float32)
    for part in parts[1:]:
        total += part.astype(jnp.float32)
    return total


def shift_dense(rows, events):
    if not cube():
        return [lax.all_gather(rows, ("batch", "expert"), axis=0, tiled=True)]
    below, above = step_up(rows), step_down(rows)
    return [rows, below, step_up(after(below, (above, events))), above]


def dense_start(line, columns, events):
    found = [rows[:, columns] for rows in line]
    if not cube():
        return [found[0][None]]
    return gather_start(after(jnp.stack(found), events))


def dense_finish(state, events=(), late=()):
    if not cube():
        return state, jnp.zeros((1, 1), jnp.int32), ()
    place = lax.axis_index("batch")
    level, core = place // 2, place % 2
    member = lax.axis_index("expert")
    mine = gather_finish(state, events)
    far = mine[3:]
    mine = mine[:3] + [after(jnp.concatenate(far, axis=0), late)]
    other = [exchange_cores(block) for block in mine]
    spots = [
        [(((level + 4 - k) % 4) * 2 + (core ^ c)) * 4 + (member ^ r) for k in range(4)]
        for c in range(2)
        for r in range(4)
    ]
    return mine + other, jnp.array(spots, jnp.int32), far


def sum_chunk(packed_grad):
    return lax.psum_scatter(packed_grad, "batch", scatter_dimension=0, tiled=True)


def exchange_cores(values):
    return lax.ppermute(values, "batch", pair_moves(8, 1))


def step_up(values):
    return lax.ppermute(values, "batch", shift_moves(1))


def step_down(values):
    return lax.ppermute(values, "batch", shift_moves(3))


def add_low(*parts):
    total = parts[0].astype(jnp.float32)
    for part in parts[1:]:
        total += part.astype(jnp.float32)
    return total.astype(jnp.bfloat16)


def join_cores(own, received):
    return [add_low(own[r], received[r]) for r in range(4)]


def line_start(plane):
    level = lax.axis_index("batch") // 2
    own, up, far, down = (
        lax.dynamic_index_in_dim(plane, (level + r) % 4, axis=0, keepdims=False) for r in range(4)
    )
    return own, step_down(add_low(down)), add_low(up, step_up(add_low(far)))


def line_finish(state, events=()):
    own, down, up = state
    return total_of([own, down, step_up(after(up, events))])


def scatter_whole(found):
    values = found[0].reshape(found[0].shape[3:])
    total = lax.psum_scatter(values, ("batch", "expert"), scatter_dimension=0, tiled=True)
    return total.astype(jnp.float32)


def pack_kernel(chunks, query, key, value, small, out, gate, up, down, dense, *packed):
    start = 0
    for part in (query, key, value, small, out):
        dense[:, start : start + part.shape[1]] = part[...]
        start += part.shape[1]
    part, hidden_width = down.shape[1], gate.shape[2]
    for n, target in enumerate(packed):
        for e in range(chunks[n], chunks[n + 1]):
            for side, source in ((0, gate), (1, up)):
                for j in range(3):
                    target[side, e - chunks[n], :, j * hidden_width : (j + 1) * hidden_width] = (
                        source[e, j * part : (j + 1) * part, :]
                    )
            target[2, e - chunks[n]] = down[e]


def pack(chunks, query, key, value, small, out, gate, up, down):
    low = jnp.bfloat16
    columns = sum(part.shape[1] for part in (query, key, value, small, out))
    return pl.pallas_call(
        partial(pack_kernel, chunks),
        in_specs=[INSIDE] * 8,
        out_specs=[INSIDE] * len(chunks),
        out_shape=[jax.ShapeDtypeStruct((query.shape[0], columns), low)]
        + [
            jax.ShapeDtypeStruct((3, b - a) + down.shape[1:], low)
            for a, b in zip(chunks[:-1], chunks[1:])
        ],
        compiler_params=pltpu.CompilerParams(vmem_limit_bytes=VMEM_BYTES),
        cost_estimate=cost(0),
        name="pack",
    )(query, key, value, small, out, gate, up, down)


def local(
    tokens,
    cotangent,
    attn_gain,
    query_weight,
    key_weight,
    value_weight,
    out_weight,
    ffn_gain,
    router_weight,
    gate_weight,
    up_weight,
    down_weight,
    routes,
    ranking,
):
    low = jnp.bfloat16
    wide = jnp.float32
    query_width = HEADS * HEAD_DIM
    kv_width = KV_HEADS * HEAD_DIM
    qkv_width = query_width + 2 * kv_width
    width = tokens.shape[2]
    experts_total = router_weight.shape[1]
    extra = -(-(experts_total + 2) // 128) * 128
    first_gain, second_gain = experts_total, experts_total + 1
    local_experts = gate_weight.shape[0]
    member_count = lax.axis_size("expert")
    member_id = lax.axis_index("expert")
    local_rows = tokens.shape[1]
    group_rows = local_rows * member_count
    cut = cube()
    line_place = lax.axis_index("batch")
    place = jnp.stack([line_place % 2, member_id, line_place // 2]).astype(jnp.int32)

    route_rows = routes[0]
    rank_rows = ranking[0]
    expert_lanes = jnp.arange(extra, dtype=jnp.int32)
    member = jnp.any(route_rows[:, :, None] == expert_lanes[None, None, :], axis=1)
    marks = jnp.where(
        expert_lanes[None, :] == experts_total,
        (rank_rows // 32)[:, None],
        jnp.where(expert_lanes[None, :] == experts_total + 1, (rank_rows % 32)[:, None], member),
    ).astype(low)
    grad_out = cotangent[0]
    small_width = qkv_width + extra
    chunks = (0, 3, local_experts)
    dense_rows, *packed_own = pack(
        chunks,
        query_weight,
        key_weight,
        value_weight,
        jnp.concatenate(
            [
                router_weight,
                attn_gain[:, None],
                ffn_gain[:, None],
                jnp.zeros((query_weight.shape[0], extra - experts_total - 2), low),
            ],
            axis=1,
        ),
        out_weight,
        gate_weight,
        up_weight,
        down_weight,
    )
    row_ids = member_id * local_rows + jnp.arange(local_rows, dtype=jnp.int32)
    half_dim = HEAD_DIM // 2
    frequency = THETA ** (-jnp.arange(half_dim, dtype=wide) / half_dim)
    angles = place_of(row_ids).astype(wide)[:, None] * frequency[None, :]
    cosine = jnp.tile(jnp.cos(angles), (1, 4))
    sine_part = jnp.tile(jnp.concatenate([-jnp.sin(angles), jnp.sin(angles)], axis=1), (1, 2))
    if member_count == 4:
        away = 1 << 20
        starts = [
            jnp.where(member_id >= 1, 0, away),
            jnp.where(member_id >= 2, local_rows, away),
            member_id * local_rows,
        ]
    else:
        starts = [(member_id ^ r) * local_rows for r in range(member_count)]
    key_ids = jnp.concatenate([s + jnp.arange(local_rows, dtype=jnp.int32) for s in starts])
    bias = jnp.where(visible(row_ids, key_ids), 0.0, -1e30).astype(wide)
    bias_turned = bias.T
    tables = (cosine, sine_part, bias, bias_turned)

    line = shift_dense(dense_rows, tables)
    grad_state = gather_start(jnp.concatenate([grad_out, marks], axis=1))
    grad_blocks = gather_finish(grad_state, line[1::2])
    marks_all = jnp.concatenate([block[:, width:] for block in grad_blocks], axis=0)
    qkv_state = dense_start(line, slice(0, small_width), ())
    plane = qkv_state[1:]
    qkv_pieces, qkv_spots, far = dense_finish(qkv_state)
    out_state = dense_start(line, slice(small_width, None), far)
    packed_all = [
        lax.all_gather(after(packed, events), "batch", axis=0)
        for packed, events in zip(packed_own, ((line, grad_blocks), plane))
    ]

    normed, query, keyval, small = enter(
        tokens[0], cosine, sine_part, qkv_pieces, qkv_spots, first_gain, query_width, kv_width
    )

    rank_all = (
        marks_all[:, experts_total].astype(wide) * 32 + marks_all[:, experts_total + 1].astype(wide)
    )
    earlier = (rank_all[None, :] < rank_rows.astype(wide)[:, None]).astype(low)
    before = product(earlier, marks_all)
    capacity = 5 * group_rows * route_rows.shape[1] // (4 * experts_total)
    member = member.astype(wide)
    kept = jnp.where(before < capacity, member, 0.0)

    keyval_blocks = gather_blocks(after(keyval, out_state[1:]))
    if member_count == 4:
        ordered = keyval_blocks[:3] + [jnp.concatenate(keyval_blocks[3:], axis=0)]
        keys = jnp.concatenate(
            [
                lax.select_n(member_id, *ordered),
                lax.select_n(member_id ^ 1, *ordered),
                keyval,
            ],
            axis=0,
        )
    else:
        keys = jnp.concatenate(keyval_blocks, axis=0)
    attended, log_totals = attend(query, keys, bias)
    out_pieces, out_spots, _ = dense_finish(out_state, keyval_blocks[3:], attended)
    residual, sent, gate_rows = project(
        attended, tokens[0], small, member, kept, second_gain, out_pieces, out_spots
    )
    sent_blocks = gather_blocks(sent)

    carry, chunk_grads = None, []
    for packed, a, b in zip(packed_all, chunks[:-1], chunks[1:]):
        first = (member_id * local_experts + a).astype(jnp.int32).reshape(1)
        packed_grads, mixture_all, row_grad = expert_pass(
            place,
            first,
            sent_blocks,
            grad_blocks,
            packed,
            carry,
            cut and b == local_experts,
            b == local_experts,
        )
        carry = (mixture_all, row_grad)
        chunk_grads.append(packed_grads)

    def blocks_of(values):
        return [values[r * local_rows : (r + 1) * local_rows] for r in range(member_count)]

    totals = [sum_chunk(chunk_grads[0][0])]
    if cut:
        own, rest, far, near = chunk_grads[1]
        far, near = exchange_cores(far), exchange_cores(near)
        far_sum, down_sum = add_low(rest[1], far[0]), add_low(rest[2], far[1])
    turn_state = scatter_start(blocks_of(row_grad))
    if cut:
        turn_state = after(turn_state, (far_sum, down_sum))
    normed_grad = scatter_finish(turn_state)
    turned = turn(
        place,
        out_spots,
        (
            normed_grad,
            residual,
            grad_out,
            small,
            gate_rows,
            member,
            kept,
            sent,
            attended,
        ),
        out_pieces,
        cut,
        second_gain,
    )
    out_found = turned[:-2]
    resid_grad, head_grad = turned[-2:]
    mixture_blocks = blocks_of(after(mixture_all, normed_grad))
    if cut:
        mixture_parts = [mixture_blocks[0]] + [send_part(mixture_blocks, r) for r in (1, 2)]
        head_grad = after(head_grad, mixture_parts[1:])
        up_part = step_up(far_sum)
    query_grad, key_grads = attend_back(
        head_grad, query, keys, bias_turned, log_totals, cosine, sine_part
    )
    if member_count == 4:
        zero = jnp.zeros((), low)
        for_first, for_second, for_own = blocks_of(key_grads)[:3]
        key_parts = []
        for r in range(4):
            part = jnp.where(member_id == r, for_first, zero)
            part += jnp.where(member_id ^ 1 == r, for_second, zero)
            key_parts.append(part + for_own if r == 0 else part)
    else:
        key_parts = blocks_of(key_grads)
    if cut:
        out_found = out_found[1], exchange_cores(out_found[0])
        key_parts = after(key_parts, up_part)
    keyval_sum = scatter_blocks(key_parts)
    if cut:
        out_state = scatter_start(join_cores(*out_found))
    if cut:
        up_sum = add_low(rest[0], near[0], up_part)
        keyval_sum = after(keyval_sum, (out_found, up_sum))
    left = leave(
        place,
        qkv_spots,
        (
            keyval_sum,
            query_grad,
            normed,
            tokens[0],
            resid_grad,
            small,
            cosine,
            sine_part,
        ),
        qkv_pieces,
        cut,
        first_gain,
    )
    qkv_found, input_grad = left[:-1], left[-1]
    if cut:
        down_term = step_down(after(down_sum, key_parts))
        received = exchange_cores(after(qkv_found[0], (totals[0], out_state[1:], down_term)))
        out_plane = scatter_finish(out_state)
        up_term = step_up(up_sum)
        qkv_parts = join_cores(qkv_found[1], after(received, out_plane))
        qkv_plane = after(scatter_blocks(qkv_parts), up_term)
        mixture_parts.append(send_part(mixture_blocks, 3, qkv_plane))
        out_sum = line_finish(line_start(out_plane))
        qkv_state = line_start(qkv_plane)
        near, down_term, up_term = after((near, down_term, up_term), qkv_plane)
        terms = [[(totals[0], 0)], [(own, None), (near, 1), (down_term, None), (up_term, None)]]
        expert_totals = unpack(terms, gate_weight.shape, down_weight.shape)
        qkv_sum = line_finish(qkv_state, (expert_totals, mixture_parts[3]))
        mixture = total_of(mixture_parts)
    else:
        mixture = scatter_blocks(mixture_blocks)
        out_sum = scatter_whole(out_found)
        qkv_sum = scatter_whole(qkv_found)
        totals += [sum_chunk(found[0]) for found in chunk_grads[1:]]
        terms = [[(total, 0)] for total in totals]
        expert_totals = unpack(terms, gate_weight.shape, down_weight.shape)
    gate_total, up_total, down_total = expert_totals
    result = (residual + mixture).astype(low)
    return (
        result[None],
        input_grad[None],
        qkv_sum[:, qkv_width + first_gain],
        qkv_sum[:, :query_width],
        qkv_sum[:, query_width : query_width + kv_width],
        qkv_sum[:, query_width + kv_width : qkv_width],
        out_sum[:, :width],
        out_sum[:, width + second_gain],
        out_sum[:, width : width + experts_total],
        gate_total,
        up_total,
        down_total,
    )


def solution(mesh):
    return jax.shard_map(
        local,
        mesh=mesh,
        in_specs=(
            P("batch", "expert", None),
            P("batch", "expert", None),
            P(("batch", "expert")),
            P(("batch", "expert"), None),
            P(("batch", "expert"), None),
            P(("batch", "expert"), None),
            P(("batch", "expert"), None),
            P(("batch", "expert")),
            P(("batch", "expert"), None),
            P("expert", "batch", None),
            P("expert", "batch", None),
            P("expert", "batch", None),
            P("batch", "expert", None),
            P("batch", "expert"),
        ),
        out_specs=(
            P("batch", "expert", None),
            P("batch", "expert", None),
            P(("batch", "expert")),
            P(("batch", "expert"), None),
            P(("batch", "expert"), None),
            P(("batch", "expert"), None),
            P(("batch", "expert"), None),
            P(("batch", "expert")),
            P(("batch", "expert"), None),
            P("expert", "batch", None),
            P("expert", "batch", None),
            P("expert", "batch", None),
        ),
        check_vma=False,
    )
```

```python
from functools import partial

import jax
import jax.numpy as jnp
from jax import lax
from jax.experimental import pallas as pl
from jax.experimental.pallas import tpu as pltpu
from jax.sharding import PartitionSpec as P

HEADS = 24
KV_HEADS = 8
HEAD_DIM = 64
PROMPT = 512
CLEN = 256


EPS = 1e-06
THETA = 10000.0


def product(left, right):
    return jnp.dot(left, right, preferred_element_type=jnp.float32)


def place_of(row_ids):
    return jnp.where(row_ids < PROMPT, row_ids, PROMPT + (row_ids - PROMPT) % CLEN)


def visible(query_ids, key_ids):
    causal = key_ids[None, :] <= query_ids[:, None]
    same_run = (key_ids[None, :] - PROMPT) // CLEN == (query_ids[:, None] - PROMPT) // CLEN
    return causal & ((key_ids[None, :] < PROMPT) | same_run)


def dot_plain(left, right):
    return lax.dot_general(left, right, (((1,), (0,)), ((), ())), preferred_element_type=jnp.float32)


def dot_right(left, right):
    return lax.dot_general(left, right, (((1,), (1,)), ((), ())), preferred_element_type=jnp.float32)


def dot_left(left, right):
    return lax.dot_general(left, right, (((0,), (0,)), ((), ())), preferred_element_type=jnp.float32)


ANYWHERE = pl.BlockSpec(memory_space=pl.ANY)
INSIDE = pl.BlockSpec(memory_space=pltpu.VMEM)
SCALARS = pl.BlockSpec(memory_space=pltpu.SMEM)
VMEM_BYTES = 62 * 1024 * 1024


def cost(flops, *arrays):
    return pl.CostEstimate(flops=1, bytes_accessed=1, transcendentals=0)


def weight_copies(spots, pieces, target, sems):
    copies = []
    for p, piece in enumerate(pieces):
        blocks, rows = piece.shape[0], piece.shape[1]
        for k in range(blocks):
            place = pl.multiple_of(spots[p, k] * rows, rows)
            copies.append(
                pltpu.make_async_copy(
                    piece.at[k], target.at[pl.ds(place, rows)], sems.at[p * blocks + k]
                )
            )
    return copies


def block_copies(blocks, target, sems, first, columns=None):
    copies = []
    start = 0
    for i, block in enumerate(blocks):
        rows = block.shape[0]
        source = block if columns is None else block.at[:, columns]
        copies.append(
            pltpu.make_async_copy(source, target.at[pl.ds(start, rows)], sems.at[first + i])
        )
        start += rows
    return copies


def swap_halves(values):
    half = HEAD_DIM // 2
    lane = lax.broadcasted_iota(jnp.int32, values.shape, 1)
    return jnp.where(
        lane % HEAD_DIM < half,
        pltpu.roll(values, 2 * HEAD_DIM - half, 1),
        pltpu.roll(values, half, 1),
    )


def mean_square_scale(values):
    return lax.rsqrt(jnp.mean(values * values, axis=-1, keepdims=True) + EPS)


def enter_kernel(count, gain_at, spots, tokens, cosine, sine, *refs):
    pieces = refs[:count]
    normed, query, keyval, small, weight, sems = refs[count:]
    low = jnp.bfloat16
    copies = weight_copies(spots, pieces, weight, sems)
    for copy in copies:
        copy.start()
    inputs = tokens[...].astype(jnp.float32)
    scaled = inputs * mean_square_scale(inputs)
    for copy in copies:
        copy.wait()
    query_width = query.shape[1]
    kv_width = keyval.shape[1] // 2
    qkv_width = query_width + 2 * kv_width
    turned = weight[:, qkv_width:].astype(jnp.float32).T
    small[...] = turned
    rows = (scaled * turned[gain_at : gain_at + 1]).astype(low)
    normed[...] = rows
    pair = 2 * HEAD_DIM
    scale = HEAD_DIM**-0.5
    for start in range(0, query_width + kv_width, 512):
        product_part = dot_plain(rows, weight[:, start : start + 512])
        for offset in range(0, 512, pair):
            part = product_part[:, offset : offset + pair]
            part = part * cosine[...] + swap_halves(part) * sine[...]
            at = start + offset
            if at < query_width:
                query[:, at : at + pair] = (part * scale).astype(low)
            else:
                keyval[:, at - query_width : at - query_width + pair] = part.astype(low)
    keyval[:, kv_width:] = dot_plain(
        rows, weight[:, query_width + kv_width : qkv_width]
    ).astype(low)


def enter(tokens, cosine, sine, pieces, spots, gain_at, query_width, kv_width):
    rows, width = tokens.shape
    columns = pieces[0].shape[2]
    low = jnp.bfloat16
    return pl.pallas_call(
        partial(enter_kernel, len(pieces), gain_at),
        in_specs=[SCALARS, INSIDE, INSIDE, INSIDE] + [ANYWHERE] * len(pieces),
        out_specs=[INSIDE] * 4,
        out_shape=[
            jax.ShapeDtypeStruct((rows, width), low),
            jax.ShapeDtypeStruct((rows, query_width), low),
            jax.ShapeDtypeStruct((rows, 2 * kv_width), low),
            jax.ShapeDtypeStruct((columns - query_width - 2 * kv_width, width), jnp.float32),
        ],
        scratch_shapes=[
            pltpu.VMEM((width, columns), low),
            pltpu.SemaphoreType.DMA((len(pieces) * pieces[0].shape[0],)),
        ],
        compiler_params=pltpu.CompilerParams(vmem_limit_bytes=VMEM_BYTES),
        cost_estimate=cost(2 * rows * width * columns, *pieces),
        name="enter",
    )(spots, tokens, cosine, sine, *pieces)


def both_places(values):
    wide = values.astype(jnp.float32)
    low_lane = lax.broadcasted_iota(jnp.int32, values.shape, 1) < HEAD_DIM
    moved = pltpu.roll(wide, HEAD_DIM, 1)
    kind = values.dtype
    return [
        [jnp.where(low_lane, wide, 0.0).astype(kind), jnp.where(low_lane, 0.0, moved).astype(kind)],
        [jnp.where(low_lane, moved, 0.0).astype(kind), jnp.where(low_lane, 0.0, wide).astype(kind)],
    ]


def attend_kernel(query, keyval, bias, attended, log_totals):
    low = jnp.bfloat16
    rows = query.shape[0]
    kv_width = keyval.shape[1] // 2
    pair_lanes = 2 * HEAD_DIM
    repeat = HEADS // KV_HEADS
    log_totals[...] = jnp.zeros_like(log_totals)
    lane = lax.broadcasted_iota(jnp.int32, log_totals.shape, 1)

    @pl.loop(0, KV_HEADS // 2)
    def _(pair):
        at = pl.ds(pl.multiple_of(pair * pair_lanes, pair_lanes), pair_lanes)
        keys = both_places(keyval[:, at])
        at = pl.ds(pl.multiple_of(kv_width + pair * pair_lanes, pair_lanes), pair_lanes)
        values = both_places(keyval[:, at])
        for i in range(repeat):
            at = pl.ds(pl.multiple_of((pair * repeat + i) * pair_lanes, pair_lanes), pair_lanes)
            queries = query[:, at]
            total = jnp.zeros((rows, pair_lanes), jnp.float32)
            for a in range(2):
                head = 2 * i + a
                scores = dot_right(queries, keys[head // repeat][a]) + bias[...]
                peak = jnp.max(scores, axis=-1, keepdims=True)
                lifted = jnp.exp(scores - peak)
                row_total = jnp.sum(lifted, axis=-1, keepdims=True)
                weights_low = (lifted * (1.0 / row_total)).astype(low)
                total += dot_plain(weights_low, values[head // repeat][a])
                log_totals[...] = jnp.where(
                    lane == pair * (2 * repeat) + head, peak + jnp.log(row_total), log_totals[...]
                )
            attended[:, at] = total.astype(low)


def attend(query, keyval, bias):
    rows, query_width = query.shape
    return pl.pallas_call(
        attend_kernel,
        in_specs=[INSIDE] * 3,
        out_specs=[INSIDE] * 2,
        out_shape=[
            jax.ShapeDtypeStruct((rows, query_width), jnp.bfloat16),
            jax.ShapeDtypeStruct((rows, 128), jnp.float32),
        ],
        compiler_params=pltpu.CompilerParams(vmem_limit_bytes=VMEM_BYTES),
        cost_estimate=cost(8 * rows * query_width * bias.shape[1], query, keyval, bias),
        name="attend",
    )(query, keyval, bias)


def project_kernel(count, gain_at, spots, attended, tokens, small, member, kept, *refs):
    pieces = refs[:count]
    residual, sent, gate_rows, weight, sems = refs[count:]
    low = jnp.bfloat16
    width = tokens.shape[1]
    copies = weight_copies(spots, pieces, weight, sems)
    for copy in copies:
        copy.start()
    for copy in copies:
        copy.wait()
    hidden = tokens[...].astype(jnp.float32) + dot_plain(attended[...], weight[...])
    residual[...] = hidden
    gain = small[gain_at : gain_at + 1, :]
    normed = (hidden * mean_square_scale(hidden) * gain).astype(low)
    logits = dot_right(normed, small[...].astype(low))
    chosen = member[...] > 0.0
    logits = jnp.where(chosen, logits, -1e30)
    lifted = jnp.where(chosen, jnp.exp(logits - jnp.max(logits, axis=-1, keepdims=True)), 0.0)
    gates = lifted / jnp.sum(lifted, axis=-1, keepdims=True)
    gate_rows[...] = gates
    sent[:, :width] = normed
    sent[:, width:] = (gates * kept[...]).astype(low)


def project(attended, tokens, small, member, kept, gain_at, pieces, spots):
    rows, width = tokens.shape
    lanes = small.shape[0]
    low = jnp.bfloat16
    return pl.pallas_call(
        partial(project_kernel, len(pieces), gain_at),
        in_specs=[SCALARS] + [INSIDE] * 5 + [ANYWHERE] * len(pieces),
        out_specs=[INSIDE] * 3,
        out_shape=[
            jax.ShapeDtypeStruct((rows, width), jnp.float32),
            jax.ShapeDtypeStruct((rows, width + lanes), low),
            jax.ShapeDtypeStruct((rows, lanes), jnp.float32),
        ],
        scratch_shapes=[
            pltpu.VMEM((attended.shape[1], width), low),
            pltpu.SemaphoreType.DMA((len(pieces) * pieces[0].shape[0],)),
        ],
        compiler_params=pltpu.CompilerParams(vmem_limit_bytes=VMEM_BYTES),
        cost_estimate=cost(2 * rows * width * width, *pieces),
        name="project",
    )(spots, attended, tokens, small, member, kept, *pieces)


def grad_shapes(cut, rows, columns):
    low = jnp.bfloat16
    if cut:
        block = rows // 32
        return (
            [jax.ShapeDtypeStruct((4, 4, block, columns), low)] * 2,
            pltpu.VMEM((4, 2, 4, block, columns), low),
        )
    return (
        [jax.ShapeDtypeStruct((1, 1, 1, rows, columns), low)],
        pltpu.VMEM((1, 1, 1, rows, columns), low),
    )


def grad_copies(cut, place, source, outs, sems):
    if not cut:
        return [pltpu.make_async_copy(source, outs[0], sems.at[0])]
    core, member = place[0], place[1]
    other, own = outs
    copies = []
    for r in range(4):
        copies.append(
            pltpu.make_async_copy(
                source.at[:, 1 - core, member ^ r], other.at[r], sems.at[2 * r]
            )
        )
        copies.append(
            pltpu.make_async_copy(source.at[:, core, member ^ r], own.at[r], sems.at[2 * r + 1])
        )
    return copies


def turn_kernel(
    count,
    cut,
    gain_at,
    place,
    spots,
    normed_grad,
    residual,
    grad_out,
    small,
    gate_rows,
    member,
    kept,
    normed,
    attended,
    *refs,
):
    pieces = refs[:count]
    refs = refs[count:]
    outs = refs[: (2 if cut else 1)]
    resid_grad, head_grad, weight, weight_grad, sems, out_sems = refs[len(outs) :]
    low = jnp.bfloat16
    rows, width = residual.shape
    lanes = gate_rows.shape[1]
    copies = weight_copies(spots, pieces, weight, sems)
    for copy in copies:
        copy.start()
    lane = lax.broadcasted_iota(jnp.int32, (rows, lanes), 1)
    gates = gate_rows[...]
    gate_grads = normed_grad[:, width:] * kept[...]
    chosen_grad = gates * (gate_grads - jnp.sum(gates * gate_grads, axis=-1, keepdims=True))
    logit_grad = (chosen_grad * member[...]).astype(low)
    hidden = residual[...]
    scale = mean_square_scale(hidden)
    row_grad = normed_grad[:, :width] + dot_plain(logit_grad, small[...].astype(low))
    gain = small[gain_at : gain_at + 1, :]
    scaled = row_grad * gain
    total_grad = (
        grad_out[...].astype(jnp.float32)
        + scale * scaled
        - hidden * (scale * scale * scale) * jnp.mean(scaled * hidden, axis=-1, keepdims=True)
    )
    resid_grad[...] = total_grad
    attn_grad = total_grad.astype(low)
    shape = weight_grad.shape[:-1]
    gain_grad = (row_grad * hidden * scale).astype(low)
    picks = jnp.where(lane == gain_at, 1.0, 0.0).astype(low)
    weight_grad[..., width:] = (
        (dot_left(normed[...][:, :width], logit_grad) + dot_left(gain_grad, picks))
        .astype(low)
        .reshape(shape + (lanes,))
    )
    for start in range(0, width, 512):
        weight_grad[..., start : start + 512] = (
            dot_left(attended[...], attn_grad[:, start : start + 512])
            .astype(low)
            .reshape(shape + (512,))
        )
    out_copies = grad_copies(cut, place, weight_grad, outs, out_sems)
    for copy in out_copies:
        copy.start()
    for copy in copies:
        copy.wait()
    head_grad[...] = dot_right(attn_grad, weight[...]).astype(low)
    for copy in out_copies:
        copy.wait()


def turn(place, spots, operands, pieces, cut, gain_at):
    residual, gate_rows, attended = operands[1], operands[4], operands[8]
    rows, width = residual.shape
    query_width = attended.shape[1]
    low = jnp.bfloat16
    grads, held = grad_shapes(cut, query_width, width + gate_rows.shape[1])
    return pl.pallas_call(
        partial(turn_kernel, len(pieces), cut, gain_at),
        in_specs=[SCALARS, SCALARS] + [INSIDE] * len(operands) + [ANYWHERE] * len(pieces),
        out_specs=[ANYWHERE] * len(grads) + [INSIDE] * 2,
        out_shape=grads
        + [
            jax.ShapeDtypeStruct((rows, width), jnp.float32),
            jax.ShapeDtypeStruct((rows, query_width), low),
        ],
        scratch_shapes=[
            pltpu.VMEM((query_width, width), low),
            held,
            pltpu.SemaphoreType.DMA((len(pieces) * pieces[0].shape[0],)),
            pltpu.SemaphoreType.DMA((8,)),
        ],
        compiler_params=pltpu.CompilerParams(vmem_limit_bytes=VMEM_BYTES),
        cost_estimate=cost(0),
        name="turn",
    )(place, spots, *operands, *pieces)


def attend_back_kernel(
    head_grad, query, keyval, bias, log_totals, cosine, sine, query_grad, keyval_grad, totals
):
    low = jnp.bfloat16
    rows = query.shape[0]
    kv_width = keyval.shape[1] // 2
    pair_lanes = 2 * HEAD_DIM
    repeat = HEADS // KV_HEADS
    totals[...] = log_totals[...].T

    @pl.loop(0, KV_HEADS // 2)
    def _(pair):
        key_at = pl.ds(pl.multiple_of(pair * pair_lanes, pair_lanes), pair_lanes)
        value_at = pl.ds(pl.multiple_of(kv_width + pair * pair_lanes, pair_lanes), pair_lanes)
        keys = both_places(keyval[:, key_at])
        values = both_places(keyval[:, value_at])
        key_grads = [[None, None], [None, None]]
        value_grads = [[None, None], [None, None]]
        for i in range(repeat):
            at = pl.ds(pl.multiple_of((pair * repeat + i) * pair_lanes, pair_lanes), pair_lanes)
            queries = query[:, at]
            grads = head_grad[:, at]
            query_part = jnp.zeros((rows, pair_lanes), jnp.float32)
            for a in range(2):
                head = 2 * i + a
                g = head // repeat
                total = totals[pl.ds(pair * (2 * repeat) + head, 1), :]
                weights = jnp.exp(dot_right(keys[g][a], queries) + bias[...] - total)
                weight_grads = dot_right(values[g][a], grads)
                delta = jnp.sum(weights * weight_grads, axis=0, keepdims=True)
                score_grads = (weights * (weight_grads - delta)).astype(low)
                value_part = dot_plain(weights.astype(low), grads)
                key_part = dot_plain(score_grads, queries)
                query_part += dot_left(score_grads, keys[g][a])
                if key_grads[g][a] is None:
                    key_grads[g][a], value_grads[g][a] = key_part, value_part
                else:
                    key_grads[g][a] += key_part
                    value_grads[g][a] += value_part
            query_part = query_part * (HEAD_DIM**-0.5)
            query_part = query_part * cosine[...] - swap_halves(query_part) * sine[...]
            query_grad[:, at] = query_part.astype(low)
        low_lane = lax.broadcasted_iota(jnp.int32, (keyval.shape[0], pair_lanes), 1) < HEAD_DIM
        for at, found in ((key_at, key_grads), (value_at, value_grads)):
            keyval_grad[:, at] = jnp.where(
                low_lane,
                found[0][0] + pltpu.roll(found[0][1], HEAD_DIM, 1),
                pltpu.roll(found[1][0], HEAD_DIM, 1) + found[1][1],
            ).astype(low)


def attend_back(head_grad, query, keyval, bias, log_totals, cosine, sine):
    rows, query_width = query.shape
    low = jnp.bfloat16
    return pl.pallas_call(
        attend_back_kernel,
        in_specs=[INSIDE] * 7,
        out_specs=[INSIDE] * 2,
        out_shape=[
            jax.ShapeDtypeStruct((rows, query_width), low),
            jax.ShapeDtypeStruct(keyval.shape, low),
        ],
        scratch_shapes=[pltpu.VMEM((128, rows), jnp.float32)],
        compiler_params=pltpu.CompilerParams(vmem_limit_bytes=VMEM_BYTES),
        cost_estimate=cost(0),
        name="attend_back",
    )(head_grad, query, keyval, bias, log_totals, cosine, sine)


def leave_kernel(
    count,
    cut,
    gain_at,
    place,
    spots,
    keyval_sum,
    query_grad,
    normed,
    tokens,
    resid_grad,
    small,
    cosine,
    sine,
    *refs,
):
    pieces = refs[:count]
    refs = refs[count:]
    outs = refs[: (2 if cut else 1)]
    input_grad, weight, weight_grad, joined, sems, out_sems = refs[len(outs) :]
    low = jnp.bfloat16
    rows, width = tokens.shape
    query_width = query_grad.shape[1]
    kv_width = keyval_sum.shape[1] // 2
    qkv_width = query_width + 2 * kv_width
    pair = 2 * HEAD_DIM
    copies = weight_copies(spots, pieces, weight, sems)
    for copy in copies:
        copy.start()
    joined[:, :query_width] = query_grad[...]
    for start in range(0, kv_width, pair):
        part = keyval_sum[:, start : start + pair]
        part = part * cosine[...] - swap_halves(part) * sine[...]
        joined[:, query_width + start : query_width + start + pair] = part.astype(low)
    joined[:, query_width + kv_width :] = keyval_sum[:, kv_width:].astype(low)
    shape = weight_grad.shape[:-1]
    for start in range(0, qkv_width, 512):
        weight_grad[..., start : start + 512] = (
            dot_left(normed[...], joined[:, start : start + 512]).astype(low).reshape(shape + (512,))
        )
    for copy in copies:
        copy.wait()
    row_grad = dot_right(joined[...], weight[:, :qkv_width])
    inputs = tokens[...].astype(jnp.float32)
    scale = mean_square_scale(inputs)
    lanes = weight_grad.shape[-1] - qkv_width
    lane = lax.broadcasted_iota(jnp.int32, (rows, lanes), 1)
    picks = jnp.where(lane == gain_at, 1.0, 0.0).astype(low)
    weight_grad[..., qkv_width:] = (
        dot_left((row_grad * inputs * scale).astype(low), picks).astype(low).reshape(shape + (lanes,))
    )
    out_copies = grad_copies(cut, place, weight_grad, outs, out_sems)
    for copy in out_copies:
        copy.start()
    scaled = row_grad * small[gain_at : gain_at + 1, :]
    input_grad[...] = (
        resid_grad[...]
        + scale * scaled
        - inputs * (scale * scale * scale) * jnp.mean(scaled * inputs, axis=-1, keepdims=True)
    )
    for copy in out_copies:
        copy.wait()


def leave(place, spots, operands, pieces, cut, gain_at):
    tokens, query_grad, keyval_sum = operands[3], operands[1], operands[0]
    rows, width = tokens.shape
    columns = pieces[0].shape[2]
    low = jnp.bfloat16
    grads, held = grad_shapes(cut, width, columns)
    return pl.pallas_call(
        partial(leave_kernel, len(pieces), cut, gain_at),
        in_specs=[SCALARS, SCALARS] + [INSIDE] * len(operands) + [ANYWHERE] * len(pieces),
        out_specs=[ANYWHERE] * len(grads) + [INSIDE],
        out_shape=grads + [jax.ShapeDtypeStruct((rows, width), jnp.float32)],
        scratch_shapes=[
            pltpu.VMEM((width, columns), low),
            held,
            pltpu.VMEM((rows, query_grad.shape[1] + keyval_sum.shape[1]), low),
            pltpu.SemaphoreType.DMA((len(pieces) * pieces[0].shape[0],)),
            pltpu.SemaphoreType.DMA((8,)),
        ],
        compiler_params=pltpu.CompilerParams(vmem_limit_bytes=VMEM_BYTES),
        cost_estimate=cost(0),
        name="leave",
    )(place, spots, *operands, *pieces)


def expert_kernel(cut, carried, last, row_blocks, grad_blocks, row_tile, place, first, packed, *refs):
    blocks_in = refs[:row_blocks]
    grads_in = refs[row_blocks : row_blocks + grad_blocks]
    refs = refs[row_blocks + grad_blocks :]
    if carried:
        mix_in, turn_in = refs[:2]
        refs = refs[2:]
    count = packed.shape[2]
    outs = 4 if cut else 1
    packed_grads = refs[:outs]
    mix_out, turn_out = refs[outs : outs + 2]
    refs = refs[outs + 2 :]
    if last:
        mix, turned = refs[:2]
        refs = refs[2:]
    else:
        mix, turned = mix_out, turn_out
    (
        rows,
        grads,
        gates,
        gate_w,
        up_w,
        down_w,
        gate_g,
        up_g,
        down_g,
        weighted,
        gate_side,
        up_side,
        load_sems,
        save_sems,
        carry_sems,
    ) = refs
    hidden_width = gate_w.shape[-1]
    total_rows, width = rows.shape
    lanes = gates.shape[1]
    low = jnp.bfloat16

    def sides(gate, up, down):
        for side, inner in ((0, gate), (1, up)):
            for j in range(3):
                yield side, pl.ds(j * hidden_width, hidden_width), inner, j
        yield 2, pl.ds(0, width), down, None

    def loads(e):
        slot = e % 2
        copies = []
        for i, (side, columns, inner, j) in enumerate(sides(gate_w, up_w, down_w)):
            outer = packed.at[:, side, e, :, columns]
            inner = inner.at[slot] if j is None else inner.at[slot, :, j]
            copies.append(pltpu.make_async_copy(outer, inner, load_sems.at[slot, i]))
        return copies

    def saves(e):
        slot = e % 2
        copies = []
        for i, (side, columns, inner, j) in enumerate(sides(gate_g, up_g, down_g)):
            if not cut:
                outer = packed_grads[0].at[:, side, e, :, columns]
                source = inner.at[slot] if j is None else inner.at[slot, :, j]
                copies.append(pltpu.make_async_copy(source, outer, save_sems.at[slot, i]))
                continue
            own, rest, far, near = packed_grads
            targets = [own, rest.at[0], rest.at[1], rest.at[2]]
            targets += [near.at[1], near.at[0], far.at[0], far.at[1]]
            for n, target in enumerate(targets):
                block = 2 * lax.rem(place[2] + n % 4, 4) + (place[0] ^ (n // 4))
                source = inner.at[slot, block] if j is None else inner.at[slot, block, j]
                outer = target.at[side, e, :, columns]
                copies.append(pltpu.make_async_copy(source, outer, save_sems.at[slot, 8 * i + n]))
        return copies

    carries = (
        block_copies(grads_in, grads, carry_sems, 0, pl.ds(0, width))
        + block_copies(blocks_in, rows, carry_sems, grad_blocks, pl.ds(0, width))
        + block_copies(
            blocks_in, gates, carry_sems, grad_blocks + row_blocks, pl.ds(width, lanes)
        )
    )
    sums = []
    if carried:
        at = grad_blocks + 2 * row_blocks
        sums = [
            pltpu.make_async_copy(mix_in, mix, carry_sems.at[at]),
            pltpu.make_async_copy(turn_in, turned, carry_sems.at[at + 1]),
        ]
    for copy in loads(0) + carries + sums:
        copy.start()
    for e in range(count):
        slot = e % 2
        if e + 1 < count:
            for copy in loads(e + 1):
                copy.start()
        for copy in loads(e):
            copy.wait()
        if e == 0:
            for copy in carries:
                copy.wait()
            if not carried:
                turned[:, width:] = jnp.zeros((total_rows, lanes), jnp.float32)

        @pl.loop(0, total_rows // row_tile)
        def _(tile):
            span = pl.ds(pl.multiple_of(tile * row_tile, row_tile), row_tile)
            gate_full = gate_w[slot].reshape(width, hidden_width)
            up_full = up_w[slot].reshape(width, hidden_width)
            down_full = down_w[slot].reshape(hidden_width, width)
            here = rows[span, :]
            slope = dot_right(grads[span, :], down_full)
            gate_pre = dot_plain(here, gate_full)
            up_pre = dot_plain(here, up_full)
            lane = lax.broadcasted_iota(jnp.int32, (row_tile, lanes), 1)
            chosen = lane == first[0] + e
            gate_column = jnp.sum(
                jnp.where(chosen, gates[span, :].astype(jnp.float32), 0.0), axis=1, keepdims=True
            )
            sigmoid_gate = jax.nn.sigmoid(gate_pre)
            activated = gate_pre * sigmoid_gate
            hidden = (activated * up_pre).astype(low).astype(jnp.float32)
            share = jnp.sum(hidden * slope, axis=1, keepdims=True)
            if e == 0 and sums:

                @pl.when(tile == 0)
                def _():
                    for copy in sums:
                        copy.wait()

            turned[span, width:] = jnp.where(chosen, share, turned[span, width:])
            part_weighted = (hidden * gate_column).astype(low)
            hidden_grad = slope * gate_column
            part_gate = (
                hidden_grad * up_pre * (sigmoid_gate + activated * (1.0 - sigmoid_gate))
            ).astype(low)
            part_up = (hidden_grad * activated).astype(low)
            weighted[span, :] = part_weighted
            gate_side[span, :] = part_gate
            up_side[span, :] = part_up
            mix_part = dot_plain(part_weighted, down_full)
            turn_part = dot_right(part_gate, gate_full) + dot_right(part_up, up_full)
            if e == 0 and not carried:
                mix[span, :] = mix_part
                turned[span, :width] = turn_part
            elif last and e == count - 1:
                mix_out[span, :] = (mix[span, :] + mix_part).astype(low)
                turn_out[span, :width] = (turned[span, :width] + turn_part).astype(low)
                turn_out[span, width:] = turned[span, width:].astype(low)
            else:
                mix[span, :] += mix_part
                turned[span, :width] += turn_part

        if e >= 2:
            for copy in saves(e - 2):
                copy.wait()
        down_g[slot] = dot_left(weighted[...], grads[...]).astype(low).reshape(down_g.shape[1:])
        gate_g[slot] = dot_left(rows[...], gate_side[...]).astype(low).reshape(gate_g.shape[1:])
        up_g[slot] = dot_left(rows[...], up_side[...]).astype(low).reshape(up_g.shape[1:])
        for copy in saves(e):
            copy.start()
    for e in range(max(0, count - 2), count):
        for copy in saves(e):
            copy.wait()


def expert_pass(place, first, rows, grads, packed, carry, cut, last):
    blocks, _, count, part, width = packed.shape
    hidden_width = blocks * part
    total_rows = sum(block.shape[0] for block in rows)
    lanes = rows[0].shape[1] - width
    low = jnp.bfloat16
    wide = jnp.float32
    carried = carry is not None
    flops = 18 * total_rows * count * hidden_width * width
    side = pltpu.VMEM((2, blocks, 3, part, hidden_width), low)
    sides = [side, side, pltpu.VMEM((2, blocks, part, width), low)]
    sums = [(total_rows, width), (total_rows, width + lanes)]
    one = packed.shape[1:]
    grads_out = [one, (3,) + one, (2,) + one, (2,) + one] if cut else [packed.shape]
    outs = len(grads_out)
    found = pl.pallas_call(
        partial(expert_kernel, cut, carried, last, len(rows), len(grads), min(512, total_rows)),
        in_specs=[SCALARS, SCALARS]
        + [ANYWHERE] * (1 + len(rows) + len(grads) + (2 if carried else 0)),
        out_specs=[ANYWHERE] * outs + [INSIDE, INSIDE],
        out_shape=[jax.ShapeDtypeStruct(shape, low) for shape in grads_out]
        + [jax.ShapeDtypeStruct(shape, low if last else wide) for shape in sums],
        scratch_shapes=([pltpu.VMEM(shape, wide) for shape in sums] if last else [])
        + [
            pltpu.VMEM((total_rows, width), low),
            pltpu.VMEM((total_rows, width), low),
            pltpu.VMEM((total_rows, lanes), low),
        ]
        + sides
        + sides
        + [pltpu.VMEM((total_rows, hidden_width), low)] * 3
        + [
            pltpu.SemaphoreType.DMA((2, 7)),
            pltpu.SemaphoreType.DMA((2, 56)),
            pltpu.SemaphoreType.DMA((2 * len(rows) + len(grads) + 2,)),
        ],
        compiler_params=pltpu.CompilerParams(vmem_limit_bytes=VMEM_BYTES),
        cost_estimate=cost(flops, packed, packed, *rows, *grads),
        name="experts",
    )(place, first, packed, *rows, *grads, *(carry or ()))
    return found[:outs], found[outs], found[outs + 1]


def unpack_kernel(counts, places, *refs):
    found, (gate, up, down) = refs[:-3], refs[-3:]
    found = [array if place is None else array.at[place] for array, place in zip(found, places)]
    hidden_width = gate.shape[2]
    base = 0
    at = 0
    for terms in counts:
        parts = found[at : at + terms]
        at += terms
        count, part = parts[0].shape[1], parts[0].shape[2]
        for e in range(count):
            for side in range(3):
                total = parts[0][side, e].astype(jnp.float32)
                for other in parts[1:]:
                    total += other[side, e].astype(jnp.float32)
                if side == 2:
                    down[base + e] = total
                    continue
                for j in range(3):
                    (gate, up)[side][base + e, j * part : (j + 1) * part, :] = total[
                        :, j * hidden_width : (j + 1) * hidden_width
                    ]
        base += count


def unpack(chunks, gate_shape, down_shape):
    arrays = [array for terms in chunks for array, _ in terms]
    places = [place for terms in chunks for _, place in terms]
    return pl.pallas_call(
        partial(unpack_kernel, [len(terms) for terms in chunks], places),
        in_specs=[INSIDE] * len(arrays),
        out_specs=[INSIDE] * 3,
        out_shape=[
            jax.ShapeDtypeStruct(gate_shape, jnp.float32),
            jax.ShapeDtypeStruct(gate_shape, jnp.float32),
            jax.ShapeDtypeStruct(down_shape, jnp.float32),
        ],
        compiler_params=pltpu.CompilerParams(vmem_limit_bytes=VMEM_BYTES),
        cost_estimate=cost(0),
        name="unpack",
    )(*arrays)


def cube():
    return lax.axis_size("batch") == 8 and lax.axis_size("expert") == 4


def pair_moves(size, flip):
    return [(i, i ^ flip) for i in range(size)]


def shift_moves(step):
    return [(2 * z + c, 2 * ((z + step) % 4) + c) for z in range(4) for c in range(2)]


def gather_start(rows):
    size = lax.axis_size("expert")
    if size != 4:
        stacked = lax.all_gather(rows, "expert", axis=0)
        own = lax.axis_index("expert")
        return [
            lax.dynamic_index_in_dim(stacked, own ^ r, axis=0, keepdims=False) for r in range(size)
        ]
    return [rows] + [lax.ppermute(rows, "expert", pair_moves(4, r)) for r in (1, 2)]


def gather_finish(state, events=()):
    if lax.axis_size("expert") != 4:
        return state
    first, second = after(state[1:], events)
    half = first.shape[0] // 2
    top = lax.ppermute(second[:half], "expert", pair_moves(4, 1))
    bottom = lax.ppermute(first[half:], "expert", pair_moves(4, 2))
    return state + [top, bottom]


def gather_blocks(rows):
    return gather_finish(gather_start(rows))


def scatter_start(parts):
    low = jnp.bfloat16
    if lax.axis_size("expert") != 4:
        own = lax.axis_index("expert")
        order = jnp.arange(len(parts), dtype=jnp.int32) ^ own
        stacked = jnp.take(jnp.stack(parts), order, axis=0).astype(low)
        return [lax.psum_scatter(stacked, "expert", scatter_dimension=0).astype(jnp.float32)]
    across, along = pair_moves(4, 1), pair_moves(4, 2)
    half = parts[0].shape[0] // 2
    top = lax.ppermute(parts[3][:half].astype(low), "expert", across)
    bottom = lax.ppermute(parts[3][half:].astype(low), "expert", along)
    first_top = lax.ppermute(parts[1][:half].astype(low), "expert", across)
    second_bottom = lax.ppermute(parts[2][half:].astype(low), "expert", along)
    for_first = add_low(parts[1][half:], bottom)
    for_second = add_low(parts[2][:half], top)
    return [parts[0], first_top, second_bottom, for_first, for_second]


def scatter_finish(state):
    if len(state) == 1:
        return state[0]
    own, first_top, second_bottom, for_first, for_second = state
    half = first_top.shape[0]
    second_top = lax.ppermute(for_second, "expert", pair_moves(4, 2))
    first_bottom = lax.ppermute(for_first, "expert", pair_moves(4, 1))
    return jnp.concatenate(
        [
            total_of([own[:half], first_top, second_top]),
            total_of([own[half:], first_bottom, second_bottom]),
        ],
        axis=0,
    )


def scatter_blocks(parts):
    return scatter_finish(scatter_start(parts))


def after(values, events):
    return lax.optimization_barrier((values, events))[0]


def send_parts(parts):
    if lax.axis_size("expert") != 4:
        return [scatter_blocks(parts)]
    low = jnp.bfloat16
    return [parts[0]] + [
        lax.ppermute(parts[r].astype(low), "expert", pair_moves(4, r)) for r in range(1, 4)
    ]


def total_of(parts):
    total = parts[0].astype(jnp.float32)
    for part in parts[1:]:
        total += part.astype(jnp.float32)
    return total


def shift_dense(rows, events):
    if not cube():
        return [lax.all_gather(rows, ("batch", "expert"), axis=0, tiled=True)]
    below, above = step_up(rows), step_down(rows)
    return [rows, below, step_up(after(below, (above, events))), above]


def dense_start(line, columns, events):
    found = [rows[:, columns] for rows in line]
    if not cube():
        return [found[0][None]]
    return gather_start(after(jnp.stack(found), events))


def dense_finish(state, events=(), late=()):
    if not cube():
        return state, jnp.zeros((1, 1), jnp.int32), ()
    place = lax.axis_index("batch")
    level, core = place // 2, place % 2
    member = lax.axis_index("expert")
    mine = gather_finish(state, events)
    far = mine[3:]
    mine = mine[:3] + [after(jnp.concatenate(far, axis=0), late)]
    other = [exchange_cores(block) for block in mine]
    spots = [
        [(((level + 4 - k) % 4) * 2 + (core ^ c)) * 4 + (member ^ r) for k in range(4)]
        for c in range(2)
        for r in range(4)
    ]
    return mine + other, jnp.array(spots, jnp.int32), far


def sum_chunk(packed_grad):
    return lax.psum_scatter(packed_grad, "batch", scatter_dimension=0, tiled=True)


def exchange_cores(values):
    return lax.ppermute(values, "batch", pair_moves(8, 1))


def step_up(values):
    return lax.ppermute(values, "batch", shift_moves(1))


def step_down(values):
    return lax.ppermute(values, "batch", shift_moves(3))


def add_low(*parts):
    total = parts[0].astype(jnp.float32)
    for part in parts[1:]:
        total += part.astype(jnp.float32)
    return total.astype(jnp.bfloat16)


def join_cores(own, received):
    return [add_low(own[r], received[r]) for r in range(4)]


def line_start(plane):
    level = lax.axis_index("batch") // 2
    own, up, far, down = (
        lax.dynamic_index_in_dim(plane, (level + r) % 4, axis=0, keepdims=False) for r in range(4)
    )
    return own, step_down(add_low(down)), add_low(up, step_up(add_low(far)))


def line_finish(state, events=()):
    own, down, up = state
    return total_of([own, down, step_up(after(up, events))])


def scatter_whole(found):
    values = found[0].reshape(found[0].shape[3:])
    total = lax.psum_scatter(values, ("batch", "expert"), scatter_dimension=0, tiled=True)
    return total.astype(jnp.float32)


def pack_kernel(chunks, query, key, value, small, out, gate, up, down, dense, *packed):
    start = 0
    for part in (query, key, value, small, out):
        dense[:, start : start + part.shape[1]] = part[...]
        start += part.shape[1]
    part, hidden_width = down.shape[1], gate.shape[2]
    for n, target in enumerate(packed):
        for e in range(chunks[n], chunks[n + 1]):
            for side, source in ((0, gate), (1, up)):
                for j in range(3):
                    target[side, e - chunks[n], :, j * hidden_width : (j + 1) * hidden_width] = (
                        source[e, j * part : (j + 1) * part, :]
                    )
            target[2, e - chunks[n]] = down[e]


def pack(chunks, query, key, value, small, out, gate, up, down):
    low = jnp.bfloat16
    columns = sum(part.shape[1] for part in (query, key, value, small, out))
    return pl.pallas_call(
        partial(pack_kernel, chunks),
        in_specs=[INSIDE] * 8,
        out_specs=[INSIDE] * len(chunks),
        out_shape=[jax.ShapeDtypeStruct((query.shape[0], columns), low)]
        + [
            jax.ShapeDtypeStruct((3, b - a) + down.shape[1:], low)
            for a, b in zip(chunks[:-1], chunks[1:])
        ],
        compiler_params=pltpu.CompilerParams(vmem_limit_bytes=VMEM_BYTES),
        cost_estimate=cost(0),
        name="pack",
    )(query, key, value, small, out, gate, up, down)


def local(
    tokens,
    cotangent,
    attn_gain,
    query_weight,
    key_weight,
    value_weight,
    out_weight,
    ffn_gain,
    router_weight,
    gate_weight,
    up_weight,
    down_weight,
    routes,
    ranking,
):
    low = jnp.bfloat16
    wide = jnp.float32
    query_width = HEADS * HEAD_DIM
    kv_width = KV_HEADS * HEAD_DIM
    qkv_width = query_width + 2 * kv_width
    width = tokens.shape[2]
    experts_total = router_weight.shape[1]
    extra = -(-(experts_total + 2) // 128) * 128
    first_gain, second_gain = experts_total, experts_total + 1
    local_experts = gate_weight.shape[0]
    member_count = lax.axis_size("expert")
    member_id = lax.axis_index("expert")
    local_rows = tokens.shape[1]
    group_rows = local_rows * member_count
    cut = cube()
    line_place = lax.axis_index("batch")
    place = jnp.stack([line_place % 2, member_id, line_place // 2]).astype(jnp.int32)

    route_rows = routes[0]
    rank_rows = ranking[0]
    expert_lanes = jnp.arange(extra, dtype=jnp.int32)
    member = jnp.any(route_rows[:, :, None] == expert_lanes[None, None, :], axis=1)
    marks = jnp.where(
        expert_lanes[None, :] == experts_total,
        (rank_rows // 32)[:, None],
        jnp.where(expert_lanes[None, :] == experts_total + 1, (rank_rows % 32)[:, None], member),
    ).astype(low)
    grad_out = cotangent[0]
    small_width = qkv_width + extra
    chunks = (0, 3, local_experts)
    dense_rows, *packed_own = pack(
        chunks,
        query_weight,
        key_weight,
        value_weight,
        jnp.concatenate(
            [
                router_weight,
                attn_gain[:, None],
                ffn_gain[:, None],
                jnp.zeros((query_weight.shape[0], extra - experts_total - 2), low),
            ],
            axis=1,
        ),
        out_weight,
        gate_weight,
        up_weight,
        down_weight,
    )
    row_ids = member_id * local_rows + jnp.arange(local_rows, dtype=jnp.int32)
    half_dim = HEAD_DIM // 2
    frequency = THETA ** (-jnp.arange(half_dim, dtype=wide) / half_dim)
    angles = place_of(row_ids).astype(wide)[:, None] * frequency[None, :]
    cosine = jnp.tile(jnp.cos(angles), (1, 4))
    sine_part = jnp.tile(jnp.concatenate([-jnp.sin(angles), jnp.sin(angles)], axis=1), (1, 2))
    if member_count == 4:
        away = 1 << 20
        starts = [
            jnp.where(member_id >= 1, 0, away),
            jnp.where(member_id >= 2, local_rows, away),
            member_id * local_rows,
        ]
    else:
        starts = [(member_id ^ r) * local_rows for r in range(member_count)]
    key_ids = jnp.concatenate([s + jnp.arange(local_rows, dtype=jnp.int32) for s in starts])
    bias = jnp.where(visible(row_ids, key_ids), 0.0, -1e30).astype(wide)
    bias_turned = bias.T
    tables = (cosine, sine_part, bias, bias_turned)

    line = shift_dense(dense_rows, tables)
    grad_state = gather_start(jnp.concatenate([grad_out, marks], axis=1))
    grad_blocks = gather_finish(grad_state, line[1::2])
    marks_all = jnp.concatenate([block[:, width:] for block in grad_blocks], axis=0)
    qkv_state = dense_start(line, slice(0, small_width), ())
    plane = qkv_state[1:]
    qkv_pieces, qkv_spots, far = dense_finish(qkv_state)
    out_state = dense_start(line, slice(small_width, None), far)
    packed_all = [
        lax.all_gather(after(packed, events), "batch", axis=0)
        for packed, events in zip(packed_own, ((line, grad_blocks), plane))
    ]

    normed, query, keyval, small = enter(
        tokens[0], cosine, sine_part, qkv_pieces, qkv_spots, first_gain, query_width, kv_width
    )

    rank_all = (
        marks_all[:, experts_total].astype(wide) * 32 + marks_all[:, experts_total + 1].astype(wide)
    )
    earlier = (rank_all[None, :] < rank_rows.astype(wide)[:, None]).astype(low)
    before = product(earlier, marks_all)
    capacity = 5 * group_rows * route_rows.shape[1] // (4 * experts_total)
    member = member.astype(wide)
    kept = jnp.where(before < capacity, member, 0.0)

    keyval_blocks = gather_blocks(after(keyval, out_state[1:]))
    if member_count == 4:
        ordered = keyval_blocks[:3] + [jnp.concatenate(keyval_blocks[3:], axis=0)]
        keys = jnp.concatenate(
            [
                lax.select_n(member_id, *ordered),
                lax.select_n(member_id ^ 1, *ordered),
                keyval,
            ],
            axis=0,
        )
    else:
        keys = jnp.concatenate(keyval_blocks, axis=0)
    attended, log_totals = attend(query, keys, bias)
    out_pieces, out_spots, _ = dense_finish(out_state, keyval_blocks[3:], attended)
    residual, sent, gate_rows = project(
        attended, tokens[0], small, member, kept, second_gain, out_pieces, out_spots
    )
    sent_blocks = gather_blocks(sent)

    carry, chunk_grads = None, []
    for packed, a, b in zip(packed_all, chunks[:-1], chunks[1:]):
        first = (member_id * local_experts + a).astype(jnp.int32).reshape(1)
        packed_grads, mixture_all, row_grad = expert_pass(
            place,
            first,
            sent_blocks,
            grad_blocks,
            packed,
            carry,
            cut and b == local_experts,
            b == local_experts,
        )
        carry = (mixture_all, row_grad)
        chunk_grads.append(packed_grads)

    def blocks_of(values):
        return [values[r * local_rows : (r + 1) * local_rows] for r in range(member_count)]

    totals = [sum_chunk(chunk_grads[0][0])]
    if cut:
        own, rest, far, near = chunk_grads[1]
        far, near = exchange_cores(far), exchange_cores(near)
        far_sum, down_sum = add_low(rest[1], far[0]), add_low(rest[2], far[1])
    turn_state = scatter_start(blocks_of(row_grad))
    if cut:
        turn_state = after(turn_state, (far_sum, down_sum, near))
    normed_grad = scatter_finish(turn_state)
    turned = turn(
        place,
        out_spots,
        (
            normed_grad,
            residual,
            grad_out,
            small,
            gate_rows,
            member,
            kept,
            sent,
            attended,
        ),
        out_pieces,
        cut,
        second_gain,
    )
    out_found = turned[:-2]
    resid_grad, head_grad = turned[-2:]
    mixture_parts = send_parts(blocks_of(after(mixture_all, normed_grad)))
    if cut:
        up_sum = add_low(rest[0], near[0], step_up(far_sum))
    query_grad, key_grads = attend_back(
        head_grad, query, keys, bias_turned, log_totals, cosine, sine_part
    )
    if member_count == 4:
        zero = jnp.zeros((), low)
        for_first, for_second, for_own = blocks_of(key_grads)[:3]
        key_parts = []
        for r in range(4):
            part = jnp.where(member_id == r, for_first, zero)
            part += jnp.where(member_id ^ 1 == r, for_second, zero)
            key_parts.append(part + for_own if r == 0 else part)
    else:
        key_parts = blocks_of(key_grads)
    if cut:
        out_found = out_found[1], exchange_cores(out_found[0])
        key_parts = after(key_parts, (mixture_parts[1:], up_sum))
    keyval_sum = scatter_blocks(key_parts)
    if cut:
        out_state = scatter_start(join_cores(*out_found))
    if cut:
        keyval_sum = after(keyval_sum, out_found)
    left = leave(
        place,
        qkv_spots,
        (
            keyval_sum,
            query_grad,
            normed,
            tokens[0],
            resid_grad,
            small,
            cosine,
            sine_part,
        ),
        qkv_pieces,
        cut,
        first_gain,
    )
    qkv_found, input_grad = left[:-1], left[-1]
    result = (residual + total_of(mixture_parts)).astype(low)
    if cut:
        down_term = step_down(after(down_sum, key_parts))
        received = exchange_cores(after(qkv_found[0], (totals[0], out_state[1:], down_term)))
        out_plane = scatter_finish(out_state)
        up_term = step_up(up_sum)
        qkv_parts = join_cores(qkv_found[1], after(received, out_plane))
        qkv_plane = after(scatter_blocks(qkv_parts), up_term)
        out_sum = line_finish(line_start(out_plane))
        qkv_state = line_start(qkv_plane)
        near, down_term, up_term = after((near, down_term, up_term), qkv_plane)
        terms = [[(totals[0], 0)], [(own, None), (near, 1), (down_term, None), (up_term, None)]]
        expert_totals = unpack(terms, gate_weight.shape, down_weight.shape)
        qkv_sum = line_finish(qkv_state, expert_totals)
    else:
        out_sum = scatter_whole(out_found)
        qkv_sum = scatter_whole(qkv_found)
        totals += [sum_chunk(found[0]) for found in chunk_grads[1:]]
        terms = [[(total, 0)] for total in totals]
        expert_totals = unpack(terms, gate_weight.shape, down_weight.shape)
    gate_total, up_total, down_total = expert_totals
    return (
        result[None],
        input_grad[None],
        qkv_sum[:, qkv_width + first_gain],
        qkv_sum[:, :query_width],
        qkv_sum[:, query_width : query_width + kv_width],
        qkv_sum[:, query_width + kv_width : qkv_width],
        out_sum[:, :width],
        out_sum[:, width + second_gain],
        out_sum[:, width : width + experts_total],
        gate_total,
        up_total,
        down_total,
    )


def solution(mesh):
    return jax.shard_map(
        local,
        mesh=mesh,
        in_specs=(
            P("batch", "expert", None),
            P("batch", "expert", None),
            P(("batch", "expert")),
            P(("batch", "expert"), None),
            P(("batch", "expert"), None),
            P(("batch", "expert"), None),
            P(("batch", "expert"), None),
            P(("batch", "expert")),
            P(("batch", "expert"), None),
            P("expert", "batch", None),
            P("expert", "batch", None),
            P("expert", "batch", None),
            P("batch", "expert", None),
            P("batch", "expert"),
        ),
        out_specs=(
            P("batch", "expert", None),
            P("batch", "expert", None),
            P(("batch", "expert")),
            P(("batch", "expert"), None),
            P(("batch", "expert"), None),
            P(("batch", "expert"), None),
            P(("batch", "expert"), None),
            P(("batch", "expert")),
            P(("batch", "expert"), None),
            P("expert", "batch", None),
            P("expert", "batch", None),
            P("expert", "batch", None),
        ),
        check_vma=False,
    )
```

```python
from functools import partial

import jax
import jax.numpy as jnp
from jax import lax
from jax.experimental import pallas as pl
from jax.experimental.pallas import tpu as pltpu
from jax.sharding import PartitionSpec as P

HEADS = 24
KV_HEADS = 8
HEAD_DIM = 64
PROMPT = 512
CLEN = 256


EPS = 1e-06
THETA = 10000.0


def product(left, right):
    return jnp.dot(left, right, preferred_element_type=jnp.float32)


def place_of(row_ids):
    return jnp.where(row_ids < PROMPT, row_ids, PROMPT + (row_ids - PROMPT) % CLEN)


def visible(query_ids, key_ids):
    causal = key_ids[None, :] <= query_ids[:, None]
    same_run = (key_ids[None, :] - PROMPT) // CLEN == (query_ids[:, None] - PROMPT) // CLEN
    return causal & ((key_ids[None, :] < PROMPT) | same_run)


def dot_plain(left, right):
    return lax.dot_general(left, right, (((1,), (0,)), ((), ())), preferred_element_type=jnp.float32)


def dot_right(left, right):
    return lax.dot_general(left, right, (((1,), (1,)), ((), ())), preferred_element_type=jnp.float32)


def dot_left(left, right):
    return lax.dot_general(left, right, (((0,), (0,)), ((), ())), preferred_element_type=jnp.float32)


ANYWHERE = pl.BlockSpec(memory_space=pl.ANY)
INSIDE = pl.BlockSpec(memory_space=pltpu.VMEM)
SCALARS = pl.BlockSpec(memory_space=pltpu.SMEM)
VMEM_BYTES = 62 * 1024 * 1024


def cost(flops, *arrays):
    return pl.CostEstimate(flops=1, bytes_accessed=1, transcendentals=0)


def weight_copies(spots, pieces, target, sems):
    copies = []
    for p, piece in enumerate(pieces):
        blocks, rows = piece.shape[0], piece.shape[1]
        for k in range(blocks):
            place = pl.multiple_of(spots[p, k] * rows, rows)
            copies.append(
                pltpu.make_async_copy(
                    piece.at[k], target.at[pl.ds(place, rows)], sems.at[p * blocks + k]
                )
            )
    return copies


def block_copies(blocks, target, sems, first, columns=None):
    copies = []
    start = 0
    for i, block in enumerate(blocks):
        rows = block.shape[0]
        source = block if columns is None else block.at[:, columns]
        copies.append(
            pltpu.make_async_copy(source, target.at[pl.ds(start, rows)], sems.at[first + i])
        )
        start += rows
    return copies


def swap_halves(values):
    half = HEAD_DIM // 2
    lane = lax.broadcasted_iota(jnp.int32, values.shape, 1)
    return jnp.where(
        lane % HEAD_DIM < half,
        pltpu.roll(values, 2 * HEAD_DIM - half, 1),
        pltpu.roll(values, half, 1),
    )


def mean_square_scale(values):
    return lax.rsqrt(jnp.mean(values * values, axis=-1, keepdims=True) + EPS)


def enter_kernel(count, gain_at, spots, tokens, cosine, sine, *refs):
    pieces = refs[:count]
    normed, query, keyval, small, weight, sems = refs[count:]
    low = jnp.bfloat16
    copies = weight_copies(spots, pieces, weight, sems)
    for copy in copies:
        copy.start()
    inputs = tokens[...].astype(jnp.float32)
    scaled = inputs * mean_square_scale(inputs)
    for copy in copies:
        copy.wait()
    query_width = query.shape[1]
    kv_width = keyval.shape[1] // 2
    qkv_width = query_width + 2 * kv_width
    turned = weight[:, qkv_width:].astype(jnp.float32).T
    small[...] = turned
    rows = (scaled * turned[gain_at : gain_at + 1]).astype(low)
    normed[...] = rows
    pair = 2 * HEAD_DIM
    scale = HEAD_DIM**-0.5
    for start in range(0, query_width + kv_width, 512):
        product_part = dot_plain(rows, weight[:, start : start + 512])
        for offset in range(0, 512, pair):
            part = product_part[:, offset : offset + pair]
            part = part * cosine[...] + swap_halves(part) * sine[...]
            at = start + offset
            if at < query_width:
                query[:, at : at + pair] = (part * scale).astype(low)
            else:
                keyval[:, at - query_width : at - query_width + pair] = part.astype(low)
    keyval[:, kv_width:] = dot_plain(
        rows, weight[:, query_width + kv_width : qkv_width]
    ).astype(low)


def enter(tokens, cosine, sine, pieces, spots, gain_at, query_width, kv_width):
    rows, width = tokens.shape
    columns = pieces[0].shape[2]
    low = jnp.bfloat16
    return pl.pallas_call(
        partial(enter_kernel, len(pieces), gain_at),
        in_specs=[SCALARS, INSIDE, INSIDE, INSIDE] + [ANYWHERE] * len(pieces),
        out_specs=[INSIDE] * 4,
        out_shape=[
            jax.ShapeDtypeStruct((rows, width), low),
            jax.ShapeDtypeStruct((rows, query_width), low),
            jax.ShapeDtypeStruct((rows, 2 * kv_width), low),
            jax.ShapeDtypeStruct((columns - query_width - 2 * kv_width, width), jnp.float32),
        ],
        scratch_shapes=[
            pltpu.VMEM((width, columns), low),
            pltpu.SemaphoreType.DMA((len(pieces) * pieces[0].shape[0],)),
        ],
        compiler_params=pltpu.CompilerParams(vmem_limit_bytes=VMEM_BYTES),
        cost_estimate=cost(2 * rows * width * columns, *pieces),
        name="enter",
    )(spots, tokens, cosine, sine, *pieces)


def both_places(values):
    wide = values.astype(jnp.float32)
    low_lane = lax.broadcasted_iota(jnp.int32, values.shape, 1) < HEAD_DIM
    moved = pltpu.roll(wide, HEAD_DIM, 1)
    kind = values.dtype
    return [
        [jnp.where(low_lane, wide, 0.0).astype(kind), jnp.where(low_lane, 0.0, moved).astype(kind)],
        [jnp.where(low_lane, moved, 0.0).astype(kind), jnp.where(low_lane, 0.0, wide).astype(kind)],
    ]


def attend_kernel(query, keyval, bias, attended, log_totals):
    low = jnp.bfloat16
    rows = query.shape[0]
    kv_width = keyval.shape[1] // 2
    pair_lanes = 2 * HEAD_DIM
    repeat = HEADS // KV_HEADS
    log_totals[...] = jnp.zeros_like(log_totals)
    lane = lax.broadcasted_iota(jnp.int32, log_totals.shape, 1)

    @pl.loop(0, KV_HEADS // 2)
    def _(pair):
        at = pl.ds(pl.multiple_of(pair * pair_lanes, pair_lanes), pair_lanes)
        keys = both_places(keyval[:, at])
        at = pl.ds(pl.multiple_of(kv_width + pair * pair_lanes, pair_lanes), pair_lanes)
        values = both_places(keyval[:, at])
        for i in range(repeat):
            at = pl.ds(pl.multiple_of((pair * repeat + i) * pair_lanes, pair_lanes), pair_lanes)
            queries = query[:, at]
            total = jnp.zeros((rows, pair_lanes), jnp.float32)
            for a in range(2):
                head = 2 * i + a
                scores = dot_right(queries, keys[head // repeat][a]) + bias[...]
                peak = jnp.max(scores, axis=-1, keepdims=True)
                lifted = jnp.exp(scores - peak)
                row_total = jnp.sum(lifted, axis=-1, keepdims=True)
                weights_low = (lifted * (1.0 / row_total)).astype(low)
                total += dot_plain(weights_low, values[head // repeat][a])
                log_totals[...] = jnp.where(
                    lane == pair * (2 * repeat) + head, peak + jnp.log(row_total), log_totals[...]
                )
            attended[:, at] = total.astype(low)


def attend(query, keyval, bias):
    rows, query_width = query.shape
    return pl.pallas_call(
        attend_kernel,
        in_specs=[INSIDE] * 3,
        out_specs=[INSIDE] * 2,
        out_shape=[
            jax.ShapeDtypeStruct((rows, query_width), jnp.bfloat16),
            jax.ShapeDtypeStruct((rows, 128), jnp.float32),
        ],
        compiler_params=pltpu.CompilerParams(vmem_limit_bytes=VMEM_BYTES),
        cost_estimate=cost(8 * rows * query_width * bias.shape[1], query, keyval, bias),
        name="attend",
    )(query, keyval, bias)


def project_kernel(count, gain_at, spots, attended, tokens, small, member, kept, *refs):
    pieces = refs[:count]
    residual, sent, gate_rows, weight, sems = refs[count:]
    low = jnp.bfloat16
    width = tokens.shape[1]
    copies = weight_copies(spots, pieces, weight, sems)
    for copy in copies:
        copy.start()
    for copy in copies:
        copy.wait()
    hidden = tokens[...].astype(jnp.float32) + dot_plain(attended[...], weight[...])
    residual[...] = hidden
    gain = small[gain_at : gain_at + 1, :]
    normed = (hidden * mean_square_scale(hidden) * gain).astype(low)
    logits = dot_right(normed, small[...].astype(low))
    chosen = member[...] > 0.0
    logits = jnp.where(chosen, logits, -1e30)
    lifted = jnp.where(chosen, jnp.exp(logits - jnp.max(logits, axis=-1, keepdims=True)), 0.0)
    gates = lifted / jnp.sum(lifted, axis=-1, keepdims=True)
    gate_rows[...] = gates
    sent[:, :width] = normed
    sent[:, width:] = (gates * kept[...]).astype(low)


def project(attended, tokens, small, member, kept, gain_at, pieces, spots):
    rows, width = tokens.shape
    lanes = small.shape[0]
    low = jnp.bfloat16
    return pl.pallas_call(
        partial(project_kernel, len(pieces), gain_at),
        in_specs=[SCALARS] + [INSIDE] * 5 + [ANYWHERE] * len(pieces),
        out_specs=[INSIDE] * 3,
        out_shape=[
            jax.ShapeDtypeStruct((rows, width), jnp.float32),
            jax.ShapeDtypeStruct((rows, width + lanes), low),
            jax.ShapeDtypeStruct((rows, lanes), jnp.float32),
        ],
        scratch_shapes=[
            pltpu.VMEM((attended.shape[1], width), low),
            pltpu.SemaphoreType.DMA((len(pieces) * pieces[0].shape[0],)),
        ],
        compiler_params=pltpu.CompilerParams(vmem_limit_bytes=VMEM_BYTES),
        cost_estimate=cost(2 * rows * width * width, *pieces),
        name="project",
    )(spots, attended, tokens, small, member, kept, *pieces)


def grad_shapes(cut, rows, columns):
    low = jnp.bfloat16
    if cut:
        block = rows // 32
        return (
            [jax.ShapeDtypeStruct((4, 4, block, columns), low)] * 2,
            pltpu.VMEM((4, 2, 4, block, columns), low),
        )
    return (
        [jax.ShapeDtypeStruct((1, 1, 1, rows, columns), low)],
        pltpu.VMEM((1, 1, 1, rows, columns), low),
    )


def grad_copies(cut, place, source, outs, sems):
    if not cut:
        return [pltpu.make_async_copy(source, outs[0], sems.at[0])]
    core, member = place[0], place[1]
    other, own = outs
    copies = []
    for r in range(4):
        copies.append(
            pltpu.make_async_copy(
                source.at[:, 1 - core, member ^ r], other.at[r], sems.at[2 * r]
            )
        )
        copies.append(
            pltpu.make_async_copy(source.at[:, core, member ^ r], own.at[r], sems.at[2 * r + 1])
        )
    return copies


def turn_kernel(
    count,
    cut,
    gain_at,
    place,
    spots,
    normed_grad,
    residual,
    grad_out,
    small,
    gate_rows,
    member,
    kept,
    normed,
    attended,
    *refs,
):
    pieces = refs[:count]
    refs = refs[count:]
    outs = refs[: (2 if cut else 1)]
    resid_grad, head_grad, weight, weight_grad, sems, out_sems = refs[len(outs) :]
    low = jnp.bfloat16
    rows, width = residual.shape
    lanes = gate_rows.shape[1]
    copies = weight_copies(spots, pieces, weight, sems)
    for copy in copies:
        copy.start()
    lane = lax.broadcasted_iota(jnp.int32, (rows, lanes), 1)
    gates = gate_rows[...]
    gate_grads = normed_grad[:, width:] * kept[...]
    chosen_grad = gates * (gate_grads - jnp.sum(gates * gate_grads, axis=-1, keepdims=True))
    logit_grad = (chosen_grad * member[...]).astype(low)
    hidden = residual[...]
    scale = mean_square_scale(hidden)
    row_grad = normed_grad[:, :width] + dot_plain(logit_grad, small[...].astype(low))
    gain = small[gain_at : gain_at + 1, :]
    scaled = row_grad * gain
    total_grad = (
        grad_out[...].astype(jnp.float32)
        + scale * scaled
        - hidden * (scale * scale * scale) * jnp.mean(scaled * hidden, axis=-1, keepdims=True)
    )
    resid_grad[...] = total_grad
    attn_grad = total_grad.astype(low)
    shape = weight_grad.shape[:-1]
    gain_grad = (row_grad * hidden * scale).astype(low)
    picks = jnp.where(lane == gain_at, 1.0, 0.0).astype(low)
    weight_grad[..., width:] = (
        (dot_left(normed[...][:, :width], logit_grad) + dot_left(gain_grad, picks))
        .astype(low)
        .reshape(shape + (lanes,))
    )
    for start in range(0, width, 512):
        weight_grad[..., start : start + 512] = (
            dot_left(attended[...], attn_grad[:, start : start + 512])
            .astype(low)
            .reshape(shape + (512,))
        )
    out_copies = grad_copies(cut, place, weight_grad, outs, out_sems)
    for copy in out_copies:
        copy.start()
    for copy in copies:
        copy.wait()
    head_grad[...] = dot_right(attn_grad, weight[...]).astype(low)
    for copy in out_copies:
        copy.wait()


def turn(place, spots, operands, pieces, cut, gain_at):
    residual, gate_rows, attended = operands[1], operands[4], operands[8]
    rows, width = residual.shape
    query_width = attended.shape[1]
    low = jnp.bfloat16
    grads, held = grad_shapes(cut, query_width, width + gate_rows.shape[1])
    return pl.pallas_call(
        partial(turn_kernel, len(pieces), cut, gain_at),
        in_specs=[SCALARS, SCALARS] + [INSIDE] * len(operands) + [ANYWHERE] * len(pieces),
        out_specs=[ANYWHERE] * len(grads) + [INSIDE] * 2,
        out_shape=grads
        + [
            jax.ShapeDtypeStruct((rows, width), jnp.float32),
            jax.ShapeDtypeStruct((rows, query_width), low),
        ],
        scratch_shapes=[
            pltpu.VMEM((query_width, width), low),
            held,
            pltpu.SemaphoreType.DMA((len(pieces) * pieces[0].shape[0],)),
            pltpu.SemaphoreType.DMA((8,)),
        ],
        compiler_params=pltpu.CompilerParams(vmem_limit_bytes=VMEM_BYTES),
        cost_estimate=cost(0),
        name="turn",
    )(place, spots, *operands, *pieces)


def attend_back_kernel(
    head_grad, query, keyval, bias, log_totals, cosine, sine, query_grad, keyval_grad, totals
):
    low = jnp.bfloat16
    rows = query.shape[0]
    kv_width = keyval.shape[1] // 2
    pair_lanes = 2 * HEAD_DIM
    repeat = HEADS // KV_HEADS
    totals[...] = log_totals[...].T

    @pl.loop(0, KV_HEADS // 2)
    def _(pair):
        key_at = pl.ds(pl.multiple_of(pair * pair_lanes, pair_lanes), pair_lanes)
        value_at = pl.ds(pl.multiple_of(kv_width + pair * pair_lanes, pair_lanes), pair_lanes)
        keys = both_places(keyval[:, key_at])
        values = both_places(keyval[:, value_at])
        key_grads = [[None, None], [None, None]]
        value_grads = [[None, None], [None, None]]
        for i in range(repeat):
            at = pl.ds(pl.multiple_of((pair * repeat + i) * pair_lanes, pair_lanes), pair_lanes)
            queries = query[:, at]
            grads = head_grad[:, at]
            query_part = jnp.zeros((rows, pair_lanes), jnp.float32)
            for a in range(2):
                head = 2 * i + a
                g = head // repeat
                total = totals[pl.ds(pair * (2 * repeat) + head, 1), :]
                weights = jnp.exp(dot_right(keys[g][a], queries) + bias[...] - total)
                weight_grads = dot_right(values[g][a], grads)
                delta = jnp.sum(weights * weight_grads, axis=0, keepdims=True)
                score_grads = (weights * (weight_grads - delta)).astype(low)
                value_part = dot_plain(weights.astype(low), grads)
                key_part = dot_plain(score_grads, queries)
                query_part += dot_left(score_grads, keys[g][a])
                if key_grads[g][a] is None:
                    key_grads[g][a], value_grads[g][a] = key_part, value_part
                else:
                    key_grads[g][a] += key_part
                    value_grads[g][a] += value_part
            query_part = query_part * (HEAD_DIM**-0.5)
            query_part = query_part * cosine[...] - swap_halves(query_part) * sine[...]
            query_grad[:, at] = query_part.astype(low)
        low_lane = lax.broadcasted_iota(jnp.int32, (keyval.shape[0], pair_lanes), 1) < HEAD_DIM
        for at, found in ((key_at, key_grads), (value_at, value_grads)):
            keyval_grad[:, at] = jnp.where(
                low_lane,
                found[0][0] + pltpu.roll(found[0][1], HEAD_DIM, 1),
                pltpu.roll(found[1][0], HEAD_DIM, 1) + found[1][1],
            ).astype(low)


def attend_back(head_grad, query, keyval, bias, log_totals, cosine, sine):
    rows, query_width = query.shape
    low = jnp.bfloat16
    return pl.pallas_call(
        attend_back_kernel,
        in_specs=[INSIDE] * 7,
        out_specs=[INSIDE] * 2,
        out_shape=[
            jax.ShapeDtypeStruct((rows, query_width), low),
            jax.ShapeDtypeStruct(keyval.shape, low),
        ],
        scratch_shapes=[pltpu.VMEM((128, rows), jnp.float32)],
        compiler_params=pltpu.CompilerParams(vmem_limit_bytes=VMEM_BYTES),
        cost_estimate=cost(0),
        name="attend_back",
    )(head_grad, query, keyval, bias, log_totals, cosine, sine)


def leave_kernel(
    count,
    cut,
    gain_at,
    place,
    spots,
    keyval_sum,
    query_grad,
    normed,
    tokens,
    resid_grad,
    small,
    cosine,
    sine,
    *refs,
):
    pieces = refs[:count]
    refs = refs[count:]
    outs = refs[: (2 if cut else 1)]
    input_grad, weight, weight_grad, joined, sems, out_sems = refs[len(outs) :]
    low = jnp.bfloat16
    rows, width = tokens.shape
    query_width = query_grad.shape[1]
    kv_width = keyval_sum.shape[1] // 2
    qkv_width = query_width + 2 * kv_width
    pair = 2 * HEAD_DIM
    copies = weight_copies(spots, pieces, weight, sems)
    for copy in copies:
        copy.start()
    joined[:, :query_width] = query_grad[...]
    for start in range(0, kv_width, pair):
        part = keyval_sum[:, start : start + pair]
        part = part * cosine[...] - swap_halves(part) * sine[...]
        joined[:, query_width + start : query_width + start + pair] = part.astype(low)
    joined[:, query_width + kv_width :] = keyval_sum[:, kv_width:].astype(low)
    shape = weight_grad.shape[:-1]
    for start in range(0, qkv_width, 512):
        weight_grad[..., start : start + 512] = (
            dot_left(normed[...], joined[:, start : start + 512]).astype(low).reshape(shape + (512,))
        )
    for copy in copies:
        copy.wait()
    row_grad = dot_right(joined[...], weight[:, :qkv_width])
    inputs = tokens[...].astype(jnp.float32)
    scale = mean_square_scale(inputs)
    lanes = weight_grad.shape[-1] - qkv_width
    lane = lax.broadcasted_iota(jnp.int32, (rows, lanes), 1)
    picks = jnp.where(lane == gain_at, 1.0, 0.0).astype(low)
    weight_grad[..., qkv_width:] = (
        dot_left((row_grad * inputs * scale).astype(low), picks).astype(low).reshape(shape + (lanes,))
    )
    out_copies = grad_copies(cut, place, weight_grad, outs, out_sems)
    for copy in out_copies:
        copy.start()
    scaled = row_grad * small[gain_at : gain_at + 1, :]
    input_grad[...] = (
        resid_grad[...]
        + scale * scaled
        - inputs * (scale * scale * scale) * jnp.mean(scaled * inputs, axis=-1, keepdims=True)
    )
    for copy in out_copies:
        copy.wait()


def leave(place, spots, operands, pieces, cut, gain_at):
    tokens, query_grad, keyval_sum = operands[3], operands[1], operands[0]
    rows, width = tokens.shape
    columns = pieces[0].shape[2]
    low = jnp.bfloat16
    grads, held = grad_shapes(cut, width, columns)
    return pl.pallas_call(
        partial(leave_kernel, len(pieces), cut, gain_at),
        in_specs=[SCALARS, SCALARS] + [INSIDE] * len(operands) + [ANYWHERE] * len(pieces),
        out_specs=[ANYWHERE] * len(grads) + [INSIDE],
        out_shape=grads + [jax.ShapeDtypeStruct((rows, width), jnp.float32)],
        scratch_shapes=[
            pltpu.VMEM((width, columns), low),
            held,
            pltpu.VMEM((rows, query_grad.shape[1] + keyval_sum.shape[1]), low),
            pltpu.SemaphoreType.DMA((len(pieces) * pieces[0].shape[0],)),
            pltpu.SemaphoreType.DMA((8,)),
        ],
        compiler_params=pltpu.CompilerParams(vmem_limit_bytes=VMEM_BYTES),
        cost_estimate=cost(0),
        name="leave",
    )(place, spots, *operands, *pieces)


def expert_kernel(cut, carried, last, row_blocks, grad_blocks, row_tile, place, first, packed, *refs):
    blocks_in = refs[:row_blocks]
    grads_in = refs[row_blocks : row_blocks + grad_blocks]
    refs = refs[row_blocks + grad_blocks :]
    if carried:
        mix_in, turn_in = refs[:2]
        refs = refs[2:]
    count = packed.shape[2]
    outs = 4 if cut else 1
    packed_grads = refs[:outs]
    mix_out, turn_out = refs[outs : outs + 2]
    refs = refs[outs + 2 :]
    if last:
        mix, turned = refs[:2]
        refs = refs[2:]
    else:
        mix, turned = mix_out, turn_out
    (
        rows,
        grads,
        gates,
        gate_w,
        up_w,
        down_w,
        gate_g,
        up_g,
        down_g,
        weighted,
        gate_side,
        up_side,
        load_sems,
        save_sems,
        carry_sems,
    ) = refs
    hidden_width = gate_w.shape[-1]
    total_rows, width = rows.shape
    lanes = gates.shape[1]
    low = jnp.bfloat16

    def sides(gate, up, down):
        for side, inner in ((0, gate), (1, up)):
            for j in range(3):
                yield side, pl.ds(j * hidden_width, hidden_width), inner, j
        yield 2, pl.ds(0, width), down, None

    def loads(e):
        slot = e % 2
        copies = []
        for i, (side, columns, inner, j) in enumerate(sides(gate_w, up_w, down_w)):
            outer = packed.at[:, side, e, :, columns]
            inner = inner.at[slot] if j is None else inner.at[slot, :, j]
            copies.append(pltpu.make_async_copy(outer, inner, load_sems.at[slot, i]))
        return copies

    def saves(e):
        slot = e % 2
        copies = []
        for i, (side, columns, inner, j) in enumerate(sides(gate_g, up_g, down_g)):
            if not cut:
                outer = packed_grads[0].at[:, side, e, :, columns]
                source = inner.at[slot] if j is None else inner.at[slot, :, j]
                copies.append(pltpu.make_async_copy(source, outer, save_sems.at[slot, i]))
                continue
            own, rest, far, near = packed_grads
            targets = [own, rest.at[0], rest.at[1], rest.at[2]]
            targets += [near.at[1], near.at[0], far.at[0], far.at[1]]
            for n, target in enumerate(targets):
                block = 2 * lax.rem(place[2] + n % 4, 4) + (place[0] ^ (n // 4))
                source = inner.at[slot, block] if j is None else inner.at[slot, block, j]
                outer = target.at[side, e, :, columns]
                copies.append(pltpu.make_async_copy(source, outer, save_sems.at[slot, 8 * i + n]))
        return copies

    carries = (
        block_copies(grads_in, grads, carry_sems, 0, pl.ds(0, width))
        + block_copies(blocks_in, rows, carry_sems, grad_blocks, pl.ds(0, width))
        + block_copies(
            blocks_in, gates, carry_sems, grad_blocks + row_blocks, pl.ds(width, lanes)
        )
    )
    sums = []
    if carried:
        at = grad_blocks + 2 * row_blocks
        sums = [
            pltpu.make_async_copy(mix_in, mix, carry_sems.at[at]),
            pltpu.make_async_copy(turn_in, turned, carry_sems.at[at + 1]),
        ]
    for copy in loads(0) + carries + sums:
        copy.start()
    for e in range(count):
        slot = e % 2
        if e + 1 < count:
            for copy in loads(e + 1):
                copy.start()
        for copy in loads(e):
            copy.wait()
        if e == 0:
            for copy in carries:
                copy.wait()
            if not carried:
                turned[:, width:] = jnp.zeros((total_rows, lanes), jnp.float32)

        @pl.loop(0, total_rows // row_tile)
        def _(tile):
            span = pl.ds(pl.multiple_of(tile * row_tile, row_tile), row_tile)
            gate_full = gate_w[slot].reshape(width, hidden_width)
            up_full = up_w[slot].reshape(width, hidden_width)
            down_full = down_w[slot].reshape(hidden_width, width)
            here = rows[span, :]
            slope = dot_right(grads[span, :], down_full)
            gate_pre = dot_plain(here, gate_full)
            up_pre = dot_plain(here, up_full)
            lane = lax.broadcasted_iota(jnp.int32, (row_tile, lanes), 1)
            chosen = lane == first[0] + e
            gate_column = jnp.sum(
                jnp.where(chosen, gates[span, :].astype(jnp.float32), 0.0), axis=1, keepdims=True
            )
            sigmoid_gate = jax.nn.sigmoid(gate_pre)
            activated = gate_pre * sigmoid_gate
            hidden = (activated * up_pre).astype(low).astype(jnp.float32)
            share = jnp.sum(hidden * slope, axis=1, keepdims=True)
            if e == 0 and sums:

                @pl.when(tile == 0)
                def _():
                    for copy in sums:
                        copy.wait()

            turned[span, width:] = jnp.where(chosen, share, turned[span, width:])
            part_weighted = (hidden * gate_column).astype(low)
            hidden_grad = slope * gate_column
            part_gate = (
                hidden_grad * up_pre * (sigmoid_gate + activated * (1.0 - sigmoid_gate))
            ).astype(low)
            part_up = (hidden_grad * activated).astype(low)
            weighted[span, :] = part_weighted
            gate_side[span, :] = part_gate
            up_side[span, :] = part_up
            mix_part = dot_plain(part_weighted, down_full)
            turn_part = dot_right(part_gate, gate_full) + dot_right(part_up, up_full)
            if e == 0 and not carried:
                mix[span, :] = mix_part
                turned[span, :width] = turn_part
            elif last and e == count - 1:
                mix_out[span, :] = (mix[span, :] + mix_part).astype(low)
                turn_out[span, :width] = (turned[span, :width] + turn_part).astype(low)
                turn_out[span, width:] = turned[span, width:].astype(low)
            else:
                mix[span, :] += mix_part
                turned[span, :width] += turn_part

        if e >= 2:
            for copy in saves(e - 2):
                copy.wait()
        down_g[slot] = dot_left(weighted[...], grads[...]).astype(low).reshape(down_g.shape[1:])
        gate_g[slot] = dot_left(rows[...], gate_side[...]).astype(low).reshape(gate_g.shape[1:])
        up_g[slot] = dot_left(rows[...], up_side[...]).astype(low).reshape(up_g.shape[1:])
        for copy in saves(e):
            copy.start()
    for e in range(max(0, count - 2), count):
        for copy in saves(e):
            copy.wait()


def expert_pass(place, first, rows, grads, packed, carry, cut, last):
    blocks, _, count, part, width = packed.shape
    hidden_width = blocks * part
    total_rows = sum(block.shape[0] for block in rows)
    lanes = rows[0].shape[1] - width
    low = jnp.bfloat16
    wide = jnp.float32
    carried = carry is not None
    flops = 18 * total_rows * count * hidden_width * width
    side = pltpu.VMEM((2, blocks, 3, part, hidden_width), low)
    sides = [side, side, pltpu.VMEM((2, blocks, part, width), low)]
    sums = [(total_rows, width), (total_rows, width + lanes)]
    one = packed.shape[1:]
    grads_out = [one, (3,) + one, (2,) + one, (2,) + one] if cut else [packed.shape]
    outs = len(grads_out)
    found = pl.pallas_call(
        partial(expert_kernel, cut, carried, last, len(rows), len(grads), min(512, total_rows)),
        in_specs=[SCALARS, SCALARS]
        + [ANYWHERE] * (1 + len(rows) + len(grads) + (2 if carried else 0)),
        out_specs=[ANYWHERE] * outs + [INSIDE, INSIDE],
        out_shape=[jax.ShapeDtypeStruct(shape, low) for shape in grads_out]
        + [jax.ShapeDtypeStruct(shape, low if last else wide) for shape in sums],
        scratch_shapes=([pltpu.VMEM(shape, wide) for shape in sums] if last else [])
        + [
            pltpu.VMEM((total_rows, width), low),
            pltpu.VMEM((total_rows, width), low),
            pltpu.VMEM((total_rows, lanes), low),
        ]
        + sides
        + sides
        + [pltpu.VMEM((total_rows, hidden_width), low)] * 3
        + [
            pltpu.SemaphoreType.DMA((2, 7)),
            pltpu.SemaphoreType.DMA((2, 56)),
            pltpu.SemaphoreType.DMA((2 * len(rows) + len(grads) + 2,)),
        ],
        compiler_params=pltpu.CompilerParams(vmem_limit_bytes=VMEM_BYTES),
        cost_estimate=cost(flops, packed, packed, *rows, *grads),
        name="experts",
    )(place, first, packed, *rows, *grads, *(carry or ()))
    return found[:outs], found[outs], found[outs + 1]


def unpack_kernel(counts, places, *refs):
    found, (gate, up, down) = refs[:-3], refs[-3:]
    found = [array if place is None else array.at[place] for array, place in zip(found, places)]
    hidden_width = gate.shape[2]
    base = 0
    at = 0
    for terms in counts:
        parts = found[at : at + terms]
        at += terms
        count, part = parts[0].shape[1], parts[0].shape[2]
        for e in range(count):
            for side in range(3):
                total = parts[0][side, e].astype(jnp.float32)
                for other in parts[1:]:
                    total += other[side, e].astype(jnp.float32)
                if side == 2:
                    down[base + e] = total
                    continue
                for j in range(3):
                    (gate, up)[side][base + e, j * part : (j + 1) * part, :] = total[
                        :, j * hidden_width : (j + 1) * hidden_width
                    ]
        base += count


def unpack(chunks, gate_shape, down_shape):
    arrays = [array for terms in chunks for array, _ in terms]
    places = [place for terms in chunks for _, place in terms]
    return pl.pallas_call(
        partial(unpack_kernel, [len(terms) for terms in chunks], places),
        in_specs=[INSIDE] * len(arrays),
        out_specs=[INSIDE] * 3,
        out_shape=[
            jax.ShapeDtypeStruct(gate_shape, jnp.float32),
            jax.ShapeDtypeStruct(gate_shape, jnp.float32),
            jax.ShapeDtypeStruct(down_shape, jnp.float32),
        ],
        compiler_params=pltpu.CompilerParams(vmem_limit_bytes=VMEM_BYTES),
        cost_estimate=cost(0),
        name="unpack",
    )(*arrays)


def cube():
    return lax.axis_size("batch") == 8 and lax.axis_size("expert") == 4


def pair_moves(size, flip):
    return [(i, i ^ flip) for i in range(size)]


def shift_moves(step):
    return [(2 * z + c, 2 * ((z + step) % 4) + c) for z in range(4) for c in range(2)]


def gather_start(rows):
    size = lax.axis_size("expert")
    if size != 4:
        stacked = lax.all_gather(rows, "expert", axis=0)
        own = lax.axis_index("expert")
        return [
            lax.dynamic_index_in_dim(stacked, own ^ r, axis=0, keepdims=False) for r in range(size)
        ]
    return [rows] + [lax.ppermute(rows, "expert", pair_moves(4, r)) for r in (1, 2)]


def gather_finish(state, events=()):
    if lax.axis_size("expert") != 4:
        return state
    first, second = after(state[1:], events)
    half = first.shape[0] // 2
    top = lax.ppermute(second[:half], "expert", pair_moves(4, 1))
    bottom = lax.ppermute(first[half:], "expert", pair_moves(4, 2))
    return state + [top, bottom]


def gather_blocks(rows):
    return gather_finish(gather_start(rows))


def scatter_start(parts):
    low = jnp.bfloat16
    if lax.axis_size("expert") != 4:
        own = lax.axis_index("expert")
        order = jnp.arange(len(parts), dtype=jnp.int32) ^ own
        stacked = jnp.take(jnp.stack(parts), order, axis=0).astype(low)
        return [lax.psum_scatter(stacked, "expert", scatter_dimension=0).astype(jnp.float32)]
    across, along = pair_moves(4, 1), pair_moves(4, 2)
    half = parts[0].shape[0] // 2
    top = lax.ppermute(parts[3][:half].astype(low), "expert", across)
    bottom = lax.ppermute(parts[3][half:].astype(low), "expert", along)
    first_top = lax.ppermute(parts[1][:half].astype(low), "expert", across)
    second_bottom = lax.ppermute(parts[2][half:].astype(low), "expert", along)
    for_first = add_low(parts[1][half:], bottom)
    for_second = add_low(parts[2][:half], top)
    return [parts[0], first_top, second_bottom, for_first, for_second]


def scatter_finish(state):
    if len(state) == 1:
        return state[0]
    own, first_top, second_bottom, for_first, for_second = state
    half = first_top.shape[0]
    second_top = lax.ppermute(for_second, "expert", pair_moves(4, 2))
    first_bottom = lax.ppermute(for_first, "expert", pair_moves(4, 1))
    return jnp.concatenate(
        [
            total_of([own[:half], first_top, second_top]),
            total_of([own[half:], first_bottom, second_bottom]),
        ],
        axis=0,
    )


def scatter_blocks(parts):
    return scatter_finish(scatter_start(parts))


def after(values, events):
    return lax.optimization_barrier((values, events))[0]


def send_parts(parts):
    if lax.axis_size("expert") != 4:
        return [scatter_blocks(parts)]
    low = jnp.bfloat16
    return [parts[0]] + [
        lax.ppermute(parts[r].astype(low), "expert", pair_moves(4, r)) for r in range(1, 4)
    ]


def total_of(parts):
    total = parts[0].astype(jnp.float32)
    for part in parts[1:]:
        total += part.astype(jnp.float32)
    return total


def shift_dense(rows, events):
    if not cube():
        return [lax.all_gather(rows, ("batch", "expert"), axis=0, tiled=True)]
    below, above = step_up(rows), step_down(rows)
    return [rows, below, step_up(after(below, (above, events))), above]


def dense_start(line, columns, events):
    found = [rows[:, columns] for rows in line]
    if not cube():
        return [found[0][None]]
    return gather_start(after(jnp.stack(found), events))


def dense_finish(state, events=(), late=()):
    if not cube():
        return state, jnp.zeros((1, 1), jnp.int32), ()
    place = lax.axis_index("batch")
    level, core = place // 2, place % 2
    member = lax.axis_index("expert")
    mine = gather_finish(state, events)
    far = mine[3:]
    mine = mine[:3] + [after(jnp.concatenate(far, axis=0), late)]
    other = [exchange_cores(block) for block in mine]
    spots = [
        [(((level + 4 - k) % 4) * 2 + (core ^ c)) * 4 + (member ^ r) for k in range(4)]
        for c in range(2)
        for r in range(4)
    ]
    return mine + other, jnp.array(spots, jnp.int32), far


def sum_chunk(packed_grad):
    return lax.psum_scatter(packed_grad, "batch", scatter_dimension=0, tiled=True)


def exchange_cores(values):
    return lax.ppermute(values, "batch", pair_moves(8, 1))


def step_up(values):
    return lax.ppermute(values, "batch", shift_moves(1))


def step_down(values):
    return lax.ppermute(values, "batch", shift_moves(3))


def add_low(*parts):
    total = parts[0].astype(jnp.float32)
    for part in parts[1:]:
        total += part.astype(jnp.float32)
    return total.astype(jnp.bfloat16)


def join_cores(own, received):
    return [add_low(own[r], received[r]) for r in range(4)]


def line_start(plane):
    level = lax.axis_index("batch") // 2
    own, up, far, down = (
        lax.dynamic_index_in_dim(plane, (level + r) % 4, axis=0, keepdims=False) for r in range(4)
    )
    return own, step_down(add_low(down)), add_low(up, step_up(add_low(far)))


def line_finish(state, events=()):
    own, down, up = state
    return total_of([own, down, step_up(after(up, events))])


def scatter_whole(found):
    values = found[0].reshape(found[0].shape[3:])
    total = lax.psum_scatter(values, ("batch", "expert"), scatter_dimension=0, tiled=True)
    return total.astype(jnp.float32)


def pack_kernel(chunks, query, key, value, small, out, gate, up, down, dense, *packed):
    start = 0
    for part in (query, key, value, small, out):
        dense[:, start : start + part.shape[1]] = part[...]
        start += part.shape[1]
    part, hidden_width = down.shape[1], gate.shape[2]
    for n, target in enumerate(packed):
        for e in range(chunks[n], chunks[n + 1]):
            for side, source in ((0, gate), (1, up)):
                for j in range(3):
                    target[side, e - chunks[n], :, j * hidden_width : (j + 1) * hidden_width] = (
                        source[e, j * part : (j + 1) * part, :]
                    )
            target[2, e - chunks[n]] = down[e]


def pack(chunks, query, key, value, small, out, gate, up, down):
    low = jnp.bfloat16
    columns = sum(part.shape[1] for part in (query, key, value, small, out))
    return pl.pallas_call(
        partial(pack_kernel, chunks),
        in_specs=[INSIDE] * 8,
        out_specs=[INSIDE] * len(chunks),
        out_shape=[jax.ShapeDtypeStruct((query.shape[0], columns), low)]
        + [
            jax.ShapeDtypeStruct((3, b - a) + down.shape[1:], low)
            for a, b in zip(chunks[:-1], chunks[1:])
        ],
        compiler_params=pltpu.CompilerParams(vmem_limit_bytes=VMEM_BYTES),
        cost_estimate=cost(0),
        name="pack",
    )(query, key, value, small, out, gate, up, down)


def local(
    tokens,
    cotangent,
    attn_gain,
    query_weight,
    key_weight,
    value_weight,
    out_weight,
    ffn_gain,
    router_weight,
    gate_weight,
    up_weight,
    down_weight,
    routes,
    ranking,
):
    low = jnp.bfloat16
    wide = jnp.float32
    query_width = HEADS * HEAD_DIM
    kv_width = KV_HEADS * HEAD_DIM
    qkv_width = query_width + 2 * kv_width
    width = tokens.shape[2]
    experts_total = router_weight.shape[1]
    extra = -(-(experts_total + 2) // 128) * 128
    first_gain, second_gain = experts_total, experts_total + 1
    local_experts = gate_weight.shape[0]
    member_count = lax.axis_size("expert")
    member_id = lax.axis_index("expert")
    local_rows = tokens.shape[1]
    group_rows = local_rows * member_count
    cut = cube()
    line_place = lax.axis_index("batch")
    place = jnp.stack([line_place % 2, member_id, line_place // 2]).astype(jnp.int32)

    route_rows = routes[0]
    rank_rows = ranking[0]
    expert_lanes = jnp.arange(extra, dtype=jnp.int32)
    member = jnp.any(route_rows[:, :, None] == expert_lanes[None, None, :], axis=1)
    marks = jnp.where(
        expert_lanes[None, :] == experts_total,
        (rank_rows // 32)[:, None],
        jnp.where(expert_lanes[None, :] == experts_total + 1, (rank_rows % 32)[:, None], member),
    ).astype(low)
    grad_out = cotangent[0]
    small_width = qkv_width + extra
    chunks = (0, 3, local_experts)
    dense_rows, *packed_own = pack(
        chunks,
        query_weight,
        key_weight,
        value_weight,
        jnp.concatenate(
            [
                router_weight,
                attn_gain[:, None],
                ffn_gain[:, None],
                jnp.zeros((query_weight.shape[0], extra - experts_total - 2), low),
            ],
            axis=1,
        ),
        out_weight,
        gate_weight,
        up_weight,
        down_weight,
    )
    row_ids = member_id * local_rows + jnp.arange(local_rows, dtype=jnp.int32)
    half_dim = HEAD_DIM // 2
    frequency = THETA ** (-jnp.arange(half_dim, dtype=wide) / half_dim)
    angles = place_of(row_ids).astype(wide)[:, None] * frequency[None, :]
    cosine = jnp.tile(jnp.cos(angles), (1, 4))
    sine_part = jnp.tile(jnp.concatenate([-jnp.sin(angles), jnp.sin(angles)], axis=1), (1, 2))
    if member_count == 4:
        away = 1 << 20
        starts = [
            jnp.where(member_id >= 1, 0, away),
            jnp.where(member_id >= 2, local_rows, away),
            member_id * local_rows,
        ]
    else:
        starts = [(member_id ^ r) * local_rows for r in range(member_count)]
    key_ids = jnp.concatenate([s + jnp.arange(local_rows, dtype=jnp.int32) for s in starts])
    bias = jnp.where(visible(row_ids, key_ids), 0.0, -1e30).astype(wide)
    bias_turned = bias.T
    tables = (cosine, sine_part, bias, bias_turned)

    line = shift_dense(dense_rows, tables)
    grad_state = gather_start(jnp.concatenate([grad_out, marks], axis=1))
    grad_blocks = gather_finish(grad_state, line[1::2])
    marks_all = jnp.concatenate([block[:, width:] for block in grad_blocks], axis=0)
    qkv_state = dense_start(line, slice(0, small_width), ())
    plane = qkv_state[1:]
    qkv_pieces, qkv_spots, far = dense_finish(qkv_state)
    out_state = dense_start(line, slice(small_width, None), far)
    packed_all = [
        lax.all_gather(after(packed, events), "batch", axis=0)
        for packed, events in zip(packed_own, ((line, grad_blocks), plane))
    ]

    normed, query, keyval, small = enter(
        tokens[0], cosine, sine_part, qkv_pieces, qkv_spots, first_gain, query_width, kv_width
    )

    rank_all = (
        marks_all[:, experts_total].astype(wide) * 32 + marks_all[:, experts_total + 1].astype(wide)
    )
    earlier = (rank_all[None, :] < rank_rows.astype(wide)[:, None]).astype(low)
    before = product(earlier, marks_all)
    capacity = 5 * group_rows * route_rows.shape[1] // (4 * experts_total)
    member = member.astype(wide)
    kept = jnp.where(before < capacity, member, 0.0)

    keyval_blocks = gather_blocks(after(keyval, out_state[1:]))
    if member_count == 4:
        ordered = keyval_blocks[:3] + [jnp.concatenate(keyval_blocks[3:], axis=0)]
        keys = jnp.concatenate(
            [
                lax.select_n(member_id, *ordered),
                lax.select_n(member_id ^ 1, *ordered),
                keyval,
            ],
            axis=0,
        )
    else:
        keys = jnp.concatenate(keyval_blocks, axis=0)
    attended, log_totals = attend(query, keys, bias)
    out_pieces, out_spots, _ = dense_finish(out_state, keyval_blocks[3:], attended)
    residual, sent, gate_rows = project(
        attended, tokens[0], small, member, kept, second_gain, out_pieces, out_spots
    )
    sent_blocks = gather_blocks(sent)

    carry, chunk_grads = None, []
    for packed, a, b in zip(packed_all, chunks[:-1], chunks[1:]):
        first = (member_id * local_experts + a).astype(jnp.int32).reshape(1)
        packed_grads, mixture_all, row_grad = expert_pass(
            place,
            first,
            sent_blocks,
            grad_blocks,
            packed,
            carry,
            cut and b == local_experts,
            b == local_experts,
        )
        carry = (mixture_all, row_grad)
        chunk_grads.append(packed_grads)

    def blocks_of(values):
        return [values[r * local_rows : (r + 1) * local_rows] for r in range(member_count)]

    totals = [sum_chunk(chunk_grads[0][0])]
    if cut:
        own, rest, far, near = chunk_grads[1]
        far, near = exchange_cores(far), exchange_cores(near)
        far_sum, down_sum = add_low(rest[1], far[0]), add_low(rest[2], far[1])
    turn_state = scatter_start(blocks_of(row_grad))
    if cut:
        turn_state = after(turn_state, (far_sum, down_sum, near))
    normed_grad = scatter_finish(turn_state)
    turned = turn(
        place,
        out_spots,
        (
            normed_grad,
            residual,
            grad_out,
            small,
            gate_rows,
            member,
            kept,
            sent,
            attended,
        ),
        out_pieces,
        cut,
        second_gain,
    )
    out_found = turned[:-2]
    resid_grad, head_grad = turned[-2:]
    mixture_parts = send_parts(blocks_of(after(mixture_all, normed_grad)))
    if cut:
        up_sum = add_low(rest[0], near[0], step_up(far_sum))
    query_grad, key_grads = attend_back(
        head_grad, query, keys, bias_turned, log_totals, cosine, sine_part
    )
    if member_count == 4:
        zero = jnp.zeros((), low)
        for_first, for_second, for_own = blocks_of(key_grads)[:3]
        key_parts = []
        for r in range(4):
            part = jnp.where(member_id == r, for_first, zero)
            part += jnp.where(member_id ^ 1 == r, for_second, zero)
            key_parts.append(part + for_own if r == 0 else part)
    else:
        key_parts = blocks_of(key_grads)
    if cut:
        out_found = out_found[1], exchange_cores(out_found[0])
        key_parts = after(key_parts, (mixture_parts[1:], up_sum))
    keyval_sum = scatter_blocks(key_parts)
    if cut:
        out_state = scatter_start(join_cores(*out_found))
    if cut:
        keyval_sum = after(keyval_sum, out_found)
    left = leave(
        place,
        qkv_spots,
        (
            keyval_sum,
            query_grad,
            normed,
            tokens[0],
            resid_grad,
            small,
            cosine,
            sine_part,
        ),
        qkv_pieces,
        cut,
        first_gain,
    )
    qkv_found, input_grad = left[:-1], left[-1]
    result = (residual + total_of(mixture_parts)).astype(low)
    if cut:
        down_term = step_down(after(down_sum, key_parts))
        received = exchange_cores(after(qkv_found[0], (totals[0], out_state[1:], down_term)))
        up_term = step_up(up_sum)
        qkv_parts = join_cores(qkv_found[1], received)
        qkv_first = scatter_start(qkv_parts)
        out_plane = scatter_finish(after(out_state, qkv_first[1:3]))
        qkv_plane = after(scatter_finish(qkv_first), up_term)
        out_sum = line_finish(line_start(out_plane))
        qkv_state = line_start(qkv_plane)
        near, down_term, up_term = after((near, down_term, up_term), qkv_plane)
        terms = [[(totals[0], 0)], [(own, None), (near, 1), (down_term, None), (up_term, None)]]
        expert_totals = unpack(terms, gate_weight.shape, down_weight.shape)
        qkv_sum = line_finish(qkv_state, expert_totals)
    else:
        out_sum = scatter_whole(out_found)
        qkv_sum = scatter_whole(qkv_found)
        totals += [sum_chunk(found[0]) for found in chunk_grads[1:]]
        terms = [[(total, 0)] for total in totals]
        expert_totals = unpack(terms, gate_weight.shape, down_weight.shape)
    gate_total, up_total, down_total = expert_totals
    return (
        result[None],
        input_grad[None],
        qkv_sum[:, qkv_width + first_gain],
        qkv_sum[:, :query_width],
        qkv_sum[:, query_width : query_width + kv_width],
        qkv_sum[:, query_width + kv_width : qkv_width],
        out_sum[:, :width],
        out_sum[:, width + second_gain],
        out_sum[:, width : width + experts_total],
        gate_total,
        up_total,
        down_total,
    )


def solution(mesh):
    return jax.shard_map(
        local,
        mesh=mesh,
        in_specs=(
            P("batch", "expert", None),
            P("batch", "expert", None),
            P(("batch", "expert")),
            P(("batch", "expert"), None),
            P(("batch", "expert"), None),
            P(("batch", "expert"), None),
            P(("batch", "expert"), None),
            P(("batch", "expert")),
            P(("batch", "expert"), None),
            P("expert", "batch", None),
            P("expert", "batch", None),
            P("expert", "batch", None),
            P("batch", "expert", None),
            P("batch", "expert"),
        ),
        out_specs=(
            P("batch", "expert", None),
            P("batch", "expert", None),
            P(("batch", "expert")),
            P(("batch", "expert"), None),
            P(("batch", "expert"), None),
            P(("batch", "expert"), None),
            P(("batch", "expert"), None),
            P(("batch", "expert")),
            P(("batch", "expert"), None),
            P("expert", "batch", None),
            P("expert", "batch", None),
            P("expert", "batch", None),
        ),
        check_vma=False,
    )
```
